32 devices in a mesh: dp: 8 (over z, y), tensor: 4 (over x, core).
Axes of the slice: x: 2, y: 2, z: 4, core: 2. Of those that a mesh axis runs over, the one named last changes fastest.
Arguments:
- tokens: bfloat16 [16384, 768], P(('dp', 'tensor')), may hold values from -6 to 6
- segment_ids: int32 [16, 1024], P('dp'), may hold values from 0 to 3, never falling along the last dimension, each value on 1 to 512 neighbouring positions
- ln1_gain: float32 [768], replicated, may hold values from 0.25 to 1.75
- ln1_bias: float32 [768], replicated, may hold values from -3 to 3
- qkv_weight: bfloat16 [3, 768, 768], P(None, None, 'tensor'), may hold values from -0.21875 to 0.21875
- qv_bias: float32 [2, 768], P(None, 'tensor'), may hold values from -1.5 to 1.5
- out_weight: bfloat16 [768, 768], P('tensor'), may hold values from -0.21875 to 0.21875
- out_bias: float32 [768], replicated, may hold values from -3 to 3
- ln2_gain: float32 [768], replicated, may hold values from 0.25 to 1.75
- ln2_bias: float32 [768], replicated, may hold values from -3 to 3
- fc1_weight: bfloat16 [768, 3072], P(None, 'tensor'), may hold values from -0.21875 to 0.21875
- fc1_bias: float32 [3072], P('tensor'), may hold values from -3 to 3
- fc2_weight: bfloat16 [3072, 768], P('tensor'), may hold values from -0.109375 to 0.109375
- fc2_bias: float32 [768], replicated, may hold values from -3 to 3
- cotangent: bfloat16 [16384, 768], P(('dp', 'tensor')), may hold values from -6 to 6
Outputs:
- output: bfloat16 [16384, 768], P(('dp', 'tensor'))
- input_grad: bfloat16 [16384, 768], P(('dp', 'tensor'))
- ln1_gain_grad: float32 [768], replicated
- ln1_bias_grad: float32 [768], replicated
- qkv_grad: float32 [3, 768, 768], P(None, None, 'tensor')
- qv_bias_grad: float32 [2, 768], P(None, 'tensor')
- out_weight_grad: float32 [768, 768], P('tensor')
- out_bias_grad: float32 [768], replicated
- ln2_gain_grad: float32 [768], replicated
- ln2_bias_grad: float32 [768], replicated
- fc1_grad: float32 [768, 3072], P(None, 'tensor')
- fc1_bias_grad: float32 [3072], P('tensor')
- fc2_grad: float32 [3072, 768], P('tensor')
- fc2_bias_grad: float32 [768], replicated
The draws below stay inside these ranges and needn't reach their ends.
Inputs may be any that keep to these rules, and one draw needn't show every extreme that they name: `segment_ids`: each sequence holds 4 documents whose ids never fall along it; each document has 1 to 512 tokens, one exactly 512.
All inputs are finite; a program needn't handle non-finite values.
Results may differ from the reference program's by a relative error of at most 0.015.
Values may be sent and summed in bfloat16 or wider, within the bound.
A program may use at most 192 MiB of HBM per device.

```python
import math
from functools import partial
import jax
import jax.numpy as jnp
import numpy as np
from jax import lax

D = 768
HEADS = 12
FF = 3072
HEAD = 64
SIDE = 16
LEN = 1024
SEQS = 16
TOKENS = 16384


def block_scale(own_key, extent, split, smallest, high):
    loudness, own = 1.0, jax.random.fold_in(own_key, 6)
    for dim, parts in split:
        heights = jnp.exp(jax.random.uniform(jax.random.fold_in(own, dim), (parts,), jnp.float32, smallest / len(split), high / len(split)))
        loudness = loudness * jnp.repeat(heights, extent[dim] // parts).reshape([-1 if axis == dim else 1 for axis in range(len(extent))])
    return loudness


def split_up(amount, total, bound, lean):
    weights = [(1 << 20) // math.isqrt(standing ** lean) + 1 for standing in range(2, amount + 1)]
    spare, counts = total - bound - (amount - 1), [1] * (amount - 1)
    while spare > 0:
        free = [i for i in range(amount - 1) if counts[i] < bound]
        mass, left = sum([weights[i] for i in free]), spare
        for i in free:
            extra = min(bound - counts[i], max(1, left * weights[i] // mass), spare)
            counts[i] = counts[i] + extra
            spare = spare - extra
    return np.array([bound] + counts)


def uneven_parts(own_key, count, total, limit, lean):
    if count == 2:
        one = jax.random.randint(own_key, (), max(1, total - limit), min(limit, total - 1) + 1)
        return jnp.stack([one, total - one])
    lengths = jnp.asarray(split_up(count, total, limit, lean), jnp.int32)
    pairs = (count - 1) // 2
    source_of, sink = lengths[1:1 + 2 * pairs:2], lengths[2:2 + 2 * pairs:2]
    room = jnp.minimum(source_of - 1, limit - sink)
    passed = jax.random.randint(jax.random.fold_in(own_key, 1), (pairs,), 0, 1 << 20) % (room + 1)
    lengths = lengths.at[1:1 + 2 * pairs:2].set(source_of - passed).at[2:2 + 2 * pairs:2].set(sink + passed)
    return lengths[jax.random.permutation(jax.random.fold_in(own_key, 2), count)]


def scatter_about(own_key, extent, width, most, split=(), kind=jnp.bfloat16):
    values = jax.random.normal(own_key, extent, jnp.float32) * width
    if len(split) > 0:
        values = block_scale(own_key, extent, split, -0.22, 0.18) * values
    return jnp.clip(values, min=-most, max=most).astype(kind)


def setup_inputs(seed: int = 0) -> dict:
    keys = jax.random.split(jax.random.key(seed), 16)
    return {
        "tokens": scatter_about(keys[0], (TOKENS, D), 1.0, 6.0, ((0, 32),)),
        "segment_ids": jax.vmap(lambda own: jnp.searchsorted(jnp.cumsum(uneven_parts(own, 4, LEN, LEN // 2, 1)), jnp.arange(LEN), side="right"))(jax.random.split(keys[1], SEQS)).reshape((SEQS, LEN)).astype(jnp.int32),
        "ln1_gain": jnp.clip(1.0 + 0.15 * jax.random.normal(keys[2], (D,), jnp.float32), 0.25, 1.75),
        "ln1_bias": scatter_about(keys[3], (D,), 0.5, 3.0, (), jnp.float32),
        "qkv_weight": scatter_about(keys[4], (3, D, D), D ** -0.5, 0.21875, ((2, 4),)),
        "qv_bias": scatter_about(keys[5], (2, D), 0.25, 1.5, ((1, 4),), jnp.float32),
        "out_weight": scatter_about(keys[6], (D, D), D ** -0.5, 0.21875, ((0, 4),)),
        "out_bias": scatter_about(keys[7], (D,), 0.5, 3.0, (), jnp.float32),
        "ln2_gain": jnp.clip(1.0 + 0.15 * jax.random.normal(keys[8], (D,), jnp.float32), 0.25, 1.75),
        "ln2_bias": scatter_about(keys[9], (D,), 0.5, 3.0, (), jnp.float32),
        "fc1_weight": scatter_about(keys[10], (D, FF), D ** -0.5, 0.21875, ((1, 4),)),
        "fc1_bias": scatter_about(keys[11], (FF,), 0.5, 3.0, ((0, 4),), jnp.float32),
        "fc2_weight": scatter_about(keys[12], (FF, D), FF ** -0.5, 0.109375, ((0, 4),)),
        "fc2_bias": scatter_about(keys[13], (D,), 0.5, 3.0, (), jnp.float32),
        "cotangent": scatter_about(keys[14], (TOKENS, D), 1.0, 6.0, ((0, 32),)),
    }


EPSILON = 1e-06
NEG_LARGE = -1e+30
HIGHEST = lax.Precision.HIGHEST

@jax.custom_vjp
def low(v):
    return lax.optimization_barrier(v.astype(jnp.bfloat16)).astype(jnp.float32)

@jax.custom_vjp
def low_back(v):
    return v

def low_keep(v):
    return (low(v), None)

def low_pass(kept, grad):
    return (grad,)

def back_keep(v):
    return (v, None)

def back_low(kept, grad):
    return (low(grad),)
low.defvjp(low_keep, low_pass)
low_back.defvjp(back_keep, back_low)

def layer_norm(hidden, gain_vec, shift_vec):
    average = lax.optimization_barrier(jnp.mean(hidden, axis=-1, keepdims=True))
    centred = hidden - average
    variance = lax.optimization_barrier(jnp.mean(centred * centred, axis=-1, keepdims=True))
    return centred * lax.rsqrt(variance + EPSILON) * gain_vec + shift_vec

def exact_gelu(hidden):
    return jax.nn.gelu(hidden, approximate=False)

def sincos(position, model_width):
    plane_size = SIDE * SIDE
    coords_all = (position // plane_size, position // SIDE % SIDE, position % SIDE)
    freq_count = model_width // 6
    frequency = 10000.0 ** (-jnp.arange(freq_count, dtype=jnp.float32) / freq_count)
    pieces = []
    for coordinate in coords_all:
        angles = coordinate.astype(jnp.float32)[:, None] * frequency[None, :]
        pieces.append(jnp.sin(angles))
        pieces.append(jnp.cos(angles))
    return jnp.concatenate(pieces, axis=-1)

def layer_block(weights_all, packed):
    stream_rows, doc_ids = packed
    gain_one, shift_one, qkv_w, qv_b, out_w, out_b, gain_two, shift_two, fc1_w, fc1_b, fc2_w, fc2_b = weights_all
    group_rows = stream_rows.shape[0]
    position_table = jnp.tile(sincos(jnp.arange(LEN, dtype=jnp.int32), D), (4, 1))
    stream_in = stream_rows + position_table
    normed_one = low(layer_norm(stream_in, gain_one, shift_one))
    bias_three = jnp.stack([qv_b[0], jnp.zeros_like(qv_b[0]), qv_b[1]])
    projected = jnp.einsum('td,cde->tce', normed_one, qkv_w, precision=HIGHEST) + bias_three
    projected = low(low_back(projected))
    pieces = projected.reshape(4, LEN, 3, HEADS, HEAD)
    queries, keys_all, values = (pieces[:, :, 0], pieces[:, :, 1], pieces[:, :, 2])
    scores = low_back(jnp.einsum('sqhd,skhd->shqk', queries, keys_all, precision=HIGHEST))
    same_doc = doc_ids[:, :, None] == doc_ids[:, None, :]
    logits = jnp.where(same_doc[:, None], scores * HEAD ** (-0.5), NEG_LARGE)
    attn_probs = low(jax.nn.softmax(logits, axis=-1))
    attended = jnp.einsum('shqk,skhd->sqhd', attn_probs, values, precision=HIGHEST).reshape(group_rows, D)
    attended = low(low_back(attended))
    branch_one = low_back(jnp.dot(attended, out_w, precision=HIGHEST))
    stream_mid = stream_in + branch_one + out_b
    normed_two = low(layer_norm(stream_mid, gain_two, shift_two))
    hidden_pre = low_back(jnp.dot(normed_two, fc1_w, precision=HIGHEST) + fc1_b)
    activated = low(exact_gelu(hidden_pre))
    branch_two = low_back(jnp.dot(activated, fc2_w, precision=HIGHEST))
    return stream_mid + branch_two + fc2_b

def reference(tokens, segment_ids, ln1_gain, ln1_bias, qkv_weight, qv_bias, out_weight, out_bias, ln2_gain, ln2_bias, fc1_weight, fc1_bias, fc2_weight, fc2_bias, cotangent):
    groups = SEQS // 4
    doc_groups = segment_ids.reshape(groups, 4, LEN)

    def forward(stream_all, *weights_all):
        packed = (stream_all.reshape(groups, 4 * LEN, D), doc_groups)
        result = lax.map(jax.checkpoint(partial(layer_block, weights_all)), packed)
        return result.reshape(SEQS * LEN, D)
    floats = [item.astype(jnp.float32) for item in (tokens, ln1_gain, ln1_bias, qkv_weight, qv_bias, out_weight, out_bias, ln2_gain, ln2_bias, fc1_weight, fc1_bias, fc2_weight, fc2_bias)]
    output, backward = jax.vjp(forward, *floats)
    gradients = backward(cotangent.astype(jnp.float32))
    return (output.astype(jnp.bfloat16), gradients[0].astype(jnp.bfloat16), gradients[1], gradients[2], gradients[3], gradients[4], gradients[5], gradients[6], gradients[7], gradients[8], gradients[9], gradients[10], gradients[11], gradients[12])
```

```python
import functools

import jax
import jax.numpy as jnp
from jax import lax
from jax.experimental import pallas as pl
from jax.experimental.pallas import tpu as pltpu
from jax.sharding import PartitionSpec as P

HEAD = 64
SIDE = 16
LEN = 1024
EPSILON = 1e-06
NEG_LARGE = -1e30
SCALE = HEAD ** (-0.5)
F32 = jnp.float32
BF16 = jnp.bfloat16
VMEM_LIMIT = 60 * 1024 * 1024


def dot(a, b):
    return jnp.dot(a, b, preferred_element_type=F32)


def dot_nt(a, b):
    return lax.dot_general(a, b, (((1,), (1,)), ((), ())), preferred_element_type=F32)


def dot_tn(a, b):
    return lax.dot_general(a, b, (((0,), (0,)), ((), ())), preferred_element_type=F32)


def lane_half(rows, upper):
    lanes = lax.broadcasted_iota(jnp.int32, (rows, 128), 1)
    return lanes >= 64 if upper else lanes < 64


def head_lanes(ref, head, filler):
    tile = ref[:, 128 * (head // 2) : 128 * (head // 2) + 128]
    return jnp.where(lane_half(tile.shape[0], head % 2 == 1), tile, filler)


def attend_forward(n1, w, b, sq, sk, q_o, k_o, v_o, kt_o, e_o, ot_o, r_o, q_s, k_s):
    rows = n1.shape[0]
    width = w.shape[3]
    n = n1[...]
    q = (dot(n, w[0, 0]) + b[0, 0]).astype(BF16) * SCALE
    k = (dot(n, w[0, 1]) + b[0, 1]).astype(BF16)
    v = (dot(n, w[0, 2]) + b[0, 2]).astype(BF16)
    q_o[0] = q
    k_o[0] = k
    v_o[0] = v
    q_s[:, :width] = q
    k_s[:, :width] = k
    kt_o[0] = k.T * SCALE
    vt = v.T
    step = 256
    for head in range(width // HEAD):
        qh = head_lanes(q_s, head, sq[...])
        kh = head_lanes(k_s, head, sk[...])
        span = slice(head * HEAD, head * HEAD + HEAD)
        for at in range(0, rows, step):
            s = dot_nt(kh, qh[at : at + step])
            m = jnp.max(s, axis=0, keepdims=True)
            e = jnp.exp(s - m)
            r = 1.0 / jnp.sum(e, axis=0, keepdims=True)
            low = e.astype(BF16)
            e_o[head, :, at : at + step] = low
            ot_o[0, span, at : at + step] = (dot(vt[span], low) * r).astype(BF16)
            r_o[0, head : head + 1, at : at + step] = r


def attend_backward(q_i, k_i, v_i, kt_i, e_i, ot_i, r_i, dm, wo, d_o, dwo_o, q_s, v_s, g_s, s_s):
    rows = dm.shape[0]
    width = wo.shape[1]
    q_s[:, :width] = q_i[0]
    v_s[:, :width] = v_i[0]
    dot_out = dot_nt(wo[0], dm[...]).astype(BF16).astype(F32)
    ot = ot_i[0]
    dwo_o[0] = dot(ot, dm[...]).astype(BF16)
    heads = width // HEAD
    scaled = []
    inners = []
    for head in range(heads):
        span = slice(head * HEAD, head * HEAD + HEAD)
        r = r_i[0, head : head + 1, :]
        g = dot_out[span]
        inners.append(jnp.sum(g * ot[span].astype(F32), axis=0, keepdims=True) * r)
        scaled.append((g * r).astype(BF16))
    gt = jnp.concatenate(scaled, axis=0)
    g_s[:, :width] = gt.T
    step = 256
    dq = []
    dk = [None, None]
    dv = [None, None]
    for head in range(heads):
        span = slice(head * HEAD, head * HEAD + HEAD)
        tile = head // 2
        zero = jnp.zeros((rows, 128), BF16)
        vh = head_lanes(v_s, head, zero)
        qh = head_lanes(q_s, head, zero)
        gh = head_lanes(g_s, head, zero)
        if 128 * tile + 128 <= width:
            gth = gt[128 * tile : 128 * tile + 128]
        else:
            gth = gt[128 * tile :]
            vh = vh[:, : gth.shape[0]]
        for at in range(0, rows, step):
            dp = dot(vh, gth[:, at : at + step])
            ds = (dp - inners[head][:, at : at + step]) * e_i[head, :, at : at + step].astype(F32)
            s_s[:, at : at + step] = ds.astype(BF16)
        dvh = dot(e_i[head], gh)
        dkh = dot(s_s[...], qh)
        dv[tile] = dvh if dv[tile] is None else dv[tile] + dvh
        dk[tile] = dkh if dk[tile] is None else dk[tile] + dkh
        dq.append(dot(kt_i[0, span], s_s[...]))
    d_o[0, 0] = jnp.concatenate(dq, axis=0).T.astype(BF16)
    for part, total in ((1, dk), (2, dv)):
        for tile in range(2):
            lo = 128 * tile
            hi = min(lo + 128, width)
            if hi > lo:
                d_o[0, part, :, lo:hi] = total[tile][:, : hi - lo].astype(BF16)


def gelu_pair(h):
    size = jnp.abs(h)
    t = 1.0 / (1.0 + (0.3275911 * 0.7071067811865476) * size)
    bell = jnp.exp(-0.5 * h * h)
    poly = ((((1.061405429 * t - 1.453152027) * t + 1.421413741) * t - 0.284496736) * t + 0.254829592) * t
    tail = 0.5 * poly * bell
    cdf = jnp.where(h < 0, tail, 1.0 - tail)
    return h * cdf, cdf + h * bell * 0.3989422804014327


def mlp(n2, cot, w1, b1, w2, out_o, gn_o, g1_o, g2_o, gb_o):
    n = n2[...]
    c = cot[...]
    h = dot(n, w1[0]) + b1[0]
    a, slope = gelu_pair(h)
    a = a.astype(BF16)
    g = (dot_nt(c, w2[0]) * slope).astype(BF16)
    g2_o[0] = dot_tn(a, c).astype(BF16)
    g1_o[0] = dot_tn(n, g).astype(BF16)
    gb_o[0] = jnp.sum(g.astype(F32), axis=0, keepdims=True)
    part = dot(a, w2[0])
    back = dot_nt(g, w1[0])
    first = (pl.program_id(0) == 0) & (pl.program_id(1) == 0)

    @pl.when(first)
    def _():
        out_o[...] = part
        gn_o[...] = back

    @pl.when(jnp.logical_not(first))
    def _():
        out_o[...] += part
        gn_o[...] += back


def whole(shape):
    return pl.BlockSpec(shape, lambda *_: (0,) * len(shape))


def by_quarter(shape):
    return pl.BlockSpec(shape, lambda j: (j,) + (0,) * (len(shape) - 1))


def call_forward(n1, w, b, sq, sk):
    rows, width = n1.shape[0], w.shape[3]
    heads = width // HEAD
    shape = jax.ShapeDtypeStruct
    return pl.pallas_call(
        attend_forward,
        grid=(2,),
        in_specs=[whole(n1.shape), by_quarter((1,) + w.shape[1:]), by_quarter((1,) + b.shape[1:]), whole(sq.shape), whole(sk.shape)],
        out_specs=[by_quarter((1, rows, width))] * 3
        + [by_quarter((1, width, rows)), by_quarter((heads, rows, rows)), by_quarter((1, width, rows)), by_quarter((1, 8, rows))],
        out_shape=[shape((2, rows, width), BF16)] * 3
        + [shape((2, width, rows), BF16), shape((2 * heads, rows, rows), BF16), shape((2, width, rows), BF16), shape((2, 8, rows), F32)],
        scratch_shapes=[pltpu.VMEM((rows, 256), BF16)] * 2,
        compiler_params=pltpu.CompilerParams(vmem_limit_bytes=VMEM_LIMIT),
        cost_estimate=pl.CostEstimate(flops=int(1.8e9 + 6 * 4 * rows * rows * 256), bytes_accessed=20_000_000, transcendentals=6 * rows * rows),
        name="attend_forward",
    )(n1, w, b, sq, sk)


def call_backward(q, k, v, kt, e, ot, r, dm, wo):
    rows, width = dm.shape[0], wo.shape[1]
    heads = width // HEAD
    shape = jax.ShapeDtypeStruct
    return pl.pallas_call(
        attend_backward,
        grid=(2,),
        in_specs=[by_quarter((1, rows, width))] * 3
        + [by_quarter((1, width, rows)), by_quarter((heads, rows, rows)), by_quarter((1, width, rows)), by_quarter((1, 8, rows)), whole(dm.shape), by_quarter((1,) + wo.shape[1:])],
        out_specs=[by_quarter((1, 3, rows, width)), by_quarter((1,) + wo.shape[1:])],
        out_shape=[shape((2, 3, rows, width), BF16), shape(wo.shape, BF16)],
        scratch_shapes=[pltpu.VMEM((rows, 256), BF16)] * 3 + [pltpu.VMEM((rows, rows), BF16)],
        compiler_params=pltpu.CompilerParams(vmem_limit_bytes=VMEM_LIMIT),
        cost_estimate=pl.CostEstimate(flops=int(1.8e9 + 6 * 8 * rows * rows * 256), bytes_accessed=25_000_000, transcendentals=0),
        name="attend_backward",
    )(q, k, v, kt, e, ot, r, dm, wo)


def call_mlp(n2, cot, w1, b1, w2):
    rows, width = n2.shape
    units = w1.shape[2]
    step = 256
    shape = jax.ShapeDtypeStruct
    across = pl.BlockSpec((1, width, step), lambda j, i: (j, 0, i))
    down = pl.BlockSpec((1, step, width), lambda j, i: (j, i, 0))
    bias = pl.BlockSpec((1, 1, step), lambda j, i: (j, 0, i))
    return pl.pallas_call(
        mlp,
        grid=(2, units // step),
        in_specs=[whole(n2.shape), whole(cot.shape), across, bias, down],
        out_specs=[whole(n2.shape), whole(n2.shape), across, down, bias],
        out_shape=[shape(n2.shape, F32), shape(n2.shape, F32), shape(w1.shape, BF16), shape(w2.shape, BF16), shape(b1.shape, F32)],
        compiler_params=pltpu.CompilerParams(vmem_limit_bytes=VMEM_LIMIT),
        cost_estimate=pl.CostEstimate(flops=12 * rows * width * 2 * units, bytes_accessed=25_000_000, transcendentals=4 * rows * units),
        name="mlp",
    )(n2, cot, w1, b1, w2)


def position_rows(count, first_plane, width):
    freq_count = width // 6
    frequency = 10000.0 ** (-jnp.arange(freq_count, dtype=F32) / freq_count)
    angles = jnp.arange(SIDE, dtype=F32)[:, None] * frequency[None, :]
    sines, cosines = lax.optimization_barrier((jnp.sin(angles), jnp.cos(angles)))
    planes = count // (SIDE * SIDE)
    full = (planes, SIDE, SIDE, freq_count)
    pieces = []
    for axis in range(3):
        for table in (sines, cosines):
            if axis == 0:
                table = lax.dynamic_slice_in_dim(table, first_plane, planes, axis=0)
            extent = [1, 1, 1, freq_count]
            extent[axis] = table.shape[0]
            pieces.append(jnp.broadcast_to(table.reshape(extent), full))
    return jnp.concatenate(pieces, axis=-1).reshape(count, width)


def norm_stats(v):
    centred = v - jnp.mean(v, axis=-1, keepdims=True)
    sigma = lax.rsqrt(jnp.mean(centred * centred, axis=-1, keepdims=True) + EPSILON)
    return centred * sigma, sigma


def norm_back(grad, gain, xhat, sigma):
    g = grad * gain
    return sigma * (g - jnp.mean(g, axis=-1, keepdims=True) - xhat * jnp.mean(g * xhat, axis=-1, keepdims=True))


def per_device(
    tokens, segment_ids, ln1_gain, ln1_bias, qkv_weight, qv_bias, out_weight, out_bias,
    ln2_gain, ln2_bias, fc1_weight, fc1_bias, fc2_weight, fc2_bias, cotangent,
):
    dp_size = lax.axis_size("dp")
    place = lax.axis_index("tensor")
    dp_place = lax.axis_index("dp")
    core = place % 2
    count, width = tokens.shape

    def swap_chip(v):
        return lax.ppermute(v, "tensor", [(i, i ^ 2) for i in range(4)])

    def swap_core(v):
        return lax.ppermute(v, "tensor", [(i, i ^ 1) for i in range(4)])

    def swap_dp(v, bit):
        return lax.ppermute(v, "dp", [(i, i ^ bit) for i in range(dp_size)])

    def both(v):
        return jnp.stack([v, swap_chip(v)])

    def gather(v):
        return jnp.concatenate([v, swap_core(v)], axis=0)

    def scatter(v):
        return v[:count] + swap_core(v[count:].astype(BF16)).astype(F32)

    bias_three = jnp.stack([qv_bias[0], jnp.zeros_like(qv_bias[0]), qv_bias[1]])[:, None, :]
    w_qkv = both(qkv_weight)
    b_qkv = both(bias_three)
    w_out = both(out_weight)
    w_one = both(fc1_weight)
    b_one = both(fc1_bias[None, :])
    w_two = both(fc2_weight)
    cot_all = gather(cotangent)

    stream_in = tokens.astype(F32) + position_rows(count, core * (count // (SIDE * SIDE)), width)
    xhat_one, sigma_one = norm_stats(stream_in)
    n1 = gather((xhat_one * ln1_gain + ln1_bias).astype(BF16))

    ids = lax.dynamic_index_in_dim(segment_ids, place // 2, axis=0, keepdims=False).reshape(2, count)
    ids = jnp.concatenate(
        [lax.dynamic_index_in_dim(ids, core, axis=0, keepdims=False), lax.dynamic_index_in_dim(ids, 1 - core, axis=0, keepdims=False)]
    )
    lanes = jnp.arange(128) % 64
    same = ids[:, None] == lanes[None, :]
    sq = jnp.where((lanes < 4)[None, :] & ~same, 1.0, 0.0).astype(BF16)
    sk = jnp.where(same, NEG_LARGE, 0.0).astype(BF16)

    q, k, v, kt, e, ot, r = call_forward(n1, w_qkv, b_qkv, sq, sk)
    attention = scatter(jnp.einsum("jet,jed->td", ot, w_out, preferred_element_type=F32))
    stream_mid = stream_in + attention + out_bias
    xhat_two, sigma_two = norm_stats(stream_mid)
    n2 = gather((xhat_two * ln2_gain + ln2_bias).astype(BF16))
    mlp_part, gn2_part, g_one, g_two, gb_one = call_mlp(n2, cot_all, w_one, b_one, w_two)
    gn2 = scatter(gn2_part)
    output = (stream_mid + scatter(mlp_part) + fc2_bias).astype(BF16)
    grad_out = cotangent.astype(F32)
    grad_mid = grad_out + norm_back(gn2, ln2_gain, xhat_two, sigma_two)
    dm = gather(grad_mid.astype(BF16))
    d_proj, g_out = call_backward(q, k, v, kt, e, ot, r, dm, w_out)
    gn1_part = jnp.einsum("jcte,jcde->td", d_proj, w_qkv, preferred_element_type=F32)
    g_qkv = jnp.einsum("td,jcte->jcde", n1, d_proj, preferred_element_type=F32).astype(BF16)
    gb_qv = jnp.sum(d_proj, axis=2, dtype=F32)
    gn1 = scatter(gn1_part)
    input_grad = (grad_mid + norm_back(gn1, ln1_gain, xhat_one, sigma_one)).astype(BF16)

    def all_sum(v):
        halved = []
        bit = 1
        while bit < min(dp_size, 8):
            side = (dp_place // bit) % 2
            pair = v.reshape(2, v.shape[0] // 2, *v.shape[1:])
            keep = lax.dynamic_index_in_dim(pair, side, axis=0, keepdims=False)
            send = lax.dynamic_index_in_dim(pair, 1 - side, axis=0, keepdims=False)
            v = (keep.astype(F32) + swap_dp(send, bit).astype(F32)).astype(BF16)
            halved.append(bit)
            bit *= 2
        while bit < dp_size:
            v = (v.astype(F32) + swap_dp(v, bit).astype(F32)).astype(BF16)
            bit *= 2
        for bit in reversed(halved):
            side = (dp_place // bit) % 2
            other = swap_dp(v, bit)
            v = jnp.where(side == 0, jnp.concatenate([v, other]), jnp.concatenate([other, v]))
        return v

    def reduce_grad(v):
        own = (v[0].astype(F32) + swap_chip(v[1]).astype(F32)).astype(BF16)
        return all_sum(own)

    g_two = reduce_grad(g_two)
    g_one = reduce_grad(g_one)
    g_out = reduce_grad(g_out)
    g_qkv = reduce_grad(g_qkv.reshape(2, 3 * width, -1)).reshape(3, width, -1)

    small = jnp.stack(
        [
            jnp.sum(gn1 * xhat_one, axis=0),
            jnp.sum(gn1, axis=0),
            jnp.sum(grad_mid, axis=0),
            jnp.sum(gn2 * xhat_two, axis=0),
            jnp.sum(gn2, axis=0),
            jnp.sum(grad_out, axis=0),
        ]
    )
    small = small + swap_core(small)
    small = small + swap_chip(small)
    split = jnp.concatenate([gb_one[:, 0], gb_qv[:, 0], gb_qv[:, 2]], axis=1)
    split = split[0] + swap_chip(split[1])
    units = fc1_bias.shape[0]
    flat = jnp.concatenate([small.reshape(-1), split])
    bit = 1
    while bit < dp_size:
        flat = flat + swap_dp(flat, bit)
        bit *= 2
    small = flat[: 6 * width].reshape(6, width)
    split = flat[6 * width :]
    return (
        output,
        input_grad,
        small[0],
        small[1],
        g_qkv.astype(F32),
        split[units:].reshape(2, -1),
        g_out.astype(F32),
        small[2],
        small[3],
        small[4],
        g_one.astype(F32),
        split[:units],
        g_two.astype(F32),
        small[5],
    )


def solution(mesh):
    placed = (
        P(("dp", "tensor"), None),
        P("dp", None),
        P(),
        P(),
        P(None, None, "tensor"),
        P(None, "tensor"),
        P("tensor", None),
        P(),
        P(),
        P(),
        P(None, "tensor"),
        P("tensor"),
        P("tensor", None),
        P(),
        P(("dp", "tensor"), None),
    )
    return jax.shard_map(
        per_device,
        mesh=mesh,
        in_specs=placed,
        out_specs=(
            P(("dp", "tensor"), None),
            P(("dp", "tensor"), None),
            P(),
            P(),
            P(None, None, "tensor"),
            P(None, "tensor"),
            P("tensor", None),
            P(),
            P(),
            P(),
            P(None, "tensor"),
            P("tensor"),
            P("tensor", None),
            P(),
        ),
        check_vma=False,
    )
```

```python
import functools

import jax
import jax.numpy as jnp
from jax import lax
from jax.experimental import pallas as pl
from jax.experimental.pallas import tpu as pltpu
from jax.sharding import PartitionSpec as P

HEAD = 64
SIDE = 16
EPSILON = 1e-06
NEG_LARGE = -1e30
SCALE = HEAD ** (-0.5)
F32 = jnp.float32
BF16 = jnp.bfloat16
VMEM_LIMIT = 64 * 1024 * 1024 - 128 * 1024
MESH = pl.DeviceIdType.MESH
BLOCK = 256


def dot(a, b):
    return jnp.dot(a, b, preferred_element_type=F32)


def dot_nt(a, b):
    return lax.dot_general(a, b, (((1,), (1,)), ((), ())), preferred_element_type=F32)


def dot_tn(a, b):
    return lax.dot_general(a, b, (((0,), (0,)), ((), ())), preferred_element_type=F32)


def lane_half(rows, upper):
    lanes = lax.broadcasted_iota(jnp.int32, (rows, 128), 1)
    return lanes >= HEAD if upper else lanes < HEAD


def head_lanes(ref, head, filler):
    tile = ref[:, 128 * (head // 2) : 128 * (head // 2) + 128]
    return jnp.where(lane_half(tile.shape[0], head % 2 == 1), tile, filler)


def gelu_pair(h):
    size = jnp.abs(h)
    t = 1.0 / (1.0 + (0.3275911 * 0.7071067811865476) * size)
    bell = jnp.exp(-0.5 * h * h)
    poly = ((((1.061405429 * t - 1.453152027) * t + 1.421413741) * t - 0.284496736) * t + 0.254829592) * t
    tail = 0.5 * poly * bell
    cdf = jnp.where(h < 0, tail, 1.0 - tail)
    return h * cdf, cdf + h * bell * 0.3989422804014327


def norm_stats(v):
    centred = v - jnp.mean(v, axis=-1, keepdims=True)
    sigma = lax.rsqrt(jnp.mean(centred * centred, axis=-1, keepdims=True) + EPSILON)
    return centred * sigma, sigma


def norm_back(grad, gain, xhat, sigma):
    g = grad * gain
    return sigma * (g - jnp.mean(g, axis=-1, keepdims=True) - xhat * jnp.mean(g * xhat, axis=-1, keepdims=True))


def column_sum(v):
    return jnp.sum(v, axis=0, keepdims=True)


def loop(count, step, body):
    def run(i, carry):
        body(pl.multiple_of(i * step, step))
        return carry

    lax.fori_loop(0, count // step, run, 0)


def layer(
    dp_size, half_bits,
    tok_h, cot_h, ids, table, vec, wq_h, wo_h, w1_h, w2_h,
    out_h, ing_h, grad_h, small_o,
    tok_s, cot_s, sin_s, mid_s, gm_s, n1_s, n2_s, n2t_s, wq_s, wo_s, w1_s, w2_s,
    q_s, v_s, kt_s, ot_s, r_s, e_s, a_s, g_s, sb1, sb2, rb1, rb2,
    own, oth, xr, *rest,
):
    rest = list(rest)
    rr = [rest.pop(0) for _ in half_bits]
    full_bits = [b for b in range(20) if (1 << b) < dp_size and b not in half_bits]
    rx = [rest.pop(0) for _ in full_bits]
    voth, sm, smr, lsem, wsem, csem, gsem, ssem = rest

    count, width = tok_s.shape
    rows = 2 * count
    quarter = wo_h.shape[0]
    units = w1_h.shape[1]
    heads = quarter // HEAD
    place = lax.axis_index("tensor")
    dp = lax.axis_index("dp")
    chip = place // 2
    core = place % 2
    sib = {"tensor": chip * 2 + 1 - core}
    across = {"tensor": (1 - chip) * 2 + core}
    all_bits = list(half_bits) + full_bits
    sides = {b: (dp // (1 << b)) % 2 for b in all_bits}
    mates = {b: {"dp": dp + (1 - 2 * sides[b]) * (1 << b)} for b in all_bits}

    barrier = pltpu.get_barrier_semaphore()
    partners = [sib, across] + [mates[b] for b in all_bits]
    for partner in partners:
        pl.semaphore_signal(barrier, inc=1, device_id=partner, device_id_type=MESH)

    sq_s, sk_s, k_s = a_s.at[:, 0:128], a_s.at[:, 128:256], a_s.at[:, 256:512]
    ds_s, go_s = a_s.at[:, 0:rows], a_s.at[:, rows : rows + 256]
    local_used = [0]

    def local(src, dst):
        copy = pltpu.make_async_copy(src, dst, lsem.at[local_used[0]])
        local_used[0] += 1
        copy.start()
        return copy

    def remote(src, dst, sems, index, device):
        copy = pltpu.make_async_remote_copy(
            src_ref=src, dst_ref=dst, send_sem=sems.at[0, index], recv_sem=sems.at[1, index], device_id=device, device_id_type=MESH
        )
        copy.start()
        return copy

    get_tok = local(tok_h, tok_s)
    get_cot = local(cot_h, cot_s.at[pl.ds(0, count)])
    get_wq = local(wq_h, wq_s.at[0])
    get_wo = local(wo_h, wo_s.at[pl.ds(0, quarter)])
    get_w1 = local(w1_h, w1_s.at[0])
    get_w2 = local(w2_h, w2_s.at[0])

    part = sides[0]

    def piece(ref, extent):
        return ref.at[pl.ds(pl.multiple_of(part * (extent // 2), 32), extent // 2)]

    def piece_q(ref):
        return ref.at[:, pl.ds(pl.multiple_of(part * (width // 2), 32), width // 2)]

    places = [piece_q(wq_s.at[1]), None, piece(w1_s.at[1], width), piece(w2_s.at[1], units)]
    wo_at = pl.multiple_of(quarter + part * (quarter // 2), 32)
    places[1] = wo_s.at[pl.ds(wo_at, quarter // 2)]
    sources = [piece_q(wq_h), piece(wo_h, quarter), piece(w1_h, width), piece(w2_h, units)]

    pl.semaphore_wait(barrier, len(partners))
    vec_copy = remote(vec.at[pl.ds(8, 8)], voth, wsem, 8, across)
    by_x, by_y = [None] * 4, [None] * 4

    def fetch_weight(i):
        by_x[i] = remote(sources[i], places[i], wsem, i, across)

    def forward_weight(i):
        by_x[i].wait_recv()
        by_y[i] = remote(places[i], places[i], wsem, 4 + i, mates[0])

    fetch_weight(0)
    fetch_weight(1)

    ln1_gain, ln1_bias, out_bias = vec[0:1], vec[1:2], vec[2:3]
    ln2_gain, ln2_bias, fc2_bias = vec[3:4], vec[4:5], vec[5:6]
    get_tok.wait()

    def first_norm(at):
        plane = core * (count // (SIDE * SIDE)) + at // (SIDE * SIDE)
        line = (at // SIDE) % SIDE
        third = width // 3
        shape = (SIDE, third)
        spot = jnp.concatenate(
            [jnp.broadcast_to(table[pl.ds(plane, 1)], shape), jnp.broadcast_to(table[pl.ds(line, 1)], shape), table[...]], axis=1
        )
        stream = tok_s[pl.ds(at, SIDE)].astype(F32) + spot
        sin_s[pl.ds(at, SIDE)] = stream
        xhat, _ = norm_stats(stream)
        n1_s[pl.ds(at, SIDE)] = (xhat * ln1_gain + ln1_bias).astype(BF16)

    loop(count, SIDE, first_norm)
    n1_copy = remote(n1_s.at[pl.ds(0, count)], n1_s.at[pl.ds(count, count)], csem, 0, sib)
    get_cot.wait()
    cot_copy = remote(cot_s.at[pl.ds(0, count)], cot_s.at[pl.ds(count, count)], csem, 1, sib)

    for at in range(2):
        side = core if at == 0 else 1 - core
        doc = ids[pl.ds(chip, 1), pl.ds(pl.multiple_of(side * count, 128), count)]
        slot = lax.broadcasted_iota(jnp.int32, (128, count), 0) % HEAD
        same = slot == doc
        mark = jnp.where((slot < 4) & jnp.logical_not(same), 1.0, 0.0)
        block = jnp.where(same, NEG_LARGE, 0.0)
        sq_s[at * count : (at + 1) * count] = mark.T.astype(BF16)
        sk_s[at * count : (at + 1) * count] = block.T.astype(BF16)

    def project(j, at):
        n = n1_s[pl.ds(at, BLOCK)]
        biases = vec if j == 0 else voth
        low = 8 if j == 0 else 0
        q = (dot(n, wq_s[j, 0]) + biases[low + 1 : low + 2, :quarter]).astype(BF16) * SCALE
        k = dot(n, wq_s[j, 1]).astype(BF16)
        v = (dot(n, wq_s[j, 2]) + biases[low + 2 : low + 3, :quarter]).astype(BF16)
        q_s[j, pl.ds(at, BLOCK), :quarter] = q
        k_s[pl.ds(at, BLOCK), :quarter] = k
        v_s[j, pl.ds(at, BLOCK), :quarter] = v
        kt_s[j * quarter : (j + 1) * quarter, pl.ds(at, BLOCK)] = k.T * SCALE

    def attend(j, service):
        vt = v_s[j, :, :quarter].T
        for head in range(heads):
            qh = head_lanes(q_s.at[j], head, sq_s[...])
            kh = head_lanes(k_s, head, sk_s[...])
            span = slice(head * HEAD, head * HEAD + HEAD)
            to = slice(j * quarter + head * HEAD, j * quarter + head * HEAD + HEAD)
            for at in range(0, rows, BLOCK):
                s = dot_nt(kh, qh[at : at + BLOCK])
                m = jnp.max(s, axis=0, keepdims=True)
                e = jnp.exp(s - m)
                r = 1.0 / column_sum(e)
                low = e.astype(BF16)
                e_s[j * heads + head, :, at : at + BLOCK] = low
                ot_s[to, at : at + BLOCK] = (dot(vt[span], low) * r).astype(BF16)
                r_s[j * heads + head : j * heads + head + 1, at : at + BLOCK] = r
            service[head]()

    get_wq.wait()
    loop(count, BLOCK, lambda at: project(0, at))
    n1_copy.wait_recv()
    loop(count, BLOCK, lambda at: project(0, count + at))
    forward_weight(0)
    fetch_weight(2)
    nothing = lambda: None
    attend(0, [lambda: (forward_weight(1), fetch_weight(3)), nothing, nothing])
    vec_copy.wait_recv()
    by_y[0].wait_recv()
    loop(rows, BLOCK, lambda at: project(1, at))
    attend(1, [lambda: forward_weight(2), nothing, lambda: forward_weight(3)])

    get_wo.wait()
    by_y[1].wait_recv()

    def out_part(at):
        return dot_tn(ot_s[:, pl.ds(at, BLOCK)], wo_s[...])

    def out_sib(at):
        sb1[pl.ds(at, BLOCK)] = out_part(count + at).astype(BF16)

    loop(count, BLOCK, out_sib)
    att_copy = remote(sb1, rb1, csem, 2, sib)

    def out_mine(at):
        mid_s[pl.ds(at, BLOCK)] = sin_s[pl.ds(at, BLOCK)] + out_part(at) + out_bias

    loop(count, BLOCK, out_mine)
    att_copy.wait_recv()

    def second_norm(at):
        spot = pl.ds(at, 64)
        mid = mid_s[spot] + rb1[spot].astype(F32)
        mid_s[spot] = mid
        xhat, _ = norm_stats(mid)
        n2 = (xhat * ln2_gain + ln2_bias).astype(BF16)
        n2_s[spot] = n2

    loop(count, 64, second_norm)
    n2_copy = remote(n2_s.at[pl.ds(0, count)], n2_s.at[pl.ds(count, count)], csem, 3, sib)

    chunk_regions = []
    for i in range(units // BLOCK):
        chunk_regions.append([(i * BLOCK, BLOCK, 0, width), (units, width, i * BLOCK, BLOCK)])
    base_a = units + width
    chunk_regions.append([(base_a, 2 * quarter, 0, width)])
    chunk_regions.append([(base_a + 2 * quarter, 2 * quarter, 0, width)])
    steps = 1 + 2 * len(half_bits) + len(full_bits)

    class Region:
        used = 0

        def __init__(self, region):
            self.row, self.size, self.col, self.cols = region
            self.base = Region.used
            Region.used += steps
            self.stage = 0
            self.sent = []

        def view(self, ref, row, size):
            return ref.at[pl.ds(row, size), pl.ds(self.col, self.cols)]

        def go(self, src, dst, device):
            self.copy = remote(src, dst, gsem, self.base + self.stage, device)
            self.sent.append(self.copy)

        def send(self):
            self.go(self.view(oth, self.row, self.size), self.view(xr, self.row, self.size), across)
            self.at, self.now, self.trail = self.row, self.size, []

        def add(self, ref, row):
            dest = xr if self.stage == len(all_bits) else own
            step = min(self.now, 48 if self.now % 64 else 64)
            while self.now % step:
                step -= 16
            at = self.at

            def body(off):
                to = (pl.ds(pl.multiple_of(at + off, 16), step), pl.ds(self.col, self.cols))
                fr = (pl.ds(pl.multiple_of(row + off, 16), step), pl.ds(self.col, self.cols))
                dest[to] = (own[to].astype(F32) + ref[fr].astype(F32)).astype(BF16)

            loop(self.now, step, body)

        def start_next(self):
            stage = self.stage - 1
            if stage < len(half_bits):
                bit = half_bits[stage]
                half = self.now // 2
                keep = pl.multiple_of(self.at + sides[bit] * half, 16)
                give = pl.multiple_of(self.at + (1 - sides[bit]) * half, 16)
                self.trail.append((self.at, self.now, keep, half))
                landing = self.row >> (stage + 1)
                self.go(self.view(own, give, half), self.view(rr[stage], landing, half), mates[bit])
                self.next_add = (rr[stage], landing)
                self.at, self.now = keep, half
            elif stage < len(half_bits) + len(full_bits):
                i = stage - len(half_bits)
                landing = self.row >> len(half_bits)
                self.go(self.view(own, self.at, self.now), self.view(rx[i], landing, self.now), mates[full_bits[i]])
                self.next_add = (rx[i], landing)
            elif self.trail:
                before, size, keep, half = self.trail.pop()
                bit = half_bits[len(self.trail)]
                mine = self.view(xr, keep, half)
                self.go(mine, mine, mates[bit])
                self.next_add = None
            else:
                self.copy = None

        def advance(self):
            if self.copy is None:
                return
            self.copy.wait_recv()
            if self.stage == 0:
                self.add(xr, self.row)
            elif self.next_add is not None:
                if self.stage > len(half_bits):
                    self.copy.wait_send()
                    self.sent.pop()
                self.add(*self.next_add)
            self.stage += 1
            self.start_next()
            if self.copy is None:
                whole = self.view(xr, self.row, self.size)
                self.done = local(whole, self.view(grad_h, self.row, self.size))

    chunks = [[Region(r) for r in regions] for regions in chunk_regions]

    def send(i):
        for region in chunks[i]:
            region.send()

    def advance(i):
        for region in chunks[i]:
            region.advance()

    get_w1.wait()
    get_w2.wait()

    def chunk_rows(j, i, at):
        span = pl.ds(at, BLOCK)
        cols = slice(j * units + i * BLOCK, j * units + (i + 1) * BLOCK)
        mine = slice(i * BLOCK, (i + 1) * BLOCK)
        bias = (vec[8:9] if j == 0 else voth[0:1])[:, mine]
        h = dot(n2_s[span], w1_s[j, :, mine]) + bias
        a, slope = gelu_pair(h)
        a_s[span, cols] = a.astype(BF16)
        g = (dot_nt(cot_s[span], w2_s[j, mine]) * slope).astype(BF16)
        g_s[span, cols] = g

    def chunk_grads(j, i):
        cols = slice(j * units + i * BLOCK, j * units + (i + 1) * BLOCK)
        mine = slice(i * BLOCK, (i + 1) * BLOCK)
        to = oth if j == 1 else own
        to[i * BLOCK : (i + 1) * BLOCK] = dot_tn(a_s[:, cols], cot_s[...]).astype(BF16)
        g = g_s[:, cols]
        to[units : units + width, mine] = dot(n2t_s[...], g).astype(BF16)
        sm[8 + 8 * j : 9 + 8 * j, mine] = column_sum(g.astype(F32))

    def feed(j, i, first=False):
        if first:
            loop(count, BLOCK, lambda at: chunk_rows(j, i, at))
            n2_copy.wait_recv()
            cot_copy.wait_recv()
            for at in range(0, rows, BLOCK):
                n2t_s[:, at : at + BLOCK] = n2_s[at : at + BLOCK].T
            loop(count, BLOCK, lambda at: chunk_rows(j, i, count + at))
        else:
            loop(rows, BLOCK, lambda at: chunk_rows(j, i, at))
        chunk_grads(j, i)

    sm[...] = jnp.zeros_like(sm)
    parts = units // BLOCK
    feed(0, 0, first=True)
    by_y[2].wait_recv()
    by_y[3].wait_recv()
    feed(1, 0)
    send(0)
    for i in range(1, parts):
        feed(1, i)
        send(i)
        feed(0, i)
    advance(0)

    def back_two(at):
        span = pl.ds(at, BLOCK)
        return dot_nt(g_s[span, :units], w1_s[0]) + dot_nt(g_s[span, units:], w1_s[1])

    def mlp_part(at):
        span = pl.ds(at, BLOCK)
        return dot(a_s[span, :units], w2_s[0]) + dot(a_s[span, units:], w2_s[1])

    def back_two_sib(at):
        sb2[pl.ds(at, BLOCK)] = back_two(count + at).astype(BF16)

    def back_two_mine(at):
        gm_s[pl.ds(at, BLOCK)] = back_two(at)

    def mlp_sib(at):
        sb1[pl.ds(at, BLOCK)] = mlp_part(count + at).astype(BF16)

    loop(count, BLOCK, back_two_sib)
    gn2_copy = remote(sb2, rb2, csem, 4, sib)
    loop(count, BLOCK, back_two_mine)
    att_copy.wait_send()
    loop(count, BLOCK, mlp_sib)
    mlp_copy = remote(sb1, rb1, csem, 5, sib)
    gn2_copy.wait_recv()
    n2_copy.wait_send()

    def second_back(at):
        spot = pl.ds(at, 64)
        xhat, sigma = norm_stats(mid_s[spot])
        grad = gm_s[spot] + rb2[spot].astype(F32)
        cot = cot_s[spot].astype(F32)
        back = cot + norm_back(grad, ln2_gain, xhat, sigma)
        gm_s[spot] = back
        n2_s[spot] = back.astype(BF16)
        sm[2:3] += column_sum(back)
        sm[3:4] += column_sum(grad * xhat)
        sm[4:5] += column_sum(grad)
        sm[5:6] += column_sum(cot)

    loop(count, 64, second_back)
    dm_copy = remote(n2_s.at[pl.ds(0, count)], n2_s.at[pl.ds(count, count)], csem, 6, sib)

    def finish_out(at):
        span = pl.ds(at, BLOCK)
        mid_s[span] = mid_s[span] + mlp_part(at) + fc2_bias

    loop(count, BLOCK, finish_out)
    mlp_copy.wait_recv()

    def write_out(at):
        spot = pl.ds(at, 64)
        tok_s[spot] = (mid_s[spot] + rb1[spot].astype(F32)).astype(BF16)

    loop(count, 64, write_out)
    put_out = local(tok_s, out_h)
    dm_copy.wait_recv()

    def attend_back(j, service):
        dm = n2_s[...]
        base = j * quarter
        ot = ot_s[base : base + quarter]
        to = oth if j == 1 else own
        to[base_a : base_a + quarter] = dot(ot, dm).astype(BF16)
        grad_t = dot_nt(wo_s[base : base + quarter], dm).astype(BF16).astype(F32)
        scaled, inners = [], []
        for head in range(heads):
            span = slice(head * HEAD, head * HEAD + HEAD)
            r = r_s[j * heads + head : j * heads + head + 1]
            g = grad_t[span]
            inners.append(column_sum(g * ot[span].astype(F32)) * r)
            scaled.append((g * r).astype(BF16))
        gt = jnp.concatenate(scaled, axis=0)
        go_s[:, :quarter] = gt.T
        dq, dk, dv = [], [None, None], [None, None]
        zero = jnp.zeros((rows, 128), BF16)
        for head in range(heads):
            tile = head // 2
            vh = head_lanes(v_s.at[j], head, zero)
            qh = head_lanes(q_s.at[j], head, zero)
            gh = head_lanes(go_s, head, zero)
            gth = gt[128 * tile : min(128 * tile + 128, quarter)]
            vh = vh[:, : gth.shape[0]]
            e_h = e_s.at[j * heads + head]
            for at in range(0, rows, BLOCK):
                dp_t = dot(vh, gth[:, at : at + BLOCK])
                ds = (dp_t - inners[head][:, at : at + BLOCK]) * e_h[:, at : at + BLOCK].astype(F32)
                ds_s[:, at : at + BLOCK] = ds.astype(BF16)
            dvh = dot(e_h[...], gh)
            dkh = dot(ds_s[...], qh)
            dv[tile] = dvh if dv[tile] is None else dv[tile] + dvh
            dk[tile] = dkh if dk[tile] is None else dk[tile] + dkh
            dq.append(dot(kt_s[base + head * HEAD : base + head * HEAD + HEAD], ds_s[...]))
            service[head]()
        dqt = jnp.concatenate(dq, axis=0).astype(BF16)
        start = base_a + quarter
        n1 = n1_s[...]
        dest = 3 * BLOCK * j

        def lanes_of(total):
            return jnp.concatenate([total[0], total[1]], axis=1)[:, :quarter].astype(BF16)

        dvf = lanes_of(dv)
        dkf = lanes_of(dk)
        dqf = dqt.T
        for c, d in ((0, dqf), (1, dkf), (2, dvf)):
            g_s[:, dest + c * BLOCK : dest + c * BLOCK + quarter] = d
        sm[9 + 8 * j : 10 + 8 * j, :quarter] = column_sum(dqf.astype(F32))
        sm[10 + 8 * j : 11 + 8 * j, :quarter] = column_sum(dvf.astype(F32))
        to[start : start + quarter] = dot(dvf.T, n1).astype(BF16)
        if j == 1:
            send(parts)
        to[start + quarter : start + 2 * quarter] = dot(dkf.T, n1).astype(BF16)
        to[start + 2 * quarter : start + 3 * quarter] = dot(dqt, n1).astype(BF16)
        if j == 1:
            send(parts + 1)

    attend_back(1, [lambda: advance(0), lambda: advance(1), lambda: advance(0)])
    advance(1)
    advance(0)
    attend_back(0, [lambda: advance(2), lambda: (advance(1), advance(0)), lambda: (advance(2), advance(1))])

    def back_one(at):
        total = None
        for j in range(2):
            for c in range(3):
                d = g_s[pl.ds(at, BLOCK), (3 * j + c) * BLOCK : (3 * j + c) * BLOCK + quarter]
                term = dot_nt(d, wq_s[j, c])
                total = term if total is None else total + term
        return total

    gn2_copy.wait_send()

    def back_one_sib(at):
        sb2[pl.ds(at, BLOCK)] = back_one(count + at).astype(BF16)

    def back_one_mine(at):
        mid_s[pl.ds(at, BLOCK)] = back_one(at)

    loop(count, BLOCK, back_one_sib)
    gn1_copy = remote(sb2, rb2, csem, 7, sib)
    loop(count, BLOCK, back_one_mine)
    advance(0)
    advance(1)
    advance(2)
    gn1_copy.wait_recv()
    mlp_copy.wait_send()

    def first_back(at):
        spot = pl.ds(at, 64)
        xhat, sigma = norm_stats(sin_s[spot])
        grad = mid_s[spot] + rb2[spot].astype(F32)
        sb1[spot] = (gm_s[spot] + norm_back(grad, ln1_gain, xhat, sigma)).astype(BF16)
        sm[0:1] += column_sum(grad * xhat)
        sm[1:2] += column_sum(grad)

    loop(count, 64, first_back)
    put_in = local(sb1, ing_h)

    state = {}

    def small_start(i):
        if i == 0:
            state["c"] = remote(sm, smr.at[0], ssem, 0, sib)
        elif i == 1:
            state["c"] = remote(sm, smr.at[1], ssem, 1, across)
        else:
            state["c"] = remote(sm.at[pl.ds(0, 16)], smr.at[i, pl.ds(0, 16)], ssem, i, mates[all_bits[i - 2]])
        state["i"] = i

    def small_step():
        i = state["i"]
        state["c"].wait()
        if i == 0:
            sm[0:8] = sm[0:8] + smr[0, 0:8]
        elif i == 1:
            sm[0:8] = sm[0:8] + smr[1, 0:8]
            sm[8:16] = sm[8:16] + smr[1, 16:24]
        else:
            sm[0:16] = sm[0:16] + smr[i, 0:16]
        if i + 1 < 2 + len(all_bits):
            small_start(i + 1)
        else:
            small_o[...] = sm[0:16]

    small_start(0)
    advance(parts)
    advance(0)
    advance(1)
    small_step()
    advance(parts + 1)
    advance(2)
    small_left = 1 + len(all_bits)
    while True:
        busy = False
        for i in range(len(chunks)):
            if chunks[i][0].copy is not None:
                advance(i)
                busy = True
        if small_left:
            small_step()
            small_left -= 1
            busy = True
        if not busy:
            break

    for copy in [vec_copy, n1_copy, cot_copy, dm_copy, gn1_copy] + by_x + by_y:
        copy.wait_send()
    for regions in chunks:
        for region in regions:
            for copy in region.sent:
                copy.wait_send()
            region.done.wait()
    put_out.wait()
    put_in.wait()


def call_layer(dp_size, tokens, cotangent, ids, table, vec, wq, wo, w1, w2):
    count, width = tokens.shape
    rows = 2 * count
    quarter = wo.shape[0]
    units = w1.shape[1]
    heads = quarter // HEAD
    grad_rows = units + width + 4 * quarter
    bits = [b for b in range(20) if (1 << b) < dp_size]
    half_bits = bits[:3]
    shape = jax.ShapeDtypeStruct
    vm = pltpu.VMEM
    regions = 2 * (units // BLOCK) + 2
    steps = 1 + 2 * len(half_bits) + len(bits) - len(half_bits)
    scratch = (
        [vm((count, width), BF16), vm((rows, width), BF16)]
        + [vm((count, width), F32)] * 3
        + [vm((rows, width), BF16)] * 2
        + [vm((width, rows), BF16)]
        + [vm((2,) + wq.shape, BF16), vm((2 * quarter, width), BF16), vm((2,) + w1.shape, BF16), vm((2,) + w2.shape, BF16)]
        + [vm((2, rows, 256), BF16)] * 2
        + [vm((2 * quarter, rows), BF16)] * 2
        + [vm((8, rows), F32), vm((2 * heads, rows, rows), BF16)]
        + [vm((rows, 2 * units), BF16)] * 2
        + [vm((count, width), BF16)] * 4
        + [vm((grad_rows, width), BF16)] * 3
        + [vm((grad_rows >> (i + 1), width), BF16) for i in range(len(half_bits))]
        + [vm((grad_rows >> len(half_bits), width), BF16)] * (len(bits) - len(half_bits))
        + [vm((8, width), F32), vm((24, width), F32), vm((2 + len(bits), 24, width), F32)]
        + [pltpu.SemaphoreType.DMA((8 + regions,))]
        + [pltpu.SemaphoreType.DMA((2, n)) for n in (9, 8, regions * steps, 2 + len(bits))]
    )
    anywhere = pl.BlockSpec(memory_space=pl.ANY)
    inside = pl.BlockSpec(memory_space=pltpu.VMEM)
    return pl.pallas_call(
        functools.partial(layer, dp_size, half_bits),
        out_shape=[shape((count, width), BF16)] * 2 + [shape((grad_rows, width), BF16), shape((16, width), F32)],
        in_specs=[anywhere] * 2 + [inside] * 3 + [anywhere] * 4,
        out_specs=[anywhere] * 3 + [inside],
        scratch_shapes=scratch,
        compiler_params=pltpu.CompilerParams(vmem_limit_bytes=VMEM_LIMIT, collective_id=0, has_side_effects=True),
        name="layer",
    )(tokens, cotangent, ids, table, vec, wq, wo, w1, w2)


def per_device(
    tokens, segment_ids, ln1_gain, ln1_bias, qkv_weight, qv_bias, out_weight, out_bias,
    ln2_gain, ln2_bias, fc1_weight, fc1_bias, fc2_weight, fc2_bias, cotangent,
):
    width = tokens.shape[1]
    quarter = out_weight.shape[0]
    units = fc1_weight.shape[1]
    freq_count = width // 6
    frequency = 10000.0 ** (-jnp.arange(freq_count, dtype=F32) / freq_count)
    angles = jnp.arange(SIDE, dtype=F32)[:, None] * frequency[None, :]
    table = jnp.concatenate([jnp.sin(angles), jnp.cos(angles)], axis=1)
    pad = ((0, 0), (0, width - quarter))
    vec = jnp.concatenate(
        [
            jnp.stack([ln1_gain, ln1_bias, out_bias, ln2_gain, ln2_bias, fc2_bias]),
            jnp.zeros((2, width), F32),
            fc1_bias[None, :],
            jnp.pad(qv_bias, pad),
            jnp.zeros((5, width), F32),
        ]
    )
    output, input_grad, grads, small = call_layer(
        lax.axis_size("dp"), tokens, cotangent, segment_ids, table, vec, qkv_weight, out_weight, fc1_weight, fc2_weight
    )
    base = units + width
    g_out = grads[base : base + quarter]
    back = grads[base + quarter :].reshape(3, quarter, width)
    qkv_grad = jnp.stack([back[2], back[1], back[0]]).transpose(0, 2, 1)
    return (
        output,
        input_grad,
        small[0],
        small[1],
        qkv_grad.astype(F32),
        small[9:11, :quarter],
        g_out.astype(F32),
        small[2],
        small[3],
        small[4],
        grads[units:base].astype(F32),
        small[8],
        grads[:units].astype(F32),
        small[5],
    )


def solution(mesh):
    placed = (
        P(("dp", "tensor"), None),
        P("dp", None),
        P(),
        P(),
        P(None, None, "tensor"),
        P(None, "tensor"),
        P("tensor", None),
        P(),
        P(),
        P(),
        P(None, "tensor"),
        P("tensor"),
        P("tensor", None),
        P(),
        P(("dp", "tensor"), None),
    )
    return jax.shard_map(
        per_device,
        mesh=mesh,
        in_specs=placed,
        out_specs=(
            P(("dp", "tensor"), None),
            P(("dp", "tensor"), None),
            P(),
            P(),
            P(None, None, "tensor"),
            P(None, "tensor"),
            P("tensor", None),
            P(),
            P(),
            P(),
            P(None, "tensor"),
            P("tensor"),
            P("tensor", None),
            P(),
        ),
        check_vma=False,
    )
```

```python
import functools

import jax
import jax.numpy as jnp
from jax import lax
from jax.experimental import pallas as pl
from jax.experimental.pallas import tpu as pltpu
from jax.sharding import PartitionSpec as P

HEAD = 64
SIDE = 16
EPSILON = 1e-06
NEG_LARGE = -1e30
SCALE = HEAD ** (-0.5)
F32 = jnp.float32
BF16 = jnp.bfloat16
VMEM_LIMIT = 64 * 1024 * 1024 - 128 * 1024
MESH = pl.DeviceIdType.MESH
BLOCK = 256
ORDERS = ((1, 0, 2), (1, 0, 2), (1, 0, 2), (1, 0, 2), (0, 1, 2), (1, 0, 2), (0, 1, 2), (1, 0, 2), (0, 1, 2), (0, 1, 2))
PLAN = {
    "f01": (0,),
    "f02": (1, 0),
    "ln2": (0, 1, 2),
    "b10": (0, 1),
    "b11": (2, 3),
    "b12": (0, 1),
    "s1": (2, 4),
    "b00": (3, 0, 1, 2),
    "b01": (4, 5),
    "b02": (3, 2, 0, 1),
    "s0": (4, 6),
    "gn1": (3, 2),
    "gn1b": (5,),
    "tail": (
        4, 9, 6, 1, 3, 5, -1, 2, 8, 4, -1, 6, 9, 5, -1, 3, 6, 4, -1, 9, 7, 5, 8,
        -1, 6, 9, 3, 4, 9, 7, 5, 8, 6, 7, 9, 8, 7, 6, 8, 5, 7, 9, 8, 7, 8, 7,
    ),
}


def dot(a, b):
    return jnp.dot(a, b, preferred_element_type=F32)


def dot_nt(a, b):
    return lax.dot_general(a, b, (((1,), (1,)), ((), ())), preferred_element_type=F32)


def dot_tn(a, b):
    return lax.dot_general(a, b, (((0,), (0,)), ((), ())), preferred_element_type=F32)


def lane_half(rows, upper):
    lanes = lax.broadcasted_iota(jnp.int32, (rows, 128), 1)
    return lanes >= HEAD if upper else lanes < HEAD


def head_lanes(ref, head, filler):
    tile = ref[:, 128 * (head // 2) : 128 * (head // 2) + 128]
    return jnp.where(lane_half(tile.shape[0], head % 2 == 1), tile, filler)


def gelu_pair(h):
    size = jnp.abs(h)
    t = 1.0 / (1.0 + (0.3275911 * 0.7071067811865476) * size)
    bell = jnp.exp(-0.5 * h * h)
    poly = ((((1.061405429 * t - 1.453152027) * t + 1.421413741) * t - 0.284496736) * t + 0.254829592) * t
    tail = 0.5 * poly * bell
    cdf = jnp.where(h < 0, tail, 1.0 - tail)
    return h * cdf, cdf + h * bell * 0.3989422804014327


def norm_stats(v):
    centred = v - jnp.mean(v, axis=-1, keepdims=True)
    sigma = lax.rsqrt(jnp.mean(centred * centred, axis=-1, keepdims=True) + EPSILON)
    return centred * sigma, sigma


def norm_back(grad, gain, xhat, sigma):
    g = grad * gain
    return sigma * (g - jnp.mean(g, axis=-1, keepdims=True) - xhat * jnp.mean(g * xhat, axis=-1, keepdims=True))


def column_sum(v):
    return jnp.sum(v, axis=0, keepdims=True)


def loop(count, step, body):
    def run(i, carry):
        body(pl.multiple_of(i * step, step))
        return carry

    lax.fori_loop(0, count // step, run, 0)


def layer(
    dp_size, half_bits,
    tok_h, cot_h, ids, table, gain1, bias1, bias_o, gain2, bias2, bias_f, bias_u, bias_qv, wq_h, wo_h, w1_h, w2_h,
    out_h, ing_h, g2_h, g1_h, go_h, gq_h, small_o,
    tok_s, cot_s, sin_s, mid_s, gm_s, n1_s, n2_s, n2t_s, wq_s, wo_s, w1_s, w2_s,
    q_s, v_s, kt_s, ot_s, r_s, e_s, a_s, g_s, sb1, sb2, rb1, rb2,
    own, oth, xr, *rest,
):
    rest = list(rest)
    rr = [rest.pop(0) for _ in half_bits]
    full_bits = [b for b in range(20) if (1 << b) < dp_size and b not in half_bits]
    rx = [rest.pop(0) for _ in full_bits]
    uoth, voth, sm, smr, lsem, wsem, csem, gsem, ssem = rest

    count, width = tok_s.shape
    rows = 2 * count
    quarter = wo_h.shape[0]
    units = w1_h.shape[1]
    heads = quarter // HEAD
    place = lax.axis_index("tensor")
    dp = lax.axis_index("dp")
    chip = place // 2
    core = place % 2
    sib = {"tensor": chip * 2 + 1 - core}
    across = {"tensor": (1 - chip) * 2 + core}
    all_bits = list(half_bits) + full_bits
    sides = {b: (dp // (1 << b)) % 2 for b in all_bits}
    mates = {b: {"dp": dp + (1 - 2 * sides[b]) * (1 << b)} for b in all_bits}

    barrier = pltpu.get_barrier_semaphore()
    partners = [sib, across] + [mates[b] for b in all_bits]
    for partner in partners:
        pl.semaphore_signal(barrier, inc=1, device_id=partner, device_id_type=MESH)

    sq_s, sk_s, k_s = a_s.at[:, 0:128], a_s.at[:, 128:256], a_s.at[:, 256:512]
    ds_s, go_s = a_s.at[:, 0:rows], a_s.at[:, rows : rows + 256]
    local_used = [0]

    def local(src, dst):
        copy = pltpu.make_async_copy(src, dst, lsem.at[local_used[0]])
        local_used[0] += 1
        copy.start()
        return copy

    def remote(src, dst, sems, index, device):
        copy = pltpu.make_async_remote_copy(
            src_ref=src, dst_ref=dst, send_sem=sems.at[0, index], recv_sem=sems.at[1, index], device_id=device, device_id_type=MESH
        )
        copy.start()
        return copy

    get_tok = local(tok_h, tok_s)
    get_cot = local(cot_h, cot_s.at[pl.ds(0, count)])
    get_wq = local(wq_h, wq_s.at[0])
    get_wo = local(wo_h, wo_s.at[pl.ds(0, quarter)])
    get_w1 = local(w1_h, w1_s.at[0])
    get_w2 = local(w2_h, w2_s.at[0])

    part = sides[0]

    def half_of(extent):
        return pl.ds(pl.multiple_of(part * (extent // 2), 32), extent // 2)

    def columns(i):
        return pl.ds(i * BLOCK, BLOCK)

    wo_other = pl.ds(pl.multiple_of(quarter + part * (quarter // 2), 32), quarter // 2)
    pieces = [(wq_h.at[c, half_of(quarter)], wq_s.at[1, c, half_of(quarter)]) for c in range(3)]
    pieces.append((wo_h.at[half_of(quarter)], wo_s.at[wo_other]))
    for i in range(units // BLOCK):
        span = pl.ds(pl.multiple_of(i * BLOCK + part * (BLOCK // 2), 32), BLOCK // 2)
        pieces.append((w1_h.at[half_of(width), columns(i)], w1_s.at[1, half_of(width), columns(i)]))
        pieces.append((w2_h.at[span], w2_s.at[1, span]))

    pl.semaphore_wait(barrier, len(partners))
    unit_copy = remote(bias_u, uoth, wsem, 2 * len(pieces), across)
    head_copy = remote(bias_qv, voth, wsem, 2 * len(pieces) + 1, across)
    by_x = [remote(src, dst, wsem, i, across) for i, (src, dst) in enumerate(pieces)]
    by_y = [None] * len(pieces)

    def forward_weight(*which):
        for i in which:
            by_x[i].wait_recv()
            by_y[i] = remote(pieces[i][1], pieces[i][1], wsem, len(pieces) + i, mates[0])

    def have_weight(*which):
        for i in which:
            by_y[i].wait_recv()

    ln1_gain, ln1_bias, out_bias, ln2_gain, ln2_bias, fc2_bias = (
        ref[...].reshape(1, width) for ref in (gain1, bias1, bias_o, gain2, bias2, bias_f)
    )
    get_tok.wait()

    def first_norm(at):
        plane = core * (count // (SIDE * SIDE)) + at // (SIDE * SIDE)
        line = (at // SIDE) % SIDE
        shape = (SIDE, width // 3)
        for k in range(4):
            spot = jnp.concatenate(
                [jnp.broadcast_to(table[pl.ds(plane, 1)], shape), jnp.broadcast_to(table[pl.ds(line + k, 1)], shape), table[...]], axis=1
            )
            span = pl.ds(pl.multiple_of(at + k * SIDE, SIDE), SIDE)
            stream = tok_s[span].astype(F32) + spot
            sin_s[span] = stream
            xhat, _ = norm_stats(stream)
            n1_s[span] = (xhat * ln1_gain + ln1_bias).astype(BF16)

    loop(count, 4 * SIDE, first_norm)
    n1_copy = remote(n1_s.at[pl.ds(0, count)], n1_s.at[pl.ds(count, count)], csem, 0, sib)
    get_cot.wait()
    cot_copy = remote(cot_s.at[pl.ds(0, count)], cot_s.at[pl.ds(count, count)], csem, 1, sib)

    for at in range(2):
        side = core if at == 0 else 1 - core
        doc = ids[pl.ds(chip, 1), pl.ds(pl.multiple_of(side * count, 128), count)]
        slot = lax.broadcasted_iota(jnp.int32, (128, count), 0) % HEAD
        same = slot == doc
        mark = jnp.where((slot < 4) & jnp.logical_not(same), 1.0, 0.0)
        block = jnp.where(same, NEG_LARGE, 0.0)
        sq_s[at * count : (at + 1) * count] = mark.T.astype(BF16)
        sk_s[at * count : (at + 1) * count] = block.T.astype(BF16)

    def project(j, at):
        n = n1_s[pl.ds(at, BLOCK)]
        biases = bias_qv if j == 0 else voth
        q = (dot_nt(n, wq_s[j, 0]) + biases[0:1]).astype(BF16) * SCALE
        k = dot_nt(n, wq_s[j, 1]).astype(BF16)
        v = (dot_nt(n, wq_s[j, 2]) + biases[1:2]).astype(BF16)
        q_s[j, pl.ds(at, BLOCK), :quarter] = q
        k_s[pl.ds(at, BLOCK), :quarter] = k
        v_s[j, pl.ds(at, BLOCK), :quarter] = v
        kt_s[j * quarter : (j + 1) * quarter, pl.ds(at, BLOCK)] = k.T * SCALE

    def attend(j, service):
        vt = v_s[j, :, :quarter].T
        for head in range(heads):
            qh = head_lanes(q_s.at[j], head, sq_s[...])
            kh = head_lanes(k_s, head, sk_s[...])
            span = slice(head * HEAD, head * HEAD + HEAD)
            to = slice(j * quarter + head * HEAD, j * quarter + head * HEAD + HEAD)
            for at in range(0, rows, BLOCK):
                s = dot_nt(kh, qh[at : at + BLOCK])
                m = jnp.max(s, axis=0, keepdims=True)
                e = jnp.exp(s - m)
                r = 1.0 / column_sum(e)
                low = e.astype(BF16)
                e_s[j * heads + head, :, at : at + BLOCK] = low
                ot_s[to, at : at + BLOCK] = (dot(vt[span], low) * r).astype(BF16)
                r_s[j * heads + head : j * heads + head + 1, at : at + BLOCK] = r
            service[head]()

    get_wq.wait()
    loop(count, BLOCK, lambda at: project(0, at))
    n1_copy.wait_recv()
    loop(count, BLOCK, lambda at: project(0, count + at))
    nothing = lambda: None
    forward_weight(0, 1)
    attend(0, [lambda: forward_weight(2), lambda: forward_weight(3), nothing])
    head_copy.wait_recv()
    have_weight(0, 1, 2)
    loop(rows, BLOCK, lambda at: project(1, at))
    attend(1, [lambda: forward_weight(4), lambda: forward_weight(5), lambda: forward_weight(6)])

    get_wo.wait()
    have_weight(3)

    def out_part(at):
        return dot_tn(ot_s[:, pl.ds(at, BLOCK)], wo_s[...])

    def out_sib(at):
        sb1[pl.ds(at, BLOCK)] = out_part(count + at).astype(BF16)

    loop(count, BLOCK, out_sib)
    att_copy = remote(sb1, rb1, csem, 2, sib)

    def out_mine(at):
        mid_s[pl.ds(at, BLOCK)] = sin_s[pl.ds(at, BLOCK)] + out_part(at) + out_bias

    loop(count, BLOCK, out_mine)
    att_copy.wait_recv()

    def second_norm(at):
        spot = pl.ds(at, 64)
        mid = mid_s[spot] + rb1[spot].astype(F32)
        mid_s[spot] = mid
        xhat, _ = norm_stats(mid)
        n2 = (xhat * ln2_gain + ln2_bias).astype(BF16)
        n2_s[spot] = n2

    loop(count, 64, second_norm)
    n2_copy = remote(n2_s.at[pl.ds(0, count)], n2_s.at[pl.ds(count, count)], csem, 3, sib)

    base_a = units + width
    parts = units // BLOCK
    steps = 1 + 2 * len(half_bits) + len(full_bits)
    last = len(half_bits) - 1

    class Region:
        def __init__(self, index, row, size, col, cols, order):
            self.row, self.size, self.col, self.cols = row, size, col, cols
            self.base = index * steps
            self.order = [half_bits[k] for k in order if k < len(half_bits)]
            self.stage, self.copy, self.sent, self.trail = 0, None, [], []

        def window(self, row, size, col, cols):
            return pl.ds(row, size), pl.ds(col, cols)

        def go(self, src, src_at, dst, dst_at, device):
            self.copy = remote(src.at[self.window(*src_at)], dst.at[self.window(*dst_at)], gsem, self.base + self.stage, device)
            self.sent.append(self.copy)

        def send(self):
            self.now = (self.row, self.size, self.col, self.cols)
            self.go(oth, self.now, xr, self.now, across)

        def landing(self, stage):
            row, size, col, cols = self.row >> (stage + 1), self.size, self.col, self.cols
            for _ in range(stage + 1):
                if (size // 2) % 16 == 0:
                    size //= 2
                else:
                    cols //= 2
            if cols != self.cols:
                slot = (self.row - base_a) // quarter
                row, col = (base_a >> (stage + 1)) + (slot // 2) * size, (slot % 2) * cols
            return row, size, col, cols

        def add(self, ref, place):
            dest = xr if self.stage == len(all_bits) else own
            row, size, col, cols = self.now
            step = 64 if size % 64 == 0 else 48 if size % 48 == 0 else 32

            def body(off):
                to = (pl.ds(pl.multiple_of(row + off, 16), step), pl.ds(col, cols))
                fr = (pl.ds(pl.multiple_of(place[0] + off, 16), step), pl.ds(place[2], cols))
                dest[to] = (own[to].astype(F32) + ref[fr].astype(F32)).astype(BF16)

            loop(size, step, body)

        def start_next(self):
            stage = self.stage - 1
            if stage < len(half_bits):
                bit = self.order[stage]
                row, size, col, cols = self.now
                if (size // 2) % 16 == 0:
                    halves = [(pl.multiple_of(row + side * (size // 2), 16), size // 2, col, cols) for side in (sides[bit], 1 - sides[bit])]
                else:
                    halves = [(row, size, pl.multiple_of(col + side * (cols // 2), 128), cols // 2) for side in (sides[bit], 1 - sides[bit])]
                keep, give = halves
                place = self.landing(stage)
                self.go(own, give, rr[stage], place, mates[bit])
                self.next_add = (rr[stage], place)
                self.trail.append((bit, keep))
                self.now = keep
            elif stage < len(all_bits):
                i = stage - len(half_bits)
                place = self.landing(last)
                self.go(own, self.now, rx[i], place, mates[full_bits[i]])
                self.next_add = (rx[i], place)
            elif self.trail:
                bit, keep = self.trail.pop()
                self.go(xr, keep, xr, keep, mates[bit])
                self.next_add = None
            else:
                self.copy = None

        def advance(self):
            if self.copy is None:
                return
            self.copy.wait_recv()
            if self.stage == 0:
                self.add(xr, self.now)
            elif self.next_add is not None:
                if self.stage > len(half_bits):
                    self.copy.wait_send()
                    self.sent.pop()
                self.add(*self.next_add)
            self.stage += 1
            self.start_next()
            if self.copy is None:
                row, size, col, cols = self.row, self.size, self.col, self.cols
                if row < units:
                    to = g2_h.at[pl.ds(row, size)]
                elif row < base_a:
                    to = g1_h.at[:, pl.ds(col, cols)]
                elif row == base_a:
                    to = go_h
                else:
                    to = gq_h.at[(row - base_a) // quarter - 1]
                self.done = local(xr.at[self.window(row, size, col, cols)], to)

    chunks = []
    for i in range(parts):
        chunks.append(Region(2 * i, i * BLOCK, BLOCK, 0, width, ORDERS[2 * i]))
        chunks.append(Region(2 * i + 1, units, width, i * BLOCK, BLOCK, ORDERS[2 * i + 1]))
    for i in range(4):
        chunks.append(Region(2 * parts + i, base_a + i * quarter, quarter, 0, width, ORDERS[2 * parts + i]))
    first_att = 2 * parts

    def send(i):
        chunks[i].send()

    def hook(name):
        for i in PLAN.get(name, ()):
            chunks[i].advance()

    get_w1.wait()
    get_w2.wait()

    def chunk_rows(j, i, at):
        span = pl.ds(at, BLOCK)
        cols = slice(j * units + i * BLOCK, j * units + (i + 1) * BLOCK)
        mine = slice(i * BLOCK, (i + 1) * BLOCK)
        bias = (bias_u if j == 0 else uoth)[mine].reshape(1, BLOCK)
        h = dot(n2_s[span], w1_s[j, :, mine]) + bias
        a, slope = gelu_pair(h)
        a_s[span, cols] = a.astype(BF16)
        g = (dot_nt(cot_s[span], w2_s[j, mine]) * slope).astype(BF16)
        g_s[span, cols] = g

    def chunk_grads(j, i):
        cols = slice(j * units + i * BLOCK, j * units + (i + 1) * BLOCK)
        mine = slice(i * BLOCK, (i + 1) * BLOCK)
        to = oth if j == 1 else own
        to[i * BLOCK : (i + 1) * BLOCK] = dot_tn(a_s[:, cols], cot_s[...]).astype(BF16)
        if j == 1:
            send(2 * i)
        g = g_s[:, cols]
        to[units : units + width, mine] = dot(n2t_s[...], g).astype(BF16)
        if j == 1:
            send(2 * i + 1)
        sm[8 + 8 * j : 9 + 8 * j, mine] = column_sum(g.astype(F32))
        hook(f"f{j}{i}")

    def feed(j, i, first=False):
        if first:
            for at in range(0, count, BLOCK):
                chunk_rows(j, i, at)
            n2_copy.wait_recv()
            cot_copy.wait_recv()
            for at in range(0, rows, BLOCK):
                n2t_s[:, at : at + BLOCK] = n2_s[at : at + BLOCK].T
            for at in range(count, rows, BLOCK):
                chunk_rows(j, i, at)
        else:
            for at in range(0, rows, BLOCK):
                chunk_rows(j, i, at)
        chunk_grads(j, i)

    sm[...] = jnp.zeros_like(sm)
    unit_copy.wait_recv()
    have_weight(4, 5)
    feed(1, 0, first=True)
    forward_weight(7)
    feed(0, 0)
    have_weight(6, 7)
    forward_weight(8)
    feed(1, 1)
    forward_weight(9)
    feed(0, 1)
    for i in range(2, parts):
        have_weight(4 + 2 * i, 5 + 2 * i)
        feed(1, i)
        feed(0, i)

    def back_two(at):
        span = pl.ds(at, BLOCK)
        return dot_nt(g_s[span, :units], w1_s[0]) + dot_nt(g_s[span, units:], w1_s[1])

    def mlp_part(at):
        span = pl.ds(at, BLOCK)
        return dot(a_s[span, :units], w2_s[0]) + dot(a_s[span, units:], w2_s[1])

    def back_two_sib(at):
        sb2[pl.ds(at, BLOCK)] = back_two(count + at).astype(BF16)

    def back_two_mine(at):
        gm_s[pl.ds(at, BLOCK)] = back_two(at)

    def mlp_sib(at):
        sb1[pl.ds(at, BLOCK)] = mlp_part(count + at).astype(BF16)

    loop(count, BLOCK, back_two_sib)
    gn2_copy = remote(sb2, rb2, csem, 4, sib)
    loop(count, BLOCK, back_two_mine)
    hook("gn2")
    att_copy.wait_send()
    loop(count, BLOCK, mlp_sib)
    mlp_copy = remote(sb1, rb1, csem, 5, sib)
    hook("gn2b")
    gn2_copy.wait_recv()
    n2_copy.wait_send()

    def second_back(at):
        spot = pl.ds(at, 64)
        xhat, sigma = norm_stats(mid_s[spot])
        grad = gm_s[spot] + rb2[spot].astype(F32)
        cot = cot_s[spot].astype(F32)
        back = cot + norm_back(grad, ln2_gain, xhat, sigma)
        gm_s[spot] = back
        n2_s[spot] = back.astype(BF16)
        sm[2:3] += column_sum(back)
        sm[3:4] += column_sum(grad * xhat)
        sm[4:5] += column_sum(grad)
        sm[5:6] += column_sum(cot)

    loop(count, 64, second_back)
    dm_copy = remote(n2_s.at[pl.ds(0, count)], n2_s.at[pl.ds(count, count)], csem, 6, sib)

    hook("ln2")

    def finish_out(at):
        span = pl.ds(at, BLOCK)
        mid_s[span] = mid_s[span] + mlp_part(at) + fc2_bias

    loop(count, BLOCK, finish_out)
    mlp_copy.wait_recv()

    def write_out(at):
        spot = pl.ds(at, 64)
        tok_s[spot] = (mid_s[spot] + rb1[spot].astype(F32)).astype(BF16)

    loop(count, 64, write_out)
    put_out = local(tok_s, out_h)
    hook("fin")
    dm_copy.wait_recv()

    def attend_back(j):
        dm = n2_s[...]
        base = j * quarter
        ot = ot_s[base : base + quarter]
        to = oth if j == 1 else own
        to[base_a : base_a + quarter] = dot(ot, dm).astype(BF16)
        if j == 1:
            send(first_att)
        grad_t = dot_nt(wo_s[base : base + quarter], dm).astype(BF16).astype(F32)
        scaled, inners = [], []
        for head in range(heads):
            span = slice(head * HEAD, head * HEAD + HEAD)
            r = r_s[j * heads + head : j * heads + head + 1]
            g = grad_t[span]
            inners.append(column_sum(g * ot[span].astype(F32)) * r)
            scaled.append((g * r).astype(BF16))
        gt = jnp.concatenate(scaled, axis=0)
        go_s[:, :quarter] = gt.T
        dq, dk, dv = [], [None, None], [None, None]
        zero = jnp.zeros((rows, 128), BF16)
        for head in range(heads):
            tile = head // 2
            vh = head_lanes(v_s.at[j], head, zero)
            qh = head_lanes(q_s.at[j], head, zero)
            gh = head_lanes(go_s, head, zero)
            gth = gt[128 * tile : min(128 * tile + 128, quarter)]
            vh = vh[:, : gth.shape[0]]
            e_h = e_s.at[j * heads + head]
            for at in range(0, rows, BLOCK):
                dp_t = dot(vh, gth[:, at : at + BLOCK])
                ds = (dp_t - inners[head][:, at : at + BLOCK]) * e_h[:, at : at + BLOCK].astype(F32)
                ds_s[:, at : at + BLOCK] = ds.astype(BF16)
            dvh = dot(e_h[...], gh)
            dkh = dot(ds_s[...], qh)
            dv[tile] = dvh if dv[tile] is None else dv[tile] + dvh
            dk[tile] = dkh if dk[tile] is None else dk[tile] + dkh
            dq.append(dot(kt_s[base + head * HEAD : base + head * HEAD + HEAD], ds_s[...]))
            hook(f"b{j}{head}")
        dqt = jnp.concatenate(dq, axis=0).astype(BF16)
        start = base_a + quarter
        n1 = n1_s[...]
        dest = 3 * BLOCK * j

        def lanes_of(total):
            return jnp.concatenate([total[0], total[1]], axis=1)[:, :quarter].astype(BF16)

        dvf = lanes_of(dv)
        dkf = lanes_of(dk)
        dqf = dqt.T
        for c, d in ((0, dqf), (1, dkf), (2, dvf)):
            g_s[:, dest + c * BLOCK : dest + c * BLOCK + quarter] = d
        sm[9 + 8 * j : 10 + 8 * j, :quarter] = column_sum(dqf.astype(F32))
        sm[10 + 8 * j : 11 + 8 * j, :quarter] = column_sum(dvf.astype(F32))
        for c, d in ((2, dvf.T), (1, dkf.T), (0, dqt)):
            to[start + c * quarter : start + (c + 1) * quarter] = dot(d, n1).astype(BF16)
            if j == 1:
                send(first_att + 1 + c)
        hook(f"s{j}")

    attend_back(1)
    attend_back(0)

    def back_one(at):
        total = None
        for j in range(2):
            for c in range(3):
                d = g_s[pl.ds(at, BLOCK), (3 * j + c) * BLOCK : (3 * j + c) * BLOCK + quarter]
                term = dot(d, wq_s[j, c])
                total = term if total is None else total + term
        return total

    gn2_copy.wait_send()

    def back_one_sib(at):
        sb2[pl.ds(at, BLOCK)] = back_one(count + at).astype(BF16)

    def back_one_mine(at):
        mid_s[pl.ds(at, BLOCK)] = back_one(at)

    loop(count, BLOCK, back_one_sib)
    gn1_copy = remote(sb2, rb2, csem, 7, sib)
    hook("gn1")
    loop(count, BLOCK, back_one_mine)
    hook("gn1b")
    gn1_copy.wait_recv()
    mlp_copy.wait_send()

    def first_back(at):
        spot = pl.ds(at, 64)
        xhat, sigma = norm_stats(sin_s[spot])
        grad = mid_s[spot] + rb2[spot].astype(F32)
        sb1[spot] = (gm_s[spot] + norm_back(grad, ln1_gain, xhat, sigma)).astype(BF16)
        sm[0:1] += column_sum(grad * xhat)
        sm[1:2] += column_sum(grad)

    loop(count, 64, first_back)
    put_in = local(sb1, ing_h)

    state = {}

    def small_start(i):
        if i == 0:
            state["c"] = remote(sm, smr.at[0], ssem, 0, sib)
        elif i == 1:
            state["c"] = remote(sm, smr.at[1], ssem, 1, across)
        else:
            state["c"] = remote(sm.at[pl.ds(0, 16)], smr.at[i, pl.ds(0, 16)], ssem, i, mates[all_bits[i - 2]])
        state["i"] = i

    def small_step():
        i = state["i"]
        state["c"].wait()
        if i == 0:
            sm[0:8] = sm[0:8] + smr[0, 0:8]
        elif i == 1:
            sm[0:8] = sm[0:8] + smr[1, 0:8]
            sm[8:16] = sm[8:16] + smr[1, 16:24]
        else:
            sm[0:16] = sm[0:16] + smr[i, 0:16]
        if i + 1 < 2 + len(all_bits):
            small_start(i + 1)
        else:
            small_o[...] = sm[0:16]

    small_start(0)
    small_left = 2 + len(all_bits)
    for i in PLAN["tail"]:
        if i >= 0:
            chunks[i].advance()
        elif small_left:
            small_step()
            small_left -= 1
    while True:
        busy = False
        for chunk in chunks:
            if chunk.copy is not None:
                chunk.advance()
                busy = True
        if small_left:
            small_step()
            small_left -= 1
            busy = True
        if not busy:
            break

    for copy in [unit_copy, head_copy, n1_copy, cot_copy, dm_copy, gn1_copy] + by_x + by_y:
        copy.wait_send()
    for chunk in chunks:
        for copy in chunk.sent:
            copy.wait_send()
        chunk.done.wait()
    put_out.wait()
    put_in.wait()


def call_layer(dp_size, tokens, cotangent, ids, table, vectors, wq, wo, w1, w2):
    count, width = tokens.shape
    rows = 2 * count
    quarter = wo.shape[0]
    units = w1.shape[1]
    heads = quarter // HEAD
    grad_rows = units + width + 4 * quarter
    bits = [b for b in range(20) if (1 << b) < dp_size]
    half_bits = bits[:3]
    shape = jax.ShapeDtypeStruct
    vm = pltpu.VMEM
    regions = 2 * (units // BLOCK) + 4
    steps = 1 + 2 * len(half_bits) + len(bits) - len(half_bits)
    fetched = 4 + 2 * (units // BLOCK)
    scratch = (
        [vm((count, width), BF16), vm((rows, width), BF16)]
        + [vm((count, width), F32)] * 3
        + [vm((rows, width), BF16)] * 2
        + [vm((width, rows), BF16)]
        + [vm((2,) + wq.shape, BF16), vm((2 * quarter, width), BF16), vm((2,) + w1.shape, BF16), vm((2,) + w2.shape, BF16)]
        + [vm((2, rows, 256), BF16)] * 2
        + [vm((2 * quarter, rows), BF16)] * 2
        + [vm((8, rows), F32), vm((2 * heads, rows, rows), BF16)]
        + [vm((rows, 2 * units), BF16)] * 2
        + [vm((count, width), BF16)] * 4
        + [vm((grad_rows, width), BF16)] * 3
        + [vm((grad_rows >> (i + 1), width), BF16) for i in range(len(half_bits))]
        + [vm((grad_rows >> len(half_bits), width), BF16)] * (len(bits) - len(half_bits))
        + [vm((units,), F32), vm((2, quarter), F32), vm((24, width), F32), vm((2 + len(bits), 24, width), F32)]
        + [pltpu.SemaphoreType.DMA((8 + regions,))]
        + [pltpu.SemaphoreType.DMA((2, n)) for n in (2 * fetched + 2, 8, regions * steps, 2 + len(bits))]
    )
    anywhere = pl.BlockSpec(memory_space=pl.ANY)
    inside = pl.BlockSpec(memory_space=pltpu.VMEM)
    return pl.pallas_call(
        functools.partial(layer, dp_size, half_bits),
        out_shape=[shape((count, width), BF16)] * 2
        + [shape(w2.shape, BF16), shape(w1.shape, BF16), shape(wo.shape, BF16), shape(wq.shape, BF16), shape((16, width), F32)],
        in_specs=[anywhere] * 2 + [inside] * (2 + len(vectors)) + [anywhere] * 4,
        out_specs=[anywhere] * 6 + [inside],
        scratch_shapes=scratch,
        compiler_params=pltpu.CompilerParams(vmem_limit_bytes=VMEM_LIMIT, collective_id=0, has_side_effects=True),
        name="layer",
    )(tokens, cotangent, ids, table, *vectors, wq, wo, w1, w2)


def finish(out, ing, g2, g1, go, gq, small, out_o, ing_o, g2_o, g1_o, go_o, gq_o, a0, a1, a2, a3, a4, a5, units_o, heads_o):
    for src, dst in ((out, out_o), (ing, ing_o), (g2, g2_o), (g1, g1_o), (go, go_o), (gq, gq_o)):
        dst[...] = src[...].astype(dst.dtype)

    @pl.when(pl.program_id(0) == 0)
    def _():
        for i, ref in enumerate((a0, a1, a2, a3, a4, a5)):
            ref[...] = small[i]
        units_o[...] = small[8, : units_o.shape[0]]
        heads_o[...] = small[9:11, : heads_o.shape[1]]


def call_finish(arrays, small, units, quarter):
    steps = 4
    width = small.shape[1]
    shape = jax.ShapeDtypeStruct

    def rows_of(a):
        axis = a.ndim - 2
        block = a.shape[:axis] + (a.shape[axis] // steps,) + a.shape[axis + 1 :]
        return pl.BlockSpec(block, lambda i, axis=axis, rank=a.ndim: tuple(i if k == axis else 0 for k in range(rank)))

    def whole(extent):
        return pl.BlockSpec(extent, lambda i, rank=len(extent): (0,) * rank)

    extents = [(width,)] * 6 + [(units,), (2, quarter)]
    kinds = [BF16, BF16, F32, F32, F32, F32]
    return pl.pallas_call(
        finish,
        grid=(steps,),
        in_specs=[rows_of(a) for a in arrays] + [whole(small.shape)],
        out_specs=[rows_of(a) for a in arrays] + [whole(e) for e in extents],
        out_shape=[shape(a.shape, k) for a, k in zip(arrays, kinds)] + [shape(e, F32) for e in extents],
        compiler_params=pltpu.CompilerParams(vmem_limit_bytes=VMEM_LIMIT),
        name="finish",
    )(*arrays, small)


def per_device(
    tokens, segment_ids, ln1_gain, ln1_bias, qkv_weight, qv_bias, out_weight, out_bias,
    ln2_gain, ln2_bias, fc1_weight, fc1_bias, fc2_weight, fc2_bias, cotangent,
):
    width = tokens.shape[1]
    freq_count = width // 6
    frequency = 10000.0 ** (-jnp.arange(freq_count, dtype=F32) / freq_count)
    angles = jnp.arange(SIDE, dtype=F32)[:, None] * frequency[None, :]
    table = jnp.concatenate([jnp.sin(angles), jnp.cos(angles)], axis=1)
    vectors = (ln1_gain, ln1_bias, out_bias, ln2_gain, ln2_bias, fc2_bias, fc1_bias, qv_bias)
    *arrays, small = call_layer(
        lax.axis_size("dp"), tokens, cotangent, segment_ids, table, vectors, qkv_weight.transpose(0, 2, 1), out_weight, fc1_weight, fc2_weight
    )
    out, ing, g2, g1, go, gq, a0, a1, a2, a3, a4, a5, g_units, g_heads = call_finish(arrays, small, fc1_weight.shape[1], out_weight.shape[0])
    return (out, ing, a0, a1, gq.transpose(0, 2, 1), g_heads, go, a2, a3, a4, g1, g_units, g2, a5)


def solution(mesh):
    placed = (
        P(("dp", "tensor"), None),
        P("dp", None),
        P(),
        P(),
        P(None, None, "tensor"),
        P(None, "tensor"),
        P("tensor", None),
        P(),
        P(),
        P(),
        P(None, "tensor"),
        P("tensor"),
        P("tensor", None),
        P(),
        P(("dp", "tensor"), None),
    )
    return jax.shard_map(
        per_device,
        mesh=mesh,
        in_specs=placed,
        out_specs=(
            P(("dp", "tensor"), None),
            P(("dp", "tensor"), None),
            P(),
            P(),
            P(None, None, "tensor"),
            P(None, "tensor"),
            P("tensor", None),
            P(),
            P(),
            P(),
            P(None, "tensor"),
            P("tensor"),
            P("tensor", None),
            P(),
        ),
        check_vma=False,
    )
```

```python
import functools

import jax
import jax.numpy as jnp
from jax import lax
from jax.experimental import pallas as pl
from jax.experimental.pallas import tpu as pltpu
from jax.sharding import PartitionSpec as P

HEAD = 64
SIDE = 16
EPSILON = 1e-06
NEG_LARGE = -1e30
SCALE = HEAD ** (-0.5)
F32 = jnp.float32
BF16 = jnp.bfloat16
VMEM_LIMIT = 64 * 1024 * 1024 - 128 * 1024
MESH = pl.DeviceIdType.MESH
BLOCK = 256
ORDERS = ((1, 0, 2), (1, 0, 2), (1, 0, 2), (1, 0, 2), (0, 1, 2), (1, 0, 2), (0, 1, 2), (1, 0, 2), (0, 1, 2), (0, 1, 2))
PLAN = {
    "f01": (0,),
    "f02": (1, 0),
    "ln2": (0, 1, 2),
    "b10": (0, 1),
    "b11": (2, 3),
    "b12": (0, 1),
    "s1": (2, 4),
    "b00": (3, 0, 1, 2),
    "b01": (4, 5),
    "b02": (3, 2, 0, 1),
    "s0": (4, 6),
    "gn1": (3, 2),
    "gn1b": (5,),
    "tail": (
        4, 9, 6, 1, 3, 5, -1, 2, 8, 4, -1, 6, 9, 5, -1, 3, 6, 4, -1, 9, 7, 5, 8,
        -1, 6, 9, 3, 4, 9, 7, 5, 8, 6, 7, 9, 8, 7, 6, 8, 5, 7, 9, 8, 7, 8, 7,
    ),
}


def dot(a, b):
    return jnp.dot(a, b, preferred_element_type=F32)


def dot_nt(a, b):
    return lax.dot_general(a, b, (((1,), (1,)), ((), ())), preferred_element_type=F32)


def dot_tn(a, b):
    return lax.dot_general(a, b, (((0,), (0,)), ((), ())), preferred_element_type=F32)


def lane_half(rows, upper):
    lanes = lax.broadcasted_iota(jnp.int32, (rows, 128), 1)
    return lanes >= HEAD if upper else lanes < HEAD


def head_lanes(ref, head, filler):
    tile = ref[:, 128 * (head // 2) : 128 * (head // 2) + 128]
    return jnp.where(lane_half(tile.shape[0], head % 2 == 1), tile, filler)


def gelu_pair(h):
    size = jnp.abs(h)
    t = 1.0 / (1.0 + (0.3275911 * 0.7071067811865476) * size)
    bell = jnp.exp(-0.5 * h * h)
    poly = ((((1.061405429 * t - 1.453152027) * t + 1.421413741) * t - 0.284496736) * t + 0.254829592) * t
    tail = 0.5 * poly * bell
    cdf = jnp.where(h < 0, tail, 1.0 - tail)
    return h * cdf, cdf + h * bell * 0.3989422804014327


def norm_stats(v):
    centred = v - jnp.mean(v, axis=-1, keepdims=True)
    sigma = lax.rsqrt(jnp.mean(centred * centred, axis=-1, keepdims=True) + EPSILON)
    return centred * sigma, sigma


def norm_back(grad, gain, xhat, sigma):
    g = grad * gain
    return sigma * (g - jnp.mean(g, axis=-1, keepdims=True) - xhat * jnp.mean(g * xhat, axis=-1, keepdims=True))


def column_sum(v):
    return jnp.sum(v, axis=0, keepdims=True)


def loop(count, step, body):
    def run(i, carry):
        body(pl.multiple_of(i * step, step))
        return carry

    lax.fori_loop(0, count // step, run, 0)


def layer(
    dp_size, half_bits,
    tok_h, cot_h, ids, table, gain1, bias1, bias_o, gain2, bias2, bias_f, bias_u, bias_qv, wq_h, wo_h, w1_h, w2_h,
    out_h, ing_h, g2_h, g1_h, go_h, gq_h, small_o,
    tok_s, cot_s, sin_s, mid_s, gm_s, n1_s, n2_s, n2t_s, wq_s, wo_s, w1_s, w2_s,
    q_s, v_s, kt_s, ot_s, r_s, e_s, a_s, g_s, sb1, sb2, rb1, rb2,
    own, oth, xr, *rest,
):
    rest = list(rest)
    rr = [rest.pop(0) for _ in half_bits]
    full_bits = [b for b in range(20) if (1 << b) < dp_size and b not in half_bits]
    rx = [rest.pop(0) for _ in full_bits]
    uoth, voth, sm, smr, lsem, wsem, csem, gsem, ssem = rest

    count, width = tok_s.shape
    rows = 2 * count
    quarter = wo_h.shape[0]
    units = w1_h.shape[1]
    heads = quarter // HEAD
    place = lax.axis_index("tensor")
    dp = lax.axis_index("dp")
    chip = place // 2
    core = place % 2
    sib = {"tensor": chip * 2 + 1 - core}
    across = {"tensor": (1 - chip) * 2 + core}
    all_bits = list(half_bits) + full_bits
    sides = {b: (dp // (1 << b)) % 2 for b in all_bits}
    mates = {b: {"dp": dp + (1 - 2 * sides[b]) * (1 << b)} for b in all_bits}

    barrier = pltpu.get_barrier_semaphore()
    partners = [sib, across] + [mates[b] for b in all_bits]
    for partner in partners:
        pl.semaphore_signal(barrier, inc=1, device_id=partner, device_id_type=MESH)

    sq_s, sk_s, k_s = a_s.at[:, 0:128], a_s.at[:, 128:256], a_s.at[:, 256:512]
    ds_s, go_s = a_s.at[:, 0:rows], a_s.at[:, rows : rows + 256]
    local_used = [0]

    def local(src, dst):
        copy = pltpu.make_async_copy(src, dst, lsem.at[local_used[0]])
        local_used[0] += 1
        copy.start()
        return copy

    def remote(src, dst, sems, index, device):
        copy = pltpu.make_async_remote_copy(
            src_ref=src, dst_ref=dst, send_sem=sems.at[0, index], recv_sem=sems.at[1, index], device_id=device, device_id_type=MESH
        )
        copy.start()
        return copy

    get_tok = local(tok_h, tok_s)
    get_cot = local(cot_h, cot_s.at[pl.ds(0, count)])
    get_wq = local(wq_h, wq_s.at[0])
    get_wo = local(wo_h, wo_s.at[pl.ds(0, quarter)])
    get_w1 = local(w1_h, w1_s.at[0])
    get_w2 = local(w2_h, w2_s.at[0])

    part = sides[0]

    def half_of(extent):
        return pl.ds(pl.multiple_of(part * (extent // 2), 32), extent // 2)

    def columns(i):
        return pl.ds(i * BLOCK, BLOCK)

    wo_other = pl.ds(pl.multiple_of(quarter + part * (quarter // 2), 32), quarter // 2)
    pieces = [(wq_h.at[c, half_of(quarter)], wq_s.at[1, c, half_of(quarter)]) for c in range(3)]
    pieces.append((wo_h.at[half_of(quarter)], wo_s.at[wo_other]))
    for i in range(units // BLOCK):
        span = pl.ds(pl.multiple_of(i * BLOCK + part * (BLOCK // 2), 32), BLOCK // 2)
        pieces.append((w1_h.at[half_of(width), columns(i)], w1_s.at[1, half_of(width), columns(i)]))
        pieces.append((w2_h.at[span], w2_s.at[1, span]))

    ln1_gain, ln1_bias, out_bias, ln2_gain, ln2_bias, fc2_bias = (
        ref[...].reshape(1, width) for ref in (gain1, bias1, bias_o, gain2, bias2, bias_f)
    )
    get_tok.wait()

    def first_norm(at):
        plane = core * (count // (SIDE * SIDE)) + at // (SIDE * SIDE)
        line = (at // SIDE) % SIDE
        shape = (SIDE, width // 3)
        for k in range(4):
            spot = jnp.concatenate(
                [jnp.broadcast_to(table[pl.ds(plane, 1)], shape), jnp.broadcast_to(table[pl.ds(line + k, 1)], shape), table[...]], axis=1
            )
            span = pl.ds(pl.multiple_of(at + k * SIDE, SIDE), SIDE)
            stream = tok_s[span].astype(F32) + spot
            sin_s[span] = stream
            xhat, _ = norm_stats(stream)
            n1_s[span] = (xhat * ln1_gain + ln1_bias).astype(BF16)

    loop(count, 4 * SIDE, first_norm)
    slots = lax.broadcasted_iota(jnp.int32, (count, 128), 1) % HEAD
    for at in range(2):
        side = core if at == 0 else 1 - core
        doc = ids[pl.ds(chip, 1), pl.ds(pl.multiple_of(side * count, 128), count)]
        doc = jnp.broadcast_to(doc.astype(F32), (8, count)).T[:, 0:1]
        same = slots.astype(F32) == doc
        sq_s[at * count : (at + 1) * count] = jnp.where((slots < 4) & jnp.logical_not(same), 1.0, 0.0).astype(BF16)
        sk_s[at * count : (at + 1) * count] = jnp.where(same, NEG_LARGE, 0.0).astype(BF16)

    pl.semaphore_wait(barrier, len(partners))
    unit_copy = remote(bias_u, uoth, wsem, 2 * len(pieces), across)
    head_copy = remote(bias_qv, voth, wsem, 2 * len(pieces) + 1, across)
    by_x = [remote(src, dst, wsem, i, across) for i, (src, dst) in enumerate(pieces)]
    by_y = [None] * len(pieces)

    def forward_weight(*which):
        for i in which:
            by_x[i].wait_recv()
            by_y[i] = remote(pieces[i][1], pieces[i][1], wsem, len(pieces) + i, mates[0])

    def have_weight(*which):
        for i in which:
            by_y[i].wait_recv()

    n1_copy = remote(n1_s.at[pl.ds(0, count)], n1_s.at[pl.ds(count, count)], csem, 0, sib)
    get_cot.wait()
    cot_copy = remote(cot_s.at[pl.ds(0, count)], cot_s.at[pl.ds(count, count)], csem, 1, sib)

    def project(j, at):
        n = n1_s[pl.ds(at, BLOCK)]
        biases = bias_qv if j == 0 else voth
        q = (dot_nt(n, wq_s[j, 0]) + biases[0:1]).astype(BF16) * SCALE
        k = dot_nt(n, wq_s[j, 1]).astype(BF16)
        v = (dot_nt(n, wq_s[j, 2]) + biases[1:2]).astype(BF16)
        q_s[j, pl.ds(at, BLOCK), :quarter] = q
        k_s[pl.ds(at, BLOCK), :quarter] = k
        v_s[j, pl.ds(at, BLOCK), :quarter] = v
        kt_s[j * quarter : (j + 1) * quarter, pl.ds(at, BLOCK)] = k.T * SCALE

    def attend(j, service):
        vt = v_s[j, :, :quarter].T
        for head in range(heads):
            qh = head_lanes(q_s.at[j], head, sq_s[...])
            kh = head_lanes(k_s, head, sk_s[...])
            first = a_s.at[:, 512 + 256 * head : 640 + 256 * head]
            second = a_s.at[:, 640 + 256 * head : 768 + 256 * head]
            first[...] = kh
            second[...] = kh
            span = slice(head * HEAD, head * HEAD + HEAD)
            to = slice(j * quarter + head * HEAD, j * quarter + head * HEAD + HEAD)

            def highest(at):
                return jnp.max(dot_nt(first[...], qh[at : at + BLOCK]), axis=0, keepdims=True)

            later = highest(0)
            for at in range(0, rows, BLOCK):
                m = later
                if at + BLOCK < rows:
                    later = highest(at + BLOCK)
                e = jnp.exp(dot_nt(second[...], qh[at : at + BLOCK]) - m)
                r = 1.0 / column_sum(e)
                low = e.astype(BF16)
                e_s[j * heads + head, :, at : at + BLOCK] = low
                ot_s[to, at : at + BLOCK] = (dot(vt[span], low) * r).astype(BF16)
                r_s[j * heads + head : j * heads + head + 1, at : at + BLOCK] = r
            service[head]()

    get_wq.wait()
    loop(count, BLOCK, lambda at: project(0, at))
    n1_copy.wait_recv()
    loop(count, BLOCK, lambda at: project(0, count + at))
    nothing = lambda: None
    forward_weight(0, 1)
    attend(0, [lambda: forward_weight(2), lambda: forward_weight(3), nothing])
    head_copy.wait_recv()
    have_weight(0, 1, 2)
    loop(rows, BLOCK, lambda at: project(1, at))
    attend(1, [lambda: forward_weight(4), lambda: forward_weight(5), lambda: forward_weight(6)])

    get_wo.wait()
    have_weight(3)

    def out_part(at):
        return dot_tn(ot_s[:, pl.ds(at, BLOCK)], wo_s[...])

    def out_sib(at):
        sb1[pl.ds(at, BLOCK)] = out_part(count + at).astype(BF16)

    loop(count, BLOCK, out_sib)
    att_copy = remote(sb1, rb1, csem, 2, sib)

    def out_mine(at):
        mid_s[pl.ds(at, BLOCK)] = sin_s[pl.ds(at, BLOCK)] + out_part(at) + out_bias

    loop(count, BLOCK, out_mine)
    att_copy.wait_recv()

    def second_norm(at):
        spot = pl.ds(at, 64)
        mid = mid_s[spot] + rb1[spot].astype(F32)
        mid_s[spot] = mid
        xhat, _ = norm_stats(mid)
        n2 = (xhat * ln2_gain + ln2_bias).astype(BF16)
        n2_s[spot] = n2

    loop(count, 64, second_norm)
    n2_copy = remote(n2_s.at[pl.ds(0, count)], n2_s.at[pl.ds(count, count)], csem, 3, sib)

    base_a = units + width
    parts = units // BLOCK
    steps = 1 + 2 * len(half_bits) + len(full_bits)
    last = len(half_bits) - 1

    class Region:
        def __init__(self, index, row, size, col, cols, order):
            self.row, self.size, self.col, self.cols = row, size, col, cols
            self.base = index * steps
            self.order = [half_bits[k] for k in order if k < len(half_bits)]
            self.stage, self.copy, self.sent, self.trail = 0, None, [], []

        def window(self, row, size, col, cols):
            return pl.ds(row, size), pl.ds(col, cols)

        def go(self, src, src_at, dst, dst_at, device):
            self.copy = remote(src.at[self.window(*src_at)], dst.at[self.window(*dst_at)], gsem, self.base + self.stage, device)
            self.sent.append(self.copy)

        def send(self):
            self.now = (self.row, self.size, self.col, self.cols)
            self.go(oth, self.now, xr, self.now, across)

        def landing(self, stage):
            row, size, col, cols = self.row >> (stage + 1), self.size, self.col, self.cols
            for _ in range(stage + 1):
                if (size // 2) % 16 == 0:
                    size //= 2
                else:
                    cols //= 2
            if cols != self.cols:
                slot = (self.row - base_a) // quarter
                row, col = (base_a >> (stage + 1)) + (slot // 2) * size, (slot % 2) * cols
            return row, size, col, cols

        def add(self, ref, place):
            dest = xr if self.stage == len(all_bits) else own
            row, size, col, cols = self.now
            step = 64 if size % 64 == 0 else 48 if size % 48 == 0 else 32

            def body(off):
                to = (pl.ds(pl.multiple_of(row + off, 16), step), pl.ds(col, cols))
                fr = (pl.ds(pl.multiple_of(place[0] + off, 16), step), pl.ds(place[2], cols))
                dest[to] = (own[to].astype(F32) + ref[fr].astype(F32)).astype(BF16)

            loop(size, step, body)

        def start_next(self):
            stage = self.stage - 1
            if stage < len(half_bits):
                bit = self.order[stage]
                row, size, col, cols = self.now
                if (size // 2) % 16 == 0:
                    halves = [(pl.multiple_of(row + side * (size // 2), 16), size // 2, col, cols) for side in (sides[bit], 1 - sides[bit])]
                else:
                    halves = [(row, size, pl.multiple_of(col + side * (cols // 2), 128), cols // 2) for side in (sides[bit], 1 - sides[bit])]
                keep, give = halves
                place = self.landing(stage)
                self.go(own, give, rr[stage], place, mates[bit])
                self.next_add = (rr[stage], place)
                self.trail.append((bit, keep))
                self.now = keep
            elif stage < len(all_bits):
                i = stage - len(half_bits)
                place = self.landing(last)
                self.go(own, self.now, rx[i], place, mates[full_bits[i]])
                self.next_add = (rx[i], place)
            elif self.trail:
                bit, keep = self.trail.pop()
                self.go(xr, keep, xr, keep, mates[bit])
                self.next_add = None
            else:
                self.copy = None

        def advance(self):
            if self.copy is None:
                return
            self.copy.wait_recv()
            if self.stage == 0:
                self.add(xr, self.now)
            elif self.next_add is not None:
                if self.stage > len(half_bits):
                    self.copy.wait_send()
                    self.sent.pop()
                self.add(*self.next_add)
            self.stage += 1
            self.start_next()
            if self.copy is None:
                row, size, col, cols = self.row, self.size, self.col, self.cols
                if row < units:
                    to = g2_h.at[pl.ds(row, size)]
                elif row < base_a:
                    to = g1_h.at[:, pl.ds(col, cols)]
                elif row == base_a:
                    to = go_h
                else:
                    to = gq_h.at[(row - base_a) // quarter - 1]
                self.done = local(xr.at[self.window(row, size, col, cols)], to)

    chunks = []
    for i in range(parts):
        chunks.append(Region(2 * i, i * BLOCK, BLOCK, 0, width, ORDERS[2 * i]))
        chunks.append(Region(2 * i + 1, units, width, i * BLOCK, BLOCK, ORDERS[2 * i + 1]))
    for i in range(4):
        chunks.append(Region(2 * parts + i, base_a + i * quarter, quarter, 0, width, ORDERS[2 * parts + i]))
    first_att = 2 * parts

    def send(i):
        chunks[i].send()

    def hook(name):
        for i in PLAN.get(name, ()):
            chunks[i].advance()

    get_w1.wait()
    get_w2.wait()

    def chunk_rows(j, i, at):
        span = pl.ds(at, BLOCK)
        cols = slice(j * units + i * BLOCK, j * units + (i + 1) * BLOCK)
        mine = slice(i * BLOCK, (i + 1) * BLOCK)
        bias = (bias_u if j == 0 else uoth)[mine].reshape(1, BLOCK)
        h = dot(n2_s[span], w1_s[j, :, mine]) + bias
        a, slope = gelu_pair(h)
        a_s[span, cols] = a.astype(BF16)
        g = (dot_nt(cot_s[span], w2_s[j, mine]) * slope).astype(BF16)
        g_s[span, cols] = g

    def chunk_grads(j, i):
        cols = slice(j * units + i * BLOCK, j * units + (i + 1) * BLOCK)
        mine = slice(i * BLOCK, (i + 1) * BLOCK)
        to = oth if j == 1 else own
        to[i * BLOCK : (i + 1) * BLOCK] = dot_tn(a_s[:, cols], cot_s[...]).astype(BF16)
        if j == 1:
            send(2 * i)
        g = g_s[:, cols]
        to[units : units + width, mine] = dot(n2t_s[...], g).astype(BF16)
        if j == 1:
            send(2 * i + 1)
        sm[8 + 8 * j : 9 + 8 * j, mine] = column_sum(g.astype(F32))
        hook(f"f{j}{i}")

    def feed(j, i, first=False):
        if first:
            for at in range(0, count, BLOCK):
                chunk_rows(j, i, at)
            n2_copy.wait_recv()
            cot_copy.wait_recv()
            for at in range(0, rows, BLOCK):
                n2t_s[:, at : at + BLOCK] = n2_s[at : at + BLOCK].T
            for at in range(count, rows, BLOCK):
                chunk_rows(j, i, at)
        else:
            for at in range(0, rows, BLOCK):
                chunk_rows(j, i, at)
        chunk_grads(j, i)

    sm[...] = jnp.zeros_like(sm)
    unit_copy.wait_recv()
    have_weight(4, 5)
    feed(1, 0, first=True)
    forward_weight(7)
    feed(0, 0)
    have_weight(6, 7)
    forward_weight(8)
    feed(1, 1)
    forward_weight(9)
    feed(0, 1)
    for i in range(2, parts):
        have_weight(4 + 2 * i, 5 + 2 * i)
        feed(1, i)
        feed(0, i)

    def back_two(at):
        span = pl.ds(at, BLOCK)
        return dot_nt(g_s[span, :units], w1_s[0]) + dot_nt(g_s[span, units:], w1_s[1])

    def mlp_part(at):
        span = pl.ds(at, BLOCK)
        return dot(a_s[span, :units], w2_s[0]) + dot(a_s[span, units:], w2_s[1])

    def back_two_sib(at):
        sb2[pl.ds(at, BLOCK)] = back_two(count + at).astype(BF16)

    def back_two_mine(at):
        gm_s[pl.ds(at, BLOCK)] = back_two(at)

    def mlp_sib(at):
        sb1[pl.ds(at, BLOCK)] = mlp_part(count + at).astype(BF16)

    loop(count, BLOCK, back_two_sib)
    gn2_copy = remote(sb2, rb2, csem, 4, sib)
    loop(count, BLOCK, back_two_mine)
    hook("gn2")
    att_copy.wait_send()
    loop(count, BLOCK, mlp_sib)
    mlp_copy = remote(sb1, rb1, csem, 5, sib)
    hook("gn2b")
    gn2_copy.wait_recv()
    n2_copy.wait_send()

    def second_back(at):
        spot = pl.ds(at, 64)
        xhat, sigma = norm_stats(mid_s[spot])
        grad = gm_s[spot] + rb2[spot].astype(F32)
        cot = cot_s[spot].astype(F32)
        back = cot + norm_back(grad, ln2_gain, xhat, sigma)
        gm_s[spot] = back
        n2_s[spot] = back.astype(BF16)
        sm[2:3] += column_sum(back)
        sm[3:4] += column_sum(grad * xhat)
        sm[4:5] += column_sum(grad)
        sm[5:6] += column_sum(cot)

    loop(count, 64, second_back)
    dm_copy = remote(n2_s.at[pl.ds(0, count)], n2_s.at[pl.ds(count, count)], csem, 6, sib)

    hook("ln2")

    def finish_out(at):
        span = pl.ds(at, BLOCK)
        mid_s[span] = mid_s[span] + mlp_part(at) + fc2_bias

    loop(count, BLOCK, finish_out)
    mlp_copy.wait_recv()

    def write_out(at):
        spot = pl.ds(at, 64)
        tok_s[spot] = (mid_s[spot] + rb1[spot].astype(F32)).astype(BF16)

    loop(count, 64, write_out)
    put_out = local(tok_s, out_h)
    hook("fin")
    dm_copy.wait_recv()

    def attend_back(j):
        dm = n2_s[...]
        base = j * quarter
        ot = ot_s[base : base + quarter]
        to = oth if j == 1 else own
        to[base_a : base_a + quarter] = dot(ot, dm).astype(BF16)
        if j == 1:
            send(first_att)
        grad_t = dot_nt(wo_s[base : base + quarter], dm).astype(BF16).astype(F32)
        scaled, inners = [], []
        for head in range(heads):
            span = slice(head * HEAD, head * HEAD + HEAD)
            r = r_s[j * heads + head : j * heads + head + 1]
            g = grad_t[span]
            inners.append(column_sum(g * ot[span].astype(F32)) * r)
            scaled.append((g * r).astype(BF16))
        gt = jnp.concatenate(scaled, axis=0)
        go_s[:, :quarter] = gt.T
        dq, dk, dv = [], [None, None], [None, None]
        zero = jnp.zeros((rows, 128), BF16)
        for head in range(heads):
            tile = head // 2
            vh = head_lanes(v_s.at[j], head, zero)
            qh = head_lanes(q_s.at[j], head, zero)
            gh = head_lanes(go_s, head, zero)
            gth = gt[128 * tile : min(128 * tile + 128, quarter)]
            vh = vh[:, : gth.shape[0]]
            e_h = e_s.at[j * heads + head]
            for at in range(0, rows, BLOCK):
                dp_t = dot(vh, gth[:, at : at + BLOCK])
                ds = (dp_t - inners[head][:, at : at + BLOCK]) * e_h[:, at : at + BLOCK].astype(F32)
                ds_s[:, at : at + BLOCK] = ds.astype(BF16)
            dvh = dot(e_h[...], gh)
            dkh = dot(ds_s[...], qh)
            dv[tile] = dvh if dv[tile] is None else dv[tile] + dvh
            dk[tile] = dkh if dk[tile] is None else dk[tile] + dkh
            dq.append(dot(kt_s[base + head * HEAD : base + head * HEAD + HEAD], ds_s[...]))
            hook(f"b{j}{head}")
        dqt = jnp.concatenate(dq, axis=0).astype(BF16)
        start = base_a + quarter
        n1 = n1_s[...]
        dest = 3 * BLOCK * j

        def lanes_of(total):
            return jnp.concatenate([total[0], total[1]], axis=1)[:, :quarter].astype(BF16)

        dvf = lanes_of(dv)
        dkf = lanes_of(dk)
        dqf = dqt.T
        for c, d in ((0, dqf), (1, dkf), (2, dvf)):
            g_s[:, dest + c * BLOCK : dest + c * BLOCK + quarter] = d
        sm[9 + 8 * j : 10 + 8 * j, :quarter] = column_sum(dqf.astype(F32))
        sm[10 + 8 * j : 11 + 8 * j, :quarter] = column_sum(dvf.astype(F32))
        for c, d in ((2, dvf.T), (1, dkf.T), (0, dqt)):
            to[start + c * quarter : start + (c + 1) * quarter] = dot(d, n1).astype(BF16)
            if j == 1:
                send(first_att + 1 + c)
        hook(f"s{j}")

    attend_back(1)
    attend_back(0)

    def back_one(at):
        total = None
        for j in range(2):
            for c in range(3):
                d = g_s[pl.ds(at, BLOCK), (3 * j + c) * BLOCK : (3 * j + c) * BLOCK + quarter]
                term = dot(d, wq_s[j, c])
                total = term if total is None else total + term
        return total

    gn2_copy.wait_send()

    def back_one_sib(at):
        sb2[pl.ds(at, BLOCK)] = back_one(count + at).astype(BF16)

    def back_one_mine(at):
        mid_s[pl.ds(at, BLOCK)] = back_one(at)

    loop(count, BLOCK, back_one_sib)
    gn1_copy = remote(sb2, rb2, csem, 7, sib)
    hook("gn1")
    loop(count, BLOCK, back_one_mine)
    hook("gn1b")
    gn1_copy.wait_recv()
    mlp_copy.wait_send()

    def first_back(at):
        spot = pl.ds(at, 64)
        xhat, sigma = norm_stats(sin_s[spot])
        grad = mid_s[spot] + rb2[spot].astype(F32)
        sb1[spot] = (gm_s[spot] + norm_back(grad, ln1_gain, xhat, sigma)).astype(BF16)
        sm[0:1] += column_sum(grad * xhat)
        sm[1:2] += column_sum(grad)

    loop(count, 64, first_back)
    put_in = local(sb1, ing_h)

    state = {}

    def small_start(i):
        if i == 0:
            state["c"] = remote(sm, smr.at[0], ssem, 0, sib)
        elif i == 1:
            state["c"] = remote(sm, smr.at[1], ssem, 1, across)
        else:
            state["c"] = remote(sm.at[pl.ds(0, 16)], smr.at[i, pl.ds(0, 16)], ssem, i, mates[all_bits[i - 2]])
        state["i"] = i

    def small_step():
        i = state["i"]
        state["c"].wait()
        if i == 0:
            sm[0:8] = sm[0:8] + smr[0, 0:8]
        elif i == 1:
            sm[0:8] = sm[0:8] + smr[1, 0:8]
            sm[8:16] = sm[8:16] + smr[1, 16:24]
        else:
            sm[0:16] = sm[0:16] + smr[i, 0:16]
        if i + 1 < 2 + len(all_bits):
            small_start(i + 1)
        else:
            small_o[...] = sm[0:16]

    small_start(0)
    small_left = 2 + len(all_bits)
    for i in PLAN["tail"]:
        if i >= 0:
            chunks[i].advance()
        elif small_left:
            small_step()
            small_left -= 1
    while True:
        busy = False
        for chunk in chunks:
            if chunk.copy is not None:
                chunk.advance()
                busy = True
        if small_left:
            small_step()
            small_left -= 1
            busy = True
        if not busy:
            break

    for copy in [unit_copy, head_copy, n1_copy, cot_copy, dm_copy, gn1_copy] + by_x + by_y:
        copy.wait_send()
    for chunk in chunks:
        for copy in chunk.sent:
            copy.wait_send()
        chunk.done.wait()
    put_out.wait()
    put_in.wait()


def call_layer(dp_size, tokens, cotangent, ids, table, vectors, wq, wo, w1, w2):
    count, width = tokens.shape
    rows = 2 * count
    quarter = wo.shape[0]
    units = w1.shape[1]
    heads = quarter // HEAD
    grad_rows = units + width + 4 * quarter
    bits = [b for b in range(20) if (1 << b) < dp_size]
    half_bits = bits[:3]
    shape = jax.ShapeDtypeStruct
    vm = pltpu.VMEM
    regions = 2 * (units // BLOCK) + 4
    steps = 1 + 2 * len(half_bits) + len(bits) - len(half_bits)
    fetched = 4 + 2 * (units // BLOCK)
    scratch = (
        [vm((count, width), BF16), vm((rows, width), BF16)]
        + [vm((count, width), F32)] * 3
        + [vm((rows, width), BF16)] * 2
        + [vm((width, rows), BF16)]
        + [vm((2,) + wq.shape, BF16), vm((2 * quarter, width), BF16), vm((2,) + w1.shape, BF16), vm((2,) + w2.shape, BF16)]
        + [vm((2, rows, 256), BF16)] * 2
        + [vm((2 * quarter, rows), BF16)] * 2
        + [vm((8, rows), F32), vm((2 * heads, rows, rows), BF16)]
        + [vm((rows, 2 * units), BF16)] * 2
        + [vm((count, width), BF16)] * 4
        + [vm((grad_rows, width), BF16)] * 3
        + [vm((grad_rows >> (i + 1), width), BF16) for i in range(len(half_bits))]
        + [vm((grad_rows >> len(half_bits), width), BF16)] * (len(bits) - len(half_bits))
        + [vm((units,), F32), vm((2, quarter), F32), vm((24, width), F32), vm((2 + len(bits), 24, width), F32)]
        + [pltpu.SemaphoreType.DMA((8 + regions,))]
        + [pltpu.SemaphoreType.DMA((2, n)) for n in (2 * fetched + 2, 8, regions * steps, 2 + len(bits))]
    )
    anywhere = pl.BlockSpec(memory_space=pl.ANY)
    inside = pl.BlockSpec(memory_space=pltpu.VMEM)
    return pl.pallas_call(
        functools.partial(layer, dp_size, half_bits),
        out_shape=[shape((count, width), BF16)] * 2
        + [shape(w2.shape, BF16), shape(w1.shape, BF16), shape(wo.shape, BF16), shape(wq.shape, BF16), shape((16, width), F32)],
        in_specs=[anywhere] * 2 + [inside] * (2 + len(vectors)) + [anywhere] * 4,
        out_specs=[anywhere] * 6 + [inside],
        scratch_shapes=scratch,
        compiler_params=pltpu.CompilerParams(vmem_limit_bytes=VMEM_LIMIT, collective_id=0, has_side_effects=True),
        name="layer",
    )(tokens, cotangent, ids, table, *vectors, wq, wo, w1, w2)


def finish(out, ing, g2, g1, go, gq, small, out_o, ing_o, g2_o, g1_o, go_o, gq_o, a0, a1, a2, a3, a4, a5, units_o, heads_o):
    for src, dst in ((out, out_o), (ing, ing_o), (g2, g2_o), (g1, g1_o), (go, go_o), (gq, gq_o)):
        dst[...] = src[...].astype(dst.dtype)

    @pl.when(pl.program_id(0) == 0)
    def _():
        for i, ref in enumerate((a0, a1, a2, a3, a4, a5)):
            ref[...] = small[i]
        units_o[...] = small[8, : units_o.shape[0]]
        heads_o[...] = small[9:11, : heads_o.shape[1]]


def call_finish(arrays, small, units, quarter):
    steps = 4
    width = small.shape[1]
    shape = jax.ShapeDtypeStruct

    def rows_of(a):
        axis = a.ndim - 2
        block = a.shape[:axis] + (a.shape[axis] // steps,) + a.shape[axis + 1 :]
        return pl.BlockSpec(block, lambda i, axis=axis, rank=a.ndim: tuple(i if k == axis else 0 for k in range(rank)))

    def whole(extent):
        return pl.BlockSpec(extent, lambda i, rank=len(extent): (0,) * rank)

    extents = [(width,)] * 6 + [(units,), (2, quarter)]
    kinds = [BF16, BF16, F32, F32, F32, F32]
    return pl.pallas_call(
        finish,
        grid=(steps,),
        in_specs=[rows_of(a) for a in arrays] + [whole(small.shape)],
        out_specs=[rows_of(a) for a in arrays] + [whole(e) for e in extents],
        out_shape=[shape(a.shape, k) for a, k in zip(arrays, kinds)] + [shape(e, F32) for e in extents],
        compiler_params=pltpu.CompilerParams(vmem_limit_bytes=VMEM_LIMIT),
        name="finish",
    )(*arrays, small)


def per_device(
    tokens, segment_ids, ln1_gain, ln1_bias, qkv_weight, qv_bias, out_weight, out_bias,
    ln2_gain, ln2_bias, fc1_weight, fc1_bias, fc2_weight, fc2_bias, cotangent,
):
    width = tokens.shape[1]
    freq_count = width // 6
    frequency = 10000.0 ** (-jnp.arange(freq_count, dtype=F32) / freq_count)
    angles = jnp.arange(SIDE, dtype=F32)[:, None] * frequency[None, :]
    table = jnp.concatenate([jnp.sin(angles), jnp.cos(angles)], axis=1)
    vectors = (ln1_gain, ln1_bias, out_bias, ln2_gain, ln2_bias, fc2_bias, fc1_bias, qv_bias)
    *arrays, small = call_layer(
        lax.axis_size("dp"), tokens, cotangent, segment_ids, table, vectors, qkv_weight.transpose(0, 2, 1), out_weight, fc1_weight, fc2_weight
    )
    out, ing, g2, g1, go, gq, a0, a1, a2, a3, a4, a5, g_units, g_heads = call_finish(arrays, small, fc1_weight.shape[1], out_weight.shape[0])
    return (out, ing, a0, a1, gq.transpose(0, 2, 1), g_heads, go, a2, a3, a4, g1, g_units, g2, a5)


def solution(mesh):
    placed = (
        P(("dp", "tensor"), None),
        P("dp", None),
        P(),
        P(),
        P(None, None, "tensor"),
        P(None, "tensor"),
        P("tensor", None),
        P(),
        P(),
        P(),
        P(None, "tensor"),
        P("tensor"),
        P("tensor", None),
        P(),
        P(("dp", "tensor"), None),
    )
    return jax.shard_map(
        per_device,
        mesh=mesh,
        in_specs=placed,
        out_specs=(
            P(("dp", "tensor"), None),
            P(("dp", "tensor"), None),
            P(),
            P(),
            P(None, None, "tensor"),
            P(None, "tensor"),
            P("tensor", None),
            P(),
            P(),
            P(),
            P(None, "tensor"),
            P("tensor"),
            P("tensor", None),
            P(),
        ),
        check_vma=False,
    )
```

```python
import functools

import jax
import jax.numpy as jnp
from jax import lax
from jax.experimental import pallas as pl
from jax.experimental.pallas import tpu as pltpu
from jax.sharding import PartitionSpec as P

HEAD = 64
SIDE = 16
EPSILON = 1e-06
NEG_LARGE = -1e30
SCALE = HEAD ** (-0.5)
F32 = jnp.float32
BF16 = jnp.bfloat16
VMEM_LIMIT = 64 * 1024 * 1024 - 128 * 1024
MESH = pl.DeviceIdType.MESH
BLOCK = 256
ORDERS = ((1, 0, 2), (1, 0, 2), (1, 0, 2), (1, 0, 2), (0, 1, 2), (1, 0, 2), (0, 1, 2), (1, 0, 2), (0, 1, 2), (0, 1, 2))
PLAN = {
    "f01": (0,),
    "f02": (1, 0),
    "ln2": (0, 2, 1),
    "v1": (0, 3, 1, 2),
    "v0": (0, 4, 2, 1),
    "b10": (3,),
    "b11": (0, 2),
    "b12": (1, 5, 4),
    "s1": (3, 2),
    "b00": (0, 1, 6),
    "b01": (3, 2, 5),
    "b02": (4, 9, 6),
    "s0": (3, 1, 5),
    "gn1": (4, 8, 2, 9),
    "gn1b": (6, 5, 3),
    "tail": (4, 9, 7, 8, 6, 5, -1, 3, 9, -1, 4, 6, 5, -1, 9, 7, -1, 8, -1, 4, 6, 7, 8, 5, 7, 6, 9, 8, 7, 8, 9, 7, 8, 7),
}


def dot(a, b):
    return jnp.dot(a, b, preferred_element_type=F32)


def dot_nt(a, b):
    return lax.dot_general(a, b, (((1,), (1,)), ((), ())), preferred_element_type=F32)


def dot_tn(a, b):
    return lax.dot_general(a, b, (((0,), (0,)), ((), ())), preferred_element_type=F32)


def lane_half(rows, upper):
    lanes = lax.broadcasted_iota(jnp.int32, (rows, 128), 1)
    return lanes >= HEAD if upper else lanes < HEAD


def head_lanes(ref, head, filler):
    tile = ref[:, 128 * (head // 2) : 128 * (head // 2) + 128]
    return jnp.where(lane_half(tile.shape[0], head % 2 == 1), tile, filler)


def gelu_pair(h):
    size = jnp.abs(h)
    t = 1.0 / (1.0 + (0.3275911 * 0.7071067811865476) * size)
    bell = jnp.exp(-0.5 * h * h)
    poly = ((((1.061405429 * t - 1.453152027) * t + 1.421413741) * t - 0.284496736) * t + 0.254829592) * t
    tail = 0.5 * poly * bell
    cdf = jnp.where(h < 0, tail, 1.0 - tail)
    return h * cdf, cdf + h * bell * 0.3989422804014327


def norm_stats(v):
    centred = v - jnp.mean(v, axis=-1, keepdims=True)
    sigma = lax.rsqrt(jnp.mean(centred * centred, axis=-1, keepdims=True) + EPSILON)
    return centred * sigma, sigma


def norm_back(grad, gain, xhat, sigma):
    g = grad * gain
    return sigma * (g - jnp.mean(g, axis=-1, keepdims=True) - xhat * jnp.mean(g * xhat, axis=-1, keepdims=True))


def column_sum(v):
    return jnp.sum(v, axis=0, keepdims=True)


def loop(count, step, body):
    def run(i, carry):
        body(pl.multiple_of(i * step, step))
        return carry

    lax.fori_loop(0, count // step, run, 0)


def layer(
    dp_size, half_bits,
    tok_h, cot_h, ids, table, gain1, bias1, bias_o, gain2, bias2, bias_f, bias_u, bias_qv, wq_h, wo_h, w1_h, w2_h,
    out_h, ing_h, g2_h, g1_h, go_h, gq_h, small_o,
    tok_s, cot_s, sin_s, mid_s, gm_s, n1_s, n2_s, n2t_s, wq_s, wo_s, w1_s, w2_s,
    q_s, v_s, kt_s, ot_s, ou_s, gt_s, r_s, in_s, e_s, roll_s, back_s, nr_s, a_s, g_s, sb1, sb2, rb1, rb2,
    own, oth, xr, *rest,
):
    rest = list(rest)
    rr = [rest.pop(0) for _ in half_bits]
    full_bits = [b for b in range(20) if (1 << b) < dp_size and b not in half_bits]
    rx = [rest.pop(0) for _ in full_bits]
    uoth, voth, sm, smr, lsem, wsem, csem, gsem, ssem = rest

    count, width = tok_s.shape
    rows = 2 * count
    quarter = wo_h.shape[0]
    units = w1_h.shape[1]
    heads = quarter // HEAD
    place = lax.axis_index("tensor")
    dp = lax.axis_index("dp")
    chip = place // 2
    core = place % 2
    sib = {"tensor": chip * 2 + 1 - core}
    across = {"tensor": (1 - chip) * 2 + core}
    all_bits = list(half_bits) + full_bits
    sides = {b: (dp // (1 << b)) % 2 for b in all_bits}
    mates = {b: {"dp": dp + (1 - 2 * sides[b]) * (1 << b)} for b in all_bits}

    barrier = pltpu.get_barrier_semaphore()
    partners = [sib, across] + [mates[b] for b in all_bits]
    for partner in partners:
        pl.semaphore_signal(barrier, inc=1, device_id=partner, device_id_type=MESH)

    sq_s, sk_s, k_s = a_s.at[:, 0:128], a_s.at[:, 128:256], a_s.at[:, 256:512]
    local_used = [0]

    def local(src, dst):
        copy = pltpu.make_async_copy(src, dst, lsem.at[local_used[0]])
        local_used[0] += 1
        copy.start()
        return copy

    def remote(src, dst, sems, index, device):
        copy = pltpu.make_async_remote_copy(
            src_ref=src, dst_ref=dst, send_sem=sems.at[0, index], recv_sem=sems.at[1, index], device_id=device, device_id_type=MESH
        )
        copy.start()
        return copy

    get_tok = local(tok_h, tok_s)
    get_cot = local(cot_h, cot_s.at[pl.ds(0, count)])
    get_wq = local(wq_h, wq_s.at[0])
    get_wo = local(wo_h, wo_s.at[pl.ds(0, quarter)])
    get_w1 = local(w1_h, w1_s.at[0])
    get_w2 = local(w2_h, w2_s.at[0])

    part = sides[0]

    def half_of(extent):
        return pl.ds(pl.multiple_of(part * (extent // 2), 32), extent // 2)

    def columns(i):
        return pl.ds(i * BLOCK, BLOCK)

    wo_other = pl.ds(pl.multiple_of(quarter + part * (quarter // 2), 32), quarter // 2)
    pieces = [(wq_h.at[c, half_of(quarter)], wq_s.at[1, c, half_of(quarter)]) for c in range(3)]
    pieces.append((wo_h.at[half_of(quarter)], wo_s.at[wo_other]))
    for i in range(units // BLOCK):
        span = pl.ds(pl.multiple_of(i * BLOCK + part * (BLOCK // 2), 32), BLOCK // 2)
        pieces.append((w1_h.at[half_of(width), columns(i)], w1_s.at[1, half_of(width), columns(i)]))
        pieces.append((w2_h.at[span], w2_s.at[1, span]))

    ln1_gain, ln1_bias, out_bias, ln2_gain, ln2_bias, fc2_bias = (
        ref[...].reshape(1, width) for ref in (gain1, bias1, bias_o, gain2, bias2, bias_f)
    )
    get_tok.wait()

    def first_norm(at):
        plane = core * (count // (SIDE * SIDE)) + at // (SIDE * SIDE)
        line = (at // SIDE) % SIDE
        shape = (SIDE, width // 3)
        for k in range(4):
            spot = jnp.concatenate(
                [jnp.broadcast_to(table[pl.ds(plane, 1)], shape), jnp.broadcast_to(table[pl.ds(line + k, 1)], shape), table[...]], axis=1
            )
            span = pl.ds(pl.multiple_of(at + k * SIDE, SIDE), SIDE)
            stream = tok_s[span].astype(F32) + spot
            sin_s[span] = stream
            xhat, _ = norm_stats(stream)
            n1_s[span] = (xhat * ln1_gain + ln1_bias).astype(BF16)

    loop(count, 4 * SIDE, first_norm)
    doc = ids[pl.ds(chip, 1), :]
    starts = [jnp.zeros((1, 1), F32)]
    starts += [jnp.sum(jnp.where(doc < v, 1.0, 0.0), axis=1, keepdims=True) for v in range(1, 4)]
    starts.append(jnp.full((1, 1), rows, F32))
    turn = jnp.zeros((1, 1), F32)
    for v in range(4):
        turn += jnp.where(starts[v + 1] - starts[v] == count, starts[v], 0.0)
    turn_here = turn - (core * count).astype(F32)

    def wrapped(v):
        v = jnp.where(v >= rows, v - rows, v)
        return jnp.where(v < 0, v + rows, v)

    def rotations(at):
        down = (lax.broadcasted_iota(jnp.int32, (64, rows), 0) + at).astype(F32)
        along = lax.broadcasted_iota(jnp.int32, (64, rows), 1).astype(F32)
        roll_s[pl.ds(at, 64)] = jnp.where(wrapped(down + turn_here) == along, 1.0, 0.0).astype(BF16)
        back_s[pl.ds(at, 64)] = jnp.where(wrapped(down - turn_here) == along, 1.0, 0.0).astype(BF16)
        where = wrapped((lax.broadcasted_iota(jnp.int32, (64, 128), 0) + at).astype(F32) + turn)
        mine = sum(jnp.where(where >= starts[v], 1.0, 0.0) for v in range(1, 4))
        slot = (lax.broadcasted_iota(jnp.int32, (64, 128), 1) % HEAD).astype(F32)
        sq_s[pl.ds(at, 64)] = jnp.where((slot < 4) & (slot != mine), 1.0, 0.0).astype(BF16)
        sk_s[pl.ds(at, 64)] = jnp.where(slot == mine, NEG_LARGE, 0.0).astype(BF16)

    loop(rows, 64, rotations)

    pl.semaphore_wait(barrier, len(partners))
    unit_copy = remote(bias_u, uoth, wsem, 2 * len(pieces), across)
    head_copy = remote(bias_qv, voth, wsem, 2 * len(pieces) + 1, across)
    by_x = [remote(src, dst, wsem, i, across) for i, (src, dst) in enumerate(pieces)]
    by_y = [None] * len(pieces)

    def forward_weight(*which):
        for i in which:
            by_x[i].wait_recv()
            by_y[i] = remote(pieces[i][1], pieces[i][1], wsem, len(pieces) + i, mates[0])

    def have_weight(*which):
        for i in which:
            by_y[i].wait_recv()

    n1_copy = remote(n1_s.at[pl.ds(0, count)], n1_s.at[pl.ds(count, count)], csem, 0, sib)
    get_cot.wait()
    cot_copy = remote(cot_s.at[pl.ds(0, count)], cot_s.at[pl.ds(count, count)], csem, 1, sib)

    def rotate(at):
        nr_s[pl.ds(at, BLOCK)] = dot(roll_s[pl.ds(at, BLOCK)], n1_s[...]).astype(BF16)

    def project(j, at):
        n = nr_s[pl.ds(at, BLOCK)]
        biases = bias_qv if j == 0 else voth
        q = (dot_nt(n, wq_s[j, 0]) + biases[0:1]).astype(BF16) * SCALE
        k = dot_nt(n, wq_s[j, 1]).astype(BF16)
        v = (dot_nt(n, wq_s[j, 2]) + biases[1:2]).astype(BF16)
        q_s[j, pl.ds(at, BLOCK), :quarter] = q
        k_s[pl.ds(at, BLOCK), :quarter] = k
        v_s[j, pl.ds(at, BLOCK), :quarter] = v
        kt_s[j * quarter : (j + 1) * quarter, pl.ds(at, BLOCK)] = k.T * SCALE

    blocks = [(b, at) for b in range(2) for at in range(0, count, BLOCK)]

    def attend(j, service):
        vt = v_s[j, :, :quarter].T
        for head in range(heads):
            qh = head_lanes(q_s.at[j], head, sq_s[...])
            kh = head_lanes(k_s, head, sk_s[...])
            span = slice(head * HEAD, head * HEAD + HEAD)
            to = slice(j * quarter + head * HEAD, j * quarter + head * HEAD + HEAD)

            def scores(b, at):
                return dot_nt(kh[b * count : (b + 1) * count], qh[b * count + at : b * count + at + BLOCK])

            later = scores(*blocks[0])
            for i, (b, at) in enumerate(blocks):
                s = later
                if i + 1 < len(blocks):
                    later = scores(*blocks[i + 1])
                m = jnp.max(s, axis=0, keepdims=True)
                e = jnp.exp(s - m)
                r = 1.0 / column_sum(e)
                low = e.astype(BF16)
                here = slice(b * count + at, b * count + at + BLOCK)
                e_s[j * heads + head, b, :, at : at + BLOCK] = low
                ot_s[to, here] = (dot(vt[span, b * count : (b + 1) * count], low) * r).astype(BF16)
                r_s[j * heads + head : j * heads + head + 1, here] = r
            service[head]()

    get_wq.wait()
    n1_copy.wait_recv()
    loop(rows, BLOCK, rotate)
    loop(rows, BLOCK, lambda at: project(0, at))
    nothing = lambda: None
    forward_weight(0, 1)
    attend(0, [lambda: forward_weight(2), lambda: forward_weight(3), nothing])
    head_copy.wait_recv()
    have_weight(0, 1, 2)
    loop(rows, BLOCK, lambda at: project(1, at))
    attend(1, [lambda: forward_weight(4), lambda: forward_weight(5), lambda: forward_weight(6)])

    get_wo.wait()
    have_weight(3)

    def unrotate(at):
        ou_s[:, pl.ds(at, BLOCK)] = dot(ot_s[...], roll_s[:, pl.ds(at, BLOCK)]).astype(BF16)

    loop(rows, BLOCK, unrotate)

    def out_part(at):
        return dot_tn(ou_s[:, pl.ds(at, BLOCK)], wo_s[...])

    def out_sib(at):
        sb1[pl.ds(at, BLOCK)] = out_part(count + at).astype(BF16)

    loop(count, BLOCK, out_sib)
    att_copy = remote(sb1, rb1, csem, 2, sib)

    def out_mine(at):
        mid_s[pl.ds(at, BLOCK)] = sin_s[pl.ds(at, BLOCK)] + out_part(at) + out_bias

    loop(count, BLOCK, out_mine)
    att_copy.wait_recv()

    def second_norm(at):
        spot = pl.ds(at, 64)
        mid = mid_s[spot] + rb1[spot].astype(F32)
        mid_s[spot] = mid
        xhat, _ = norm_stats(mid)
        n2 = (xhat * ln2_gain + ln2_bias).astype(BF16)
        n2_s[spot] = n2

    loop(count, 64, second_norm)
    n2_copy = remote(n2_s.at[pl.ds(0, count)], n2_s.at[pl.ds(count, count)], csem, 3, sib)

    base_a = units + width
    parts = units // BLOCK
    steps = 1 + 2 * len(half_bits) + len(full_bits)
    last = len(half_bits) - 1

    class Region:
        def __init__(self, index, row, size, col, cols, order):
            self.row, self.size, self.col, self.cols = row, size, col, cols
            self.base = index * steps
            self.order = [half_bits[k] for k in order if k < len(half_bits)]
            self.stage, self.copy, self.sent, self.trail = 0, None, [], []

        def window(self, row, size, col, cols):
            return pl.ds(row, size), pl.ds(col, cols)

        def go(self, src, src_at, dst, dst_at, device):
            self.copy = remote(src.at[self.window(*src_at)], dst.at[self.window(*dst_at)], gsem, self.base + self.stage, device)
            self.sent.append(self.copy)

        def send(self):
            self.now = (self.row, self.size, self.col, self.cols)
            self.go(oth, self.now, xr, self.now, across)

        def landing(self, stage):
            row, size, col, cols = self.row >> (stage + 1), self.size, self.col, self.cols
            for _ in range(stage + 1):
                if (size // 2) % 16 == 0:
                    size //= 2
                else:
                    cols //= 2
            if cols != self.cols:
                slot = (self.row - base_a) // quarter
                row, col = (base_a >> (stage + 1)) + (slot // 2) * size, (slot % 2) * cols
            return row, size, col, cols

        def add(self, ref, place):
            dest = xr if self.stage == len(all_bits) else own
            row, size, col, cols = self.now
            step = 64 if size % 64 == 0 else 48 if size % 48 == 0 else 32

            def body(off):
                to = (pl.ds(pl.multiple_of(row + off, 16), step), pl.ds(col, cols))
                fr = (pl.ds(pl.multiple_of(place[0] + off, 16), step), pl.ds(place[2], cols))
                dest[to] = (own[to].astype(F32) + ref[fr].astype(F32)).astype(BF16)

            loop(size, step, body)

        def start_next(self):
            stage = self.stage - 1
            if stage < len(half_bits):
                bit = self.order[stage]
                row, size, col, cols = self.now
                if (size // 2) % 16 == 0:
                    halves = [(pl.multiple_of(row + side * (size // 2), 16), size // 2, col, cols) for side in (sides[bit], 1 - sides[bit])]
                else:
                    halves = [(row, size, pl.multiple_of(col + side * (cols // 2), 128), cols // 2) for side in (sides[bit], 1 - sides[bit])]
                keep, give = halves
                place = self.landing(stage)
                self.go(own, give, rr[stage], place, mates[bit])
                self.next_add = (rr[stage], place)
                self.trail.append((bit, keep))
                self.now = keep
            elif stage < len(all_bits):
                i = stage - len(half_bits)
                place = self.landing(last)
                self.go(own, self.now, rx[i], place, mates[full_bits[i]])
                self.next_add = (rx[i], place)
            elif self.trail:
                bit, keep = self.trail.pop()
                self.go(xr, keep, xr, keep, mates[bit])
                self.next_add = None
            else:
                self.copy = None

        def advance(self):
            if self.copy is None:
                return
            self.copy.wait_recv()
            if self.stage == 0:
                self.add(xr, self.now)
            elif self.next_add is not None:
                if self.stage > len(half_bits):
                    self.copy.wait_send()
                    self.sent.pop()
                self.add(*self.next_add)
            self.stage += 1
            self.start_next()
            if self.copy is None:
                row, size, col, cols = self.row, self.size, self.col, self.cols
                if row < units:
                    to = g2_h.at[pl.ds(row, size)]
                elif row < base_a:
                    to = g1_h.at[:, pl.ds(col, cols)]
                elif row == base_a:
                    to = go_h
                else:
                    to = gq_h.at[(row - base_a) // quarter - 1]
                self.done = local(xr.at[self.window(row, size, col, cols)], to)

    chunks = []
    for i in range(parts):
        chunks.append(Region(2 * i, i * BLOCK, BLOCK, 0, width, ORDERS[2 * i]))
        chunks.append(Region(2 * i + 1, units, width, i * BLOCK, BLOCK, ORDERS[2 * i + 1]))
    for i in range(4):
        chunks.append(Region(2 * parts + i, base_a + i * quarter, quarter, 0, width, ORDERS[2 * parts + i]))
    first_att = 2 * parts

    def send(i):
        chunks[i].send()

    def hook(name):
        for i in PLAN.get(name, ()):
            chunks[i].advance()

    get_w1.wait()
    get_w2.wait()

    def chunk_rows(j, i, at):
        span = pl.ds(at, BLOCK)
        cols = slice(j * units + i * BLOCK, j * units + (i + 1) * BLOCK)
        mine = slice(i * BLOCK, (i + 1) * BLOCK)
        bias = (bias_u if j == 0 else uoth)[mine].reshape(1, BLOCK)
        h = dot(n2_s[span], w1_s[j, :, mine]) + bias
        a, slope = gelu_pair(h)
        a_s[span, cols] = a.astype(BF16)
        g = (dot_nt(cot_s[span], w2_s[j, mine]) * slope).astype(BF16)
        g_s[span, cols] = g

    def chunk_grads(j, i):
        cols = slice(j * units + i * BLOCK, j * units + (i + 1) * BLOCK)
        mine = slice(i * BLOCK, (i + 1) * BLOCK)
        to = oth if j == 1 else own
        to[i * BLOCK : (i + 1) * BLOCK] = dot_tn(a_s[:, cols], cot_s[...]).astype(BF16)
        if j == 1:
            send(2 * i)
        g = g_s[:, cols]
        to[units : units + width, mine] = dot(n2t_s[...], g).astype(BF16)
        if j == 1:
            send(2 * i + 1)
        sm[8 + 8 * j : 9 + 8 * j, mine] = column_sum(g.astype(F32))
        hook(f"f{j}{i}")

    def feed(j, i, first=False):
        if first:
            for at in range(0, count, BLOCK):
                chunk_rows(j, i, at)
            n2_copy.wait_recv()
            cot_copy.wait_recv()
            for at in range(0, rows, BLOCK):
                n2t_s[:, at : at + BLOCK] = n2_s[at : at + BLOCK].T
            for at in range(count, rows, BLOCK):
                chunk_rows(j, i, at)
        else:
            for at in range(0, rows, BLOCK):
                chunk_rows(j, i, at)
        chunk_grads(j, i)

    sm[...] = jnp.zeros_like(sm)
    unit_copy.wait_recv()
    have_weight(4, 5)
    feed(1, 0, first=True)
    forward_weight(7)
    feed(0, 0)
    have_weight(6, 7)
    forward_weight(8)
    feed(1, 1)
    forward_weight(9)
    feed(0, 1)
    for i in range(2, parts):
        have_weight(4 + 2 * i, 5 + 2 * i)
        feed(1, i)
        feed(0, i)

    def back_two(at):
        span = pl.ds(at, BLOCK)
        return dot_nt(g_s[span, :units], w1_s[0]) + dot_nt(g_s[span, units:], w1_s[1])

    def mlp_part(at):
        span = pl.ds(at, BLOCK)
        return dot(a_s[span, :units], w2_s[0]) + dot(a_s[span, units:], w2_s[1])

    def back_two_sib(at):
        sb2[pl.ds(at, BLOCK)] = back_two(count + at).astype(BF16)

    def back_two_mine(at):
        gm_s[pl.ds(at, BLOCK)] = back_two(at)

    def mlp_sib(at):
        sb1[pl.ds(at, BLOCK)] = mlp_part(count + at).astype(BF16)

    loop(count, BLOCK, back_two_sib)
    gn2_copy = remote(sb2, rb2, csem, 4, sib)
    loop(count, BLOCK, back_two_mine)
    hook("gn2")
    att_copy.wait_send()
    loop(count, BLOCK, mlp_sib)
    mlp_copy = remote(sb1, rb1, csem, 5, sib)
    hook("gn2b")
    gn2_copy.wait_recv()
    n2_copy.wait_send()

    def second_back(at):
        spot = pl.ds(at, 64)
        xhat, sigma = norm_stats(mid_s[spot])
        grad = gm_s[spot] + rb2[spot].astype(F32)
        cot = cot_s[spot].astype(F32)
        back = cot + norm_back(grad, ln2_gain, xhat, sigma)
        gm_s[spot] = back
        n2_s[spot] = back.astype(BF16)
        sm[2:3] += column_sum(back)
        sm[3:4] += column_sum(grad * xhat)
        sm[4:5] += column_sum(grad)
        sm[5:6] += column_sum(cot)

    loop(count, 64, second_back)
    dm_copy = remote(n2_s.at[pl.ds(0, count)], n2_s.at[pl.ds(count, count)], csem, 6, sib)

    hook("ln2")

    def finish_out(at):
        span = pl.ds(at, BLOCK)
        mid_s[span] = mid_s[span] + mlp_part(at) + fc2_bias

    loop(count, BLOCK, finish_out)
    mlp_copy.wait_recv()

    def write_out(at):
        spot = pl.ds(at, 64)
        tok_s[spot] = (mid_s[spot] + rb1[spot].astype(F32)).astype(BF16)

    loop(count, 64, write_out)
    put_out = local(tok_s, out_h)
    hook("fin")
    dm_copy.wait_recv()

    zero = jnp.zeros((rows, 128), BF16)
    start = base_a + quarter

    def lanes_of(total):
        return jnp.concatenate([total[0], total[1]], axis=1)[:, :quarter].astype(BF16)

    def keep_gradient(j, c, d, dt):
        to = oth if j == 1 else own
        g_s[:, (3 * j + c) * BLOCK : (3 * j + c) * BLOCK + quarter] = d
        to[start + c * quarter : start + (c + 1) * quarter] = dot(dt, nr_s[...]).astype(BF16)
        if j == 1:
            send(first_att + 1 + c)
        if c != 1:
            sm[9 + c // 2 + 8 * j : 10 + c // 2 + 8 * j, :quarter] = column_sum(d.astype(F32))

    def both_blocks(parts_of):
        return jnp.concatenate([parts_of(0), parts_of(1)], axis=0)

    def values_back(j):
        base = j * quarter
        to = oth if j == 1 else own
        dm = n2_s[...]
        to[base_a : base_a + quarter] = dot(ou_s[base : base + quarter], dm).astype(BF16)
        if j == 1:
            send(first_att)
        grad_t = dot_nt(wo_s[base : base + quarter], dm).astype(BF16)
        grad_t = dot_nt(grad_t, roll_s[...])
        scaled = []
        for head in range(heads):
            span = slice(head * HEAD, head * HEAD + HEAD)
            row = j * heads + head
            r = r_s[row : row + 1]
            g = grad_t[span]
            in_s[row : row + 1] = column_sum(g * ot_s[base + head * HEAD : base + head * HEAD + HEAD].astype(F32)) * r
            scaled.append((g * r).astype(BF16))
        gt = jnp.concatenate(scaled, axis=0)
        gt_s[base : base + quarter] = gt
        go_s = a_s.at[:, rows + 256 * j : rows + 256 * (j + 1)]
        go_s[:, :quarter] = gt.T
        dv = [None, None]
        for head in range(heads):
            gh = head_lanes(go_s, head, zero)
            part = both_blocks(lambda b: dot(e_s[j * heads + head, b], gh[b * count : (b + 1) * count]))
            tile = head // 2
            dv[tile] = part if dv[tile] is None else dv[tile] + part
        dv = lanes_of(dv)
        keep_gradient(j, 2, dv, dv.T)
        hook(f"v{j}")

    def scores_back(j):
        base = j * quarter
        dq, dk = [], [None, None]
        for head in range(heads):
            tile = head // 2
            row = j * heads + head
            vh = head_lanes(v_s.at[j], head, zero)
            qh = head_lanes(q_s.at[j], head, zero)
            last_row = min(128 * tile + 128, quarter)
            gth = gt_s[base + 128 * tile : base + last_row]
            vh = vh[:, : gth.shape[0]]
            ds = a_s.at[:, (head % 2) * count : (head % 2 + 1) * count]
            for b, at in blocks:
                here = slice(b * count + at, b * count + at + BLOCK)
                dp_t = dot(vh[b * count : (b + 1) * count], gth[:, here])
                grad = (dp_t - in_s[row : row + 1, here]) * e_s[row, b, :, at : at + BLOCK].astype(F32)
                ds[b * count : (b + 1) * count, at : at + BLOCK] = grad.astype(BF16)
            part = both_blocks(lambda b: dot(ds[b * count : (b + 1) * count], qh[b * count : (b + 1) * count]))
            dk[tile] = part if dk[tile] is None else dk[tile] + part
            kth = kt_s.at[base + head * HEAD : base + head * HEAD + HEAD]
            dq.append(
                jnp.concatenate(
                    [dot(kth[:, b * count : (b + 1) * count], ds[b * count : (b + 1) * count]) for b in range(2)], axis=1
                )
            )
            hook(f"b{j}{head}")
        dk = lanes_of(dk)
        keep_gradient(j, 1, dk, dk.T)
        dqt = jnp.concatenate(dq, axis=0).astype(BF16)
        keep_gradient(j, 0, dqt.T, dqt)
        hook(f"s{j}")

    values_back(1)
    values_back(0)
    scores_back(1)
    scores_back(0)

    def back_one(at):
        total = None
        for j in range(2):
            for c in range(3):
                d = g_s[pl.ds(at, BLOCK), (3 * j + c) * BLOCK : (3 * j + c) * BLOCK + quarter]
                term = dot(d, wq_s[j, c])
                total = term if total is None else total + term
        n2_s[pl.ds(at, BLOCK)] = total.astype(BF16)

    dm_copy.wait_send()
    loop(rows, BLOCK, back_one)
    hook("gn1")
    gn2_copy.wait_send()

    def back_one_sib(at):
        sb2[pl.ds(at, BLOCK)] = dot(back_s[pl.ds(count + at, BLOCK)], n2_s[...]).astype(BF16)

    def back_one_mine(at):
        mid_s[pl.ds(at, BLOCK)] = dot(back_s[pl.ds(at, BLOCK)], n2_s[...])

    loop(count, BLOCK, back_one_sib)
    gn1_copy = remote(sb2, rb2, csem, 7, sib)
    loop(count, BLOCK, back_one_mine)
    hook("gn1b")
    gn1_copy.wait_recv()
    mlp_copy.wait_send()

    def first_back(at):
        spot = pl.ds(at, 64)
        xhat, sigma = norm_stats(sin_s[spot])
        grad = mid_s[spot] + rb2[spot].astype(F32)
        sb1[spot] = (gm_s[spot] + norm_back(grad, ln1_gain, xhat, sigma)).astype(BF16)
        sm[0:1] += column_sum(grad * xhat)
        sm[1:2] += column_sum(grad)

    loop(count, 64, first_back)
    put_in = local(sb1, ing_h)

    state = {}

    def small_start(i):
        if i == 0:
            state["c"] = remote(sm, smr.at[0], ssem, 0, sib)
        elif i == 1:
            state["c"] = remote(sm, smr.at[1], ssem, 1, across)
        else:
            state["c"] = remote(sm.at[pl.ds(0, 16)], smr.at[i, pl.ds(0, 16)], ssem, i, mates[all_bits[i - 2]])
        state["i"] = i

    def small_step():
        i = state["i"]
        state["c"].wait()
        if i == 0:
            sm[0:8] = sm[0:8] + smr[0, 0:8]
        elif i == 1:
            sm[0:8] = sm[0:8] + smr[1, 0:8]
            sm[8:16] = sm[8:16] + smr[1, 16:24]
        else:
            sm[0:16] = sm[0:16] + smr[i, 0:16]
        if i + 1 < 2 + len(all_bits):
            small_start(i + 1)
        else:
            small_o[...] = sm[0:16]

    small_start(0)
    small_left = 2 + len(all_bits)
    for i in PLAN["tail"]:
        if i >= 0:
            chunks[i].advance()
        elif small_left:
            small_step()
            small_left -= 1
    while True:
        busy = False
        for chunk in chunks:
            if chunk.copy is not None:
                chunk.advance()
                busy = True
        if small_left:
            small_step()
            small_left -= 1
            busy = True
        if not busy:
            break

    for copy in [unit_copy, head_copy, n1_copy, cot_copy, gn1_copy] + by_x + by_y:
        copy.wait_send()
    for chunk in chunks:
        for copy in chunk.sent:
            copy.wait_send()
        chunk.done.wait()
    put_out.wait()
    put_in.wait()


def call_layer(dp_size, tokens, cotangent, ids, table, vectors, wq, wo, w1, w2):
    count, width = tokens.shape
    rows = 2 * count
    quarter = wo.shape[0]
    units = w1.shape[1]
    heads = quarter // HEAD
    grad_rows = units + width + 4 * quarter
    bits = [b for b in range(20) if (1 << b) < dp_size]
    half_bits = bits[:3]
    shape = jax.ShapeDtypeStruct
    vm = pltpu.VMEM
    regions = 2 * (units // BLOCK) + 4
    steps = 1 + 2 * len(half_bits) + len(bits) - len(half_bits)
    fetched = 4 + 2 * (units // BLOCK)
    scratch = (
        [vm((count, width), BF16), vm((rows, width), BF16)]
        + [vm((count, width), F32)] * 3
        + [vm((rows, width), BF16)] * 2
        + [vm((width, rows), BF16)]
        + [vm((2,) + wq.shape, BF16), vm((2 * quarter, width), BF16), vm((2,) + w1.shape, BF16), vm((2,) + w2.shape, BF16)]
        + [vm((2, rows, 256), BF16)] * 2
        + [vm((2 * quarter, rows), BF16)] * 4
        + [vm((8, rows), F32)] * 2
        + [vm((2 * heads, 2, count, count), BF16)]
        + [vm((rows, rows), BF16)] * 2
        + [vm((rows, width), BF16)]
        + [vm((rows, 2 * units), BF16)] * 2
        + [vm((count, width), BF16)] * 4
        + [vm((grad_rows, width), BF16)] * 3
        + [vm((grad_rows >> (i + 1), width), BF16) for i in range(len(half_bits))]
        + [vm((grad_rows >> len(half_bits), width), BF16)] * (len(bits) - len(half_bits))
        + [vm((units,), F32), vm((2, quarter), F32), vm((24, width), F32), vm((2 + len(bits), 24, width), F32)]
        + [pltpu.SemaphoreType.DMA((8 + regions,))]
        + [pltpu.SemaphoreType.DMA((2, n)) for n in (2 * fetched + 2, 8, regions * steps, 2 + len(bits))]
    )
    anywhere = pl.BlockSpec(memory_space=pl.ANY)
    inside = pl.BlockSpec(memory_space=pltpu.VMEM)
    return pl.pallas_call(
        functools.partial(layer, dp_size, half_bits),
        out_shape=[shape((count, width), BF16)] * 2
        + [shape(w2.shape, BF16), shape(w1.shape, BF16), shape(wo.shape, BF16), shape(wq.shape, BF16), shape((16, width), F32)],
        in_specs=[anywhere] * 2 + [inside] * (2 + len(vectors)) + [anywhere] * 4,
        out_specs=[anywhere] * 6 + [inside],
        scratch_shapes=scratch,
        compiler_params=pltpu.CompilerParams(vmem_limit_bytes=VMEM_LIMIT, collective_id=0, has_side_effects=True),
        name="layer",
    )(tokens, cotangent, ids, table, *vectors, wq, wo, w1, w2)


def finish(out, ing, g2, g1, go, gq, small, out_o, ing_o, g2_o, g1_o, go_o, gq_o, a0, a1, a2, a3, a4, a5, units_o, heads_o):
    for src, dst in ((out, out_o), (ing, ing_o), (g2, g2_o), (g1, g1_o), (go, go_o), (gq, gq_o)):
        dst[...] = src[...].astype(dst.dtype)

    @pl.when(pl.program_id(0) == 0)
    def _():
        for i, ref in enumerate((a0, a1, a2, a3, a4, a5)):
            ref[...] = small[i]
        units_o[...] = small[8, : units_o.shape[0]]
        heads_o[...] = small[9:11, : heads_o.shape[1]]


def call_finish(arrays, small, units, quarter):
    steps = 4
    width = small.shape[1]
    shape = jax.ShapeDtypeStruct

    def rows_of(a):
        axis = a.ndim - 2
        block = a.shape[:axis] + (a.shape[axis] // steps,) + a.shape[axis + 1 :]
        return pl.BlockSpec(block, lambda i, axis=axis, rank=a.ndim: tuple(i if k == axis else 0 for k in range(rank)))

    def whole(extent):
        return pl.BlockSpec(extent, lambda i, rank=len(extent): (0,) * rank)

    extents = [(width,)] * 6 + [(units,), (2, quarter)]
    kinds = [BF16, BF16, F32, F32, F32, F32]
    return pl.pallas_call(
        finish,
        grid=(steps,),
        in_specs=[rows_of(a) for a in arrays] + [whole(small.shape)],
        out_specs=[rows_of(a) for a in arrays] + [whole(e) for e in extents],
        out_shape=[shape(a.shape, k) for a, k in zip(arrays, kinds)] + [shape(e, F32) for e in extents],
        compiler_params=pltpu.CompilerParams(vmem_limit_bytes=VMEM_LIMIT),
        name="finish",
    )(*arrays, small)


def per_device(
    tokens, segment_ids, ln1_gain, ln1_bias, qkv_weight, qv_bias, out_weight, out_bias,
    ln2_gain, ln2_bias, fc1_weight, fc1_bias, fc2_weight, fc2_bias, cotangent,
):
    width = tokens.shape[1]
    freq_count = width // 6
    frequency = 10000.0 ** (-jnp.arange(freq_count, dtype=F32) / freq_count)
    angles = jnp.arange(SIDE, dtype=F32)[:, None] * frequency[None, :]
    table = jnp.concatenate([jnp.sin(angles), jnp.cos(angles)], axis=1)
    vectors = (ln1_gain, ln1_bias, out_bias, ln2_gain, ln2_bias, fc2_bias, fc1_bias, qv_bias)
    *arrays, small = call_layer(
        lax.axis_size("dp"), tokens, cotangent, segment_ids, table, vectors, qkv_weight.transpose(0, 2, 1), out_weight, fc1_weight, fc2_weight
    )
    out, ing, g2, g1, go, gq, a0, a1, a2, a3, a4, a5, g_units, g_heads = call_finish(arrays, small, fc1_weight.shape[1], out_weight.shape[0])
    return (out, ing, a0, a1, gq.transpose(0, 2, 1), g_heads, go, a2, a3, a4, g1, g_units, g2, a5)


def solution(mesh):
    placed = (
        P(("dp", "tensor"), None),
        P("dp", None),
        P(),
        P(),
        P(None, None, "tensor"),
        P(None, "tensor"),
        P("tensor", None),
        P(),
        P(),
        P(),
        P(None, "tensor"),
        P("tensor"),
        P("tensor", None),
        P(),
        P(("dp", "tensor"), None),
    )
    return jax.shard_map(
        per_device,
        mesh=mesh,
        in_specs=placed,
        out_specs=(
            P(("dp", "tensor"), None),
            P(("dp", "tensor"), None),
            P(),
            P(),
            P(None, None, "tensor"),
            P(None, "tensor"),
            P("tensor", None),
            P(),
            P(),
            P(),
            P(None, "tensor"),
            P("tensor"),
            P("tensor", None),
            P(),
        ),
        check_vma=False,
    )
```

```python
import functools

import jax
import jax.numpy as jnp
from jax import lax
from jax.experimental import pallas as pl
from jax.experimental.pallas import tpu as pltpu
from jax.sharding import PartitionSpec as P

HEAD = 64
SIDE = 16
EPSILON = 1e-06
NEG_LARGE = -1e30
SCALE = HEAD ** (-0.5)
F32 = jnp.float32
BF16 = jnp.bfloat16
VMEM_LIMIT = 64 * 1024 * 1024 - 128 * 1024
MESH = pl.DeviceIdType.MESH
BLOCK = 256
KINDS = {
    "A": (None, ((0,), (1,), (2,))),
    "B": (None, ((1,), (0,), (2,))),
    "D": (None, ((0,), (1, 2))),
    "E": (None, ((0, 1, 2),)),
    "Y": (0, ((1,), (2,))),
    "Z": (1, ((0,), (2,))),
    "YD": (0, ((1, 2),)),
}
ORDERS = ("Z", "E", "E", "YD", "A", "A", "B", "D", "D", "B")
PLAN = {
    "f01": (1, 0),
    "f02": (2,),
    "gn2": (3, 0),
    "gn2b": (1,),
    "ln2": (4,),
    "fin": (0, 2),
    "v0": (5, 4, 1, 3, 0),
    "b12": (4, 6),
    "s1": (5, 2),
    "b02": (9, 3, 6, 0),
    "s0": (5, 4),
    "gn1": (8, 6, 9),
    "gn1b": (0,),
    "tail": (3, 7, 5, 4, 8, 6, 9, -1, 0, -1, 5, 3, 4, -1, 8, 7, 6, -1, 9, 5, -1, 4, 8, 6, 7, 9, 5, 6, 8, 7, 9, 7, 9),
}


def dot(a, b):
    return jnp.dot(a, b, preferred_element_type=F32)


def dot_nt(a, b):
    return lax.dot_general(a, b, (((1,), (1,)), ((), ())), preferred_element_type=F32)


def dot_tn(a, b):
    return lax.dot_general(a, b, (((0,), (0,)), ((), ())), preferred_element_type=F32)


def lane_half(rows, upper):
    lanes = lax.broadcasted_iota(jnp.int32, (rows, 128), 1)
    return lanes >= HEAD if upper else lanes < HEAD


def head_lanes(ref, head, filler):
    tile = ref[:, 128 * (head // 2) : 128 * (head // 2) + 128]
    return jnp.where(lane_half(tile.shape[0], head % 2 == 1), tile, filler)


def gelu_pair(h):
    size = jnp.abs(h)
    t = 1.0 / (1.0 + (0.3275911 * 0.7071067811865476) * size)
    bell = jnp.exp(-0.5 * h * h)
    poly = ((((1.061405429 * t - 1.453152027) * t + 1.421413741) * t - 0.284496736) * t + 0.254829592) * t
    tail = 0.5 * poly * bell
    cdf = jnp.where(h < 0, tail, 1.0 - tail)
    return h * cdf, cdf + h * bell * 0.3989422804014327


def norm_stats(v):
    centred = v - jnp.mean(v, axis=-1, keepdims=True)
    sigma = lax.rsqrt(jnp.mean(centred * centred, axis=-1, keepdims=True) + EPSILON)
    return centred * sigma, sigma


def norm_back(grad, gain, xhat, sigma):
    g = grad * gain
    return sigma * (g - jnp.mean(g, axis=-1, keepdims=True) - xhat * jnp.mean(g * xhat, axis=-1, keepdims=True))


def column_sum(v):
    return jnp.sum(v, axis=0, keepdims=True)


def loop(count, step, body):
    def run(i, carry):
        body(pl.multiple_of(i * step, step))
        return carry

    lax.fori_loop(0, count // step, run, 0)


def layer(
    dp_size, half_bits,
    tok_h, cot_h, ids, table, gain1, bias1, bias_o, gain2, bias2, bias_f, bias_u, bias_qv, wq_h, wo_h, w1_h, w2_h,
    out_h, ing_h, g2_h, g1_h, go_h, gq_h, small_o,
    tok_s, cot_s, sin_s, mid_s, gm_s, n1_s, n2_s, n2t_s, wq_s, wo_s, w1_s, w2_s,
    q_s, v_s, kt_s, ot_s, ou_s, gt_s, r_s, in_s, e_s, roll_s, back_s, nr_s, a_s, g_s, sb1, sb2, rb1, rb2,
    own, oth, xr, land, land_both, *rest,
):
    rest = list(rest)
    full_bits = [b for b in range(20) if (1 << b) < dp_size and b not in half_bits]
    rx = [rest.pop(0) for _ in full_bits]
    uoth, voth, sm, smr, lsem, wsem, csem, gsem, ssem = rest

    count, width = tok_s.shape
    rows = 2 * count
    quarter = wo_h.shape[0]
    units = w1_h.shape[1]
    heads = quarter // HEAD
    place = lax.axis_index("tensor")
    dp = lax.axis_index("dp")
    chip = place // 2
    core = place % 2
    sib = {"tensor": chip * 2 + 1 - core}
    across = {"tensor": (1 - chip) * 2 + core}
    all_bits = list(half_bits) + full_bits
    sides = {b: (dp // (1 << b)) % 2 for b in all_bits}

    def mate(bits):
        return {"dp": dp + sum((1 - 2 * sides[b]) * (1 << b) for b in bits)}

    mates = {b: mate((b,)) for b in all_bits}
    groups = {(b,) for b in all_bits}
    for kind in ORDERS:
        for bits in KINDS[kind][1]:
            for mask in range(1, 1 << len(bits)):
                groups.add(tuple(b for k, b in enumerate(bits) if mask >> k & 1))

    barrier = pltpu.get_barrier_semaphore()
    partners = [sib, across] + [mate(bits) for bits in sorted(groups)]
    for partner in partners:
        pl.semaphore_signal(barrier, inc=1, device_id=partner, device_id_type=MESH)

    sq_s, sk_s, k_s = a_s.at[:, 0:128], a_s.at[:, 128:256], a_s.at[:, 256:512]
    local_used = [0]

    def local(src, dst):
        copy = pltpu.make_async_copy(src, dst, lsem.at[local_used[0]])
        local_used[0] += 1
        copy.start()
        return copy

    def remote(src, dst, sems, index, device):
        copy = pltpu.make_async_remote_copy(
            src_ref=src, dst_ref=dst, send_sem=sems.at[0, index], recv_sem=sems.at[1, index], device_id=device, device_id_type=MESH
        )
        copy.start()
        return copy

    get_tok = local(tok_h, tok_s)
    get_cot = local(cot_h, cot_s.at[pl.ds(0, count)])
    get_wq = local(wq_h, wq_s.at[0])
    get_wo = local(wo_h, wo_s.at[pl.ds(0, quarter)])
    get_w1 = local(w1_h, w1_s.at[0])
    get_w2 = local(w2_h, w2_s.at[0])

    part = sides[0]

    def half_of(extent):
        return pl.ds(pl.multiple_of(part * (extent // 2), 32), extent // 2)

    def columns(i):
        return pl.ds(i * BLOCK, BLOCK)

    wo_other = pl.ds(pl.multiple_of(quarter + part * (quarter // 2), 32), quarter // 2)
    pieces = [(wq_h.at[c, half_of(quarter)], wq_s.at[1, c, half_of(quarter)]) for c in range(3)]
    pieces.append((wo_h.at[half_of(quarter)], wo_s.at[wo_other]))
    for i in range(units // BLOCK):
        span = pl.ds(pl.multiple_of(i * BLOCK + part * (BLOCK // 2), 32), BLOCK // 2)
        pieces.append((w1_h.at[half_of(width), columns(i)], w1_s.at[1, half_of(width), columns(i)]))
        pieces.append((w2_h.at[span], w2_s.at[1, span]))

    ln1_gain, ln1_bias, out_bias, ln2_gain, ln2_bias, fc2_bias = (
        ref[...].reshape(1, width) for ref in (gain1, bias1, bias_o, gain2, bias2, bias_f)
    )
    get_tok.wait()

    def first_norm(at):
        plane = core * (count // (SIDE * SIDE)) + at // (SIDE * SIDE)
        line = (at // SIDE) % SIDE
        shape = (SIDE, width // 3)
        for k in range(4):
            spot = jnp.concatenate(
                [jnp.broadcast_to(table[pl.ds(plane, 1)], shape), jnp.broadcast_to(table[pl.ds(line + k, 1)], shape), table[...]], axis=1
            )
            span = pl.ds(pl.multiple_of(at + k * SIDE, SIDE), SIDE)
            stream = tok_s[span].astype(F32) + spot
            sin_s[span] = stream
            xhat, _ = norm_stats(stream)
            n1_s[span] = (xhat * ln1_gain + ln1_bias).astype(BF16)

    loop(count, 4 * SIDE, first_norm)
    doc = ids[pl.ds(chip, 1), :]
    starts = [jnp.zeros((1, 1), F32)]
    starts += [jnp.sum(jnp.where(doc < v, 1.0, 0.0), axis=1, keepdims=True) for v in range(1, 4)]
    starts.append(jnp.full((1, 1), rows, F32))
    turn = jnp.zeros((1, 1), F32)
    for v in range(4):
        turn += jnp.where(starts[v + 1] - starts[v] == count, starts[v], 0.0)
    turn_here = turn - (core * count).astype(F32)

    def wrapped(v):
        v = jnp.where(v >= rows, v - rows, v)
        return jnp.where(v < 0, v + rows, v)

    def rotations(at):
        down = (lax.broadcasted_iota(jnp.int32, (64, rows), 0) + at).astype(F32)
        along = lax.broadcasted_iota(jnp.int32, (64, rows), 1).astype(F32)
        roll_s[pl.ds(at, 64)] = jnp.where(wrapped(down + turn_here) == along, 1.0, 0.0).astype(BF16)
        back_s[pl.ds(at, 64)] = jnp.where(wrapped(down - turn_here) == along, 1.0, 0.0).astype(BF16)
        where = wrapped((lax.broadcasted_iota(jnp.int32, (64, 128), 0) + at).astype(F32) + turn)
        mine = sum(jnp.where(where >= starts[v], 1.0, 0.0) for v in range(1, 4))
        slot = (lax.broadcasted_iota(jnp.int32, (64, 128), 1) % HEAD).astype(F32)
        sq_s[pl.ds(at, 64)] = jnp.where((slot < 4) & (slot != mine), 1.0, 0.0).astype(BF16)
        sk_s[pl.ds(at, 64)] = jnp.where(slot == mine, NEG_LARGE, 0.0).astype(BF16)

    loop(rows, 64, rotations)

    pl.semaphore_wait(barrier, len(partners))
    unit_copy = remote(bias_u, uoth, wsem, 2 * len(pieces), across)
    head_copy = remote(bias_qv, voth, wsem, 2 * len(pieces) + 1, across)
    by_x = [remote(src, dst, wsem, i, across) for i, (src, dst) in enumerate(pieces)]
    by_y = [None] * len(pieces)

    def forward_weight(*which):
        for i in which:
            by_x[i].wait_recv()
            by_y[i] = remote(pieces[i][1], pieces[i][1], wsem, len(pieces) + i, mates[0])

    def have_weight(*which):
        for i in which:
            by_y[i].wait_recv()

    n1_copy = remote(n1_s.at[pl.ds(0, count)], n1_s.at[pl.ds(count, count)], csem, 0, sib)
    get_cot.wait()
    cot_copy = remote(cot_s.at[pl.ds(0, count)], cot_s.at[pl.ds(count, count)], csem, 1, sib)

    def rotate(at):
        nr_s[pl.ds(at, BLOCK)] = dot(roll_s[pl.ds(at, BLOCK)], n1_s[...]).astype(BF16)

    def project(j, at):
        n = nr_s[pl.ds(at, BLOCK)]
        biases = bias_qv if j == 0 else voth
        q = (dot_nt(n, wq_s[j, 0]) + biases[0:1]).astype(BF16) * SCALE
        k = dot_nt(n, wq_s[j, 1]).astype(BF16)
        v = (dot_nt(n, wq_s[j, 2]) + biases[1:2]).astype(BF16)
        q_s[j, pl.ds(at, BLOCK), :quarter] = q
        k_s[pl.ds(at, BLOCK), :quarter] = k
        v_s[j, pl.ds(at, BLOCK), :quarter] = v
        kt_s[j * quarter : (j + 1) * quarter, pl.ds(at, BLOCK)] = k.T * SCALE

    blocks = [(b, at) for b in range(2) for at in range(0, count, BLOCK)]

    def attend(j, service):
        vt = v_s[j, :, :quarter].T
        for head in range(heads):
            qh = head_lanes(q_s.at[j], head, sq_s[...])
            kh = head_lanes(k_s, head, sk_s[...])
            span = slice(head * HEAD, head * HEAD + HEAD)
            to = slice(j * quarter + head * HEAD, j * quarter + head * HEAD + HEAD)

            def scores(b, at):
                return dot_nt(kh[b * count : (b + 1) * count], qh[b * count + at : b * count + at + BLOCK])

            later = scores(*blocks[0])
            for i, (b, at) in enumerate(blocks):
                s = later
                if i + 1 < len(blocks):
                    later = scores(*blocks[i + 1])
                m = jnp.max(s, axis=0, keepdims=True)
                e = jnp.exp(s - m)
                r = 1.0 / column_sum(e)
                low = e.astype(BF16)
                here = slice(b * count + at, b * count + at + BLOCK)
                e_s[j * heads + head, b, :, at : at + BLOCK] = low
                ot_s[to, here] = (dot(vt[span, b * count : (b + 1) * count], low) * r).astype(BF16)
                r_s[j * heads + head : j * heads + head + 1, here] = r
            service[head]()

    get_wq.wait()
    n1_copy.wait_recv()
    loop(rows, BLOCK, rotate)
    loop(rows, BLOCK, lambda at: project(0, at))
    nothing = lambda: None
    forward_weight(0, 1)
    attend(0, [lambda: forward_weight(2), lambda: forward_weight(3), nothing])
    head_copy.wait_recv()
    have_weight(0, 1, 2)
    loop(rows, BLOCK, lambda at: project(1, at))
    attend(1, [lambda: forward_weight(4), lambda: forward_weight(5), nothing])

    get_wo.wait()
    have_weight(3)

    def unrotate(at):
        ou_s[:, pl.ds(at, BLOCK)] = dot(ot_s[...], roll_s[:, pl.ds(at, BLOCK)]).astype(BF16)

    loop(rows, BLOCK, unrotate)

    def out_part(at):
        return dot_tn(ou_s[:, pl.ds(at, BLOCK)], wo_s[...])

    def out_sib(at):
        sb1[pl.ds(at, BLOCK)] = out_part(count + at).astype(BF16)

    loop(count, BLOCK, out_sib)
    att_copy = remote(sb1, rb1, csem, 2, sib)

    def out_mine(at):
        mid_s[pl.ds(at, BLOCK)] = sin_s[pl.ds(at, BLOCK)] + out_part(at) + out_bias

    loop(count, BLOCK, out_mine)
    att_copy.wait_recv()

    def second_norm(at):
        spot = pl.ds(at, 64)
        mid = mid_s[spot] + rb1[spot].astype(F32)
        mid_s[spot] = mid
        xhat, _ = norm_stats(mid)
        n2 = (xhat * ln2_gain + ln2_bias).astype(BF16)
        n2_s[spot] = n2

    loop(count, 64, second_norm)
    n2_copy = remote(n2_s.at[pl.ds(0, count)], n2_s.at[pl.ds(count, count)], csem, 3, sib)

    forward_weight(6)

    base_a = units + width
    parts = units // BLOCK
    steps = copies_of(len(full_bits))

    class Region:
        def __init__(self, index, row, size, col, cols, slot, kind):
            self.place = self.now = (row, size, col, cols)
            self.index, self.slot, self.used = index, slot, 0
            self.first, self.after = KINDS[kind]
            self.stages = [] if self.first is None else ["first"]
            self.stages += ["x"] + [("halve", bits) for bits in self.after] + [("full", i) for i in range(len(full_bits))]
            self.last_sum = len(self.stages) - 1
            self.stages += [("gather", bits) for bits in reversed(self.after)]
            if self.first is not None:
                self.stages.append(("gather", (self.first,)))
            self.stage, self.flying, self.sent, self.trail = -1, [], [], []
            self.parts, self.slots_used = 8, 0
            self.finished = False

        def window(self, where):
            row, size, col, cols = where
            return pl.ds(row, size), pl.ds(col, cols)

        def go(self, src, src_at, dst, dst_at, device):
            copy = remote(src.at[self.window(src_at)], dst.at[self.window(dst_at)], gsem, self.index * steps + self.used, device)
            self.used += 1
            self.flying.append(copy)
            self.sent.append(copy)

        def cut(self, where, side):
            row, size, col, cols = where
            if (size // 2) % 16 == 0:
                return pl.multiple_of(row + side * (size // 2), 16), size // 2, col, cols
            return row, size, pl.multiple_of(col + side * (cols // 2), 128), cols // 2

        def piece(self, bits, mask):
            where = self.now
            for k, b in enumerate(bits):
                where = self.cut(where, 1 - sides[b] if mask >> k & 1 else sides[b])
            return where

        def landing(self, at, parts_here):
            row, col, rows_one, cols_one = self.slot
            full = self.place[3]
            if cols_one == full:
                return row + at * rows_one, parts_here * rows_one, col, full
            if parts_here == 1:
                return row + at // 2 * rows_one, rows_one, col + at % 2 * cols_one, cols_one
            return row + at // 2 * rows_one, parts_here // 2 * rows_one, col, full

        def ready(self, j):
            if self.first is not None:
                self.stage = 0
                give = self.piece((self.first,), 1)
                if j == 0:
                    self.go(own, give, land, self.landing(0, 4), mates[self.first])
                else:
                    row, size, col, cols = self.place
                    self.both = (row // 2, size // 2, col, cols)
                    self.go(oth, give, land_both, self.both, mates[self.first])
            elif j == 1:
                self.stage = 0
                self.go(oth, self.now, xr, self.now, across)

        def add(self, into, base, where, *terms):
            row, size, col, cols = where
            step = 64 if size % 64 == 0 else 48 if size % 48 == 0 else 32

            def body(off):
                to = (pl.ds(pl.multiple_of(row + off, 16), step), pl.ds(col, cols))
                total = base[to].astype(F32)
                for ref, (r, _, c, _) in terms:
                    total += ref[pl.ds(pl.multiple_of(r + off, 16), step), pl.ds(c, cols)].astype(F32)
                into[to] = total.astype(BF16)

            loop(size, step, body)

        def finish_stage(self):
            what = self.stages[self.stage]
            dest = xr if self.stage == self.last_sum else own
            if what == "first":
                keep = self.piece((self.first,), 0)
                self.add(own, own, keep, (land, self.landing(0, 4)))
                self.add(oth, oth, keep, (land_both, self.both))
                self.trail.append(((self.first,), keep))
                self.now, self.parts, self.slots_used = keep, 4, 4
            elif what == "x":
                self.add(dest, own, self.now, (xr, self.now))
            elif what[0] == "halve":
                self.add(dest, own, self.keep, *[(land, at) for at in self.landed])
                self.trail.append((what[1], self.keep))
                self.now = self.keep
            elif what[0] == "full":
                for copy in self.flying:
                    copy.wait_send()
                    self.sent = [c for c in self.sent if c is not copy]
                self.add(dest, own, self.now, (rx[what[1]], self.small_place()))

        def small_place(self):
            row, col, rows_one, cols_one = self.slot
            if row < 7 * units // 8:
                return row // 7, rows_one, col, cols_one
            if cols_one == self.place[3]:
                return units // 8, rows_one, col, cols_one
            k = (self.place[0] - base_a) // quarter
            return (units + width) // 8 + k // 2 * rows_one, rows_one, k % 2 * cols_one, cols_one

        def start_stage(self):
            what = self.stages[self.stage]
            if what == "x":
                self.go(oth, self.now, xr, self.now, across)
            elif what[0] == "halve":
                bits = what[1]
                self.parts >>= len(bits)
                self.keep = self.piece(bits, 0)
                self.landed = []
                for mask in range(1, 1 << len(bits)):
                    there = self.landing(self.slots_used, self.parts)
                    self.slots_used += self.parts
                    self.landed.append(there)
                    to = mate([b for k, b in enumerate(bits) if mask >> k & 1])
                    self.go(own, self.piece(bits, mask), land, there, to)
            elif what[0] == "full":
                self.go(own, self.now, rx[what[1]], self.small_place(), mates[full_bits[what[1]]])
            else:
                bits, keep = self.trail.pop()
                for mask in range(1, 1 << len(bits)):
                    self.go(xr, keep, xr, keep, mate([b for k, b in enumerate(bits) if mask >> k & 1]))

        def advance(self):
            if self.finished or self.stage < 0:
                return
            for copy in self.flying:
                copy.wait_recv()
            self.finish_stage()
            self.flying = []
            self.stage += 1
            if self.stage < len(self.stages):
                self.start_stage()
                return
            self.finished = True
            row, size, col, cols = self.place
            if row < units:
                to = g2_h.at[pl.ds(row, size)]
            elif row < base_a:
                to = g1_h.at[:, pl.ds(col, cols)]
            elif row == base_a:
                to = go_h
            else:
                to = gq_h.at[(row - base_a) // quarter - 1]
            self.done = local(xr.at[self.window(self.place)], to)

    chunks = []
    low = 7 * units // 8
    for i in range(parts):
        slot = (i * 7 * (BLOCK // 8), 0, BLOCK // 8, width)
        chunks.append(Region(2 * i, i * BLOCK, BLOCK, 0, width, slot, ORDERS[2 * i]))
        slot = (low, i * BLOCK, width // 8, BLOCK)
        chunks.append(Region(2 * i + 1, units, width, i * BLOCK, BLOCK, slot, ORDERS[2 * i + 1]))
    low += 7 * width // 8
    for i in range(4):
        slot = (low + i * quarter, 0, quarter // 4, width // 2)
        chunks.append(Region(2 * parts + i, base_a + i * quarter, quarter, 0, width, slot, ORDERS[2 * parts + i]))
    first_att = 2 * parts

    def ready(i, j):
        chunks[i].ready(j)

    def hook(name):
        for i in PLAN.get(name, ()):
            chunks[i].advance()

    get_w1.wait()
    get_w2.wait()

    def chunk_rows(j, i, at):
        span = pl.ds(at, BLOCK)
        cols = slice(j * units + i * BLOCK, j * units + (i + 1) * BLOCK)
        mine = slice(i * BLOCK, (i + 1) * BLOCK)
        bias = (bias_u if j == 0 else uoth)[mine].reshape(1, BLOCK)
        h = dot(n2_s[span], w1_s[j, :, mine]) + bias
        a, slope = gelu_pair(h)
        a_s[span, cols] = a.astype(BF16)
        g = (dot_nt(cot_s[span], w2_s[j, mine]) * slope).astype(BF16)
        g_s[span, cols] = g

    def chunk_grads(j, i):
        cols = slice(j * units + i * BLOCK, j * units + (i + 1) * BLOCK)
        mine = slice(i * BLOCK, (i + 1) * BLOCK)
        to = oth if j == 1 else own
        to[i * BLOCK : (i + 1) * BLOCK] = dot_tn(a_s[:, cols], cot_s[...]).astype(BF16)
        ready(2 * i, j)
        g = g_s[:, cols]
        to[units : units + width, mine] = dot(n2t_s[...], g).astype(BF16)
        ready(2 * i + 1, j)
        sm[8 + 8 * j : 9 + 8 * j, mine] = column_sum(g.astype(F32))
        hook(f"f{j}{i}")

    def feed(j, i, first=False):
        if first:
            for at in range(0, count, BLOCK):
                chunk_rows(j, i, at)
            n2_copy.wait_recv()
            cot_copy.wait_recv()
            for at in range(0, rows, BLOCK):
                n2t_s[:, at : at + BLOCK] = n2_s[at : at + BLOCK].T
            for at in range(count, rows, BLOCK):
                chunk_rows(j, i, at)
        else:
            for at in range(0, rows, BLOCK):
                chunk_rows(j, i, at)
        chunk_grads(j, i)

    sm[...] = jnp.zeros_like(sm)
    unit_copy.wait_recv()
    have_weight(4, 5)
    feed(1, 0, first=True)
    forward_weight(7)
    feed(0, 0)
    have_weight(6, 7)
    forward_weight(8)
    feed(1, 1)
    forward_weight(9)
    feed(0, 1)
    for i in range(2, parts):
        have_weight(4 + 2 * i, 5 + 2 * i)
        feed(1, i)
        feed(0, i)

    def back_two(at):
        span = pl.ds(at, BLOCK)
        return dot_nt(g_s[span, :units], w1_s[0]) + dot_nt(g_s[span, units:], w1_s[1])

    def mlp_part(at):
        span = pl.ds(at, BLOCK)
        return dot(a_s[span, :units], w2_s[0]) + dot(a_s[span, units:], w2_s[1])

    def back_two_sib(at):
        sb2[pl.ds(at, BLOCK)] = back_two(count + at).astype(BF16)

    def back_two_mine(at):
        gm_s[pl.ds(at, BLOCK)] = back_two(at)

    def mlp_sib(at):
        sb1[pl.ds(at, BLOCK)] = mlp_part(count + at).astype(BF16)

    loop(count, BLOCK, back_two_sib)
    gn2_copy = remote(sb2, rb2, csem, 4, sib)
    loop(count, BLOCK, back_two_mine)
    hook("gn2")
    att_copy.wait_send()
    loop(count, BLOCK, mlp_sib)
    mlp_copy = remote(sb1, rb1, csem, 5, sib)
    hook("gn2b")
    gn2_copy.wait_recv()
    n2_copy.wait_send()

    def second_back(at):
        spot = pl.ds(at, 64)
        xhat, sigma = norm_stats(mid_s[spot])
        grad = gm_s[spot] + rb2[spot].astype(F32)
        cot = cot_s[spot].astype(F32)
        back = cot + norm_back(grad, ln2_gain, xhat, sigma)
        gm_s[spot] = back
        n2_s[spot] = back.astype(BF16)
        sm[2:3] += column_sum(back)
        sm[3:4] += column_sum(grad * xhat)
        sm[4:5] += column_sum(grad)
        sm[5:6] += column_sum(cot)

    loop(count, 64, second_back)
    dm_copy = remote(n2_s.at[pl.ds(0, count)], n2_s.at[pl.ds(count, count)], csem, 6, sib)

    hook("ln2")

    def finish_out(at):
        span = pl.ds(at, BLOCK)
        mid_s[span] = mid_s[span] + mlp_part(at) + fc2_bias

    loop(count, BLOCK, finish_out)
    mlp_copy.wait_recv()

    def write_out(at):
        spot = pl.ds(at, 64)
        tok_s[spot] = (mid_s[spot] + rb1[spot].astype(F32)).astype(BF16)

    loop(count, 64, write_out)
    put_out = local(tok_s, out_h)
    hook("fin")
    dm_copy.wait_recv()

    zero = jnp.zeros((rows, 128), BF16)
    start = base_a + quarter

    def lanes_of(total):
        return jnp.concatenate([total[0], total[1]], axis=1)[:, :quarter].astype(BF16)

    def keep_gradient(j, c, d, dt):
        to = oth if j == 1 else own
        g_s[:, (3 * j + c) * BLOCK : (3 * j + c) * BLOCK + quarter] = d
        to[start + c * quarter : start + (c + 1) * quarter] = dot(dt, nr_s[...]).astype(BF16)
        ready(first_att + 1 + c, j)
        if c != 1:
            sm[9 + c // 2 + 8 * j : 10 + c // 2 + 8 * j, :quarter] = column_sum(d.astype(F32))

    def both_blocks(parts_of):
        return jnp.concatenate([parts_of(0), parts_of(1)], axis=0)

    def values_back(j):
        base = j * quarter
        to = oth if j == 1 else own
        dm = n2_s[...]
        to[base_a : base_a + quarter] = dot(ou_s[base : base + quarter], dm).astype(BF16)
        ready(first_att, j)
        grad_t = dot_nt(wo_s[base : base + quarter], dm).astype(BF16)
        grad_t = dot_nt(grad_t, roll_s[...])
        scaled = []
        for head in range(heads):
            span = slice(head * HEAD, head * HEAD + HEAD)
            row = j * heads + head
            r = r_s[row : row + 1]
            g = grad_t[span]
            in_s[row : row + 1] = column_sum(g * ot_s[base + head * HEAD : base + head * HEAD + HEAD].astype(F32)) * r
            scaled.append((g * r).astype(BF16))
        gt = jnp.concatenate(scaled, axis=0)
        gt_s[base : base + quarter] = gt
        go_s = a_s.at[:, rows + 256 * j : rows + 256 * (j + 1)]
        go_s[:, :quarter] = gt.T
        dv = [None, None]
        for head in range(heads):
            gh = head_lanes(go_s, head, zero)
            part = both_blocks(lambda b: dot(e_s[j * heads + head, b], gh[b * count : (b + 1) * count]))
            tile = head // 2
            dv[tile] = part if dv[tile] is None else dv[tile] + part
        dv = lanes_of(dv)
        keep_gradient(j, 2, dv, dv.T)
        hook(f"v{j}")

    def scores_back(j):
        base = j * quarter
        dq, dk = [], [None, None]
        for head in range(heads):
            tile = head // 2
            row = j * heads + head
            vh = head_lanes(v_s.at[j], head, zero)
            qh = head_lanes(q_s.at[j], head, zero)
            last_row = min(128 * tile + 128, quarter)
            gth = gt_s[base + 128 * tile : base + last_row]
            vh = vh[:, : gth.shape[0]]
            ds = a_s.at[:, (head % 2) * count : (head % 2 + 1) * count]
            for b, at in blocks:
                here = slice(b * count + at, b * count + at + BLOCK)
                dp_t = dot(vh[b * count : (b + 1) * count], gth[:, here])
                grad = (dp_t - in_s[row : row + 1, here]) * e_s[row, b, :, at : at + BLOCK].astype(F32)
                ds[b * count : (b + 1) * count, at : at + BLOCK] = grad.astype(BF16)
            part = both_blocks(lambda b: dot(ds[b * count : (b + 1) * count], qh[b * count : (b + 1) * count]))
            dk[tile] = part if dk[tile] is None else dk[tile] + part
            kth = kt_s.at[base + head * HEAD : base + head * HEAD + HEAD]
            dq.append(
                jnp.concatenate(
                    [dot(kth[:, b * count : (b + 1) * count], ds[b * count : (b + 1) * count]) for b in range(2)], axis=1
                )
            )
            hook(f"b{j}{head}")
        dk = lanes_of(dk)
        keep_gradient(j, 1, dk, dk.T)
        dqt = jnp.concatenate(dq, axis=0).astype(BF16)
        keep_gradient(j, 0, dqt.T, dqt)
        hook(f"s{j}")

    values_back(1)
    values_back(0)
    scores_back(1)
    scores_back(0)

    def back_one(at):
        total = None
        for j in range(2):
            for c in range(3):
                d = g_s[pl.ds(at, BLOCK), (3 * j + c) * BLOCK : (3 * j + c) * BLOCK + quarter]
                term = dot(d, wq_s[j, c])
                total = term if total is None else total + term
        n2_s[pl.ds(at, BLOCK)] = total.astype(BF16)

    dm_copy.wait_send()
    loop(rows, BLOCK, back_one)
    hook("gn1")
    gn2_copy.wait_send()

    def back_one_sib(at):
        sb2[pl.ds(at, BLOCK)] = dot(back_s[pl.ds(count + at, BLOCK)], n2_s[...]).astype(BF16)

    def back_one_mine(at):
        mid_s[pl.ds(at, BLOCK)] = dot(back_s[pl.ds(at, BLOCK)], n2_s[...])

    loop(count, BLOCK, back_one_sib)
    gn1_copy = remote(sb2, rb2, csem, 7, sib)
    loop(count, BLOCK, back_one_mine)
    hook("gn1b")
    gn1_copy.wait_recv()
    mlp_copy.wait_send()

    def first_back(at):
        spot = pl.ds(at, 64)
        xhat, sigma = norm_stats(sin_s[spot])
        grad = mid_s[spot] + rb2[spot].astype(F32)
        sb1[spot] = (gm_s[spot] + norm_back(grad, ln1_gain, xhat, sigma)).astype(BF16)
        sm[0:1] += column_sum(grad * xhat)
        sm[1:2] += column_sum(grad)

    loop(count, 64, first_back)
    put_in = local(sb1, ing_h)

    state = {}

    def small_start(i):
        if i == 0:
            state["c"] = remote(sm, smr.at[0], ssem, 0, sib)
        elif i == 1:
            state["c"] = remote(sm, smr.at[1], ssem, 1, across)
        else:
            state["c"] = remote(sm.at[pl.ds(0, 16)], smr.at[i, pl.ds(0, 16)], ssem, i, mates[all_bits[i - 2]])
        state["i"] = i

    def small_step():
        i = state["i"]
        state["c"].wait()
        if i == 0:
            sm[0:8] = sm[0:8] + smr[0, 0:8]
        elif i == 1:
            sm[0:8] = sm[0:8] + smr[1, 0:8]
            sm[8:16] = sm[8:16] + smr[1, 16:24]
        else:
            sm[0:16] = sm[0:16] + smr[i, 0:16]
        if i + 1 < 2 + len(all_bits):
            small_start(i + 1)
        else:
            small_o[...] = sm[0:16]

    small_start(0)
    small_left = 2 + len(all_bits)
    for i in PLAN["tail"]:
        if i >= 0:
            chunks[i].advance()
        elif small_left:
            small_step()
            small_left -= 1
    while True:
        busy = False
        for chunk in chunks:
            if not chunk.finished:
                chunk.advance()
                busy = True
        if small_left:
            small_step()
            small_left -= 1
            busy = True
        if not busy:
            break

    for copy in [unit_copy, head_copy, n1_copy, cot_copy, gn1_copy] + by_x + by_y:
        copy.wait_send()
    for chunk in chunks:
        for copy in chunk.sent:
            copy.wait_send()
        chunk.done.wait()
    put_out.wait()
    put_in.wait()


def copies_of(full):
    most = 0
    for kind in ORDERS:
        first, after = KINDS[kind]
        most = max(most, 1 + full + 2 * sum((1 << len(bits)) - 1 for bits in after) + (0 if first is None else 3))
    return most


def call_layer(dp_size, tokens, cotangent, ids, table, vectors, wq, wo, w1, w2):
    count, width = tokens.shape
    rows = 2 * count
    quarter = wo.shape[0]
    units = w1.shape[1]
    heads = quarter // HEAD
    grad_rows = units + width + 4 * quarter
    bits = [b for b in range(20) if (1 << b) < dp_size]
    half_bits = bits[:3]
    shape = jax.ShapeDtypeStruct
    vm = pltpu.VMEM
    regions = 2 * (units // BLOCK) + 4
    steps = copies_of(len(bits) - len(half_bits))
    fetched = 4 + 2 * (units // BLOCK)
    scratch = (
        [vm((count, width), BF16), vm((rows, width), BF16)]
        + [vm((count, width), F32)] * 3
        + [vm((rows, width), BF16)] * 2
        + [vm((width, rows), BF16)]
        + [vm((2,) + wq.shape, BF16), vm((2 * quarter, width), BF16), vm((2,) + w1.shape, BF16), vm((2,) + w2.shape, BF16)]
        + [vm((2, rows, 256), BF16)] * 2
        + [vm((2 * quarter, rows), BF16)] * 4
        + [vm((8, rows), F32)] * 2
        + [vm((2 * heads, 2, count, count), BF16)]
        + [vm((rows, rows), BF16)] * 2
        + [vm((rows, width), BF16)]
        + [vm((rows, 2 * units), BF16)] * 2
        + [vm((count, width), BF16)] * 4
        + [vm((grad_rows, width), BF16)] * 3
        + [vm((7 * (units // 8 + width // 8) + 4 * quarter, width), BF16), vm(((units + width) // 2, width), BF16)]
        + [vm((grad_rows >> len(half_bits), width), BF16)] * (len(bits) - len(half_bits))
        + [vm((units,), F32), vm((2, quarter), F32), vm((24, width), F32), vm((2 + len(bits), 24, width), F32)]
        + [pltpu.SemaphoreType.DMA((8 + regions,))]
        + [pltpu.SemaphoreType.DMA((2, n)) for n in (2 * fetched + 2, 8, regions * steps, 2 + len(bits))]
    )
    anywhere = pl.BlockSpec(memory_space=pl.ANY)
    inside = pl.BlockSpec(memory_space=pltpu.VMEM)
    return pl.pallas_call(
        functools.partial(layer, dp_size, half_bits),
        out_shape=[shape((count, width), BF16)] * 2
        + [shape(w2.shape, BF16), shape(w1.shape, BF16), shape(wo.shape, BF16), shape(wq.shape, BF16), shape((16, width), F32)],
        in_specs=[anywhere] * 2 + [inside] * (2 + len(vectors)) + [anywhere] * 4,
        out_specs=[anywhere] * 6 + [inside],
        scratch_shapes=scratch,
        compiler_params=pltpu.CompilerParams(vmem_limit_bytes=VMEM_LIMIT, collective_id=0, has_side_effects=True),
        name="layer",
    )(tokens, cotangent, ids, table, *vectors, wq, wo, w1, w2)


def finish(out, ing, g2, g1, go, gq, small, out_o, ing_o, g2_o, g1_o, go_o, gq_o, a0, a1, a2, a3, a4, a5, units_o, heads_o):
    for src, dst in ((out, out_o), (ing, ing_o), (g2, g2_o), (g1, g1_o), (go, go_o), (gq, gq_o)):
        dst[...] = src[...].astype(dst.dtype)

    @pl.when(pl.program_id(0) == 0)
    def _():
        for i, ref in enumerate((a0, a1, a2, a3, a4, a5)):
            ref[...] = small[i]
        units_o[...] = small[8, : units_o.shape[0]]
        heads_o[...] = small[9:11, : heads_o.shape[1]]


def call_finish(arrays, small, units, quarter):
    steps = 4
    width = small.shape[1]
    shape = jax.ShapeDtypeStruct

    def rows_of(a):
        axis = a.ndim - 2
        block = a.shape[:axis] + (a.shape[axis] // steps,) + a.shape[axis + 1 :]
        return pl.BlockSpec(block, lambda i, axis=axis, rank=a.ndim: tuple(i if k == axis else 0 for k in range(rank)))

    def whole(extent):
        return pl.BlockSpec(extent, lambda i, rank=len(extent): (0,) * rank)

    extents = [(width,)] * 6 + [(units,), (2, quarter)]
    kinds = [BF16, BF16, F32, F32, F32, F32]
    return pl.pallas_call(
        finish,
        grid=(steps,),
        in_specs=[rows_of(a) for a in arrays] + [whole(small.shape)],
        out_specs=[rows_of(a) for a in arrays] + [whole(e) for e in extents],
        out_shape=[shape(a.shape, k) for a, k in zip(arrays, kinds)] + [shape(e, F32) for e in extents],
        compiler_params=pltpu.CompilerParams(vmem_limit_bytes=VMEM_LIMIT),
        name="finish",
    )(*arrays, small)


def per_device(
    tokens, segment_ids, ln1_gain, ln1_bias, qkv_weight, qv_bias, out_weight, out_bias,
    ln2_gain, ln2_bias, fc1_weight, fc1_bias, fc2_weight, fc2_bias, cotangent,
):
    width = tokens.shape[1]
    freq_count = width // 6
    frequency = 10000.0 ** (-jnp.arange(freq_count, dtype=F32) / freq_count)
    angles = jnp.arange(SIDE, dtype=F32)[:, None] * frequency[None, :]
    table = jnp.concatenate([jnp.sin(angles), jnp.cos(angles)], axis=1)
    vectors = (ln1_gain, ln1_bias, out_bias, ln2_gain, ln2_bias, fc2_bias, fc1_bias, qv_bias)
    *arrays, small = call_layer(
        lax.axis_size("dp"), tokens, cotangent, segment_ids, table, vectors, qkv_weight.transpose(0, 2, 1), out_weight, fc1_weight, fc2_weight
    )
    out, ing, g2, g1, go, gq, a0, a1, a2, a3, a4, a5, g_units, g_heads = call_finish(arrays, small, fc1_weight.shape[1], out_weight.shape[0])
    return (out, ing, a0, a1, gq.transpose(0, 2, 1), g_heads, go, a2, a3, a4, g1, g_units, g2, a5)


def solution(mesh):
    placed = (
        P(("dp", "tensor"), None),
        P("dp", None),
        P(),
        P(),
        P(None, None, "tensor"),
        P(None, "tensor"),
        P("tensor", None),
        P(),
        P(),
        P(),
        P(None, "tensor"),
        P("tensor"),
        P("tensor", None),
        P(),
        P(("dp", "tensor"), None),
    )
    return jax.shard_map(
        per_device,
        mesh=mesh,
        in_specs=placed,
        out_specs=(
            P(("dp", "tensor"), None),
            P(("dp", "tensor"), None),
            P(),
            P(),
            P(None, None, "tensor"),
            P(None, "tensor"),
            P("tensor", None),
            P(),
            P(),
            P(),
            P(None, "tensor"),
            P("tensor"),
            P("tensor", None),
            P(),
        ),
        check_vma=False,
    )
```

```python
import functools

import jax
import jax.numpy as jnp
from jax import lax
from jax.experimental import pallas as pl
from jax.experimental.pallas import tpu as pltpu
from jax.sharding import PartitionSpec as P

HEAD = 64
SIDE = 16
EPSILON = 1e-06
NEG_LARGE = -1e30
SCALE = HEAD ** (-0.5)
F32 = jnp.float32
BF16 = jnp.bfloat16
VMEM_LIMIT = 64 * 1024 * 1024 - 128 * 1024
MESH = pl.DeviceIdType.MESH
BLOCK = 256
KINDS = {
    "A": (None, ((0,), (1,), (2,))),
    "B": (None, ((1,), (0,), (2,))),
    "D": (None, ((0,), (1, 2))),
    "E": (None, ((0, 1, 2),)),
    "Y": (0, ((1,), (2,))),
    "Z": (1, ((0,), (2,))),
    "YD": (0, ((1, 2),)),
}
ORDERS = ("Z", "E", "E", "YD", "A", "A", "B", "D", "D", "B")
PLAN = {
    "f01": (1, 0),
    "f02": (2,),
    "gn2": (3, 0),
    "gn2b": (1,),
    "ln2": (4,),
    "fin": (0, 2),
    "v0": (5, 4, 1, 3, 0),
    "b12": (4, 6),
    "s1": (5, 2),
    "b02": (9, 3, 6, 0),
    "s0": (5, 4),
    "gn1": (8, 6, 9),
    "gn1b": (0,),
    "tail": (3, 7, 5, 4, 8, 6, 9, -1, 0, -1, 5, 3, 4, -1, 8, 7, 6, -1, 9, 5, -1, 4, 8, 6, 7, 9, 5, 6, 8, 7, 9, 7, 9),
}


def dot(a, b):
    return jnp.dot(a, b, preferred_element_type=F32)


def dot_nt(a, b):
    return lax.dot_general(a, b, (((1,), (1,)), ((), ())), preferred_element_type=F32)


def dot_tn(a, b):
    return lax.dot_general(a, b, (((0,), (0,)), ((), ())), preferred_element_type=F32)


def lane_half(rows, upper):
    lanes = lax.broadcasted_iota(jnp.int32, (rows, 128), 1)
    return lanes >= HEAD if upper else lanes < HEAD


def head_lanes(ref, head, filler):
    tile = ref[:, 128 * (head // 2) : 128 * (head // 2) + 128]
    return jnp.where(lane_half(tile.shape[0], head % 2 == 1), tile, filler)


def gelu_pair(h):
    size = jnp.abs(h)
    t = 1.0 / (1.0 + (0.3275911 * 0.7071067811865476) * size)
    bell = jnp.exp(-0.5 * h * h)
    poly = ((((1.061405429 * t - 1.453152027) * t + 1.421413741) * t - 0.284496736) * t + 0.254829592) * t
    tail = 0.5 * poly * bell
    cdf = jnp.where(h < 0, tail, 1.0 - tail)
    return h * cdf, cdf + h * bell * 0.3989422804014327


def norm_stats(v):
    centred = v - jnp.mean(v, axis=-1, keepdims=True)
    sigma = lax.rsqrt(jnp.mean(centred * centred, axis=-1, keepdims=True) + EPSILON)
    return centred * sigma, sigma


def norm_back(grad, gain, xhat, sigma):
    g = grad * gain
    return sigma * (g - jnp.mean(g, axis=-1, keepdims=True) - xhat * jnp.mean(g * xhat, axis=-1, keepdims=True))


def column_sum(v):
    return jnp.sum(v, axis=0, keepdims=True)


def loop(count, step, body):
    def run(i, carry):
        body(pl.multiple_of(i * step, step))
        return carry

    lax.fori_loop(0, count // step, run, 0)


def layer(
    dp_size, half_bits,
    tok_h, cot_h, ids, table, gain1, bias1, bias_o, gain2, bias2, bias_f, bias_u, bias_qv, wq_h, wo_h, w1_h, w2_h,
    out_h, ing_h, g2_h, g1_h, go_h, gq_h, small_o,
    tok_s, cot_s, sin_s, mid_s, gm_s, n1_s, n2_s, n2t_s, wq_s, wo_s, w1_s, w2_s,
    q_s, v_s, kt_s, ot_s, ou_s, gt_s, r_s, in_s, e_s, roll_s, back_s, nr_s, a_s, g_s, sb1, sb2, rb1, rb2,
    own, oth, xr, land, land_both, own1, oth1, xr1, land1, land1_both, *rest,
):
    rest = list(rest)
    full_bits = [b for b in range(20) if (1 << b) < dp_size and b not in half_bits]
    rx = [rest.pop(0) for _ in full_bits]
    rx1 = [rest.pop(0) for _ in full_bits]
    uoth, voth, sm, smr, lsem, wsem, csem, gsem, ssem = rest

    count, width = tok_s.shape
    rows = 2 * count
    quarter = wo_h.shape[0]
    units = w1_h.shape[1]
    heads = quarter // HEAD
    place = lax.axis_index("tensor")
    dp = lax.axis_index("dp")
    chip = place // 2
    core = place % 2
    sib = {"tensor": chip * 2 + 1 - core}
    across = {"tensor": (1 - chip) * 2 + core}
    all_bits = list(half_bits) + full_bits
    sides = {b: (dp // (1 << b)) % 2 for b in all_bits}

    def mate(bits):
        return {"dp": dp + sum((1 - 2 * sides[b]) * (1 << b) for b in bits)}

    mates = {b: mate((b,)) for b in all_bits}
    groups = {(b,) for b in all_bits}
    for kind in ORDERS:
        for bits in KINDS[kind][1]:
            for mask in range(1, 1 << len(bits)):
                groups.add(tuple(b for k, b in enumerate(bits) if mask >> k & 1))

    barrier = pltpu.get_barrier_semaphore()
    partners = [sib, across] + [mate(bits) for bits in sorted(groups)]
    for partner in partners:
        pl.semaphore_signal(barrier, inc=1, device_id=partner, device_id_type=MESH)

    sq_s, sk_s, k_s = a_s.at[:, 0:128], a_s.at[:, 128:256], a_s.at[:, 256:512]
    local_used = [0]

    def local(src, dst):
        copy = pltpu.make_async_copy(src, dst, lsem.at[local_used[0]])
        local_used[0] += 1
        copy.start()
        return copy

    def remote(src, dst, sems, index, device):
        copy = pltpu.make_async_remote_copy(
            src_ref=src, dst_ref=dst, send_sem=sems.at[0, index], recv_sem=sems.at[1, index], device_id=device, device_id_type=MESH
        )
        copy.start()
        return copy

    get_tok = local(tok_h, tok_s)
    get_cot = local(cot_h, cot_s.at[pl.ds(0, count)])
    get_wq = local(wq_h, wq_s.at[0])
    get_wo = local(wo_h, wo_s.at[pl.ds(0, quarter)])
    get_w1 = [local(w1_h.at[:, pl.ds(i * BLOCK, BLOCK)], w1_s.at[0, i]) for i in range(units // BLOCK)]
    get_w2 = local(w2_h, w2_s.at[0])

    part = sides[0]

    def half_of(extent):
        return pl.ds(pl.multiple_of(part * (extent // 2), 32), extent // 2)

    wo_other = pl.ds(pl.multiple_of(quarter + part * (quarter // 2), 32), quarter // 2)
    pieces = [(wq_s.at[0, c, half_of(quarter)], wq_s.at[1, c, half_of(quarter)]) for c in range(3)]
    pieces.append((wo_s.at[half_of(quarter)], wo_s.at[wo_other]))
    for i in range(units // BLOCK):
        span = pl.ds(pl.multiple_of(i * BLOCK + part * (BLOCK // 2), 32), BLOCK // 2)
        pieces.append((w1_s.at[0, i, half_of(width)], w1_s.at[1, i, half_of(width)]))
        pieces.append((w2_s.at[0, span], w2_s.at[1, span]))

    ln1_gain, ln1_bias, out_bias, ln2_gain, ln2_bias, fc2_bias = (
        ref[...].reshape(1, width) for ref in (gain1, bias1, bias_o, gain2, bias2, bias_f)
    )
    get_tok.wait()

    def first_norm(at):
        plane = core * (count // (SIDE * SIDE)) + at // (SIDE * SIDE)
        line = (at // SIDE) % SIDE
        shape = (SIDE, width // 3)
        for k in range(4):
            spot = jnp.concatenate(
                [jnp.broadcast_to(table[pl.ds(plane, 1)], shape), jnp.broadcast_to(table[pl.ds(line + k, 1)], shape), table[...]], axis=1
            )
            span = pl.ds(pl.multiple_of(at + k * SIDE, SIDE), SIDE)
            stream = tok_s[span].astype(F32) + spot
            sin_s[span] = stream
            xhat, _ = norm_stats(stream)
            n1_s[span] = (xhat * ln1_gain + ln1_bias).astype(BF16)

    loop(count, 4 * SIDE, first_norm)
    doc = ids[pl.ds(chip, 1), :]
    starts = [jnp.zeros((1, 1), F32)]
    starts += [jnp.sum(jnp.where(doc < v, 1.0, 0.0), axis=1, keepdims=True) for v in range(1, 4)]
    starts.append(jnp.full((1, 1), rows, F32))
    turn = jnp.zeros((1, 1), F32)
    for v in range(4):
        turn += jnp.where(starts[v + 1] - starts[v] == count, starts[v], 0.0)
    turn_here = turn - (core * count).astype(F32)

    def wrapped(v):
        v = jnp.where(v >= rows, v - rows, v)
        return jnp.where(v < 0, v + rows, v)

    def rotations(at):
        down = (lax.broadcasted_iota(jnp.int32, (64, rows), 0) + at).astype(F32)
        along = lax.broadcasted_iota(jnp.int32, (64, rows), 1).astype(F32)
        roll_s[pl.ds(at, 64)] = jnp.where(wrapped(down + turn_here) == along, 1.0, 0.0).astype(BF16)
        back_s[pl.ds(at, 64)] = jnp.where(wrapped(down - turn_here) == along, 1.0, 0.0).astype(BF16)
        where = wrapped((lax.broadcasted_iota(jnp.int32, (64, 128), 0) + at).astype(F32) + turn)
        mine = sum(jnp.where(where >= starts[v], 1.0, 0.0) for v in range(1, 4))
        slot = (lax.broadcasted_iota(jnp.int32, (64, 128), 1) % HEAD).astype(F32)
        sq_s[pl.ds(at, 64)] = jnp.where((slot < 4) & (slot != mine), 1.0, 0.0).astype(BF16)
        sk_s[pl.ds(at, 64)] = jnp.where(slot == mine, NEG_LARGE, 0.0).astype(BF16)

    loop(rows, 64, rotations)

    pl.semaphore_wait(barrier, len(partners))
    unit_copy = remote(bias_u, uoth, wsem, 2 * len(pieces), across)
    head_copy = remote(bias_qv, voth, wsem, 2 * len(pieces) + 1, across)
    get_wq.wait()
    get_wo.wait()
    for copy in get_w1:
        copy.wait()
    get_w2.wait()
    by_x = [remote(src, dst, wsem, i, across) for i, (src, dst) in enumerate(pieces)]
    by_y = [None] * len(pieces)

    def forward_weight(*which):
        for i in which:
            by_x[i].wait_recv()
            by_y[i] = remote(pieces[i][1], pieces[i][1], wsem, len(pieces) + i, mates[0])

    def have_weight(*which):
        for i in which:
            by_y[i].wait_recv()

    n1_copy = remote(n1_s.at[pl.ds(0, count)], n1_s.at[pl.ds(count, count)], csem, 0, sib)
    get_cot.wait()
    cot_copy = remote(cot_s.at[pl.ds(0, count)], cot_s.at[pl.ds(count, count)], csem, 1, sib)

    def rotate(at):
        nr_s[pl.ds(at, BLOCK)] = dot(roll_s[pl.ds(at, BLOCK)], n1_s[...]).astype(BF16)

    def project(j, at):
        n = nr_s[pl.ds(at, BLOCK)]
        biases = bias_qv if j == 0 else voth
        q = (dot_nt(n, wq_s[j, 0]) + biases[0:1]).astype(BF16) * SCALE
        k = dot_nt(n, wq_s[j, 1]).astype(BF16)
        v = (dot_nt(n, wq_s[j, 2]) + biases[1:2]).astype(BF16)
        q_s[j, pl.ds(at, BLOCK), :quarter] = q
        k_s[pl.ds(at, BLOCK), :quarter] = k
        v_s[j, pl.ds(at, BLOCK), :quarter] = v
        kt_s[j * quarter : (j + 1) * quarter, pl.ds(at, BLOCK)] = k.T * SCALE

    blocks = [(b, at) for b in range(2) for at in range(0, count, BLOCK)]

    def attend(j, service):
        vt = v_s[j, :, :quarter].T
        for head in range(heads):
            qh = head_lanes(q_s.at[j], head, sq_s[...])
            kh = head_lanes(k_s, head, sk_s[...])
            span = slice(head * HEAD, head * HEAD + HEAD)
            to = slice(j * quarter + head * HEAD, j * quarter + head * HEAD + HEAD)

            def scores(b, at):
                return dot_nt(kh[b * count : (b + 1) * count], qh[b * count + at : b * count + at + BLOCK])

            later = scores(*blocks[0])
            for i, (b, at) in enumerate(blocks):
                s = later
                if i + 1 < len(blocks):
                    later = scores(*blocks[i + 1])
                m = jnp.max(s, axis=0, keepdims=True)
                e = jnp.exp(s - m)
                r = 1.0 / column_sum(e)
                low = e.astype(BF16)
                here = slice(b * count + at, b * count + at + BLOCK)
                e_s[j * heads + head, b, :, at : at + BLOCK] = low
                ot_s[to, here] = (dot(vt[span, b * count : (b + 1) * count], low) * r).astype(BF16)
                r_s[j * heads + head : j * heads + head + 1, here] = r
            service[head]()

    n1_copy.wait_recv()
    loop(rows, BLOCK, rotate)
    loop(rows, BLOCK, lambda at: project(0, at))
    nothing = lambda: None
    forward_weight(0, 1)
    attend(0, [lambda: forward_weight(2), lambda: forward_weight(3), nothing])
    head_copy.wait_recv()
    have_weight(0, 1, 2)
    loop(rows, BLOCK, lambda at: project(1, at))
    attend(1, [lambda: forward_weight(4), lambda: forward_weight(5), nothing])

    have_weight(3)

    def unrotate(at):
        ou_s[:, pl.ds(at, BLOCK)] = dot(ot_s[...], roll_s[:, pl.ds(at, BLOCK)]).astype(BF16)

    loop(rows, BLOCK, unrotate)

    def out_part(at):
        return dot_tn(ou_s[:, pl.ds(at, BLOCK)], wo_s[...])

    def out_sib(at):
        sb1[pl.ds(at, BLOCK)] = out_part(count + at).astype(BF16)

    loop(count, BLOCK, out_sib)
    att_copy = remote(sb1, rb1, csem, 2, sib)

    def out_mine(at):
        mid_s[pl.ds(at, BLOCK)] = sin_s[pl.ds(at, BLOCK)] + out_part(at) + out_bias

    loop(count, BLOCK, out_mine)
    att_copy.wait_recv()

    def second_norm(at):
        spot = pl.ds(at, 64)
        mid = mid_s[spot] + rb1[spot].astype(F32)
        mid_s[spot] = mid
        xhat, _ = norm_stats(mid)
        n2 = (xhat * ln2_gain + ln2_bias).astype(BF16)
        n2_s[spot] = n2

    loop(count, 64, second_norm)
    n2_copy = remote(n2_s.at[pl.ds(0, count)], n2_s.at[pl.ds(count, count)], csem, 3, sib)

    forward_weight(6)

    base_a = units
    parts = units // BLOCK
    steps = copies_of(len(full_bits))

    class Region:
        def __init__(self, index, row, size, cols, slot, kind, refs, to):
            self.place = self.now = (row, size, 0, cols)
            self.own, self.oth, self.xr, self.land, self.land_both, self.rx = refs
            self.to = to
            self.index, self.slot, self.used = index, slot, 0
            self.first, self.after = KINDS[kind]
            self.stages = [] if self.first is None else ["first"]
            self.stages += ["x"] + [("halve", bits) for bits in self.after] + [("full", i) for i in range(len(full_bits))]
            self.last_sum = len(self.stages) - 1
            self.stages += [("gather", bits) for bits in reversed(self.after)]
            if self.first is not None:
                self.stages.append(("gather", (self.first,)))
            self.stage, self.flying, self.sent, self.trail = -1, [], [], []
            self.parts, self.slots_used = 8, 0
            self.finished = False

        def window(self, where):
            row, size, col, cols = where
            return pl.ds(row, size), pl.ds(col, cols)

        def go(self, src, src_at, dst, dst_at, device):
            copy = remote(src.at[self.window(src_at)], dst.at[self.window(dst_at)], gsem, self.index * steps + self.used, device)
            self.used += 1
            self.flying.append(copy)
            self.sent.append(copy)

        def cut(self, where, side):
            row, size, col, cols = where
            if (size // 2) % 16 == 0:
                return pl.multiple_of(row + side * (size // 2), 16), size // 2, col, cols
            return row, size, pl.multiple_of(col + side * (cols // 2), 128), cols // 2

        def piece(self, bits, mask):
            where = self.now
            for k, b in enumerate(bits):
                where = self.cut(where, 1 - sides[b] if mask >> k & 1 else sides[b])
            return where

        def landing(self, at, parts_here):
            row, rows_one, cols_one = self.slot
            full = self.place[3]
            if cols_one == full:
                return row + at * rows_one, parts_here * rows_one, 0, full
            if parts_here == 1:
                return row + at // 2 * rows_one, rows_one, at % 2 * cols_one, cols_one
            return row + at // 2 * rows_one, parts_here // 2 * rows_one, 0, full

        def ready(self, j):
            if self.first is not None:
                self.stage = 0
                give = self.piece((self.first,), 1)
                if j == 0:
                    self.go(self.own, give, self.land, self.landing(0, 4), mates[self.first])
                else:
                    row, size, col, cols = self.place
                    self.both = (row // 2, size // 2, col, cols)
                    self.go(self.oth, give, self.land_both, self.both, mates[self.first])
            elif j == 1:
                self.stage = 0
                self.go(self.oth, self.now, self.xr, self.now, across)

        def add(self, into, base, where, *terms):
            row, size, col, cols = where
            step = 64 if size % 64 == 0 else 48 if size % 48 == 0 else 32

            def body(off):
                to = (pl.ds(pl.multiple_of(row + off, 16), step), pl.ds(col, cols))
                total = base[to].astype(F32)
                for ref, (r, _, c, _) in terms:
                    total += ref[pl.ds(pl.multiple_of(r + off, 16), step), pl.ds(c, cols)].astype(F32)
                into[to] = total.astype(BF16)

            loop(size, step, body)

        def finish_stage(self):
            what = self.stages[self.stage]
            dest = self.xr if self.stage == self.last_sum else self.own
            if what == "first":
                keep = self.piece((self.first,), 0)
                self.add(self.own, self.own, keep, (self.land, self.landing(0, 4)))
                self.add(self.oth, self.oth, keep, (self.land_both, self.both))
                self.trail.append(((self.first,), keep))
                self.now, self.parts, self.slots_used = keep, 4, 4
            elif what == "x":
                self.add(dest, self.own, self.now, (self.xr, self.now))
            elif what[0] == "halve":
                self.add(dest, self.own, self.keep, *[(self.land, at) for at in self.landed])
                self.trail.append((what[1], self.keep))
                self.now = self.keep
            elif what[0] == "full":
                for copy in self.flying:
                    copy.wait_send()
                    self.sent = [c for c in self.sent if c is not copy]
                self.add(dest, self.own, self.now, (self.rx[what[1]], self.small_place()))

        def small_place(self):
            row, rows_one, cols_one = self.slot
            if cols_one == self.place[3]:
                return row // 7, rows_one, 0, cols_one
            k = (self.place[0] - base_a) // quarter
            return units // 8 + k // 2 * rows_one, rows_one, k % 2 * cols_one, cols_one

        def start_stage(self):
            what = self.stages[self.stage]
            if what == "x":
                self.go(self.oth, self.now, self.xr, self.now, across)
            elif what[0] == "halve":
                bits = what[1]
                self.parts >>= len(bits)
                self.keep = self.piece(bits, 0)
                self.landed = []
                for mask in range(1, 1 << len(bits)):
                    there = self.landing(self.slots_used, self.parts)
                    self.slots_used += self.parts
                    self.landed.append(there)
                    to = mate([b for k, b in enumerate(bits) if mask >> k & 1])
                    self.go(self.own, self.piece(bits, mask), self.land, there, to)
            elif what[0] == "full":
                self.go(self.own, self.now, self.rx[what[1]], self.small_place(), mates[full_bits[what[1]]])
            else:
                bits, keep = self.trail.pop()
                for mask in range(1, 1 << len(bits)):
                    self.go(self.xr, keep, self.xr, keep, mate([b for k, b in enumerate(bits) if mask >> k & 1]))

        def advance(self):
            if self.finished or self.stage < 0:
                return
            for copy in self.flying:
                copy.wait_recv()
            self.finish_stage()
            self.flying = []
            self.stage += 1
            if self.stage < len(self.stages):
                self.start_stage()
                return
            self.finished = True
            self.done = local(self.xr.at[self.window(self.place)], self.to)

    chunks = []
    refs = (own, oth, xr, land, land_both, rx)
    for i in range(parts):
        slot = (i * 7 * (BLOCK // 8), BLOCK // 8, width)
        to = g2_h.at[pl.ds(i * BLOCK, BLOCK)]
        chunks.append(Region(2 * i, i * BLOCK, BLOCK, width, slot, ORDERS[2 * i], refs, to))
        refs_one = tuple(ref.at[i] for ref in (own1, oth1, xr1, land1, land1_both)) + ([ref.at[i] for ref in rx1],)
        to = g1_h.at[:, pl.ds(i * BLOCK, BLOCK)]
        chunks.append(Region(2 * i + 1, 0, width, BLOCK, (0, width // 8, BLOCK), ORDERS[2 * i + 1], refs_one, to))
    for i in range(4):
        slot = (7 * units // 8 + i * quarter, quarter // 4, width // 2)
        to = go_h if i == 0 else gq_h.at[i - 1]
        chunks.append(Region(2 * parts + i, base_a + i * quarter, quarter, width, slot, ORDERS[2 * parts + i], refs, to))
    first_att = 2 * parts

    def ready(i, j):
        chunks[i].ready(j)

    def hook(name):
        for i in PLAN.get(name, ()):
            chunks[i].advance()

    def chunk_rows(j, i, at):
        span = pl.ds(at, BLOCK)
        cols = slice(j * units + i * BLOCK, j * units + (i + 1) * BLOCK)
        mine = slice(i * BLOCK, (i + 1) * BLOCK)
        bias = (bias_u if j == 0 else uoth)[mine].reshape(1, BLOCK)
        h = dot(n2_s[span], w1_s[j, i]) + bias
        a, slope = gelu_pair(h)
        a_s[span, cols] = a.astype(BF16)
        g = (dot_nt(cot_s[span], w2_s[j, mine]) * slope).astype(BF16)
        g_s[span, cols] = g

    def chunk_grads(j, i):
        cols = slice(j * units + i * BLOCK, j * units + (i + 1) * BLOCK)
        mine = slice(i * BLOCK, (i + 1) * BLOCK)
        to = oth if j == 1 else own
        to[i * BLOCK : (i + 1) * BLOCK] = dot_tn(a_s[:, cols], cot_s[...]).astype(BF16)
        ready(2 * i, j)
        g = g_s[:, cols]
        (oth1 if j == 1 else own1)[i] = dot(n2t_s[...], g).astype(BF16)
        ready(2 * i + 1, j)
        sm[8 + 8 * j : 9 + 8 * j, mine] = column_sum(g.astype(F32))
        hook(f"f{j}{i}")

    def feed(j, i, first=False):
        if first:
            for at in range(0, count, BLOCK):
                chunk_rows(j, i, at)
            n2_copy.wait_recv()
            cot_copy.wait_recv()
            for at in range(0, rows, BLOCK):
                n2t_s[:, at : at + BLOCK] = n2_s[at : at + BLOCK].T
            for at in range(count, rows, BLOCK):
                chunk_rows(j, i, at)
        else:
            for at in range(0, rows, BLOCK):
                chunk_rows(j, i, at)
        chunk_grads(j, i)

    sm[...] = jnp.zeros_like(sm)
    unit_copy.wait_recv()
    have_weight(4, 5)
    feed(1, 0, first=True)
    forward_weight(7)
    feed(0, 0)
    have_weight(6, 7)
    forward_weight(8)
    feed(1, 1)
    forward_weight(9)
    feed(0, 1)
    for i in range(2, parts):
        have_weight(4 + 2 * i, 5 + 2 * i)
        feed(1, i)
        feed(0, i)

    def back_two(at):
        span = pl.ds(at, BLOCK)
        total = None
        for j in range(2):
            for i in range(parts):
                at_col = j * units + i * BLOCK
                term = dot_nt(g_s[span, at_col : at_col + BLOCK], w1_s[j, i])
                total = term if total is None else total + term
        return total

    def mlp_part(at):
        span = pl.ds(at, BLOCK)
        return dot(a_s[span, :units], w2_s[0]) + dot(a_s[span, units:], w2_s[1])

    def back_two_sib(at):
        sb2[pl.ds(at, BLOCK)] = back_two(count + at).astype(BF16)

    def back_two_mine(at):
        gm_s[pl.ds(at, BLOCK)] = back_two(at)

    def mlp_sib(at):
        sb1[pl.ds(at, BLOCK)] = mlp_part(count + at).astype(BF16)

    loop(count, BLOCK, back_two_sib)
    gn2_copy = remote(sb2, rb2, csem, 4, sib)
    loop(count, BLOCK, back_two_mine)
    hook("gn2")
    att_copy.wait_send()
    loop(count, BLOCK, mlp_sib)
    mlp_copy = remote(sb1, rb1, csem, 5, sib)
    hook("gn2b")
    gn2_copy.wait_recv()
    n2_copy.wait_send()

    def second_back(at):
        spot = pl.ds(at, 64)
        xhat, sigma = norm_stats(mid_s[spot])
        grad = gm_s[spot] + rb2[spot].astype(F32)
        cot = cot_s[spot].astype(F32)
        back = cot + norm_back(grad, ln2_gain, xhat, sigma)
        gm_s[spot] = back
        n2_s[spot] = back.astype(BF16)
        sm[2:3] += column_sum(back)
        sm[3:4] += column_sum(grad * xhat)
        sm[4:5] += column_sum(grad)
        sm[5:6] += column_sum(cot)

    loop(count, 64, second_back)
    dm_copy = remote(n2_s.at[pl.ds(0, count)], n2_s.at[pl.ds(count, count)], csem, 6, sib)

    hook("ln2")

    def finish_out(at):
        span = pl.ds(at, BLOCK)
        mid_s[span] = mid_s[span] + mlp_part(at) + fc2_bias

    loop(count, BLOCK, finish_out)
    mlp_copy.wait_recv()

    def write_out(at):
        spot = pl.ds(at, 64)
        tok_s[spot] = (mid_s[spot] + rb1[spot].astype(F32)).astype(BF16)

    loop(count, 64, write_out)
    put_out = local(tok_s, out_h)
    hook("fin")
    dm_copy.wait_recv()

    zero = jnp.zeros((rows, 128), BF16)
    start = base_a + quarter

    def lanes_of(total):
        return jnp.concatenate([total[0], total[1]], axis=1)[:, :quarter].astype(BF16)

    def keep_gradient(j, c, d, dt):
        to = oth if j == 1 else own
        g_s[:, (3 * j + c) * BLOCK : (3 * j + c) * BLOCK + quarter] = d
        to[start + c * quarter : start + (c + 1) * quarter] = dot(dt, nr_s[...]).astype(BF16)
        ready(first_att + 1 + c, j)
        if c != 1:
            sm[9 + c // 2 + 8 * j : 10 + c // 2 + 8 * j, :quarter] = column_sum(d.astype(F32))

    def both_blocks(parts_of):
        return jnp.concatenate([parts_of(0), parts_of(1)], axis=0)

    def values_back(j):
        base = j * quarter
        to = oth if j == 1 else own
        dm = n2_s[...]
        to[base_a : base_a + quarter] = dot(ou_s[base : base + quarter], dm).astype(BF16)
        ready(first_att, j)
        grad_t = dot_nt(wo_s[base : base + quarter], dm).astype(BF16)
        grad_t = dot_nt(grad_t, roll_s[...])
        scaled = []
        for head in range(heads):
            span = slice(head * HEAD, head * HEAD + HEAD)
            row = j * heads + head
            r = r_s[row : row + 1]
            g = grad_t[span]
            in_s[row : row + 1] = column_sum(g * ot_s[base + head * HEAD : base + head * HEAD + HEAD].astype(F32)) * r
            scaled.append((g * r).astype(BF16))
        gt = jnp.concatenate(scaled, axis=0)
        gt_s[base : base + quarter] = gt
        go_s = a_s.at[:, rows + 256 * j : rows + 256 * (j + 1)]
        go_s[:, :quarter] = gt.T
        dv = [None, None]
        for head in range(heads):
            gh = head_lanes(go_s, head, zero)
            part = both_blocks(lambda b: dot(e_s[j * heads + head, b], gh[b * count : (b + 1) * count]))
            tile = head // 2
            dv[tile] = part if dv[tile] is None else dv[tile] + part
        dv = lanes_of(dv)
        keep_gradient(j, 2, dv, dv.T)
        hook(f"v{j}")

    def scores_back(j):
        base = j * quarter
        dq, dk = [], [None, None]
        for head in range(heads):
            tile = head // 2
            row = j * heads + head
            vh = head_lanes(v_s.at[j], head, zero)
            qh = head_lanes(q_s.at[j], head, zero)
            last_row = min(128 * tile + 128, quarter)
            gth = gt_s[base + 128 * tile : base + last_row]
            vh = vh[:, : gth.shape[0]]
            ds = a_s.at[:, (head % 2) * count : (head % 2 + 1) * count]
            for b, at in blocks:
                here = slice(b * count + at, b * count + at + BLOCK)
                dp_t = dot(vh[b * count : (b + 1) * count], gth[:, here])
                grad = (dp_t - in_s[row : row + 1, here]) * e_s[row, b, :, at : at + BLOCK].astype(F32)
                ds[b * count : (b + 1) * count, at : at + BLOCK] = grad.astype(BF16)
            part = both_blocks(lambda b: dot(ds[b * count : (b + 1) * count], qh[b * count : (b + 1) * count]))
            dk[tile] = part if dk[tile] is None else dk[tile] + part
            kth = kt_s.at[base + head * HEAD : base + head * HEAD + HEAD]
            dq.append(
                jnp.concatenate(
                    [dot(kth[:, b * count : (b + 1) * count], ds[b * count : (b + 1) * count]) for b in range(2)], axis=1
                )
            )
            hook(f"b{j}{head}")
        dk = lanes_of(dk)
        keep_gradient(j, 1, dk, dk.T)
        dqt = jnp.concatenate(dq, axis=0).astype(BF16)
        keep_gradient(j, 0, dqt.T, dqt)
        hook(f"s{j}")

    values_back(1)
    values_back(0)
    scores_back(1)
    scores_back(0)

    def back_one(at):
        total = None
        for j in range(2):
            for c in range(3):
                d = g_s[pl.ds(at, BLOCK), (3 * j + c) * BLOCK : (3 * j + c) * BLOCK + quarter]
                term = dot(d, wq_s[j, c])
                total = term if total is None else total + term
        n2_s[pl.ds(at, BLOCK)] = total.astype(BF16)

    dm_copy.wait_send()
    loop(rows, BLOCK, back_one)
    hook("gn1")
    gn2_copy.wait_send()

    def back_one_sib(at):
        sb2[pl.ds(at, BLOCK)] = dot(back_s[pl.ds(count + at, BLOCK)], n2_s[...]).astype(BF16)

    def back_one_mine(at):
        mid_s[pl.ds(at, BLOCK)] = dot(back_s[pl.ds(at, BLOCK)], n2_s[...])

    loop(count, BLOCK, back_one_sib)
    gn1_copy = remote(sb2, rb2, csem, 7, sib)
    loop(count, BLOCK, back_one_mine)
    hook("gn1b")
    gn1_copy.wait_recv()
    mlp_copy.wait_send()

    def first_back(at):
        spot = pl.ds(at, 64)
        xhat, sigma = norm_stats(sin_s[spot])
        grad = mid_s[spot] + rb2[spot].astype(F32)
        sb1[spot] = (gm_s[spot] + norm_back(grad, ln1_gain, xhat, sigma)).astype(BF16)
        sm[0:1] += column_sum(grad * xhat)
        sm[1:2] += column_sum(grad)

    loop(count, 64, first_back)
    put_in = local(sb1, ing_h)

    state = {}

    def small_start(i):
        if i == 0:
            state["c"] = remote(sm, smr.at[0], ssem, 0, sib)
        elif i == 1:
            state["c"] = remote(sm, smr.at[1], ssem, 1, across)
        else:
            state["c"] = remote(sm.at[pl.ds(0, 16)], smr.at[i, pl.ds(0, 16)], ssem, i, mates[all_bits[i - 2]])
        state["i"] = i

    def small_step():
        i = state["i"]
        state["c"].wait()
        if i == 0:
            sm[0:8] = sm[0:8] + smr[0, 0:8]
        elif i == 1:
            sm[0:8] = sm[0:8] + smr[1, 0:8]
            sm[8:16] = sm[8:16] + smr[1, 16:24]
        else:
            sm[0:16] = sm[0:16] + smr[i, 0:16]
        if i + 1 < 2 + len(all_bits):
            small_start(i + 1)
        else:
            small_o[...] = sm[0:16]

    small_start(0)
    small_left = 2 + len(all_bits)
    for i in PLAN["tail"]:
        if i >= 0:
            chunks[i].advance()
        elif small_left:
            small_step()
            small_left -= 1
    while True:
        busy = False
        for chunk in chunks:
            if not chunk.finished:
                chunk.advance()
                busy = True
        if small_left:
            small_step()
            small_left -= 1
            busy = True
        if not busy:
            break

    for copy in [unit_copy, head_copy, n1_copy, cot_copy, gn1_copy] + by_x + by_y:
        copy.wait_send()
    for chunk in chunks:
        for copy in chunk.sent:
            copy.wait_send()
        chunk.done.wait()
    put_out.wait()
    put_in.wait()


def copies_of(full):
    most = 0
    for kind in ORDERS:
        first, after = KINDS[kind]
        most = max(most, 1 + full + 2 * sum((1 << len(bits)) - 1 for bits in after) + (0 if first is None else 3))
    return most


def call_layer(dp_size, tokens, cotangent, ids, table, vectors, wq, wo, w1, w2):
    count, width = tokens.shape
    rows = 2 * count
    quarter = wo.shape[0]
    units = w1.shape[1]
    heads = quarter // HEAD
    grad_rows = units + 4 * quarter
    parts = units // BLOCK
    bits = [b for b in range(20) if (1 << b) < dp_size]
    half_bits = bits[:3]
    shape = jax.ShapeDtypeStruct
    vm = pltpu.VMEM
    regions = 2 * (units // BLOCK) + 4
    steps = copies_of(len(bits) - len(half_bits))
    fetched = 4 + 2 * (units // BLOCK)
    scratch = (
        [vm((count, width), BF16), vm((rows, width), BF16)]
        + [vm((count, width), F32)] * 3
        + [vm((rows, width), BF16)] * 2
        + [vm((width, rows), BF16)]
        + [vm((2,) + wq.shape, BF16), vm((2 * quarter, width), BF16), vm((2, units // BLOCK, width, BLOCK), BF16), vm((2,) + w2.shape, BF16)]
        + [vm((2, rows, 256), BF16)] * 2
        + [vm((2 * quarter, rows), BF16)] * 4
        + [vm((8, rows), F32)] * 2
        + [vm((2 * heads, 2, count, count), BF16)]
        + [vm((rows, rows), BF16)] * 2
        + [vm((rows, width), BF16)]
        + [vm((rows, 2 * units), BF16)] * 2
        + [vm((count, width), BF16)] * 4
        + [vm((grad_rows, width), BF16)] * 3
        + [vm((7 * units // 8 + 4 * quarter, width), BF16), vm((units // 2, width), BF16)]
        + [vm((parts, width, BLOCK), BF16)] * 3
        + [vm((parts, 7 * width // 8, BLOCK), BF16), vm((parts, width // 2, BLOCK), BF16)]
        + [vm((grad_rows >> len(half_bits), width), BF16)] * (len(bits) - len(half_bits))
        + [vm((parts, width // 8, BLOCK), BF16)] * (len(bits) - len(half_bits))
        + [vm((units,), F32), vm((2, quarter), F32), vm((24, width), F32), vm((2 + len(bits), 24, width), F32)]
        + [pltpu.SemaphoreType.DMA((8 + units // BLOCK + regions,))]
        + [pltpu.SemaphoreType.DMA((2, n)) for n in (2 * fetched + 2, 8, regions * steps, 2 + len(bits))]
    )
    anywhere = pl.BlockSpec(memory_space=pl.ANY)
    inside = pl.BlockSpec(memory_space=pltpu.VMEM)
    return pl.pallas_call(
        functools.partial(layer, dp_size, half_bits),
        out_shape=[shape((count, width), BF16)] * 2
        + [shape(w2.shape, BF16), shape(w1.shape, BF16), shape(wo.shape, BF16), shape(wq.shape, BF16), shape((16, width), F32)],
        in_specs=[anywhere] * 2 + [inside] * (2 + len(vectors)) + [anywhere] * 4,
        out_specs=[anywhere] * 6 + [inside],
        scratch_shapes=scratch,
        compiler_params=pltpu.CompilerParams(vmem_limit_bytes=VMEM_LIMIT, collective_id=0, has_side_effects=True),
        name="layer",
    )(tokens, cotangent, ids, table, *vectors, wq, wo, w1, w2)


def finish(out, ing, g2, g1, go, gq, small, out_o, ing_o, g2_o, g1_o, go_o, gq_o, a0, a1, a2, a3, a4, a5, units_o, heads_o):
    for src, dst in ((out, out_o), (ing, ing_o), (g2, g2_o), (g1, g1_o), (go, go_o), (gq, gq_o)):
        dst[...] = src[...].astype(dst.dtype)

    @pl.when(pl.program_id(0) == 0)
    def _():
        for i, ref in enumerate((a0, a1, a2, a3, a4, a5)):
            ref[...] = small[i]
        units_o[...] = small[8, : units_o.shape[0]]
        heads_o[...] = small[9:11, : heads_o.shape[1]]


def call_finish(arrays, small, units, quarter):
    steps = 4
    width = small.shape[1]
    shape = jax.ShapeDtypeStruct

    def rows_of(a):
        axis = a.ndim - 2
        block = a.shape[:axis] + (a.shape[axis] // steps,) + a.shape[axis + 1 :]
        return pl.BlockSpec(block, lambda i, axis=axis, rank=a.ndim: tuple(i if k == axis else 0 for k in range(rank)))

    def whole(extent):
        return pl.BlockSpec(extent, lambda i, rank=len(extent): (0,) * rank)

    extents = [(width,)] * 6 + [(units,), (2, quarter)]
    kinds = [BF16, BF16, F32, F32, F32, F32]
    return pl.pallas_call(
        finish,
        grid=(steps,),
        in_specs=[rows_of(a) for a in arrays] + [whole(small.shape)],
        out_specs=[rows_of(a) for a in arrays] + [whole(e) for e in extents],
        out_shape=[shape(a.shape, k) for a, k in zip(arrays, kinds)] + [shape(e, F32) for e in extents],
        compiler_params=pltpu.CompilerParams(vmem_limit_bytes=VMEM_LIMIT),
        name="finish",
    )(*arrays, small)


def per_device(
    tokens, segment_ids, ln1_gain, ln1_bias, qkv_weight, qv_bias, out_weight, out_bias,
    ln2_gain, ln2_bias, fc1_weight, fc1_bias, fc2_weight, fc2_bias, cotangent,
):
    width = tokens.shape[1]
    freq_count = width // 6
    frequency = 10000.0 ** (-jnp.arange(freq_count, dtype=F32) / freq_count)
    angles = jnp.arange(SIDE, dtype=F32)[:, None] * frequency[None, :]
    table = jnp.concatenate([jnp.sin(angles), jnp.cos(angles)], axis=1)
    vectors = (ln1_gain, ln1_bias, out_bias, ln2_gain, ln2_bias, fc2_bias, fc1_bias, qv_bias)
    *arrays, small = call_layer(
        lax.axis_size("dp"), tokens, cotangent, segment_ids, table, vectors, qkv_weight.transpose(0, 2, 1), out_weight, fc1_weight, fc2_weight
    )
    out, ing, g2, g1, go, gq, a0, a1, a2, a3, a4, a5, g_units, g_heads = call_finish(arrays, small, fc1_weight.shape[1], out_weight.shape[0])
    return (out, ing, a0, a1, gq.transpose(0, 2, 1), g_heads, go, a2, a3, a4, g1, g_units, g2, a5)


def solution(mesh):
    placed = (
        P(("dp", "tensor"), None),
        P("dp", None),
        P(),
        P(),
        P(None, None, "tensor"),
        P(None, "tensor"),
        P("tensor", None),
        P(),
        P(),
        P(),
        P(None, "tensor"),
        P("tensor"),
        P("tensor", None),
        P(),
        P(("dp", "tensor"), None),
    )
    return jax.shard_map(
        per_device,
        mesh=mesh,
        in_specs=placed,
        out_specs=(
            P(("dp", "tensor"), None),
            P(("dp", "tensor"), None),
            P(),
            P(),
            P(None, None, "tensor"),
            P(None, "tensor"),
            P("tensor", None),
            P(),
            P(),
            P(),
            P(None, "tensor"),
            P("tensor"),
            P("tensor", None),
            P(),
        ),
        check_vma=False,
    )
```

```python
import functools

import jax
import jax.numpy as jnp
from jax import lax
from jax.experimental import pallas as pl
from jax.experimental.pallas import tpu as pltpu
from jax.sharding import PartitionSpec as P

HEAD = 64
SIDE = 16
EPSILON = 1e-06
NEG_LARGE = -1e30
SCALE = HEAD ** (-0.5)
F32 = jnp.float32
BF16 = jnp.bfloat16
VMEM_LIMIT = 64 * 1024 * 1024 - 128 * 1024
MESH = pl.DeviceIdType.MESH
BLOCK = 256
KINDS = {
    "A": (None, ((0,), (1,), (2,))),
    "B": (None, ((1,), (0,), (2,))),
    "D": (None, ((0,), (1, 2))),
    "E": (None, ((0, 1, 2),)),
    "Y": (0, ((1,), (2,))),
    "Z": (1, ((0,), (2,))),
    "YD": (0, ((1, 2),)),
}
ORDERS = ("Z", "E", "E", "YD", "A", "A", "B", "D", "D", "B")
PLAN = {
    "f01": (1, 0),
    "f02": (2,),
    "gn2": (3, 0),
    "gn2b": (1,),
    "ln2": (4,),
    "fin": (0, 2),
    "v0": (5, 4, 1, 3, 0),
    "b1": (4, 6),
    "s1": (5, 2),
    "b0": (9, 3, 6, 0),
    "s0": (5, 4),
    "gn1": (8, 6, 9),
    "gn1b": (0,),
    "tail": (3, 7, 5, 4, 8, 6, 9, -1, 0, -1, 5, 3, 4, -1, 8, 7, 6, -1, 9, 5, -1, 4, 8, 6, 7, 9, 5, 6, 8, 7, 9, 7, 9),
}


def dot(a, b):
    return jnp.dot(a, b, preferred_element_type=F32)


def dot_nt(a, b):
    return lax.dot_general(a, b, (((1,), (1,)), ((), ())), preferred_element_type=F32)


def dot_tn(a, b):
    return lax.dot_general(a, b, (((0,), (0,)), ((), ())), preferred_element_type=F32)


def lane_half(rows, upper):
    lanes = lax.broadcasted_iota(jnp.int32, (rows, 128), 1)
    return lanes >= HEAD if upper else lanes < HEAD


def head_lanes(ref, head, filler):
    tile = ref[:, 128 * (head // 2) : 128 * (head // 2) + 128]
    return jnp.where(lane_half(tile.shape[0], head % 2 == 1), tile, filler)


def gelu_pair(h):
    size = jnp.abs(h)
    t = 1.0 / (1.0 + (0.3275911 * 0.7071067811865476) * size)
    bell = jnp.exp(-0.5 * h * h)
    poly = ((((1.061405429 * t - 1.453152027) * t + 1.421413741) * t - 0.284496736) * t + 0.254829592) * t
    tail = 0.5 * poly * bell
    cdf = jnp.where(h < 0, tail, 1.0 - tail)
    return h * cdf, cdf + h * bell * 0.3989422804014327


def norm_stats(v):
    centred = v - jnp.mean(v, axis=-1, keepdims=True)
    sigma = lax.rsqrt(jnp.mean(centred * centred, axis=-1, keepdims=True) + EPSILON)
    return centred * sigma, sigma


def norm_back(grad, gain, xhat, sigma):
    g = grad * gain
    return sigma * (g - jnp.mean(g, axis=-1, keepdims=True) - xhat * jnp.mean(g * xhat, axis=-1, keepdims=True))


def column_sum(v):
    return jnp.sum(v, axis=0, keepdims=True)


def loop(count, step, body):
    def run(i, carry):
        body(pl.multiple_of(i * step, step))
        return carry

    lax.fori_loop(0, count // step, run, 0)


def layer(
    dp_size, half_bits,
    tok_h, cot_h, ids, table, gain1, bias1, bias_o, gain2, bias2, bias_f, bias_u, bias_qv, wq_h, wo_h, w1_h, w2_h,
    out_h, ing_h, g2_h, g1_h, go_h, gq_h, small_o,
    tok_s, cot_s, sin_s, mid_s, gm_s, n1_s, n2_s, n2t_s, wq_s, wo_s, w1_s, w2_s,
    q_s, v_s, kt_s, ot_s, ou_s, gt_s, gr_s, r_s, in_s, e_s, roll_s, back_s, nr_s, a_s, g_s, sb1, sb2, rb1, rb2,
    own, oth, xr, land, land_both, own1, oth1, xr1, land1, land1_both, *rest,
):
    rest = list(rest)
    full_bits = [b for b in range(20) if (1 << b) < dp_size and b not in half_bits]
    rx = [rest.pop(0) for _ in full_bits]
    rx1 = [rest.pop(0) for _ in full_bits]
    uoth, voth, sm, smr, lsem, wsem, csem, gsem, ssem = rest

    count, width = tok_s.shape
    rows = 2 * count
    quarter = wo_h.shape[0]
    units = w1_h.shape[1]
    heads = quarter // HEAD
    place = lax.axis_index("tensor")
    dp = lax.axis_index("dp")
    chip = place // 2
    core = place % 2
    sib = {"tensor": chip * 2 + 1 - core}
    across = {"tensor": (1 - chip) * 2 + core}
    all_bits = list(half_bits) + full_bits
    sides = {b: (dp // (1 << b)) % 2 for b in all_bits}

    def mate(bits):
        return {"dp": dp + sum((1 - 2 * sides[b]) * (1 << b) for b in bits)}

    mates = {b: mate((b,)) for b in all_bits}
    groups = {(b,) for b in all_bits}
    for kind in ORDERS:
        for bits in KINDS[kind][1]:
            for mask in range(1, 1 << len(bits)):
                groups.add(tuple(b for k, b in enumerate(bits) if mask >> k & 1))

    barrier = pltpu.get_barrier_semaphore()
    partners = [sib, across] + [mate(bits) for bits in sorted(groups)]
    for partner in partners:
        pl.semaphore_signal(barrier, inc=1, device_id=partner, device_id_type=MESH)

    sq_s, sk_s, k_s = a_s.at[:, 0:128], a_s.at[:, 128:256], a_s.at[:, 256:512]
    local_used = [0]

    def local(src, dst):
        copy = pltpu.make_async_copy(src, dst, lsem.at[local_used[0]])
        local_used[0] += 1
        copy.start()
        return copy

    def remote(src, dst, sems, index, device):
        copy = pltpu.make_async_remote_copy(
            src_ref=src, dst_ref=dst, send_sem=sems.at[0, index], recv_sem=sems.at[1, index], device_id=device, device_id_type=MESH
        )
        copy.start()
        return copy

    get_tok = local(tok_h, tok_s)
    get_cot = local(cot_h, cot_s.at[pl.ds(0, count)])
    get_wq = local(wq_h, wq_s.at[0])
    get_wo = local(wo_h, wo_s.at[pl.ds(0, quarter)])
    get_w1 = [local(w1_h.at[:, pl.ds(i * BLOCK, BLOCK)], w1_s.at[0, i]) for i in range(units // BLOCK)]
    get_w2 = local(w2_h, w2_s.at[0])

    part = sides[0]

    def half_of(extent):
        return pl.ds(pl.multiple_of(part * (extent // 2), 32), extent // 2)

    wo_other = pl.ds(pl.multiple_of(quarter + part * (quarter // 2), 32), quarter // 2)
    pieces = [(wq_s.at[0, c, half_of(quarter)], wq_s.at[1, c, half_of(quarter)]) for c in range(3)]
    pieces.append((wo_s.at[half_of(quarter)], wo_s.at[wo_other]))
    for i in range(units // BLOCK):
        span = pl.ds(pl.multiple_of(i * BLOCK + part * (BLOCK // 2), 32), BLOCK // 2)
        pieces.append((w1_s.at[0, i, half_of(width)], w1_s.at[1, i, half_of(width)]))
        pieces.append((w2_s.at[0, span], w2_s.at[1, span]))

    ln1_gain, ln1_bias, out_bias, ln2_gain, ln2_bias, fc2_bias = (
        ref[...].reshape(1, width) for ref in (gain1, bias1, bias_o, gain2, bias2, bias_f)
    )
    get_tok.wait()

    def first_norm(at):
        plane = core * (count // (SIDE * SIDE)) + at // (SIDE * SIDE)
        line = (at // SIDE) % SIDE
        shape = (SIDE, width // 3)
        for k in range(4):
            spot = jnp.concatenate(
                [jnp.broadcast_to(table[pl.ds(plane, 1)], shape), jnp.broadcast_to(table[pl.ds(line + k, 1)], shape), table[...]], axis=1
            )
            span = pl.ds(pl.multiple_of(at + k * SIDE, SIDE), SIDE)
            stream = tok_s[span].astype(F32) + spot
            sin_s[span] = stream
            xhat, _ = norm_stats(stream)
            n1_s[span] = (xhat * ln1_gain + ln1_bias).astype(BF16)

    loop(count, 4 * SIDE, first_norm)
    doc = ids[pl.ds(chip, 1), :]
    starts = [jnp.zeros((1, 1), F32)]
    starts += [jnp.sum(jnp.where(doc < v, 1.0, 0.0), axis=1, keepdims=True) for v in range(1, 4)]
    starts.append(jnp.full((1, 1), rows, F32))
    turn = jnp.zeros((1, 1), F32)
    for v in range(4):
        turn += jnp.where(starts[v + 1] - starts[v] == count, starts[v], 0.0)
    turn_here = turn - (core * count).astype(F32)

    def wrapped(v):
        v = jnp.where(v >= rows, v - rows, v)
        return jnp.where(v < 0, v + rows, v)

    def rotations(at):
        down = (lax.broadcasted_iota(jnp.int32, (64, rows), 0) + at).astype(F32)
        along = lax.broadcasted_iota(jnp.int32, (64, rows), 1).astype(F32)
        roll_s[pl.ds(at, 64)] = jnp.where(wrapped(down + turn_here) == along, 1.0, 0.0).astype(BF16)
        back_s[pl.ds(at, 64)] = jnp.where(wrapped(down - turn_here) == along, 1.0, 0.0).astype(BF16)
        where = wrapped((lax.broadcasted_iota(jnp.int32, (64, 128), 0) + at).astype(F32) + turn)
        mine = sum(jnp.where(where >= starts[v], 1.0, 0.0) for v in range(1, 4))
        slot = (lax.broadcasted_iota(jnp.int32, (64, 128), 1) % HEAD).astype(F32)
        sq_s[pl.ds(at, 64)] = jnp.where((slot < 4) & (slot != mine), 1.0, 0.0).astype(BF16)
        sk_s[pl.ds(at, 64)] = jnp.where(slot == mine, NEG_LARGE, 0.0).astype(BF16)

    loop(rows, 64, rotations)

    pl.semaphore_wait(barrier, len(partners))
    unit_copy = remote(bias_u, uoth, wsem, 2 * len(pieces), across)
    head_copy = remote(bias_qv, voth, wsem, 2 * len(pieces) + 1, across)
    get_wq.wait()
    get_wo.wait()
    for copy in get_w1:
        copy.wait()
    get_w2.wait()
    by_x = [remote(src, dst, wsem, i, across) for i, (src, dst) in enumerate(pieces)]
    by_y = [None] * len(pieces)

    def forward_weight(*which):
        for i in which:
            by_x[i].wait_recv()
            by_y[i] = remote(pieces[i][1], pieces[i][1], wsem, len(pieces) + i, mates[0])

    def have_weight(*which):
        for i in which:
            by_y[i].wait_recv()

    n1_copy = remote(n1_s.at[pl.ds(0, count)], n1_s.at[pl.ds(count, count)], csem, 0, sib)
    get_cot.wait()
    cot_copy = remote(cot_s.at[pl.ds(0, count)], cot_s.at[pl.ds(count, count)], csem, 1, sib)

    def rotate(at):
        nr_s[pl.ds(at, BLOCK)] = dot(roll_s[pl.ds(at, BLOCK)], n1_s[...]).astype(BF16)

    def project(j, at):
        n = nr_s[pl.ds(at, BLOCK)]
        biases = bias_qv if j == 0 else voth
        q = (dot_nt(n, wq_s[j, 0]) + biases[0:1]).astype(BF16) * SCALE
        k = dot_nt(n, wq_s[j, 1]).astype(BF16)
        v = (dot_nt(n, wq_s[j, 2]) + biases[1:2]).astype(BF16)
        q_s[j, pl.ds(at, BLOCK), :quarter] = q
        k_s[pl.ds(at, BLOCK), :quarter] = k
        v_s[j, pl.ds(at, BLOCK), :quarter] = v
        kt_s[j * quarter : (j + 1) * quarter, pl.ds(at, BLOCK)] = k.T * SCALE

    blocks = [(b, at) for b in range(2) for at in range(0, count, BLOCK)]

    def attend(j):
        for head in range(heads):
            at = 512 + 256 * head
            a_s[:, at : at + 128] = head_lanes(q_s.at[j], head, sq_s[...])
            a_s[:, at + 128 : at + 256] = head_lanes(k_s, head, sk_s[...])
        for at in range(0, rows, BLOCK):
            ou_s[:quarter, at : at + BLOCK] = v_s[j, at : at + BLOCK, :quarter].T

        def tile(here):
            b = here // count
            at = pl.multiple_of(here % count, BLOCK)
            keys = pl.ds(pl.multiple_of(b * count, count), count)
            for head in range(heads):
                column = 512 + 256 * head
                s = dot_nt(a_s[keys, column + 128 : column + 256], a_s[pl.ds(here, BLOCK), column : column + 128])
                m = jnp.max(s, axis=0, keepdims=True)
                e = jnp.exp(s - m)
                r = 1.0 / column_sum(e)
                low = e.astype(BF16)
                span = slice(head * HEAD, head * HEAD + HEAD)
                to = slice(j * quarter + head * HEAD, j * quarter + head * HEAD + HEAD)
                e_s[j * heads + head, b, :, pl.ds(at, BLOCK)] = low
                ot_s[to, pl.ds(here, BLOCK)] = (dot(ou_s[span, keys], low) * r).astype(BF16)
                r_s[j * heads + head : j * heads + head + 1, pl.ds(here, BLOCK)] = r

        return tile

    n1_copy.wait_recv()
    loop(rows, BLOCK, rotate)
    loop(rows, BLOCK, lambda at: project(0, at))
    forward_weight(0, 1)
    tile = attend(0)
    loop(rows // 2, BLOCK, tile)
    forward_weight(2)
    loop(rows // 2, BLOCK, lambda at: tile(at + rows // 2))
    forward_weight(3)
    head_copy.wait_recv()
    have_weight(0, 1, 2)
    loop(rows, BLOCK, lambda at: project(1, at))
    tile = attend(1)
    loop(rows // 2, BLOCK, tile)
    forward_weight(4)
    loop(rows // 2, BLOCK, lambda at: tile(at + rows // 2))
    forward_weight(5)

    have_weight(3)

    def unrotate(at):
        ou_s[:, pl.ds(at, BLOCK)] = dot(ot_s[...], roll_s[:, pl.ds(at, BLOCK)]).astype(BF16)

    loop(rows, BLOCK, unrotate)

    def out_part(at):
        return dot_tn(ou_s[:, pl.ds(at, BLOCK)], wo_s[...])

    def out_sib(at):
        sb1[pl.ds(at, BLOCK)] = out_part(count + at).astype(BF16)

    loop(count, BLOCK, out_sib)
    att_copy = remote(sb1, rb1, csem, 2, sib)

    def out_mine(at):
        mid_s[pl.ds(at, BLOCK)] = sin_s[pl.ds(at, BLOCK)] + out_part(at) + out_bias

    loop(count, BLOCK, out_mine)
    att_copy.wait_recv()

    def second_norm(at):
        spot = pl.ds(at, 64)
        mid = mid_s[spot] + rb1[spot].astype(F32)
        mid_s[spot] = mid
        xhat, _ = norm_stats(mid)
        n2 = (xhat * ln2_gain + ln2_bias).astype(BF16)
        n2_s[spot] = n2

    loop(count, 64, second_norm)
    n2_copy = remote(n2_s.at[pl.ds(0, count)], n2_s.at[pl.ds(count, count)], csem, 3, sib)

    forward_weight(6)

    base_a = units
    parts = units // BLOCK
    steps = copies_of(len(full_bits))

    class Region:
        def __init__(self, index, row, size, cols, slot, kind, refs, to):
            self.place = self.now = (row, size, 0, cols)
            self.own, self.oth, self.xr, self.land, self.land_both, self.rx = refs
            self.to = to
            self.index, self.slot, self.used = index, slot, 0
            self.first, self.after = KINDS[kind]
            self.stages = [] if self.first is None else ["first"]
            self.stages += ["x"] + [("halve", bits) for bits in self.after] + [("full", i) for i in range(len(full_bits))]
            self.last_sum = len(self.stages) - 1
            self.stages += [("gather", bits) for bits in reversed(self.after)]
            if self.first is not None:
                self.stages.append(("gather", (self.first,)))
            self.stage, self.flying, self.sent, self.trail = -1, [], [], []
            self.parts, self.slots_used = 8, 0
            self.finished = False

        def window(self, where):
            row, size, col, cols = where
            return pl.ds(row, size), pl.ds(col, cols)

        def go(self, src, src_at, dst, dst_at, device):
            copy = remote(src.at[self.window(src_at)], dst.at[self.window(dst_at)], gsem, self.index * steps + self.used, device)
            self.used += 1
            self.flying.append(copy)
            self.sent.append(copy)

        def cut(self, where, side):
            row, size, col, cols = where
            if (size // 2) % 16 == 0:
                return pl.multiple_of(row + side * (size // 2), 16), size // 2, col, cols
            return row, size, pl.multiple_of(col + side * (cols // 2), 128), cols // 2

        def piece(self, bits, mask):
            where = self.now
            for k, b in enumerate(bits):
                where = self.cut(where, 1 - sides[b] if mask >> k & 1 else sides[b])
            return where

        def landing(self, at, parts_here):
            row, rows_one, cols_one = self.slot
            full = self.place[3]
            if cols_one == full:
                return row + at * rows_one, parts_here * rows_one, 0, full
            if parts_here == 1:
                return row + at // 2 * rows_one, rows_one, at % 2 * cols_one, cols_one
            return row + at // 2 * rows_one, parts_here // 2 * rows_one, 0, full

        def ready(self, j):
            if self.first is not None:
                self.stage = 0
                give = self.piece((self.first,), 1)
                if j == 0:
                    self.go(self.own, give, self.land, self.landing(0, 4), mates[self.first])
                else:
                    row, size, col, cols = self.place
                    self.both = (row // 2, size // 2, col, cols)
                    self.go(self.oth, give, self.land_both, self.both, mates[self.first])
            elif j == 1:
                self.stage = 0
                self.go(self.oth, self.now, self.xr, self.now, across)

        def add(self, into, base, where, *terms):
            row, size, col, cols = where
            step = 64 if size % 64 == 0 else 48 if size % 48 == 0 else 32

            def body(off):
                to = (pl.ds(pl.multiple_of(row + off, 16), step), pl.ds(col, cols))
                total = base[to].astype(F32)
                for ref, (r, _, c, _) in terms:
                    total += ref[pl.ds(pl.multiple_of(r + off, 16), step), pl.ds(c, cols)].astype(F32)
                into[to] = total.astype(BF16)

            loop(size, step, body)

        def finish_stage(self):
            what = self.stages[self.stage]
            dest = self.xr if self.stage == self.last_sum else self.own
            if what == "first":
                keep = self.piece((self.first,), 0)
                self.add(self.own, self.own, keep, (self.land, self.landing(0, 4)))
                self.add(self.oth, self.oth, keep, (self.land_both, self.both))
                self.trail.append(((self.first,), keep))
                self.now, self.parts, self.slots_used = keep, 4, 4
            elif what == "x":
                self.add(dest, self.own, self.now, (self.xr, self.now))
            elif what[0] == "halve":
                self.add(dest, self.own, self.keep, *[(self.land, at) for at in self.landed])
                self.trail.append((what[1], self.keep))
                self.now = self.keep
            elif what[0] == "full":
                for copy in self.flying:
                    copy.wait_send()
                    self.sent = [c for c in self.sent if c is not copy]
                self.add(dest, self.own, self.now, (self.rx[what[1]], self.small_place()))

        def small_place(self):
            row, rows_one, cols_one = self.slot
            if cols_one == self.place[3]:
                return row // 7, rows_one, 0, cols_one
            k = (self.place[0] - base_a) // quarter
            return units // 8 + k // 2 * rows_one, rows_one, k % 2 * cols_one, cols_one

        def start_stage(self):
            what = self.stages[self.stage]
            if what == "x":
                self.go(self.oth, self.now, self.xr, self.now, across)
            elif what[0] == "halve":
                bits = what[1]
                self.parts >>= len(bits)
                self.keep = self.piece(bits, 0)
                self.landed = []
                for mask in range(1, 1 << len(bits)):
                    there = self.landing(self.slots_used, self.parts)
                    self.slots_used += self.parts
                    self.landed.append(there)
                    to = mate([b for k, b in enumerate(bits) if mask >> k & 1])
                    self.go(self.own, self.piece(bits, mask), self.land, there, to)
            elif what[0] == "full":
                self.go(self.own, self.now, self.rx[what[1]], self.small_place(), mates[full_bits[what[1]]])
            else:
                bits, keep = self.trail.pop()
                for mask in range(1, 1 << len(bits)):
                    self.go(self.xr, keep, self.xr, keep, mate([b for k, b in enumerate(bits) if mask >> k & 1]))

        def advance(self):
            if self.finished or self.stage < 0:
                return
            for copy in self.flying:
                copy.wait_recv()
            self.finish_stage()
            self.flying = []
            self.stage += 1
            if self.stage < len(self.stages):
                self.start_stage()
                return
            self.finished = True
            self.done = local(self.xr.at[self.window(self.place)], self.to)

    chunks = []
    refs = (own, oth, xr, land, land_both, rx)
    for i in range(parts):
        slot = (i * 7 * (BLOCK // 8), BLOCK // 8, width)
        to = g2_h.at[pl.ds(i * BLOCK, BLOCK)]
        chunks.append(Region(2 * i, i * BLOCK, BLOCK, width, slot, ORDERS[2 * i], refs, to))
        refs_one = tuple(ref.at[i] for ref in (own1, oth1, xr1, land1, land1_both)) + ([ref.at[i] for ref in rx1],)
        to = g1_h.at[:, pl.ds(i * BLOCK, BLOCK)]
        chunks.append(Region(2 * i + 1, 0, width, BLOCK, (0, width // 8, BLOCK), ORDERS[2 * i + 1], refs_one, to))
    for i in range(4):
        slot = (7 * units // 8 + i * quarter, quarter // 4, width // 2)
        to = go_h if i == 0 else gq_h.at[i - 1]
        chunks.append(Region(2 * parts + i, base_a + i * quarter, quarter, width, slot, ORDERS[2 * parts + i], refs, to))
    first_att = 2 * parts

    def ready(i, j):
        chunks[i].ready(j)

    def hook(name):
        for i in PLAN.get(name, ()):
            chunks[i].advance()

    def chunk_rows(j, i, at):
        span = pl.ds(at, BLOCK)
        cols = slice(j * units + i * BLOCK, j * units + (i + 1) * BLOCK)
        mine = slice(i * BLOCK, (i + 1) * BLOCK)
        bias = (bias_u if j == 0 else uoth)[mine].reshape(1, BLOCK)
        h = dot(n2_s[span], w1_s[j, i]) + bias
        a, slope = gelu_pair(h)
        a_s[span, cols] = a.astype(BF16)
        g = (dot_nt(cot_s[span], w2_s[j, mine]) * slope).astype(BF16)
        g_s[span, cols] = g

    def chunk_grads(j, i):
        cols = slice(j * units + i * BLOCK, j * units + (i + 1) * BLOCK)
        mine = slice(i * BLOCK, (i + 1) * BLOCK)
        to = oth if j == 1 else own

        def second(at):
            to[pl.ds(i * BLOCK + at, 128)] = dot_tn(a_s[:, pl.ds(cols.start + at, 128)], cot_s[...]).astype(BF16)

        loop(BLOCK, 128, second)
        ready(2 * i, j)
        g = g_s[:, cols]

        def first(at):
            (oth1 if j == 1 else own1)[i, pl.ds(at, BLOCK)] = dot(n2t_s[pl.ds(at, BLOCK)], g_s[:, cols]).astype(BF16)

        loop(width, BLOCK, first)
        ready(2 * i + 1, j)
        sm[8 + 8 * j : 9 + 8 * j, mine] = column_sum(g.astype(F32))
        hook(f"f{j}{i}")

    def feed(j, i, first=False):
        if first:
            loop(count, BLOCK, lambda at: chunk_rows(j, i, at))
            n2_copy.wait_recv()
            cot_copy.wait_recv()
            for at in range(0, rows, BLOCK):
                n2t_s[:, at : at + BLOCK] = n2_s[at : at + BLOCK].T
            loop(count, BLOCK, lambda at: chunk_rows(j, i, count + at))
        else:
            loop(rows, BLOCK, lambda at: chunk_rows(j, i, at))
        chunk_grads(j, i)

    sm[...] = jnp.zeros_like(sm)
    unit_copy.wait_recv()
    have_weight(4, 5)
    feed(1, 0, first=True)
    forward_weight(7)
    feed(0, 0)
    have_weight(6, 7)
    forward_weight(8)
    feed(1, 1)
    forward_weight(9)
    feed(0, 1)
    for i in range(2, parts):
        have_weight(4 + 2 * i, 5 + 2 * i)
        feed(1, i)
        feed(0, i)

    def back_two(at):
        span = pl.ds(at, BLOCK)
        total = None
        for j in range(2):
            for i in range(parts):
                at_col = j * units + i * BLOCK
                term = dot_nt(g_s[span, at_col : at_col + BLOCK], w1_s[j, i])
                total = term if total is None else total + term
        return total

    def mlp_part(at):
        span = pl.ds(at, BLOCK)
        return dot(a_s[span, :units], w2_s[0]) + dot(a_s[span, units:], w2_s[1])

    def back_two_sib(at):
        sb2[pl.ds(at, BLOCK)] = back_two(count + at).astype(BF16)

    def back_two_mine(at):
        gm_s[pl.ds(at, BLOCK)] = back_two(at)

    def mlp_sib(at):
        sb1[pl.ds(at, BLOCK)] = mlp_part(count + at).astype(BF16)

    loop(count, BLOCK, back_two_sib)
    gn2_copy = remote(sb2, rb2, csem, 4, sib)
    loop(count, BLOCK, back_two_mine)
    hook("gn2")
    att_copy.wait_send()
    loop(count, BLOCK, mlp_sib)
    mlp_copy = remote(sb1, rb1, csem, 5, sib)
    hook("gn2b")
    gn2_copy.wait_recv()
    n2_copy.wait_send()

    def second_back(at):
        spot = pl.ds(at, 64)
        xhat, sigma = norm_stats(mid_s[spot])
        grad = gm_s[spot] + rb2[spot].astype(F32)
        cot = cot_s[spot].astype(F32)
        back = cot + norm_back(grad, ln2_gain, xhat, sigma)
        gm_s[spot] = back
        n2_s[spot] = back.astype(BF16)
        sm[2:3] += column_sum(back)
        sm[3:4] += column_sum(grad * xhat)
        sm[4:5] += column_sum(grad)
        sm[5:6] += column_sum(cot)

    loop(count, 64, second_back)
    dm_copy = remote(n2_s.at[pl.ds(0, count)], n2_s.at[pl.ds(count, count)], csem, 6, sib)

    hook("ln2")

    def finish_out(at):
        span = pl.ds(at, BLOCK)
        mid_s[span] = mid_s[span] + mlp_part(at) + fc2_bias

    loop(count, BLOCK, finish_out)
    mlp_copy.wait_recv()

    def write_out(at):
        spot = pl.ds(at, 64)
        tok_s[spot] = (mid_s[spot] + rb1[spot].astype(F32)).astype(BF16)

    loop(count, 64, write_out)
    put_out = local(tok_s, out_h)
    hook("fin")
    dm_copy.wait_recv()

    start = base_a + quarter
    zero = jnp.zeros((count, 128), BF16)
    grad_s = dq_s = gr_s

    def keep_gradient(j, c):
        to = oth if j == 1 else own
        low = start + c * quarter
        dt = ot_s.at[j * quarter : (j + 1) * quarter]

        def columns(at):
            to[low : low + quarter, pl.ds(at, BLOCK)] = dot(dt[...], nr_s[:, pl.ds(at, BLOCK)]).astype(BF16)

        loop(width, BLOCK, columns)
        ready(first_att + 1 + c, j)
        if c != 1:
            d = g_s[:, (3 * j + c) * BLOCK : (3 * j + c) * BLOCK + quarter]
            sm[9 + c // 2 + 8 * j : 10 + c // 2 + 8 * j, :quarter] = column_sum(d.astype(F32))

    def values_back(j):
        base = j * quarter
        to = oth if j == 1 else own

        def weight(at):
            to[base_a : base_a + quarter, pl.ds(at, BLOCK)] = dot(ou_s[base : base + quarter], n2_s[:, pl.ds(at, BLOCK)]).astype(BF16)

        loop(width, BLOCK, weight)
        ready(first_att, j)

        def output(at):
            grad_s[base : base + quarter, pl.ds(at, BLOCK)] = dot_nt(wo_s[base : base + quarter], n2_s[pl.ds(at, BLOCK)]).astype(BF16)

        loop(rows, BLOCK, output)
        go_s = a_s.at[:, rows + 256 * j : rows + 256 * (j + 1)]

        def scale(at):
            here = pl.ds(at, BLOCK)
            grad_t = dot_nt(grad_s[base : base + quarter], roll_s[here])
            for head in range(heads):
                row = j * heads + head
                r = r_s[row : row + 1, here]
                g = grad_t[head * HEAD : (head + 1) * HEAD]
                at_head = slice(base + head * HEAD, base + (head + 1) * HEAD)
                in_s[row : row + 1, here] = column_sum(g * ot_s[at_head, here].astype(F32)) * r
                gt_s[at_head, here] = (g * r).astype(BF16)
            go_s[here, :quarter] = gt_s[base : base + quarter, here].T

        loop(rows, BLOCK, scale)

        def block(at):
            here = pl.ds(at, count)
            b = at // count
            dv = [None, None]
            for head in range(heads):
                tile = head // 2
                gh = jnp.where(lane_half(count, head % 2 == 1), go_s[here, 128 * tile : 128 * tile + 128], zero)
                part = dot(e_s[j * heads + head, b], gh)
                dv[tile] = part if dv[tile] is None else dv[tile] + part
            dv = jnp.concatenate(dv, axis=1)[:, :quarter].astype(BF16)
            g_s[here, (3 * j + 2) * BLOCK : (3 * j + 2) * BLOCK + quarter] = dv
            ot_s[base : base + quarter, here] = dv.T

        loop(rows, count, block)
        keep_gradient(j, 2)
        hook(f"v{j}")

    def scores_back(j):
        base = j * quarter

        def block(at):
            here = pl.ds(at, count)
            b = at // count
            dk = [None, None]
            for head in range(heads):
                tile = head // 2
                row = j * heads + head
                half = lane_half(count, head % 2 == 1)
                lanes = slice(128 * tile, 128 * tile + 128)
                vh = jnp.where(half, v_s[j, here, lanes], zero)
                qh = jnp.where(half, q_s[j, here, lanes], zero)
                last_row = min(128 * tile + 128, quarter)
                vh = vh[:, : last_row - 128 * tile]
                ds = a_s.at[:count, head * count : (head + 1) * count] if head < 2 else a_s.at[count:, :count]
                for off in range(0, count, BLOCK):
                    some = pl.ds(pl.multiple_of(at + off, BLOCK), BLOCK)
                    dp_t = dot(vh, gt_s[base + 128 * tile : base + last_row, some])
                    grad = (dp_t - in_s[row : row + 1, some]) * e_s[row, b, :, off : off + BLOCK].astype(F32)
                    ds[:, off : off + BLOCK] = grad.astype(BF16)
                part = dot(ds[...], qh)
                dk[tile] = part if dk[tile] is None else dk[tile] + part
                kth = kt_s[base + head * HEAD : base + head * HEAD + HEAD, here]
                dq_s[base + head * HEAD : base + head * HEAD + HEAD, here] = dot(kth, ds[...]).astype(BF16)
            dk = jnp.concatenate(dk, axis=1)[:, :quarter].astype(BF16)
            g_s[here, (3 * j + 1) * BLOCK : (3 * j + 1) * BLOCK + quarter] = dk
            ot_s[base : base + quarter, here] = dk.T
            g_s[here, 3 * j * BLOCK : 3 * j * BLOCK + quarter] = dq_s[base : base + quarter, here].T

        loop(rows, count, block)
        hook(f"b{j}")
        keep_gradient(j, 1)
        ot_s[base : base + quarter] = dq_s[base : base + quarter]
        keep_gradient(j, 0)
        hook(f"s{j}")

    values_back(1)
    values_back(0)
    scores_back(1)
    scores_back(0)

    def back_one(at):
        total = None
        for j in range(2):
            for c in range(3):
                d = g_s[pl.ds(at, BLOCK), (3 * j + c) * BLOCK : (3 * j + c) * BLOCK + quarter]
                term = dot(d, wq_s[j, c])
                total = term if total is None else total + term
        n2_s[pl.ds(at, BLOCK)] = total.astype(BF16)

    dm_copy.wait_send()
    loop(rows, BLOCK, back_one)
    hook("gn1")
    gn2_copy.wait_send()

    def back_one_sib(at):
        sb2[pl.ds(at, BLOCK)] = dot(back_s[pl.ds(count + at, BLOCK)], n2_s[...]).astype(BF16)

    def back_one_mine(at):
        mid_s[pl.ds(at, BLOCK)] = dot(back_s[pl.ds(at, BLOCK)], n2_s[...])

    loop(count, BLOCK, back_one_sib)
    gn1_copy = remote(sb2, rb2, csem, 7, sib)
    loop(count, BLOCK, back_one_mine)
    hook("gn1b")
    gn1_copy.wait_recv()
    mlp_copy.wait_send()

    def first_back(at):
        spot = pl.ds(at, 64)
        xhat, sigma = norm_stats(sin_s[spot])
        grad = mid_s[spot] + rb2[spot].astype(F32)
        sb1[spot] = (gm_s[spot] + norm_back(grad, ln1_gain, xhat, sigma)).astype(BF16)
        sm[0:1] += column_sum(grad * xhat)
        sm[1:2] += column_sum(grad)

    loop(count, 64, first_back)
    put_in = local(sb1, ing_h)

    state = {}

    def small_start(i):
        if i == 0:
            state["c"] = remote(sm, smr.at[0], ssem, 0, sib)
        elif i == 1:
            state["c"] = remote(sm, smr.at[1], ssem, 1, across)
        else:
            state["c"] = remote(sm.at[pl.ds(0, 16)], smr.at[i, pl.ds(0, 16)], ssem, i, mates[all_bits[i - 2]])
        state["i"] = i

    def small_step():
        i = state["i"]
        state["c"].wait()
        if i == 0:
            sm[0:8] = sm[0:8] + smr[0, 0:8]
        elif i == 1:
            sm[0:8] = sm[0:8] + smr[1, 0:8]
            sm[8:16] = sm[8:16] + smr[1, 16:24]
        else:
            sm[0:16] = sm[0:16] + smr[i, 0:16]
        if i + 1 < 2 + len(all_bits):
            small_start(i + 1)
        else:
            small_o[...] = sm[0:16]

    small_start(0)
    small_left = 2 + len(all_bits)
    for i in PLAN["tail"]:
        if i >= 0:
            chunks[i].advance()
        elif small_left:
            small_step()
            small_left -= 1
    while True:
        busy = False
        for chunk in chunks:
            if not chunk.finished:
                chunk.advance()
                busy = True
        if small_left:
            small_step()
            small_left -= 1
            busy = True
        if not busy:
            break

    for copy in [unit_copy, head_copy, n1_copy, cot_copy, gn1_copy] + by_x + by_y:
        copy.wait_send()
    for chunk in chunks:
        for copy in chunk.sent:
            copy.wait_send()
        chunk.done.wait()
    put_out.wait()
    put_in.wait()


def copies_of(full):
    most = 0
    for kind in ORDERS:
        first, after = KINDS[kind]
        most = max(most, 1 + full + 2 * sum((1 << len(bits)) - 1 for bits in after) + (0 if first is None else 3))
    return most


def call_layer(dp_size, tokens, cotangent, ids, table, vectors, wq, wo, w1, w2):
    count, width = tokens.shape
    rows = 2 * count
    quarter = wo.shape[0]
    units = w1.shape[1]
    heads = quarter // HEAD
    grad_rows = units + 4 * quarter
    parts = units // BLOCK
    bits = [b for b in range(20) if (1 << b) < dp_size]
    half_bits = bits[:3]
    shape = jax.ShapeDtypeStruct
    vm = pltpu.VMEM
    regions = 2 * (units // BLOCK) + 4
    steps = copies_of(len(bits) - len(half_bits))
    fetched = 4 + 2 * (units // BLOCK)
    scratch = (
        [vm((count, width), BF16), vm((rows, width), BF16)]
        + [vm((count, width), F32)] * 3
        + [vm((rows, width), BF16)] * 2
        + [vm((width, rows), BF16)]
        + [vm((2,) + wq.shape, BF16), vm((2 * quarter, width), BF16), vm((2, units // BLOCK, width, BLOCK), BF16), vm((2,) + w2.shape, BF16)]
        + [vm((2, rows, 256), BF16)] * 2
        + [vm((2 * quarter, rows), BF16)] * 5
        + [vm((8, rows), F32)] * 2
        + [vm((2 * heads, 2, count, count), BF16)]
        + [vm((rows, rows), BF16)] * 2
        + [vm((rows, width), BF16)]
        + [vm((rows, 2 * units), BF16)] * 2
        + [vm((count, width), BF16)] * 4
        + [vm((grad_rows, width), BF16)] * 3
        + [vm((7 * units // 8 + 4 * quarter, width), BF16), vm((units // 2, width), BF16)]
        + [vm((parts, width, BLOCK), BF16)] * 3
        + [vm((parts, 7 * width // 8, BLOCK), BF16), vm((parts, width // 2, BLOCK), BF16)]
        + [vm((grad_rows >> len(half_bits), width), BF16)] * (len(bits) - len(half_bits))
        + [vm((parts, width // 8, BLOCK), BF16)] * (len(bits) - len(half_bits))
        + [vm((units,), F32), vm((2, quarter), F32), vm((24, width), F32), vm((2 + len(bits), 24, width), F32)]
        + [pltpu.SemaphoreType.DMA((8 + units // BLOCK + regions,))]
        + [pltpu.SemaphoreType.DMA((2, n)) for n in (2 * fetched + 2, 8, regions * steps, 2 + len(bits))]
    )
    anywhere = pl.BlockSpec(memory_space=pl.ANY)
    inside = pl.BlockSpec(memory_space=pltpu.VMEM)
    return pl.pallas_call(
        functools.partial(layer, dp_size, half_bits),
        out_shape=[shape((count, width), BF16)] * 2
        + [shape(w2.shape, BF16), shape(w1.shape, BF16), shape(wo.shape, BF16), shape(wq.shape, BF16), shape((16, width), F32)],
        in_specs=[anywhere] * 2 + [inside] * (2 + len(vectors)) + [anywhere] * 4,
        out_specs=[anywhere] * 6 + [inside],
        scratch_shapes=scratch,
        compiler_params=pltpu.CompilerParams(vmem_limit_bytes=VMEM_LIMIT, collective_id=0, has_side_effects=True),
        name="layer",
    )(tokens, cotangent, ids, table, *vectors, wq, wo, w1, w2)


def finish(out, ing, g2, g1, go, gq, small, out_o, ing_o, g2_o, g1_o, go_o, gq_o, a0, a1, a2, a3, a4, a5, units_o, heads_o):
    for src, dst in ((out, out_o), (ing, ing_o), (g2, g2_o), (g1, g1_o), (go, go_o), (gq, gq_o)):
        dst[...] = src[...].astype(dst.dtype)

    @pl.when(pl.program_id(0) == 0)
    def _():
        for i, ref in enumerate((a0, a1, a2, a3, a4, a5)):
            ref[...] = small[i]
        units_o[...] = small[8, : units_o.shape[0]]
        heads_o[...] = small[9:11, : heads_o.shape[1]]


def call_finish(arrays, small, units, quarter):
    steps = 4
    width = small.shape[1]
    shape = jax.ShapeDtypeStruct

    def rows_of(a):
        axis = a.ndim - 2
        block = a.shape[:axis] + (a.shape[axis] // steps,) + a.shape[axis + 1 :]
        return pl.BlockSpec(block, lambda i, axis=axis, rank=a.ndim: tuple(i if k == axis else 0 for k in range(rank)))

    def whole(extent):
        return pl.BlockSpec(extent, lambda i, rank=len(extent): (0,) * rank)

    extents = [(width,)] * 6 + [(units,), (2, quarter)]
    kinds = [BF16, BF16, F32, F32, F32, F32]
    return pl.pallas_call(
        finish,
        grid=(steps,),
        in_specs=[rows_of(a) for a in arrays] + [whole(small.shape)],
        out_specs=[rows_of(a) for a in arrays] + [whole(e) for e in extents],
        out_shape=[shape(a.shape, k) for a, k in zip(arrays, kinds)] + [shape(e, F32) for e in extents],
        compiler_params=pltpu.CompilerParams(vmem_limit_bytes=VMEM_LIMIT),
        name="finish",
    )(*arrays, small)


def per_device(
    tokens, segment_ids, ln1_gain, ln1_bias, qkv_weight, qv_bias, out_weight, out_bias,
    ln2_gain, ln2_bias, fc1_weight, fc1_bias, fc2_weight, fc2_bias, cotangent,
):
    width = tokens.shape[1]
    freq_count = width // 6
    frequency = 10000.0 ** (-jnp.arange(freq_count, dtype=F32) / freq_count)
    angles = jnp.arange(SIDE, dtype=F32)[:, None] * frequency[None, :]
    table = jnp.concatenate([jnp.sin(angles), jnp.cos(angles)], axis=1)
    vectors = (ln1_gain, ln1_bias, out_bias, ln2_gain, ln2_bias, fc2_bias, fc1_bias, qv_bias)
    *arrays, small = call_layer(
        lax.axis_size("dp"), tokens, cotangent, segment_ids, table, vectors, qkv_weight.transpose(0, 2, 1), out_weight, fc1_weight, fc2_weight
    )
    out, ing, g2, g1, go, gq, a0, a1, a2, a3, a4, a5, g_units, g_heads = call_finish(arrays, small, fc1_weight.shape[1], out_weight.shape[0])
    return (out, ing, a0, a1, gq.transpose(0, 2, 1), g_heads, go, a2, a3, a4, g1, g_units, g2, a5)


def solution(mesh):
    placed = (
        P(("dp", "tensor"), None),
        P("dp", None),
        P(),
        P(),
        P(None, None, "tensor"),
        P(None, "tensor"),
        P("tensor", None),
        P(),
        P(),
        P(),
        P(None, "tensor"),
        P("tensor"),
        P("tensor", None),
        P(),
        P(("dp", "tensor"), None),
    )
    return jax.shard_map(
        per_device,
        mesh=mesh,
        in_specs=placed,
        out_specs=(
            P(("dp", "tensor"), None),
            P(("dp", "tensor"), None),
            P(),
            P(),
            P(None, None, "tensor"),
            P(None, "tensor"),
            P("tensor", None),
            P(),
            P(),
            P(),
            P(None, "tensor"),
            P("tensor"),
            P("tensor", None),
            P(),
        ),
        check_vma=False,
    )
```

```python
import functools

import jax
import jax.numpy as jnp
from jax import lax
from jax.experimental import pallas as pl
from jax.experimental.pallas import tpu as pltpu
from jax.sharding import PartitionSpec as P

HEAD = 64
SIDE = 16
EPSILON = 1e-06
NEG_LARGE = -1e30
SCALE = HEAD ** (-0.5)
F32 = jnp.float32
BF16 = jnp.bfloat16
VMEM_LIMIT = 64 * 1024 * 1024 - 128 * 1024
MESH = pl.DeviceIdType.MESH
BLOCK = 256
KINDS = {
    "A": (None, ((0,), (1,), (2,))),
    "B": (None, ((1,), (0,), (2,))),
    "D": (None, ((0,), (1, 2))),
    "E": (None, ((0, 1, 2),)),
    "Y": (0, ((1,), (2,))),
    "Z": (1, ((0,), (2,))),
    "YD": (0, ((1, 2),)),
}
ORDERS = ("D", "A", "Y", "Z", "D", "Z", "B", "D", "D", "D")
WEIGHT_PLAN = {"p0": (0,), "a0": (1,), "a1": (2,), "p1": (3, 4), "a2": (5,), "u": (6,), "n": (7,), "f10": (8,), "f11": (9,)}
PLAN = {
    "f12": (0,),
    "gn2": (1, 2, 3),
    "ln2": (0,),
    "fin": (4, 1, -1, 5),
    "v1": (2, 0, 3, 1),
    "v0": (4, -1, 5, 2),
    "b1": (3, 0, 1, 6, 5),
    "s1": (4,),
    "b0": (2, 9, 3, 0, 6, 1),
    "s0": (5, 8),
    "gn1": (4, 9),
    "tail": (1, 6, 2, 7, 3, 8, 5, -2, 4, 9, 6, 2, 1, 8, 7, 3, 5, 9, -2, 6, 8, 2, 3, 7, 9, 6, 5, 8, 7, 6, 7),
}


def dot(a, b):
    return jnp.dot(a, b, preferred_element_type=F32)


def dot_nt(a, b):
    return lax.dot_general(a, b, (((1,), (1,)), ((), ())), preferred_element_type=F32)


def dot_tn(a, b):
    return lax.dot_general(a, b, (((0,), (0,)), ((), ())), preferred_element_type=F32)


def lane_half(rows, upper):
    lanes = lax.broadcasted_iota(jnp.int32, (rows, 128), 1)
    return lanes >= HEAD if upper else lanes < HEAD


def head_lanes(ref, head, filler):
    tile = ref[:, 128 * (head // 2) : 128 * (head // 2) + 128]
    return jnp.where(lane_half(tile.shape[0], head % 2 == 1), tile, filler)


def gelu_pair(h):
    cdf = 0.5 + 0.5 * lax.erf(h * 0.7071067811865476)
    return h * cdf, cdf + h * jnp.exp(-0.5 * h * h) * 0.3989422804014327


def norm_stats(v):
    centred = v - jnp.mean(v, axis=-1, keepdims=True)
    sigma = lax.rsqrt(jnp.mean(centred * centred, axis=-1, keepdims=True) + EPSILON)
    return centred * sigma, sigma


def norm_back(grad, gain, xhat, sigma):
    g = grad * gain
    return sigma * (g - jnp.mean(g, axis=-1, keepdims=True) - xhat * jnp.mean(g * xhat, axis=-1, keepdims=True))


def column_sum(v):
    return jnp.sum(v, axis=0, keepdims=True)


def loop(count, step, body):
    def run(i, carry):
        body(pl.multiple_of(i * step, step))
        return carry

    lax.fori_loop(0, count // step, run, 0)


def layer(
    dp_size, half_bits,
    tok_h, cot_h, ids, table, gain1, bias1, bias_o, gain2, bias2, bias_f, bias_u, bias_qv, wq_h, wo_h, w1_h, w2_h,
    out_h, ing_h, g2_h, g1_h, go_h, gq_h, small_o,
    tok_s, cot_s, sin_s, mid_s, gm_s, n1_s, n2_s, n2t_s, wq_s, wo_s, w1_s, w2_s,
    q_s, v_s, kt_s, ot_s, ou_s, gt_s, gr_s, r_s, in_s, e_s, roll_s, back_s, nr_s, a_s, g_s, sb1, sb2, rb1, rb2,
    own, oth, xr, land, land_both, own1, oth1, xr1, land1, land1_both, *rest,
):
    rest = list(rest)
    full_bits = [b for b in range(20) if (1 << b) < dp_size and b not in half_bits]
    rx = [rest.pop(0) for _ in full_bits]
    rx1 = [rest.pop(0) for _ in full_bits]
    uoth, voth, early, late, near, far, lsem, wsem, csem, gsem, ssem = rest

    count, width = tok_s.shape
    rows = 2 * count
    quarter = wo_h.shape[0]
    units = w1_h.shape[1]
    heads = quarter // HEAD
    place = lax.axis_index("tensor")
    dp = lax.axis_index("dp")
    chip = place // 2
    core = place % 2
    sib = {"tensor": chip * 2 + 1 - core}
    across = {"tensor": (1 - chip) * 2 + core}
    facing = {"tensor": (1 - chip) * 2 + 1 - core}
    all_bits = list(half_bits) + full_bits
    sides = {b: (dp // (1 << b)) % 2 for b in all_bits}

    def mate(bits):
        return {"dp": dp + sum((1 - 2 * sides[b]) * (1 << b) for b in bits)}

    mates = {b: mate((b,)) for b in all_bits}
    groups = {(b,) for b in full_bits}
    for mask in range(1, 1 << len(half_bits)):
        groups.add(tuple(b for k, b in enumerate(half_bits) if mask >> k & 1))

    barrier = pltpu.get_barrier_semaphore()
    partners = [sib, across, facing] + [mate(bits) for bits in sorted(groups)]
    for partner in partners:
        pl.semaphore_signal(barrier, inc=1, device_id=partner, device_id_type=MESH)

    sq_s, sk_s, k_s = a_s.at[:, 0:128], a_s.at[:, 128:256], a_s.at[:, 256:512]
    local_used = [0]

    def local(src, dst):
        copy = pltpu.make_async_copy(src, dst, lsem.at[local_used[0]])
        local_used[0] += 1
        copy.start()
        return copy

    def remote(src, dst, sems, index, device):
        copy = pltpu.make_async_remote_copy(
            src_ref=src, dst_ref=dst, send_sem=sems.at[0, index], recv_sem=sems.at[1, index], device_id=device, device_id_type=MESH
        )
        copy.start()
        return copy

    def half_copy(src, dst, first, at):
        return pltpu.make_async_remote_copy(
            src_ref=src,
            dst_ref=dst,
            send_sem=csem.at[0, first + at // BLOCK],
            recv_sem=csem.at[1, first + at // BLOCK],
            device_id=sib,
            device_id_type=MESH,
        )

    get_tok = local(tok_h, tok_s)
    get_cot = local(cot_h, cot_s.at[pl.ds(0, count)])
    get_wq = local(wq_h, wq_s.at[0])
    get_wo = local(wo_h, wo_s.at[pl.ds(0, quarter)])
    get_w1 = [local(w1_h.at[:, pl.ds(i * BLOCK, BLOCK)], w1_s.at[0, i]) for i in range(units // BLOCK)]
    get_w2 = local(w2_h, w2_s.at[0])

    ln1_gain, ln1_bias, out_bias, ln2_gain, ln2_bias, fc2_bias = (
        ref[...].reshape(1, width) for ref in (gain1, bias1, bias_o, gain2, bias2, bias_f)
    )
    get_tok.wait()

    def first_norm(at):
        plane = core * (count // (SIDE * SIDE)) + at // (SIDE * SIDE)
        line = (at // SIDE) % SIDE
        shape = (SIDE, width // 3)
        for k in range(4):
            spot = jnp.concatenate(
                [jnp.broadcast_to(table[pl.ds(plane, 1)], shape), jnp.broadcast_to(table[pl.ds(line + k, 1)], shape), table[...]], axis=1
            )
            span = pl.ds(pl.multiple_of(at + k * SIDE, SIDE), SIDE)
            stream = tok_s[span].astype(F32) + spot
            sin_s[span] = stream
            xhat, _ = norm_stats(stream)
            n1_s[span] = (xhat * ln1_gain + ln1_bias).astype(BF16)

    loop(count, 4 * SIDE, first_norm)
    doc = ids[pl.ds(chip, 1), :]
    starts = [jnp.zeros((1, 1), F32)]
    starts += [jnp.sum(jnp.where(doc < v, 1.0, 0.0), axis=1, keepdims=True) for v in range(1, 4)]
    starts.append(jnp.full((1, 1), rows, F32))
    turn = jnp.zeros((1, 1), F32)
    for v in range(4):
        turn += jnp.where(starts[v + 1] - starts[v] == count, starts[v], 0.0)
    turn_here = turn - (core * count).astype(F32)

    def wrapped(v):
        v = jnp.where(v >= rows, v - rows, v)
        return jnp.where(v < 0, v + rows, v)

    def rotations(at):
        down = (lax.broadcasted_iota(jnp.int32, (64, rows), 0) + at).astype(F32)
        along = lax.broadcasted_iota(jnp.int32, (64, rows), 1).astype(F32)
        roll_s[pl.ds(at, 64)] = jnp.where(wrapped(down + turn_here) == along, 1.0, 0.0).astype(BF16)
        back_s[pl.ds(at, 64)] = jnp.where(wrapped(down - turn_here) == along, 1.0, 0.0).astype(BF16)
        where = wrapped((lax.broadcasted_iota(jnp.int32, (64, 128), 0) + at).astype(F32) + turn)
        mine = sum(jnp.where(where >= starts[v], 1.0, 0.0) for v in range(1, 4))
        slot = (lax.broadcasted_iota(jnp.int32, (64, 128), 1) % HEAD).astype(F32)
        sq_s[pl.ds(at, 64)] = jnp.where((slot < 4) & (slot != mine), 1.0, 0.0).astype(BF16)
        sk_s[pl.ds(at, 64)] = jnp.where(slot == mine, NEG_LARGE, 0.0).astype(BF16)


    pl.semaphore_wait(barrier, len(partners))
    unit_copy = remote(bias_u, uoth, wsem, 3 * (4 + 2 * (units // BLOCK)), across)
    head_copy = remote(bias_qv, voth, wsem, 3 * (4 + 2 * (units // BLOCK)) + 1, across)
    get_wq.wait()
    get_wo.wait()
    for copy in get_w1:
        copy.wait()
    get_w2.wait()

    part = (sides[0] + sides[1]) % 2

    class Piece:
        def __init__(self, index, refs, at, extent):
            self.index, self.refs, self.at, self.size = index, refs, at, extent // 4
            self.stage, self.sent = 0, []

        def rows(self, k, first, size):
            row = pl.multiple_of(self.at[k] + 2 * part * self.size + first, 16)
            return self.refs[k].at[pl.ds(row, size)]

        def go(self, src, dst, k, device):
            self.sent.append(remote(src, dst, wsem, 3 * self.index + k, device))

        def start(self):
            self.go(self.rows(0, 0, 2 * self.size), self.rows(1, 0, 2 * self.size), 0, across)

        def advance(self):
            if self.stage == 0:
                self.sent[0].wait_recv()
                for k in range(2):
                    some = self.rows(1, k * self.size, self.size)
                    self.go(some, some, 1 + k, mates[k])
            else:
                self.sent[1].wait_recv()
                self.sent[2].wait_recv()
            self.stage += 1

    pieces = [Piece(c, (wq_s.at[0, c], wq_s.at[1, c]), (0, 0), quarter) for c in range(3)]
    pieces.append(Piece(3, (wo_s, wo_s), (0, quarter), quarter))
    for i in range(units // BLOCK):
        pieces.append(Piece(4 + 2 * i, (w1_s.at[0, i], w1_s.at[1, i]), (0, 0), width))
        pieces.append(Piece(5 + 2 * i, (w2_s.at[0], w2_s.at[1]), (i * BLOCK, i * BLOCK), BLOCK))
    for item in pieces:
        item.start()

    def pass_on(name):
        for i in WEIGHT_PLAN.get(name, ()):
            if pieces[i].stage < 1:
                pieces[i].advance()

    def have_weight(*which):
        for i in which:
            while pieces[i].stage < 2:
                pieces[i].advance()

    n1_copy = remote(n1_s.at[pl.ds(0, count)], n1_s.at[pl.ds(count, count)], csem, 0, sib)
    get_cot.wait()
    cot_copy = remote(cot_s.at[pl.ds(0, count)], cot_s.at[pl.ds(count, count)], csem, 1, sib)

    def rotate(at):
        nr_s[pl.ds(at, BLOCK)] = dot(roll_s[pl.ds(at, BLOCK)], n1_s[...]).astype(BF16)

    def project(j, at):
        n = nr_s[pl.ds(at, BLOCK)]
        biases = bias_qv if j == 0 else voth
        q = (dot_nt(n, wq_s[j, 0]) + biases[0:1]).astype(BF16) * SCALE
        k = dot_nt(n, wq_s[j, 1]).astype(BF16)
        v = (dot_nt(n, wq_s[j, 2]) + biases[1:2]).astype(BF16)
        q_s[j, pl.ds(at, BLOCK), :quarter] = q
        k_s[pl.ds(at, BLOCK), :quarter] = k
        v_s[j, pl.ds(at, BLOCK), :quarter] = v
        kt_s[j * quarter : (j + 1) * quarter, pl.ds(at, BLOCK)] = k.T * SCALE

    blocks = [(b, at) for b in range(2) for at in range(0, count, BLOCK)]

    def attend(j):
        for head in range(heads):
            at = 512 + 256 * head
            a_s[:, at : at + 128] = head_lanes(q_s.at[j], head, sq_s[...])
            a_s[:, at + 128 : at + 256] = head_lanes(k_s, head, sk_s[...])
        for at in range(0, rows, BLOCK):
            ou_s[:quarter, at : at + BLOCK] = v_s[j, at : at + BLOCK, :quarter].T

        def tile(here):
            b = here // count
            at = pl.multiple_of(here % count, BLOCK)
            keys = pl.ds(pl.multiple_of(b * count, count), count)
            for head in range(heads):
                column = 512 + 256 * head
                s = dot_nt(a_s[keys, column + 128 : column + 256], a_s[pl.ds(here, BLOCK), column : column + 128])
                m = jnp.max(s, axis=0, keepdims=True)
                e = jnp.exp(s - m)
                r = 1.0 / column_sum(e)
                low = e.astype(BF16)
                span = slice(head * HEAD, head * HEAD + HEAD)
                to = slice(j * quarter + head * HEAD, j * quarter + head * HEAD + HEAD)
                e_s[j * heads + head, b, :, pl.ds(at, BLOCK)] = low
                ot_s[to, pl.ds(here, BLOCK)] = (dot(ou_s[span, keys], low) * r).astype(BF16)
                r_s[j * heads + head : j * heads + head + 1, pl.ds(here, BLOCK)] = r

        return tile

    loop(rows, 64, rotations)
    n1_copy.wait_recv()
    loop(rows, BLOCK, rotate)
    loop(rows, BLOCK, lambda at: project(0, at))
    pass_on("p0")
    tile = attend(0)
    loop(rows // 2, BLOCK, tile)
    pass_on("a0")
    loop(rows // 2, BLOCK, lambda at: tile(at + rows // 2))
    pass_on("a1")
    head_copy.wait_recv()
    have_weight(0, 1, 2)
    loop(rows, BLOCK, lambda at: project(1, at))
    pass_on("p1")
    tile = attend(1)
    loop(rows // 2, BLOCK, tile)
    pass_on("a2")
    loop(rows // 2, BLOCK, lambda at: tile(at + rows // 2))
    pass_on("a3")

    have_weight(3)

    def unrotate(at):
        ou_s[:, pl.ds(at, BLOCK)] = dot(ot_s[...], roll_s[:, pl.ds(at, BLOCK)]).astype(BF16)

    loop(rows, BLOCK, unrotate)
    pass_on("u")

    def out_part(at):
        return dot_tn(ou_s[:, pl.ds(at, BLOCK)], wo_s[...])

    def att_half(at):
        return half_copy(sb1.at[pl.ds(at, BLOCK)], rb1.at[pl.ds(at, BLOCK)], 2, at)

    def n2_half(at):
        return half_copy(n2_s.at[pl.ds(at, BLOCK)], n2_s.at[pl.ds(pl.multiple_of(count + at, BLOCK), BLOCK)], 4, at)

    def out_sib(at):
        sb1[pl.ds(at, BLOCK)] = out_part(count + at).astype(BF16)
        att_half(at).start()

    loop(count, BLOCK, out_sib)

    def out_mine(at):
        mid_s[pl.ds(at, BLOCK)] = sin_s[pl.ds(at, BLOCK)] + out_part(at) + out_bias

    loop(count, BLOCK, out_mine)
    pass_on("o")

    def second_norm(at):
        att_half(at).wait_recv()
        for off in range(0, BLOCK, 128):
            spot = pl.ds(pl.multiple_of(at + off, 128), 128)
            mid = mid_s[spot] + rb1[spot].astype(F32)
            mid_s[spot] = mid
            xhat, _ = norm_stats(mid)
            n2_s[spot] = (xhat * ln2_gain + ln2_bias).astype(BF16)
        n2_half(at).start()

    loop(count, BLOCK, second_norm)
    pass_on("n")

    base_a = units
    parts = units // BLOCK
    steps = copies_of(len(full_bits))

    class Region:
        def __init__(self, index, row, size, cols, slot, kind, refs, to):
            self.place = self.now = (row, size, 0, cols)
            self.own, self.oth, self.xr, self.land, self.land_both, self.rx = refs
            self.to = to
            self.index, self.slot, self.used = index, slot, 0
            self.first, self.after = KINDS[kind]
            self.stages = [] if self.first is None else ["first"]
            self.stages += ["x"] + [("halve", bits) for bits in self.after] + [("full", i) for i in range(len(full_bits))]
            self.last_sum = len(self.stages) - 1
            self.stages += [("gather", bits) for bits in reversed(self.after)]
            if self.first is not None:
                self.stages.append(("gather", (self.first,)))
            self.stage, self.flying, self.sent, self.trail = -1, [], [], []
            self.parts, self.slots_used = 8, 0
            self.finished = False

        def window(self, where):
            row, size, col, cols = where
            return pl.ds(row, size), pl.ds(col, cols)

        def go(self, src, src_at, dst, dst_at, device):
            copy = remote(src.at[self.window(src_at)], dst.at[self.window(dst_at)], gsem, self.index * steps + self.used, device)
            self.used += 1
            self.flying.append(copy)
            self.sent.append(copy)

        def cut(self, where, side):
            row, size, col, cols = where
            if (size // 2) % 16 == 0:
                return pl.multiple_of(row + side * (size // 2), 16), size // 2, col, cols
            return row, size, pl.multiple_of(col + side * (cols // 2), 128), cols // 2

        def piece(self, bits, mask):
            where = self.now
            for k, b in enumerate(bits):
                where = self.cut(where, 1 - sides[b] if mask >> k & 1 else sides[b])
            return where

        def landing(self, at, parts_here):
            row, rows_one, cols_one = self.slot
            full = self.place[3]
            if cols_one == full:
                return row + at * rows_one, parts_here * rows_one, 0, full
            if parts_here == 1:
                return row + at // 2 * rows_one, rows_one, at % 2 * cols_one, cols_one
            return row + at // 2 * rows_one, parts_here // 2 * rows_one, 0, full

        def ready(self, j):
            if self.first is not None:
                self.stage = 0
                give = self.piece((self.first,), 1)
                if j == 0:
                    self.go(self.own, give, self.land, self.landing(0, 4), mates[self.first])
                else:
                    row, size, col, cols = self.place
                    self.both = (row // 2, size // 2, col, cols)
                    self.go(self.oth, give, self.land_both, self.both, mates[self.first])
            elif j == 1:
                self.stage = 0
                self.go(self.oth, self.now, self.xr, self.now, across)

        def add(self, into, base, where, *terms):
            row, size, col, cols = where
            step = 64 if size % 64 == 0 else 48 if size % 48 == 0 else 32

            def body(off):
                to = (pl.ds(pl.multiple_of(row + off, 16), step), pl.ds(col, cols))
                total = base[to].astype(F32)
                for ref, (r, _, c, _) in terms:
                    total += ref[pl.ds(pl.multiple_of(r + off, 16), step), pl.ds(c, cols)].astype(F32)
                into[to] = total.astype(BF16)

            loop(size, step, body)

        def finish_stage(self):
            what = self.stages[self.stage]
            dest = self.xr if self.stage == self.last_sum else self.own
            if what == "first":
                keep = self.piece((self.first,), 0)
                self.add(self.own, self.own, keep, (self.land, self.landing(0, 4)))
                self.add(self.oth, self.oth, keep, (self.land_both, self.both))
                self.trail.append(((self.first,), keep))
                self.now, self.parts, self.slots_used = keep, 4, 4
            elif what == "x":
                self.add(dest, self.own, self.now, (self.xr, self.now))
            elif what[0] == "halve":
                self.add(dest, self.own, self.keep, *[(self.land, at) for at in self.landed])
                self.trail.append((what[1], self.keep))
                self.now = self.keep
            elif what[0] == "full":
                for copy in self.flying:
                    copy.wait_send()
                    self.sent = [c for c in self.sent if c is not copy]
                self.add(dest, self.own, self.now, (self.rx[what[1]], self.small_place()))

        def small_place(self):
            row, rows_one, cols_one = self.slot
            if cols_one == self.place[3]:
                return row // 7, rows_one, 0, cols_one
            k = (self.place[0] - base_a) // quarter
            return units // 8 + k // 2 * rows_one, rows_one, k % 2 * cols_one, cols_one

        def start_stage(self):
            what = self.stages[self.stage]
            if what == "x":
                self.go(self.oth, self.now, self.xr, self.now, across)
            elif what[0] == "halve":
                bits = what[1]
                self.parts >>= len(bits)
                self.keep = self.piece(bits, 0)
                self.landed = []
                for mask in range(1, 1 << len(bits)):
                    there = self.landing(self.slots_used, self.parts)
                    self.slots_used += self.parts
                    self.landed.append(there)
                    to = mate([b for k, b in enumerate(bits) if mask >> k & 1])
                    self.go(self.own, self.piece(bits, mask), self.land, there, to)
            elif what[0] == "full":
                self.go(self.own, self.now, self.rx[what[1]], self.small_place(), mates[full_bits[what[1]]])
            else:
                bits, keep = self.trail.pop()
                for mask in range(1, 1 << len(bits)):
                    self.go(self.xr, keep, self.xr, keep, mate([b for k, b in enumerate(bits) if mask >> k & 1]))

        def advance(self):
            if self.finished or self.stage < 0:
                return
            for copy in self.flying:
                copy.wait_recv()
            self.finish_stage()
            self.flying = []
            self.stage += 1
            if self.stage < len(self.stages):
                self.start_stage()
                return
            self.finished = True
            self.done = local(self.xr.at[self.window(self.place)], self.to)

    chunks = []
    refs = (own, oth, xr, land, land_both, rx)
    for i in range(parts):
        slot = (i * 7 * (BLOCK // 8), BLOCK // 8, width)
        to = g2_h.at[pl.ds(i * BLOCK, BLOCK)]
        chunks.append(Region(2 * i, i * BLOCK, BLOCK, width, slot, ORDERS[2 * i], refs, to))
        refs_one = tuple(ref.at[i] for ref in (own1, oth1, xr1, land1, land1_both)) + ([ref.at[i] for ref in rx1],)
        to = g1_h.at[:, pl.ds(i * BLOCK, BLOCK)]
        chunks.append(Region(2 * i + 1, 0, width, BLOCK, (0, width // 8, BLOCK), ORDERS[2 * i + 1], refs_one, to))
    for i in range(4):
        slot = (7 * units // 8 + i * quarter, quarter // 4, width // 2)
        to = go_h if i == 0 else gq_h.at[i - 1]
        chunks.append(Region(2 * parts + i, base_a + i * quarter, quarter, width, slot, ORDERS[2 * parts + i], refs, to))
    first_att = 2 * parts

    class Small:
        def __init__(self, tile, index, everywhere, paired):
            self.tile, self.everywhere, self.paired = tile, everywhere, paired
            self.near = [near.at[3 * index + k] for k in range(3)]
            self.far = [far.at[(7 + len(full_bits)) * index + k] for k in range(7 + len(full_bits))]
            self.base, self.used = index * (10 + len(full_bits)), 0
            self.stage, self.flying, self.sent, self.finished = -1, [], [], False

        def go(self, landing, device):
            copy = remote(self.tile, landing, ssem, self.base + self.used, device)
            self.used += 1
            self.flying.append(copy)
            self.sent.append(copy)

        def start(self):
            self.stage = 0
            for landing, device in zip(self.near, (sib, across, facing)):
                self.go(landing, device)

        def advance(self):
            if self.finished or self.stage < 0:
                return
            for copy in self.flying:
                copy.wait()
            self.sent, self.flying = [], []
            tile = self.tile
            if self.stage == 0:
                beside, over, facing_ = self.near
                n, p = self.everywhere, self.paired
                tile[0:n] = (tile[0:n] + beside[0:n]) + (over[0:n] + facing_[0:n])
                tile[n : n + p] = tile[n : n + p] + over[n + p : n + 2 * p]
            elif self.stage == 1:
                got = [tile] + self.far[:7]
                pairs = [got[2 * k][...] + got[2 * k + 1][...] for k in range(4)]
                tile[...] = (pairs[0] + pairs[1]) + (pairs[2] + pairs[3])
            else:
                tile[...] = tile[...] + self.far[5 + self.stage][...]
            self.stage += 1
            if self.stage == 1:
                for mask in range(1, 8):
                    self.go(self.far[mask - 1], mate([b for k, b in enumerate(half_bits) if mask >> k & 1]))
            elif self.stage - 2 < len(full_bits):
                self.go(self.far[5 + self.stage], mates[full_bits[self.stage - 2]])
            else:
                self.finished = True

    first_small = Small(early, 0, 4, 1)
    last_small = Small(late, 1, 2, 2)

    def ready(i, j):
        chunks[i].ready(j)

    def hook(name):
        for i in PLAN.get(name, ()):
            (chunks + [last_small, first_small])[i].advance()

    def chunk_rows(j, i, at):
        span = pl.ds(at, BLOCK)
        cols = slice(j * units + i * BLOCK, j * units + (i + 1) * BLOCK)
        mine = slice(i * BLOCK, (i + 1) * BLOCK)
        bias = (bias_u if j == 0 else uoth)[mine].reshape(1, BLOCK)
        h = dot(n2_s[span], w1_s[j, i]) + bias
        a, slope = gelu_pair(h)
        a_s[span, cols] = a.astype(BF16)
        g = (dot_nt(cot_s[span], w2_s[j, mine]) * slope).astype(BF16)
        g_s[span, cols] = g

    def chunk_grads(j, i):
        cols = slice(j * units + i * BLOCK, j * units + (i + 1) * BLOCK)
        mine = slice(i * BLOCK, (i + 1) * BLOCK)
        to = oth if j == 1 else own

        def second(at):
            to[pl.ds(i * BLOCK + at, 128)] = dot_tn(a_s[:, pl.ds(cols.start + at, 128)], cot_s[...]).astype(BF16)

        loop(BLOCK, 128, second)
        ready(2 * i, j)
        g = g_s[:, cols]

        def first(at):
            (oth1 if j == 1 else own1)[i, pl.ds(at, BLOCK)] = dot(n2t_s[pl.ds(at, BLOCK)], g_s[:, cols]).astype(BF16)

        loop(width, BLOCK, first)
        ready(2 * i + 1, j)
        early[4 + j : 5 + j, mine] = column_sum(g.astype(F32))
        hook(f"f{j}{i}")

    def feed(j, i, first=False):
        if first:
            loop(count, BLOCK, lambda at: chunk_rows(j, i, at))
            cot_copy.wait_recv()

            def received(at):
                n2_half(at).wait_recv()
                chunk_rows(j, i, count + at)

            loop(count, BLOCK, received)

            def turned(at):
                n2t_s[:, pl.ds(at, BLOCK)] = n2_s[pl.ds(at, BLOCK)].T

            loop(rows, BLOCK, turned)
        else:
            loop(rows, BLOCK, lambda at: chunk_rows(j, i, at))
        chunk_grads(j, i)

    early[...] = jnp.zeros_like(early)
    late[...] = jnp.zeros_like(late)
    unit_copy.wait_recv()
    for i in range(parts):
        have_weight(4 + 2 * i, 5 + 2 * i)
        feed(1, i, first=i == 0)
        pass_on(f"f1{i}")
        feed(0, i)
        pass_on(f"f0{i}")

    def back_two(at):
        span = pl.ds(at, BLOCK)
        total = None
        for j in range(2):
            for i in range(parts):
                at_col = j * units + i * BLOCK
                term = dot_nt(g_s[span, at_col : at_col + BLOCK], w1_s[j, i])
                total = term if total is None else total + term
        return total

    def mlp_part(at):
        span = pl.ds(at, BLOCK)
        return dot(a_s[span, :units], w2_s[0]) + dot(a_s[span, units:], w2_s[1])

    def gn2_half(at):
        return half_copy(sb2.at[pl.ds(at, BLOCK)], rb2.at[pl.ds(at, BLOCK)], 6, at)

    def dm_half(at):
        return half_copy(n2_s.at[pl.ds(at, BLOCK)], n2_s.at[pl.ds(pl.multiple_of(count + at, BLOCK), BLOCK)], 10, at)

    def back_two_sib(at):
        sb2[pl.ds(at, BLOCK)] = back_two(count + at).astype(BF16)
        gn2_half(at).start()

    def back_two_mine(at):
        gm_s[pl.ds(at, BLOCK)] = back_two(at)

    def mlp_sib(at):
        sb1[pl.ds(at, BLOCK)] = mlp_part(count + at).astype(BF16)

    loop(count, BLOCK, back_two_sib)
    loop(count, BLOCK, back_two_mine)
    hook("gn2")

    def second_back(at):
        gn2_half(at).wait_recv()
        n2_half(at).wait_send()
        for off in range(0, BLOCK, 128):
            spot = pl.ds(pl.multiple_of(at + off, 128), 128)
            xhat, sigma = norm_stats(mid_s[spot])
            grad = gm_s[spot] + rb2[spot].astype(F32)
            cot = cot_s[spot].astype(F32)
            back = cot + norm_back(grad, ln2_gain, xhat, sigma)
            gm_s[spot] = back
            n2_s[spot] = back.astype(BF16)
            early[0:1] += column_sum(back)
            early[1:2] += column_sum(grad * xhat)
            early[2:3] += column_sum(grad)
            early[3:4] += column_sum(cot)
        dm_half(at).start()

    loop(count, BLOCK, second_back)
    for at in range(0, count, BLOCK):
        att_half(at).wait_send()
    loop(count, BLOCK, mlp_sib)
    mlp_copy = remote(sb1, rb1, csem, 8, sib)
    first_small.start()
    hook("ln2")

    def finish_out(at):
        span = pl.ds(at, BLOCK)
        mid_s[span] = mid_s[span] + mlp_part(at) + fc2_bias

    loop(count, BLOCK, finish_out)
    mlp_copy.wait_recv()

    def write_out(at):
        spot = pl.ds(at, 128)
        tok_s[spot] = (mid_s[spot] + rb1[spot].astype(F32)).astype(BF16)

    loop(count, 128, write_out)
    put_out = local(tok_s, out_h)
    hook("fin")
    for at in range(0, count, BLOCK):
        dm_half(at).wait_recv()

    start = base_a + quarter
    zero = jnp.zeros((count, 128), BF16)
    grad_s = dq_s = gr_s

    def keep_gradient(j, c):
        to = oth if j == 1 else own
        low = start + c * quarter
        dt = ot_s.at[j * quarter : (j + 1) * quarter]

        def columns(at):
            to[low : low + quarter, pl.ds(at, BLOCK)] = dot(dt[...], nr_s[:, pl.ds(at, BLOCK)]).astype(BF16)

        loop(width, BLOCK, columns)
        ready(first_att + 1 + c, j)
        if c != 1:
            d = g_s[:, (3 * j + c) * BLOCK : (3 * j + c) * BLOCK + quarter]
            late[2 + c // 2 + 2 * j : 3 + c // 2 + 2 * j, :quarter] = column_sum(d.astype(F32))

    def values_back(j):
        base = j * quarter
        to = oth if j == 1 else own

        def weight(at):
            to[base_a : base_a + quarter, pl.ds(at, BLOCK)] = dot(ou_s[base : base + quarter], n2_s[:, pl.ds(at, BLOCK)]).astype(BF16)

        loop(width, BLOCK, weight)
        ready(first_att, j)

        def output(at):
            grad_s[base : base + quarter, pl.ds(at, BLOCK)] = dot_nt(wo_s[base : base + quarter], n2_s[pl.ds(at, BLOCK)]).astype(BF16)

        loop(rows, BLOCK, output)
        go_s = a_s.at[:, rows + 256 * j : rows + 256 * (j + 1)]

        def scale(at):
            here = pl.ds(at, BLOCK)
            grad_t = dot_nt(grad_s[base : base + quarter], roll_s[here])
            for head in range(heads):
                row = j * heads + head
                r = r_s[row : row + 1, here]
                g = grad_t[head * HEAD : (head + 1) * HEAD]
                at_head = slice(base + head * HEAD, base + (head + 1) * HEAD)
                in_s[row : row + 1, here] = column_sum(g * ot_s[at_head, here].astype(F32)) * r
                gt_s[at_head, here] = (g * r).astype(BF16)
            go_s[here, :quarter] = gt_s[base : base + quarter, here].T

        loop(rows, BLOCK, scale)

        def block(at):
            here = pl.ds(at, count)
            b = at // count
            dv = [None, None]
            for head in range(heads):
                tile = head // 2
                gh = jnp.where(lane_half(count, head % 2 == 1), go_s[here, 128 * tile : 128 * tile + 128], zero)
                part = dot(e_s[j * heads + head, b], gh)
                dv[tile] = part if dv[tile] is None else dv[tile] + part
            dv = jnp.concatenate(dv, axis=1)[:, :quarter].astype(BF16)
            g_s[here, (3 * j + 2) * BLOCK : (3 * j + 2) * BLOCK + quarter] = dv
            ot_s[base : base + quarter, here] = dv.T

        loop(rows, count, block)
        keep_gradient(j, 2)
        hook(f"v{j}")

    def scores_back(j):
        base = j * quarter

        def block(at):
            here = pl.ds(at, count)
            b = at // count
            dk = [None, None]
            for head in range(heads):
                tile = head // 2
                row = j * heads + head
                half = lane_half(count, head % 2 == 1)
                lanes = slice(128 * tile, 128 * tile + 128)
                vh = jnp.where(half, v_s[j, here, lanes], zero)
                qh = jnp.where(half, q_s[j, here, lanes], zero)
                last_row = min(128 * tile + 128, quarter)
                vh = vh[:, : last_row - 128 * tile]
                ds = a_s.at[:count, head * count : (head + 1) * count] if head < 2 else a_s.at[count:, :count]
                for off in range(0, count, BLOCK):
                    some = pl.ds(pl.multiple_of(at + off, BLOCK), BLOCK)
                    dp_t = dot(vh, gt_s[base + 128 * tile : base + last_row, some])
                    grad = (dp_t - in_s[row : row + 1, some]) * e_s[row, b, :, off : off + BLOCK].astype(F32)
                    ds[:, off : off + BLOCK] = grad.astype(BF16)
                part = dot(ds[...], qh)
                dk[tile] = part if dk[tile] is None else dk[tile] + part
                kth = kt_s[base + head * HEAD : base + head * HEAD + HEAD, here]
                dq_s[base + head * HEAD : base + head * HEAD + HEAD, here] = dot(kth, ds[...]).astype(BF16)
            dk = jnp.concatenate(dk, axis=1)[:, :quarter].astype(BF16)
            g_s[here, (3 * j + 1) * BLOCK : (3 * j + 1) * BLOCK + quarter] = dk
            ot_s[base : base + quarter, here] = dk.T
            g_s[here, 3 * j * BLOCK : 3 * j * BLOCK + quarter] = dq_s[base : base + quarter, here].T

        loop(rows, count, block)
        hook(f"b{j}")
        keep_gradient(j, 1)
        ot_s[base : base + quarter] = dq_s[base : base + quarter]
        keep_gradient(j, 0)
        hook(f"s{j}")

    values_back(1)
    values_back(0)
    scores_back(1)
    scores_back(0)

    def back_one(at):
        total = None
        for j in range(2):
            for c in range(3):
                d = g_s[pl.ds(at, BLOCK), (3 * j + c) * BLOCK : (3 * j + c) * BLOCK + quarter]
                term = dot(d, wq_s[j, c])
                total = term if total is None else total + term
        n2_s[pl.ds(at, BLOCK)] = total.astype(BF16)

    for at in range(0, count, BLOCK):
        dm_half(at).wait_send()
    loop(rows, BLOCK, back_one)
    for at in range(0, count, BLOCK):
        gn2_half(at).wait_send()

    def gn1_half(at):
        return half_copy(sb2.at[pl.ds(at, BLOCK)], rb2.at[pl.ds(at, BLOCK)], 12, at)

    def back_one_sib(at):
        sb2[pl.ds(at, BLOCK)] = dot(back_s[pl.ds(count + at, BLOCK)], n2_s[...]).astype(BF16)
        gn1_half(at).start()

    def back_one_mine(at):
        mid_s[pl.ds(at, BLOCK)] = dot(back_s[pl.ds(at, BLOCK)], n2_s[...])

    loop(count, BLOCK, back_one_sib)
    hook("gn1")
    loop(count, BLOCK, back_one_mine)
    mlp_copy.wait_send()

    def first_back(at):
        gn1_half(at).wait_recv()
        for off in range(0, BLOCK, 128):
            spot = pl.ds(pl.multiple_of(at + off, 128), 128)
            xhat, sigma = norm_stats(sin_s[spot])
            grad = mid_s[spot] + rb2[spot].astype(F32)
            sb1[spot] = (gm_s[spot] + norm_back(grad, ln1_gain, xhat, sigma)).astype(BF16)
            late[0:1] += column_sum(grad * xhat)
            late[1:2] += column_sum(grad)

    loop(count, BLOCK, first_back)
    put_in = local(sb1, ing_h)
    last_small.start()
    hook("tail")
    left = [first_small, last_small] + chunks
    while left:
        for item in left:
            item.advance()
        left = [item for item in left if not item.finished]

    for row, source, at in ((0, late, 0), (1, late, 1), (2, early, 0), (3, early, 1), (4, early, 2), (5, early, 3), (8, early, 4), (9, late, 2), (10, late, 3)):
        small_o[row : row + 1] = source[at : at + 1]

    passed = [copy for item in pieces for copy in item.sent]
    for copy in [unit_copy, head_copy, n1_copy, cot_copy] + [gn1_half(at) for at in range(0, count, BLOCK)] + passed:
        copy.wait_send()
    for chunk in chunks:
        for copy in chunk.sent:
            copy.wait_send()
        chunk.done.wait()
    for small in (first_small, last_small):
        for copy in small.sent:
            copy.wait_send()
    put_out.wait()
    put_in.wait()


def copies_of(full):
    most = 0
    for kind in ORDERS:
        first, after = KINDS[kind]
        most = max(most, 1 + full + 2 * sum((1 << len(bits)) - 1 for bits in after) + (0 if first is None else 3))
    return most


def call_layer(dp_size, tokens, cotangent, ids, table, vectors, wq, wo, w1, w2):
    count, width = tokens.shape
    rows = 2 * count
    quarter = wo.shape[0]
    units = w1.shape[1]
    heads = quarter // HEAD
    grad_rows = units + 4 * quarter
    parts = units // BLOCK
    bits = [b for b in range(20) if (1 << b) < dp_size]
    half_bits = bits[:3]
    shape = jax.ShapeDtypeStruct
    vm = pltpu.VMEM
    regions = 2 * (units // BLOCK) + 4
    steps = copies_of(len(bits) - len(half_bits))
    fetched = 4 + 2 * (units // BLOCK)
    scratch = (
        [vm((count, width), BF16), vm((rows, width), BF16)]
        + [vm((count, width), F32)] * 3
        + [vm((rows, width), BF16)] * 2
        + [vm((width, rows), BF16)]
        + [vm((2,) + wq.shape, BF16), vm((2 * quarter, width), BF16), vm((2, units // BLOCK, width, BLOCK), BF16), vm((2,) + w2.shape, BF16)]
        + [vm((2, rows, 256), BF16)] * 2
        + [vm((2 * quarter, rows), BF16)] * 5
        + [vm((8, rows), F32)] * 2
        + [vm((2 * heads, 2, count, count), BF16)]
        + [vm((rows, rows), BF16)] * 2
        + [vm((rows, width), BF16)]
        + [vm((rows, 2 * units), BF16)] * 2
        + [vm((count, width), BF16)] * 4
        + [vm((grad_rows, width), BF16)] * 3
        + [vm((7 * units // 8 + 4 * quarter, width), BF16), vm((units // 2, width), BF16)]
        + [vm((parts, width, BLOCK), BF16)] * 3
        + [vm((parts, 7 * width // 8, BLOCK), BF16), vm((parts, width // 2, BLOCK), BF16)]
        + [vm((grad_rows >> len(half_bits), width), BF16)] * (len(bits) - len(half_bits))
        + [vm((parts, width // 8, BLOCK), BF16)] * (len(bits) - len(half_bits))
        + [vm((units,), F32), vm((2, quarter), F32), vm((8, width), F32), vm((8, width), F32)]
        + [vm((6, 8, width), F32), vm((14 + 2 * (len(bits) - 3), 8, width), F32)]
        + [pltpu.SemaphoreType.DMA((8 + units // BLOCK + regions,))]
        + [pltpu.SemaphoreType.DMA((2, n)) for n in (3 * fetched + 2, 14, regions * steps, 2 * (10 + len(bits) - 3))]
    )
    anywhere = pl.BlockSpec(memory_space=pl.ANY)
    inside = pl.BlockSpec(memory_space=pltpu.VMEM)
    return pl.pallas_call(
        functools.partial(layer, dp_size, half_bits),
        out_shape=[shape((count, width), BF16)] * 2
        + [shape(w2.shape, BF16), shape(w1.shape, BF16), shape(wo.shape, BF16), shape(wq.shape, BF16), shape((16, width), F32)],
        in_specs=[anywhere] * 2 + [inside] * (2 + len(vectors)) + [anywhere] * 4,
        out_specs=[anywhere] * 6 + [inside],
        scratch_shapes=scratch,
        compiler_params=pltpu.CompilerParams(vmem_limit_bytes=VMEM_LIMIT, collective_id=0, has_side_effects=True),
        name="layer",
    )(tokens, cotangent, ids, table, *vectors, wq, wo, w1, w2)


def finish(out, ing, g2, g1, go, gq, small, out_o, ing_o, g2_o, g1_o, go_o, gq_o, a0, a1, a2, a3, a4, a5, units_o, heads_o):
    for src, dst in ((out, out_o), (ing, ing_o), (g2, g2_o), (g1, g1_o), (go, go_o), (gq, gq_o)):
        dst[...] = src[...].astype(dst.dtype)

    @pl.when(pl.program_id(0) == 0)
    def _():
        for i, ref in enumerate((a0, a1, a2, a3, a4, a5)):
            ref[...] = small[i]
        units_o[...] = small[8, : units_o.shape[0]]
        heads_o[...] = small[9:11, : heads_o.shape[1]]


def call_finish(arrays, small, units, quarter):
    steps = 8
    width = small.shape[1]
    shape = jax.ShapeDtypeStruct

    def rows_of(a):
        axis = a.ndim - 2
        block = a.shape[:axis] + (a.shape[axis] // steps,) + a.shape[axis + 1 :]
        return pl.BlockSpec(block, lambda i, axis=axis, rank=a.ndim: tuple(i if k == axis else 0 for k in range(rank)))

    def whole(extent):
        return pl.BlockSpec(extent, lambda i, rank=len(extent): (0,) * rank)

    extents = [(width,)] * 6 + [(units,), (2, quarter)]
    kinds = [BF16, BF16, F32, F32, F32, F32]
    return pl.pallas_call(
        finish,
        grid=(steps,),
        in_specs=[rows_of(a) for a in arrays] + [whole(small.shape)],
        out_specs=[rows_of(a) for a in arrays] + [whole(e) for e in extents],
        out_shape=[shape(a.shape, k) for a, k in zip(arrays, kinds)] + [shape(e, F32) for e in extents],
        compiler_params=pltpu.CompilerParams(vmem_limit_bytes=VMEM_LIMIT),
        name="finish",
    )(*arrays, small)


def per_device(
    tokens, segment_ids, ln1_gain, ln1_bias, qkv_weight, qv_bias, out_weight, out_bias,
    ln2_gain, ln2_bias, fc1_weight, fc1_bias, fc2_weight, fc2_bias, cotangent,
):
    width = tokens.shape[1]
    freq_count = width // 6
    frequency = 10000.0 ** (-jnp.arange(freq_count, dtype=F32) / freq_count)
    angles = jnp.arange(SIDE, dtype=F32)[:, None] * frequency[None, :]
    table = jnp.concatenate([jnp.sin(angles), jnp.cos(angles)], axis=1)
    vectors = (ln1_gain, ln1_bias, out_bias, ln2_gain, ln2_bias, fc2_bias, fc1_bias, qv_bias)
    *arrays, small = call_layer(
        lax.axis_size("dp"), tokens, cotangent, segment_ids, table, vectors, qkv_weight.transpose(0, 2, 1), out_weight, fc1_weight, fc2_weight
    )
    out, ing, g2, g1, go, gq, a0, a1, a2, a3, a4, a5, g_units, g_heads = call_finish(arrays, small, fc1_weight.shape[1], out_weight.shape[0])
    return (out, ing, a0, a1, gq.transpose(0, 2, 1), g_heads, go, a2, a3, a4, g1, g_units, g2, a5)


def solution(mesh):
    placed = (
        P(("dp", "tensor"), None),
        P("dp", None),
        P(),
        P(),
        P(None, None, "tensor"),
        P(None, "tensor"),
        P("tensor", None),
        P(),
        P(),
        P(),
        P(None, "tensor"),
        P("tensor"),
        P("tensor", None),
        P(),
        P(("dp", "tensor"), None),
    )
    return jax.shard_map(
        per_device,
        mesh=mesh,
        in_specs=placed,
        out_specs=(
            P(("dp", "tensor"), None),
            P(("dp", "tensor"), None),
            P(),
            P(),
            P(None, None, "tensor"),
            P(None, "tensor"),
            P("tensor", None),
            P(),
            P(),
            P(),
            P(None, "tensor"),
            P("tensor"),
            P("tensor", None),
            P(),
        ),
        check_vma=False,
    )
```

```python
import functools

import jax
import jax.numpy as jnp
from jax import lax
from jax.experimental import pallas as pl
from jax.experimental.pallas import tpu as pltpu
from jax.sharding import PartitionSpec as P

HEAD = 64
SIDE = 16
EPSILON = 1e-06
NEG_LARGE = -1e30
SCALE = HEAD ** (-0.5)
F32 = jnp.float32
BF16 = jnp.bfloat16
VMEM_LIMIT = 64 * 1024 * 1024 - 128 * 1024
MESH = pl.DeviceIdType.MESH
BLOCK = 256
KINDS = {
    "A": (None, ((0,), (1,), (2,))),
    "B": (None, ((1,), (0,), (2,))),
    "D": (None, ((0,), (1, 2))),
    "E": (None, ((0, 1, 2),)),
    "Y": (0, ((1,), (2,))),
    "Z": (1, ((0,), (2,))),
    "YD": (0, ((1, 2),)),
    "S": (None, (("p",), ("q",), (2,))),
    "SD": (None, (("p",), ("q", 2))),
    "SF": ("p", (("q",), (2,))),
    "SFD": ("p", (("q", 2),)),
}
ORDERS = ("SFD", "SD", "A", "SF", "SF", "D", "S", "SD", "SD", "D")
WEIGHT_PLAN = {"p0": (0,), "a2": (1,), "p1": (3, 4), "c2": (5,), "o": (6,), "r10.0": (7,), "r00.0": (8,), "r11.1": (9,)}
PLAN = {
    "f01": (0,),
    "r12.1": (1,),
    "f02": (3, 1),
    "g0": (2,),
    "lb": (0, 4),
    "ln2": (1,),
    "fin": (2,),
    "w1.0": (-1,),
    "w1.1": (0, 5),
    "w0.0": (2, 1, 3),
    "b1.0": (4, -1, 5),
    "b1.1": (1, 0, 3),
    "k1": (4, 2, 6),
    "b0.0": (5, 0),
    "b0.1": (3, 9, 4),
    "k0": (6,),
    "s0": (2,),
    "d.0": (8,),
    "d.1": (5, 9, 6),
    "e.0": (3, 2),
    "e.1": (4, 7, 8),
    "tail": (9, 5, 6, 3, -2, 2, 4, 7, 9, 8, 6, 3, -2, 4, 7, 9, 8, 6, 7, 8, 6, 7),
}


def dot(a, b):
    return jnp.dot(a, b, preferred_element_type=F32)


def dot_nt(a, b):
    return lax.dot_general(a, b, (((1,), (1,)), ((), ())), preferred_element_type=F32)


def dot_tn(a, b):
    return lax.dot_general(a, b, (((0,), (0,)), ((), ())), preferred_element_type=F32)


def lane_half(rows, upper):
    lanes = lax.broadcasted_iota(jnp.int32, (rows, 128), 1)
    return lanes >= HEAD if upper else lanes < HEAD


def head_lanes(ref, head, filler):
    tile = ref[:, 128 * (head // 2) : 128 * (head // 2) + 128]
    return jnp.where(lane_half(tile.shape[0], head % 2 == 1), tile, filler)


def gelu_pair(h):
    cdf = 0.5 + 0.5 * lax.erf(h * 0.7071067811865476)
    return h * cdf, cdf + h * jnp.exp(-0.5 * h * h) * 0.3989422804014327


def norm_stats(v):
    centred = v - jnp.mean(v, axis=-1, keepdims=True)
    sigma = lax.rsqrt(jnp.mean(centred * centred, axis=-1, keepdims=True) + EPSILON)
    return centred * sigma, sigma


def norm_back(grad, gain, xhat, sigma):
    g = grad * gain
    return sigma * (g - jnp.mean(g, axis=-1, keepdims=True) - xhat * jnp.mean(g * xhat, axis=-1, keepdims=True))


def column_sum(v):
    return jnp.sum(v, axis=0, keepdims=True)


def aligned(v, unit):
    return v if isinstance(v, int) else pl.multiple_of(v, unit)


def loop(count, step, body, service=None, every=1):
    def run(i, carry):
        body(aligned(i * step, step))
        if service is not None:
            for k in range(count // step // every):
                if service(k, True):
                    pl.when(i == every * (k + 1) - 1)(functools.partial(service, k, False))
        return carry

    lax.fori_loop(0, count // step, run, 0)


def layer(
    dp_size, half_bits,
    tok_h, cot_h, ids, table, gain1, bias1, bias_o, gain2, bias2, bias_f, bias_u, bias_qv, wq_h, wo_h, w1_h, w2_h,
    out_h, ing_h, g2_h, g1_h, go_h, gq_h, small_o,
    tok_s, cot_s, sin_s, mid_s, gm_s, n1_s, n2_s, n2t_s, wq_s, wo_s, w1_s, w2_s,
    q_s, v_s, kt_s, ot_s, ou_s, gt_s, gr_s, r_s, in_s, e_s, roll_s, back_s, nr_s, a_s, g_s, sb1, sb2, rb1, rb2,
    own, oth, xr, land, land_both, own1, oth1, xr1, land1, land1_both, *rest,
):
    rest = list(rest)
    full_bits = [b for b in range(20) if (1 << b) < dp_size and b not in half_bits]
    rx = [rest.pop(0) for _ in full_bits]
    rx1 = [rest.pop(0) for _ in full_bits]
    uoth, voth, early, late, near, far, lsem, wsem, csem, gsem, ssem = rest

    count, width = tok_s.shape
    rows = 2 * count
    quarter = wo_h.shape[0]
    units = w1_h.shape[1]
    heads = quarter // HEAD
    place = lax.axis_index("tensor")
    dp = lax.axis_index("dp")
    chip = place // 2
    core = place % 2
    sib = {"tensor": chip * 2 + 1 - core}
    across = {"tensor": (1 - chip) * 2 + core}
    facing = {"tensor": (1 - chip) * 2 + 1 - core}
    all_bits = list(half_bits) + full_bits
    sides = {b: (dp // (1 << b)) % 2 for b in all_bits}

    ways = {b: (1 - 2 * sides[b]) * (1 << b) for b in all_bits}
    sides["p"] = sides[0] + (sides[1] - sides[0]) * core
    sides["q"] = sides[1] + (sides[0] - sides[1]) * core
    ways["p"] = ways[0] + (ways[1] - ways[0]) * core
    ways["q"] = ways[1] + (ways[0] - ways[1]) * core

    def mate(bits):
        return {"dp": dp + sum(ways[b] for b in bits)}

    def described(src, dst, sems, index, device):
        return pltpu.make_async_remote_copy(
            src_ref=src, dst_ref=dst, send_sem=sems.at[0, index], recv_sem=sems.at[1, index], device_id=device, device_id_type=MESH
        )

    mates = {b: mate((b,)) for b in all_bits}
    groups = {(b,) for b in full_bits}
    for mask in range(1, 1 << len(half_bits)):
        groups.add(tuple(b for k, b in enumerate(half_bits) if mask >> k & 1))

    barrier = pltpu.get_barrier_semaphore()
    partners = [sib, across, facing] + [mate(bits) for bits in sorted(groups)]
    for partner in partners:
        pl.semaphore_signal(barrier, inc=1, device_id=partner, device_id_type=MESH)

    sq_s, sk_s, k_s = a_s.at[:, 0:128], a_s.at[:, 128:256], a_s.at[:, 256:512]
    local_used = [0]

    def local(src, dst):
        copy = pltpu.make_async_copy(src, dst, lsem.at[local_used[0]])
        local_used[0] += 1
        copy.start()
        return copy

    def remote(src, dst, sems, index, device):
        copy = pltpu.make_async_remote_copy(
            src_ref=src, dst_ref=dst, send_sem=sems.at[0, index], recv_sem=sems.at[1, index], device_id=device, device_id_type=MESH
        )
        copy.start()
        return copy

    def half_copy(src, dst, first, at):
        return pltpu.make_async_remote_copy(
            src_ref=src,
            dst_ref=dst,
            send_sem=csem.at[0, first + at // BLOCK],
            recv_sem=csem.at[1, first + at // BLOCK],
            device_id=sib,
            device_id_type=MESH,
        )

    get_tok = local(tok_h, tok_s)
    get_cot = local(cot_h, cot_s.at[pl.ds(0, count)])
    get_wq = local(wq_h, wq_s.at[0])
    get_wo = local(wo_h, wo_s.at[pl.ds(0, quarter)])
    get_w1 = [local(w1_h.at[:, pl.ds(i * BLOCK, BLOCK)], w1_s.at[0, i]) for i in range(units // BLOCK)]
    get_w2 = local(w2_h, w2_s.at[0])

    ln1_gain, ln1_bias, out_bias, ln2_gain, ln2_bias, fc2_bias = (
        ref[...].reshape(1, width) for ref in (gain1, bias1, bias_o, gain2, bias2, bias_f)
    )
    get_tok.wait()

    def first_norm(at):
        plane = core * (count // (SIDE * SIDE)) + at // (SIDE * SIDE)
        line = (at // SIDE) % SIDE
        shape = (SIDE, width // 3)
        for k in range(4):
            spot = jnp.concatenate(
                [jnp.broadcast_to(table[pl.ds(plane, 1)], shape), jnp.broadcast_to(table[pl.ds(line + k, 1)], shape), table[...]], axis=1
            )
            span = pl.ds(aligned(at + k * SIDE, SIDE), SIDE)
            stream = tok_s[span].astype(F32) + spot
            sin_s[span] = stream
            xhat, _ = norm_stats(stream)
            n1_s[span] = (xhat * ln1_gain + ln1_bias).astype(BF16)

    loop(count, 4 * SIDE, first_norm)
    doc = ids[pl.ds(chip, 1), :]
    starts = [jnp.zeros((1, 1), F32)]
    starts += [jnp.sum(jnp.where(doc < v, 1.0, 0.0), axis=1, keepdims=True) for v in range(1, 4)]
    starts.append(jnp.full((1, 1), rows, F32))
    turn = jnp.zeros((1, 1), F32)
    for v in range(4):
        turn += jnp.where(starts[v + 1] - starts[v] == count, starts[v], 0.0)
    turn_here = turn - (core * count).astype(F32)

    def wrapped(v):
        v = jnp.where(v >= rows, v - rows, v)
        return jnp.where(v < 0, v + rows, v)

    def rotations(at):
        down = (lax.broadcasted_iota(jnp.int32, (64, rows), 0) + at).astype(F32)
        along = lax.broadcasted_iota(jnp.int32, (64, rows), 1).astype(F32)
        roll_s[pl.ds(at, 64)] = jnp.where(wrapped(down + turn_here) == along, 1.0, 0.0).astype(BF16)
        back_s[pl.ds(at, 64)] = jnp.where(wrapped(down - turn_here) == along, 1.0, 0.0).astype(BF16)
        where = wrapped((lax.broadcasted_iota(jnp.int32, (64, 128), 0) + at).astype(F32) + turn)
        mine = sum(jnp.where(where >= starts[v], 1.0, 0.0) for v in range(1, 4))
        slot = (lax.broadcasted_iota(jnp.int32, (64, 128), 1) % HEAD).astype(F32)
        sq_s[pl.ds(at, 64)] = jnp.where((slot < 4) & (slot != mine), 1.0, 0.0).astype(BF16)
        sk_s[pl.ds(at, 64)] = jnp.where(slot == mine, NEG_LARGE, 0.0).astype(BF16)


    pl.semaphore_wait(barrier, len(partners))
    unit_copy = remote(bias_u, uoth, wsem, 3 * (4 + 2 * (units // BLOCK)), across)
    head_copy = remote(bias_qv, voth, wsem, 3 * (4 + 2 * (units // BLOCK)) + 1, across)
    get_wq.wait()
    get_wo.wait()
    for copy in get_w1:
        copy.wait()
    get_w2.wait()

    part = (sides[0] + sides[1]) % 2

    class Piece:
        def __init__(self, index, refs, at, extent):
            size = extent // 4

            def some(k, first, size):
                return refs[k].at[pl.ds(aligned(at[k] + part * (extent // 2) + first, 16), size)]

            self.copies = [described(some(0, 0, 2 * size), some(1, 0, 2 * size), wsem, 3 * index, across)]
            for k in range(2):
                block = some(1, k * size, size)
                self.copies.append(described(block, block, wsem, 3 * index + 1 + k, mates[k]))
            self.stage = 0

        def advance(self):
            if self.stage == 0:
                self.copies[0].wait_recv()
                self.copies[1].start()
                self.copies[2].start()
            else:
                self.copies[1].wait_recv()
                self.copies[2].wait_recv()
            self.stage += 1

    pieces = [Piece(c, (wq_s.at[0, c], wq_s.at[1, c]), (0, 0), quarter) for c in range(3)]
    pieces.append(Piece(3, (wo_s, wo_s), (0, quarter), quarter))
    for i in range(units // BLOCK):
        pieces.append(Piece(4 + 2 * i, (w1_s.at[0, i], w1_s.at[1, i]), (0, 0), width))
        pieces.append(Piece(5 + 2 * i, (w2_s.at[0], w2_s.at[1]), (i * BLOCK, i * BLOCK), BLOCK))
    for item in pieces:
        item.copies[0].start()

    inside_loop = []

    def service(name, act):
        def at_point(k, ask):
            full = f"{name}{k}"
            if ask:
                return full in PLAN or full in WEIGHT_PLAN
            inside_loop.append(full)
            act(full)
            inside_loop.pop()

        return at_point

    def pass_on(name):
        for i in WEIGHT_PLAN.get(name, ()):
            if pieces[i].stage < 1:
                pieces[i].advance()

    def have_weight(*which):
        for i in which:
            while pieces[i].stage < 2:
                pieces[i].advance()

    n1_copy = remote(n1_s.at[pl.ds(0, count)], n1_s.at[pl.ds(count, count)], csem, 0, sib)
    get_cot.wait()
    cot_copy = remote(cot_s.at[pl.ds(0, count)], cot_s.at[pl.ds(count, count)], csem, 1, sib)

    def rotate(at):
        nr_s[pl.ds(at, BLOCK)] = dot(roll_s[pl.ds(at, BLOCK)], n1_s[...]).astype(BF16)

    def project(j, at):
        n = nr_s[pl.ds(at, BLOCK)]
        biases = bias_qv if j == 0 else voth
        q = (dot_nt(n, wq_s[j, 0]) + biases[0:1]).astype(BF16) * SCALE
        k = dot_nt(n, wq_s[j, 1]).astype(BF16)
        v = (dot_nt(n, wq_s[j, 2]) + biases[1:2]).astype(BF16)
        q_s[j, pl.ds(at, BLOCK), :quarter] = q
        k_s[pl.ds(at, BLOCK), :quarter] = k
        v_s[j, pl.ds(at, BLOCK), :quarter] = v
        kt_s[j * quarter : (j + 1) * quarter, pl.ds(at, BLOCK)] = k.T * SCALE

    blocks = [(b, at) for b in range(2) for at in range(0, count, BLOCK)]

    def attend(j):
        for head in range(heads):
            at = 512 + 256 * head
            a_s[:, at : at + 128] = head_lanes(q_s.at[j], head, sq_s[...])
            a_s[:, at + 128 : at + 256] = head_lanes(k_s, head, sk_s[...])
        for at in range(0, rows, BLOCK):
            ou_s[:quarter, at : at + BLOCK] = v_s[j, at : at + BLOCK, :quarter].T

        def tile(here):
            b = here // count
            at = aligned(here % count, BLOCK)
            keys = pl.ds(aligned(b * count, count), count)
            for head in range(heads):
                column = 512 + 256 * head
                s = dot_nt(a_s[keys, column + 128 : column + 256], a_s[pl.ds(here, BLOCK), column : column + 128])
                m = jnp.max(s, axis=0, keepdims=True)
                e = jnp.exp(s - m)
                r = 1.0 / column_sum(e)
                low = e.astype(BF16)
                span = slice(head * HEAD, head * HEAD + HEAD)
                to = slice(j * quarter + head * HEAD, j * quarter + head * HEAD + HEAD)
                e_s[j * heads + head, b, :, pl.ds(at, BLOCK)] = low
                ot_s[to, pl.ds(here, BLOCK)] = (dot(ou_s[span, keys], low) * r).astype(BF16)
                r_s[j * heads + head : j * heads + head + 1, pl.ds(here, BLOCK)] = r

        return tile

    loop(rows, 64, rotations)
    n1_copy.wait_recv()
    loop(rows, BLOCK, rotate)
    loop(rows, BLOCK, lambda at: project(0, at))
    pass_on("p0")
    loop(rows, BLOCK, attend(0), service("a", pass_on))
    head_copy.wait_recv()
    have_weight(0, 1, 2)
    loop(rows, BLOCK, lambda at: project(1, at))
    pass_on("p1")
    loop(rows, BLOCK, attend(1), service("c", pass_on))

    have_weight(3)

    def unrotate(at):
        ou_s[:, pl.ds(at, BLOCK)] = dot(ot_s[...], roll_s[:, pl.ds(at, BLOCK)]).astype(BF16)

    loop(rows, BLOCK, unrotate)
    pass_on("u")

    def out_part(at):
        return dot_tn(ou_s[:, pl.ds(at, BLOCK)], wo_s[...])

    def att_half(at):
        return half_copy(sb1.at[pl.ds(at, BLOCK)], rb1.at[pl.ds(at, BLOCK)], 2, at)

    def n2_half(at):
        return half_copy(n2_s.at[pl.ds(at, BLOCK)], n2_s.at[pl.ds(aligned(count + at, BLOCK), BLOCK)], 4, at)

    def out_sib(at):
        sb1[pl.ds(at, BLOCK)] = out_part(count + at).astype(BF16)
        att_half(at).start()

    loop(count, BLOCK, out_sib)

    def out_mine(at):
        mid_s[pl.ds(at, BLOCK)] = sin_s[pl.ds(at, BLOCK)] + out_part(at) + out_bias

    loop(count, BLOCK, out_mine)
    pass_on("o")

    def second_norm(at):
        att_half(at).wait_recv()
        for off in range(0, BLOCK, 128):
            spot = pl.ds(aligned(at + off, 128), 128)
            mid = mid_s[spot] + rb1[spot].astype(F32)
            mid_s[spot] = mid
            xhat, _ = norm_stats(mid)
            n2_s[spot] = (xhat * ln2_gain + ln2_bias).astype(BF16)
        n2_half(at).start()

    loop(count, BLOCK, second_norm)
    pass_on("n")

    base_a = units
    parts = units // BLOCK
    steps = copies_of(len(full_bits))

    class Region:
        def __init__(self, index, row, size, cols, slot, kind, refs, to):
            own_r, oth_r, xr_r, land_r, both_r, rx_r = refs
            self.place, self.slot, self.to, self.xr = (row, size, 0, cols), slot, to, xr_r
            first, after = KINDS[kind]
            self.first = first is not None
            self.stages, self.stage, self.finished, self.sent = [], -1, False, []
            now, parts, used, trail = self.place, 8, 0, []
            sems = iter(range(index * steps, (index + 1) * steps))

            def copy(src, src_at, dst, dst_at, device):
                return described(src.at[self.window(src_at)], dst.at[self.window(dst_at)], gsem, next(sems), device)

            def piece(bits, mask):
                where = now
                for k, b in enumerate(bits):
                    where = self.cut(where, 1 - sides[b] if mask >> k & 1 else sides[b])
                return where

            sums = 1 + len(after) + len(full_bits)
            if self.first:
                keep, give, there = piece((first,), 0), piece((first,), 1), (row // 2, size // 2, 0, cols)
                place = self.landing(0, 4)
                copies = [copy(own_r, give, land_r, place, mate((first,))), copy(oth_r, give, both_r, there, mate((first,)))]
                adds = [(own_r, own_r, keep, [(land_r, place)]), (oth_r, oth_r, keep, [(both_r, there)])]
                self.stages.append((copies, adds, False))
                trail.append(((first,), keep))
                now, parts, used = keep, 4, 4
            self.stages.append(([copy(oth_r, now, xr_r, now, across)], [(own_r, own_r, now, [(xr_r, now)])], False))
            for bits in after:
                parts >>= len(bits)
                keep, copies, terms = piece(bits, 0), [], []
                for mask in range(1, 1 << len(bits)):
                    place = self.landing(used, parts)
                    used += parts
                    terms.append((land_r, place))
                    copies.append(copy(own_r, piece(bits, mask), land_r, place, mate([b for k, b in enumerate(bits) if mask >> k & 1])))
                self.stages.append((copies, [(own_r, own_r, keep, terms)], False))
                trail.append((bits, keep))
                now = keep
            for i, b in enumerate(full_bits):
                place = self.small_place()
                self.stages.append(([copy(own_r, now, rx_r[i], place, mates[b])], [(own_r, own_r, now, [(rx_r[i], place)])], True))
            copies, adds, full = self.stages[-1]
            self.stages[-1] = (copies, [(xr_r,) + adds[0][1:]], full)
            for bits, keep in reversed(trail):
                copies = []
                for mask in range(1, 1 << len(bits)):
                    copies.append(copy(xr_r, keep, xr_r, keep, mate([b for k, b in enumerate(bits) if mask >> k & 1])))
                self.stages.append((copies, [], False))

        def window(self, where):
            row, size, col, cols = where
            return pl.ds(row, size), pl.ds(col, cols)

        def cut(self, where, side):
            row, size, col, cols = where
            if (size // 2) % 16 == 0:
                return aligned(row + side * (size // 2), 16), size // 2, col, cols
            return row, size, aligned(col + side * (cols // 2), 128), cols // 2

        def landing(self, at, parts_here):
            row, rows_one, cols_one = self.slot
            full = self.place[3]
            if cols_one == full:
                return row + at * rows_one, parts_here * rows_one, 0, full
            if parts_here == 1:
                return row + at // 2 * rows_one, rows_one, at % 2 * cols_one, cols_one
            return row + at // 2 * rows_one, parts_here // 2 * rows_one, 0, full

        def small_place(self):
            row, rows_one, cols_one = self.slot
            if cols_one == self.place[3]:
                return row // 7, rows_one, 0, cols_one
            k = (self.place[0] - base_a) // quarter
            return units // 8 + k // 2 * rows_one, rows_one, k % 2 * cols_one, cols_one

        def begin(self, copies):
            for copy in copies:
                copy.start()
            self.sent += copies

        def ready(self, j):
            if self.first:
                self.stage = 0
                self.begin([self.stages[0][0][j]])
            elif j == 1:
                self.stage = 0
                self.begin(self.stages[0][0])

        def add(self, into, base, where, terms):
            row, size, col, cols = where
            step = 64 if size % 64 == 0 else 48 if size % 48 == 0 else 32

            def body(off):
                to = (pl.ds(aligned(row + off, 16), step), pl.ds(col, cols))
                total = base[to].astype(F32)
                for ref, (r, _, c, _) in terms:
                    total += ref[pl.ds(aligned(r + off, 16), step), pl.ds(c, cols)].astype(F32)
                into[to] = total.astype(BF16)

            if inside_loop:
                for off in range(0, size, step):
                    body(off)
            else:
                loop(size, step, body)

        def advance(self):
            if self.finished or self.stage < 0:
                return
            copies, adds, full = self.stages[self.stage]
            for copy in copies:
                copy.wait_recv()
            if full:
                for copy in copies:
                    copy.wait_send()
                self.sent = [c for c in self.sent if all(c is not d for d in copies)]
            for item in adds:
                self.add(*item)
            self.stage += 1
            if self.stage < len(self.stages):
                self.begin(self.stages[self.stage][0])
                return
            self.finished = True
            to_write.append(self)

    chunks = []
    refs = (own, oth, xr, land, land_both, rx)
    for i in range(parts):
        slot = (i * 7 * (BLOCK // 8), BLOCK // 8, width)
        to = g2_h.at[pl.ds(i * BLOCK, BLOCK)]
        chunks.append(Region(2 * i, i * BLOCK, BLOCK, width, slot, ORDERS[2 * i], refs, to))
        refs_one = tuple(ref.at[i] for ref in (own1, oth1, xr1, land1, land1_both)) + ([ref.at[i] for ref in rx1],)
        to = g1_h.at[:, pl.ds(i * BLOCK, BLOCK)]
        chunks.append(Region(2 * i + 1, 0, width, BLOCK, (0, width // 8, BLOCK), ORDERS[2 * i + 1], refs_one, to))
    for i in range(4):
        slot = (7 * units // 8 + i * quarter, quarter // 4, width // 2)
        to = go_h if i == 0 else gq_h.at[i - 1]
        chunks.append(Region(2 * parts + i, base_a + i * quarter, quarter, width, slot, ORDERS[2 * parts + i], refs, to))
    first_att = 2 * parts

    class Small:
        def __init__(self, tile, index, everywhere, paired):
            self.tile, self.everywhere, self.paired = tile, everywhere, paired
            self.near = [near.at[3 * index + k] for k in range(3)]
            self.far = [far.at[(7 + len(full_bits)) * index + k] for k in range(7 + len(full_bits))]
            devices = [sib, across, facing]
            devices += [mate([b for k, b in enumerate(half_bits) if mask >> k & 1]) for mask in range(1, 8)]
            devices += [mates[b] for b in full_bits]
            base = index * len(devices)
            copies = [described(tile, dst, ssem, base + k, d) for k, (dst, d) in enumerate(zip(self.near + self.far, devices))]
            self.stages = [copies[:3], copies[3:10]] + [[copy] for copy in copies[10:]]
            self.stage, self.finished = -1, False

        def start(self):
            self.stage = 0
            for copy in self.stages[0]:
                copy.start()

        def advance(self):
            if self.finished or self.stage < 0:
                return
            for copy in self.stages[self.stage]:
                copy.wait()
            tile = self.tile
            if self.stage == 0:
                beside, over, facing_ = self.near
                n, p = self.everywhere, self.paired
                tile[0:n] = (tile[0:n] + beside[0:n]) + (over[0:n] + facing_[0:n])
                tile[n : n + p] = tile[n : n + p] + over[n + p : n + 2 * p]
            elif self.stage == 1:
                got = [tile] + self.far[:7]
                pairs = [got[2 * k][...] + got[2 * k + 1][...] for k in range(4)]
                tile[...] = (pairs[0] + pairs[1]) + (pairs[2] + pairs[3])
            else:
                tile[...] = tile[...] + self.far[5 + self.stage][...]
            self.stage += 1
            if self.stage == len(self.stages):
                self.finished = True
                return
            for copy in self.stages[self.stage]:
                copy.start()

    first_small = Small(early, 0, 4, 1)
    last_small = Small(late, 1, 2, 2)

    def ready(i, j):
        chunks[i].ready(j)

    to_write = []

    def write_finished():
        while to_write:
            region = to_write.pop()
            region.done = local(region.xr.at[region.window(region.place)], region.to)

    def hook(name):
        pass_on(name)
        for i in PLAN.get(name, ()):
            (chunks + [last_small, first_small])[i].advance()
            if not inside_loop:
                write_finished()

    def chunk_rows(j, i, at):
        span = pl.ds(at, BLOCK)
        cols = slice(j * units + i * BLOCK, j * units + (i + 1) * BLOCK)
        mine = slice(i * BLOCK, (i + 1) * BLOCK)
        bias = (bias_u if j == 0 else uoth)[mine].reshape(1, BLOCK)
        h = dot(n2_s[span], w1_s[j, i]) + bias
        a, slope = gelu_pair(h)
        a_s[span, cols] = a.astype(BF16)
        g = (dot_nt(cot_s[span], w2_s[j, mine]) * slope).astype(BF16)
        g_s[span, cols] = g

    def chunk_grads(j, i):
        cols = slice(j * units + i * BLOCK, j * units + (i + 1) * BLOCK)
        mine = slice(i * BLOCK, (i + 1) * BLOCK)
        to = oth if j == 1 else own

        def second(at):
            to[pl.ds(i * BLOCK + at, 128)] = dot_tn(a_s[:, pl.ds(cols.start + at, 128)], cot_s[...]).astype(BF16)

        loop(BLOCK, 128, second)
        ready(2 * i, j)
        g = g_s[:, cols]

        def first(at):
            (oth1 if j == 1 else own1)[i, pl.ds(at, BLOCK)] = dot(n2t_s[pl.ds(at, BLOCK)], g_s[:, cols]).astype(BF16)

        loop(width, BLOCK, first)
        ready(2 * i + 1, j)
        early[4 + j : 5 + j, mine] = column_sum(g.astype(F32))
        hook(f"f{j}{i}")

    def feed(j, i, first=False):
        if first:
            loop(count, BLOCK, lambda at: chunk_rows(j, i, at))
            hook(f"r{j}{i}.0")
            cot_copy.wait_recv()

            def received(at):
                n2_half(at).wait_recv()
                chunk_rows(j, i, count + at)

            loop(count, BLOCK, received)
            hook(f"r{j}{i}.1")

            def turned(at):
                n2t_s[:, pl.ds(at, BLOCK)] = n2_s[pl.ds(at, BLOCK)].T

            loop(rows, BLOCK, turned)
        else:
            loop(rows, BLOCK, lambda at: chunk_rows(j, i, at), service(f"r{j}{i}.", hook), 2)
        chunk_grads(j, i)

    early[...] = jnp.zeros_like(early)
    late[...] = jnp.zeros_like(late)
    unit_copy.wait_recv()
    for i in range(parts):
        have_weight(4 + 2 * i, 5 + 2 * i)
        feed(1, i, first=i == 0)
        feed(0, i)

    def back_two(at):
        span = pl.ds(at, BLOCK)
        total = None
        for j in range(2):
            for i in range(parts):
                at_col = j * units + i * BLOCK
                term = dot_nt(g_s[span, at_col : at_col + BLOCK], w1_s[j, i])
                total = term if total is None else total + term
        return total

    def mlp_part(at):
        span = pl.ds(at, BLOCK)
        return dot(a_s[span, :units], w2_s[0]) + dot(a_s[span, units:], w2_s[1])

    def gn2_half(at):
        return half_copy(sb2.at[pl.ds(at, BLOCK)], rb2.at[pl.ds(at, BLOCK)], 6, at)

    def dm_half(at):
        return half_copy(n2_s.at[pl.ds(at, BLOCK)], n2_s.at[pl.ds(aligned(count + at, BLOCK), BLOCK)], 10, at)

    def back_two_sib(at):
        sb2[pl.ds(at, BLOCK)] = back_two(count + at).astype(BF16)
        gn2_half(at).start()

    def back_two_mine(at):
        gm_s[pl.ds(at, BLOCK)] = back_two(at)

    def mlp_sib(at):
        sb1[pl.ds(at, BLOCK)] = mlp_part(count + at).astype(BF16)

    loop(count, BLOCK, back_two_sib)
    hook("g0")
    loop(count, BLOCK, back_two_mine)
    hook("gn2")

    def second_back(at):
        gn2_half(at).wait_recv()
        n2_half(at).wait_send()
        for off in range(0, BLOCK, 128):
            spot = pl.ds(aligned(at + off, 128), 128)
            xhat, sigma = norm_stats(mid_s[spot])
            grad = gm_s[spot] + rb2[spot].astype(F32)
            cot = cot_s[spot].astype(F32)
            back = cot + norm_back(grad, ln2_gain, xhat, sigma)
            gm_s[spot] = back
            n2_s[spot] = back.astype(BF16)
            early[0:1] += column_sum(back)
            early[1:2] += column_sum(grad * xhat)
            early[2:3] += column_sum(grad)
            early[3:4] += column_sum(cot)
        dm_half(at).start()

    loop(count, BLOCK, second_back)
    hook("lb")
    for at in range(0, count, BLOCK):
        att_half(at).wait_send()
    loop(count, BLOCK, mlp_sib)
    mlp_copy = remote(sb1, rb1, csem, 8, sib)
    first_small.start()
    hook("ln2")

    def finish_out(at):
        span = pl.ds(at, BLOCK)
        mid_s[span] = mid_s[span] + mlp_part(at) + fc2_bias

    loop(count, BLOCK, finish_out)
    hook("fo")
    mlp_copy.wait_recv()

    def write_out(at):
        spot = pl.ds(at, 128)
        tok_s[spot] = (mid_s[spot] + rb1[spot].astype(F32)).astype(BF16)

    loop(count, 128, write_out)
    put_out = local(tok_s, out_h)
    hook("fin")
    for at in range(0, count, BLOCK):
        dm_half(at).wait_recv()

    start = base_a + quarter
    zero = jnp.zeros((count, 128), BF16)
    grad_s = dq_s = gr_s

    def keep_gradient(j, c):
        to = oth if j == 1 else own
        low = start + c * quarter
        dt = ot_s.at[j * quarter : (j + 1) * quarter]

        def columns(at):
            to[low : low + quarter, pl.ds(at, BLOCK)] = dot(dt[...], nr_s[:, pl.ds(at, BLOCK)]).astype(BF16)

        loop(width, BLOCK, columns)
        ready(first_att + 1 + c, j)
        if c != 1:
            d = g_s[:, (3 * j + c) * BLOCK : (3 * j + c) * BLOCK + quarter]
            late[2 + c // 2 + 2 * j : 3 + c // 2 + 2 * j, :quarter] = column_sum(d.astype(F32))

    def values_back(j):
        base = j * quarter
        to = oth if j == 1 else own

        def weight(at):
            to[base_a : base_a + quarter, pl.ds(at, BLOCK)] = dot(ou_s[base : base + quarter], n2_s[:, pl.ds(at, BLOCK)]).astype(BF16)

        loop(width, BLOCK, weight)
        ready(first_att, j)

        def output(at):
            grad_s[base : base + quarter, pl.ds(at, BLOCK)] = dot_nt(wo_s[base : base + quarter], n2_s[pl.ds(at, BLOCK)]).astype(BF16)

        loop(rows, BLOCK, output)
        hook(f"w{j}.0")
        go_s = a_s.at[:, rows + 256 * j : rows + 256 * (j + 1)]

        def scale(at):
            here = pl.ds(at, BLOCK)
            grad_t = dot_nt(grad_s[base : base + quarter], roll_s[here])
            for head in range(heads):
                row = j * heads + head
                r = r_s[row : row + 1, here]
                g = grad_t[head * HEAD : (head + 1) * HEAD]
                at_head = slice(base + head * HEAD, base + (head + 1) * HEAD)
                in_s[row : row + 1, here] = column_sum(g * ot_s[at_head, here].astype(F32)) * r
                gt_s[at_head, here] = (g * r).astype(BF16)
            go_s[here, :quarter] = gt_s[base : base + quarter, here].T

        loop(rows, BLOCK, scale)

        def block(at):
            here = pl.ds(at, count)
            b = at // count
            dv = [None, None]
            for head in range(heads):
                tile = head // 2
                gh = jnp.where(lane_half(count, head % 2 == 1), go_s[here, 128 * tile : 128 * tile + 128], zero)
                part = dot(e_s[j * heads + head, b], gh)
                dv[tile] = part if dv[tile] is None else dv[tile] + part
            dv = jnp.concatenate(dv, axis=1)[:, :quarter].astype(BF16)
            g_s[here, (3 * j + 2) * BLOCK : (3 * j + 2) * BLOCK + quarter] = dv
            ot_s[base : base + quarter, here] = dv.T

        loop(rows, count, block)
        hook(f"w{j}.1")
        keep_gradient(j, 2)
        hook(f"v{j}")

    def scores_back(j):
        base = j * quarter

        def block(at):
            here = pl.ds(at, count)
            b = at // count
            dk = [None, None]
            for head in range(heads):
                tile = head // 2
                row = j * heads + head
                half = lane_half(count, head % 2 == 1)
                lanes = slice(128 * tile, 128 * tile + 128)
                vh = jnp.where(half, v_s[j, here, lanes], zero)
                qh = jnp.where(half, q_s[j, here, lanes], zero)
                last_row = min(128 * tile + 128, quarter)
                vh = vh[:, : last_row - 128 * tile]
                ds = a_s.at[:count, head * count : (head + 1) * count] if head < 2 else a_s.at[count:, :count]
                for off in range(0, count, BLOCK):
                    some = pl.ds(aligned(at + off, BLOCK), BLOCK)
                    dp_t = dot(vh, gt_s[base + 128 * tile : base + last_row, some])
                    grad = (dp_t - in_s[row : row + 1, some]) * e_s[row, b, :, off : off + BLOCK].astype(F32)
                    ds[:, off : off + BLOCK] = grad.astype(BF16)
                part = dot(ds[...], qh)
                dk[tile] = part if dk[tile] is None else dk[tile] + part
                kth = kt_s[base + head * HEAD : base + head * HEAD + HEAD, here]
                dq_s[base + head * HEAD : base + head * HEAD + HEAD, here] = dot(kth, ds[...]).astype(BF16)
            dk = jnp.concatenate(dk, axis=1)[:, :quarter].astype(BF16)
            g_s[here, (3 * j + 1) * BLOCK : (3 * j + 1) * BLOCK + quarter] = dk
            ot_s[base : base + quarter, here] = dk.T
            g_s[here, 3 * j * BLOCK : 3 * j * BLOCK + quarter] = dq_s[base : base + quarter, here].T

        loop(rows, count, block, service(f"b{j}.", hook))
        keep_gradient(j, 1)
        hook(f"k{j}")
        ot_s[base : base + quarter] = dq_s[base : base + quarter]
        keep_gradient(j, 0)
        hook(f"s{j}")

    values_back(1)
    values_back(0)
    scores_back(1)
    scores_back(0)

    def back_one(at):
        total = None
        for j in range(2):
            for c in range(3):
                d = g_s[pl.ds(at, BLOCK), (3 * j + c) * BLOCK : (3 * j + c) * BLOCK + quarter]
                term = dot(d, wq_s[j, c])
                total = term if total is None else total + term
        n2_s[pl.ds(at, BLOCK)] = total.astype(BF16)

    for at in range(0, count, BLOCK):
        dm_half(at).wait_send()
    loop(rows, BLOCK, back_one, service("d.", hook), 2)
    for at in range(0, count, BLOCK):
        gn2_half(at).wait_send()

    def gn1_half(at):
        return half_copy(sb2.at[pl.ds(at, BLOCK)], rb2.at[pl.ds(at, BLOCK)], 12, at)

    def back_one_sib(at):
        sb2[pl.ds(at, BLOCK)] = dot(back_s[pl.ds(count + at, BLOCK)], n2_s[...]).astype(BF16)
        gn1_half(at).start()

    def back_one_mine(at):
        mid_s[pl.ds(at, BLOCK)] = dot(back_s[pl.ds(at, BLOCK)], n2_s[...])

    loop(count, BLOCK, back_one_sib)
    loop(count, BLOCK, back_one_mine)
    hook("e.0")
    mlp_copy.wait_send()

    def first_back(at):
        gn1_half(at).wait_recv()
        for off in range(0, BLOCK, 128):
            spot = pl.ds(aligned(at + off, 128), 128)
            xhat, sigma = norm_stats(sin_s[spot])
            grad = mid_s[spot] + rb2[spot].astype(F32)
            sb1[spot] = (gm_s[spot] + norm_back(grad, ln1_gain, xhat, sigma)).astype(BF16)
            late[0:1] += column_sum(grad * xhat)
            late[1:2] += column_sum(grad)

    loop(count, BLOCK, first_back)
    put_in = local(sb1, ing_h)
    last_small.start()
    hook("e.1")
    hook("tail")
    left = [first_small, last_small] + chunks
    while left:
        for item in left:
            item.advance()
            write_finished()
        left = [item for item in left if not item.finished]

    for row, source, at in ((0, late, 0), (1, late, 1), (2, early, 0), (3, early, 1), (4, early, 2), (5, early, 3), (8, early, 4), (9, late, 2), (10, late, 3)):
        small_o[row : row + 1] = source[at : at + 1]

    passed = [copy for item in pieces for copy in item.copies]
    for copy in [unit_copy, head_copy, n1_copy, cot_copy] + [gn1_half(at) for at in range(0, count, BLOCK)] + passed:
        copy.wait_send()
    for chunk in chunks:
        for copy in chunk.sent:
            copy.wait_send()
        chunk.done.wait()
    put_out.wait()
    put_in.wait()


def copies_of(full):
    most = 0
    for kind in ORDERS:
        first, after = KINDS[kind]
        most = max(most, 1 + full + 2 * sum((1 << len(bits)) - 1 for bits in after) + (0 if first is None else 3))
    return most


def call_layer(dp_size, tokens, cotangent, ids, table, vectors, wq, wo, w1, w2):
    count, width = tokens.shape
    rows = 2 * count
    quarter = wo.shape[0]
    units = w1.shape[1]
    heads = quarter // HEAD
    grad_rows = units + 4 * quarter
    parts = units // BLOCK
    bits = [b for b in range(20) if (1 << b) < dp_size]
    half_bits = bits[:3]
    shape = jax.ShapeDtypeStruct
    vm = pltpu.VMEM
    regions = 2 * (units // BLOCK) + 4
    steps = copies_of(len(bits) - len(half_bits))
    fetched = 4 + 2 * (units // BLOCK)
    scratch = (
        [vm((count, width), BF16), vm((rows, width), BF16)]
        + [vm((count, width), F32)] * 3
        + [vm((rows, width), BF16)] * 2
        + [vm((width, rows), BF16)]
        + [vm((2,) + wq.shape, BF16), vm((2 * quarter, width), BF16), vm((2, units // BLOCK, width, BLOCK), BF16), vm((2,) + w2.shape, BF16)]
        + [vm((2, rows, 256), BF16)] * 2
        + [vm((2 * quarter, rows), BF16)] * 5
        + [vm((8, rows), F32)] * 2
        + [vm((2 * heads, 2, count, count), BF16)]
        + [vm((rows, rows), BF16)] * 2
        + [vm((rows, width), BF16)]
        + [vm((rows, 2 * units), BF16)] * 2
        + [vm((count, width), BF16)] * 4
        + [vm((grad_rows, width), BF16)] * 3
        + [vm((7 * units // 8 + 4 * quarter, width), BF16), vm((units // 2, width), BF16)]
        + [vm((parts, width, BLOCK), BF16)] * 3
        + [vm((parts, 7 * width // 8, BLOCK), BF16), vm((parts, width // 2, BLOCK), BF16)]
        + [vm((grad_rows >> len(half_bits), width), BF16)] * (len(bits) - len(half_bits))
        + [vm((parts, width // 8, BLOCK), BF16)] * (len(bits) - len(half_bits))
        + [vm((units,), F32), vm((2, quarter), F32), vm((8, width), F32), vm((8, width), F32)]
        + [vm((6, 8, width), F32), vm((14 + 2 * (len(bits) - 3), 8, width), F32)]
        + [pltpu.SemaphoreType.DMA((8 + units // BLOCK + regions,))]
        + [pltpu.SemaphoreType.DMA((2, n)) for n in (3 * fetched + 2, 14, regions * steps, 2 * (10 + len(bits) - 3))]
    )
    anywhere = pl.BlockSpec(memory_space=pl.ANY)
    inside = pl.BlockSpec(memory_space=pltpu.VMEM)
    return pl.pallas_call(
        functools.partial(layer, dp_size, half_bits),
        out_shape=[shape((count, width), BF16)] * 2
        + [shape(w2.shape, BF16), shape(w1.shape, BF16), shape(wo.shape, BF16), shape(wq.shape, BF16), shape((16, width), F32)],
        in_specs=[anywhere] * 2 + [inside] * (2 + len(vectors)) + [anywhere] * 4,
        out_specs=[anywhere] * 6 + [inside],
        scratch_shapes=scratch,
        compiler_params=pltpu.CompilerParams(vmem_limit_bytes=VMEM_LIMIT, collective_id=0, has_side_effects=True),
        name="layer",
    )(tokens, cotangent, ids, table, *vectors, wq, wo, w1, w2)


def finish(out, ing, g2, g1, go, gq, small, out_o, ing_o, g2_o, g1_o, go_o, gq_o, a0, a1, a2, a3, a4, a5, units_o, heads_o, *rest):
    narrow, wide = rest[:4], rest[4:8]
    get, put = rest[8:]
    blocks = []
    for k, (src, dst) in enumerate(((g2, g2_o), (g1, g1_o), (go, go_o), (gq, gq_o))):
        for i in range(src.shape[0] // BLOCK if src.ndim == 2 and src.shape[0] > BLOCK else 1 if src.ndim == 2 else src.shape[0]):
            at = i if src.ndim == 3 else pl.ds(i * BLOCK, min(BLOCK, src.shape[0]))
            blocks.append((src.at[at], narrow[k].at[at], wide[k].at[at], dst.at[at]))
    reads = [pltpu.make_async_copy(src, low, get.at[n]) for n, (src, low, _, _) in enumerate(blocks)]
    writes = [pltpu.make_async_copy(high, dst, put.at[n]) for n, (_, _, high, dst) in enumerate(blocks)]
    moves = [pltpu.make_async_copy(out, out_o, put.at[len(blocks)]), pltpu.make_async_copy(ing, ing_o, put.at[len(blocks) + 1])]
    for copy in reads + moves:
        copy.start()
    for i, ref in enumerate((a0, a1, a2, a3, a4, a5)):
        ref[...] = small[i]
    units_o[...] = small[8, : units_o.shape[0]]
    heads_o[...] = small[9:11, : heads_o.shape[1]]
    for read, write, (_, low, high, _) in zip(reads, writes, blocks):
        read.wait()
        size = low.shape[0]

        def cast(at, low=low, high=high):
            high[pl.ds(at, 64)] = low[pl.ds(at, 64)].astype(F32)

        loop(size, 64, cast)
        write.start()
    for copy in writes + moves:
        copy.wait()


def call_finish(arrays, small, units, quarter):
    width = small.shape[1]
    shape = jax.ShapeDtypeStruct
    extents = [(width,)] * 6 + [(units,), (2, quarter)]
    kinds = [BF16, BF16, F32, F32, F32, F32]
    anywhere = pl.BlockSpec(memory_space=pl.ANY)
    inside = pl.BlockSpec(memory_space=pltpu.VMEM)
    grads = arrays[2:]
    return pl.pallas_call(
        finish,
        in_specs=[anywhere] * len(arrays) + [inside],
        out_specs=[anywhere] * len(arrays) + [inside] * len(extents),
        out_shape=[shape(a.shape, k) for a, k in zip(arrays, kinds)] + [shape(e, F32) for e in extents],
        scratch_shapes=[pltpu.VMEM(a.shape, BF16) for a in grads]
        + [pltpu.VMEM(a.shape, F32) for a in grads]
        + [pltpu.SemaphoreType.DMA((16,)), pltpu.SemaphoreType.DMA((16,))],
        compiler_params=pltpu.CompilerParams(vmem_limit_bytes=VMEM_LIMIT),
        name="finish",
    )(*arrays, small)


def per_device(
    tokens, segment_ids, ln1_gain, ln1_bias, qkv_weight, qv_bias, out_weight, out_bias,
    ln2_gain, ln2_bias, fc1_weight, fc1_bias, fc2_weight, fc2_bias, cotangent,
):
    width = tokens.shape[1]
    freq_count = width // 6
    frequency = 10000.0 ** (-jnp.arange(freq_count, dtype=F32) / freq_count)
    angles = jnp.arange(SIDE, dtype=F32)[:, None] * frequency[None, :]
    table = jnp.concatenate([jnp.sin(angles), jnp.cos(angles)], axis=1)
    vectors = (ln1_gain, ln1_bias, out_bias, ln2_gain, ln2_bias, fc2_bias, fc1_bias, qv_bias)
    *arrays, small = call_layer(
        lax.axis_size("dp"), tokens, cotangent, segment_ids, table, vectors, qkv_weight.transpose(0, 2, 1), out_weight, fc1_weight, fc2_weight
    )
    out, ing, g2, g1, go, gq, a0, a1, a2, a3, a4, a5, g_units, g_heads = call_finish(arrays, small, fc1_weight.shape[1], out_weight.shape[0])
    return (out, ing, a0, a1, gq.transpose(0, 2, 1), g_heads, go, a2, a3, a4, g1, g_units, g2, a5)


def solution(mesh):
    placed = (
        P(("dp", "tensor"), None),
        P("dp", None),
        P(),
        P(),
        P(None, None, "tensor"),
        P(None, "tensor"),
        P("tensor", None),
        P(),
        P(),
        P(),
        P(None, "tensor"),
        P("tensor"),
        P("tensor", None),
        P(),
        P(("dp", "tensor"), None),
    )
    return jax.shard_map(
        per_device,
        mesh=mesh,
        in_specs=placed,
        out_specs=(
            P(("dp", "tensor"), None),
            P(("dp", "tensor"), None),
            P(),
            P(),
            P(None, None, "tensor"),
            P(None, "tensor"),
            P("tensor", None),
            P(),
            P(),
            P(),
            P(None, "tensor"),
            P("tensor"),
            P("tensor", None),
            P(),
        ),
        check_vma=False,
    )
```

```python
import functools

import jax
import jax.numpy as jnp
from jax import lax
from jax.experimental import pallas as pl
from jax.experimental.pallas import tpu as pltpu
from jax.sharding import PartitionSpec as P

HEAD = 64
SIDE = 16
EPSILON = 1e-06
NEG_LARGE = -1e30
SCALE = HEAD ** (-0.5)
F32 = jnp.float32
BF16 = jnp.bfloat16
VMEM_LIMIT = 64 * 1024 * 1024 - 128 * 1024
MESH = pl.DeviceIdType.MESH
BLOCK = 256
KINDS = {
    "A": (None, ((0,), (1,), (2,))),
    "B": (None, ((1,), (0,), (2,))),
    "D": (None, ((0,), (1, 2))),
    "E": (None, ((0, 1, 2),)),
    "Y": (0, ((1,), (2,))),
    "Z": (1, ((0,), (2,))),
    "YD": (0, ((1, 2),)),
    "S": (None, (("p",), ("q",), (2,))),
    "SD": (None, (("p",), ("q", 2))),
    "SF": ("p", (("q",), (2,))),
    "SFD": ("p", (("q", 2),)),
}
ORDERS = ("SFD", "SD", "A", "SF", "SF", "D", "S", "SD", "SD", "D")
WEIGHT_PLAN = {"p0": (0,), "a2": (1,), "p1": (3, 4), "c2": (5,), "o": (6,), "r10.0": (7,), "r00.0": (8,), "r11.1": (9,)}
PLAN = {
    "f01": (0,),
    "r12.1": (1,),
    "f02": (3, 1),
    "g0": (2,),
    "lb": (0, 4),
    "ln2": (1,),
    "fin": (2,),
    "w1.0": (-1,),
    "w1.1": (0, 5),
    "w0.0": (2, 1, 3),
    "b1.0": (4, -1, 5),
    "b1.1": (1, 0, 3),
    "k1": (4, 2, 6),
    "b0.0": (5, 0),
    "b0.1": (3, 9, 4),
    "k0": (6,),
    "s0": (2,),
    "d.0": (8,),
    "d.1": (5, 9, 6),
    "e.0": (3, 2),
    "e.1": (4, 7, 8),
    "tail": (9, 5, 6, 3, -2, 2, 4, 7, 9, 8, 6, 3, -2, 4, 7, 9, 8, 6, 7, 8, 6, 7),
}


def dot(a, b):
    return jnp.dot(a, b, preferred_element_type=F32)


def dot_nt(a, b):
    return lax.dot_general(a, b, (((1,), (1,)), ((), ())), preferred_element_type=F32)


def dot_tn(a, b):
    return lax.dot_general(a, b, (((0,), (0,)), ((), ())), preferred_element_type=F32)


def lane_half(rows, upper):
    lanes = lax.broadcasted_iota(jnp.int32, (rows, 128), 1)
    return lanes >= HEAD if upper else lanes < HEAD


def head_lanes(ref, head, filler):
    tile = ref[:, 128 * (head // 2) : 128 * (head // 2) + 128]
    return jnp.where(lane_half(tile.shape[0], head % 2 == 1), tile, filler)


def gelu_pair(h):
    cdf = 0.5 + 0.5 * lax.erf(h * 0.7071067811865476)
    return h * cdf, cdf + h * jnp.exp(-0.5 * h * h) * 0.3989422804014327


def norm_stats(v):
    centred = v - jnp.mean(v, axis=-1, keepdims=True)
    sigma = lax.rsqrt(jnp.mean(centred * centred, axis=-1, keepdims=True) + EPSILON)
    return centred * sigma, sigma


def norm_back(grad, gain, xhat, sigma):
    g = grad * gain
    return sigma * (g - jnp.mean(g, axis=-1, keepdims=True) - xhat * jnp.mean(g * xhat, axis=-1, keepdims=True))


def column_sum(v):
    return jnp.sum(v, axis=0, keepdims=True)


def aligned(v, unit):
    return v if isinstance(v, int) else pl.multiple_of(v, unit)


def loop(count, step, body, service=None, every=1):
    def run(i, carry):
        body(aligned(i * step, step))
        if service is not None:
            for k in range(count // step // every):
                if service(k, True):
                    pl.when(i == every * (k + 1) - 1)(functools.partial(service, k, False))
        return carry

    lax.fori_loop(0, count // step, run, 0)


def layer(
    dp_size, half_bits,
    tok_h, cot_h, ids, table, gain1, bias1, bias_o, gain2, bias2, bias_f, bias_u, bias_qv, wq_h, wo_h, w1_h, w2_h,
    out_h, ing_h, g2_h, g1_h, go_h, gq_h, small_o,
    tok_s, cot_s, sin_s, mid_s, gm_s, n1_s, n2_s, n2t_s, wq_s, wo_s, w1_s, w2_s,
    q_s, v_s, kt_s, ot_s, ou_s, gt_s, gr_s, r_s, in_s, e_s, roll_s, back_s, nr_s, a_s, g_s, sb1, sb2, rb1, rb2,
    own, oth, xr, land, land_both, own1, oth1, xr1, land1, land1_both, *rest,
):
    rest = list(rest)
    full_bits = [b for b in range(20) if (1 << b) < dp_size and b not in half_bits]
    rx = [rest.pop(0) for _ in full_bits]
    rx1 = [rest.pop(0) for _ in full_bits]
    uoth, voth, early, late, near, far, lsem, wsem, csem, gsem, ssem = rest

    count, width = tok_s.shape
    rows = 2 * count
    quarter = wo_h.shape[0]
    units = w1_h.shape[1]
    heads = quarter // HEAD
    place = lax.axis_index("tensor")
    dp = lax.axis_index("dp")
    chip = place // 2
    core = place % 2
    sib = {"tensor": chip * 2 + 1 - core}
    across = {"tensor": (1 - chip) * 2 + core}
    facing = {"tensor": (1 - chip) * 2 + 1 - core}
    all_bits = list(half_bits) + full_bits
    sides = {b: (dp // (1 << b)) % 2 for b in all_bits}

    ways = {b: (1 - 2 * sides[b]) * (1 << b) for b in all_bits}
    sides["p"] = sides[0] + (sides[1] - sides[0]) * core
    sides["q"] = sides[1] + (sides[0] - sides[1]) * core
    ways["p"] = ways[0] + (ways[1] - ways[0]) * core
    ways["q"] = ways[1] + (ways[0] - ways[1]) * core

    def mate(bits):
        return {"dp": dp + sum(ways[b] for b in bits)}

    def described(src, dst, sems, index, device):
        return pltpu.make_async_remote_copy(
            src_ref=src, dst_ref=dst, send_sem=sems.at[0, index], recv_sem=sems.at[1, index], device_id=device, device_id_type=MESH
        )

    mates = {b: mate((b,)) for b in all_bits}
    groups = {(b,) for b in full_bits}
    for mask in range(1, 1 << len(half_bits)):
        groups.add(tuple(b for k, b in enumerate(half_bits) if mask >> k & 1))

    barrier = pltpu.get_barrier_semaphore()
    partners = [sib, across, facing] + [mate(bits) for bits in sorted(groups)]
    for partner in partners:
        pl.semaphore_signal(barrier, inc=1, device_id=partner, device_id_type=MESH)

    sq_s, sk_s, k_s = a_s.at[:, 0:128], a_s.at[:, 128:256], a_s.at[:, 256:512]
    local_used = [0]

    def local(src, dst):
        copy = pltpu.make_async_copy(src, dst, lsem.at[local_used[0]])
        local_used[0] += 1
        copy.start()
        return copy

    def remote(src, dst, sems, index, device):
        copy = pltpu.make_async_remote_copy(
            src_ref=src, dst_ref=dst, send_sem=sems.at[0, index], recv_sem=sems.at[1, index], device_id=device, device_id_type=MESH
        )
        copy.start()
        return copy

    def half_copy(src, dst, first, at):
        return pltpu.make_async_remote_copy(
            src_ref=src,
            dst_ref=dst,
            send_sem=csem.at[0, first + at // BLOCK],
            recv_sem=csem.at[1, first + at // BLOCK],
            device_id=sib,
            device_id_type=MESH,
        )

    get_tok = local(tok_h, tok_s)
    get_cot = local(cot_h, cot_s.at[pl.ds(0, count)])
    get_wq = local(wq_h, wq_s.at[0])
    get_wo = local(wo_h, wo_s.at[pl.ds(0, quarter)])
    get_w1 = [local(w1_h.at[:, pl.ds(i * BLOCK, BLOCK)], w1_s.at[0, i]) for i in range(units // BLOCK)]
    get_w2 = local(w2_h, w2_s.at[0])

    ln1_gain, ln1_bias, out_bias, ln2_gain, ln2_bias, fc2_bias = (
        ref[...].reshape(1, width) for ref in (gain1, bias1, bias_o, gain2, bias2, bias_f)
    )
    get_tok.wait()

    def first_norm(at):
        plane = core * (count // (SIDE * SIDE)) + at // (SIDE * SIDE)
        line = (at // SIDE) % SIDE
        shape = (SIDE, width // 3)
        for k in range(4):
            spot = jnp.concatenate(
                [jnp.broadcast_to(table[pl.ds(plane, 1)], shape), jnp.broadcast_to(table[pl.ds(line + k, 1)], shape), table[...]], axis=1
            )
            span = pl.ds(aligned(at + k * SIDE, SIDE), SIDE)
            stream = tok_s[span].astype(F32) + spot
            sin_s[span] = stream
            xhat, _ = norm_stats(stream)
            n1_s[span] = (xhat * ln1_gain + ln1_bias).astype(BF16)

    loop(count, 4 * SIDE, first_norm)
    doc = ids[pl.ds(chip, 1), :]
    starts = [jnp.zeros((1, 1), F32)]
    starts += [jnp.sum(jnp.where(doc < v, 1.0, 0.0), axis=1, keepdims=True) for v in range(1, 4)]
    starts.append(jnp.full((1, 1), rows, F32))
    turn = jnp.zeros((1, 1), F32)
    for v in range(4):
        turn += jnp.where(starts[v + 1] - starts[v] == count, starts[v], 0.0)
    turn_here = turn - (core * count).astype(F32)

    def wrapped(v):
        v = jnp.where(v >= rows, v - rows, v)
        return jnp.where(v < 0, v + rows, v)

    def rotations(at):
        down = (lax.broadcasted_iota(jnp.int32, (64, rows), 0) + at).astype(F32)
        along = lax.broadcasted_iota(jnp.int32, (64, rows), 1).astype(F32)
        roll_s[pl.ds(at, 64)] = jnp.where(wrapped(down + turn_here) == along, 1.0, 0.0).astype(BF16)
        back_s[pl.ds(at, 64)] = jnp.where(wrapped(down - turn_here) == along, 1.0, 0.0).astype(BF16)
        where = wrapped((lax.broadcasted_iota(jnp.int32, (64, 128), 0) + at).astype(F32) + turn)
        mine = sum(jnp.where(where >= starts[v], 1.0, 0.0) for v in range(1, 4))
        slot = (lax.broadcasted_iota(jnp.int32, (64, 128), 1) % HEAD).astype(F32)
        sq_s[pl.ds(at, 64)] = jnp.where((slot < 4) & (slot != mine), 1.0, 0.0).astype(BF16)
        sk_s[pl.ds(at, 64)] = jnp.where(slot == mine, NEG_LARGE, 0.0).astype(BF16)


    pl.semaphore_wait(barrier, len(partners))
    unit_copy = remote(bias_u, uoth, wsem, 3 * (4 + 2 * (units // BLOCK)), across)
    head_copy = remote(bias_qv, voth, wsem, 3 * (4 + 2 * (units // BLOCK)) + 1, across)
    get_wq.wait()
    get_wo.wait()
    for copy in get_w1:
        copy.wait()
    get_w2.wait()

    part = (sides[0] + sides[1]) % 2

    class Piece:
        def __init__(self, index, refs, at, extent):
            size = extent // 4

            def some(k, first, size):
                return refs[k].at[pl.ds(aligned(at[k] + part * (extent // 2) + first, 16), size)]

            self.copies = [described(some(0, 0, 2 * size), some(1, 0, 2 * size), wsem, 3 * index, across)]
            for k in range(2):
                block = some(1, k * size, size)
                self.copies.append(described(block, block, wsem, 3 * index + 1 + k, mates[k]))
            self.stage = 0

        def advance(self):
            if self.stage == 0:
                self.copies[0].wait_recv()
                self.copies[1].start()
                self.copies[2].start()
            else:
                self.copies[1].wait_recv()
                self.copies[2].wait_recv()
            self.stage += 1

    pieces = [Piece(c, (wq_s.at[0, c], wq_s.at[1, c]), (0, 0), quarter) for c in range(3)]
    pieces.append(Piece(3, (wo_s, wo_s), (0, quarter), quarter))
    for i in range(units // BLOCK):
        pieces.append(Piece(4 + 2 * i, (w1_s.at[0, i], w1_s.at[1, i]), (0, 0), width))
        pieces.append(Piece(5 + 2 * i, (w2_s.at[0], w2_s.at[1]), (i * BLOCK, i * BLOCK), BLOCK))
    for item in pieces:
        item.copies[0].start()

    inside_loop = []

    def service(name, act):
        def at_point(k, ask):
            full = f"{name}{k}"
            if ask:
                return full in PLAN or full in WEIGHT_PLAN
            inside_loop.append(full)
            act(full)
            inside_loop.pop()

        return at_point

    def pass_on(name):
        for i in WEIGHT_PLAN.get(name, ()):
            if pieces[i].stage < 1:
                pieces[i].advance()

    def have_weight(*which):
        for i in which:
            while pieces[i].stage < 2:
                pieces[i].advance()

    n1_copy = remote(n1_s.at[pl.ds(0, count)], n1_s.at[pl.ds(count, count)], csem, 0, sib)
    get_cot.wait()
    cot_copy = remote(cot_s.at[pl.ds(0, count)], cot_s.at[pl.ds(count, count)], csem, 1, sib)

    def rotate(at):
        nr_s[pl.ds(at, BLOCK)] = dot(roll_s[pl.ds(at, BLOCK)], n1_s[...]).astype(BF16)

    def project(j, at):
        n = nr_s[pl.ds(at, BLOCK)]
        biases = bias_qv if j == 0 else voth
        q = (dot_nt(n, wq_s[j, 0]) + biases[0:1]).astype(BF16) * SCALE
        k = dot_nt(n, wq_s[j, 1]).astype(BF16)
        v = (dot_nt(n, wq_s[j, 2]) + biases[1:2]).astype(BF16)
        q_s[j, pl.ds(at, BLOCK), :quarter] = q
        k_s[pl.ds(at, BLOCK), :quarter] = k
        v_s[j, pl.ds(at, BLOCK), :quarter] = v
        kt_s[j * quarter : (j + 1) * quarter, pl.ds(at, BLOCK)] = k.T * SCALE

    blocks = [(b, at) for b in range(2) for at in range(0, count, BLOCK)]

    def attend(j):
        for head in range(heads):
            at = 512 + 256 * head
            a_s[:, at : at + 128] = head_lanes(q_s.at[j], head, sq_s[...])
            a_s[:, at + 128 : at + 256] = head_lanes(k_s, head, sk_s[...])
        for at in range(0, rows, BLOCK):
            ou_s[:quarter, at : at + BLOCK] = v_s[j, at : at + BLOCK, :quarter].T

        def tile(here):
            b = here // count
            at = aligned(here % count, BLOCK)
            keys = pl.ds(aligned(b * count, count), count)
            for head in range(heads):
                column = 512 + 256 * head
                s = dot_nt(a_s[keys, column + 128 : column + 256], a_s[pl.ds(here, BLOCK), column : column + 128])
                m = jnp.max(s, axis=0, keepdims=True)
                e = jnp.exp(s - m)
                r = 1.0 / column_sum(e)
                low = e.astype(BF16)
                span = slice(head * HEAD, head * HEAD + HEAD)
                to = slice(j * quarter + head * HEAD, j * quarter + head * HEAD + HEAD)
                e_s[j * heads + head, b, :, pl.ds(at, BLOCK)] = low
                ot_s[to, pl.ds(here, BLOCK)] = (dot(ou_s[span, keys], low) * r).astype(BF16)
                r_s[j * heads + head : j * heads + head + 1, pl.ds(here, BLOCK)] = r

        return tile

    loop(rows, 64, rotations)
    n1_copy.wait_recv()
    loop(rows, BLOCK, rotate)
    loop(rows, BLOCK, lambda at: project(0, at))
    pass_on("p0")
    loop(rows, BLOCK, attend(0), service("a", pass_on))
    head_copy.wait_recv()
    have_weight(0, 1, 2)
    loop(rows, BLOCK, lambda at: project(1, at))
    pass_on("p1")
    loop(rows, BLOCK, attend(1), service("c", pass_on))

    have_weight(3)

    def unrotate(at):
        ou_s[:, pl.ds(at, BLOCK)] = dot(ot_s[...], roll_s[:, pl.ds(at, BLOCK)]).astype(BF16)

    loop(rows, BLOCK, unrotate)
    pass_on("u")

    def out_part(at):
        return dot_tn(ou_s[:, pl.ds(at, BLOCK)], wo_s[...])

    def att_half(at):
        return half_copy(sb1.at[pl.ds(at, BLOCK)], rb1.at[pl.ds(at, BLOCK)], 2, at)

    def n2_half(at):
        return half_copy(n2_s.at[pl.ds(at, BLOCK)], n2_s.at[pl.ds(aligned(count + at, BLOCK), BLOCK)], 4, at)

    def out_sib(at):
        sb1[pl.ds(at, BLOCK)] = out_part(count + at).astype(BF16)
        att_half(at).start()

    loop(count, BLOCK, out_sib)

    def out_mine(at):
        mid_s[pl.ds(at, BLOCK)] = sin_s[pl.ds(at, BLOCK)] + out_part(at) + out_bias

    loop(count, BLOCK, out_mine)
    pass_on("o")

    def second_norm(at):
        att_half(at).wait_recv()
        for off in range(0, BLOCK, 128):
            spot = pl.ds(aligned(at + off, 128), 128)
            mid = mid_s[spot] + rb1[spot].astype(F32)
            mid_s[spot] = mid
            xhat, _ = norm_stats(mid)
            n2_s[spot] = (xhat * ln2_gain + ln2_bias).astype(BF16)
        n2_half(at).start()

    loop(count, BLOCK, second_norm)
    pass_on("n")

    base_a = units
    parts = units // BLOCK
    steps = copies_of(len(full_bits))

    class Region:
        def __init__(self, index, row, size, cols, slot, kind, refs, to):
            own_r, oth_r, xr_r, land_r, both_r, rx_r = refs
            self.place, self.slot, self.to, self.xr = (row, size, 0, cols), slot, to, xr_r
            first, after = KINDS[kind]
            self.first = first is not None
            self.stages, self.stage, self.finished, self.sent = [], -1, False, []
            now, parts, used, trail = self.place, 8, 0, []
            sems = iter(range(index * steps, (index + 1) * steps))

            def copy(src, src_at, dst, dst_at, device):
                return described(src.at[self.window(src_at)], dst.at[self.window(dst_at)], gsem, next(sems), device)

            def piece(bits, mask):
                where = now
                for k, b in enumerate(bits):
                    where = self.cut(where, 1 - sides[b] if mask >> k & 1 else sides[b])
                return where

            sums = 1 + len(after) + len(full_bits)
            if self.first:
                keep, give, there = piece((first,), 0), piece((first,), 1), (row // 2, size // 2, 0, cols)
                place = self.landing(0, 4)
                copies = [copy(own_r, give, land_r, place, mate((first,))), copy(oth_r, give, both_r, there, mate((first,)))]
                adds = [(own_r, own_r, keep, [(land_r, place)]), (oth_r, oth_r, keep, [(both_r, there)])]
                self.stages.append((copies, adds, False))
                trail.append(((first,), keep))
                now, parts, used = keep, 4, 4
            self.stages.append(([copy(oth_r, now, xr_r, now, across)], [(own_r, own_r, now, [(xr_r, now)])], False))
            for bits in after:
                parts >>= len(bits)
                keep, copies, terms = piece(bits, 0), [], []
                for mask in range(1, 1 << len(bits)):
                    place = self.landing(used, parts)
                    used += parts
                    terms.append((land_r, place))
                    copies.append(copy(own_r, piece(bits, mask), land_r, place, mate([b for k, b in enumerate(bits) if mask >> k & 1])))
                self.stages.append((copies, [(own_r, own_r, keep, terms)], False))
                trail.append((bits, keep))
                now = keep
            for i, b in enumerate(full_bits):
                place = self.small_place()
                self.stages.append(([copy(own_r, now, rx_r[i], place, mates[b])], [(own_r, own_r, now, [(rx_r[i], place)])], True))
            copies, adds, full = self.stages[-1]
            self.stages[-1] = (copies, [(xr_r,) + adds[0][1:]], full)
            for bits, keep in reversed(trail):
                copies = []
                for mask in range(1, 1 << len(bits)):
                    copies.append(copy(xr_r, keep, xr_r, keep, mate([b for k, b in enumerate(bits) if mask >> k & 1])))
                self.stages.append((copies, [], False))

        def window(self, where):
            row, size, col, cols = where
            return pl.ds(row, size), pl.ds(col, cols)

        def cut(self, where, side):
            row, size, col, cols = where
            if (size // 2) % 16 == 0:
                return aligned(row + side * (size // 2), 16), size // 2, col, cols
            return row, size, aligned(col + side * (cols // 2), 128), cols // 2

        def landing(self, at, parts_here):
            row, rows_one, cols_one = self.slot
            full = self.place[3]
            if cols_one == full:
                return row + at * rows_one, parts_here * rows_one, 0, full
            if parts_here == 1:
                return row + at // 2 * rows_one, rows_one, at % 2 * cols_one, cols_one
            return row + at // 2 * rows_one, parts_here // 2 * rows_one, 0, full

        def small_place(self):
            row, rows_one, cols_one = self.slot
            if cols_one == self.place[3]:
                return row // 7, rows_one, 0, cols_one
            k = (self.place[0] - base_a) // quarter
            return units // 8 + k // 2 * rows_one, rows_one, k % 2 * cols_one, cols_one

        def begin(self, copies):
            for copy in copies:
                copy.start()
            self.sent += copies

        def ready(self, j):
            if self.first:
                self.stage = 0
                self.begin([self.stages[0][0][j]])
            elif j == 1:
                self.stage = 0
                self.begin(self.stages[0][0])

        def add(self, into, base, where, terms):
            row, size, col, cols = where
            step = 64 if size % 64 == 0 else 48 if size % 48 == 0 else 32

            def body(off):
                to = (pl.ds(aligned(row + off, 16), step), pl.ds(col, cols))
                total = base[to].astype(F32)
                for ref, (r, _, c, _) in terms:
                    total += ref[pl.ds(aligned(r + off, 16), step), pl.ds(c, cols)].astype(F32)
                into[to] = total.astype(BF16)

            if inside_loop:
                for off in range(0, size, step):
                    body(off)
            else:
                loop(size, step, body)

        def advance(self):
            if self.finished or self.stage < 0:
                return
            copies, adds, full = self.stages[self.stage]
            for copy in copies:
                copy.wait_recv()
            if full:
                for copy in copies:
                    copy.wait_send()
                self.sent = [c for c in self.sent if all(c is not d for d in copies)]
            for item in adds:
                self.add(*item)
            self.stage += 1
            if self.stage < len(self.stages):
                self.begin(self.stages[self.stage][0])
                return
            self.finished = True
            to_write.append(self)

    chunks = []
    refs = (own, oth, xr, land, land_both, rx)
    for i in range(parts):
        slot = (i * 7 * (BLOCK // 8), BLOCK // 8, width)
        to = g2_h.at[pl.ds(i * BLOCK, BLOCK)]
        chunks.append(Region(2 * i, i * BLOCK, BLOCK, width, slot, ORDERS[2 * i], refs, to))
        refs_one = tuple(ref.at[i] for ref in (own1, oth1, xr1, land1, land1_both)) + ([ref.at[i] for ref in rx1],)
        to = g1_h.at[:, pl.ds(i * BLOCK, BLOCK)]
        chunks.append(Region(2 * i + 1, 0, width, BLOCK, (0, width // 8, BLOCK), ORDERS[2 * i + 1], refs_one, to))
    for i in range(4):
        slot = (7 * units // 8 + i * quarter, quarter // 4, width // 2)
        to = go_h if i == 0 else gq_h.at[i - 1]
        chunks.append(Region(2 * parts + i, base_a + i * quarter, quarter, width, slot, ORDERS[2 * parts + i], refs, to))
    first_att = 2 * parts

    class Small:
        def __init__(self, tile, index, everywhere, paired):
            self.tile, self.everywhere, self.paired = tile, everywhere, paired
            self.near = [near.at[3 * index + k] for k in range(3)]
            self.far = [far.at[(7 + len(full_bits)) * index + k] for k in range(7 + len(full_bits))]
            devices = [sib, across, facing]
            devices += [mate([b for k, b in enumerate(half_bits) if mask >> k & 1]) for mask in range(1, 8)]
            devices += [mates[b] for b in full_bits]
            base = index * len(devices)
            copies = [described(tile, dst, ssem, base + k, d) for k, (dst, d) in enumerate(zip(self.near + self.far, devices))]
            self.stages = [copies[:3], copies[3:10]] + [[copy] for copy in copies[10:]]
            self.stage, self.finished = -1, False

        def start(self):
            self.stage = 0
            for copy in self.stages[0]:
                copy.start()

        def advance(self):
            if self.finished or self.stage < 0:
                return
            for copy in self.stages[self.stage]:
                copy.wait()
            tile = self.tile
            if self.stage == 0:
                beside, over, facing_ = self.near
                n, p = self.everywhere, self.paired
                tile[0:n] = (tile[0:n] + beside[0:n]) + (over[0:n] + facing_[0:n])
                tile[n : n + p] = tile[n : n + p] + over[n + p : n + 2 * p]
            elif self.stage == 1:
                got = [tile] + self.far[:7]
                pairs = [got[2 * k][...] + got[2 * k + 1][...] for k in range(4)]
                tile[...] = (pairs[0] + pairs[1]) + (pairs[2] + pairs[3])
            else:
                tile[...] = tile[...] + self.far[5 + self.stage][...]
            self.stage += 1
            if self.stage == len(self.stages):
                self.finished = True
                return
            for copy in self.stages[self.stage]:
                copy.start()

    first_small = Small(early, 0, 4, 1)
    last_small = Small(late, 1, 2, 2)

    def ready(i, j):
        chunks[i].ready(j)

    to_write = []

    def write_finished():
        while to_write:
            region = to_write.pop()
            region.done = local(region.xr.at[region.window(region.place)], region.to)

    def hook(name):
        pass_on(name)
        for i in PLAN.get(name, ()):
            (chunks + [last_small, first_small])[i].advance()
            if not inside_loop:
                write_finished()

    def chunk_rows(j, i, at):
        span = pl.ds(at, BLOCK)
        cols = slice(j * units + i * BLOCK, j * units + (i + 1) * BLOCK)
        mine = slice(i * BLOCK, (i + 1) * BLOCK)
        bias = (bias_u if j == 0 else uoth)[mine].reshape(1, BLOCK)
        h = dot(n2_s[span], w1_s[j, i]) + bias
        a, slope = gelu_pair(h)
        a_s[span, cols] = a.astype(BF16)
        g = (dot_nt(cot_s[span], w2_s[j, mine]) * slope).astype(BF16)
        g_s[span, cols] = g

    def chunk_grads(j, i):
        cols = slice(j * units + i * BLOCK, j * units + (i + 1) * BLOCK)
        mine = slice(i * BLOCK, (i + 1) * BLOCK)
        to = oth if j == 1 else own

        def second(at):
            to[pl.ds(i * BLOCK + at, 128)] = dot_tn(a_s[:, pl.ds(cols.start + at, 128)], cot_s[...]).astype(BF16)

        loop(BLOCK, 128, second)
        ready(2 * i, j)
        g = g_s[:, cols]

        def first(at):
            (oth1 if j == 1 else own1)[i, pl.ds(at, BLOCK)] = dot(n2t_s[pl.ds(at, BLOCK)], g_s[:, cols]).astype(BF16)

        loop(width, BLOCK, first)
        ready(2 * i + 1, j)
        early[4 + j : 5 + j, mine] = column_sum(g.astype(F32))
        hook(f"f{j}{i}")

    def feed(j, i, first=False):
        if first:
            loop(count, BLOCK, lambda at: chunk_rows(j, i, at))
            hook(f"r{j}{i}.0")
            cot_copy.wait_recv()

            def received(at):
                n2_half(at).wait_recv()
                chunk_rows(j, i, count + at)

            loop(count, BLOCK, received)
            hook(f"r{j}{i}.1")

            def turned(at):
                n2t_s[:, pl.ds(at, BLOCK)] = n2_s[pl.ds(at, BLOCK)].T

            loop(rows, BLOCK, turned)
        else:
            loop(rows, BLOCK, lambda at: chunk_rows(j, i, at), service(f"r{j}{i}.", hook), 2)
        chunk_grads(j, i)

    early[...] = jnp.zeros_like(early)
    late[...] = jnp.zeros_like(late)
    unit_copy.wait_recv()
    for i in range(parts):
        have_weight(4 + 2 * i, 5 + 2 * i)
        feed(1, i, first=i == 0)
        feed(0, i)

    def back_two(at):
        span = pl.ds(at, BLOCK)
        total = None
        for j in range(2):
            for i in range(parts):
                at_col = j * units + i * BLOCK
                term = dot_nt(g_s[span, at_col : at_col + BLOCK], w1_s[j, i])
                total = term if total is None else total + term
        return total

    def mlp_part(at):
        span = pl.ds(at, BLOCK)
        return dot(a_s[span, :units], w2_s[0]) + dot(a_s[span, units:], w2_s[1])

    def gn2_half(at):
        return half_copy(sb2.at[pl.ds(at, BLOCK)], rb2.at[pl.ds(at, BLOCK)], 6, at)

    def dm_half(at):
        return half_copy(n2_s.at[pl.ds(at, BLOCK)], n2_s.at[pl.ds(aligned(count + at, BLOCK), BLOCK)], 10, at)

    def back_two_sib(at):
        sb2[pl.ds(at, BLOCK)] = back_two(count + at).astype(BF16)
        gn2_half(at).start()

    def back_two_mine(at):
        gm_s[pl.ds(at, BLOCK)] = back_two(at)

    def mlp_sib(at):
        sb1[pl.ds(at, BLOCK)] = mlp_part(count + at).astype(BF16)

    loop(count, BLOCK, back_two_sib)
    hook("g0")
    loop(count, BLOCK, back_two_mine)
    hook("gn2")

    def second_back(at):
        gn2_half(at).wait_recv()
        n2_half(at).wait_send()
        for off in range(0, BLOCK, 128):
            spot = pl.ds(aligned(at + off, 128), 128)
            xhat, sigma = norm_stats(mid_s[spot])
            grad = gm_s[spot] + rb2[spot].astype(F32)
            cot = cot_s[spot].astype(F32)
            back = cot + norm_back(grad, ln2_gain, xhat, sigma)
            gm_s[spot] = back
            n2_s[spot] = back.astype(BF16)
            early[0:1] += column_sum(back)
            early[1:2] += column_sum(grad * xhat)
            early[2:3] += column_sum(grad)
            early[3:4] += column_sum(cot)
        dm_half(at).start()

    loop(count, BLOCK, second_back)
    hook("lb")
    for at in range(0, count, BLOCK):
        att_half(at).wait_send()
    loop(count, BLOCK, mlp_sib)
    mlp_copy = remote(sb1, rb1, csem, 8, sib)
    first_small.start()
    hook("ln2")

    def finish_out(at):
        span = pl.ds(at, BLOCK)
        mid_s[span] = mid_s[span] + mlp_part(at) + fc2_bias

    loop(count, BLOCK, finish_out)
    hook("fo")
    mlp_copy.wait_recv()

    def write_out(at):
        spot = pl.ds(at, 128)
        tok_s[spot] = (mid_s[spot] + rb1[spot].astype(F32)).astype(BF16)

    loop(count, 128, write_out)
    put_out = local(tok_s, out_h)
    hook("fin")
    for at in range(0, count, BLOCK):
        dm_half(at).wait_recv()

    start = base_a + quarter
    zero = jnp.zeros((count, 128), BF16)
    grad_s = dq_s = gr_s

    def keep_gradient(j, c):
        to = oth if j == 1 else own
        low = start + c * quarter
        dt = ot_s.at[j * quarter : (j + 1) * quarter]

        def columns(at):
            to[low : low + quarter, pl.ds(at, BLOCK)] = dot(dt[...], nr_s[:, pl.ds(at, BLOCK)]).astype(BF16)

        loop(width, BLOCK, columns)
        ready(first_att + 1 + c, j)
        if c != 1:
            d = g_s[:, (3 * j + c) * BLOCK : (3 * j + c) * BLOCK + quarter]
            late[2 + c // 2 + 2 * j : 3 + c // 2 + 2 * j, :quarter] = column_sum(d.astype(F32))

    def values_back(j):
        base = j * quarter
        to = oth if j == 1 else own

        def weight(at):
            to[base_a : base_a + quarter, pl.ds(at, BLOCK)] = dot(ou_s[base : base + quarter], n2_s[:, pl.ds(at, BLOCK)]).astype(BF16)

        loop(width, BLOCK, weight)
        ready(first_att, j)

        def output(at):
            grad_s[base : base + quarter, pl.ds(at, BLOCK)] = dot_nt(wo_s[base : base + quarter], n2_s[pl.ds(at, BLOCK)]).astype(BF16)

        loop(rows, BLOCK, output)
        hook(f"w{j}.0")
        go_s = a_s.at[:, rows + 256 * j : rows + 256 * (j + 1)]

        def scale(at):
            here = pl.ds(at, BLOCK)
            grad_t = dot_nt(grad_s[base : base + quarter], roll_s[here])
            for head in range(heads):
                row = j * heads + head
                r = r_s[row : row + 1, here]
                g = grad_t[head * HEAD : (head + 1) * HEAD]
                at_head = slice(base + head * HEAD, base + (head + 1) * HEAD)
                in_s[row : row + 1, here] = column_sum(g * ot_s[at_head, here].astype(F32)) * r
                gt_s[at_head, here] = (g * r).astype(BF16)
            go_s[here, :quarter] = gt_s[base : base + quarter, here].T

        loop(rows, BLOCK, scale)

        def block(at):
            here = pl.ds(at, count)
            b = at // count
            dv = [None, None]
            for head in range(heads):
                tile = head // 2
                gh = jnp.where(lane_half(count, head % 2 == 1), go_s[here, 128 * tile : 128 * tile + 128], zero)
                part = dot(e_s[j * heads + head, b], gh)
                dv[tile] = part if dv[tile] is None else dv[tile] + part
            dv = jnp.concatenate(dv, axis=1)[:, :quarter].astype(BF16)
            g_s[here, (3 * j + 2) * BLOCK : (3 * j + 2) * BLOCK + quarter] = dv
            ot_s[base : base + quarter, here] = dv.T

        loop(rows, count, block)
        hook(f"w{j}.1")
        keep_gradient(j, 2)
        hook(f"v{j}")

    def scores_back(j):
        base = j * quarter

        def block(at):
            here = pl.ds(at, count)
            b = at // count
            dk = [None, None]
            for head in range(heads):
                tile = head // 2
                row = j * heads + head
                half = lane_half(count, head % 2 == 1)
                lanes = slice(128 * tile, 128 * tile + 128)
                vh = jnp.where(half, v_s[j, here, lanes], zero)
                qh = jnp.where(half, q_s[j, here, lanes], zero)
                last_row = min(128 * tile + 128, quarter)
                vh = vh[:, : last_row - 128 * tile]
                ds = a_s.at[:count, head * count : (head + 1) * count] if head < 2 else a_s.at[count:, :count]
                for off in range(0, count, BLOCK):
                    some = pl.ds(aligned(at + off, BLOCK), BLOCK)
                    dp_t = dot(vh, gt_s[base + 128 * tile : base + last_row, some])
                    grad = (dp_t - in_s[row : row + 1, some]) * e_s[row, b, :, off : off + BLOCK].astype(F32)
                    ds[:, off : off + BLOCK] = grad.astype(BF16)
                part = dot(ds[...], qh)
                dk[tile] = part if dk[tile] is None else dk[tile] + part
                kth = kt_s[base + head * HEAD : base + head * HEAD + HEAD, here]
                dq_s[base + head * HEAD : base + head * HEAD + HEAD, here] = dot(kth, ds[...]).astype(BF16)
            dk = jnp.concatenate(dk, axis=1)[:, :quarter].astype(BF16)
            g_s[here, (3 * j + 1) * BLOCK : (3 * j + 1) * BLOCK + quarter] = dk
            ot_s[base : base + quarter, here] = dk.T
            g_s[here, 3 * j * BLOCK : 3 * j * BLOCK + quarter] = dq_s[base : base + quarter, here].T

        loop(rows, count, block, service(f"b{j}.", hook))
        keep_gradient(j, 1)
        hook(f"k{j}")
        ot_s[base : base + quarter] = dq_s[base : base + quarter]
        keep_gradient(j, 0)
        hook(f"s{j}")

    values_back(1)
    values_back(0)
    scores_back(1)
    scores_back(0)

    def back_one(at):
        total = None
        for j in range(2):
            for c in range(3):
                d = g_s[pl.ds(at, BLOCK), (3 * j + c) * BLOCK : (3 * j + c) * BLOCK + quarter]
                term = dot(d, wq_s[j, c])
                total = term if total is None else total + term
        n2_s[pl.ds(at, BLOCK)] = total.astype(BF16)

    for at in range(0, count, BLOCK):
        dm_half(at).wait_send()
    loop(rows, BLOCK, back_one, service("d.", hook), 2)
    for at in range(0, count, BLOCK):
        gn2_half(at).wait_send()

    def gn1_half(at):
        return half_copy(sb2.at[pl.ds(at, BLOCK)], rb2.at[pl.ds(at, BLOCK)], 12, at)

    def back_one_sib(at):
        sb2[pl.ds(at, BLOCK)] = dot(back_s[pl.ds(count + at, BLOCK)], n2_s[...]).astype(BF16)
        gn1_half(at).start()

    def back_one_mine(at):
        mid_s[pl.ds(at, BLOCK)] = dot(back_s[pl.ds(at, BLOCK)], n2_s[...])

    loop(count, BLOCK, back_one_sib)
    loop(count, BLOCK, back_one_mine)
    hook("e.0")
    mlp_copy.wait_send()

    def first_back(at):
        gn1_half(at).wait_recv()
        for off in range(0, BLOCK, 128):
            spot = pl.ds(aligned(at + off, 128), 128)
            xhat, sigma = norm_stats(sin_s[spot])
            grad = mid_s[spot] + rb2[spot].astype(F32)
            sb1[spot] = (gm_s[spot] + norm_back(grad, ln1_gain, xhat, sigma)).astype(BF16)
            late[0:1] += column_sum(grad * xhat)
            late[1:2] += column_sum(grad)

    loop(count, BLOCK, first_back)
    put_in = local(sb1, ing_h)
    last_small.start()
    hook("e.1")
    hook("tail")
    left = [first_small, last_small] + chunks
    while left:
        for item in left:
            item.advance()
            write_finished()
        left = [item for item in left if not item.finished]

    for row, source, at in ((0, late, 0), (1, late, 1), (2, early, 0), (3, early, 1), (4, early, 2), (5, early, 3), (8, early, 4), (9, late, 2), (10, late, 3)):
        small_o[row : row + 1] = source[at : at + 1]

    passed = [copy for item in pieces for copy in item.copies]
    for copy in [unit_copy, head_copy, n1_copy, cot_copy] + [gn1_half(at) for at in range(0, count, BLOCK)] + passed:
        copy.wait_send()
    for chunk in chunks:
        for copy in chunk.sent:
            copy.wait_send()
        chunk.done.wait()
    put_out.wait()
    put_in.wait()


def copies_of(full):
    most = 0
    for kind in ORDERS:
        first, after = KINDS[kind]
        most = max(most, 1 + full + 2 * sum((1 << len(bits)) - 1 for bits in after) + (0 if first is None else 3))
    return most


def call_layer(dp_size, tokens, cotangent, ids, table, vectors, wq, wo, w1, w2):
    count, width = tokens.shape
    rows = 2 * count
    quarter = wo.shape[0]
    units = w1.shape[1]
    heads = quarter // HEAD
    grad_rows = units + 4 * quarter
    parts = units // BLOCK
    bits = [b for b in range(20) if (1 << b) < dp_size]
    half_bits = bits[:3]
    shape = jax.ShapeDtypeStruct
    vm = pltpu.VMEM
    regions = 2 * (units // BLOCK) + 4
    steps = copies_of(len(bits) - len(half_bits))
    fetched = 4 + 2 * (units // BLOCK)
    scratch = (
        [vm((count, width), BF16), vm((rows, width), BF16)]
        + [vm((count, width), F32)] * 3
        + [vm((rows, width), BF16)] * 2
        + [vm((width, rows), BF16)]
        + [vm((2,) + wq.shape, BF16), vm((2 * quarter, width), BF16), vm((2, units // BLOCK, width, BLOCK), BF16), vm((2,) + w2.shape, BF16)]
        + [vm((2, rows, 256), BF16)] * 2
        + [vm((2 * quarter, rows), BF16)] * 5
        + [vm((8, rows), F32)] * 2
        + [vm((2 * heads, 2, count, count), BF16)]
        + [vm((rows, rows), BF16)] * 2
        + [vm((rows, width), BF16)]
        + [vm((rows, 2 * units), BF16)] * 2
        + [vm((count, width), BF16)] * 4
        + [vm((grad_rows, width), BF16)] * 3
        + [vm((7 * units // 8 + 4 * quarter, width), BF16), vm((units // 2, width), BF16)]
        + [vm((parts, width, BLOCK), BF16)] * 3
        + [vm((parts, 7 * width // 8, BLOCK), BF16), vm((parts, width // 2, BLOCK), BF16)]
        + [vm((grad_rows >> len(half_bits), width), BF16)] * (len(bits) - len(half_bits))
        + [vm((parts, width // 8, BLOCK), BF16)] * (len(bits) - len(half_bits))
        + [vm((units,), F32), vm((2, quarter), F32), vm((8, width), F32), vm((8, width), F32)]
        + [vm((6, 8, width), F32), vm((14 + 2 * (len(bits) - 3), 8, width), F32)]
        + [pltpu.SemaphoreType.DMA((8 + units // BLOCK + regions,))]
        + [pltpu.SemaphoreType.DMA((2, n)) for n in (3 * fetched + 2, 14, regions * steps, 2 * (10 + len(bits) - 3))]
    )
    anywhere = pl.BlockSpec(memory_space=pl.ANY)
    inside = pl.BlockSpec(memory_space=pltpu.VMEM)
    return pl.pallas_call(
        functools.partial(layer, dp_size, half_bits),
        out_shape=[shape((count, width), BF16)] * 2
        + [shape(w2.shape, BF16), shape(w1.shape, BF16), shape(wo.shape, BF16), shape(wq.shape, BF16), shape((16, width), F32)],
        in_specs=[anywhere] * 2 + [inside] * (2 + len(vectors)) + [anywhere] * 4,
        out_specs=[anywhere] * 6 + [inside],
        scratch_shapes=scratch,
        compiler_params=pltpu.CompilerParams(vmem_limit_bytes=VMEM_LIMIT, collective_id=0, has_side_effects=True),
        name="layer",
    )(tokens, cotangent, ids, table, *vectors, wq, wo, w1, w2)


def finish(*refs):
    sources, small, rest = refs[:6], refs[6], refs[7:]
    results, vectors, rest = rest[:6], rest[6:14], rest[14:]
    narrow, wide, (get, put) = rest[:6], rest[6:10], rest[10:]
    blocks = []
    for k, src in enumerate(sources):
        if src.ndim == 3:
            places = list(range(src.shape[0]))
        else:
            step = min(BLOCK, src.shape[0])
            places = [pl.ds(at, step) for at in range(0, src.shape[0], step)]
        for at in places:
            low = narrow[k].at[at]
            blocks.append((src.at[at], low, low if k < 2 else wide[k - 2].at[at], results[k].at[at]))
    reads = [pltpu.make_async_copy(src, low, get.at[n]) for n, (src, low, _, _) in enumerate(blocks)]
    writes = [pltpu.make_async_copy(high, dst, put.at[n]) for n, (_, _, high, dst) in enumerate(blocks)]
    for copy in reads:
        copy.start()
    for i in range(6):
        vectors[i][...] = small[i]
    vectors[6][...] = small[8, : vectors[6].shape[0]]
    vectors[7][...] = small[9:11, : vectors[7].shape[1]]
    for read, write, (_, low, high, _) in zip(reads, writes, blocks):
        read.wait()
        if high is not low:

            def cast(at, low=low, high=high):
                high[pl.ds(at, 64)] = low[pl.ds(at, 64)].astype(F32)

            loop(low.shape[0], 64, cast)
        write.start()
    for copy in writes:
        copy.wait()


def call_finish(arrays, small, units, quarter):
    width = small.shape[1]
    shape = jax.ShapeDtypeStruct
    extents = [(width,)] * 6 + [(units,), (2, quarter)]
    kinds = [BF16, BF16, F32, F32, F32, F32]
    anywhere = pl.BlockSpec(memory_space=pl.ANY)
    inside = pl.BlockSpec(memory_space=pltpu.VMEM)
    grads = arrays[2:]
    return pl.pallas_call(
        finish,
        in_specs=[anywhere] * len(arrays) + [inside],
        out_specs=[anywhere] * len(arrays) + [inside] * len(extents),
        out_shape=[shape(a.shape, k) for a, k in zip(arrays, kinds)] + [shape(e, F32) for e in extents],
        scratch_shapes=[pltpu.VMEM(a.shape, BF16) for a in arrays]
        + [pltpu.VMEM(a.shape, F32) for a in grads]
        + [pltpu.SemaphoreType.DMA((16,)), pltpu.SemaphoreType.DMA((16,))],
        compiler_params=pltpu.CompilerParams(vmem_limit_bytes=VMEM_LIMIT),
        name="finish",
    )(*arrays, small)


def per_device(
    tokens, segment_ids, ln1_gain, ln1_bias, qkv_weight, qv_bias, out_weight, out_bias,
    ln2_gain, ln2_bias, fc1_weight, fc1_bias, fc2_weight, fc2_bias, cotangent,
):
    width = tokens.shape[1]
    freq_count = width // 6
    frequency = 10000.0 ** (-jnp.arange(freq_count, dtype=F32) / freq_count)
    angles = jnp.arange(SIDE, dtype=F32)[:, None] * frequency[None, :]
    table = jnp.concatenate([jnp.sin(angles), jnp.cos(angles)], axis=1)
    vectors = (ln1_gain, ln1_bias, out_bias, ln2_gain, ln2_bias, fc2_bias, fc1_bias, qv_bias)
    *arrays, small = call_layer(
        lax.axis_size("dp"), tokens, cotangent, segment_ids, table, vectors, qkv_weight.transpose(0, 2, 1), out_weight, fc1_weight, fc2_weight
    )
    out, ing, g2, g1, go, gq, a0, a1, a2, a3, a4, a5, g_units, g_heads = call_finish(arrays, small, fc1_weight.shape[1], out_weight.shape[0])
    return (out, ing, a0, a1, gq.transpose(0, 2, 1), g_heads, go, a2, a3, a4, g1, g_units, g2, a5)


def solution(mesh):
    placed = (
        P(("dp", "tensor"), None),
        P("dp", None),
        P(),
        P(),
        P(None, None, "tensor"),
        P(None, "tensor"),
        P("tensor", None),
        P(),
        P(),
        P(),
        P(None, "tensor"),
        P("tensor"),
        P("tensor", None),
        P(),
        P(("dp", "tensor"), None),
    )
    return jax.shard_map(
        per_device,
        mesh=mesh,
        in_specs=placed,
        out_specs=(
            P(("dp", "tensor"), None),
            P(("dp", "tensor"), None),
            P(),
            P(),
            P(None, None, "tensor"),
            P(None, "tensor"),
            P("tensor", None),
            P(),
            P(),
            P(),
            P(None, "tensor"),
            P("tensor"),
            P("tensor", None),
            P(),
        ),
        check_vma=False,
    )
```

```python
import functools

import jax
import jax.numpy as jnp
from jax import lax
from jax.experimental import pallas as pl
from jax.experimental.pallas import tpu as pltpu
from jax.sharding import PartitionSpec as P

HEAD = 64
SIDE = 16
EPSILON = 1e-06
NEG_LARGE = -1e30
SCALE = HEAD ** (-0.5)
F32 = jnp.float32
BF16 = jnp.bfloat16
VMEM_LIMIT = 64 * 1024 * 1024 - 128 * 1024
MESH = pl.DeviceIdType.MESH
BLOCK = 256
KINDS = {
    "A": (None, ((0,), (1,), (2,))),
    "B": (None, ((1,), (0,), (2,))),
    "D": (None, ((0,), (1, 2))),
    "E": (None, ((0, 1, 2),)),
    "Y": (0, ((1,), (2,))),
    "Z": (1, ((0,), (2,))),
    "YD": (0, ((1, 2),)),
    "S": (None, (("p",), ("q",), (2,))),
    "SD": (None, (("p",), ("q", 2))),
    "SF": ("p", (("q",), (2,))),
    "SFD": ("p", (("q", 2),)),
}
ORDERS = ("SFD", "SD", "SFD", "SFD", "A", "SF", "D", "SD", "SD", "S")
WEIGHT_PLAN = {"p0": (0,), "a2": (1,), "p1": (3, 4), "c1": (5,), "o": (6,), "r10.0": (7,), "f10": (8,), "f00": (9,)}
PLAN = {
    "f01": (0, 1),
    "r02.0": (2,),
    "r02.1": (0,),
    "f02": (3,),
    "g0": (1,),
    "lb": (4, 0),
    "fo": (5, 2),
    "fin": (1, -1),
    "w1.0": (3, 4, 0),
    "w0.0": (5, 2),
    "v0": (1,),
    "b1.0": (6,),
    "b1.1": (-1, 4, 0, 9, 5, 3),
    "b0.0": (6, 1, 2),
    "b0.1": (4, 9, 5),
    "s0": (8,),
    "d.0": (3,),
    "d.1": (2, 6, 9),
    "e.0": (7, 4, 8),
    "e.1": (5, 3),
    "tail": (6, 9, -2, 7, 4, 6, 8, 5, 9, -2, 4, 7, 8, 5, 9, 7, 8, 9, 7),
}


def dot(a, b):
    return jnp.dot(a, b, preferred_element_type=F32)


def dot_nt(a, b):
    return lax.dot_general(a, b, (((1,), (1,)), ((), ())), preferred_element_type=F32)


def dot_tn(a, b):
    return lax.dot_general(a, b, (((0,), (0,)), ((), ())), preferred_element_type=F32)


def lane_half(rows, upper):
    lanes = lax.broadcasted_iota(jnp.int32, (rows, 128), 1)
    return lanes >= HEAD if upper else lanes < HEAD


def head_lanes(ref, head, filler):
    tile = ref[:, 128 * (head // 2) : 128 * (head // 2) + 128]
    return jnp.where(lane_half(tile.shape[0], head % 2 == 1), tile, filler)


def gelu_pair(h):
    cdf = 0.5 + 0.5 * lax.erf(h * 0.7071067811865476)
    return h * cdf, cdf + h * jnp.exp(-0.5 * h * h) * 0.3989422804014327


def norm_stats(v):
    centred = v - jnp.mean(v, axis=-1, keepdims=True)
    sigma = lax.rsqrt(jnp.mean(centred * centred, axis=-1, keepdims=True) + EPSILON)
    return centred * sigma, sigma


def norm_back(grad, gain, xhat, sigma):
    g = grad * gain
    return sigma * (g - jnp.mean(g, axis=-1, keepdims=True) - xhat * jnp.mean(g * xhat, axis=-1, keepdims=True))


def column_sum(v):
    return jnp.sum(v, axis=0, keepdims=True)


def aligned(v, unit):
    return v if isinstance(v, int) else pl.multiple_of(v, unit)


def loop(count, step, body, service=None, every=1):
    def run(i, carry):
        body(aligned(i * step, step))
        if service is not None:
            for k in range(count // step // every):
                if service(k, True):
                    pl.when(i == every * (k + 1) - 1)(functools.partial(service, k, False))
        return carry

    lax.fori_loop(0, count // step, run, 0)


def layer(
    dp_size, half_bits,
    tok_h, cot_h, ids, table, gain1, bias1, bias_o, gain2, bias2, bias_f, bias_u, bias_qv, wq_h, wo_h, w1_h, w2_h,
    out_h, ing_h, g2_h, g1_h, go_h, gq_h, small_o,
    tok_s, cot_s, sin_s, mid_s, gm_s, n1_s, n2_s, n2t_s, wq_s, wo_s, w1_s, w2_s,
    q_s, v_s, kt_s, ot_s, ou_s, gt_s, gr_s, r_s, in_s, e_s, roll_s, back_s, nr_s, a_s, g_s, sb1, sb2, rb1, rb2,
    own, oth, xr, land, land_both, own1, oth1, xr1, land1, land1_both, *rest,
):
    rest = list(rest)
    full_bits = [b for b in range(20) if (1 << b) < dp_size and b not in half_bits]
    rx = [rest.pop(0) for _ in full_bits]
    rx1 = [rest.pop(0) for _ in full_bits]
    uoth, voth, early, late, near, far, lsem, wsem, csem, gsem, ssem = rest

    count, width = tok_s.shape
    rows = 2 * count
    quarter = wo_h.shape[0]
    units = w1_h.shape[1]
    heads = quarter // HEAD
    place = lax.axis_index("tensor")
    dp = lax.axis_index("dp")
    chip = place // 2
    core = place % 2
    sib = {"tensor": chip * 2 + 1 - core}
    across = {"tensor": (1 - chip) * 2 + core}
    facing = {"tensor": (1 - chip) * 2 + 1 - core}
    all_bits = list(half_bits) + full_bits
    sides = {b: (dp // (1 << b)) % 2 for b in all_bits}

    ways = {b: (1 - 2 * sides[b]) * (1 << b) for b in all_bits}
    sides["p"] = sides[0] + (sides[1] - sides[0]) * core
    sides["q"] = sides[1] + (sides[0] - sides[1]) * core
    ways["p"] = ways[0] + (ways[1] - ways[0]) * core
    ways["q"] = ways[1] + (ways[0] - ways[1]) * core

    def mate(bits):
        return {"dp": dp + sum(ways[b] for b in bits)}

    def described(src, dst, sems, index, device):
        return pltpu.make_async_remote_copy(
            src_ref=src, dst_ref=dst, send_sem=sems.at[0, index], recv_sem=sems.at[1, index], device_id=device, device_id_type=MESH
        )

    mates = {b: mate((b,)) for b in all_bits}
    groups = {(b,) for b in full_bits}
    for mask in range(1, 1 << len(half_bits)):
        groups.add(tuple(b for k, b in enumerate(half_bits) if mask >> k & 1))

    barrier = pltpu.get_barrier_semaphore()
    partners = [sib, across, facing] + [mate(bits) for bits in sorted(groups)]
    for partner in partners:
        pl.semaphore_signal(barrier, inc=1, device_id=partner, device_id_type=MESH)

    sq_s, sk_s, k_s = a_s.at[:, 0:128], a_s.at[:, 128:256], a_s.at[:, 256:512]
    local_used = [0]

    def local(src, dst):
        copy = pltpu.make_async_copy(src, dst, lsem.at[local_used[0]])
        local_used[0] += 1
        copy.start()
        return copy

    def remote(src, dst, sems, index, device):
        copy = pltpu.make_async_remote_copy(
            src_ref=src, dst_ref=dst, send_sem=sems.at[0, index], recv_sem=sems.at[1, index], device_id=device, device_id_type=MESH
        )
        copy.start()
        return copy

    def half_copy(src, dst, first, at):
        return pltpu.make_async_remote_copy(
            src_ref=src,
            dst_ref=dst,
            send_sem=csem.at[0, first + at // BLOCK],
            recv_sem=csem.at[1, first + at // BLOCK],
            device_id=sib,
            device_id_type=MESH,
        )

    get_tok = local(tok_h, tok_s)
    get_cot = local(cot_h, cot_s.at[pl.ds(0, count)])
    get_wq = local(wq_h, wq_s.at[0])
    get_wo = local(wo_h, wo_s.at[pl.ds(0, quarter)])
    get_w1 = [local(w1_h.at[:, pl.ds(i * BLOCK, BLOCK)], w1_s.at[0, i]) for i in range(units // BLOCK)]
    get_w2 = local(w2_h, w2_s.at[0])

    ln1_gain, ln1_bias, out_bias, ln2_gain, ln2_bias, fc2_bias = (
        ref[...].reshape(1, width) for ref in (gain1, bias1, bias_o, gain2, bias2, bias_f)
    )
    get_tok.wait()

    def first_norm(at):
        plane = core * (count // (SIDE * SIDE)) + at // (SIDE * SIDE)
        line = (at // SIDE) % SIDE
        shape = (SIDE, width // 3)
        for k in range(4):
            spot = jnp.concatenate(
                [jnp.broadcast_to(table[pl.ds(plane, 1)], shape), jnp.broadcast_to(table[pl.ds(line + k, 1)], shape), table[...]], axis=1
            )
            span = pl.ds(aligned(at + k * SIDE, SIDE), SIDE)
            stream = tok_s[span].astype(F32) + spot
            sin_s[span] = stream
            xhat, _ = norm_stats(stream)
            n1_s[span] = (xhat * ln1_gain + ln1_bias).astype(BF16)

    loop(count, 4 * SIDE, first_norm)
    doc = ids[pl.ds(chip, 1), :]
    starts = [jnp.zeros((1, 1), F32)]
    starts += [jnp.sum(jnp.where(doc < v, 1.0, 0.0), axis=1, keepdims=True) for v in range(1, 4)]
    starts.append(jnp.full((1, 1), rows, F32))
    turn = jnp.zeros((1, 1), F32)
    for v in range(4):
        turn += jnp.where(starts[v + 1] - starts[v] == count, starts[v], 0.0)
    turn_here = turn - (core * count).astype(F32)

    def wrapped(v):
        v = jnp.where(v >= rows, v - rows, v)
        return jnp.where(v < 0, v + rows, v)

    def rotations(at):
        down = (lax.broadcasted_iota(jnp.int32, (64, rows), 0) + at).astype(F32)
        along = lax.broadcasted_iota(jnp.int32, (64, rows), 1).astype(F32)
        roll_s[pl.ds(at, 64)] = jnp.where(wrapped(down + turn_here) == along, 1.0, 0.0).astype(BF16)
        back_s[pl.ds(at, 64)] = jnp.where(wrapped(down - turn_here) == along, 1.0, 0.0).astype(BF16)
        where = wrapped((lax.broadcasted_iota(jnp.int32, (64, 128), 0) + at).astype(F32) + turn)
        mine = sum(jnp.where(where >= starts[v], 1.0, 0.0) for v in range(1, 4))
        slot = (lax.broadcasted_iota(jnp.int32, (64, 128), 1) % HEAD).astype(F32)
        sq_s[pl.ds(at, 64)] = jnp.where((slot < 4) & (slot != mine), 1.0, 0.0).astype(BF16)
        sk_s[pl.ds(at, 64)] = jnp.where(slot == mine, NEG_LARGE, 0.0).astype(BF16)


    pl.semaphore_wait(barrier, len(partners))
    unit_copy = remote(bias_u, uoth, wsem, 3 * (4 + 2 * (units // BLOCK)), across)
    head_copy = remote(bias_qv, voth, wsem, 3 * (4 + 2 * (units // BLOCK)) + 1, across)
    get_wq.wait()
    get_wo.wait()
    for copy in get_w1:
        copy.wait()
    get_w2.wait()

    part = (sides[0] + sides[1]) % 2

    class Piece:
        def __init__(self, index, refs, at, extent):
            size = extent // 4

            def some(k, first, size):
                return refs[k].at[pl.ds(aligned(at[k] + part * (extent // 2) + first, 16), size)]

            self.copies = [described(some(0, 0, 2 * size), some(1, 0, 2 * size), wsem, 3 * index, across)]
            for k in range(2):
                block = some(1, k * size, size)
                self.copies.append(described(block, block, wsem, 3 * index + 1 + k, mates[k]))
            self.stage = 0

        def advance(self):
            if self.stage == 0:
                self.copies[0].wait_recv()
                self.copies[1].start()
                self.copies[2].start()
            else:
                self.copies[1].wait_recv()
                self.copies[2].wait_recv()
            self.stage += 1

    pieces = [Piece(c, (wq_s.at[0, c], wq_s.at[1, c]), (0, 0), quarter) for c in range(3)]
    pieces.append(Piece(3, (wo_s, wo_s), (0, quarter), quarter))
    for i in range(units // BLOCK):
        pieces.append(Piece(4 + 2 * i, (w1_s.at[0, i], w1_s.at[1, i]), (0, 0), width))
        pieces.append(Piece(5 + 2 * i, (w2_s.at[0], w2_s.at[1]), (i * BLOCK, i * BLOCK), BLOCK))
    for item in pieces:
        item.copies[0].start()

    inside_loop = []

    def service(name, act):
        def at_point(k, ask):
            full = f"{name}{k}"
            if ask:
                return full in PLAN or full in WEIGHT_PLAN
            inside_loop.append(full)
            act(full)
            inside_loop.pop()

        return at_point

    def pass_on(name):
        for i in WEIGHT_PLAN.get(name, ()):
            if pieces[i].stage < 1:
                pieces[i].advance()

    def have_weight(*which):
        for i in which:
            while pieces[i].stage < 2:
                pieces[i].advance()

    n1_copy = remote(n1_s.at[pl.ds(0, count)], n1_s.at[pl.ds(count, count)], csem, 0, sib)
    get_cot.wait()
    cot_copy = remote(cot_s.at[pl.ds(0, count)], cot_s.at[pl.ds(count, count)], csem, 1, sib)

    def rotate(at):
        nr_s[pl.ds(at, BLOCK)] = dot(roll_s[pl.ds(at, BLOCK)], n1_s[...]).astype(BF16)

    def project(j, at):
        n = nr_s[pl.ds(at, BLOCK)]
        biases = bias_qv if j == 0 else voth
        q = (dot_nt(n, wq_s[j, 0]) + biases[0:1]).astype(BF16) * SCALE
        k = dot_nt(n, wq_s[j, 1]).astype(BF16)
        v = (dot_nt(n, wq_s[j, 2]) + biases[1:2]).astype(BF16)
        q_s[j, pl.ds(at, BLOCK), :quarter] = q
        k_s[pl.ds(at, BLOCK), :quarter] = k
        v_s[j, pl.ds(at, BLOCK), :quarter] = v
        kt_s[j * quarter : (j + 1) * quarter, pl.ds(at, BLOCK)] = k.T * SCALE

    blocks = [(b, at) for b in range(2) for at in range(0, count, BLOCK)]

    def attend(j):
        for head in range(heads):
            at = 512 + 256 * head
            a_s[:, at : at + 128] = head_lanes(q_s.at[j], head, sq_s[...])
            a_s[:, at + 128 : at + 256] = head_lanes(k_s, head, sk_s[...])
        for at in range(0, rows, BLOCK):
            ou_s[:quarter, at : at + BLOCK] = v_s[j, at : at + BLOCK, :quarter].T

        def tile(here):
            b = here // count
            at = aligned(here % count, BLOCK)
            keys = pl.ds(aligned(b * count, count), count)
            for head in range(heads):
                column = 512 + 256 * head
                s = dot_nt(a_s[keys, column + 128 : column + 256], a_s[pl.ds(here, BLOCK), column : column + 128])
                m = jnp.max(s, axis=0, keepdims=True)
                e = jnp.exp(s - m)
                r = 1.0 / column_sum(e)
                low = e.astype(BF16)
                span = slice(head * HEAD, head * HEAD + HEAD)
                to = slice(j * quarter + head * HEAD, j * quarter + head * HEAD + HEAD)
                e_s[j * heads + head, b, :, pl.ds(at, BLOCK)] = low
                ot_s[to, pl.ds(here, BLOCK)] = (dot(ou_s[span, keys], low) * r).astype(BF16)
                r_s[j * heads + head : j * heads + head + 1, pl.ds(here, BLOCK)] = r

        return tile

    loop(rows, 64, rotations)
    n1_copy.wait_recv()
    loop(rows, BLOCK, rotate)
    loop(rows, BLOCK, lambda at: project(0, at))
    pass_on("p0")
    loop(rows, BLOCK, attend(0), service("a", pass_on))
    head_copy.wait_recv()
    have_weight(0, 1, 2)
    loop(rows, BLOCK, lambda at: project(1, at))
    pass_on("p1")
    loop(rows, BLOCK, attend(1), service("c", pass_on))

    have_weight(3)

    def unrotate(at):
        ou_s[:, pl.ds(at, BLOCK)] = dot(ot_s[...], roll_s[:, pl.ds(at, BLOCK)]).astype(BF16)

    loop(rows, BLOCK, unrotate)
    pass_on("u")

    def out_part(at):
        return dot_tn(ou_s[:, pl.ds(at, BLOCK)], wo_s[...])

    def att_half(at):
        return half_copy(sb1.at[pl.ds(at, BLOCK)], rb1.at[pl.ds(at, BLOCK)], 2, at)

    def n2_half(at):
        return half_copy(n2_s.at[pl.ds(at, BLOCK)], n2_s.at[pl.ds(aligned(count + at, BLOCK), BLOCK)], 4, at)

    def out_sib(at):
        sb1[pl.ds(at, BLOCK)] = out_part(count + at).astype(BF16)
        att_half(at).start()

    loop(count, BLOCK, out_sib)

    def out_mine(at):
        mid_s[pl.ds(at, BLOCK)] = sin_s[pl.ds(at, BLOCK)] + out_part(at) + out_bias

    loop(count, BLOCK, out_mine)
    pass_on("o")

    def second_norm(at):
        att_half(at).wait_recv()
        for off in range(0, BLOCK, 128):
            spot = pl.ds(aligned(at + off, 128), 128)
            mid = mid_s[spot] + rb1[spot].astype(F32)
            mid_s[spot] = mid
            xhat, _ = norm_stats(mid)
            n2_s[spot] = (xhat * ln2_gain + ln2_bias).astype(BF16)
        n2_half(at).start()

    loop(count, BLOCK, second_norm)
    pass_on("n")

    base_a = units
    parts = units // BLOCK
    steps = copies_of(len(full_bits))

    class Region:
        def __init__(self, index, row, size, cols, slot, kind, refs, to):
            own_r, oth_r, xr_r, land_r, both_r, rx_r = refs
            self.place, self.slot, self.to, self.xr = (row, size, 0, cols), slot, to, xr_r
            first, after = KINDS[kind]
            self.first = first is not None
            self.stages, self.stage, self.finished, self.sent = [], -1, False, []
            now, parts, used, trail = self.place, 8, 0, []
            sems = iter(range(index * steps, (index + 1) * steps))

            def copy(src, src_at, dst, dst_at, device):
                return described(src.at[self.window(src_at)], dst.at[self.window(dst_at)], gsem, next(sems), device)

            def piece(bits, mask):
                where = now
                for k, b in enumerate(bits):
                    where = self.cut(where, 1 - sides[b] if mask >> k & 1 else sides[b])
                return where

            sums = 1 + len(after) + len(full_bits)
            if self.first:
                keep, give, there = piece((first,), 0), piece((first,), 1), (row // 2, size // 2, 0, cols)
                place = self.landing(0, 4)
                copies = [copy(own_r, give, land_r, place, mate((first,))), copy(oth_r, give, both_r, there, mate((first,)))]
                adds = [(own_r, own_r, keep, [(land_r, place)]), (oth_r, oth_r, keep, [(both_r, there)])]
                self.stages.append((copies, adds, False))
                trail.append(((first,), keep))
                now, parts, used = keep, 4, 4
            self.stages.append(([copy(oth_r, now, xr_r, now, across)], [(own_r, own_r, now, [(xr_r, now)])], False))
            for bits in after:
                parts >>= len(bits)
                keep, copies, terms = piece(bits, 0), [], []
                for mask in range(1, 1 << len(bits)):
                    place = self.landing(used, parts)
                    used += parts
                    terms.append((land_r, place))
                    copies.append(copy(own_r, piece(bits, mask), land_r, place, mate([b for k, b in enumerate(bits) if mask >> k & 1])))
                self.stages.append((copies, [(own_r, own_r, keep, terms)], False))
                trail.append((bits, keep))
                now = keep
            for i, b in enumerate(full_bits):
                place = self.small_place()
                self.stages.append(([copy(own_r, now, rx_r[i], place, mates[b])], [(own_r, own_r, now, [(rx_r[i], place)])], True))
            copies, adds, full = self.stages[-1]
            self.stages[-1] = (copies, [(xr_r,) + adds[0][1:]], full)
            for bits, keep in reversed(trail):
                copies = []
                for mask in range(1, 1 << len(bits)):
                    copies.append(copy(xr_r, keep, xr_r, keep, mate([b for k, b in enumerate(bits) if mask >> k & 1])))
                self.stages.append((copies, [], False))

        def window(self, where):
            row, size, col, cols = where
            return pl.ds(row, size), pl.ds(col, cols)

        def cut(self, where, side):
            row, size, col, cols = where
            if (size // 2) % 16 == 0:
                return aligned(row + side * (size // 2), 16), size // 2, col, cols
            return row, size, aligned(col + side * (cols // 2), 128), cols // 2

        def landing(self, at, parts_here):
            row, rows_one, cols_one = self.slot
            full = self.place[3]
            if cols_one == full:
                return row + at * rows_one, parts_here * rows_one, 0, full
            if parts_here == 1:
                return row + at // 2 * rows_one, rows_one, at % 2 * cols_one, cols_one
            return row + at // 2 * rows_one, parts_here // 2 * rows_one, 0, full

        def small_place(self):
            row, rows_one, cols_one = self.slot
            if cols_one == self.place[3]:
                return row // 7, rows_one, 0, cols_one
            k = (self.place[0] - base_a) // quarter
            return units // 8 + k // 2 * rows_one, rows_one, k % 2 * cols_one, cols_one

        def begin(self, copies):
            for copy in copies:
                copy.start()
            self.sent += copies

        def ready(self, j):
            if self.first:
                self.stage = 0
                self.begin([self.stages[0][0][j]])
            elif j == 1:
                self.stage = 0
                self.begin(self.stages[0][0])

        def add(self, into, base, where, terms):
            row, size, col, cols = where
            step = 64 if size % 64 == 0 else 48 if size % 48 == 0 else 32

            def body(off):
                to = (pl.ds(aligned(row + off, 16), step), pl.ds(col, cols))
                total = base[to].astype(F32)
                for ref, (r, _, c, _) in terms:
                    total += ref[pl.ds(aligned(r + off, 16), step), pl.ds(c, cols)].astype(F32)
                into[to] = total.astype(BF16)

            if inside_loop:
                for off in range(0, size, step):
                    body(off)
            else:
                loop(size, step, body)

        def advance(self):
            if self.finished or self.stage < 0:
                return
            copies, adds, full = self.stages[self.stage]
            for copy in copies:
                copy.wait_recv()
            if full:
                for copy in copies:
                    copy.wait_send()
                self.sent = [c for c in self.sent if all(c is not d for d in copies)]
            for item in adds:
                self.add(*item)
            self.stage += 1
            if self.stage < len(self.stages):
                self.begin(self.stages[self.stage][0])
                return
            self.finished = True
            to_write.append(self)

    chunks = []
    refs = (own, oth, xr, land, land_both, rx)
    for i in range(parts):
        slot = (i * 7 * (BLOCK // 8), BLOCK // 8, width)
        to = g2_h.at[pl.ds(i * BLOCK, BLOCK)]
        chunks.append(Region(2 * i, i * BLOCK, BLOCK, width, slot, ORDERS[2 * i], refs, to))
        refs_one = tuple(ref.at[i] for ref in (own1, oth1, xr1, land1, land1_both)) + ([ref.at[i] for ref in rx1],)
        to = g1_h.at[:, pl.ds(i * BLOCK, BLOCK)]
        chunks.append(Region(2 * i + 1, 0, width, BLOCK, (0, width // 8, BLOCK), ORDERS[2 * i + 1], refs_one, to))
    for i in range(4):
        slot = (7 * units // 8 + i * quarter, quarter // 4, width // 2)
        to = go_h if i == 0 else gq_h.at[i - 1]
        chunks.append(Region(2 * parts + i, base_a + i * quarter, quarter, width, slot, ORDERS[2 * parts + i], refs, to))
    first_att = 2 * parts

    class Small:
        def __init__(self, tile, index, everywhere, paired):
            self.tile, self.everywhere, self.paired = tile, everywhere, paired
            self.near = [near.at[3 * index + k] for k in range(3)]
            self.far = [far.at[(7 + len(full_bits)) * index + k] for k in range(7 + len(full_bits))]
            devices = [sib, across, facing]
            devices += [mate([b for k, b in enumerate(half_bits) if mask >> k & 1]) for mask in range(1, 8)]
            devices += [mates[b] for b in full_bits]
            base = index * len(devices)
            copies = [described(tile, dst, ssem, base + k, d) for k, (dst, d) in enumerate(zip(self.near + self.far, devices))]
            self.stages = [copies[:3], copies[3:10]] + [[copy] for copy in copies[10:]]
            self.stage, self.finished = -1, False

        def start(self):
            self.stage = 0
            for copy in self.stages[0]:
                copy.start()

        def advance(self):
            if self.finished or self.stage < 0:
                return
            for copy in self.stages[self.stage]:
                copy.wait()
            tile = self.tile
            if self.stage == 0:
                beside, over, facing_ = self.near
                n, p = self.everywhere, self.paired
                tile[0:n] = (tile[0:n] + beside[0:n]) + (over[0:n] + facing_[0:n])
                tile[n : n + p] = tile[n : n + p] + over[n + p : n + 2 * p]
            elif self.stage == 1:
                got = [tile] + self.far[:7]
                pairs = [got[2 * k][...] + got[2 * k + 1][...] for k in range(4)]
                tile[...] = (pairs[0] + pairs[1]) + (pairs[2] + pairs[3])
            else:
                tile[...] = tile[...] + self.far[5 + self.stage][...]
            self.stage += 1
            if self.stage == len(self.stages):
                self.finished = True
                return
            for copy in self.stages[self.stage]:
                copy.start()

    first_small = Small(early, 0, 4, 1)
    last_small = Small(late, 1, 2, 2)

    def ready(i, j):
        chunks[i].ready(j)

    to_write = []

    def write_finished():
        while to_write:
            region = to_write.pop()
            region.done = local(region.xr.at[region.window(region.place)], region.to)

    def hook(name):
        pass_on(name)
        for i in PLAN.get(name, ()):
            (chunks + [last_small, first_small])[i].advance()
            if not inside_loop:
                write_finished()

    def chunk_rows(j, i, at):
        span = pl.ds(at, BLOCK)
        cols = slice(j * units + i * BLOCK, j * units + (i + 1) * BLOCK)
        mine = slice(i * BLOCK, (i + 1) * BLOCK)
        bias = (bias_u if j == 0 else uoth)[mine].reshape(1, BLOCK)
        h = dot(n2_s[span], w1_s[j, i]) + bias
        a, slope = gelu_pair(h)
        a_s[span, cols] = a.astype(BF16)
        g = (dot_nt(cot_s[span], w2_s[j, mine]) * slope).astype(BF16)
        g_s[span, cols] = g

    def chunk_grads(j, i):
        cols = slice(j * units + i * BLOCK, j * units + (i + 1) * BLOCK)
        mine = slice(i * BLOCK, (i + 1) * BLOCK)
        to = oth if j == 1 else own

        def second(at):
            to[pl.ds(i * BLOCK + at, 128)] = dot_tn(a_s[:, pl.ds(cols.start + at, 128)], cot_s[...]).astype(BF16)

        loop(BLOCK, 128, second)
        ready(2 * i, j)
        g = g_s[:, cols]

        def first(at):
            (oth1 if j == 1 else own1)[i, pl.ds(at, BLOCK)] = dot(n2t_s[pl.ds(at, BLOCK)], g_s[:, cols]).astype(BF16)

        loop(width, BLOCK, first)
        ready(2 * i + 1, j)
        early[4 + j : 5 + j, mine] = column_sum(g.astype(F32))
        hook(f"f{j}{i}")

    def feed(j, i, first=False):
        if first:
            loop(count, BLOCK, lambda at: chunk_rows(j, i, at))
            hook(f"r{j}{i}.0")
            cot_copy.wait_recv()

            def received(at):
                n2_half(at).wait_recv()
                chunk_rows(j, i, count + at)

            loop(count, BLOCK, received)
            hook(f"r{j}{i}.1")

            def turned(at):
                n2t_s[:, pl.ds(at, BLOCK)] = n2_s[pl.ds(at, BLOCK)].T

            loop(rows, BLOCK, turned)
        else:
            loop(rows, BLOCK, lambda at: chunk_rows(j, i, at), service(f"r{j}{i}.", hook), 2)
        chunk_grads(j, i)

    early[...] = jnp.zeros_like(early)
    late[...] = jnp.zeros_like(late)
    unit_copy.wait_recv()
    for i in range(parts):
        have_weight(4 + 2 * i, 5 + 2 * i)
        feed(1, i, first=i == 0)
        feed(0, i)

    def back_two(at):
        span = pl.ds(at, BLOCK)
        total = None
        for j in range(2):
            for i in range(parts):
                at_col = j * units + i * BLOCK
                term = dot_nt(g_s[span, at_col : at_col + BLOCK], w1_s[j, i])
                total = term if total is None else total + term
        return total

    def mlp_part(at):
        span = pl.ds(at, BLOCK)
        return dot(a_s[span, :units], w2_s[0]) + dot(a_s[span, units:], w2_s[1])

    def gn2_half(at):
        return half_copy(sb2.at[pl.ds(at, BLOCK)], rb2.at[pl.ds(at, BLOCK)], 6, at)

    def dm_half(at):
        return half_copy(n2_s.at[pl.ds(at, BLOCK)], n2_s.at[pl.ds(aligned(count + at, BLOCK), BLOCK)], 10, at)

    def back_two_sib(at):
        sb2[pl.ds(at, BLOCK)] = back_two(count + at).astype(BF16)
        gn2_half(at).start()

    def back_two_mine(at):
        gm_s[pl.ds(at, BLOCK)] = back_two(at)

    def mlp_sib(at):
        sb1[pl.ds(at, BLOCK)] = mlp_part(count + at).astype(BF16)

    loop(count, BLOCK, back_two_sib)
    hook("g0")
    loop(count, BLOCK, back_two_mine)
    hook("gn2")

    def second_back(at):
        gn2_half(at).wait_recv()
        n2_half(at).wait_send()
        for off in range(0, BLOCK, 128):
            spot = pl.ds(aligned(at + off, 128), 128)
            xhat, sigma = norm_stats(mid_s[spot])
            grad = gm_s[spot] + rb2[spot].astype(F32)
            cot = cot_s[spot].astype(F32)
            back = cot + norm_back(grad, ln2_gain, xhat, sigma)
            gm_s[spot] = back
            n2_s[spot] = back.astype(BF16)
            early[0:1] += column_sum(back)
            early[1:2] += column_sum(grad * xhat)
            early[2:3] += column_sum(grad)
            early[3:4] += column_sum(cot)
        dm_half(at).start()

    loop(count, BLOCK, second_back)
    hook("lb")
    for at in range(0, count, BLOCK):
        att_half(at).wait_send()
    loop(count, BLOCK, mlp_sib)
    mlp_copy = remote(sb1, rb1, csem, 8, sib)
    first_small.start()
    hook("ln2")

    def finish_out(at):
        span = pl.ds(at, BLOCK)
        mid_s[span] = mid_s[span] + mlp_part(at) + fc2_bias

    loop(count, BLOCK, finish_out)
    hook("fo")
    mlp_copy.wait_recv()

    def write_out(at):
        spot = pl.ds(at, 128)
        tok_s[spot] = (mid_s[spot] + rb1[spot].astype(F32)).astype(BF16)

    loop(count, 128, write_out)
    put_out = local(tok_s, out_h)
    hook("fin")
    for at in range(0, count, BLOCK):
        dm_half(at).wait_recv()

    start = base_a + quarter
    zero = jnp.zeros((count, 128), BF16)
    grad_s = dq_s = gr_s

    def keep_gradient(j, c):
        to = oth if j == 1 else own
        low = start + c * quarter
        dt = ot_s.at[j * quarter : (j + 1) * quarter]

        def columns(at):
            to[low : low + quarter, pl.ds(at, BLOCK)] = dot(dt[...], nr_s[:, pl.ds(at, BLOCK)]).astype(BF16)

        loop(width, BLOCK, columns)
        ready(first_att + 1 + c, j)
        if c != 1:
            d = g_s[:, (3 * j + c) * BLOCK : (3 * j + c) * BLOCK + quarter]
            late[2 + c // 2 + 2 * j : 3 + c // 2 + 2 * j, :quarter] = column_sum(d.astype(F32))

    def values_back(j):
        base = j * quarter
        to = oth if j == 1 else own

        def weight(at):
            to[base_a : base_a + quarter, pl.ds(at, BLOCK)] = dot(ou_s[base : base + quarter], n2_s[:, pl.ds(at, BLOCK)]).astype(BF16)

        loop(width, BLOCK, weight)
        ready(first_att, j)

        def output(at):
            grad_s[base : base + quarter, pl.ds(at, BLOCK)] = dot_nt(wo_s[base : base + quarter], n2_s[pl.ds(at, BLOCK)]).astype(BF16)

        loop(rows, BLOCK, output)
        hook(f"w{j}.0")
        go_s = a_s.at[:, rows + 256 * j : rows + 256 * (j + 1)]

        def scale(at):
            here = pl.ds(at, BLOCK)
            grad_t = dot_nt(grad_s[base : base + quarter], roll_s[here])
            for head in range(heads):
                row = j * heads + head
                r = r_s[row : row + 1, here]
                g = grad_t[head * HEAD : (head + 1) * HEAD]
                at_head = slice(base + head * HEAD, base + (head + 1) * HEAD)
                in_s[row : row + 1, here] = column_sum(g * ot_s[at_head, here].astype(F32)) * r
                gt_s[at_head, here] = (g * r).astype(BF16)
            go_s[here, :quarter] = gt_s[base : base + quarter, here].T

        loop(rows, BLOCK, scale)

        def block(at):
            here = pl.ds(at, count)
            b = at // count
            dv = [None, None]
            for head in range(heads):
                tile = head // 2
                gh = jnp.where(lane_half(count, head % 2 == 1), go_s[here, 128 * tile : 128 * tile + 128], zero)
                part = dot(e_s[j * heads + head, b], gh)
                dv[tile] = part if dv[tile] is None else dv[tile] + part
            dv = jnp.concatenate(dv, axis=1)[:, :quarter].astype(BF16)
            g_s[here, (3 * j + 2) * BLOCK : (3 * j + 2) * BLOCK + quarter] = dv
            ot_s[base : base + quarter, here] = dv.T

        loop(rows, count, block)
        hook(f"w{j}.1")
        keep_gradient(j, 2)
        hook(f"v{j}")

    def scores_back(j):
        base = j * quarter

        def block(at):
            here = pl.ds(at, count)
            b = at // count
            dk = [None, None]
            for head in range(heads):
                tile = head // 2
                row = j * heads + head
                half = lane_half(count, head % 2 == 1)
                lanes = slice(128 * tile, 128 * tile + 128)
                vh = jnp.where(half, v_s[j, here, lanes], zero)
                qh = jnp.where(half, q_s[j, here, lanes], zero)
                last_row = min(128 * tile + 128, quarter)
                vh = vh[:, : last_row - 128 * tile]
                ds = a_s.at[:count, head * count : (head + 1) * count] if head < 2 else a_s.at[count:, :count]
                for off in range(0, count, BLOCK):
                    some = pl.ds(aligned(at + off, BLOCK), BLOCK)
                    dp_t = dot(vh, gt_s[base + 128 * tile : base + last_row, some])
                    grad = (dp_t - in_s[row : row + 1, some]) * e_s[row, b, :, off : off + BLOCK].astype(F32)
                    ds[:, off : off + BLOCK] = grad.astype(BF16)
                part = dot(ds[...], qh)
                dk[tile] = part if dk[tile] is None else dk[tile] + part
                kth = kt_s[base + head * HEAD : base + head * HEAD + HEAD, here]
                dq_s[base + head * HEAD : base + head * HEAD + HEAD, here] = dot(kth, ds[...]).astype(BF16)
            dk = jnp.concatenate(dk, axis=1)[:, :quarter].astype(BF16)
            g_s[here, (3 * j + 1) * BLOCK : (3 * j + 1) * BLOCK + quarter] = dk
            ot_s[base : base + quarter, here] = dk.T
            g_s[here, 3 * j * BLOCK : 3 * j * BLOCK + quarter] = dq_s[base : base + quarter, here].T

        loop(rows, count, block, service(f"b{j}.", hook))
        keep_gradient(j, 1)
        hook(f"k{j}")
        ot_s[base : base + quarter] = dq_s[base : base + quarter]
        keep_gradient(j, 0)
        hook(f"s{j}")

    values_back(1)
    values_back(0)
    scores_back(1)
    scores_back(0)

    def back_one(at):
        total = None
        for j in range(2):
            for c in range(3):
                d = g_s[pl.ds(at, BLOCK), (3 * j + c) * BLOCK : (3 * j + c) * BLOCK + quarter]
                term = dot(d, wq_s[j, c])
                total = term if total is None else total + term
        n2_s[pl.ds(at, BLOCK)] = total.astype(BF16)

    for at in range(0, count, BLOCK):
        dm_half(at).wait_send()
    loop(rows, BLOCK, back_one, service("d.", hook), 2)
    for at in range(0, count, BLOCK):
        gn2_half(at).wait_send()

    def gn1_half(at):
        return half_copy(sb2.at[pl.ds(at, BLOCK)], rb2.at[pl.ds(at, BLOCK)], 12, at)

    def back_one_sib(at):
        sb2[pl.ds(at, BLOCK)] = dot(back_s[pl.ds(count + at, BLOCK)], n2_s[...]).astype(BF16)
        gn1_half(at).start()

    def back_one_mine(at):
        mid_s[pl.ds(at, BLOCK)] = dot(back_s[pl.ds(at, BLOCK)], n2_s[...])

    loop(count, BLOCK, back_one_sib)
    loop(count, BLOCK, back_one_mine)
    hook("e.0")
    mlp_copy.wait_send()

    def first_back(at):
        gn1_half(at).wait_recv()
        for off in range(0, BLOCK, 128):
            spot = pl.ds(aligned(at + off, 128), 128)
            xhat, sigma = norm_stats(sin_s[spot])
            grad = mid_s[spot] + rb2[spot].astype(F32)
            sb1[spot] = (gm_s[spot] + norm_back(grad, ln1_gain, xhat, sigma)).astype(BF16)
            late[0:1] += column_sum(grad * xhat)
            late[1:2] += column_sum(grad)

    loop(count, BLOCK, first_back)
    put_in = local(sb1, ing_h)
    last_small.start()
    hook("e.1")
    hook("tail")
    left = [first_small, last_small] + chunks
    while left:
        for item in left:
            item.advance()
            write_finished()
        left = [item for item in left if not item.finished]

    for row, source, at in ((0, late, 0), (1, late, 1), (2, early, 0), (3, early, 1), (4, early, 2), (5, early, 3), (8, early, 4), (9, late, 2), (10, late, 3)):
        small_o[row : row + 1] = source[at : at + 1]

    passed = [copy for item in pieces for copy in item.copies]
    for copy in [unit_copy, head_copy, n1_copy, cot_copy] + [gn1_half(at) for at in range(0, count, BLOCK)] + passed:
        copy.wait_send()
    for chunk in chunks:
        for copy in chunk.sent:
            copy.wait_send()
        chunk.done.wait()
    put_out.wait()
    put_in.wait()


def copies_of(full):
    most = 0
    for kind in ORDERS:
        first, after = KINDS[kind]
        most = max(most, 1 + full + 2 * sum((1 << len(bits)) - 1 for bits in after) + (0 if first is None else 3))
    return most


def call_layer(dp_size, tokens, cotangent, ids, table, vectors, wq, wo, w1, w2):
    count, width = tokens.shape
    rows = 2 * count
    quarter = wo.shape[0]
    units = w1.shape[1]
    heads = quarter // HEAD
    grad_rows = units + 4 * quarter
    parts = units // BLOCK
    bits = [b for b in range(20) if (1 << b) < dp_size]
    half_bits = bits[:3]
    shape = jax.ShapeDtypeStruct
    vm = pltpu.VMEM
    regions = 2 * (units // BLOCK) + 4
    steps = copies_of(len(bits) - len(half_bits))
    fetched = 4 + 2 * (units // BLOCK)
    scratch = (
        [vm((count, width), BF16), vm((rows, width), BF16)]
        + [vm((count, width), F32)] * 3
        + [vm((rows, width), BF16)] * 2
        + [vm((width, rows), BF16)]
        + [vm((2,) + wq.shape, BF16), vm((2 * quarter, width), BF16), vm((2, units // BLOCK, width, BLOCK), BF16), vm((2,) + w2.shape, BF16)]
        + [vm((2, rows, 256), BF16)] * 2
        + [vm((2 * quarter, rows), BF16)] * 5
        + [vm((8, rows), F32)] * 2
        + [vm((2 * heads, 2, count, count), BF16)]
        + [vm((rows, rows), BF16)] * 2
        + [vm((rows, width), BF16)]
        + [vm((rows, 2 * units), BF16)] * 2
        + [vm((count, width), BF16)] * 4
        + [vm((grad_rows, width), BF16)] * 3
        + [vm((7 * units // 8 + 4 * quarter, width), BF16), vm((units // 2, width), BF16)]
        + [vm((parts, width, BLOCK), BF16)] * 3
        + [vm((parts, 7 * width // 8, BLOCK), BF16), vm((parts, width // 2, BLOCK), BF16)]
        + [vm((grad_rows >> len(half_bits), width), BF16)] * (len(bits) - len(half_bits))
        + [vm((parts, width // 8, BLOCK), BF16)] * (len(bits) - len(half_bits))
        + [vm((units,), F32), vm((2, quarter), F32), vm((8, width), F32), vm((8, width), F32)]
        + [vm((6, 8, width), F32), vm((14 + 2 * (len(bits) - 3), 8, width), F32)]
        + [pltpu.SemaphoreType.DMA((8 + units // BLOCK + regions,))]
        + [pltpu.SemaphoreType.DMA((2, n)) for n in (3 * fetched + 2, 14, regions * steps, 2 * (10 + len(bits) - 3))]
    )
    anywhere = pl.BlockSpec(memory_space=pl.ANY)
    inside = pl.BlockSpec(memory_space=pltpu.VMEM)
    return pl.pallas_call(
        functools.partial(layer, dp_size, half_bits),
        out_shape=[shape((count, width), BF16)] * 2
        + [shape(w2.shape, BF16), shape(w1.shape, BF16), shape(wo.shape, BF16), shape(wq.shape, BF16), shape((16, width), F32)],
        in_specs=[anywhere] * 2 + [inside] * (2 + len(vectors)) + [anywhere] * 4,
        out_specs=[anywhere] * 6 + [inside],
        scratch_shapes=scratch,
        compiler_params=pltpu.CompilerParams(vmem_limit_bytes=VMEM_LIMIT, collective_id=0, has_side_effects=True),
        name="layer",
    )(tokens, cotangent, ids, table, *vectors, wq, wo, w1, w2)


def finish(*refs):
    sources, small, rest = refs[:6], refs[6], refs[7:]
    results, vectors, rest = rest[:6], rest[6:14], rest[14:]
    narrow, wide, (get, put) = rest[:6], rest[6:10], rest[10:]
    blocks = []
    for k, src in enumerate(sources):
        if src.ndim == 3:
            places = list(range(src.shape[0]))
        else:
            step = min(BLOCK, src.shape[0])
            places = [pl.ds(at, step) for at in range(0, src.shape[0], step)]
        for at in places:
            low = narrow[k].at[at]
            blocks.append((src.at[at], low, low if k < 2 else wide[k - 2].at[at], results[k].at[at]))
    reads = [pltpu.make_async_copy(src, low, get.at[n]) for n, (src, low, _, _) in enumerate(blocks)]
    writes = [pltpu.make_async_copy(high, dst, put.at[n]) for n, (_, _, high, dst) in enumerate(blocks)]
    for copy in reads:
        copy.start()
    for i in range(6):
        vectors[i][...] = small[i]
    vectors[6][...] = small[8, : vectors[6].shape[0]]
    vectors[7][...] = small[9:11, : vectors[7].shape[1]]
    for read, write, (_, low, high, _) in zip(reads, writes, blocks):
        read.wait()
        if high is not low:

            def cast(at, low=low, high=high):
                high[pl.ds(at, 64)] = low[pl.ds(at, 64)].astype(F32)

            loop(low.shape[0], 64, cast)
        write.start()
    for copy in writes:
        copy.wait()


def call_finish(arrays, small, units, quarter):
    width = small.shape[1]
    shape = jax.ShapeDtypeStruct
    extents = [(width,)] * 6 + [(units,), (2, quarter)]
    kinds = [BF16, BF16, F32, F32, F32, F32]
    anywhere = pl.BlockSpec(memory_space=pl.ANY)
    inside = pl.BlockSpec(memory_space=pltpu.VMEM)
    grads = arrays[2:]
    return pl.pallas_call(
        finish,
        in_specs=[anywhere] * len(arrays) + [inside],
        out_specs=[anywhere] * len(arrays) + [inside] * len(extents),
        out_shape=[shape(a.shape, k) for a, k in zip(arrays, kinds)] + [shape(e, F32) for e in extents],
        scratch_shapes=[pltpu.VMEM(a.shape, BF16) for a in arrays]
        + [pltpu.VMEM(a.shape, F32) for a in grads]
        + [pltpu.SemaphoreType.DMA((16,)), pltpu.SemaphoreType.DMA((16,))],
        compiler_params=pltpu.CompilerParams(vmem_limit_bytes=VMEM_LIMIT),
        name="finish",
    )(*arrays, small)


def per_device(
    tokens, segment_ids, ln1_gain, ln1_bias, qkv_weight, qv_bias, out_weight, out_bias,
    ln2_gain, ln2_bias, fc1_weight, fc1_bias, fc2_weight, fc2_bias, cotangent,
):
    width = tokens.shape[1]
    freq_count = width // 6
    frequency = 10000.0 ** (-jnp.arange(freq_count, dtype=F32) / freq_count)
    angles = jnp.arange(SIDE, dtype=F32)[:, None] * frequency[None, :]
    table = jnp.concatenate([jnp.sin(angles), jnp.cos(angles)], axis=1)
    vectors = (ln1_gain, ln1_bias, out_bias, ln2_gain, ln2_bias, fc2_bias, fc1_bias, qv_bias)
    *arrays, small = call_layer(
        lax.axis_size("dp"), tokens, cotangent, segment_ids, table, vectors, qkv_weight.transpose(0, 2, 1), out_weight, fc1_weight, fc2_weight
    )
    out, ing, g2, g1, go, gq, a0, a1, a2, a3, a4, a5, g_units, g_heads = call_finish(arrays, small, fc1_weight.shape[1], out_weight.shape[0])
    return (out, ing, a0, a1, gq.transpose(0, 2, 1), g_heads, go, a2, a3, a4, g1, g_units, g2, a5)


def solution(mesh):
    placed = (
        P(("dp", "tensor"), None),
        P("dp", None),
        P(),
        P(),
        P(None, None, "tensor"),
        P(None, "tensor"),
        P("tensor", None),
        P(),
        P(),
        P(),
        P(None, "tensor"),
        P("tensor"),
        P("tensor", None),
        P(),
        P(("dp", "tensor"), None),
    )
    return jax.shard_map(
        per_device,
        mesh=mesh,
        in_specs=placed,
        out_specs=(
            P(("dp", "tensor"), None),
            P(("dp", "tensor"), None),
            P(),
            P(),
            P(None, None, "tensor"),
            P(None, "tensor"),
            P("tensor", None),
            P(),
            P(),
            P(),
            P(None, "tensor"),
            P("tensor"),
            P("tensor", None),
            P(),
        ),
        check_vma=False,
    )
```

```python
import functools

import jax
import jax.numpy as jnp
from jax import lax
from jax.experimental import pallas as pl
from jax.experimental.pallas import tpu as pltpu
from jax.sharding import PartitionSpec as P

HEAD = 64
SIDE = 16
EPSILON = 1e-06
NEG_LARGE = -1e30
SCALE = HEAD ** (-0.5)
F32 = jnp.float32
BF16 = jnp.bfloat16
VMEM_LIMIT = 64 * 1024 * 1024 - 128 * 1024
MESH = pl.DeviceIdType.MESH
BLOCK = 256
KINDS = {
    "A": (None, ((0,), (1,), (2,))),
    "B": (None, ((1,), (0,), (2,))),
    "D": (None, ((0,), (1, 2))),
    "E": (None, ((0, 1, 2),)),
    "C": (None, ((0, 1), (2,))),
    "Y": (0, ((1,), (2,))),
    "Z": (1, ((0,), (2,))),
    "YD": (0, ((1, 2),)),
    "S": (None, (("p",), ("q",), (2,))),
    "SD": (None, (("p",), ("q", 2))),
    "SF": ("p", (("q",), (2,))),
    "SFD": ("p", (("q", 2),)),
}
ORDERS = ("E", "SFD", "YD", "D", "SF", "A", "D", "SD", "C", "S")
WEIGHT_PLAN = {"p0": (0,), "a2": (1,), "p1": (3, 4), "c1": (5,), "o": (6,), "r10.0": (7,), "f10": (8,), "f00": (9,)}
PLAN = {
    "f01": (1, 0),
    "f02": (3, 2),
    "g0": (1,),
    "lb": (0,),
    "fo": (4,),
    "fin": (5, -1),
    "w1.0": (3, 1, 2),
    "w0.0": (4, 0),
    "w0.1": (5, -1),
    "v0": (3,),
    "b1.0": (6, 1),
    "b1.1": (4, 5, -1, 9, 2),
    "b0.0": (6, 3, 1, 4),
    "b0.1": (5, 9, -1),
    "s0": (8,),
    "d.0": (2, 3),
    "d.1": (6, 9),
    "e.0": (7, 4, 8, 5),
    "tail": (2, 6, 7, 9, -2, 4, 8, 5, 6, 7, 9, 4, -2, 8, 5, 9, 7, 8, 9, 7),
}


def dot(a, b):
    return jnp.dot(a, b, preferred_element_type=F32)


def dot_nt(a, b):
    return lax.dot_general(a, b, (((1,), (1,)), ((), ())), preferred_element_type=F32)


def dot_tn(a, b):
    return lax.dot_general(a, b, (((0,), (0,)), ((), ())), preferred_element_type=F32)


def lane_half(rows, upper):
    lanes = lax.broadcasted_iota(jnp.int32, (rows, 128), 1)
    return lanes >= HEAD if upper else lanes < HEAD


def head_lanes(ref, head, filler):
    tile = ref[:, 128 * (head // 2) : 128 * (head // 2) + 128]
    return jnp.where(lane_half(tile.shape[0], head % 2 == 1), tile, filler)


def gelu_pair(h):
    cdf = 0.5 + 0.5 * lax.erf(h * 0.7071067811865476)
    return h * cdf, cdf + h * jnp.exp(-0.5 * h * h) * 0.3989422804014327


def norm_stats(v):
    centred = v - jnp.mean(v, axis=-1, keepdims=True)
    sigma = lax.rsqrt(jnp.mean(centred * centred, axis=-1, keepdims=True) + EPSILON)
    return centred * sigma, sigma


def norm_back(grad, gain, xhat, sigma):
    g = grad * gain
    return sigma * (g - jnp.mean(g, axis=-1, keepdims=True) - xhat * jnp.mean(g * xhat, axis=-1, keepdims=True))


def column_sum(v):
    return jnp.sum(v, axis=0, keepdims=True)


def aligned(v, unit):
    return v if isinstance(v, int) else pl.multiple_of(v, unit)


def loop(count, step, body, service=None, every=1):
    def run(i, carry):
        body(aligned(i * step, step))
        if service is not None:
            for k in range(count // step // every):
                if service(k, True):
                    pl.when(i == every * (k + 1) - 1)(functools.partial(service, k, False))
        return carry

    lax.fori_loop(0, count // step, run, 0)


def layer(
    dp_size, half_bits,
    tok_h, cot_h, ids, table, gain1, bias1, bias_o, gain2, bias2, bias_f, bias_u, bias_qv, wq_h, wo_h, w1_h, w2_h,
    out_h, ing_h, g2_h, g1_h, go_h, gq_h, small_o,
    tok_s, cot_s, sin_s, mid_s, gm_s, n1_s, n2_s, n2t_s, wq_s, wo_s, w1_s, w2_s,
    q_s, v_s, kt_s, ot_s, ou_s, gt_s, gr_s, r_s, in_s, e_s, roll_s, back_s, nr_s, a_s, g_s, sb1, sb2, rb1, rb2,
    own, oth, xr, land, land_both, own1, oth1, xr1, land1, land1_both, *rest,
):
    rest = list(rest)
    full_bits = [b for b in range(20) if (1 << b) < dp_size and b not in half_bits]
    rx = [rest.pop(0) for _ in full_bits]
    rx1 = [rest.pop(0) for _ in full_bits]
    uoth, voth, early, late, near, far, lsem, wsem, csem, gsem, ssem = rest

    count, width = tok_s.shape
    rows = 2 * count
    quarter = wo_h.shape[0]
    units = w1_h.shape[1]
    heads = quarter // HEAD
    place = lax.axis_index("tensor")
    dp = lax.axis_index("dp")
    chip = place // 2
    core = place % 2
    sib = {"tensor": chip * 2 + 1 - core}
    across = {"tensor": (1 - chip) * 2 + core}
    facing = {"tensor": (1 - chip) * 2 + 1 - core}
    all_bits = list(half_bits) + full_bits
    sides = {b: (dp // (1 << b)) % 2 for b in all_bits}

    ways = {b: (1 - 2 * sides[b]) * (1 << b) for b in all_bits}
    sides["p"] = sides[0] + (sides[1] - sides[0]) * core
    sides["q"] = sides[1] + (sides[0] - sides[1]) * core
    ways["p"] = ways[0] + (ways[1] - ways[0]) * core
    ways["q"] = ways[1] + (ways[0] - ways[1]) * core

    def mate(bits):
        return {"dp": dp + sum(ways[b] for b in bits)}

    def described(src, dst, sems, index, device):
        return pltpu.make_async_remote_copy(
            src_ref=src, dst_ref=dst, send_sem=sems.at[0, index], recv_sem=sems.at[1, index], device_id=device, device_id_type=MESH
        )

    mates = {b: mate((b,)) for b in all_bits}
    groups = {(b,) for b in full_bits}
    for mask in range(1, 1 << len(half_bits)):
        groups.add(tuple(b for k, b in enumerate(half_bits) if mask >> k & 1))

    barrier = pltpu.get_barrier_semaphore()
    partners = [sib, across, facing] + [mate(bits) for bits in sorted(groups)]
    for partner in partners:
        pl.semaphore_signal(barrier, inc=1, device_id=partner, device_id_type=MESH)

    sq_s, sk_s, k_s = a_s.at[:, 0:128], a_s.at[:, 128:256], a_s.at[:, 256:512]
    local_used = [0]

    def local(src, dst):
        copy = pltpu.make_async_copy(src, dst, lsem.at[local_used[0]])
        local_used[0] += 1
        copy.start()
        return copy

    def remote(src, dst, sems, index, device):
        copy = pltpu.make_async_remote_copy(
            src_ref=src, dst_ref=dst, send_sem=sems.at[0, index], recv_sem=sems.at[1, index], device_id=device, device_id_type=MESH
        )
        copy.start()
        return copy

    def half_copy(src, dst, first, at):
        return pltpu.make_async_remote_copy(
            src_ref=src,
            dst_ref=dst,
            send_sem=csem.at[0, first + at // BLOCK],
            recv_sem=csem.at[1, first + at // BLOCK],
            device_id=sib,
            device_id_type=MESH,
        )

    get_tok = local(tok_h, tok_s)
    get_cot = local(cot_h, cot_s.at[pl.ds(0, count)])
    get_wq = local(wq_h, wq_s.at[0])
    get_wo = local(wo_h, wo_s.at[pl.ds(0, quarter)])
    get_w1 = [local(w1_h.at[:, pl.ds(i * BLOCK, BLOCK)], w1_s.at[0, i]) for i in range(units // BLOCK)]
    get_w2 = local(w2_h, w2_s.at[0])

    ln1_gain, ln1_bias, out_bias, ln2_gain, ln2_bias, fc2_bias = (
        ref[...].reshape(1, width) for ref in (gain1, bias1, bias_o, gain2, bias2, bias_f)
    )
    get_tok.wait()

    def first_norm(at):
        plane = core * (count // (SIDE * SIDE)) + at // (SIDE * SIDE)
        line = (at // SIDE) % SIDE
        shape = (SIDE, width // 3)
        for k in range(4):
            spot = jnp.concatenate(
                [jnp.broadcast_to(table[pl.ds(plane, 1)], shape), jnp.broadcast_to(table[pl.ds(line + k, 1)], shape), table[...]], axis=1
            )
            span = pl.ds(aligned(at + k * SIDE, SIDE), SIDE)
            stream = tok_s[span].astype(F32) + spot
            sin_s[span] = stream
            xhat, _ = norm_stats(stream)
            n1_s[span] = (xhat * ln1_gain + ln1_bias).astype(BF16)

    loop(count, 4 * SIDE, first_norm)
    doc = ids[pl.ds(chip, 1), :]
    starts = [jnp.zeros((1, 1), F32)]
    starts += [jnp.sum(jnp.where(doc < v, 1.0, 0.0), axis=1, keepdims=True) for v in range(1, 4)]
    starts.append(jnp.full((1, 1), rows, F32))
    turn = jnp.zeros((1, 1), F32)
    for v in range(4):
        turn += jnp.where(starts[v + 1] - starts[v] == count, starts[v], 0.0)
    turn_here = turn - (core * count).astype(F32)

    def wrapped(v):
        v = jnp.where(v >= rows, v - rows, v)
        return jnp.where(v < 0, v + rows, v)

    def rotations(at):
        down = (lax.broadcasted_iota(jnp.int32, (64, rows), 0) + at).astype(F32)
        along = lax.broadcasted_iota(jnp.int32, (64, rows), 1).astype(F32)
        roll_s[pl.ds(at, 64)] = jnp.where(wrapped(down + turn_here) == along, 1.0, 0.0).astype(BF16)
        back_s[pl.ds(at, 64)] = jnp.where(wrapped(down - turn_here) == along, 1.0, 0.0).astype(BF16)
        where = wrapped((lax.broadcasted_iota(jnp.int32, (64, 128), 0) + at).astype(F32) + turn)
        mine = sum(jnp.where(where >= starts[v], 1.0, 0.0) for v in range(1, 4))
        slot = (lax.broadcasted_iota(jnp.int32, (64, 128), 1) % HEAD).astype(F32)
        sq_s[pl.ds(at, 64)] = jnp.where((slot < 4) & (slot != mine), 1.0, 0.0).astype(BF16)
        sk_s[pl.ds(at, 64)] = jnp.where(slot == mine, NEG_LARGE, 0.0).astype(BF16)


    pl.semaphore_wait(barrier, len(partners))
    unit_copy = remote(bias_u, uoth, wsem, 3 * (4 + 2 * (units // BLOCK)), across)
    head_copy = remote(bias_qv, voth, wsem, 3 * (4 + 2 * (units // BLOCK)) + 1, across)
    get_wq.wait()
    get_wo.wait()
    for copy in get_w1:
        copy.wait()
    get_w2.wait()

    part = (sides[0] + sides[1]) % 2

    class Piece:
        def __init__(self, index, refs, at, extent):
            size = extent // 4

            def some(k, first, size):
                return refs[k].at[pl.ds(aligned(at[k] + part * (extent // 2) + first, 16), size)]

            self.copies = [described(some(0, 0, 2 * size), some(1, 0, 2 * size), wsem, 3 * index, across)]
            for k in range(2):
                block = some(1, k * size, size)
                self.copies.append(described(block, block, wsem, 3 * index + 1 + k, mates[k]))
            self.stage = 0

        def advance(self):
            if self.stage == 0:
                self.copies[0].wait_recv()
                self.copies[1].start()
                self.copies[2].start()
            else:
                self.copies[1].wait_recv()
                self.copies[2].wait_recv()
            self.stage += 1

    pieces = [Piece(c, (wq_s.at[0, c], wq_s.at[1, c]), (0, 0), quarter) for c in range(3)]
    pieces.append(Piece(3, (wo_s, wo_s), (0, quarter), quarter))
    for i in range(units // BLOCK):
        pieces.append(Piece(4 + 2 * i, (w1_s.at[0, i], w1_s.at[1, i]), (0, 0), width))
        pieces.append(Piece(5 + 2 * i, (w2_s.at[0], w2_s.at[1]), (i * BLOCK, i * BLOCK), BLOCK))
    for item in pieces:
        item.copies[0].start()

    inside_loop = []

    def service(name, act):
        def at_point(k, ask):
            full = f"{name}{k}"
            if ask:
                return full in PLAN or full in WEIGHT_PLAN
            inside_loop.append(full)
            act(full)
            inside_loop.pop()

        return at_point

    def pass_on(name):
        for i in WEIGHT_PLAN.get(name, ()):
            if pieces[i].stage < 1:
                pieces[i].advance()

    def have_weight(*which):
        for i in which:
            while pieces[i].stage < 2:
                pieces[i].advance()

    n1_copy = remote(n1_s.at[pl.ds(0, count)], n1_s.at[pl.ds(count, count)], csem, 0, sib)
    get_cot.wait()
    cot_copy = remote(cot_s.at[pl.ds(0, count)], cot_s.at[pl.ds(count, count)], csem, 1, sib)

    def rotate(at):
        nr_s[pl.ds(at, BLOCK)] = dot(roll_s[pl.ds(at, BLOCK)], n1_s[...]).astype(BF16)

    def project(j, at):
        n = nr_s[pl.ds(at, BLOCK)]
        biases = bias_qv if j == 0 else voth
        q = (dot_nt(n, wq_s[j, 0]) + biases[0:1]).astype(BF16) * SCALE
        k = dot_nt(n, wq_s[j, 1]).astype(BF16)
        v = (dot_nt(n, wq_s[j, 2]) + biases[1:2]).astype(BF16)
        q_s[j, pl.ds(at, BLOCK), :quarter] = q
        k_s[pl.ds(at, BLOCK), :quarter] = k
        v_s[j, pl.ds(at, BLOCK), :quarter] = v
        kt_s[j * quarter : (j + 1) * quarter, pl.ds(at, BLOCK)] = k.T * SCALE

    blocks = [(b, at) for b in range(2) for at in range(0, count, BLOCK)]

    def attend(j):
        for head in range(heads):
            at = 512 + 256 * head
            a_s[:, at : at + 128] = head_lanes(q_s.at[j], head, sq_s[...])
            a_s[:, at + 128 : at + 256] = head_lanes(k_s, head, sk_s[...])
        for at in range(0, rows, BLOCK):
            ou_s[:quarter, at : at + BLOCK] = v_s[j, at : at + BLOCK, :quarter].T

        def tile(here):
            b = here // count
            at = aligned(here % count, BLOCK)
            keys = pl.ds(aligned(b * count, count), count)
            for head in range(heads):
                column = 512 + 256 * head
                s = dot_nt(a_s[keys, column + 128 : column + 256], a_s[pl.ds(here, BLOCK), column : column + 128])
                m = jnp.max(s, axis=0, keepdims=True)
                e = jnp.exp(s - m)
                r = 1.0 / column_sum(e)
                low = e.astype(BF16)
                span = slice(head * HEAD, head * HEAD + HEAD)
                to = slice(j * quarter + head * HEAD, j * quarter + head * HEAD + HEAD)
                e_s[j * heads + head, b, :, pl.ds(at, BLOCK)] = low
                ot_s[to, pl.ds(here, BLOCK)] = (dot(ou_s[span, keys], low) * r).astype(BF16)
                r_s[j * heads + head : j * heads + head + 1, pl.ds(here, BLOCK)] = r

        return tile

    loop(rows, 64, rotations)
    n1_copy.wait_recv()
    loop(rows, BLOCK, rotate)
    loop(rows, BLOCK, lambda at: project(0, at))
    pass_on("p0")
    loop(rows, BLOCK, attend(0), service("a", pass_on))
    head_copy.wait_recv()
    have_weight(0, 1, 2)
    loop(rows, BLOCK, lambda at: project(1, at))
    pass_on("p1")
    loop(rows, BLOCK, attend(1), service("c", pass_on))

    have_weight(3)

    def unrotate(at):
        ou_s[:, pl.ds(at, BLOCK)] = dot(ot_s[...], roll_s[:, pl.ds(at, BLOCK)]).astype(BF16)

    loop(rows, BLOCK, unrotate)
    pass_on("u")

    def out_part(at):
        return dot_tn(ou_s[:, pl.ds(at, BLOCK)], wo_s[...])

    def att_half(at):
        return half_copy(sb1.at[pl.ds(at, BLOCK)], rb1.at[pl.ds(at, BLOCK)], 2, at)

    def n2_half(at):
        return half_copy(n2_s.at[pl.ds(at, BLOCK)], n2_s.at[pl.ds(aligned(count + at, BLOCK), BLOCK)], 4, at)

    def out_sib(at):
        sb1[pl.ds(at, BLOCK)] = out_part(count + at).astype(BF16)
        att_half(at).start()

    loop(count, BLOCK, out_sib)

    def out_mine(at):
        mid_s[pl.ds(at, BLOCK)] = sin_s[pl.ds(at, BLOCK)] + out_part(at) + out_bias

    loop(count, BLOCK, out_mine)
    pass_on("o")

    def second_norm(at):
        att_half(at).wait_recv()
        for off in range(0, BLOCK, 128):
            spot = pl.ds(aligned(at + off, 128), 128)
            mid = mid_s[spot] + rb1[spot].astype(F32)
            mid_s[spot] = mid
            xhat, _ = norm_stats(mid)
            n2_s[spot] = (xhat * ln2_gain + ln2_bias).astype(BF16)
        n2_half(at).start()

    loop(count, BLOCK, second_norm)
    pass_on("n")

    base_a = units
    parts = units // BLOCK
    steps = copies_of(len(full_bits))

    class Region:
        def __init__(self, index, row, size, cols, slot, kind, refs, to):
            own_r, oth_r, xr_r, land_r, both_r, rx_r = refs
            self.place, self.slot, self.to, self.xr = (row, size, 0, cols), slot, to, xr_r
            first, after = KINDS[kind]
            self.first = first is not None
            self.stages, self.stage, self.finished, self.sent = [], -1, False, []
            now, parts, used, trail = self.place, 8, 0, []
            sems = iter(range(index * steps, (index + 1) * steps))

            def copy(src, src_at, dst, dst_at, device):
                return described(src.at[self.window(src_at)], dst.at[self.window(dst_at)], gsem, next(sems), device)

            def piece(bits, mask):
                where = now
                for k, b in enumerate(bits):
                    where = self.cut(where, 1 - sides[b] if mask >> k & 1 else sides[b])
                return where

            sums = 1 + len(after) + len(full_bits)
            if self.first:
                keep, give, there = piece((first,), 0), piece((first,), 1), (row // 2, size // 2, 0, cols)
                place = self.landing(0, 4)
                copies = [copy(own_r, give, land_r, place, mate((first,))), copy(oth_r, give, both_r, there, mate((first,)))]
                adds = [(own_r, own_r, keep, [(land_r, place)]), (oth_r, oth_r, keep, [(both_r, there)])]
                self.stages.append((copies, adds, False))
                trail.append(((first,), keep))
                now, parts, used = keep, 4, 4
            self.stages.append(([copy(oth_r, now, xr_r, now, across)], [(own_r, own_r, now, [(xr_r, now)])], False))
            for bits in after:
                parts >>= len(bits)
                keep, copies, terms = piece(bits, 0), [], []
                for mask in range(1, 1 << len(bits)):
                    place = self.landing(used, parts)
                    used += parts
                    terms.append((land_r, place))
                    copies.append(copy(own_r, piece(bits, mask), land_r, place, mate([b for k, b in enumerate(bits) if mask >> k & 1])))
                self.stages.append((copies, [(own_r, own_r, keep, terms)], False))
                trail.append((bits, keep))
                now = keep
            for i, b in enumerate(full_bits):
                place = self.small_place()
                self.stages.append(([copy(own_r, now, rx_r[i], place, mates[b])], [(own_r, own_r, now, [(rx_r[i], place)])], True))
            copies, adds, full = self.stages[-1]
            self.stages[-1] = (copies, [(xr_r,) + adds[0][1:]], full)
            for bits, keep in reversed(trail):
                copies = []
                for mask in range(1, 1 << len(bits)):
                    copies.append(copy(xr_r, keep, xr_r, keep, mate([b for k, b in enumerate(bits) if mask >> k & 1])))
                self.stages.append((copies, [], False))

        def window(self, where):
            row, size, col, cols = where
            return pl.ds(row, size), pl.ds(col, cols)

        def cut(self, where, side):
            row, size, col, cols = where
            if (size // 2) % 16 == 0:
                return aligned(row + side * (size // 2), 16), size // 2, col, cols
            return row, size, aligned(col + side * (cols // 2), 128), cols // 2

        def landing(self, at, parts_here):
            row, rows_one, cols_one = self.slot
            full = self.place[3]
            if cols_one == full:
                return row + at * rows_one, parts_here * rows_one, 0, full
            if parts_here == 1:
                return row + at // 2 * rows_one, rows_one, at % 2 * cols_one, cols_one
            return row + at // 2 * rows_one, parts_here // 2 * rows_one, 0, full

        def small_place(self):
            row, rows_one, cols_one = self.slot
            if cols_one == self.place[3]:
                return row // 7, rows_one, 0, cols_one
            k = (self.place[0] - base_a) // quarter
            return units // 8 + k // 2 * rows_one, rows_one, k % 2 * cols_one, cols_one

        def begin(self, copies):
            for copy in copies:
                copy.start()
            self.sent += copies

        def ready(self, j):
            if self.first:
                self.stage = 0
                self.begin([self.stages[0][0][j]])
            elif j == 1:
                self.stage = 0
                self.begin(self.stages[0][0])

        def add(self, into, base, where, terms):
            row, size, col, cols = where
            step = 64 if size % 64 == 0 else 48 if size % 48 == 0 else 32

            def body(off):
                to = (pl.ds(aligned(row + off, 16), step), pl.ds(col, cols))
                total = base[to].astype(F32)
                for ref, (r, _, c, _) in terms:
                    total += ref[pl.ds(aligned(r + off, 16), step), pl.ds(c, cols)].astype(F32)
                into[to] = total.astype(BF16)

            if inside_loop:
                for off in range(0, size, step):
                    body(off)
            else:
                loop(size, step, body)

        def advance(self):
            if self.finished or self.stage < 0:
                return
            copies, adds, full = self.stages[self.stage]
            for copy in copies:
                copy.wait_recv()
            if full:
                for copy in copies:
                    copy.wait_send()
                self.sent = [c for c in self.sent if all(c is not d for d in copies)]
            for item in adds:
                self.add(*item)
            self.stage += 1
            if self.stage < len(self.stages):
                self.begin(self.stages[self.stage][0])
                return
            self.finished = True
            to_write.append(self)

    chunks = []
    refs = (own, oth, xr, land, land_both, rx)
    for i in range(parts):
        slot = (i * 7 * (BLOCK // 8), BLOCK // 8, width)
        to = g2_h.at[pl.ds(i * BLOCK, BLOCK)]
        chunks.append(Region(2 * i, i * BLOCK, BLOCK, width, slot, ORDERS[2 * i], refs, to))
        refs_one = tuple(ref.at[i] for ref in (own1, oth1, xr1, land1, land1_both)) + ([ref.at[i] for ref in rx1],)
        to = g1_h.at[:, pl.ds(i * BLOCK, BLOCK)]
        chunks.append(Region(2 * i + 1, 0, width, BLOCK, (0, width // 8, BLOCK), ORDERS[2 * i + 1], refs_one, to))
    for i in range(4):
        slot = (7 * units // 8 + i * quarter, quarter // 4, width // 2)
        to = go_h if i == 0 else gq_h.at[i - 1]
        chunks.append(Region(2 * parts + i, base_a + i * quarter, quarter, width, slot, ORDERS[2 * parts + i], refs, to))
    first_att = 2 * parts

    class Small:
        def __init__(self, tile, index, everywhere, paired, groups):
            self.tile, self.everywhere, self.paired = tile, everywhere, paired
            landings = [near.at[3 * index + k] for k in range(3)] + [far.at[(7 + len(full_bits)) * index + k] for k in range(7 + len(full_bits))]
            sems = iter(range(index * len(landings), (index + 1) * len(landings)))
            landings = iter(landings)

            def stage(devices):
                places = [next(landings) for _ in devices]
                return places, [described(tile, dst, ssem, next(sems), d) for dst, d in zip(places, devices)]

            self.stages = [stage([sib, across, facing])]
            for bits in groups + [(b,) for b in full_bits]:
                masks = range(1, 1 << len(bits))
                self.stages.append(stage([mate([b for k, b in enumerate(bits) if mask >> k & 1]) for mask in masks]))
            self.stage, self.finished = -1, False

        def start(self):
            self.stage = 0
            for copy in self.stages[0][1]:
                copy.start()

        def advance(self):
            if self.finished or self.stage < 0:
                return
            places, copies = self.stages[self.stage]
            for copy in copies:
                copy.wait()
            tile = self.tile
            if self.stage == 0:
                beside, over, facing_ = places
                n, p = self.everywhere, self.paired
                tile[0:n] = (tile[0:n] + beside[0:n]) + (over[0:n] + facing_[0:n])
                tile[n : n + p] = tile[n : n + p] + over[n + p : n + 2 * p]
            else:
                got = [tile[...]] + [place[...] for place in places]
                while len(got) > 1:
                    got = [got[k] + got[k + 1] for k in range(0, len(got), 2)]
                tile[...] = got[0]
            self.stage += 1
            if self.stage == len(self.stages):
                self.finished = True
                return
            for copy in self.stages[self.stage][1]:
                copy.start()

    first_small = Small(early, 0, 4, 1, [(b,) for b in half_bits])
    last_small = Small(late, 1, 2, 2, [tuple(half_bits)])

    def ready(i, j):
        chunks[i].ready(j)

    to_write = []

    def write_finished():
        while to_write:
            region = to_write.pop()
            region.done = local(region.xr.at[region.window(region.place)], region.to)

    def hook(name):
        pass_on(name)
        for i in PLAN.get(name, ()):
            (chunks + [last_small, first_small])[i].advance()
            if not inside_loop:
                write_finished()

    def chunk_rows(j, i, at):
        span = pl.ds(at, BLOCK)
        cols = slice(j * units + i * BLOCK, j * units + (i + 1) * BLOCK)
        mine = slice(i * BLOCK, (i + 1) * BLOCK)
        bias = (bias_u if j == 0 else uoth)[mine].reshape(1, BLOCK)
        h = dot(n2_s[span], w1_s[j, i]) + bias
        a, slope = gelu_pair(h)
        a_s[span, cols] = a.astype(BF16)
        g = (dot_nt(cot_s[span], w2_s[j, mine]) * slope).astype(BF16)
        g_s[span, cols] = g

    def chunk_grads(j, i):
        cols = slice(j * units + i * BLOCK, j * units + (i + 1) * BLOCK)
        mine = slice(i * BLOCK, (i + 1) * BLOCK)
        to = oth if j == 1 else own

        def second(at):
            to[pl.ds(i * BLOCK + at, 128)] = dot_tn(a_s[:, pl.ds(cols.start + at, 128)], cot_s[...]).astype(BF16)

        loop(BLOCK, 128, second)
        ready(2 * i, j)
        g = g_s[:, cols]

        def first(at):
            (oth1 if j == 1 else own1)[i, pl.ds(at, BLOCK)] = dot(n2t_s[pl.ds(at, BLOCK)], g_s[:, cols]).astype(BF16)

        loop(width, BLOCK, first)
        ready(2 * i + 1, j)
        early[4 + j : 5 + j, mine] = column_sum(g.astype(F32))
        hook(f"f{j}{i}")

    def feed(j, i, first=False):
        if first:
            loop(count, BLOCK, lambda at: chunk_rows(j, i, at))
            hook(f"r{j}{i}.0")
            cot_copy.wait_recv()

            def received(at):
                n2_half(at).wait_recv()
                chunk_rows(j, i, count + at)

            loop(count, BLOCK, received)
            hook(f"r{j}{i}.1")

            def turned(at):
                n2t_s[:, pl.ds(at, BLOCK)] = n2_s[pl.ds(at, BLOCK)].T

            loop(rows, BLOCK, turned)
        else:
            loop(rows, BLOCK, lambda at: chunk_rows(j, i, at), service(f"r{j}{i}.", hook), 2)
        chunk_grads(j, i)

    early[...] = jnp.zeros_like(early)
    late[...] = jnp.zeros_like(late)
    unit_copy.wait_recv()
    for i in range(parts):
        have_weight(4 + 2 * i, 5 + 2 * i)
        feed(1, i, first=i == 0)
        feed(0, i)

    def back_two(at):
        span = pl.ds(at, BLOCK)
        total = None
        for j in range(2):
            for i in range(parts):
                at_col = j * units + i * BLOCK
                term = dot_nt(g_s[span, at_col : at_col + BLOCK], w1_s[j, i])
                total = term if total is None else total + term
        return total

    def mlp_part(at):
        span = pl.ds(at, BLOCK)
        return dot(a_s[span, :units], w2_s[0]) + dot(a_s[span, units:], w2_s[1])

    def gn2_half(at):
        return half_copy(sb2.at[pl.ds(at, BLOCK)], rb2.at[pl.ds(at, BLOCK)], 6, at)

    def dm_half(at):
        return half_copy(n2_s.at[pl.ds(at, BLOCK)], n2_s.at[pl.ds(aligned(count + at, BLOCK), BLOCK)], 10, at)

    def back_two_sib(at):
        sb2[pl.ds(at, BLOCK)] = back_two(count + at).astype(BF16)
        gn2_half(at).start()

    def back_two_mine(at):
        gm_s[pl.ds(at, BLOCK)] = back_two(at)

    def mlp_sib(at):
        sb1[pl.ds(at, BLOCK)] = mlp_part(count + at).astype(BF16)

    loop(count, BLOCK, back_two_sib)
    hook("g0")
    loop(count, BLOCK, back_two_mine)
    hook("gn2")

    def second_back(at):
        gn2_half(at).wait_recv()
        n2_half(at).wait_send()
        for off in range(0, BLOCK, 128):
            spot = pl.ds(aligned(at + off, 128), 128)
            xhat, sigma = norm_stats(mid_s[spot])
            grad = gm_s[spot] + rb2[spot].astype(F32)
            cot = cot_s[spot].astype(F32)
            back = cot + norm_back(grad, ln2_gain, xhat, sigma)
            gm_s[spot] = back
            n2_s[spot] = back.astype(BF16)
            early[0:1] += column_sum(back)
            early[1:2] += column_sum(grad * xhat)
            early[2:3] += column_sum(grad)
            early[3:4] += column_sum(cot)
        dm_half(at).start()

    loop(count, BLOCK, second_back)
    hook("lb")
    for at in range(0, count, BLOCK):
        att_half(at).wait_send()
    loop(count, BLOCK, mlp_sib)
    mlp_copy = remote(sb1, rb1, csem, 8, sib)
    first_small.start()
    hook("ln2")

    def finish_out(at):
        span = pl.ds(at, BLOCK)
        mid_s[span] = mid_s[span] + mlp_part(at) + fc2_bias

    loop(count, BLOCK, finish_out)
    hook("fo")
    mlp_copy.wait_recv()

    def write_out(at):
        spot = pl.ds(at, 128)
        tok_s[spot] = (mid_s[spot] + rb1[spot].astype(F32)).astype(BF16)

    loop(count, 128, write_out)
    put_out = local(tok_s, out_h)
    hook("fin")
    for at in range(0, count, BLOCK):
        dm_half(at).wait_recv()

    start = base_a + quarter
    zero = jnp.zeros((count, 128), BF16)
    grad_s = dq_s = gr_s

    def keep_gradient(j, c):
        to = oth if j == 1 else own
        low = start + c * quarter
        dt = ot_s.at[j * quarter : (j + 1) * quarter]

        def columns(at):
            to[low : low + quarter, pl.ds(at, BLOCK)] = dot(dt[...], nr_s[:, pl.ds(at, BLOCK)]).astype(BF16)

        loop(width, BLOCK, columns)
        ready(first_att + 1 + c, j)
        if c != 1:
            d = g_s[:, (3 * j + c) * BLOCK : (3 * j + c) * BLOCK + quarter]
            late[2 + c // 2 + 2 * j : 3 + c // 2 + 2 * j, :quarter] = column_sum(d.astype(F32))

    def values_back(j):
        base = j * quarter
        to = oth if j == 1 else own

        def weight(at):
            to[base_a : base_a + quarter, pl.ds(at, BLOCK)] = dot(ou_s[base : base + quarter], n2_s[:, pl.ds(at, BLOCK)]).astype(BF16)

        loop(width, BLOCK, weight)
        ready(first_att, j)

        def output(at):
            grad_s[base : base + quarter, pl.ds(at, BLOCK)] = dot_nt(wo_s[base : base + quarter], n2_s[pl.ds(at, BLOCK)]).astype(BF16)

        loop(rows, BLOCK, output)
        hook(f"w{j}.0")
        go_s = a_s.at[:, rows + 256 * j : rows + 256 * (j + 1)]

        def scale(at):
            here = pl.ds(at, BLOCK)
            grad_t = dot_nt(grad_s[base : base + quarter], roll_s[here])
            for head in range(heads):
                row = j * heads + head
                r = r_s[row : row + 1, here]
                g = grad_t[head * HEAD : (head + 1) * HEAD]
                at_head = slice(base + head * HEAD, base + (head + 1) * HEAD)
                in_s[row : row + 1, here] = column_sum(g * ot_s[at_head, here].astype(F32)) * r
                gt_s[at_head, here] = (g * r).astype(BF16)
            go_s[here, :quarter] = gt_s[base : base + quarter, here].T

        loop(rows, BLOCK, scale)

        def block(at):
            here = pl.ds(at, count)
            b = at // count
            dv = [None, None]
            for head in range(heads):
                tile = head // 2
                gh = jnp.where(lane_half(count, head % 2 == 1), go_s[here, 128 * tile : 128 * tile + 128], zero)
                part = dot(e_s[j * heads + head, b], gh)
                dv[tile] = part if dv[tile] is None else dv[tile] + part
            dv = jnp.concatenate(dv, axis=1)[:, :quarter].astype(BF16)
            g_s[here, (3 * j + 2) * BLOCK : (3 * j + 2) * BLOCK + quarter] = dv
            ot_s[base : base + quarter, here] = dv.T

        loop(rows, count, block)
        hook(f"w{j}.1")
        keep_gradient(j, 2)
        hook(f"v{j}")

    def scores_back(j):
        base = j * quarter

        def block(at):
            here = pl.ds(at, count)
            b = at // count
            dk = [None, None]
            for head in range(heads):
                tile = head // 2
                row = j * heads + head
                half = lane_half(count, head % 2 == 1)
                lanes = slice(128 * tile, 128 * tile + 128)
                vh = jnp.where(half, v_s[j, here, lanes], zero)
                qh = jnp.where(half, q_s[j, here, lanes], zero)
                last_row = min(128 * tile + 128, quarter)
                vh = vh[:, : last_row - 128 * tile]
                ds = a_s.at[:count, head * count : (head + 1) * count] if head < 2 else a_s.at[count:, :count]
                for off in range(0, count, BLOCK):
                    some = pl.ds(aligned(at + off, BLOCK), BLOCK)
                    dp_t = dot(vh, gt_s[base + 128 * tile : base + last_row, some])
                    grad = (dp_t - in_s[row : row + 1, some]) * e_s[row, b, :, off : off + BLOCK].astype(F32)
                    ds[:, off : off + BLOCK] = grad.astype(BF16)
                part = dot(ds[...], qh)
                dk[tile] = part if dk[tile] is None else dk[tile] + part
                kth = kt_s[base + head * HEAD : base + head * HEAD + HEAD, here]
                dq_s[base + head * HEAD : base + head * HEAD + HEAD, here] = dot(kth, ds[...]).astype(BF16)
            dk = jnp.concatenate(dk, axis=1)[:, :quarter].astype(BF16)
            g_s[here, (3 * j + 1) * BLOCK : (3 * j + 1) * BLOCK + quarter] = dk
            ot_s[base : base + quarter, here] = dk.T
            g_s[here, 3 * j * BLOCK : 3 * j * BLOCK + quarter] = dq_s[base : base + quarter, here].T

        loop(rows, count, block, service(f"b{j}.", hook))
        keep_gradient(j, 1)
        hook(f"k{j}")
        ot_s[base : base + quarter] = dq_s[base : base + quarter]
        keep_gradient(j, 0)
        hook(f"s{j}")

    values_back(1)
    values_back(0)
    scores_back(1)
    scores_back(0)

    def back_one(at):
        total = None
        for j in range(2):
            for c in range(3):
                d = g_s[pl.ds(at, BLOCK), (3 * j + c) * BLOCK : (3 * j + c) * BLOCK + quarter]
                term = dot(d, wq_s[j, c])
                total = term if total is None else total + term
        n2_s[pl.ds(at, BLOCK)] = total.astype(BF16)

    for at in range(0, count, BLOCK):
        dm_half(at).wait_send()
    loop(rows, BLOCK, back_one, service("d.", hook), 2)
    for at in range(0, count, BLOCK):
        gn2_half(at).wait_send()

    def gn1_half(at):
        return half_copy(sb2.at[pl.ds(at, BLOCK)], rb2.at[pl.ds(at, BLOCK)], 12, at)

    def back_one_sib(at):
        sb2[pl.ds(at, BLOCK)] = dot(back_s[pl.ds(count + at, BLOCK)], n2_s[...]).astype(BF16)
        gn1_half(at).start()

    def back_one_mine(at):
        mid_s[pl.ds(at, BLOCK)] = dot(back_s[pl.ds(at, BLOCK)], n2_s[...])

    loop(count, BLOCK, back_one_sib)
    loop(count, BLOCK, back_one_mine)
    hook("e.0")
    mlp_copy.wait_send()

    def first_back(at):
        gn1_half(at).wait_recv()
        for off in range(0, BLOCK, 128):
            spot = pl.ds(aligned(at + off, 128), 128)
            xhat, sigma = norm_stats(sin_s[spot])
            grad = mid_s[spot] + rb2[spot].astype(F32)
            sb1[spot] = (gm_s[spot] + norm_back(grad, ln1_gain, xhat, sigma)).astype(BF16)
            late[0:1] += column_sum(grad * xhat)
            late[1:2] += column_sum(grad)

    loop(count, BLOCK, first_back)
    put_in = local(sb1, ing_h)
    last_small.start()
    hook("e.1")
    hook("tail")
    left = [first_small, last_small] + chunks
    while left:
        for item in left:
            item.advance()
            write_finished()
        left = [item for item in left if not item.finished]

    for row, source, at in ((0, late, 0), (1, late, 1), (2, early, 0), (3, early, 1), (4, early, 2), (5, early, 3), (8, early, 4), (9, late, 2), (10, late, 3)):
        small_o[row : row + 1] = source[at : at + 1]

    passed = [copy for item in pieces for copy in item.copies]
    for copy in [unit_copy, head_copy, n1_copy, cot_copy] + [gn1_half(at) for at in range(0, count, BLOCK)] + passed:
        copy.wait_send()
    for chunk in chunks:
        for copy in chunk.sent:
            copy.wait_send()
        chunk.done.wait()
    put_out.wait()
    put_in.wait()


def copies_of(full):
    most = 0
    for kind in ORDERS:
        first, after = KINDS[kind]
        most = max(most, 1 + full + 2 * sum((1 << len(bits)) - 1 for bits in after) + (0 if first is None else 3))
    return most


def call_layer(dp_size, tokens, cotangent, ids, table, vectors, wq, wo, w1, w2):
    count, width = tokens.shape
    rows = 2 * count
    quarter = wo.shape[0]
    units = w1.shape[1]
    heads = quarter // HEAD
    grad_rows = units + 4 * quarter
    parts = units // BLOCK
    bits = [b for b in range(20) if (1 << b) < dp_size]
    half_bits = bits[:3]
    shape = jax.ShapeDtypeStruct
    vm = pltpu.VMEM
    regions = 2 * (units // BLOCK) + 4
    steps = copies_of(len(bits) - len(half_bits))
    fetched = 4 + 2 * (units // BLOCK)
    scratch = (
        [vm((count, width), BF16), vm((rows, width), BF16)]
        + [vm((count, width), F32)] * 3
        + [vm((rows, width), BF16)] * 2
        + [vm((width, rows), BF16)]
        + [vm((2,) + wq.shape, BF16), vm((2 * quarter, width), BF16), vm((2, units // BLOCK, width, BLOCK), BF16), vm((2,) + w2.shape, BF16)]
        + [vm((2, rows, 256), BF16)] * 2
        + [vm((2 * quarter, rows), BF16)] * 5
        + [vm((8, rows), F32)] * 2
        + [vm((2 * heads, 2, count, count), BF16)]
        + [vm((rows, rows), BF16)] * 2
        + [vm((rows, width), BF16)]
        + [vm((rows, 2 * units), BF16)] * 2
        + [vm((count, width), BF16)] * 4
        + [vm((grad_rows, width), BF16)] * 3
        + [vm((7 * units // 8 + 4 * quarter, width), BF16), vm((units // 2, width), BF16)]
        + [vm((parts, width, BLOCK), BF16)] * 3
        + [vm((parts, 7 * width // 8, BLOCK), BF16), vm((parts, width // 2, BLOCK), BF16)]
        + [vm((grad_rows >> len(half_bits), width), BF16)] * (len(bits) - len(half_bits))
        + [vm((parts, width // 8, BLOCK), BF16)] * (len(bits) - len(half_bits))
        + [vm((units,), F32), vm((2, quarter), F32), vm((8, width), F32), vm((8, width), F32)]
        + [vm((6, 8, width), F32), vm((14 + 2 * (len(bits) - 3), 8, width), F32)]
        + [pltpu.SemaphoreType.DMA((8 + units // BLOCK + regions,))]
        + [pltpu.SemaphoreType.DMA((2, n)) for n in (3 * fetched + 2, 14, regions * steps, 2 * (10 + len(bits) - 3))]
    )
    anywhere = pl.BlockSpec(memory_space=pl.ANY)
    inside = pl.BlockSpec(memory_space=pltpu.VMEM)
    return pl.pallas_call(
        functools.partial(layer, dp_size, half_bits),
        out_shape=[shape((count, width), BF16)] * 2
        + [shape(w2.shape, BF16), shape(w1.shape, BF16), shape(wo.shape, BF16), shape(wq.shape, BF16), shape((16, width), F32)],
        in_specs=[anywhere] * 2 + [inside] * (2 + len(vectors)) + [anywhere] * 4,
        out_specs=[anywhere] * 6 + [inside],
        scratch_shapes=scratch,
        compiler_params=pltpu.CompilerParams(vmem_limit_bytes=VMEM_LIMIT, collective_id=0, has_side_effects=True),
        name="layer",
    )(tokens, cotangent, ids, table, *vectors, wq, wo, w1, w2)


def finish(*refs):
    sources, small, rest = refs[:6], refs[6], refs[7:]
    results, vectors, rest = rest[:6], rest[6:14], rest[14:]
    narrow, wide, (get, put) = rest[:6], rest[6:10], rest[10:]
    blocks = []
    for k, src in enumerate(sources):
        if src.ndim == 3:
            places = list(range(src.shape[0]))
        else:
            step = min(BLOCK, src.shape[0])
            places = [pl.ds(at, step) for at in range(0, src.shape[0], step)]
        for at in places:
            low = narrow[k].at[at]
            blocks.append((src.at[at], low, low if k < 2 else wide[k - 2].at[at], results[k].at[at]))
    reads = [pltpu.make_async_copy(src, low, get.at[n]) for n, (src, low, _, _) in enumerate(blocks)]
    writes = [pltpu.make_async_copy(high, dst, put.at[n]) for n, (_, _, high, dst) in enumerate(blocks)]
    for copy in reads:
        copy.start()
    for i in range(6):
        vectors[i][...] = small[i]
    vectors[6][...] = small[8, : vectors[6].shape[0]]
    vectors[7][...] = small[9:11, : vectors[7].shape[1]]
    for read, write, (_, low, high, _) in zip(reads, writes, blocks):
        read.wait()
        if high is not low:

            def cast(at, low=low, high=high):
                high[pl.ds(at, 64)] = low[pl.ds(at, 64)].astype(F32)

            loop(low.shape[0], 64, cast)
        write.start()
    for copy in writes:
        copy.wait()


def call_finish(arrays, small, units, quarter):
    width = small.shape[1]
    shape = jax.ShapeDtypeStruct
    extents = [(width,)] * 6 + [(units,), (2, quarter)]
    kinds = [BF16, BF16, F32, F32, F32, F32]
    anywhere = pl.BlockSpec(memory_space=pl.ANY)
    inside = pl.BlockSpec(memory_space=pltpu.VMEM)
    grads = arrays[2:]
    return pl.pallas_call(
        finish,
        in_specs=[anywhere] * len(arrays) + [inside],
        out_specs=[anywhere] * len(arrays) + [inside] * len(extents),
        out_shape=[shape(a.shape, k) for a, k in zip(arrays, kinds)] + [shape(e, F32) for e in extents],
        scratch_shapes=[pltpu.VMEM(a.shape, BF16) for a in arrays]
        + [pltpu.VMEM(a.shape, F32) for a in grads]
        + [pltpu.SemaphoreType.DMA((16,)), pltpu.SemaphoreType.DMA((16,))],
        compiler_params=pltpu.CompilerParams(vmem_limit_bytes=VMEM_LIMIT),
        name="finish",
    )(*arrays, small)


def per_device(
    tokens, segment_ids, ln1_gain, ln1_bias, qkv_weight, qv_bias, out_weight, out_bias,
    ln2_gain, ln2_bias, fc1_weight, fc1_bias, fc2_weight, fc2_bias, cotangent,
):
    width = tokens.shape[1]
    freq_count = width // 6
    frequency = 10000.0 ** (-jnp.arange(freq_count, dtype=F32) / freq_count)
    angles = jnp.arange(SIDE, dtype=F32)[:, None] * frequency[None, :]
    table = jnp.concatenate([jnp.sin(angles), jnp.cos(angles)], axis=1)
    vectors = (ln1_gain, ln1_bias, out_bias, ln2_gain, ln2_bias, fc2_bias, fc1_bias, qv_bias)
    *arrays, small = call_layer(
        lax.axis_size("dp"), tokens, cotangent, segment_ids, table, vectors, qkv_weight.transpose(0, 2, 1), out_weight, fc1_weight, fc2_weight
    )
    out, ing, g2, g1, go, gq, a0, a1, a2, a3, a4, a5, g_units, g_heads = call_finish(arrays, small, fc1_weight.shape[1], out_weight.shape[0])
    return (out, ing, a0, a1, gq.transpose(0, 2, 1), g_heads, go, a2, a3, a4, g1, g_units, g2, a5)


def solution(mesh):
    placed = (
        P(("dp", "tensor"), None),
        P("dp", None),
        P(),
        P(),
        P(None, None, "tensor"),
        P(None, "tensor"),
        P("tensor", None),
        P(),
        P(),
        P(),
        P(None, "tensor"),
        P("tensor"),
        P("tensor", None),
        P(),
        P(("dp", "tensor"), None),
    )
    return jax.shard_map(
        per_device,
        mesh=mesh,
        in_specs=placed,
        out_specs=(
            P(("dp", "tensor"), None),
            P(("dp", "tensor"), None),
            P(),
            P(),
            P(None, None, "tensor"),
            P(None, "tensor"),
            P("tensor", None),
            P(),
            P(),
            P(),
            P(None, "tensor"),
            P("tensor"),
            P("tensor", None),
            P(),
        ),
        check_vma=False,
    )
```

```python
import functools

import jax
import jax.numpy as jnp
from jax import lax
from jax.experimental import pallas as pl
from jax.experimental.pallas import tpu as pltpu
from jax.sharding import PartitionSpec as P

HEAD = 64
SIDE = 16
EPSILON = 1e-06
NEG_LARGE = -1e30
SCALE = HEAD ** (-0.5)
F32 = jnp.float32
BF16 = jnp.bfloat16
VMEM_LIMIT = 64 * 1024 * 1024 - 128 * 1024
MESH = pl.DeviceIdType.MESH
BLOCK = 256
KINDS = {
    "A": (None, ((0,), (1,), (2,))),
    "B": (None, ((1,), (0,), (2,))),
    "D": (None, ((0,), (1, 2))),
    "E": (None, ((0, 1, 2),)),
    "C": (None, ((0, 1), (2,))),
    "Y": (0, ((1,), (2,))),
    "Z": (1, ((0,), (2,))),
    "YD": (0, ((1, 2),)),
    "S": (None, (("p",), ("q",), (2,))),
    "SD": (None, (("p",), ("q", 2))),
    "SF": ("p", (("q",), (2,))),
    "SFD": ("p", (("q", 2),)),
}
ORDERS = ("D", "SFD", "SFD", "SF", "A", "Y", "S", "SD", "SD", "S")
WEIGHT_PLAN = {"p0": (0,), "a2": (1,), "p1": (3, 4), "c1": (5,), "o": (6,), "r10.0": (7,), "f10": (8,), "f00": (9,)}
PLAN = {
    "f01": (1, 0),
    "r02.0": (2,),
    "r02.1": (1,),
    "f02": (3,),
    "lb": (0, 4, 1),
    "w1.0": (2,),
    "w1.1": (-1,),
    "v1": (5, 0, 3),
    "b1.0": (4, 1),
    "b1.1": (-1,),
    "k1": (2, 3),
    "w0.0": (6, 4, 0, 1, -1),
    "v0": (9, 5, 2),
    "b0.0": (6, 3),
    "b0.1": (4, -1, 0, 9, 5),
    "k0": (8, 2, 6),
    "s0": (3,),
    "fo": (7, 9, 4),
    "d.0": (5, 8, 6, 3),
    "d.1": (7, 9),
    "e.0": (4,),
    "e.1": (5,),
    "tail": (8, 6, 3, -2, 4, 7, 9, 5, 6, 8, -2, 5, 9, 6, 7, 8, 9, 7),
}


def dot(a, b):
    return jnp.dot(a, b, preferred_element_type=F32)


def dot_nt(a, b):
    return lax.dot_general(a, b, (((1,), (1,)), ((), ())), preferred_element_type=F32)


def dot_tn(a, b):
    return lax.dot_general(a, b, (((0,), (0,)), ((), ())), preferred_element_type=F32)


def lane_half(rows, upper):
    lanes = lax.broadcasted_iota(jnp.int32, (rows, 128), 1)
    return lanes >= HEAD if upper else lanes < HEAD


def head_lanes(ref, head, filler):
    tile = ref[:, 128 * (head // 2) : 128 * (head // 2) + 128]
    return jnp.where(lane_half(tile.shape[0], head % 2 == 1), tile, filler)


def gelu_pair(h):
    cdf = 0.5 + 0.5 * lax.erf(h * 0.7071067811865476)
    return h * cdf, cdf + h * jnp.exp(-0.5 * h * h) * 0.3989422804014327


def norm_stats(v):
    centred = v - jnp.mean(v, axis=-1, keepdims=True)
    sigma = lax.rsqrt(jnp.mean(centred * centred, axis=-1, keepdims=True) + EPSILON)
    return centred * sigma, sigma


def norm_back(grad, gain, xhat, sigma):
    g = grad * gain
    return sigma * (g - jnp.mean(g, axis=-1, keepdims=True) - xhat * jnp.mean(g * xhat, axis=-1, keepdims=True))


def column_sum(v):
    return jnp.sum(v, axis=0, keepdims=True)


def aligned(v, unit):
    return v if isinstance(v, int) else pl.multiple_of(v, unit)


def loop(count, step, body, service=None, every=1):
    def run(i, carry):
        body(aligned(i * step, step))
        if service is not None:
            for k in range(count // step // every):
                if service(k, True):
                    pl.when(i == every * (k + 1) - 1)(functools.partial(service, k, False))
        return carry

    lax.fori_loop(0, count // step, run, 0)


def layer(
    dp_size, half_bits,
    tok_h, cot_h, ids, table, gain1, bias1, bias_o, gain2, bias2, bias_f, bias_u, bias_qv, wq_h, wo_h, w1_h, w2_h,
    out_h, ing_h, g2_h, g1_h, go_h, gq_h, small_o,
    tok_s, cot_s, sin_s, mid_s, gm_s, n1_s, n2_s, n2t_s, wq_s, wo_s, w1_s, w2_s,
    q_s, v_s, kt_s, ot_s, ou_s, gt_s, r_s, in_s, e_s, roll_s, back_s, nr_s, ds_s, a_s, g_s, sb1, sb2, rb1, rb2,
    own, oth, xr, land, land_both, own1, oth1, xr1, land1, land1_both, *rest,
):
    rest = list(rest)
    full_bits = [b for b in range(20) if (1 << b) < dp_size and b not in half_bits]
    rx = [rest.pop(0) for _ in full_bits]
    rx1 = [rest.pop(0) for _ in full_bits]
    uoth, voth, early, late, near, far, lsem, wsem, csem, gsem, ssem = rest

    count, width = tok_s.shape
    rows = 2 * count
    quarter = wo_h.shape[0]
    units = w1_h.shape[1]
    heads = quarter // HEAD
    place = lax.axis_index("tensor")
    dp = lax.axis_index("dp")
    chip = place // 2
    core = place % 2
    sib = {"tensor": chip * 2 + 1 - core}
    across = {"tensor": (1 - chip) * 2 + core}
    facing = {"tensor": (1 - chip) * 2 + 1 - core}
    all_bits = list(half_bits) + full_bits
    sides = {b: (dp // (1 << b)) % 2 for b in all_bits}

    ways = {b: (1 - 2 * sides[b]) * (1 << b) for b in all_bits}
    sides["p"] = sides[0] + (sides[1] - sides[0]) * core
    sides["q"] = sides[1] + (sides[0] - sides[1]) * core
    ways["p"] = ways[0] + (ways[1] - ways[0]) * core
    ways["q"] = ways[1] + (ways[0] - ways[1]) * core

    def mate(bits):
        return {"dp": dp + sum(ways[b] for b in bits)}

    def described(src, dst, sems, index, device):
        return pltpu.make_async_remote_copy(
            src_ref=src, dst_ref=dst, send_sem=sems.at[0, index], recv_sem=sems.at[1, index], device_id=device, device_id_type=MESH
        )

    mates = {b: mate((b,)) for b in all_bits}
    groups = {(b,) for b in full_bits}
    for mask in range(1, 1 << len(half_bits)):
        groups.add(tuple(b for k, b in enumerate(half_bits) if mask >> k & 1))

    barrier = pltpu.get_barrier_semaphore()
    partners = [sib, across, facing] + [mate(bits) for bits in sorted(groups)]
    for partner in partners:
        pl.semaphore_signal(barrier, inc=1, device_id=partner, device_id_type=MESH)

    sq_s, sk_s, k_s = a_s.at[:, 0:128], a_s.at[:, 128:256], a_s.at[:, 256:512]
    local_used = [0]

    def local(src, dst):
        copy = pltpu.make_async_copy(src, dst, lsem.at[local_used[0]])
        local_used[0] += 1
        copy.start()
        return copy

    def remote(src, dst, sems, index, device):
        copy = pltpu.make_async_remote_copy(
            src_ref=src, dst_ref=dst, send_sem=sems.at[0, index], recv_sem=sems.at[1, index], device_id=device, device_id_type=MESH
        )
        copy.start()
        return copy

    def half_copy(src, dst, first, at):
        return pltpu.make_async_remote_copy(
            src_ref=src,
            dst_ref=dst,
            send_sem=csem.at[0, first + at // BLOCK],
            recv_sem=csem.at[1, first + at // BLOCK],
            device_id=sib,
            device_id_type=MESH,
        )

    get_tok = local(tok_h, tok_s)
    get_cot = local(cot_h, cot_s.at[pl.ds(0, count)])
    get_wq = local(wq_h, wq_s.at[0])
    get_wo = local(wo_h, wo_s.at[pl.ds(0, quarter)])
    get_w1 = [local(w1_h.at[:, pl.ds(i * BLOCK, BLOCK)], w1_s.at[0, i]) for i in range(units // BLOCK)]
    get_w2 = local(w2_h, w2_s.at[0])

    ln1_gain, ln1_bias, out_bias, ln2_gain, ln2_bias, fc2_bias = (
        ref[...].reshape(1, width) for ref in (gain1, bias1, bias_o, gain2, bias2, bias_f)
    )
    get_tok.wait()

    def first_norm(at):
        plane = core * (count // (SIDE * SIDE)) + at // (SIDE * SIDE)
        line = (at // SIDE) % SIDE
        shape = (SIDE, width // 3)
        for k in range(4):
            spot = jnp.concatenate(
                [jnp.broadcast_to(table[pl.ds(plane, 1)], shape), jnp.broadcast_to(table[pl.ds(line + k, 1)], shape), table[...]], axis=1
            )
            span = pl.ds(aligned(at + k * SIDE, SIDE), SIDE)
            stream = tok_s[span].astype(F32) + spot
            sin_s[span] = stream
            xhat, _ = norm_stats(stream)
            n1_s[span] = (xhat * ln1_gain + ln1_bias).astype(BF16)

    loop(count, 4 * SIDE, first_norm)
    doc = ids[pl.ds(chip, 1), :]
    starts = [jnp.zeros((1, 1), F32)]
    starts += [jnp.sum(jnp.where(doc < v, 1.0, 0.0), axis=1, keepdims=True) for v in range(1, 4)]
    starts.append(jnp.full((1, 1), rows, F32))
    turn = jnp.zeros((1, 1), F32)
    for v in range(4):
        turn += jnp.where(starts[v + 1] - starts[v] == count, starts[v], 0.0)
    turn_here = turn - (core * count).astype(F32)

    def wrapped(v):
        v = jnp.where(v >= rows, v - rows, v)
        return jnp.where(v < 0, v + rows, v)

    def rotations(at):
        down = (lax.broadcasted_iota(jnp.int32, (64, rows), 0) + at).astype(F32)
        along = lax.broadcasted_iota(jnp.int32, (64, rows), 1).astype(F32)
        roll_s[pl.ds(at, 64)] = jnp.where(wrapped(down + turn_here) == along, 1.0, 0.0).astype(BF16)
        back_s[pl.ds(at, 64)] = jnp.where(wrapped(down - turn_here) == along, 1.0, 0.0).astype(BF16)
        where = wrapped((lax.broadcasted_iota(jnp.int32, (64, 128), 0) + at).astype(F32) + turn)
        mine = sum(jnp.where(where >= starts[v], 1.0, 0.0) for v in range(1, 4))
        slot = (lax.broadcasted_iota(jnp.int32, (64, 128), 1) % HEAD).astype(F32)
        sq_s[pl.ds(at, 64)] = jnp.where((slot < 4) & (slot != mine), 1.0, 0.0).astype(BF16)
        sk_s[pl.ds(at, 64)] = jnp.where(slot == mine, NEG_LARGE, 0.0).astype(BF16)


    pl.semaphore_wait(barrier, len(partners))
    unit_copy = remote(bias_u, uoth, wsem, 3 * (4 + 2 * (units // BLOCK)), across)
    head_copy = remote(bias_qv, voth, wsem, 3 * (4 + 2 * (units // BLOCK)) + 1, across)
    get_wq.wait()
    get_wo.wait()
    for copy in get_w1:
        copy.wait()
    get_w2.wait()

    part = (sides[0] + sides[1]) % 2

    class Piece:
        def __init__(self, index, refs, at, extent):
            size = extent // 4

            def some(k, first, size):
                return refs[k].at[pl.ds(aligned(at[k] + part * (extent // 2) + first, 16), size)]

            self.copies = [described(some(0, 0, 2 * size), some(1, 0, 2 * size), wsem, 3 * index, across)]
            for k in range(2):
                block = some(1, k * size, size)
                self.copies.append(described(block, block, wsem, 3 * index + 1 + k, mates[k]))
            self.stage = 0

        def advance(self):
            if self.stage == 0:
                self.copies[0].wait_recv()
                self.copies[1].start()
                self.copies[2].start()
            else:
                self.copies[1].wait_recv()
                self.copies[2].wait_recv()
            self.stage += 1

    pieces = [Piece(c, (wq_s.at[0, c], wq_s.at[1, c]), (0, 0), quarter) for c in range(3)]
    pieces.append(Piece(3, (wo_s, wo_s), (0, quarter), quarter))
    for i in range(units // BLOCK):
        pieces.append(Piece(4 + 2 * i, (w1_s.at[0, i], w1_s.at[1, i]), (0, 0), width))
        pieces.append(Piece(5 + 2 * i, (w2_s.at[0], w2_s.at[1]), (i * BLOCK, i * BLOCK), BLOCK))
    for item in pieces:
        item.copies[0].start()

    inside_loop = []

    def service(name, act):
        def at_point(k, ask):
            full = f"{name}{k}"
            if ask:
                return full in PLAN or full in WEIGHT_PLAN
            inside_loop.append(full)
            act(full)
            inside_loop.pop()

        return at_point

    def pass_on(name):
        for i in WEIGHT_PLAN.get(name, ()):
            if pieces[i].stage < 1:
                pieces[i].advance()

    def have_weight(*which):
        for i in which:
            while pieces[i].stage < 2:
                pieces[i].advance()

    n1_copy = remote(n1_s.at[pl.ds(0, count)], n1_s.at[pl.ds(count, count)], csem, 0, sib)
    get_cot.wait()
    cot_copy = remote(cot_s.at[pl.ds(0, count)], cot_s.at[pl.ds(count, count)], csem, 1, sib)

    def rotate(at):
        nr_s[pl.ds(at, BLOCK)] = dot(roll_s[pl.ds(at, BLOCK)], n1_s[...]).astype(BF16)

    def project(j, at):
        n = nr_s[pl.ds(at, BLOCK)]
        biases = bias_qv if j == 0 else voth
        q = (dot_nt(n, wq_s[j, 0]) + biases[0:1]).astype(BF16) * SCALE
        k = dot_nt(n, wq_s[j, 1]).astype(BF16)
        v = (dot_nt(n, wq_s[j, 2]) + biases[1:2]).astype(BF16)
        q_s[j, pl.ds(at, BLOCK), :quarter] = q
        k_s[pl.ds(at, BLOCK), :quarter] = k
        v_s[j, pl.ds(at, BLOCK), :quarter] = v
        kt_s[j * quarter : (j + 1) * quarter, pl.ds(at, BLOCK)] = k.T * SCALE

    blocks = [(b, at) for b in range(2) for at in range(0, count, BLOCK)]

    def attend(j):
        for head in range(heads):
            at = 512 + 256 * head
            a_s[:, at : at + 128] = head_lanes(q_s.at[j], head, sq_s[...])
            a_s[:, at + 128 : at + 256] = head_lanes(k_s, head, sk_s[...])
        for at in range(0, rows, BLOCK):
            ou_s[:quarter, at : at + BLOCK] = v_s[j, at : at + BLOCK, :quarter].T

        def tile(here):
            b = here // count
            at = aligned(here % count, BLOCK)
            keys = pl.ds(aligned(b * count, count), count)
            for head in range(heads):
                column = 512 + 256 * head
                s = dot_nt(a_s[keys, column + 128 : column + 256], a_s[pl.ds(here, BLOCK), column : column + 128])
                m = jnp.max(s, axis=0, keepdims=True)
                e = jnp.exp(s - m)
                r = 1.0 / column_sum(e)
                low = e.astype(BF16)
                span = slice(head * HEAD, head * HEAD + HEAD)
                to = slice(j * quarter + head * HEAD, j * quarter + head * HEAD + HEAD)
                e_s[j * heads + head, b, :, pl.ds(at, BLOCK)] = low
                ot_s[to, pl.ds(here, BLOCK)] = (dot(ou_s[span, keys], low) * r).astype(BF16)
                r_s[j * heads + head : j * heads + head + 1, pl.ds(here, BLOCK)] = r

        return tile

    loop(rows, 64, rotations)
    n1_copy.wait_recv()
    loop(rows, BLOCK, rotate)
    loop(rows, BLOCK, lambda at: project(0, at))
    pass_on("p0")
    loop(rows, BLOCK, attend(0), service("a", pass_on))
    head_copy.wait_recv()
    have_weight(0, 1, 2)
    loop(rows, BLOCK, lambda at: project(1, at))
    pass_on("p1")
    loop(rows, BLOCK, attend(1), service("c", pass_on))

    have_weight(3)

    def unrotate(at):
        ou_s[:, pl.ds(at, BLOCK)] = dot(ot_s[...], roll_s[:, pl.ds(at, BLOCK)]).astype(BF16)

    loop(rows, BLOCK, unrotate)
    pass_on("u")

    def out_part(at):
        return dot_tn(ou_s[:, pl.ds(at, BLOCK)], wo_s[...])

    def att_half(at):
        return half_copy(sb1.at[pl.ds(at, BLOCK)], rb1.at[pl.ds(at, BLOCK)], 2, at)

    def n2_half(at):
        return half_copy(n2_s.at[pl.ds(at, BLOCK)], n2_s.at[pl.ds(aligned(count + at, BLOCK), BLOCK)], 4, at)

    def out_sib(at):
        sb1[pl.ds(at, BLOCK)] = out_part(count + at).astype(BF16)
        att_half(at).start()

    loop(count, BLOCK, out_sib)

    def out_mine(at):
        mid_s[pl.ds(at, BLOCK)] = sin_s[pl.ds(at, BLOCK)] + out_part(at) + out_bias

    loop(count, BLOCK, out_mine)
    pass_on("o")

    def second_norm(at):
        att_half(at).wait_recv()
        for off in range(0, BLOCK, 128):
            spot = pl.ds(aligned(at + off, 128), 128)
            mid = mid_s[spot] + rb1[spot].astype(F32)
            mid_s[spot] = mid
            xhat, _ = norm_stats(mid)
            n2_s[spot] = (xhat * ln2_gain + ln2_bias).astype(BF16)
        n2_half(at).start()

    loop(count, BLOCK, second_norm)
    pass_on("n")

    base_a = units
    parts = units // BLOCK
    steps = copies_of(len(full_bits))

    class Region:
        def __init__(self, index, row, size, cols, slot, kind, refs, to):
            own_r, oth_r, xr_r, land_r, both_r, rx_r = refs
            self.place, self.slot, self.to, self.xr = (row, size, 0, cols), slot, to, xr_r
            first, after = KINDS[kind]
            self.first = first is not None
            self.stages, self.stage, self.finished, self.sent = [], -1, False, []
            now, parts, used, trail = self.place, 8, 0, []
            sems = iter(range(index * steps, (index + 1) * steps))

            def copy(src, src_at, dst, dst_at, device):
                return described(src.at[self.window(src_at)], dst.at[self.window(dst_at)], gsem, next(sems), device)

            def piece(bits, mask):
                where = now
                for k, b in enumerate(bits):
                    where = self.cut(where, 1 - sides[b] if mask >> k & 1 else sides[b])
                return where

            sums = 1 + len(after) + len(full_bits)
            if self.first:
                keep, give, there = piece((first,), 0), piece((first,), 1), (row // 2, size // 2, 0, cols)
                place = self.landing(0, 4)
                copies = [copy(own_r, give, land_r, place, mate((first,))), copy(oth_r, give, both_r, there, mate((first,)))]
                adds = [(own_r, own_r, keep, [(land_r, place)]), (oth_r, oth_r, keep, [(both_r, there)])]
                self.stages.append((copies, adds, False))
                trail.append(((first,), keep))
                now, parts, used = keep, 4, 4
            self.stages.append(([copy(oth_r, now, xr_r, now, across)], [(own_r, own_r, now, [(xr_r, now)])], False))
            for bits in after:
                parts >>= len(bits)
                keep, copies, terms = piece(bits, 0), [], []
                for mask in range(1, 1 << len(bits)):
                    place = self.landing(used, parts)
                    used += parts
                    terms.append((land_r, place))
                    copies.append(copy(own_r, piece(bits, mask), land_r, place, mate([b for k, b in enumerate(bits) if mask >> k & 1])))
                self.stages.append((copies, [(own_r, own_r, keep, terms)], False))
                trail.append((bits, keep))
                now = keep
            for i, b in enumerate(full_bits):
                place = self.small_place()
                self.stages.append(([copy(own_r, now, rx_r[i], place, mates[b])], [(own_r, own_r, now, [(rx_r[i], place)])], True))
            copies, adds, full = self.stages[-1]
            self.stages[-1] = (copies, [(xr_r,) + adds[0][1:]], full)
            for bits, keep in reversed(trail):
                copies = []
                for mask in range(1, 1 << len(bits)):
                    copies.append(copy(xr_r, keep, xr_r, keep, mate([b for k, b in enumerate(bits) if mask >> k & 1])))
                self.stages.append((copies, [], False))

        def window(self, where):
            row, size, col, cols = where
            return pl.ds(row, size), pl.ds(col, cols)

        def cut(self, where, side):
            row, size, col, cols = where
            if (size // 2) % 16 == 0:
                return aligned(row + side * (size // 2), 16), size // 2, col, cols
            return row, size, aligned(col + side * (cols // 2), 128), cols // 2

        def landing(self, at, parts_here):
            row, rows_one, cols_one = self.slot
            full = self.place[3]
            if cols_one == full:
                return row + at * rows_one, parts_here * rows_one, 0, full
            if parts_here == 1:
                return row + at // 2 * rows_one, rows_one, at % 2 * cols_one, cols_one
            return row + at // 2 * rows_one, parts_here // 2 * rows_one, 0, full

        def small_place(self):
            row, rows_one, cols_one = self.slot
            if cols_one == self.place[3]:
                return row // 7, rows_one, 0, cols_one
            k = (self.place[0] - base_a) // quarter
            return units // 8 + k // 2 * rows_one, rows_one, k % 2 * cols_one, cols_one

        def begin(self, copies):
            for copy in copies:
                copy.start()
            self.sent += copies

        def ready(self, j):
            if self.first:
                self.stage = 0
                self.begin([self.stages[0][0][j]])
            elif j == 1:
                self.stage = 0
                self.begin(self.stages[0][0])

        def add(self, into, base, where, terms):
            row, size, col, cols = where
            step = 64 if size % 64 == 0 else 48 if size % 48 == 0 else 32

            def body(off):
                to = (pl.ds(aligned(row + off, 16), step), pl.ds(col, cols))
                parts_in = [ref[pl.ds(aligned(r + off, 16), step), pl.ds(c, cols)] for ref, (r, _, c, _) in terms]
                if len(parts_in) == 1:
                    into[to] = base[to] + parts_in[0]
                else:
                    into[to] = sum((v.astype(F32) for v in parts_in), base[to].astype(F32)).astype(BF16)

            if inside_loop:
                for off in range(0, size, step):
                    body(off)
            else:
                loop(size, step, body)

        def advance(self):
            if self.finished or self.stage < 0:
                return
            copies, adds, full = self.stages[self.stage]
            for copy in copies:
                copy.wait_recv()
            if full:
                for copy in copies:
                    copy.wait_send()
                self.sent = [c for c in self.sent if all(c is not d for d in copies)]
            for item in adds:
                self.add(*item)
            self.stage += 1
            if self.stage < len(self.stages):
                self.begin(self.stages[self.stage][0])
                return
            self.finished = True
            to_write.append(self)

    chunks = []
    refs = (own, oth, xr, land, land_both, rx)
    for i in range(parts):
        slot = (i * 7 * (BLOCK // 8), BLOCK // 8, width)
        to = g2_h.at[pl.ds(i * BLOCK, BLOCK)]
        chunks.append(Region(2 * i, i * BLOCK, BLOCK, width, slot, ORDERS[2 * i], refs, to))
        refs_one = tuple(ref.at[i] for ref in (own1, oth1, xr1, land1, land1_both)) + ([ref.at[i] for ref in rx1],)
        to = g1_h.at[:, pl.ds(i * BLOCK, BLOCK)]
        chunks.append(Region(2 * i + 1, 0, width, BLOCK, (0, width // 8, BLOCK), ORDERS[2 * i + 1], refs_one, to))
    for i in range(4):
        slot = (7 * units // 8 + i * quarter, quarter // 4, width // 2)
        to = go_h if i == 0 else gq_h.at[i - 1]
        chunks.append(Region(2 * parts + i, base_a + i * quarter, quarter, width, slot, ORDERS[2 * parts + i], refs, to))
    first_att = 2 * parts

    class Small:
        def __init__(self, tile, index, everywhere, paired, groups):
            self.tile, self.everywhere, self.paired = tile, everywhere, paired
            landings = [near.at[3 * index + k] for k in range(3)] + [far.at[(7 + len(full_bits)) * index + k] for k in range(7 + len(full_bits))]
            sems = iter(range(index * len(landings), (index + 1) * len(landings)))
            landings = iter(landings)

            def stage(devices):
                places = [next(landings) for _ in devices]
                return places, [described(tile, dst, ssem, next(sems), d) for dst, d in zip(places, devices)]

            self.stages = [stage([sib, across, facing])]
            for bits in groups + [(b,) for b in full_bits]:
                masks = range(1, 1 << len(bits))
                self.stages.append(stage([mate([b for k, b in enumerate(bits) if mask >> k & 1]) for mask in masks]))
            self.stage, self.finished = -1, False

        def start(self):
            self.stage = 0
            for copy in self.stages[0][1]:
                copy.start()

        def advance(self):
            if self.finished or self.stage < 0:
                return
            places, copies = self.stages[self.stage]
            for copy in copies:
                copy.wait()
            tile = self.tile
            if self.stage == 0:
                beside, over, facing_ = places
                n, p = self.everywhere, self.paired
                tile[0:n] = (tile[0:n] + beside[0:n]) + (over[0:n] + facing_[0:n])
                tile[n : n + p] = tile[n : n + p] + over[n + p : n + 2 * p]
            else:
                got = [tile[...]] + [place[...] for place in places]
                while len(got) > 1:
                    got = [got[k] + got[k + 1] for k in range(0, len(got), 2)]
                tile[...] = got[0]
            self.stage += 1
            if self.stage == len(self.stages):
                self.finished = True
                return
            for copy in self.stages[self.stage][1]:
                copy.start()

    first_small = Small(early, 0, 4, 1, [(b,) for b in half_bits])
    last_small = Small(late, 1, 2, 2, [tuple(half_bits)])

    def ready(i, j):
        chunks[i].ready(j)

    to_write = []

    def write_finished():
        while to_write:
            region = to_write.pop()
            region.done = local(region.xr.at[region.window(region.place)], region.to)

    def hook(name):
        pass_on(name)
        for i in PLAN.get(name, ()):
            (chunks + [last_small, first_small])[i].advance()
            if not inside_loop:
                write_finished()

    def chunk_rows(j, i, at):
        span = pl.ds(at, BLOCK)
        cols = slice(j * units + i * BLOCK, j * units + (i + 1) * BLOCK)
        mine = slice(i * BLOCK, (i + 1) * BLOCK)
        bias = (bias_u if j == 0 else uoth)[mine].reshape(1, BLOCK)
        h = dot(n2_s[span], w1_s[j, i]) + bias
        a, slope = gelu_pair(h)
        a_s[span, cols] = a.astype(BF16)
        g = (dot_nt(cot_s[span], w2_s[j, mine]) * slope).astype(BF16)
        g_s[span, cols] = g

    def chunk_grads(j, i):
        cols = slice(j * units + i * BLOCK, j * units + (i + 1) * BLOCK)
        mine = slice(i * BLOCK, (i + 1) * BLOCK)
        to = oth if j == 1 else own

        def second(at):
            to[pl.ds(i * BLOCK + at, 128)] = dot_tn(a_s[:, pl.ds(cols.start + at, 128)], cot_s[...]).astype(BF16)

        loop(BLOCK, 128, second)
        ready(2 * i, j)
        g = g_s[:, cols]

        def first(at):
            (oth1 if j == 1 else own1)[i, pl.ds(at, BLOCK)] = dot(n2t_s[pl.ds(at, BLOCK)], g_s[:, cols]).astype(BF16)

        loop(width, BLOCK, first)
        ready(2 * i + 1, j)
        early[4 + j : 5 + j, mine] = column_sum(g.astype(F32))
        hook(f"f{j}{i}")

    def feed(j, i, first=False):
        if first:
            loop(count, BLOCK, lambda at: chunk_rows(j, i, at))
            hook(f"r{j}{i}.0")
            cot_copy.wait_recv()

            def received(at):
                n2_half(at).wait_recv()
                chunk_rows(j, i, count + at)

            loop(count, BLOCK, received)
            hook(f"r{j}{i}.1")

            def turned(at):
                n2t_s[:, pl.ds(at, BLOCK)] = n2_s[pl.ds(at, BLOCK)].T

            loop(rows, BLOCK, turned)
        else:
            loop(rows, BLOCK, lambda at: chunk_rows(j, i, at), service(f"r{j}{i}.", hook), 2)
        chunk_grads(j, i)

    early[...] = jnp.zeros_like(early)
    late[...] = jnp.zeros_like(late)
    unit_copy.wait_recv()
    for i in range(parts):
        have_weight(4 + 2 * i, 5 + 2 * i)
        feed(1, i, first=i == 0)
        feed(0, i)

    def back_two(at):
        span = pl.ds(at, BLOCK)
        total = None
        for j in range(2):
            for i in range(parts):
                at_col = j * units + i * BLOCK
                term = dot_nt(g_s[span, at_col : at_col + BLOCK], w1_s[j, i])
                total = term if total is None else total + term
        return total

    def mlp_part(at):
        span = pl.ds(at, BLOCK)
        return dot(a_s[span, :units], w2_s[0]) + dot(a_s[span, units:], w2_s[1])

    def gn2_half(at):
        return half_copy(sb2.at[pl.ds(at, BLOCK)], rb2.at[pl.ds(at, BLOCK)], 6, at)

    def dm_half(at):
        return half_copy(n2_s.at[pl.ds(at, BLOCK)], n2_s.at[pl.ds(aligned(count + at, BLOCK), BLOCK)], 10, at)

    def back_two_sib(at):
        sb2[pl.ds(at, BLOCK)] = back_two(count + at).astype(BF16)
        gn2_half(at).start()

    def back_two_mine(at):
        gm_s[pl.ds(at, BLOCK)] = back_two(at)

    def mlp_sib(at):
        sb1[pl.ds(at, BLOCK)] = mlp_part(count + at).astype(BF16)

    loop(count, BLOCK, back_two_sib)
    hook("g0")
    loop(count, BLOCK, back_two_mine)
    hook("gn2")

    def second_back(at):
        gn2_half(at).wait_recv()
        n2_half(at).wait_send()
        for off in range(0, BLOCK, 128):
            spot = pl.ds(aligned(at + off, 128), 128)
            xhat, sigma = norm_stats(mid_s[spot])
            grad = gm_s[spot] + rb2[spot].astype(F32)
            cot = cot_s[spot].astype(F32)
            back = cot + norm_back(grad, ln2_gain, xhat, sigma)
            gm_s[spot] = back
            n2_s[spot] = back.astype(BF16)
            early[0:1] += column_sum(back)
            early[1:2] += column_sum(grad * xhat)
            early[2:3] += column_sum(grad)
            early[3:4] += column_sum(cot)
        dm_half(at).start()

    loop(count, BLOCK, second_back)
    hook("lb")
    for at in range(0, count, BLOCK):
        att_half(at).wait_send()
    loop(count, BLOCK, mlp_sib)
    mlp_copy = remote(sb1, rb1, csem, 8, sib)
    first_small.start()
    hook("ln2")

    for at in range(0, count, BLOCK):
        dm_half(at).wait_recv()

    start = base_a + quarter
    zero = jnp.zeros((count, 128), BF16)
    grad_s = dq_s = ou_s
    n1_copy.wait_send()

    def keep_gradient(j, c):
        to = oth if j == 1 else own
        low = start + c * quarter
        dt = ot_s.at[j * quarter : (j + 1) * quarter]

        def columns(at):
            to[low : low + quarter, pl.ds(at, BLOCK)] = dot(dt[...], nr_s[:, pl.ds(at, BLOCK)]).astype(BF16)

        loop(width, BLOCK, columns)
        ready(first_att + 1 + c, j)
        if c != 1:
            d = g_s[:, (3 * j + c) * BLOCK : (3 * j + c) * BLOCK + quarter]
            late[2 + c // 2 + 2 * j : 3 + c // 2 + 2 * j, :quarter] = column_sum(d.astype(F32))

    def values_back(j):
        base = j * quarter
        to = oth if j == 1 else own

        def weight(at):
            to[base_a : base_a + quarter, pl.ds(at, BLOCK)] = dot(ou_s[base : base + quarter], n2_s[:, pl.ds(at, BLOCK)]).astype(BF16)

        loop(width, BLOCK, weight)
        ready(first_att, j)

        def output(at):
            grad_s[base : base + quarter, pl.ds(at, BLOCK)] = dot_nt(wo_s[base : base + quarter], n2_s[pl.ds(at, BLOCK)]).astype(BF16)

        loop(rows, BLOCK, output)
        hook(f"w{j}.0")
        go_s = n1_s.at[:, 256 * j : 256 * (j + 1)]

        def scale(at):
            here = pl.ds(at, BLOCK)
            grad_t = dot_nt(grad_s[base : base + quarter], roll_s[here])
            for head in range(heads):
                row = j * heads + head
                r = r_s[row : row + 1, here]
                g = grad_t[head * HEAD : (head + 1) * HEAD]
                at_head = slice(base + head * HEAD, base + (head + 1) * HEAD)
                in_s[row : row + 1, here] = column_sum(g * ot_s[at_head, here].astype(F32)) * r
                gt_s[at_head, here] = (g * r).astype(BF16)
            go_s[here, :quarter] = gt_s[base : base + quarter, here].T

        loop(rows, BLOCK, scale)

        def block(at):
            here = pl.ds(at, count)
            b = at // count
            dv = [None, None]
            for head in range(heads):
                tile = head // 2
                gh = jnp.where(lane_half(count, head % 2 == 1), go_s[here, 128 * tile : 128 * tile + 128], zero)
                part = dot(e_s[j * heads + head, b], gh)
                dv[tile] = part if dv[tile] is None else dv[tile] + part
            dv = jnp.concatenate(dv, axis=1)[:, :quarter].astype(BF16)
            g_s[here, (3 * j + 2) * BLOCK : (3 * j + 2) * BLOCK + quarter] = dv
            ot_s[base : base + quarter, here] = dv.T

        loop(rows, count, block)
        hook(f"w{j}.1")
        keep_gradient(j, 2)
        hook(f"v{j}")

    def scores_back(j):
        base = j * quarter

        def block(at):
            here = pl.ds(at, count)
            b = at // count
            dk = [None, None]
            for head in range(heads):
                tile = head // 2
                row = j * heads + head
                half = lane_half(count, head % 2 == 1)
                lanes = slice(128 * tile, 128 * tile + 128)
                vh = jnp.where(half, v_s[j, here, lanes], zero)
                qh = jnp.where(half, q_s[j, here, lanes], zero)
                last_row = min(128 * tile + 128, quarter)
                vh = vh[:, : last_row - 128 * tile]
                ds = n2t_s.at[:count, head * count : (head + 1) * count] if head < 2 else ds_s
                for off in range(0, count, BLOCK):
                    some = pl.ds(aligned(at + off, BLOCK), BLOCK)
                    dp_t = dot(vh, gt_s[base + 128 * tile : base + last_row, some])
                    grad = (dp_t - in_s[row : row + 1, some]).astype(BF16)
                    ds[:, off : off + BLOCK] = grad * e_s[row, b, :, off : off + BLOCK]
                part = dot(ds[...], qh)
                dk[tile] = part if dk[tile] is None else dk[tile] + part
                kth = kt_s[base + head * HEAD : base + head * HEAD + HEAD, here]
                dq_s[base + head * HEAD : base + head * HEAD + HEAD, here] = dot(kth, ds[...]).astype(BF16)
            dk = jnp.concatenate(dk, axis=1)[:, :quarter].astype(BF16)
            g_s[here, (3 * j + 1) * BLOCK : (3 * j + 1) * BLOCK + quarter] = dk
            ot_s[base : base + quarter, here] = dk.T
            g_s[here, 3 * j * BLOCK : 3 * j * BLOCK + quarter] = dq_s[base : base + quarter, here].T

        loop(rows, count, block, service(f"b{j}.", hook))
        keep_gradient(j, 1)
        hook(f"k{j}")
        ot_s[base : base + quarter] = dq_s[base : base + quarter]
        keep_gradient(j, 0)
        hook(f"s{j}")

    values_back(1)
    scores_back(1)
    values_back(0)
    scores_back(0)

    def finish_out(at):
        span = pl.ds(at, BLOCK)
        mid_s[span] = mid_s[span] + mlp_part(at) + fc2_bias

    loop(count, BLOCK, finish_out)
    hook("fo")
    mlp_copy.wait_recv()

    def write_out(at):
        spot = pl.ds(at, 128)
        tok_s[spot] = (mid_s[spot] + rb1[spot].astype(F32)).astype(BF16)

    loop(count, 128, write_out)
    put_out = local(tok_s, out_h)
    hook("fin")

    def back_one(at):
        total = None
        for j in range(2):
            for c in range(3):
                d = g_s[pl.ds(at, BLOCK), (3 * j + c) * BLOCK : (3 * j + c) * BLOCK + quarter]
                term = dot(d, wq_s[j, c])
                total = term if total is None else total + term
        n2_s[pl.ds(at, BLOCK)] = total.astype(BF16)

    for at in range(0, count, BLOCK):
        dm_half(at).wait_send()
    loop(rows, BLOCK, back_one, service("d.", hook), 2)
    for at in range(0, count, BLOCK):
        gn2_half(at).wait_send()

    def gn1_half(at):
        return half_copy(sb2.at[pl.ds(at, BLOCK)], rb2.at[pl.ds(at, BLOCK)], 12, at)

    def back_one_sib(at):
        sb2[pl.ds(at, BLOCK)] = dot(back_s[pl.ds(count + at, BLOCK)], n2_s[...]).astype(BF16)
        gn1_half(at).start()

    def back_one_mine(at):
        mid_s[pl.ds(at, BLOCK)] = dot(back_s[pl.ds(at, BLOCK)], n2_s[...])

    loop(count, BLOCK, back_one_sib)
    loop(count, BLOCK, back_one_mine)
    hook("e.0")
    mlp_copy.wait_send()

    def first_back(at):
        gn1_half(at).wait_recv()
        for off in range(0, BLOCK, 128):
            spot = pl.ds(aligned(at + off, 128), 128)
            xhat, sigma = norm_stats(sin_s[spot])
            grad = mid_s[spot] + rb2[spot].astype(F32)
            sb1[spot] = (gm_s[spot] + norm_back(grad, ln1_gain, xhat, sigma)).astype(BF16)
            late[0:1] += column_sum(grad * xhat)
            late[1:2] += column_sum(grad)

    loop(count, BLOCK, first_back)
    put_in = local(sb1, ing_h)
    last_small.start()
    hook("e.1")
    hook("tail")
    left = [first_small, last_small] + chunks
    while left:
        for item in left:
            item.advance()
            write_finished()
        left = [item for item in left if not item.finished]

    for row, source, at in ((0, late, 0), (1, late, 1), (2, early, 0), (3, early, 1), (4, early, 2), (5, early, 3), (8, early, 4), (9, late, 2), (10, late, 3)):
        small_o[row : row + 1] = source[at : at + 1]

    passed = [copy for item in pieces for copy in item.copies]
    for copy in [unit_copy, head_copy, cot_copy] + [gn1_half(at) for at in range(0, count, BLOCK)] + passed:
        copy.wait_send()
    for chunk in chunks:
        for copy in chunk.sent:
            copy.wait_send()
        chunk.done.wait()
    put_out.wait()
    put_in.wait()


def copies_of(full):
    most = 0
    for kind in ORDERS:
        first, after = KINDS[kind]
        most = max(most, 1 + full + 2 * sum((1 << len(bits)) - 1 for bits in after) + (0 if first is None else 3))
    return most


def call_layer(dp_size, tokens, cotangent, ids, table, vectors, wq, wo, w1, w2):
    count, width = tokens.shape
    rows = 2 * count
    quarter = wo.shape[0]
    units = w1.shape[1]
    heads = quarter // HEAD
    grad_rows = units + 4 * quarter
    parts = units // BLOCK
    bits = [b for b in range(20) if (1 << b) < dp_size]
    half_bits = bits[:3]
    shape = jax.ShapeDtypeStruct
    vm = pltpu.VMEM
    regions = 2 * (units // BLOCK) + 4
    steps = copies_of(len(bits) - len(half_bits))
    fetched = 4 + 2 * (units // BLOCK)
    scratch = (
        [vm((count, width), BF16), vm((rows, width), BF16)]
        + [vm((count, width), F32)] * 3
        + [vm((rows, width), BF16)] * 2
        + [vm((width, rows), BF16)]
        + [vm((2,) + wq.shape, BF16), vm((2 * quarter, width), BF16), vm((2, units // BLOCK, width, BLOCK), BF16), vm((2,) + w2.shape, BF16)]
        + [vm((2, rows, 256), BF16)] * 2
        + [vm((2 * quarter, rows), BF16)] * 4
        + [vm((8, rows), F32)] * 2
        + [vm((2 * heads, 2, count, count), BF16)]
        + [vm((rows, rows), BF16)] * 2
        + [vm((rows, width), BF16), vm((count, count), BF16)]
        + [vm((rows, 2 * units), BF16)] * 2
        + [vm((count, width), BF16)] * 4
        + [vm((grad_rows, width), BF16)] * 3
        + [vm((7 * units // 8 + 4 * quarter, width), BF16), vm((units // 2, width), BF16)]
        + [vm((parts, width, BLOCK), BF16)] * 3
        + [vm((parts, 7 * width // 8, BLOCK), BF16), vm((parts, width // 2, BLOCK), BF16)]
        + [vm((grad_rows >> len(half_bits), width), BF16)] * (len(bits) - len(half_bits))
        + [vm((parts, width // 8, BLOCK), BF16)] * (len(bits) - len(half_bits))
        + [vm((units,), F32), vm((2, quarter), F32), vm((8, width), F32), vm((8, width), F32)]
        + [vm((6, 8, width), F32), vm((14 + 2 * (len(bits) - 3), 8, width), F32)]
        + [pltpu.SemaphoreType.DMA((8 + units // BLOCK + regions,))]
        + [pltpu.SemaphoreType.DMA((2, n)) for n in (3 * fetched + 2, 14, regions * steps, 2 * (10 + len(bits) - 3))]
    )
    anywhere = pl.BlockSpec(memory_space=pl.ANY)
    inside = pl.BlockSpec(memory_space=pltpu.VMEM)
    return pl.pallas_call(
        functools.partial(layer, dp_size, half_bits),
        out_shape=[shape((count, width), BF16)] * 2
        + [shape(w2.shape, BF16), shape(w1.shape, BF16), shape(wo.shape, BF16), shape(wq.shape, BF16), shape((16, width), F32)],
        in_specs=[anywhere] * 2 + [inside] * (2 + len(vectors)) + [anywhere] * 4,
        out_specs=[anywhere] * 6 + [inside],
        scratch_shapes=scratch,
        compiler_params=pltpu.CompilerParams(vmem_limit_bytes=VMEM_LIMIT, collective_id=0, has_side_effects=True),
        name="layer",
    )(tokens, cotangent, ids, table, *vectors, wq, wo, w1, w2)


def finish(*refs):
    sources, small, rest = refs[:6], refs[6], refs[7:]
    results, vectors, rest = rest[:6], rest[6:14], rest[14:]
    narrow, wide, (get, put) = rest[:6], rest[6:10], rest[10:]
    blocks = []
    for k, src in enumerate(sources):
        if src.ndim == 3:
            places = list(range(src.shape[0]))
        else:
            step = min(BLOCK, src.shape[0])
            places = [pl.ds(at, step) for at in range(0, src.shape[0], step)]
        for at in places:
            low = narrow[k].at[at]
            blocks.append((src.at[at], low, low if k < 2 else wide[k - 2].at[at], results[k].at[at]))
    reads = [pltpu.make_async_copy(src, low, get.at[n]) for n, (src, low, _, _) in enumerate(blocks)]
    writes = [pltpu.make_async_copy(high, dst, put.at[n]) for n, (_, _, high, dst) in enumerate(blocks)]
    for copy in reads:
        copy.start()
    for i in range(6):
        vectors[i][...] = small[i]
    vectors[6][...] = small[8, : vectors[6].shape[0]]
    vectors[7][...] = small[9:11, : vectors[7].shape[1]]
    for read, write, (_, low, high, _) in zip(reads, writes, blocks):
        read.wait()
        if high is not low:

            def cast(at, low=low, high=high):
                high[pl.ds(at, 64)] = low[pl.ds(at, 64)].astype(F32)

            loop(low.shape[0], 64, cast)
        write.start()
    for copy in writes:
        copy.wait()


def call_finish(arrays, small, units, quarter):
    width = small.shape[1]
    shape = jax.ShapeDtypeStruct
    extents = [(width,)] * 6 + [(units,), (2, quarter)]
    kinds = [BF16, BF16, F32, F32, F32, F32]
    anywhere = pl.BlockSpec(memory_space=pl.ANY)
    inside = pl.BlockSpec(memory_space=pltpu.VMEM)
    grads = arrays[2:]
    return pl.pallas_call(
        finish,
        in_specs=[anywhere] * len(arrays) + [inside],
        out_specs=[anywhere] * len(arrays) + [inside] * len(extents),
        out_shape=[shape(a.shape, k) for a, k in zip(arrays, kinds)] + [shape(e, F32) for e in extents],
        scratch_shapes=[pltpu.VMEM(a.shape, BF16) for a in arrays]
        + [pltpu.VMEM(a.shape, F32) for a in grads]
        + [pltpu.SemaphoreType.DMA((16,)), pltpu.SemaphoreType.DMA((16,))],
        compiler_params=pltpu.CompilerParams(vmem_limit_bytes=VMEM_LIMIT),
        name="finish",
    )(*arrays, small)


def per_device(
    tokens, segment_ids, ln1_gain, ln1_bias, qkv_weight, qv_bias, out_weight, out_bias,
    ln2_gain, ln2_bias, fc1_weight, fc1_bias, fc2_weight, fc2_bias, cotangent,
):
    width = tokens.shape[1]
    freq_count = width // 6
    frequency = 10000.0 ** (-jnp.arange(freq_count, dtype=F32) / freq_count)
    angles = jnp.arange(SIDE, dtype=F32)[:, None] * frequency[None, :]
    table = jnp.concatenate([jnp.sin(angles), jnp.cos(angles)], axis=1)
    vectors = (ln1_gain, ln1_bias, out_bias, ln2_gain, ln2_bias, fc2_bias, fc1_bias, qv_bias)
    *arrays, small = call_layer(
        lax.axis_size("dp"), tokens, cotangent, segment_ids, table, vectors, qkv_weight.transpose(0, 2, 1), out_weight, fc1_weight, fc2_weight
    )
    out, ing, g2, g1, go, gq, a0, a1, a2, a3, a4, a5, g_units, g_heads = call_finish(arrays, small, fc1_weight.shape[1], out_weight.shape[0])
    return (out, ing, a0, a1, gq.transpose(0, 2, 1), g_heads, go, a2, a3, a4, g1, g_units, g2, a5)


def solution(mesh):
    placed = (
        P(("dp", "tensor"), None),
        P("dp", None),
        P(),
        P(),
        P(None, None, "tensor"),
        P(None, "tensor"),
        P("tensor", None),
        P(),
        P(),
        P(),
        P(None, "tensor"),
        P("tensor"),
        P("tensor", None),
        P(),
        P(("dp", "tensor"), None),
    )
    return jax.shard_map(
        per_device,
        mesh=mesh,
        in_specs=placed,
        out_specs=(
            P(("dp", "tensor"), None),
            P(("dp", "tensor"), None),
            P(),
            P(),
            P(None, None, "tensor"),
            P(None, "tensor"),
            P("tensor", None),
            P(),
            P(),
            P(),
            P(None, "tensor"),
            P("tensor"),
            P("tensor", None),
            P(),
        ),
        check_vma=False,
    )
```

```python
import functools

import jax
import jax.numpy as jnp
from jax import lax
from jax.experimental import pallas as pl
from jax.experimental.pallas import tpu as pltpu
from jax.sharding import PartitionSpec as P

HEAD = 64
SIDE = 16
EPSILON = 1e-06
NEG_LARGE = -1e30
SCALE = HEAD ** (-0.5)
F32 = jnp.float32
BF16 = jnp.bfloat16
VMEM_LIMIT = 64 * 1024 * 1024 - 128 * 1024
MESH = pl.DeviceIdType.MESH
BLOCK = 256
KINDS = {
    "A": (None, ((0,), (1,), (2,))),
    "B": (None, ((1,), (0,), (2,))),
    "D": (None, ((0,), (1, 2))),
    "E": (None, ((0, 1, 2),)),
    "C": (None, ((0, 1), (2,))),
    "Y": (0, ((1,), (2,))),
    "Z": (1, ((0,), (2,))),
    "YD": (0, ((1, 2),)),
    "S": (None, (("p",), ("q",), (2,))),
    "SD": (None, (("p",), ("q", 2))),
    "SF": ("p", (("q",), (2,))),
    "SFD": ("p", (("q", 2),)),
}
ORDERS = ("D", "SFD", "SFD", "Z", "A", "YD", "D", "D", "C", "B")
WEIGHT_PLAN = {"p0": (0,), "a0": (1,), "a2": (2,), "p1": (3,), "c0": (4,), "c3": (5,), "n": (6,), "r10.1": (7,), "r00.1": (8,), "r11.1": (9,)}
PLAN = {
    "f01": (1,),
    "r12.1": (0,),
    "r02.0": (2,),
    "r02.1": (1,),
    "g0": (0,),
    "lb": (3, 4, 1),
    "w1.0": (2, 0),
    "w1.1": (-1, 5),
    "v1": (3,),
    "b1.0": (4, 1),
    "b1.1": (-1, 2, 3),
    "k1": (0,),
    "s1": (4, 5),
    "w0.0": (6, 1, -1),
    "v0": (2, 9),
    "b0.0": (0, 3, 4, 6),
    "b0.1": (2, 5),
    "k0": (8, -1, 9),
    "s0": (3,),
    "fo": (7, 4),
    "d.0": (6,),
    "d.1": (9,),
    "e.0": (5, 8, 3),
    "e.1": (4, 7),
    "tail": (6, 9, 8, -2, 5, 3, 4, 7, 9, 8, 6, -2, 9, 7, 8, 9, 7),
}


def dot(a, b):
    return jnp.dot(a, b, preferred_element_type=F32)


def dot_nt(a, b):
    return lax.dot_general(a, b, (((1,), (1,)), ((), ())), preferred_element_type=F32)


def dot_tn(a, b):
    return lax.dot_general(a, b, (((0,), (0,)), ((), ())), preferred_element_type=F32)


def lane_half(rows, upper):
    lanes = lax.broadcasted_iota(jnp.int32, (rows, 128), 1)
    return lanes >= HEAD if upper else lanes < HEAD


def head_lanes(ref, head, filler):
    tile = ref[:, 128 * (head // 2) : 128 * (head // 2) + 128]
    return jnp.where(lane_half(tile.shape[0], head % 2 == 1), tile, filler)


def gelu_pair(h):
    cdf = 0.5 + 0.5 * lax.erf(h * 0.7071067811865476)
    return h * cdf, cdf + h * jnp.exp(-0.5 * h * h) * 0.3989422804014327


def norm_stats(v):
    centred = v - jnp.mean(v, axis=-1, keepdims=True)
    sigma = lax.rsqrt(jnp.mean(centred * centred, axis=-1, keepdims=True) + EPSILON)
    return centred * sigma, sigma


def norm_back(grad, gain, xhat, sigma):
    g = grad * gain
    return sigma * (g - jnp.mean(g, axis=-1, keepdims=True) - xhat * jnp.mean(g * xhat, axis=-1, keepdims=True))


def column_sum(v):
    return jnp.sum(v, axis=0, keepdims=True)


def aligned(v, unit):
    return v if isinstance(v, int) else pl.multiple_of(v, unit)


def loop(count, step, body, service=None, every=1):
    def run(i, carry):
        body(aligned(i * step, step))
        if service is not None:
            for k in range(count // step // every):
                if service(k, True):
                    pl.when(i == every * (k + 1) - 1)(functools.partial(service, k, False))
        return carry

    lax.fori_loop(0, count // step, run, 0)


def layer(
    dp_size, half_bits,
    tok_h, cot_h, ids, table, gain1, bias1, bias_o, gain2, bias2, bias_f, bias_u, bias_qv, wq_h, wo_h, w1_h, w2_h,
    out_h, ing_h, g2_h, g1_h, go_h, gq_h, small_o,
    tok_s, cot_s, sin_s, mid_s, gm_s, n1_s, n2_s, n2t_s, wq_s, wo_s, w1_s, w2_s,
    q_s, v_s, kt_s, ot_s, ou_s, gt_s, r_s, in_s, e_s, roll_s, back_s, nr_s, ds_s, a_s, g_s, sb1, sb2, rb1, rb2,
    own, oth, xr, land, land_both, own1, oth1, xr1, land1, land1_both, *rest,
):
    rest = list(rest)
    full_bits = [b for b in range(20) if (1 << b) < dp_size and b not in half_bits]
    rx = [rest.pop(0) for _ in full_bits]
    rx1 = [rest.pop(0) for _ in full_bits]
    uoth, voth, early, late, near, far, lsem, wsem, csem, gsem, ssem = rest

    count, width = tok_s.shape
    rows = 2 * count
    quarter = wo_h.shape[0]
    units = w1_h.shape[1]
    heads = quarter // HEAD
    place = lax.axis_index("tensor")
    dp = lax.axis_index("dp")
    chip = place // 2
    core = place % 2
    sib = {"tensor": chip * 2 + 1 - core}
    across = {"tensor": (1 - chip) * 2 + core}
    facing = {"tensor": (1 - chip) * 2 + 1 - core}
    all_bits = list(half_bits) + full_bits
    sides = {b: (dp // (1 << b)) % 2 for b in all_bits}

    ways = {b: (1 - 2 * sides[b]) * (1 << b) for b in all_bits}
    sides["p"] = sides[0] + (sides[1] - sides[0]) * core
    sides["q"] = sides[1] + (sides[0] - sides[1]) * core
    ways["p"] = ways[0] + (ways[1] - ways[0]) * core
    ways["q"] = ways[1] + (ways[0] - ways[1]) * core

    def mate(bits):
        return {"dp": dp + sum(ways[b] for b in bits)}

    def described(src, dst, sems, index, device):
        return pltpu.make_async_remote_copy(
            src_ref=src, dst_ref=dst, send_sem=sems.at[0, index], recv_sem=sems.at[1, index], device_id=device, device_id_type=MESH
        )

    mates = {b: mate((b,)) for b in all_bits}
    groups = {(b,) for b in full_bits}
    for mask in range(1, 1 << len(half_bits)):
        groups.add(tuple(b for k, b in enumerate(half_bits) if mask >> k & 1))

    barrier = pltpu.get_barrier_semaphore()
    partners = [sib, across, facing] + [mate(bits) for bits in sorted(groups)]
    for partner in partners:
        pl.semaphore_signal(barrier, inc=1, device_id=partner, device_id_type=MESH)

    sq_s, sk_s, k_s = a_s.at[:, 0:128], a_s.at[:, 128:256], a_s.at[:, 256:512]
    local_used = [0]

    def local(src, dst):
        copy = pltpu.make_async_copy(src, dst, lsem.at[local_used[0]])
        local_used[0] += 1
        copy.start()
        return copy

    def remote(src, dst, sems, index, device):
        copy = pltpu.make_async_remote_copy(
            src_ref=src, dst_ref=dst, send_sem=sems.at[0, index], recv_sem=sems.at[1, index], device_id=device, device_id_type=MESH
        )
        copy.start()
        return copy

    def half_copy(src, dst, first, at):
        return pltpu.make_async_remote_copy(
            src_ref=src,
            dst_ref=dst,
            send_sem=csem.at[0, first + at // BLOCK],
            recv_sem=csem.at[1, first + at // BLOCK],
            device_id=sib,
            device_id_type=MESH,
        )

    get_wq = local(wq_h, wq_s.at[0])
    get_tok = local(tok_h, tok_s)
    get_cot = local(cot_h, cot_s.at[pl.ds(0, count)])
    get_wo = local(wo_h, wo_s.at[pl.ds(0, quarter)])
    get_w1 = [local(w1_h.at[:, pl.ds(i * BLOCK, BLOCK)], w1_s.at[0, i]) for i in range(units // BLOCK)]
    get_w2 = local(w2_h, w2_s.at[0])

    part = (sides[0] + sides[1]) % 2

    class Piece:
        def __init__(self, index, refs, at, extent):
            size = extent // 4

            def some(k, first, size):
                return refs[k].at[pl.ds(aligned(at[k] + part * (extent // 2) + first, 16), size)]

            self.copies = [described(some(0, 0, 2 * size), some(1, 0, 2 * size), wsem, 3 * index, across)]
            for k in range(2):
                block = some(1, k * size, size)
                self.copies.append(described(block, block, wsem, 3 * index + 1 + k, mates[k]))
            self.stage = 0

        def advance(self):
            if self.stage == 0:
                self.copies[0].wait_recv()
                self.copies[1].start()
                self.copies[2].start()
            else:
                self.copies[1].wait_recv()
                self.copies[2].wait_recv()
            self.stage += 1

    pieces = [Piece(c, (wq_s.at[0, c], wq_s.at[1, c]), (0, 0), quarter) for c in range(3)]
    pieces.append(Piece(3, (wo_s, wo_s), (0, quarter), quarter))
    for i in range(units // BLOCK):
        pieces.append(Piece(4 + 2 * i, (w1_s.at[0, i], w1_s.at[1, i]), (0, 0), width))
        pieces.append(Piece(5 + 2 * i, (w2_s.at[0], w2_s.at[1]), (i * BLOCK, i * BLOCK), BLOCK))
    pl.semaphore_wait(barrier, len(partners))
    unit_copy = remote(bias_u, uoth, wsem, 3 * len(pieces), across)
    head_copy = remote(bias_qv, voth, wsem, 3 * len(pieces) + 1, across)
    get_wq.wait()
    get_wo.wait()
    for item in pieces[:4]:
        item.copies[0].start()

    inside_loop = []

    def service(name, act):
        def at_point(k, ask):
            full = f"{name}{k}"
            if ask:
                return full in PLAN or full in WEIGHT_PLAN
            inside_loop.append(full)
            act(full)
            inside_loop.pop()

        return at_point

    def pass_on(name):
        for i in WEIGHT_PLAN.get(name, ()):
            if pieces[i].stage < 1:
                pieces[i].advance()

    def have_weight(*which):
        for i in which:
            while pieces[i].stage < 2:
                pieces[i].advance()

    ln1_gain, ln1_bias, out_bias, ln2_gain, ln2_bias, fc2_bias = (
        ref[...].reshape(1, width) for ref in (gain1, bias1, bias_o, gain2, bias2, bias_f)
    )
    get_tok.wait()

    def first_norm(at):
        plane = core * (count // (SIDE * SIDE)) + at // (SIDE * SIDE)
        line = (at // SIDE) % SIDE
        shape = (SIDE, width // 3)
        for k in range(4):
            spot = jnp.concatenate(
                [jnp.broadcast_to(table[pl.ds(plane, 1)], shape), jnp.broadcast_to(table[pl.ds(line + k, 1)], shape), table[...]], axis=1
            )
            span = pl.ds(aligned(at + k * SIDE, SIDE), SIDE)
            stream = tok_s[span].astype(F32) + spot
            sin_s[span] = stream
            xhat, _ = norm_stats(stream)
            n1_s[span] = (xhat * ln1_gain + ln1_bias).astype(BF16)

    loop(count, 4 * SIDE, first_norm)
    doc = ids[pl.ds(chip, 1), :]
    starts = [jnp.zeros((1, 1), F32)]
    starts += [jnp.sum(jnp.where(doc < v, 1.0, 0.0), axis=1, keepdims=True) for v in range(1, 4)]
    starts.append(jnp.full((1, 1), rows, F32))
    turn = jnp.zeros((1, 1), F32)
    for v in range(4):
        turn += jnp.where(starts[v + 1] - starts[v] == count, starts[v], 0.0)
    turn_here = turn - (core * count).astype(F32)

    def wrapped(v):
        v = jnp.where(v >= rows, v - rows, v)
        return jnp.where(v < 0, v + rows, v)

    def rotations(at):
        down = (lax.broadcasted_iota(jnp.int32, (64, rows), 0) + at).astype(F32)
        along = lax.broadcasted_iota(jnp.int32, (64, rows), 1).astype(F32)
        roll_s[pl.ds(at, 64)] = jnp.where(wrapped(down + turn_here) == along, 1.0, 0.0).astype(BF16)
        back_s[pl.ds(at, 64)] = jnp.where(wrapped(down - turn_here) == along, 1.0, 0.0).astype(BF16)
        where = wrapped((lax.broadcasted_iota(jnp.int32, (64, 128), 0) + at).astype(F32) + turn)
        mine = sum(jnp.where(where >= starts[v], 1.0, 0.0) for v in range(1, 4))
        slot = (lax.broadcasted_iota(jnp.int32, (64, 128), 1) % HEAD).astype(F32)
        sq_s[pl.ds(at, 64)] = jnp.where((slot < 4) & (slot != mine), 1.0, 0.0).astype(BF16)
        sk_s[pl.ds(at, 64)] = jnp.where(slot == mine, NEG_LARGE, 0.0).astype(BF16)


    for copy in get_w1:
        copy.wait()
    get_w2.wait()
    for item in pieces[4:]:
        item.copies[0].start()
    n1_copy = remote(n1_s.at[pl.ds(0, count)], n1_s.at[pl.ds(count, count)], csem, 0, sib)
    get_cot.wait()
    cot_copy = remote(cot_s.at[pl.ds(0, count)], cot_s.at[pl.ds(count, count)], csem, 1, sib)

    def rotate(at):
        nr_s[pl.ds(at, BLOCK)] = dot(roll_s[pl.ds(at, BLOCK)], n1_s[...]).astype(BF16)

    def project(j, at):
        n = nr_s[pl.ds(at, BLOCK)]
        biases = bias_qv if j == 0 else voth
        q = (dot_nt(n, wq_s[j, 0]) + biases[0:1]).astype(BF16) * SCALE
        k = dot_nt(n, wq_s[j, 1]).astype(BF16)
        v = (dot_nt(n, wq_s[j, 2]) + biases[1:2]).astype(BF16)
        q_s[j, pl.ds(at, BLOCK), :quarter] = q
        k_s[pl.ds(at, BLOCK), :quarter] = k
        v_s[j, pl.ds(at, BLOCK), :quarter] = v
        kt_s[j * quarter : (j + 1) * quarter, pl.ds(at, BLOCK)] = k.T * SCALE

    blocks = [(b, at) for b in range(2) for at in range(0, count, BLOCK)]

    def attend(j):
        for head in range(heads):
            at = 512 + 256 * head
            a_s[:, at : at + 128] = head_lanes(q_s.at[j], head, sq_s[...])
            a_s[:, at + 128 : at + 256] = head_lanes(k_s, head, sk_s[...])
        for at in range(0, rows, BLOCK):
            ou_s[:quarter, at : at + BLOCK] = v_s[j, at : at + BLOCK, :quarter].T

        def tile(here):
            b = here // count
            at = aligned(here % count, BLOCK)
            keys = pl.ds(aligned(b * count, count), count)
            for head in range(heads):
                column = 512 + 256 * head
                s = dot_nt(a_s[keys, column + 128 : column + 256], a_s[pl.ds(here, BLOCK), column : column + 128])
                m = jnp.max(s, axis=0, keepdims=True)
                e = jnp.exp(s - m)
                r = 1.0 / column_sum(e)
                low = e.astype(BF16)
                span = slice(head * HEAD, head * HEAD + HEAD)
                to = slice(j * quarter + head * HEAD, j * quarter + head * HEAD + HEAD)
                e_s[j * heads + head, b, :, pl.ds(at, BLOCK)] = low
                ot_s[to, pl.ds(here, BLOCK)] = (dot(ou_s[span, keys], low) * r).astype(BF16)
                r_s[j * heads + head : j * heads + head + 1, pl.ds(here, BLOCK)] = r

        return tile

    loop(rows, 64, rotations)
    n1_copy.wait_recv()
    loop(rows, BLOCK, rotate)
    loop(rows, BLOCK, lambda at: project(0, at))
    pass_on("p0")
    loop(rows, BLOCK, attend(0), service("a", pass_on))
    head_copy.wait_recv()
    have_weight(0, 1, 2)
    loop(rows, BLOCK, lambda at: project(1, at))
    pass_on("p1")
    loop(rows, BLOCK, attend(1), service("c", pass_on))

    have_weight(3)

    def unrotate(at):
        ou_s[:, pl.ds(at, BLOCK)] = dot(ot_s[...], roll_s[:, pl.ds(at, BLOCK)]).astype(BF16)

    loop(rows, BLOCK, unrotate)
    pass_on("u")

    def out_part(at):
        return dot_tn(ou_s[:, pl.ds(at, BLOCK)], wo_s[...])

    def att_half(at):
        return half_copy(sb1.at[pl.ds(at, BLOCK)], rb1.at[pl.ds(at, BLOCK)], 2, at)

    def n2_half(at):
        return half_copy(n2_s.at[pl.ds(at, BLOCK)], n2_s.at[pl.ds(aligned(count + at, BLOCK), BLOCK)], 4, at)

    def out_sib(at):
        sb1[pl.ds(at, BLOCK)] = out_part(count + at).astype(BF16)
        att_half(at).start()

    loop(count, BLOCK, out_sib)

    def out_mine(at):
        mid_s[pl.ds(at, BLOCK)] = sin_s[pl.ds(at, BLOCK)] + out_part(at) + out_bias

    loop(count, BLOCK, out_mine)
    pass_on("o")

    def second_norm(at):
        att_half(at).wait_recv()
        for off in range(0, BLOCK, 128):
            spot = pl.ds(aligned(at + off, 128), 128)
            mid = mid_s[spot] + rb1[spot].astype(F32)
            mid_s[spot] = mid
            xhat, _ = norm_stats(mid)
            n2_s[spot] = (xhat * ln2_gain + ln2_bias).astype(BF16)
        n2_half(at).start()

    loop(count, BLOCK, second_norm)
    pass_on("n")

    base_a = units
    parts = units // BLOCK
    steps = copies_of(len(full_bits))

    class Region:
        def __init__(self, index, row, size, cols, slot, kind, refs, to):
            own_r, oth_r, xr_r, land_r, both_r, rx_r = refs
            self.place, self.slot, self.to, self.xr = (row, size, 0, cols), slot, to, xr_r
            first, after = KINDS[kind]
            self.first = first is not None
            self.stages, self.stage, self.finished, self.sent = [], -1, False, []
            now, parts, used, trail = self.place, 8, 0, []
            sems = iter(range(index * steps, (index + 1) * steps))

            def copy(src, src_at, dst, dst_at, device):
                return described(src.at[self.window(src_at)], dst.at[self.window(dst_at)], gsem, next(sems), device)

            def piece(bits, mask):
                where = now
                for k, b in enumerate(bits):
                    where = self.cut(where, 1 - sides[b] if mask >> k & 1 else sides[b])
                return where

            sums = 1 + len(after) + len(full_bits)
            if self.first:
                keep, give, there = piece((first,), 0), piece((first,), 1), (row // 2, size // 2, 0, cols)
                place = self.landing(0, 4)
                copies = [copy(own_r, give, land_r, place, mate((first,))), copy(oth_r, give, both_r, there, mate((first,)))]
                adds = [(own_r, own_r, keep, [(land_r, place)]), (oth_r, oth_r, keep, [(both_r, there)])]
                self.stages.append((copies, adds, False))
                trail.append(((first,), keep))
                now, parts, used = keep, 4, 4
            self.stages.append(([copy(oth_r, now, xr_r, now, across)], [(own_r, own_r, now, [(xr_r, now)])], False))
            for bits in after:
                parts >>= len(bits)
                keep, copies, terms = piece(bits, 0), [], []
                for mask in range(1, 1 << len(bits)):
                    place = self.landing(used, parts)
                    used += parts
                    terms.append((land_r, place))
                    copies.append(copy(own_r, piece(bits, mask), land_r, place, mate([b for k, b in enumerate(bits) if mask >> k & 1])))
                self.stages.append((copies, [(own_r, own_r, keep, terms)], False))
                trail.append((bits, keep))
                now = keep
            for i, b in enumerate(full_bits):
                place = self.small_place()
                self.stages.append(([copy(own_r, now, rx_r[i], place, mates[b])], [(own_r, own_r, now, [(rx_r[i], place)])], True))
            copies, adds, full = self.stages[-1]
            self.stages[-1] = (copies, [(xr_r,) + adds[0][1:]], full)
            for bits, keep in reversed(trail):
                copies = []
                for mask in range(1, 1 << len(bits)):
                    copies.append(copy(xr_r, keep, xr_r, keep, mate([b for k, b in enumerate(bits) if mask >> k & 1])))
                self.stages.append((copies, [], False))

        def window(self, where):
            row, size, col, cols = where
            return pl.ds(row, size), pl.ds(col, cols)

        def cut(self, where, side):
            row, size, col, cols = where
            if (size // 2) % 16 == 0:
                return aligned(row + side * (size // 2), 16), size // 2, col, cols
            return row, size, aligned(col + side * (cols // 2), 128), cols // 2

        def landing(self, at, parts_here):
            row, rows_one, cols_one = self.slot
            full = self.place[3]
            if cols_one == full:
                return row + at * rows_one, parts_here * rows_one, 0, full
            if parts_here == 1:
                return row + at // 2 * rows_one, rows_one, at % 2 * cols_one, cols_one
            return row + at // 2 * rows_one, parts_here // 2 * rows_one, 0, full

        def small_place(self):
            row, rows_one, cols_one = self.slot
            if cols_one == self.place[3]:
                return row // 7, rows_one, 0, cols_one
            k = (self.place[0] - base_a) // quarter
            return units // 8 + k // 2 * rows_one, rows_one, k % 2 * cols_one, cols_one

        def begin(self, copies):
            for copy in copies:
                copy.start()
            self.sent += copies

        def ready(self, j):
            if self.first:
                self.stage = 0
                self.begin([self.stages[0][0][j]])
            elif j == 1:
                self.stage = 0
                self.begin(self.stages[0][0])

        def add(self, into, base, where, terms):
            row, size, col, cols = where
            step = 64 if size % 64 == 0 else 48 if size % 48 == 0 else 32

            def body(off):
                to = (pl.ds(aligned(row + off, 16), step), pl.ds(col, cols))
                parts_in = [ref[pl.ds(aligned(r + off, 16), step), pl.ds(c, cols)] for ref, (r, _, c, _) in terms]
                if len(parts_in) == 1:
                    into[to] = base[to] + parts_in[0]
                else:
                    into[to] = sum((v.astype(F32) for v in parts_in), base[to].astype(F32)).astype(BF16)

            if inside_loop:
                for off in range(0, size, step):
                    body(off)
            else:
                loop(size, step, body)

        def advance(self):
            if self.finished or self.stage < 0:
                return
            copies, adds, full = self.stages[self.stage]
            for copy in copies:
                copy.wait_recv()
            if full:
                for copy in copies:
                    copy.wait_send()
                self.sent = [c for c in self.sent if all(c is not d for d in copies)]
            for item in adds:
                self.add(*item)
            self.stage += 1
            if self.stage < len(self.stages):
                self.begin(self.stages[self.stage][0])
                return
            self.finished = True
            to_write.append(self)

    chunks = []
    refs = (own, oth, xr, land, land_both, rx)
    for i in range(parts):
        slot = (i * 7 * (BLOCK // 8), BLOCK // 8, width)
        to = g2_h.at[pl.ds(i * BLOCK, BLOCK)]
        chunks.append(Region(2 * i, i * BLOCK, BLOCK, width, slot, ORDERS[2 * i], refs, to))
        refs_one = tuple(ref.at[i] for ref in (own1, oth1, xr1, land1, land1_both)) + ([ref.at[i] for ref in rx1],)
        to = g1_h.at[:, pl.ds(i * BLOCK, BLOCK)]
        chunks.append(Region(2 * i + 1, 0, width, BLOCK, (0, width // 8, BLOCK), ORDERS[2 * i + 1], refs_one, to))
    for i in range(4):
        slot = (7 * units // 8 + i * quarter, quarter // 4, width // 2)
        to = go_h if i == 0 else gq_h.at[i - 1]
        chunks.append(Region(2 * parts + i, base_a + i * quarter, quarter, width, slot, ORDERS[2 * parts + i], refs, to))
    first_att = 2 * parts

    class Small:
        def __init__(self, tile, index, everywhere, paired, groups):
            self.tile, self.everywhere, self.paired = tile, everywhere, paired
            landings = [near.at[3 * index + k] for k in range(3)] + [far.at[(7 + len(full_bits)) * index + k] for k in range(7 + len(full_bits))]
            sems = iter(range(index * len(landings), (index + 1) * len(landings)))
            landings = iter(landings)

            def stage(devices):
                places = [next(landings) for _ in devices]
                return places, [described(tile, dst, ssem, next(sems), d) for dst, d in zip(places, devices)]

            self.stages = [stage([sib, across, facing])]
            for bits in groups + [(b,) for b in full_bits]:
                masks = range(1, 1 << len(bits))
                self.stages.append(stage([mate([b for k, b in enumerate(bits) if mask >> k & 1]) for mask in masks]))
            self.stage, self.finished = -1, False

        def start(self):
            self.stage = 0
            for copy in self.stages[0][1]:
                copy.start()

        def advance(self):
            if self.finished or self.stage < 0:
                return
            places, copies = self.stages[self.stage]
            for copy in copies:
                copy.wait()
            tile = self.tile
            if self.stage == 0:
                beside, over, facing_ = places
                n, p = self.everywhere, self.paired
                tile[0:n] = (tile[0:n] + beside[0:n]) + (over[0:n] + facing_[0:n])
                tile[n : n + p] = tile[n : n + p] + over[n + p : n + 2 * p]
            else:
                got = [tile[...]] + [place[...] for place in places]
                while len(got) > 1:
                    got = [got[k] + got[k + 1] for k in range(0, len(got), 2)]
                tile[...] = got[0]
            self.stage += 1
            if self.stage == len(self.stages):
                self.finished = True
                return
            for copy in self.stages[self.stage][1]:
                copy.start()

    first_small = Small(early, 0, 4, 1, [(b,) for b in half_bits])
    last_small = Small(late, 1, 2, 2, [tuple(half_bits)])

    def ready(i, j):
        chunks[i].ready(j)

    to_write = []

    def write_finished():
        while to_write:
            region = to_write.pop()
            region.done = local(region.xr.at[region.window(region.place)], region.to)

    def hook(name):
        pass_on(name)
        for i in PLAN.get(name, ()):
            (chunks + [last_small, first_small])[i].advance()
            if not inside_loop:
                write_finished()

    def chunk_rows(j, i, at):
        span = pl.ds(at, BLOCK)
        cols = slice(j * units + i * BLOCK, j * units + (i + 1) * BLOCK)
        mine = slice(i * BLOCK, (i + 1) * BLOCK)
        bias = (bias_u if j == 0 else uoth)[mine].reshape(1, BLOCK)
        h = dot(n2_s[span], w1_s[j, i]) + bias
        a, slope = gelu_pair(h)
        a_s[span, cols] = a.astype(BF16)
        g = (dot_nt(cot_s[span], w2_s[j, mine]) * slope).astype(BF16)
        g_s[span, cols] = g

    def chunk_grads(j, i):
        cols = slice(j * units + i * BLOCK, j * units + (i + 1) * BLOCK)
        mine = slice(i * BLOCK, (i + 1) * BLOCK)
        to = oth if j == 1 else own

        def second(at):
            to[pl.ds(i * BLOCK + at, 128)] = dot_tn(a_s[:, pl.ds(cols.start + at, 128)], cot_s[...]).astype(BF16)

        loop(BLOCK, 128, second)
        ready(2 * i, j)
        g = g_s[:, cols]

        def first(at):
            (oth1 if j == 1 else own1)[i, pl.ds(at, BLOCK)] = dot(n2t_s[pl.ds(at, BLOCK)], g_s[:, cols]).astype(BF16)

        loop(width, BLOCK, first)
        ready(2 * i + 1, j)
        early[4 + j : 5 + j, mine] = column_sum(g.astype(F32))
        hook(f"f{j}{i}")

    def feed(j, i, first=False):
        if first:
            loop(count, BLOCK, lambda at: chunk_rows(j, i, at))
            hook(f"r{j}{i}.0")
            cot_copy.wait_recv()

            def received(at):
                n2_half(at).wait_recv()
                chunk_rows(j, i, count + at)

            loop(count, BLOCK, received)
            hook(f"r{j}{i}.1")

            def turned(at):
                n2t_s[:, pl.ds(at, BLOCK)] = n2_s[pl.ds(at, BLOCK)].T

            loop(rows, BLOCK, turned)
        else:
            loop(rows, BLOCK, lambda at: chunk_rows(j, i, at), service(f"r{j}{i}.", hook), 2)
        chunk_grads(j, i)

    early[...] = jnp.zeros_like(early)
    late[...] = jnp.zeros_like(late)
    unit_copy.wait_recv()
    for i in range(parts):
        have_weight(4 + 2 * i, 5 + 2 * i)
        feed(1, i, first=i == 0)
        feed(0, i)

    def back_two(at):
        span = pl.ds(at, BLOCK)
        total = None
        for j in range(2):
            for i in range(parts):
                at_col = j * units + i * BLOCK
                term = dot_nt(g_s[span, at_col : at_col + BLOCK], w1_s[j, i])
                total = term if total is None else total + term
        return total

    def mlp_part(at):
        span = pl.ds(at, BLOCK)
        return dot(a_s[span, :units], w2_s[0]) + dot(a_s[span, units:], w2_s[1])

    def gn2_half(at):
        return half_copy(sb2.at[pl.ds(at, BLOCK)], rb2.at[pl.ds(at, BLOCK)], 6, at)

    def dm_half(at):
        return half_copy(n2_s.at[pl.ds(at, BLOCK)], n2_s.at[pl.ds(aligned(count + at, BLOCK), BLOCK)], 10, at)

    def back_two_sib(at):
        sb2[pl.ds(at, BLOCK)] = back_two(count + at).astype(BF16)
        gn2_half(at).start()

    def back_two_mine(at):
        gm_s[pl.ds(at, BLOCK)] = back_two(at)

    def mlp_sib(at):
        sb1[pl.ds(at, BLOCK)] = mlp_part(count + at).astype(BF16)

    loop(count, BLOCK, back_two_sib)
    hook("g0")
    loop(count, BLOCK, back_two_mine)
    hook("gn2")

    def second_back(at):
        gn2_half(at).wait_recv()
        n2_half(at).wait_send()
        for off in range(0, BLOCK, 128):
            spot = pl.ds(aligned(at + off, 128), 128)
            xhat, sigma = norm_stats(mid_s[spot])
            grad = gm_s[spot] + rb2[spot].astype(F32)
            cot = cot_s[spot].astype(F32)
            back = cot + norm_back(grad, ln2_gain, xhat, sigma)
            gm_s[spot] = back
            n2_s[spot] = back.astype(BF16)
            early[0:1] += column_sum(back)
            early[1:2] += column_sum(grad * xhat)
            early[2:3] += column_sum(grad)
            early[3:4] += column_sum(cot)
        dm_half(at).start()

    loop(count, BLOCK, second_back)
    hook("lb")
    for at in range(0, count, BLOCK):
        att_half(at).wait_send()
    loop(count, BLOCK, mlp_sib)
    mlp_copy = remote(sb1, rb1, csem, 8, sib)
    first_small.start()
    hook("ln2")

    for at in range(0, count, BLOCK):
        dm_half(at).wait_recv()

    start = base_a + quarter
    zero = jnp.zeros((count, 128), BF16)
    grad_s = dq_s = ou_s
    n1_copy.wait_send()

    def keep_gradient(j, c):
        to = oth if j == 1 else own
        low = start + c * quarter
        dt = ot_s.at[j * quarter : (j + 1) * quarter]

        def columns(at):
            to[low : low + quarter, pl.ds(at, BLOCK)] = dot(dt[...], nr_s[:, pl.ds(at, BLOCK)]).astype(BF16)

        loop(width, BLOCK, columns)
        ready(first_att + 1 + c, j)
        if c != 1:
            d = g_s[:, (3 * j + c) * BLOCK : (3 * j + c) * BLOCK + quarter]
            late[2 + c // 2 + 2 * j : 3 + c // 2 + 2 * j, :quarter] = column_sum(d.astype(F32))

    def values_back(j):
        base = j * quarter
        to = oth if j == 1 else own

        def weight(at):
            to[base_a : base_a + quarter, pl.ds(at, BLOCK)] = dot(ou_s[base : base + quarter], n2_s[:, pl.ds(at, BLOCK)]).astype(BF16)

        loop(width, BLOCK, weight)
        ready(first_att, j)

        def output(at):
            grad_s[base : base + quarter, pl.ds(at, BLOCK)] = dot_nt(wo_s[base : base + quarter], n2_s[pl.ds(at, BLOCK)]).astype(BF16)

        loop(rows, BLOCK, output)
        hook(f"w{j}.0")
        go_s = n1_s.at[:, 256 * j : 256 * (j + 1)]

        def scale(at):
            here = pl.ds(at, BLOCK)
            grad_t = dot_nt(grad_s[base : base + quarter], roll_s[here])
            for head in range(heads):
                row = j * heads + head
                r = r_s[row : row + 1, here]
                g = grad_t[head * HEAD : (head + 1) * HEAD]
                at_head = slice(base + head * HEAD, base + (head + 1) * HEAD)
                in_s[row : row + 1, here] = column_sum(g * ot_s[at_head, here].astype(F32)) * r
                gt_s[at_head, here] = (g * r).astype(BF16)
            go_s[here, :quarter] = gt_s[base : base + quarter, here].T

        loop(rows, BLOCK, scale)

        def block(at):
            here = pl.ds(at, count)
            b = at // count
            dv = [None, None]
            for head in range(heads):
                tile = head // 2
                gh = jnp.where(lane_half(count, head % 2 == 1), go_s[here, 128 * tile : 128 * tile + 128], zero)
                part = dot(e_s[j * heads + head, b], gh)
                dv[tile] = part if dv[tile] is None else dv[tile] + part
            dv = jnp.concatenate(dv, axis=1)[:, :quarter].astype(BF16)
            g_s[here, (3 * j + 2) * BLOCK : (3 * j + 2) * BLOCK + quarter] = dv
            ot_s[base : base + quarter, here] = dv.T

        loop(rows, count, block)
        hook(f"w{j}.1")
        keep_gradient(j, 2)
        hook(f"v{j}")

    def scores_back(j):
        base = j * quarter

        def block(at):
            here = pl.ds(at, count)
            b = at // count
            dk = [None, None]
            for head in range(heads):
                tile = head // 2
                row = j * heads + head
                half = lane_half(count, head % 2 == 1)
                lanes = slice(128 * tile, 128 * tile + 128)
                vh = jnp.where(half, v_s[j, here, lanes], zero)
                qh = jnp.where(half, q_s[j, here, lanes], zero)
                last_row = min(128 * tile + 128, quarter)
                vh = vh[:, : last_row - 128 * tile]
                ds = n2t_s.at[:count, head * count : (head + 1) * count] if head < 2 else ds_s
                for off in range(0, count, BLOCK):
                    some = pl.ds(aligned(at + off, BLOCK), BLOCK)
                    dp_t = dot(vh, gt_s[base + 128 * tile : base + last_row, some])
                    grad = (dp_t - in_s[row : row + 1, some]).astype(BF16)
                    ds[:, off : off + BLOCK] = grad * e_s[row, b, :, off : off + BLOCK]
                part = dot(ds[...], qh)
                dk[tile] = part if dk[tile] is None else dk[tile] + part
                kth = kt_s[base + head * HEAD : base + head * HEAD + HEAD, here]
                dq_s[base + head * HEAD : base + head * HEAD + HEAD, here] = dot(kth, ds[...]).astype(BF16)
            dk = jnp.concatenate(dk, axis=1)[:, :quarter].astype(BF16)
            g_s[here, (3 * j + 1) * BLOCK : (3 * j + 1) * BLOCK + quarter] = dk
            ot_s[base : base + quarter, here] = dk.T
            g_s[here, 3 * j * BLOCK : 3 * j * BLOCK + quarter] = dq_s[base : base + quarter, here].T

        loop(rows, count, block, service(f"b{j}.", hook))
        keep_gradient(j, 1)
        hook(f"k{j}")
        ot_s[base : base + quarter] = dq_s[base : base + quarter]
        keep_gradient(j, 0)
        hook(f"s{j}")

    values_back(1)
    scores_back(1)
    values_back(0)
    scores_back(0)

    def finish_out(at):
        span = pl.ds(at, BLOCK)
        mid_s[span] = mid_s[span] + mlp_part(at) + fc2_bias

    loop(count, BLOCK, finish_out)
    hook("fo")
    mlp_copy.wait_recv()

    def write_out(at):
        spot = pl.ds(at, 128)
        tok_s[spot] = (mid_s[spot] + rb1[spot].astype(F32)).astype(BF16)

    loop(count, 128, write_out)
    put_out = local(tok_s, out_h)
    hook("fin")

    def back_one(at):
        total = None
        for j in range(2):
            for c in range(3):
                d = g_s[pl.ds(at, BLOCK), (3 * j + c) * BLOCK : (3 * j + c) * BLOCK + quarter]
                term = dot(d, wq_s[j, c])
                total = term if total is None else total + term
        n2_s[pl.ds(at, BLOCK)] = total.astype(BF16)

    for at in range(0, count, BLOCK):
        dm_half(at).wait_send()
    loop(rows, BLOCK, back_one, service("d.", hook), 2)
    for at in range(0, count, BLOCK):
        gn2_half(at).wait_send()

    def gn1_half(at):
        return half_copy(sb2.at[pl.ds(at, BLOCK)], rb2.at[pl.ds(at, BLOCK)], 12, at)

    def back_one_sib(at):
        sb2[pl.ds(at, BLOCK)] = dot(back_s[pl.ds(count + at, BLOCK)], n2_s[...]).astype(BF16)
        gn1_half(at).start()

    def back_one_mine(at):
        mid_s[pl.ds(at, BLOCK)] = dot(back_s[pl.ds(at, BLOCK)], n2_s[...])

    loop(count, BLOCK, back_one_sib)
    loop(count, BLOCK, back_one_mine)
    hook("e.0")
    mlp_copy.wait_send()

    def first_back(at):
        gn1_half(at).wait_recv()
        for off in range(0, BLOCK, 128):
            spot = pl.ds(aligned(at + off, 128), 128)
            xhat, sigma = norm_stats(sin_s[spot])
            grad = mid_s[spot] + rb2[spot].astype(F32)
            sb1[spot] = (gm_s[spot] + norm_back(grad, ln1_gain, xhat, sigma)).astype(BF16)
            late[0:1] += column_sum(grad * xhat)
            late[1:2] += column_sum(grad)

    loop(count, BLOCK, first_back)
    put_in = local(sb1, ing_h)
    last_small.start()
    hook("e.1")
    hook("tail")
    left = [first_small, last_small] + chunks
    while left:
        for item in left:
            item.advance()
            write_finished()
        left = [item for item in left if not item.finished]

    for row, source, at in ((0, late, 0), (1, late, 1), (2, early, 0), (3, early, 1), (4, early, 2), (5, early, 3), (8, early, 4), (9, late, 2), (10, late, 3)):
        small_o[row : row + 1] = source[at : at + 1]

    passed = [copy for item in pieces for copy in item.copies]
    for copy in [unit_copy, head_copy, cot_copy] + [gn1_half(at) for at in range(0, count, BLOCK)] + passed:
        copy.wait_send()
    for chunk in chunks:
        for copy in chunk.sent:
            copy.wait_send()
        chunk.done.wait()
    put_out.wait()
    put_in.wait()


def copies_of(full):
    most = 0
    for kind in ORDERS:
        first, after = KINDS[kind]
        most = max(most, 1 + full + 2 * sum((1 << len(bits)) - 1 for bits in after) + (0 if first is None else 3))
    return most


def call_layer(dp_size, tokens, cotangent, ids, table, vectors, wq, wo, w1, w2):
    count, width = tokens.shape
    rows = 2 * count
    quarter = wo.shape[0]
    units = w1.shape[1]
    heads = quarter // HEAD
    grad_rows = units + 4 * quarter
    parts = units // BLOCK
    bits = [b for b in range(20) if (1 << b) < dp_size]
    half_bits = bits[:3]
    shape = jax.ShapeDtypeStruct
    vm = pltpu.VMEM
    regions = 2 * (units // BLOCK) + 4
    steps = copies_of(len(bits) - len(half_bits))
    fetched = 4 + 2 * (units // BLOCK)
    scratch = (
        [vm((count, width), BF16), vm((rows, width), BF16)]
        + [vm((count, width), F32)] * 3
        + [vm((rows, width), BF16)] * 2
        + [vm((width, rows), BF16)]
        + [vm((2,) + wq.shape, BF16), vm((2 * quarter, width), BF16), vm((2, units // BLOCK, width, BLOCK), BF16), vm((2,) + w2.shape, BF16)]
        + [vm((2, rows, 256), BF16)] * 2
        + [vm((2 * quarter, rows), BF16)] * 4
        + [vm((8, rows), F32)] * 2
        + [vm((2 * heads, 2, count, count), BF16)]
        + [vm((rows, rows), BF16)] * 2
        + [vm((rows, width), BF16), vm((count, count), BF16)]
        + [vm((rows, 2 * units), BF16)] * 2
        + [vm((count, width), BF16)] * 4
        + [vm((grad_rows, width), BF16)] * 3
        + [vm((7 * units // 8 + 4 * quarter, width), BF16), vm((units // 2, width), BF16)]
        + [vm((parts, width, BLOCK), BF16)] * 3
        + [vm((parts, 7 * width // 8, BLOCK), BF16), vm((parts, width // 2, BLOCK), BF16)]
        + [vm((grad_rows >> len(half_bits), width), BF16)] * (len(bits) - len(half_bits))
        + [vm((parts, width // 8, BLOCK), BF16)] * (len(bits) - len(half_bits))
        + [vm((units,), F32), vm((2, quarter), F32), vm((8, width), F32), vm((8, width), F32)]
        + [vm((6, 8, width), F32), vm((14 + 2 * (len(bits) - 3), 8, width), F32)]
        + [pltpu.SemaphoreType.DMA((8 + units // BLOCK + regions,))]
        + [pltpu.SemaphoreType.DMA((2, n)) for n in (3 * fetched + 2, 14, regions * steps, 2 * (10 + len(bits) - 3))]
    )
    anywhere = pl.BlockSpec(memory_space=pl.ANY)
    inside = pl.BlockSpec(memory_space=pltpu.VMEM)
    return pl.pallas_call(
        functools.partial(layer, dp_size, half_bits),
        out_shape=[shape((count, width), BF16)] * 2
        + [shape(w2.shape, BF16), shape(w1.shape, BF16), shape(wo.shape, BF16), shape(wq.shape, BF16), shape((16, width), F32)],
        in_specs=[anywhere] * 2 + [inside] * (2 + len(vectors)) + [anywhere] * 4,
        out_specs=[anywhere] * 6 + [inside],
        scratch_shapes=scratch,
        compiler_params=pltpu.CompilerParams(vmem_limit_bytes=VMEM_LIMIT, collective_id=0, has_side_effects=True),
        name="layer",
    )(tokens, cotangent, ids, table, *vectors, wq, wo, w1, w2)


def finish(*refs):
    sources, small, rest = refs[:6], refs[6], refs[7:]
    results, vectors, rest = rest[:6], rest[6:14], rest[14:]
    narrow, wide, (get, put) = rest[:6], rest[6:10], rest[10:]
    blocks = []
    for k, src in enumerate(sources):
        if src.ndim == 3:
            places = list(range(src.shape[0]))
        else:
            step = min(BLOCK, src.shape[0])
            places = [pl.ds(at, step) for at in range(0, src.shape[0], step)]
        for at in places:
            low = narrow[k].at[at]
            blocks.append((src.at[at], low, low if k < 2 else wide[k - 2].at[at], results[k].at[at]))
    reads = [pltpu.make_async_copy(src, low, get.at[n]) for n, (src, low, _, _) in enumerate(blocks)]
    writes = [pltpu.make_async_copy(high, dst, put.at[n]) for n, (_, _, high, dst) in enumerate(blocks)]
    for copy in reads:
        copy.start()
    for i in range(6):
        vectors[i][...] = small[i]
    vectors[6][...] = small[8, : vectors[6].shape[0]]
    vectors[7][...] = small[9:11, : vectors[7].shape[1]]
    for read, write, (_, low, high, _) in zip(reads, writes, blocks):
        read.wait()
        if high is not low:

            def cast(at, low=low, high=high):
                high[pl.ds(at, 64)] = low[pl.ds(at, 64)].astype(F32)

            loop(low.shape[0], 64, cast)
        write.start()
    for copy in writes:
        copy.wait()


def call_finish(arrays, small, units, quarter):
    width = small.shape[1]
    shape = jax.ShapeDtypeStruct
    extents = [(width,)] * 6 + [(units,), (2, quarter)]
    kinds = [BF16, BF16, F32, F32, F32, F32]
    anywhere = pl.BlockSpec(memory_space=pl.ANY)
    inside = pl.BlockSpec(memory_space=pltpu.VMEM)
    grads = arrays[2:]
    return pl.pallas_call(
        finish,
        in_specs=[anywhere] * len(arrays) + [inside],
        out_specs=[anywhere] * len(arrays) + [inside] * len(extents),
        out_shape=[shape(a.shape, k) for a, k in zip(arrays, kinds)] + [shape(e, F32) for e in extents],
        scratch_shapes=[pltpu.VMEM(a.shape, BF16) for a in arrays]
        + [pltpu.VMEM(a.shape, F32) for a in grads]
        + [pltpu.SemaphoreType.DMA((16,)), pltpu.SemaphoreType.DMA((16,))],
        compiler_params=pltpu.CompilerParams(vmem_limit_bytes=VMEM_LIMIT),
        name="finish",
    )(*arrays, small)


def per_device(
    tokens, segment_ids, ln1_gain, ln1_bias, qkv_weight, qv_bias, out_weight, out_bias,
    ln2_gain, ln2_bias, fc1_weight, fc1_bias, fc2_weight, fc2_bias, cotangent,
):
    width = tokens.shape[1]
    freq_count = width // 6
    frequency = 10000.0 ** (-jnp.arange(freq_count, dtype=F32) / freq_count)
    angles = jnp.arange(SIDE, dtype=F32)[:, None] * frequency[None, :]
    table = jnp.concatenate([jnp.sin(angles), jnp.cos(angles)], axis=1)
    vectors = (ln1_gain, ln1_bias, out_bias, ln2_gain, ln2_bias, fc2_bias, fc1_bias, qv_bias)
    *arrays, small = call_layer(
        lax.axis_size("dp"), tokens, cotangent, segment_ids, table, vectors, qkv_weight.transpose(0, 2, 1), out_weight, fc1_weight, fc2_weight
    )
    out, ing, g2, g1, go, gq, a0, a1, a2, a3, a4, a5, g_units, g_heads = call_finish(arrays, small, fc1_weight.shape[1], out_weight.shape[0])
    return (out, ing, a0, a1, gq.transpose(0, 2, 1), g_heads, go, a2, a3, a4, g1, g_units, g2, a5)


def solution(mesh):
    placed = (
        P(("dp", "tensor"), None),
        P("dp", None),
        P(),
        P(),
        P(None, None, "tensor"),
        P(None, "tensor"),
        P("tensor", None),
        P(),
        P(),
        P(),
        P(None, "tensor"),
        P("tensor"),
        P("tensor", None),
        P(),
        P(("dp", "tensor"), None),
    )
    return jax.shard_map(
        per_device,
        mesh=mesh,
        in_specs=placed,
        out_specs=(
            P(("dp", "tensor"), None),
            P(("dp", "tensor"), None),
            P(),
            P(),
            P(None, None, "tensor"),
            P(None, "tensor"),
            P("tensor", None),
            P(),
            P(),
            P(),
            P(None, "tensor"),
            P("tensor"),
            P("tensor", None),
            P(),
        ),
        check_vma=False,
    )
```

```python
import functools

import jax
import jax.numpy as jnp
from jax import lax
from jax.experimental import pallas as pl
from jax.experimental.pallas import tpu as pltpu
from jax.sharding import PartitionSpec as P

HEAD = 64
SIDE = 16
EPSILON = 1e-06
NEG_LARGE = -1e30
SCALE = HEAD ** (-0.5)
F32 = jnp.float32
BF16 = jnp.bfloat16
VMEM_LIMIT = 64 * 1024 * 1024 - 128 * 1024
MESH = pl.DeviceIdType.MESH
BLOCK = 256
KINDS = {
    "A": (None, ((0,), (1,), (2,))),
    "B": (None, ((1,), (0,), (2,))),
    "D": (None, ((0,), (1, 2))),
    "E": (None, ((0, 1, 2),)),
    "C": (None, ((0, 1), (2,))),
    "Y": (0, ((1,), (2,))),
    "Z": (1, ((0,), (2,))),
    "YD": (0, ((1, 2),)),
    "S": (None, (("p",), ("q",), (2,))),
    "SD": (None, (("p",), ("q", 2))),
    "SF": ("p", (("q",), (2,))),
    "SFD": ("p", (("q", 2),)),
}
ORDERS = ("D", "SFD", "SFD", "Z", "SD", "Y", "B", "SD", "D", "D")
WEIGHT_PLAN = {"p0": (0,), "a0": (1,), "a3": (2,), "p1": (3, 4), "c2": (5,), "n": (6,), "r10.1": (7,), "r00.1": (8,), "r11.1": (9,)}
PLAN = {
    "f01": (1,),
    "r12.1": (0,),
    "r02.0": (2,),
    "r02.1": (1,),
    "g0": (0,),
    "lb": (3, 4, 1),
    "w1.0": (2, 0),
    "w1.1": (-1, 5),
    "v1": (3, 4, 1),
    "b1.0": (-1,),
    "b1.1": (2, 3),
    "k1": (0,),
    "s1": (5,),
    "w0.0": (6, 1, -1, 4),
    "v0": (9,),
    "b0.0": (0, 2, 5, 3, 6, -1),
    "b0.1": (9, 4),
    "k0": (8, 2),
    "s0": (5, 6),
    "fo": (7, 3),
    "d.0": (9, 4),
    "d.1": (8, 5, 6),
    "e.0": (7, 3),
    "e.1": (9,),
    "tail": (8, 5, -2, 6, 9, 7, 3, 5, 8, 6, -2, 7, 8, 6, 7),
}


def dot(a, b):
    return jnp.dot(a, b, preferred_element_type=F32)


def dot_nt(a, b):
    return lax.dot_general(a, b, (((1,), (1,)), ((), ())), preferred_element_type=F32)


def dot_tn(a, b):
    return lax.dot_general(a, b, (((0,), (0,)), ((), ())), preferred_element_type=F32)


def lane_half(rows, upper):
    lanes = lax.broadcasted_iota(jnp.int32, (rows, 128), 1)
    return lanes >= HEAD if upper else lanes < HEAD


def head_lanes(ref, head, filler):
    tile = ref[:, 128 * (head // 2) : 128 * (head // 2) + 128]
    return jnp.where(lane_half(tile.shape[0], head % 2 == 1), tile, filler)


def gelu_pair(h):
    cdf = 0.5 + 0.5 * lax.erf(h * 0.7071067811865476)
    return h * cdf, cdf + h * jnp.exp(-0.5 * h * h) * 0.3989422804014327


def norm_stats(v):
    centred = v - jnp.mean(v, axis=-1, keepdims=True)
    sigma = lax.rsqrt(jnp.mean(centred * centred, axis=-1, keepdims=True) + EPSILON)
    return centred * sigma, sigma


def norm_back(grad, gain, xhat, sigma):
    g = grad * gain
    return sigma * (g - jnp.mean(g, axis=-1, keepdims=True) - xhat * jnp.mean(g * xhat, axis=-1, keepdims=True))


def column_sum(v):
    return jnp.sum(v, axis=0, keepdims=True)


def aligned(v, unit):
    return v if isinstance(v, int) else pl.multiple_of(v, unit)


def loop(count, step, body, service=None, every=1):
    def run(i, carry):
        body(aligned(i * step, step))
        if service is not None:
            for k in range(count // step // every):
                if service(k, True):
                    pl.when(i == every * (k + 1) - 1)(functools.partial(service, k, False))
        return carry

    lax.fori_loop(0, count // step, run, 0)


def layer(
    dp_size, half_bits,
    tok_h, cot_h, ids, table, gain1, bias1, bias_o, gain2, bias2, bias_f, bias_u, bias_qv, wq_h, wo_h, w1_h, w2_h,
    out_h, ing_h, g2_h, g1_h, go_h, gq_h, small_o,
    tok_s, cot_s, sin_s, mid_s, gm_s, n1_s, n2_s, n2t_s, wq_s, wo_s, w1_s, w2_s,
    q_s, v_s, kt_s, ot_s, ou_s, gt_s, r_s, in_s, e_s, roll_s, back_s, nr_s, ds_s, a_s, g_s, sb1, sb2, rb1, rb2,
    own, oth, xr, land, land_both, own1, oth1, xr1, land1, land1_both, *rest,
):
    rest = list(rest)
    full_bits = [b for b in range(20) if (1 << b) < dp_size and b not in half_bits]
    rx = [rest.pop(0) for _ in full_bits]
    rx1 = [rest.pop(0) for _ in full_bits]
    uoth, voth, early, late, near, far, lsem, wsem, csem, gsem, ssem = rest

    count, width = tok_s.shape
    rows = 2 * count
    quarter = wo_h.shape[0]
    units = w1_h.shape[1]
    heads = quarter // HEAD
    place = lax.axis_index("tensor")
    dp = lax.axis_index("dp")
    chip = place // 2
    core = place % 2
    sib = {"tensor": chip * 2 + 1 - core}
    across = {"tensor": (1 - chip) * 2 + core}
    facing = {"tensor": (1 - chip) * 2 + 1 - core}
    all_bits = list(half_bits) + full_bits
    sides = {b: (dp // (1 << b)) % 2 for b in all_bits}

    ways = {b: (1 - 2 * sides[b]) * (1 << b) for b in all_bits}
    sides["p"] = sides[0] + (sides[1] - sides[0]) * core
    sides["q"] = sides[1] + (sides[0] - sides[1]) * core
    ways["p"] = ways[0] + (ways[1] - ways[0]) * core
    ways["q"] = ways[1] + (ways[0] - ways[1]) * core

    def mate(bits):
        return {"dp": dp + sum(ways[b] for b in bits)}

    def described(src, dst, sems, index, device):
        return pltpu.make_async_remote_copy(
            src_ref=src, dst_ref=dst, send_sem=sems.at[0, index], recv_sem=sems.at[1, index], device_id=device, device_id_type=MESH
        )

    mates = {b: mate((b,)) for b in all_bits}
    groups = {(b,) for b in full_bits}
    for mask in range(1, 1 << len(half_bits)):
        groups.add(tuple(b for k, b in enumerate(half_bits) if mask >> k & 1))

    barrier = pltpu.get_barrier_semaphore()
    partners = [sib, across, facing] + [mate(bits) for bits in sorted(groups)]
    for partner in partners:
        pl.semaphore_signal(barrier, inc=1, device_id=partner, device_id_type=MESH)

    sq_s, sk_s, k_s = a_s.at[:, 0:128], a_s.at[:, 128:256], a_s.at[:, 256:512]
    local_used = [0]

    def local(src, dst):
        copy = pltpu.make_async_copy(src, dst, lsem.at[local_used[0]])
        local_used[0] += 1
        copy.start()
        return copy

    def remote(src, dst, sems, index, device):
        copy = pltpu.make_async_remote_copy(
            src_ref=src, dst_ref=dst, send_sem=sems.at[0, index], recv_sem=sems.at[1, index], device_id=device, device_id_type=MESH
        )
        copy.start()
        return copy

    def half_copy(src, dst, first, at):
        return pltpu.make_async_remote_copy(
            src_ref=src,
            dst_ref=dst,
            send_sem=csem.at[0, first + at // BLOCK],
            recv_sem=csem.at[1, first + at // BLOCK],
            device_id=sib,
            device_id_type=MESH,
        )

    get_wq = local(wq_h, wq_s.at[0])
    get_tok = local(tok_h, tok_s)
    get_cot = local(cot_h, cot_s.at[pl.ds(0, count)])
    get_wo = local(wo_h, wo_s.at[pl.ds(0, quarter)])
    get_w1 = [local(w1_h.at[:, pl.ds(i * BLOCK, BLOCK)], w1_s.at[0, i]) for i in range(units // BLOCK)]
    get_w2 = local(w2_h, w2_s.at[0])

    part = (sides[0] + sides[1]) % 2

    class Piece:
        def __init__(self, index, refs, at, extent):
            size = extent // 4

            def some(k, first, size):
                return refs[k].at[pl.ds(aligned(at[k] + part * (extent // 2) + first, 16), size)]

            self.copies = [described(some(0, 0, 2 * size), some(1, 0, 2 * size), wsem, 3 * index, across)]
            for k in range(2):
                block = some(1, k * size, size)
                self.copies.append(described(block, block, wsem, 3 * index + 1 + k, mates[k]))
            self.stage = 0

        def advance(self):
            if self.stage == 0:
                self.copies[0].wait_recv()
                self.copies[1].start()
                self.copies[2].start()
            else:
                self.copies[1].wait_recv()
                self.copies[2].wait_recv()
            self.stage += 1

    pieces = [Piece(c, (wq_s.at[0, c], wq_s.at[1, c]), (0, 0), quarter) for c in range(3)]
    pieces.append(Piece(3, (wo_s, wo_s), (0, quarter), quarter))
    for i in range(units // BLOCK):
        pieces.append(Piece(4 + 2 * i, (w1_s.at[0, i], w1_s.at[1, i]), (0, 0), width))
        pieces.append(Piece(5 + 2 * i, (w2_s.at[0], w2_s.at[1]), (i * BLOCK, i * BLOCK), BLOCK))
    pl.semaphore_wait(barrier, len(partners))
    unit_copy = remote(bias_u, uoth, wsem, 3 * len(pieces), across)
    head_copy = remote(bias_qv, voth, wsem, 3 * len(pieces) + 1, across)
    get_wq.wait()
    get_wo.wait()
    for item in pieces[:4]:
        item.copies[0].start()

    inside_loop = []

    def service(name, act):
        def at_point(k, ask):
            full = f"{name}{k}"
            if ask:
                return full in PLAN or full in WEIGHT_PLAN
            inside_loop.append(full)
            act(full)
            inside_loop.pop()

        return at_point

    def pass_on(name):
        for i in WEIGHT_PLAN.get(name, ()):
            if pieces[i].stage < 1:
                pieces[i].advance()

    def have_weight(*which):
        for i in which:
            while pieces[i].stage < 2:
                pieces[i].advance()

    ln1_gain, ln1_bias, out_bias, ln2_gain, ln2_bias, fc2_bias = (
        ref[...].reshape(1, width) for ref in (gain1, bias1, bias_o, gain2, bias2, bias_f)
    )
    get_tok.wait()

    def first_norm(at):
        plane = core * (count // (SIDE * SIDE)) + at // (SIDE * SIDE)
        line = (at // SIDE) % SIDE
        shape = (SIDE, width // 3)
        for k in range(8):
            spot = jnp.concatenate(
                [jnp.broadcast_to(table[pl.ds(plane, 1)], shape), jnp.broadcast_to(table[pl.ds(line + k, 1)], shape), table[...]], axis=1
            )
            span = pl.ds(aligned(at + k * SIDE, SIDE), SIDE)
            stream = tok_s[span].astype(F32) + spot
            sin_s[span] = stream
            xhat, _ = norm_stats(stream)
            n1_s[span] = (xhat * ln1_gain + ln1_bias).astype(BF16)

    loop(count, 8 * SIDE, first_norm)
    doc = ids[pl.ds(chip, 1), :]
    starts = [jnp.zeros((1, 1), F32)]
    starts += [jnp.sum(jnp.where(doc < v, 1.0, 0.0), axis=1, keepdims=True) for v in range(1, 4)]
    starts.append(jnp.full((1, 1), rows, F32))
    turn = jnp.zeros((1, 1), F32)
    for v in range(4):
        turn += jnp.where(starts[v + 1] - starts[v] == count, starts[v], 0.0)
    turn_here = turn - (core * count).astype(F32)

    def wrapped(v):
        v = jnp.where(v >= rows, v - rows, v)
        return jnp.where(v < 0, v + rows, v)

    along = lax.broadcasted_iota(jnp.int32, (64, rows), 1).astype(F32)

    def matches(at, shift):
        down = (lax.broadcasted_iota(jnp.int32, (64, 128), 0) + at).astype(F32)
        target = jnp.concatenate([wrapped(down + shift)] * (rows // 128), axis=1)
        return jnp.where(target == along, 1.0, 0.0).astype(BF16)

    def rotations(at):
        roll_s[pl.ds(at, 64)] = matches(at, turn_here)
        where = wrapped((lax.broadcasted_iota(jnp.int32, (64, 128), 0) + at).astype(F32) + turn)
        mine = sum(jnp.where(where >= starts[v], 1.0, 0.0) for v in range(1, 4))
        slot = (lax.broadcasted_iota(jnp.int32, (64, 128), 1) % HEAD).astype(F32)
        sq_s[pl.ds(at, 64)] = jnp.where((slot < 4) & (slot != mine), 1.0, 0.0).astype(BF16)
        sk_s[pl.ds(at, 64)] = jnp.where(slot == mine, NEG_LARGE, 0.0).astype(BF16)

    def back_rotations(at):
        back_s[pl.ds(at, 64)] = matches(at, -turn_here)

    for copy in get_w1:
        copy.wait()
    get_w2.wait()
    for item in pieces[4:]:
        item.copies[0].start()
    n1_copy = remote(n1_s.at[pl.ds(0, count)], n1_s.at[pl.ds(count, count)], csem, 0, sib)
    get_cot.wait()
    cot_copy = remote(cot_s.at[pl.ds(0, count)], cot_s.at[pl.ds(count, count)], csem, 1, sib)

    def rotate(at):
        nr_s[pl.ds(at, BLOCK)] = dot(roll_s[pl.ds(at, BLOCK)], n1_s[...]).astype(BF16)

    def project(j, at):
        n = nr_s[pl.ds(at, BLOCK)]
        biases = bias_qv if j == 0 else voth
        q = (dot_nt(n, wq_s[j, 0]) + biases[0:1]).astype(BF16) * SCALE
        k = dot_nt(n, wq_s[j, 1]).astype(BF16)
        v = (dot_nt(n, wq_s[j, 2]) + biases[1:2]).astype(BF16)
        q_s[j, pl.ds(at, BLOCK), :quarter] = q
        k_s[pl.ds(at, BLOCK), :quarter] = k
        v_s[j, pl.ds(at, BLOCK), :quarter] = v
        kt_s[j * quarter : (j + 1) * quarter, pl.ds(at, BLOCK)] = k.T * SCALE

    blocks = [(b, at) for b in range(2) for at in range(0, count, BLOCK)]

    def attend(j):
        for head in range(heads):
            at = 512 + 256 * head
            a_s[:, at : at + 128] = head_lanes(q_s.at[j], head, sq_s[...])
            a_s[:, at + 128 : at + 256] = head_lanes(k_s, head, sk_s[...])
        for at in range(0, rows, BLOCK):
            ou_s[:quarter, at : at + BLOCK] = v_s[j, at : at + BLOCK, :quarter].T

        def tile(here):
            b = here // count
            at = aligned(here % count, BLOCK)
            keys = pl.ds(aligned(b * count, count), count)
            for head in range(heads):
                column = 512 + 256 * head
                s = dot_nt(a_s[keys, column + 128 : column + 256], a_s[pl.ds(here, BLOCK), column : column + 128])
                m = jnp.max(s, axis=0, keepdims=True)
                e = jnp.exp(s - m)
                r = 1.0 / column_sum(e)
                low = e.astype(BF16)
                span = slice(head * HEAD, head * HEAD + HEAD)
                to = slice(j * quarter + head * HEAD, j * quarter + head * HEAD + HEAD)
                e_s[j * heads + head, b, :, pl.ds(at, BLOCK)] = low
                ot_s[to, pl.ds(here, BLOCK)] = (dot(ou_s[span, keys], low) * r).astype(BF16)
                r_s[j * heads + head : j * heads + head + 1, pl.ds(here, BLOCK)] = r

        return tile

    loop(rows, 64, rotations)
    n1_copy.wait_recv()
    loop(rows, BLOCK, rotate)
    loop(rows, BLOCK, lambda at: project(0, at))
    pass_on("p0")
    loop(rows, BLOCK, attend(0), service("a", pass_on))
    head_copy.wait_recv()
    have_weight(0, 1, 2)
    loop(rows, BLOCK, lambda at: project(1, at))
    pass_on("p1")
    loop(rows, BLOCK, attend(1), service("c", pass_on))

    have_weight(3)

    def unrotate(at):
        ou_s[:, pl.ds(at, BLOCK)] = dot(ot_s[...], roll_s[:, pl.ds(at, BLOCK)]).astype(BF16)

    loop(count, BLOCK, lambda at: unrotate(count + at))

    def out_part(at):
        return dot_tn(ou_s[:, pl.ds(at, BLOCK)], wo_s[...])

    def att_half(at):
        return half_copy(sb1.at[pl.ds(at, BLOCK)], rb1.at[pl.ds(at, BLOCK)], 2, at)

    def n2_half(at):
        return half_copy(n2_s.at[pl.ds(at, BLOCK)], n2_s.at[pl.ds(aligned(count + at, BLOCK), BLOCK)], 4, at)

    def out_sib(at):
        sb1[pl.ds(at, BLOCK)] = out_part(count + at).astype(BF16)
        att_half(at).start()

    loop(count, BLOCK, out_sib)
    pass_on("u")
    loop(count, BLOCK, unrotate)

    def out_mine(at):
        mid_s[pl.ds(at, BLOCK)] = sin_s[pl.ds(at, BLOCK)] + out_part(at) + out_bias

    loop(count, BLOCK, out_mine)
    pass_on("o")

    def second_norm(at):
        att_half(at).wait_recv()
        for off in range(0, BLOCK, 128):
            spot = pl.ds(aligned(at + off, 128), 128)
            mid = mid_s[spot] + rb1[spot].astype(F32)
            mid_s[spot] = mid
            xhat, _ = norm_stats(mid)
            n2_s[spot] = (xhat * ln2_gain + ln2_bias).astype(BF16)
        n2_half(at).start()

    loop(count, BLOCK, second_norm)
    pass_on("n")

    base_a = units
    parts = units // BLOCK
    steps = copies_of(len(full_bits))

    class Region:
        def __init__(self, index, row, size, cols, slot, kind, refs, to):
            own_r, oth_r, xr_r, land_r, both_r, rx_r = refs
            self.place, self.slot, self.to, self.xr = (row, size, 0, cols), slot, to, xr_r
            first, after = KINDS[kind]
            self.first = first is not None
            self.stages, self.stage, self.finished, self.sent = [], -1, False, []
            now, parts, used, trail = self.place, 8, 0, []
            sems = iter(range(index * steps, (index + 1) * steps))

            def copy(src, src_at, dst, dst_at, device):
                return described(src.at[self.window(src_at)], dst.at[self.window(dst_at)], gsem, next(sems), device)

            def piece(bits, mask):
                where = now
                for k, b in enumerate(bits):
                    where = self.cut(where, 1 - sides[b] if mask >> k & 1 else sides[b])
                return where

            sums = 1 + len(after) + len(full_bits)
            if self.first:
                keep, give, there = piece((first,), 0), piece((first,), 1), (row // 2, size // 2, 0, cols)
                place = self.landing(0, 4)
                copies = [copy(own_r, give, land_r, place, mate((first,))), copy(oth_r, give, both_r, there, mate((first,)))]
                adds = [(own_r, own_r, keep, [(land_r, place)]), (oth_r, oth_r, keep, [(both_r, there)])]
                self.stages.append((copies, adds, False))
                trail.append(((first,), keep))
                now, parts, used = keep, 4, 4
            self.stages.append(([copy(oth_r, now, xr_r, now, across)], [(own_r, own_r, now, [(xr_r, now)])], False))
            for bits in after:
                parts >>= len(bits)
                keep, copies, terms = piece(bits, 0), [], []
                for mask in range(1, 1 << len(bits)):
                    place = self.landing(used, parts)
                    used += parts
                    terms.append((land_r, place))
                    copies.append(copy(own_r, piece(bits, mask), land_r, place, mate([b for k, b in enumerate(bits) if mask >> k & 1])))
                self.stages.append((copies, [(own_r, own_r, keep, terms)], False))
                trail.append((bits, keep))
                now = keep
            for i, b in enumerate(full_bits):
                place = self.small_place()
                self.stages.append(([copy(own_r, now, rx_r[i], place, mates[b])], [(own_r, own_r, now, [(rx_r[i], place)])], True))
            copies, adds, full = self.stages[-1]
            self.stages[-1] = (copies, [(xr_r,) + adds[0][1:]], full)
            for bits, keep in reversed(trail):
                copies = []
                for mask in range(1, 1 << len(bits)):
                    copies.append(copy(xr_r, keep, xr_r, keep, mate([b for k, b in enumerate(bits) if mask >> k & 1])))
                self.stages.append((copies, [], False))

        def window(self, where):
            row, size, col, cols = where
            return pl.ds(row, size), pl.ds(col, cols)

        def cut(self, where, side):
            row, size, col, cols = where
            if (size // 2) % 16 == 0:
                return aligned(row + side * (size // 2), 16), size // 2, col, cols
            return row, size, aligned(col + side * (cols // 2), 128), cols // 2

        def landing(self, at, parts_here):
            row, rows_one, cols_one = self.slot
            full = self.place[3]
            if cols_one == full:
                return row + at * rows_one, parts_here * rows_one, 0, full
            if parts_here == 1:
                return row + at // 2 * rows_one, rows_one, at % 2 * cols_one, cols_one
            return row + at // 2 * rows_one, parts_here // 2 * rows_one, 0, full

        def small_place(self):
            row, rows_one, cols_one = self.slot
            if cols_one == self.place[3]:
                return row // 7, rows_one, 0, cols_one
            k = (self.place[0] - base_a) // quarter
            return units // 8 + k // 2 * rows_one, rows_one, k % 2 * cols_one, cols_one

        def begin(self, copies):
            for copy in copies:
                copy.start()
            self.sent += copies

        def ready(self, j):
            if self.first:
                self.stage = 0
                self.begin([self.stages[0][0][j]])
            elif j == 1:
                self.stage = 0
                self.begin(self.stages[0][0])

        def add(self, into, base, where, terms):
            row, size, col, cols = where
            step = 64 if size % 64 == 0 else 48 if size % 48 == 0 else 32

            def body(off):
                to = (pl.ds(aligned(row + off, 16), step), pl.ds(col, cols))
                parts_in = [ref[pl.ds(aligned(r + off, 16), step), pl.ds(c, cols)] for ref, (r, _, c, _) in terms]
                if len(parts_in) == 1:
                    into[to] = base[to] + parts_in[0]
                else:
                    into[to] = sum((v.astype(F32) for v in parts_in), base[to].astype(F32)).astype(BF16)

            if inside_loop:
                for off in range(0, size, step):
                    body(off)
            else:
                loop(size, step, body)

        def advance(self):
            if self.finished or self.stage < 0:
                return
            copies, adds, full = self.stages[self.stage]
            for copy in copies:
                copy.wait_recv()
            if full:
                for copy in copies:
                    copy.wait_send()
                self.sent = [c for c in self.sent if all(c is not d for d in copies)]
            for item in adds:
                self.add(*item)
            self.stage += 1
            if self.stage < len(self.stages):
                self.begin(self.stages[self.stage][0])
                return
            self.finished = True
            to_write.append(self)

    chunks = []
    refs = (own, oth, xr, land, land_both, rx)
    for i in range(parts):
        slot = (i * 7 * (BLOCK // 8), BLOCK // 8, width)
        to = g2_h.at[pl.ds(i * BLOCK, BLOCK)]
        chunks.append(Region(2 * i, i * BLOCK, BLOCK, width, slot, ORDERS[2 * i], refs, to))
        refs_one = tuple(ref.at[i] for ref in (own1, oth1, xr1, land1, land1_both)) + ([ref.at[i] for ref in rx1],)
        to = g1_h.at[:, pl.ds(i * BLOCK, BLOCK)]
        chunks.append(Region(2 * i + 1, 0, width, BLOCK, (0, width // 8, BLOCK), ORDERS[2 * i + 1], refs_one, to))
    for i in range(4):
        slot = (7 * units // 8 + i * quarter, quarter // 4, width // 2)
        to = go_h if i == 0 else gq_h.at[i - 1]
        chunks.append(Region(2 * parts + i, base_a + i * quarter, quarter, width, slot, ORDERS[2 * parts + i], refs, to))
    first_att = 2 * parts

    class Small:
        def __init__(self, tile, index, everywhere, paired, groups):
            self.tile, self.everywhere, self.paired = tile, everywhere, paired
            landings = [near.at[3 * index + k] for k in range(3)] + [far.at[(7 + len(full_bits)) * index + k] for k in range(7 + len(full_bits))]
            sems = iter(range(index * len(landings), (index + 1) * len(landings)))
            landings = iter(landings)

            def stage(devices):
                places = [next(landings) for _ in devices]
                return places, [described(tile, dst, ssem, next(sems), d) for dst, d in zip(places, devices)]

            self.stages = [stage([sib, across, facing])]
            for bits in groups + [(b,) for b in full_bits]:
                masks = range(1, 1 << len(bits))
                self.stages.append(stage([mate([b for k, b in enumerate(bits) if mask >> k & 1]) for mask in masks]))
            self.stage, self.finished = -1, False

        def start(self):
            self.stage = 0
            for copy in self.stages[0][1]:
                copy.start()

        def advance(self):
            if self.finished or self.stage < 0:
                return
            places, copies = self.stages[self.stage]
            for copy in copies:
                copy.wait()
            tile = self.tile
            if self.stage == 0:
                beside, over, facing_ = places
                n, p = self.everywhere, self.paired
                tile[0:n] = (tile[0:n] + beside[0:n]) + (over[0:n] + facing_[0:n])
                tile[n : n + p] = tile[n : n + p] + over[n + p : n + 2 * p]
            else:
                got = [tile[...]] + [place[...] for place in places]
                while len(got) > 1:
                    got = [got[k] + got[k + 1] for k in range(0, len(got), 2)]
                tile[...] = got[0]
            self.stage += 1
            if self.stage == len(self.stages):
                self.finished = True
                return
            for copy in self.stages[self.stage][1]:
                copy.start()

    first_small = Small(early, 0, 4, 1, [(b,) for b in half_bits])
    last_small = Small(late, 1, 2, 2, [tuple(half_bits)])

    def ready(i, j):
        chunks[i].ready(j)

    to_write = []

    def write_finished():
        while to_write:
            region = to_write.pop()
            region.done = local(region.xr.at[region.window(region.place)], region.to)

    def hook(name):
        pass_on(name)
        for i in PLAN.get(name, ()):
            (chunks + [last_small, first_small])[i].advance()
            if not inside_loop:
                write_finished()

    def chunk_rows(j, i, at):
        span = pl.ds(at, BLOCK)
        cols = slice(j * units + i * BLOCK, j * units + (i + 1) * BLOCK)
        mine = slice(i * BLOCK, (i + 1) * BLOCK)
        bias = (bias_u if j == 0 else uoth)[mine].reshape(1, BLOCK)
        h = dot(n2_s[span], w1_s[j, i]) + bias
        a, slope = gelu_pair(h)
        a_s[span, cols] = a.astype(BF16)
        g = (dot_nt(cot_s[span], w2_s[j, mine]) * slope).astype(BF16)
        g_s[span, cols] = g

    def chunk_grads(j, i):
        cols = slice(j * units + i * BLOCK, j * units + (i + 1) * BLOCK)
        mine = slice(i * BLOCK, (i + 1) * BLOCK)
        to = oth if j == 1 else own

        def second(at):
            to[pl.ds(i * BLOCK + at, 128)] = dot_tn(a_s[:, pl.ds(cols.start + at, 128)], cot_s[...]).astype(BF16)

        loop(BLOCK, 128, second)
        ready(2 * i, j)
        g = g_s[:, cols]

        if j == 1 and i == 0:

            def turned(at):
                n2t_s[:, pl.ds(at, BLOCK)] = n2_s[pl.ds(at, BLOCK)].T

            loop(rows, BLOCK, turned)

        def first(at):
            (oth1 if j == 1 else own1)[i, pl.ds(at, BLOCK)] = dot(n2t_s[pl.ds(at, BLOCK)], g_s[:, cols]).astype(BF16)

        loop(width, BLOCK, first)
        ready(2 * i + 1, j)
        early[4 + j : 5 + j, mine] = column_sum(g.astype(F32))
        hook(f"f{j}{i}")

    def feed(j, i, first=False):
        if first:
            loop(count, BLOCK, lambda at: chunk_rows(j, i, at))
            hook(f"r{j}{i}.0")
            cot_copy.wait_recv()

            def received(at):
                n2_half(at).wait_recv()
                chunk_rows(j, i, count + at)

            loop(count, BLOCK, received)
            hook(f"r{j}{i}.1")

        else:
            loop(rows, BLOCK, lambda at: chunk_rows(j, i, at), service(f"r{j}{i}.", hook), 2)
        chunk_grads(j, i)

    early[...] = jnp.zeros_like(early)
    late[...] = jnp.zeros_like(late)
    unit_copy.wait_recv()
    for i in range(parts):
        have_weight(4 + 2 * i, 5 + 2 * i)
        feed(1, i, first=i == 0)
        feed(0, i)

    def back_two(at):
        span = pl.ds(at, BLOCK)
        total = None
        for j in range(2):
            for i in range(parts):
                at_col = j * units + i * BLOCK
                term = dot_nt(g_s[span, at_col : at_col + BLOCK], w1_s[j, i])
                total = term if total is None else total + term
        return total

    def mlp_part(at):
        span = pl.ds(at, BLOCK)
        return dot(a_s[span, :units], w2_s[0]) + dot(a_s[span, units:], w2_s[1])

    def gn2_half(at):
        return half_copy(sb2.at[pl.ds(at, BLOCK)], rb2.at[pl.ds(at, BLOCK)], 6, at)

    def dm_half(at):
        return half_copy(n2_s.at[pl.ds(at, BLOCK)], n2_s.at[pl.ds(aligned(count + at, BLOCK), BLOCK)], 10, at)

    def back_two_sib(at):
        sb2[pl.ds(at, BLOCK)] = back_two(count + at).astype(BF16)
        gn2_half(at).start()

    def back_two_mine(at):
        gm_s[pl.ds(at, BLOCK)] = back_two(at)

    def mlp_sib(at):
        sb1[pl.ds(at, BLOCK)] = mlp_part(count + at).astype(BF16)

    loop(count, BLOCK, back_two_sib)
    hook("g0")
    loop(count, BLOCK, back_two_mine)
    hook("gn2")

    def second_back(at):
        gn2_half(at).wait_recv()
        n2_half(at).wait_send()
        for off in range(0, BLOCK, 128):
            spot = pl.ds(aligned(at + off, 128), 128)
            xhat, sigma = norm_stats(mid_s[spot])
            grad = gm_s[spot] + rb2[spot].astype(F32)
            cot = cot_s[spot].astype(F32)
            back = cot + norm_back(grad, ln2_gain, xhat, sigma)
            gm_s[spot] = back
            n2_s[spot] = back.astype(BF16)
            early[0:1] += column_sum(back)
            early[1:2] += column_sum(grad * xhat)
            early[2:3] += column_sum(grad)
            early[3:4] += column_sum(cot)
        dm_half(at).start()

    loop(count, BLOCK, second_back)
    hook("lb")
    for at in range(0, count, BLOCK):
        att_half(at).wait_send()
    loop(count, BLOCK, mlp_sib)
    mlp_copy = remote(sb1, rb1, csem, 8, sib)
    first_small.start()
    hook("ln2")

    loop(rows, 64, back_rotations)
    for at in range(0, count, BLOCK):
        dm_half(at).wait_recv()

    start = base_a + quarter
    zero = jnp.zeros((count, 128), BF16)
    grad_s = dq_s = ou_s
    n1_copy.wait_send()

    def keep_gradient(j, c):
        to = oth if j == 1 else own
        low = start + c * quarter
        dt = ot_s.at[j * quarter : (j + 1) * quarter]

        def columns(at):
            to[low : low + quarter, pl.ds(at, BLOCK)] = dot(dt[...], nr_s[:, pl.ds(at, BLOCK)]).astype(BF16)

        loop(width, BLOCK, columns)
        ready(first_att + 1 + c, j)
        if c != 1:
            d = g_s[:, (3 * j + c) * BLOCK : (3 * j + c) * BLOCK + quarter]
            late[2 + c // 2 + 2 * j : 3 + c // 2 + 2 * j, :quarter] = column_sum(d.astype(F32))

    def values_back(j):
        base = j * quarter
        to = oth if j == 1 else own

        def weight(at):
            to[base_a : base_a + quarter, pl.ds(at, BLOCK)] = dot(ou_s[base : base + quarter], n2_s[:, pl.ds(at, BLOCK)]).astype(BF16)

        loop(width, BLOCK, weight)
        ready(first_att, j)

        def output(at):
            grad_s[base : base + quarter, pl.ds(at, BLOCK)] = dot_nt(wo_s[base : base + quarter], n2_s[pl.ds(at, BLOCK)]).astype(BF16)

        loop(rows, BLOCK, output)
        hook(f"w{j}.0")
        go_s = n1_s.at[:, 256 * j : 256 * (j + 1)]

        def scale(at):
            here = pl.ds(at, BLOCK)
            grad_t = dot_nt(grad_s[base : base + quarter], roll_s[here])
            for head in range(heads):
                row = j * heads + head
                r = r_s[row : row + 1, here]
                g = grad_t[head * HEAD : (head + 1) * HEAD]
                at_head = slice(base + head * HEAD, base + (head + 1) * HEAD)
                in_s[row : row + 1, here] = column_sum(g * ot_s[at_head, here].astype(F32)) * r
                gt_s[at_head, here] = (g * r).astype(BF16)
            go_s[here, :quarter] = gt_s[base : base + quarter, here].T

        loop(rows, BLOCK, scale)

        def block(at):
            here = pl.ds(at, count)
            b = at // count
            dv = [None, None]
            for head in range(heads):
                tile = head // 2
                gh = jnp.where(lane_half(count, head % 2 == 1), go_s[here, 128 * tile : 128 * tile + 128], zero)
                part = dot(e_s[j * heads + head, b], gh)
                dv[tile] = part if dv[tile] is None else dv[tile] + part
            dv = jnp.concatenate(dv, axis=1)[:, :quarter].astype(BF16)
            g_s[here, (3 * j + 2) * BLOCK : (3 * j + 2) * BLOCK + quarter] = dv
            ot_s[base : base + quarter, here] = dv.T

        loop(rows, count, block)
        hook(f"w{j}.1")
        keep_gradient(j, 2)
        hook(f"v{j}")

    def scores_back(j):
        base = j * quarter

        def block(at):
            here = pl.ds(at, count)
            b = at // count
            dk = [None, None]
            for head in range(heads):
                tile = head // 2
                row = j * heads + head
                half = lane_half(count, head % 2 == 1)
                lanes = slice(128 * tile, 128 * tile + 128)
                vh = jnp.where(half, v_s[j, here, lanes], zero)
                qh = jnp.where(half, q_s[j, here, lanes], zero)
                last_row = min(128 * tile + 128, quarter)
                vh = vh[:, : last_row - 128 * tile]
                ds = n2t_s.at[:count, head * count : (head + 1) * count] if head < 2 else ds_s
                for off in range(0, count, BLOCK):
                    some = pl.ds(aligned(at + off, BLOCK), BLOCK)
                    dp_t = dot(vh, gt_s[base + 128 * tile : base + last_row, some])
                    grad = (dp_t - in_s[row : row + 1, some]).astype(BF16)
                    ds[:, off : off + BLOCK] = grad * e_s[row, b, :, off : off + BLOCK]
                part = dot(ds[...], qh)
                dk[tile] = part if dk[tile] is None else dk[tile] + part
                kth = kt_s[base + head * HEAD : base + head * HEAD + HEAD, here]
                dq_s[base + head * HEAD : base + head * HEAD + HEAD, here] = dot(kth, ds[...]).astype(BF16)
            dk = jnp.concatenate(dk, axis=1)[:, :quarter].astype(BF16)
            g_s[here, (3 * j + 1) * BLOCK : (3 * j + 1) * BLOCK + quarter] = dk
            ot_s[base : base + quarter, here] = dk.T
            g_s[here, 3 * j * BLOCK : 3 * j * BLOCK + quarter] = dq_s[base : base + quarter, here].T

        loop(rows, count, block, service(f"b{j}.", hook))
        keep_gradient(j, 1)
        hook(f"k{j}")
        ot_s[base : base + quarter] = dq_s[base : base + quarter]
        keep_gradient(j, 0)
        hook(f"s{j}")

    values_back(1)
    scores_back(1)
    values_back(0)
    scores_back(0)

    def finish_out(at):
        span = pl.ds(at, BLOCK)
        mid_s[span] = mid_s[span] + mlp_part(at) + fc2_bias

    loop(count, BLOCK, finish_out)
    hook("fo")
    mlp_copy.wait_recv()

    def write_out(at):
        spot = pl.ds(at, 128)
        tok_s[spot] = (mid_s[spot] + rb1[spot].astype(F32)).astype(BF16)

    loop(count, 128, write_out)
    put_out = local(tok_s, out_h)
    hook("fin")

    def back_one(at):
        total = None
        for j in range(2):
            for c in range(3):
                d = g_s[pl.ds(at, BLOCK), (3 * j + c) * BLOCK : (3 * j + c) * BLOCK + quarter]
                term = dot(d, wq_s[j, c])
                total = term if total is None else total + term
        n2_s[pl.ds(at, BLOCK)] = total.astype(BF16)

    for at in range(0, count, BLOCK):
        dm_half(at).wait_send()
    loop(rows, BLOCK, back_one, service("d.", hook), 2)
    for at in range(0, count, BLOCK):
        gn2_half(at).wait_send()

    def gn1_half(at):
        return half_copy(sb2.at[pl.ds(at, BLOCK)], rb2.at[pl.ds(at, BLOCK)], 12, at)

    def back_one_sib(at):
        sb2[pl.ds(at, BLOCK)] = dot(back_s[pl.ds(count + at, BLOCK)], n2_s[...]).astype(BF16)
        gn1_half(at).start()

    def back_one_mine(at):
        mid_s[pl.ds(at, BLOCK)] = dot(back_s[pl.ds(at, BLOCK)], n2_s[...])

    loop(count, BLOCK, back_one_sib)
    loop(count, BLOCK, back_one_mine)
    hook("e.0")
    mlp_copy.wait_send()

    def first_back(at):
        gn1_half(at).wait_recv()
        for off in range(0, BLOCK, 128):
            spot = pl.ds(aligned(at + off, 128), 128)
            xhat, sigma = norm_stats(sin_s[spot])
            grad = mid_s[spot] + rb2[spot].astype(F32)
            sb1[spot] = (gm_s[spot] + norm_back(grad, ln1_gain, xhat, sigma)).astype(BF16)
            late[0:1] += column_sum(grad * xhat)
            late[1:2] += column_sum(grad)

    loop(count, BLOCK, first_back)
    put_in = local(sb1, ing_h)
    last_small.start()
    hook("e.1")
    hook("tail")
    left = [first_small, last_small] + chunks
    while left:
        for item in left:
            item.advance()
            write_finished()
        left = [item for item in left if not item.finished]

    for row, source, at in ((0, late, 0), (1, late, 1), (2, early, 0), (3, early, 1), (4, early, 2), (5, early, 3), (8, early, 4), (9, late, 2), (10, late, 3)):
        small_o[row : row + 1] = source[at : at + 1]

    passed = [copy for item in pieces for copy in item.copies]
    for copy in [unit_copy, head_copy, cot_copy] + [gn1_half(at) for at in range(0, count, BLOCK)] + passed:
        copy.wait_send()
    for chunk in chunks:
        for copy in chunk.sent:
            copy.wait_send()
        chunk.done.wait()
    put_out.wait()
    put_in.wait()


def copies_of(full):
    most = 0
    for kind in ORDERS:
        first, after = KINDS[kind]
        most = max(most, 1 + full + 2 * sum((1 << len(bits)) - 1 for bits in after) + (0 if first is None else 3))
    return most


def call_layer(dp_size, tokens, cotangent, ids, table, vectors, wq, wo, w1, w2):
    count, width = tokens.shape
    rows = 2 * count
    quarter = wo.shape[0]
    units = w1.shape[1]
    heads = quarter // HEAD
    grad_rows = units + 4 * quarter
    parts = units // BLOCK
    bits = [b for b in range(20) if (1 << b) < dp_size]
    half_bits = bits[:3]
    shape = jax.ShapeDtypeStruct
    vm = pltpu.VMEM
    regions = 2 * (units // BLOCK) + 4
    steps = copies_of(len(bits) - len(half_bits))
    fetched = 4 + 2 * (units // BLOCK)
    scratch = (
        [vm((count, width), BF16), vm((rows, width), BF16)]
        + [vm((count, width), F32)] * 3
        + [vm((rows, width), BF16)] * 2
        + [vm((width, rows), BF16)]
        + [vm((2,) + wq.shape, BF16), vm((2 * quarter, width), BF16), vm((2, units // BLOCK, width, BLOCK), BF16), vm((2,) + w2.shape, BF16)]
        + [vm((2, rows, 256), BF16)] * 2
        + [vm((2 * quarter, rows), BF16)] * 4
        + [vm((8, rows), F32)] * 2
        + [vm((2 * heads, 2, count, count), BF16)]
        + [vm((rows, rows), BF16)] * 2
        + [vm((rows, width), BF16), vm((count, count), BF16)]
        + [vm((rows, 2 * units), BF16)] * 2
        + [vm((count, width), BF16)] * 4
        + [vm((grad_rows, width), BF16)] * 3
        + [vm((7 * units // 8 + 4 * quarter, width), BF16), vm((units // 2, width), BF16)]
        + [vm((parts, width, BLOCK), BF16)] * 3
        + [vm((parts, 7 * width // 8, BLOCK), BF16), vm((parts, width // 2, BLOCK), BF16)]
        + [vm((grad_rows >> len(half_bits), width), BF16)] * (len(bits) - len(half_bits))
        + [vm((parts, width // 8, BLOCK), BF16)] * (len(bits) - len(half_bits))
        + [vm((units,), F32), vm((2, quarter), F32), vm((8, width), F32), vm((8, width), F32)]
        + [vm((6, 8, width), F32), vm((14 + 2 * (len(bits) - 3), 8, width), F32)]
        + [pltpu.SemaphoreType.DMA((8 + units // BLOCK + regions,))]
        + [pltpu.SemaphoreType.DMA((2, n)) for n in (3 * fetched + 2, 14, regions * steps, 2 * (10 + len(bits) - 3))]
    )
    anywhere = pl.BlockSpec(memory_space=pl.ANY)
    inside = pl.BlockSpec(memory_space=pltpu.VMEM)
    return pl.pallas_call(
        functools.partial(layer, dp_size, half_bits),
        out_shape=[shape((count, width), BF16)] * 2
        + [shape(w2.shape, BF16), shape(w1.shape, BF16), shape(wo.shape, BF16), shape(wq.shape, BF16), shape((16, width), F32)],
        in_specs=[anywhere] * 2 + [inside] * (2 + len(vectors)) + [anywhere] * 4,
        out_specs=[anywhere] * 6 + [inside],
        scratch_shapes=scratch,
        compiler_params=pltpu.CompilerParams(vmem_limit_bytes=VMEM_LIMIT, collective_id=0, has_side_effects=True),
        name="layer",
    )(tokens, cotangent, ids, table, *vectors, wq, wo, w1, w2)


def finish(*refs):
    sources, small, rest = refs[:6], refs[6], refs[7:]
    results, vectors, rest = rest[:6], rest[6:14], rest[14:]
    narrow, wide, (get, put) = rest[:6], rest[6:10], rest[10:]
    blocks = []
    for k, src in enumerate(sources):
        if src.ndim == 3:
            places = list(range(src.shape[0]))
        else:
            step = min(BLOCK, src.shape[0])
            places = [pl.ds(at, step) for at in range(0, src.shape[0], step)]
        for at in places:
            low = narrow[k].at[at]
            blocks.append((src.at[at], low, low if k < 2 else wide[k - 2].at[at], results[k].at[at]))
    reads = [pltpu.make_async_copy(src, low, get.at[n]) for n, (src, low, _, _) in enumerate(blocks)]
    writes = [pltpu.make_async_copy(high, dst, put.at[n]) for n, (_, _, high, dst) in enumerate(blocks)]
    for copy in reads:
        copy.start()
    for i in range(6):
        vectors[i][...] = small[i]
    vectors[6][...] = small[8, : vectors[6].shape[0]]
    vectors[7][...] = small[9:11, : vectors[7].shape[1]]
    for read, write, (_, low, high, _) in zip(reads, writes, blocks):
        read.wait()
        if high is not low:

            def cast(at, low=low, high=high):
                high[pl.ds(at, 64)] = low[pl.ds(at, 64)].astype(F32)

            loop(low.shape[0], 64, cast)
        write.start()
    for copy in writes:
        copy.wait()


def call_finish(arrays, small, units, quarter):
    width = small.shape[1]
    shape = jax.ShapeDtypeStruct
    extents = [(width,)] * 6 + [(units,), (2, quarter)]
    kinds = [BF16, BF16, F32, F32, F32, F32]
    anywhere = pl.BlockSpec(memory_space=pl.ANY)
    inside = pl.BlockSpec(memory_space=pltpu.VMEM)
    grads = arrays[2:]
    return pl.pallas_call(
        finish,
        in_specs=[anywhere] * len(arrays) + [inside],
        out_specs=[anywhere] * len(arrays) + [inside] * len(extents),
        out_shape=[shape(a.shape, k) for a, k in zip(arrays, kinds)] + [shape(e, F32) for e in extents],
        scratch_shapes=[pltpu.VMEM(a.shape, BF16) for a in arrays]
        + [pltpu.VMEM(a.shape, F32) for a in grads]
        + [pltpu.SemaphoreType.DMA((16,)), pltpu.SemaphoreType.DMA((16,))],
        compiler_params=pltpu.CompilerParams(vmem_limit_bytes=VMEM_LIMIT),
        name="finish",
    )(*arrays, small)


def per_device(
    tokens, segment_ids, ln1_gain, ln1_bias, qkv_weight, qv_bias, out_weight, out_bias,
    ln2_gain, ln2_bias, fc1_weight, fc1_bias, fc2_weight, fc2_bias, cotangent,
):
    width = tokens.shape[1]
    freq_count = width // 6
    frequency = 10000.0 ** (-jnp.arange(freq_count, dtype=F32) / freq_count)
    angles = jnp.arange(SIDE, dtype=F32)[:, None] * frequency[None, :]
    table = jnp.concatenate([jnp.sin(angles), jnp.cos(angles)], axis=1)
    vectors = (ln1_gain, ln1_bias, out_bias, ln2_gain, ln2_bias, fc2_bias, fc1_bias, qv_bias)
    *arrays, small = call_layer(
        lax.axis_size("dp"), tokens, cotangent, segment_ids, table, vectors, qkv_weight.transpose(0, 2, 1), out_weight, fc1_weight, fc2_weight
    )
    out, ing, g2, g1, go, gq, a0, a1, a2, a3, a4, a5, g_units, g_heads = call_finish(arrays, small, fc1_weight.shape[1], out_weight.shape[0])
    return (out, ing, a0, a1, gq.transpose(0, 2, 1), g_heads, go, a2, a3, a4, g1, g_units, g2, a5)


def solution(mesh):
    placed = (
        P(("dp", "tensor"), None),
        P("dp", None),
        P(),
        P(),
        P(None, None, "tensor"),
        P(None, "tensor"),
        P("tensor", None),
        P(),
        P(),
        P(),
        P(None, "tensor"),
        P("tensor"),
        P("tensor", None),
        P(),
        P(("dp", "tensor"), None),
    )
    return jax.shard_map(
        per_device,
        mesh=mesh,
        in_specs=placed,
        out_specs=(
            P(("dp", "tensor"), None),
            P(("dp", "tensor"), None),
            P(),
            P(),
            P(None, None, "tensor"),
            P(None, "tensor"),
            P("tensor", None),
            P(),
            P(),
            P(),
            P(None, "tensor"),
            P("tensor"),
            P("tensor", None),
            P(),
        ),
        check_vma=False,
    )
```

```python
import functools
import math

import jax
import jax.numpy as jnp
from jax import lax
from jax.experimental import pallas as pl
from jax.experimental.pallas import tpu as pltpu
from jax.sharding import PartitionSpec as P

HEAD = 64
SIDE = 16
EPSILON = 1e-06
NEG_LARGE = -1e30
SCALE = HEAD ** (-0.5)
F32 = jnp.float32
BF16 = jnp.bfloat16
VMEM_LIMIT = 64 * 1024 * 1024 - 128 * 1024
MESH = pl.DeviceIdType.MESH
BLOCK = 256
KINDS = {
    "A": (None, ((0,), (1,), (2,))),
    "B": (None, ((1,), (0,), (2,))),
    "D": (None, ((0,), (1, 2))),
    "E": (None, ((0, 1, 2),)),
    "C": (None, ((0, 1), (2,))),
    "Y": (0, ((1,), (2,))),
    "Z": (1, ((0,), (2,))),
    "YD": (0, ((1, 2),)),
    "S": (None, (("p",), ("q",), (2,))),
    "SD": (None, (("p",), ("q", 2))),
    "SF": ("p", (("q",), (2,))),
    "SFD": ("p", (("q", 2),)),
}
ORDERS = ("D", "SFD", "SFD", "Z", "A", "YD", "D", "D", "C", "B")
WEIGHT_PLAN = {"p0": (0,), "a0": (1,), "a2": (2,), "p1": (3,), "c0": (4,), "c3": (5,), "n": (6,), "r10.1": (7,), "r00.1": (8,), "r11.1": (9,)}
PLAN = {
    "f01": (1,),
    "r12.1": (0,),
    "r02.0": (2,),
    "r02.1": (1,),
    "g0": (0,),
    "lb": (3, 4, 1),
    "w1.0": (2, 0),
    "w1.1": (-1, 5),
    "v1": (3,),
    "b1.0": (4, 1),
    "b1.1": (-1, 2, 3),
    "k1": (0,),
    "s1": (4, 5),
    "w0.0": (6, 1, -1),
    "v0": (2, 9),
    "b0.0": (0, 3, 4, 6),
    "b0.1": (2, 5),
    "k0": (8, -1, 9),
    "s0": (3,),
    "fo": (7, 4),
    "d.0": (6,),
    "d.1": (9,),
    "e.0": (5, 8, 3),
    "e.1": (4, 7),
    "tail": (6, 9, 8, -2, 5, 3, 4, 7, 9, 8, 6, -2, 9, 7, 8, 9, 7),
}


def dot(a, b):
    return jnp.dot(a, b, preferred_element_type=F32)


def dot_nt(a, b):
    return lax.dot_general(a, b, (((1,), (1,)), ((), ())), preferred_element_type=F32)


def dot_tn(a, b):
    return lax.dot_general(a, b, (((0,), (0,)), ((), ())), preferred_element_type=F32)


def lane_half(rows, upper):
    lanes = lax.broadcasted_iota(jnp.int32, (rows, 128), 1)
    return lanes >= HEAD if upper else lanes < HEAD


def head_lanes(ref, head, filler):
    tile = ref[:, 128 * (head // 2) : 128 * (head // 2) + 128]
    return jnp.where(lane_half(tile.shape[0], head % 2 == 1), tile, filler)


def gelu_pair(h):
    cdf = 0.5 + 0.5 * lax.erf(h * 0.7071067811865476)
    return h * cdf, cdf + h * jnp.exp(-0.5 * h * h) * 0.3989422804014327


def norm_stats(v):
    centred = v - jnp.mean(v, axis=-1, keepdims=True)
    sigma = lax.rsqrt(jnp.mean(centred * centred, axis=-1, keepdims=True) + EPSILON)
    return centred * sigma, sigma


def norm_back(grad, gain, xhat, sigma):
    g = grad * gain
    return sigma * (g - jnp.mean(g, axis=-1, keepdims=True) - xhat * jnp.mean(g * xhat, axis=-1, keepdims=True))


def column_sum(v):
    return jnp.sum(v, axis=0, keepdims=True)


def aligned(v, unit):
    return v if isinstance(v, int) else pl.multiple_of(v, unit)


def loop(count, step, body, service=None, every=1):
    def run(i, carry):
        body(aligned(i * step, step))
        if service is not None:
            for k in range(count // step // every):
                if service(k, True):
                    pl.when(i == every * (k + 1) - 1)(functools.partial(service, k, False))
        return carry

    lax.fori_loop(0, count // step, run, 0)


def layer(
    dp_size, half_bits,
    tok_h, cot_h, ids, gain1, bias1, bias_o, gain2, bias2, bias_f, bias_u, bias_qv, wq_h, wo_h, w1_h, w2_h,
    out_h, ing_h, g2_h, g1_h, go_h, gq_h, small_o,
    tok_s, cot_s, sin_s, mid_s, gm_s, n1_s, n2_s, n2t_s, wq_s, wo_s, w1_s, w2_s,
    q_s, v_s, kt_s, ot_s, ou_s, gt_s, r_s, in_s, e_s, roll_s, back_s, nr_s, ds_s, a_s, g_s, sb1, sb2, rb1, rb2,
    own, oth, xr, land, land_both, own1, oth1, xr1, land1, land1_both, *rest,
):
    rest = list(rest)
    full_bits = [b for b in range(20) if (1 << b) < dp_size and b not in half_bits]
    rx = [rest.pop(0) for _ in full_bits]
    rx1 = [rest.pop(0) for _ in full_bits]
    table, uoth, voth, early, late, near, far, lsem, wsem, csem, gsem, ssem = rest

    count, width = tok_s.shape
    rows = 2 * count
    quarter = wo_h.shape[0]
    units = w1_h.shape[1]
    heads = quarter // HEAD
    place = lax.axis_index("tensor")
    dp = lax.axis_index("dp")
    chip = place // 2
    core = place % 2
    sib = {"tensor": chip * 2 + 1 - core}
    across = {"tensor": (1 - chip) * 2 + core}
    facing = {"tensor": (1 - chip) * 2 + 1 - core}
    all_bits = list(half_bits) + full_bits
    sides = {b: (dp // (1 << b)) % 2 for b in all_bits}

    ways = {b: (1 - 2 * sides[b]) * (1 << b) for b in all_bits}
    sides["p"] = sides[0] + (sides[1] - sides[0]) * core
    sides["q"] = sides[1] + (sides[0] - sides[1]) * core
    ways["p"] = ways[0] + (ways[1] - ways[0]) * core
    ways["q"] = ways[1] + (ways[0] - ways[1]) * core

    def mate(bits):
        return {"dp": dp + sum(ways[b] for b in bits)}

    def described(src, dst, sems, index, device):
        return pltpu.make_async_remote_copy(
            src_ref=src, dst_ref=dst, send_sem=sems.at[0, index], recv_sem=sems.at[1, index], device_id=device, device_id_type=MESH
        )

    mates = {b: mate((b,)) for b in all_bits}
    groups = {(b,) for b in full_bits}
    for mask in range(1, 1 << len(half_bits)):
        groups.add(tuple(b for k, b in enumerate(half_bits) if mask >> k & 1))

    barrier = pltpu.get_barrier_semaphore()
    partners = [sib, across, facing] + [mate(bits) for bits in sorted(groups)]
    for partner in partners:
        pl.semaphore_signal(barrier, inc=1, device_id=partner, device_id_type=MESH)

    sq_s, sk_s, k_s = a_s.at[:, 0:128], a_s.at[:, 128:256], a_s.at[:, 256:512]
    local_used = [0]

    def local(src, dst):
        copy = pltpu.make_async_copy(src, dst, lsem.at[local_used[0]])
        local_used[0] += 1
        copy.start()
        return copy

    def remote(src, dst, sems, index, device):
        copy = pltpu.make_async_remote_copy(
            src_ref=src, dst_ref=dst, send_sem=sems.at[0, index], recv_sem=sems.at[1, index], device_id=device, device_id_type=MESH
        )
        copy.start()
        return copy

    def half_copy(src, dst, first, at):
        return pltpu.make_async_remote_copy(
            src_ref=src,
            dst_ref=dst,
            send_sem=csem.at[0, first + at // BLOCK],
            recv_sem=csem.at[1, first + at // BLOCK],
            device_id=sib,
            device_id_type=MESH,
        )

    part = (sides[0] + sides[1]) % 2

    class Piece:
        def __init__(self, index, refs, at, extent):
            size = extent // 4

            def some(k, first, size):
                return refs[k].at[pl.ds(aligned(at[k] + part * (extent // 2) + first, 16), size)]

            self.copies = [described(some(0, 0, 2 * size), some(1, 0, 2 * size), wsem, 3 * index, across)]
            for k in range(2):
                block = some(1, k * size, size)
                self.copies.append(described(block, block, wsem, 3 * index + 1 + k, mates[k]))
            self.stage = 0

        def advance(self):
            if self.stage == 0:
                self.copies[0].wait_recv()
                self.copies[1].start()
                self.copies[2].start()
            else:
                self.copies[1].wait_recv()
                self.copies[2].wait_recv()
            self.stage += 1

    pieces = [Piece(c, (wq_h.at[c], wq_s.at[1, c]), (0, 0), quarter) for c in range(3)]
    pieces.append(Piece(3, (wo_h, wo_s), (0, quarter), quarter))
    for i in range(units // BLOCK):
        pieces.append(Piece(4 + 2 * i, (w1_s.at[0, i], w1_s.at[1, i]), (0, 0), width))
        pieces.append(Piece(5 + 2 * i, (w2_s.at[0], w2_s.at[1]), (i * BLOCK, i * BLOCK), BLOCK))
    pl.semaphore_wait(barrier, len(partners))
    unit_copy = remote(bias_u, uoth, wsem, 3 * len(pieces), across)
    head_copy = remote(bias_qv, voth, wsem, 3 * len(pieces) + 1, across)
    for item in pieces[:4]:
        item.copies[0].start()
    get_tok = local(tok_h, tok_s)
    get_wq = local(wq_h, wq_s.at[0])
    get_cot = local(cot_h, cot_s.at[pl.ds(0, count)])
    get_wo = local(wo_h, wo_s.at[pl.ds(0, quarter)])
    get_w1 = [local(w1_h.at[:, pl.ds(i * BLOCK, BLOCK)], w1_s.at[0, i]) for i in range(units // BLOCK)]
    get_w2 = local(w2_h, w2_s.at[0])

    inside_loop = []

    def service(name, act):
        def at_point(k, ask):
            full = f"{name}{k}"
            if ask:
                return full in PLAN or full in WEIGHT_PLAN
            inside_loop.append(full)
            act(full)
            inside_loop.pop()

        return at_point

    def pass_on(name):
        for i in WEIGHT_PLAN.get(name, ()):
            if pieces[i].stage < 1:
                pieces[i].advance()

    def have_weight(*which):
        for i in which:
            while pieces[i].stage < 2:
                pieces[i].advance()

    ln1_gain, ln1_bias, out_bias, ln2_gain, ln2_bias, fc2_bias = (
        ref[...].reshape(1, width) for ref in (gain1, bias1, bias_o, gain2, bias2, bias_f)
    )
    third = width // 6
    place_k = lax.broadcasted_iota(jnp.int32, (SIDE, third), 1).astype(F32)
    angles = lax.broadcasted_iota(jnp.int32, (SIDE, third), 0).astype(F32) * jnp.exp(place_k * (-math.log(10000.0) / third))
    table[:, :third] = jnp.sin(angles)
    table[:, third:] = jnp.cos(angles)
    get_tok.wait()

    def first_norm(at):
        plane = core * (count // (SIDE * SIDE)) + at // (SIDE * SIDE)
        line = (at // SIDE) % SIDE
        shape = (SIDE, width // 3)
        for k in range(8):
            spot = jnp.concatenate(
                [jnp.broadcast_to(table[pl.ds(plane, 1)], shape), jnp.broadcast_to(table[pl.ds(line + k, 1)], shape), table[...]], axis=1
            )
            span = pl.ds(aligned(at + k * SIDE, SIDE), SIDE)
            stream = tok_s[span].astype(F32) + spot
            sin_s[span] = stream
            xhat, _ = norm_stats(stream)
            n1_s[span] = (xhat * ln1_gain + ln1_bias).astype(BF16)

    loop(count, 8 * SIDE, first_norm)
    doc = ids[pl.ds(chip, 1), :]
    starts = [jnp.zeros((1, 1), F32)]
    starts += [jnp.sum(jnp.where(doc < v, 1.0, 0.0), axis=1, keepdims=True) for v in range(1, 4)]
    starts.append(jnp.full((1, 1), rows, F32))
    turn = jnp.zeros((1, 1), F32)
    for v in range(4):
        turn += jnp.where(starts[v + 1] - starts[v] == count, starts[v], 0.0)
    turn_here = turn - (core * count).astype(F32)

    def wrapped(v):
        v = jnp.where(v >= rows, v - rows, v)
        return jnp.where(v < 0, v + rows, v)

    along = lax.broadcasted_iota(jnp.int32, (64, rows), 1).astype(F32)

    def matches(at, shift):
        down = (lax.broadcasted_iota(jnp.int32, (64, 128), 0) + at).astype(F32)
        target = jnp.concatenate([wrapped(down + shift)] * (rows // 128), axis=1)
        return jnp.where(target == along, 1.0, 0.0).astype(BF16)

    def rotations(at):
        roll_s[pl.ds(at, 64)] = matches(at, turn_here)
        where = wrapped((lax.broadcasted_iota(jnp.int32, (64, 128), 0) + at).astype(F32) + turn)
        mine = sum(jnp.where(where >= starts[v], 1.0, 0.0) for v in range(1, 4))
        slot = (lax.broadcasted_iota(jnp.int32, (64, 128), 1) % HEAD).astype(F32)
        sq_s[pl.ds(at, 64)] = jnp.where((slot < 4) & (slot != mine), 1.0, 0.0).astype(BF16)
        sk_s[pl.ds(at, 64)] = jnp.where(slot == mine, NEG_LARGE, 0.0).astype(BF16)

    def back_rotations(at):
        back_s[pl.ds(at, 64)] = matches(at, -turn_here)

    get_wq.wait()
    get_wo.wait()
    for copy in get_w1:
        copy.wait()
    get_w2.wait()
    for item in pieces[4:]:
        item.copies[0].start()
    n1_copy = remote(n1_s.at[pl.ds(0, count)], n1_s.at[pl.ds(count, count)], csem, 0, sib)
    get_cot.wait()
    cot_copy = remote(cot_s.at[pl.ds(0, count)], cot_s.at[pl.ds(count, count)], csem, 1, sib)

    def rotate(at):
        nr_s[pl.ds(at, BLOCK)] = dot(roll_s[pl.ds(at, BLOCK)], n1_s[...]).astype(BF16)

    def project(j, at):
        n = nr_s[pl.ds(at, BLOCK)]
        biases = bias_qv if j == 0 else voth
        q = (dot_nt(n, wq_s[j, 0]) + biases[0:1]).astype(BF16) * SCALE
        k = dot_nt(n, wq_s[j, 1]).astype(BF16)
        v = (dot_nt(n, wq_s[j, 2]) + biases[1:2]).astype(BF16)
        q_s[j, pl.ds(at, BLOCK), :quarter] = q
        k_s[pl.ds(at, BLOCK), :quarter] = k
        v_s[j, pl.ds(at, BLOCK), :quarter] = v
        kt_s[j * quarter : (j + 1) * quarter, pl.ds(at, BLOCK)] = k.T * SCALE

    blocks = [(b, at) for b in range(2) for at in range(0, count, BLOCK)]

    def attend(j):
        for head in range(heads):
            at = 512 + 256 * head
            a_s[:, at : at + 128] = head_lanes(q_s.at[j], head, sq_s[...])
            a_s[:, at + 128 : at + 256] = head_lanes(k_s, head, sk_s[...])
        for at in range(0, rows, BLOCK):
            ou_s[:quarter, at : at + BLOCK] = v_s[j, at : at + BLOCK, :quarter].T

        def tile(here):
            b = here // count
            at = aligned(here % count, BLOCK)
            keys = pl.ds(aligned(b * count, count), count)
            for head in range(heads):
                column = 512 + 256 * head
                s = dot_nt(a_s[keys, column + 128 : column + 256], a_s[pl.ds(here, BLOCK), column : column + 128])
                m = jnp.max(s, axis=0, keepdims=True)
                e = jnp.exp(s - m)
                r = 1.0 / column_sum(e)
                low = e.astype(BF16)
                span = slice(head * HEAD, head * HEAD + HEAD)
                to = slice(j * quarter + head * HEAD, j * quarter + head * HEAD + HEAD)
                e_s[j * heads + head, b, :, pl.ds(at, BLOCK)] = low
                ot_s[to, pl.ds(here, BLOCK)] = (dot(ou_s[span, keys], low) * r).astype(BF16)
                r_s[j * heads + head : j * heads + head + 1, pl.ds(here, BLOCK)] = r

        return tile

    loop(rows, 64, rotations)
    n1_copy.wait_recv()
    loop(rows, BLOCK, rotate)
    loop(rows, BLOCK, lambda at: project(0, at))
    pass_on("p0")
    loop(rows, BLOCK, attend(0), service("a", pass_on))
    head_copy.wait_recv()
    have_weight(0, 1, 2)
    loop(rows, BLOCK, lambda at: project(1, at))
    pass_on("p1")
    loop(rows, BLOCK, attend(1), service("c", pass_on))

    have_weight(3)

    def unrotate(at):
        ou_s[:, pl.ds(at, BLOCK)] = dot(ot_s[...], roll_s[:, pl.ds(at, BLOCK)]).astype(BF16)

    loop(count, BLOCK, lambda at: unrotate(count + at))

    def out_part(at):
        return dot_tn(ou_s[:, pl.ds(at, BLOCK)], wo_s[...])

    def att_half(at):
        return half_copy(sb1.at[pl.ds(at, BLOCK)], rb1.at[pl.ds(at, BLOCK)], 2, at)

    def n2_half(at):
        return half_copy(n2_s.at[pl.ds(at, BLOCK)], n2_s.at[pl.ds(aligned(count + at, BLOCK), BLOCK)], 4, at)

    def out_sib(at):
        sb1[pl.ds(at, BLOCK)] = out_part(count + at).astype(BF16)
        att_half(at).start()

    loop(count, BLOCK, out_sib)
    pass_on("u")
    loop(count, BLOCK, unrotate)

    def out_mine(at):
        mid_s[pl.ds(at, BLOCK)] = sin_s[pl.ds(at, BLOCK)] + out_part(at) + out_bias

    loop(count, BLOCK, out_mine)
    pass_on("o")

    def second_norm(at):
        att_half(at).wait_recv()
        for off in range(0, BLOCK, 128):
            spot = pl.ds(aligned(at + off, 128), 128)
            mid = mid_s[spot] + rb1[spot].astype(F32)
            mid_s[spot] = mid
            xhat, _ = norm_stats(mid)
            n2_s[spot] = (xhat * ln2_gain + ln2_bias).astype(BF16)
        n2_half(at).start()

    loop(count, BLOCK, second_norm)
    pass_on("n")

    base_a = units
    parts = units // BLOCK
    steps = copies_of(len(full_bits))

    class Region:
        def __init__(self, index, row, size, cols, slot, kind, refs, to):
            own_r, oth_r, xr_r, land_r, both_r, rx_r = refs
            self.place, self.slot, self.to, self.xr = (row, size, 0, cols), slot, to, xr_r
            first, after = KINDS[kind]
            self.first = first is not None
            self.stages, self.stage, self.finished, self.sent = [], -1, False, []
            now, parts, used, trail = self.place, 8, 0, []
            sems = iter(range(index * steps, (index + 1) * steps))

            def copy(src, src_at, dst, dst_at, device):
                return described(src.at[self.window(src_at)], dst.at[self.window(dst_at)], gsem, next(sems), device)

            def piece(bits, mask):
                where = now
                for k, b in enumerate(bits):
                    where = self.cut(where, 1 - sides[b] if mask >> k & 1 else sides[b])
                return where

            sums = 1 + len(after) + len(full_bits)
            if self.first:
                keep, give, there = piece((first,), 0), piece((first,), 1), (row // 2, size // 2, 0, cols)
                place = self.landing(0, 4)
                copies = [copy(own_r, give, land_r, place, mate((first,))), copy(oth_r, give, both_r, there, mate((first,)))]
                adds = [(own_r, own_r, keep, [(land_r, place)]), (oth_r, oth_r, keep, [(both_r, there)])]
                self.stages.append((copies, adds, False))
                trail.append(((first,), keep))
                now, parts, used = keep, 4, 4
            self.stages.append(([copy(oth_r, now, xr_r, now, across)], [(own_r, own_r, now, [(xr_r, now)])], False))
            for bits in after:
                parts >>= len(bits)
                keep, copies, terms = piece(bits, 0), [], []
                for mask in range(1, 1 << len(bits)):
                    place = self.landing(used, parts)
                    used += parts
                    terms.append((land_r, place))
                    copies.append(copy(own_r, piece(bits, mask), land_r, place, mate([b for k, b in enumerate(bits) if mask >> k & 1])))
                self.stages.append((copies, [(own_r, own_r, keep, terms)], False))
                trail.append((bits, keep))
                now = keep
            for i, b in enumerate(full_bits):
                place = self.small_place()
                self.stages.append(([copy(own_r, now, rx_r[i], place, mates[b])], [(own_r, own_r, now, [(rx_r[i], place)])], True))
            copies, adds, full = self.stages[-1]
            self.stages[-1] = (copies, [(xr_r,) + adds[0][1:]], full)
            for bits, keep in reversed(trail):
                copies = []
                for mask in range(1, 1 << len(bits)):
                    copies.append(copy(xr_r, keep, xr_r, keep, mate([b for k, b in enumerate(bits) if mask >> k & 1])))
                self.stages.append((copies, [], False))

        def window(self, where):
            row, size, col, cols = where
            return pl.ds(row, size), pl.ds(col, cols)

        def cut(self, where, side):
            row, size, col, cols = where
            if (size // 2) % 16 == 0:
                return aligned(row + side * (size // 2), 16), size // 2, col, cols
            return row, size, aligned(col + side * (cols // 2), 128), cols // 2

        def landing(self, at, parts_here):
            row, rows_one, cols_one = self.slot
            full = self.place[3]
            if cols_one == full:
                return row + at * rows_one, parts_here * rows_one, 0, full
            if parts_here == 1:
                return row + at // 2 * rows_one, rows_one, at % 2 * cols_one, cols_one
            return row + at // 2 * rows_one, parts_here // 2 * rows_one, 0, full

        def small_place(self):
            row, rows_one, cols_one = self.slot
            if cols_one == self.place[3]:
                return row // 7, rows_one, 0, cols_one
            k = (self.place[0] - base_a) // quarter
            return units // 8 + k // 2 * rows_one, rows_one, k % 2 * cols_one, cols_one

        def begin(self, copies):
            for copy in copies:
                copy.start()
            self.sent += copies

        def ready(self, j):
            if self.first:
                self.stage = 0
                self.begin([self.stages[0][0][j]])
            elif j == 1:
                self.stage = 0
                self.begin(self.stages[0][0])

        def add(self, into, base, where, terms):
            row, size, col, cols = where
            step = 64 if size % 64 == 0 else 48 if size % 48 == 0 else 32

            def body(off):
                to = (pl.ds(aligned(row + off, 16), step), pl.ds(col, cols))
                parts_in = [ref[pl.ds(aligned(r + off, 16), step), pl.ds(c, cols)] for ref, (r, _, c, _) in terms]
                if len(parts_in) == 1:
                    into[to] = base[to] + parts_in[0]
                else:
                    into[to] = sum((v.astype(F32) for v in parts_in), base[to].astype(F32)).astype(BF16)

            if inside_loop:
                for off in range(0, size, step):
                    body(off)
            else:
                loop(size, step, body)

        def advance(self):
            if self.finished or self.stage < 0:
                return
            copies, adds, full = self.stages[self.stage]
            for copy in copies:
                copy.wait_recv()
            if full:
                for copy in copies:
                    copy.wait_send()
                self.sent = [c for c in self.sent if all(c is not d for d in copies)]
            for item in adds:
                self.add(*item)
            self.stage += 1
            if self.stage < len(self.stages):
                self.begin(self.stages[self.stage][0])
                return
            self.finished = True
            to_write.append(self)

    chunks = []
    refs = (own, oth, xr, land, land_both, rx)
    for i in range(parts):
        slot = (i * 7 * (BLOCK // 8), BLOCK // 8, width)
        to = g2_h.at[pl.ds(i * BLOCK, BLOCK)]
        chunks.append(Region(2 * i, i * BLOCK, BLOCK, width, slot, ORDERS[2 * i], refs, to))
        refs_one = tuple(ref.at[i] for ref in (own1, oth1, xr1, land1, land1_both)) + ([ref.at[i] for ref in rx1],)
        to = g1_h.at[:, pl.ds(i * BLOCK, BLOCK)]
        chunks.append(Region(2 * i + 1, 0, width, BLOCK, (0, width // 8, BLOCK), ORDERS[2 * i + 1], refs_one, to))
    for i in range(4):
        slot = (7 * units // 8 + i * quarter, quarter // 4, width // 2)
        to = go_h if i == 0 else gq_h.at[i - 1]
        chunks.append(Region(2 * parts + i, base_a + i * quarter, quarter, width, slot, ORDERS[2 * parts + i], refs, to))
    first_att = 2 * parts

    class Small:
        def __init__(self, tile, index, everywhere, paired, groups):
            self.tile, self.everywhere, self.paired = tile, everywhere, paired
            landings = [near.at[3 * index + k] for k in range(3)] + [far.at[(7 + len(full_bits)) * index + k] for k in range(7 + len(full_bits))]
            sems = iter(range(index * len(landings), (index + 1) * len(landings)))
            landings = iter(landings)

            def stage(devices):
                places = [next(landings) for _ in devices]
                return places, [described(tile, dst, ssem, next(sems), d) for dst, d in zip(places, devices)]

            self.stages = [stage([sib, across, facing])]
            for bits in groups + [(b,) for b in full_bits]:
                masks = range(1, 1 << len(bits))
                self.stages.append(stage([mate([b for k, b in enumerate(bits) if mask >> k & 1]) for mask in masks]))
            self.stage, self.finished = -1, False

        def start(self):
            self.stage = 0
            for copy in self.stages[0][1]:
                copy.start()

        def advance(self):
            if self.finished or self.stage < 0:
                return
            places, copies = self.stages[self.stage]
            for copy in copies:
                copy.wait()
            tile = self.tile
            if self.stage == 0:
                beside, over, facing_ = places
                n, p = self.everywhere, self.paired
                tile[0:n] = (tile[0:n] + beside[0:n]) + (over[0:n] + facing_[0:n])
                tile[n : n + p] = tile[n : n + p] + over[n + p : n + 2 * p]
            else:
                got = [tile[...]] + [place[...] for place in places]
                while len(got) > 1:
                    got = [got[k] + got[k + 1] for k in range(0, len(got), 2)]
                tile[...] = got[0]
            self.stage += 1
            if self.stage == len(self.stages):
                self.finished = True
                return
            for copy in self.stages[self.stage][1]:
                copy.start()

    first_small = Small(early, 0, 4, 1, [(b,) for b in half_bits])
    last_small = Small(late, 1, 2, 2, [tuple(half_bits)])

    def ready(i, j):
        chunks[i].ready(j)

    to_write = []

    def write_finished():
        while to_write:
            region = to_write.pop()
            region.done = local(region.xr.at[region.window(region.place)], region.to)

    def hook(name):
        pass_on(name)
        for i in PLAN.get(name, ()):
            (chunks + [last_small, first_small])[i].advance()
            if not inside_loop:
                write_finished()

    def chunk_rows(j, i, at):
        span = pl.ds(at, BLOCK)
        cols = slice(j * units + i * BLOCK, j * units + (i + 1) * BLOCK)
        mine = slice(i * BLOCK, (i + 1) * BLOCK)
        bias = (bias_u if j == 0 else uoth)[mine].reshape(1, BLOCK)
        h = dot(n2_s[span], w1_s[j, i]) + bias
        a, slope = gelu_pair(h)
        a_s[span, cols] = a.astype(BF16)
        g = (dot_nt(cot_s[span], w2_s[j, mine]) * slope).astype(BF16)
        g_s[span, cols] = g

    def chunk_grads(j, i):
        cols = slice(j * units + i * BLOCK, j * units + (i + 1) * BLOCK)
        mine = slice(i * BLOCK, (i + 1) * BLOCK)
        to = oth if j == 1 else own

        def second(at):
            to[pl.ds(i * BLOCK + at, 128)] = dot_tn(a_s[:, pl.ds(cols.start + at, 128)], cot_s[...]).astype(BF16)

        loop(BLOCK, 128, second)
        ready(2 * i, j)
        g = g_s[:, cols]

        if j == 1 and i == 0:

            def turned(at):
                n2t_s[:, pl.ds(at, BLOCK)] = n2_s[pl.ds(at, BLOCK)].T

            loop(rows, BLOCK, turned)

        def first(at):
            (oth1 if j == 1 else own1)[i, pl.ds(at, BLOCK)] = dot(n2t_s[pl.ds(at, BLOCK)], g_s[:, cols]).astype(BF16)

        loop(width, BLOCK, first)
        ready(2 * i + 1, j)
        early[4 + j : 5 + j, mine] = column_sum(g.astype(F32))
        hook(f"f{j}{i}")

    def feed(j, i, first=False):
        if first:
            loop(count, BLOCK, lambda at: chunk_rows(j, i, at))
            hook(f"r{j}{i}.0")
            cot_copy.wait_recv()

            def received(at):
                n2_half(at).wait_recv()
                chunk_rows(j, i, count + at)

            loop(count, BLOCK, received)
            hook(f"r{j}{i}.1")

        else:
            loop(rows, BLOCK, lambda at: chunk_rows(j, i, at), service(f"r{j}{i}.", hook), 2)
        chunk_grads(j, i)

    early[...] = jnp.zeros_like(early)
    late[...] = jnp.zeros_like(late)
    unit_copy.wait_recv()
    for i in range(parts):
        have_weight(4 + 2 * i, 5 + 2 * i)
        feed(1, i, first=i == 0)
        feed(0, i)

    def back_two(at):
        span = pl.ds(at, BLOCK)
        total = None
        for j in range(2):
            for i in range(parts):
                at_col = j * units + i * BLOCK
                term = dot_nt(g_s[span, at_col : at_col + BLOCK], w1_s[j, i])
                total = term if total is None else total + term
        return total

    def mlp_part(at):
        span = pl.ds(at, BLOCK)
        return dot(a_s[span, :units], w2_s[0]) + dot(a_s[span, units:], w2_s[1])

    def gn2_half(at):
        return half_copy(sb2.at[pl.ds(at, BLOCK)], rb2.at[pl.ds(at, BLOCK)], 6, at)

    def dm_half(at):
        return half_copy(n2_s.at[pl.ds(at, BLOCK)], n2_s.at[pl.ds(aligned(count + at, BLOCK), BLOCK)], 10, at)

    def back_two_sib(at):
        sb2[pl.ds(at, BLOCK)] = back_two(count + at).astype(BF16)
        gn2_half(at).start()

    def back_two_mine(at):
        gm_s[pl.ds(at, BLOCK)] = back_two(at)

    def mlp_sib(at):
        sb1[pl.ds(at, BLOCK)] = mlp_part(count + at).astype(BF16)

    loop(count, BLOCK, back_two_sib)
    hook("g0")
    loop(count, BLOCK, back_two_mine)
    hook("gn2")

    def second_back(at):
        gn2_half(at).wait_recv()
        n2_half(at).wait_send()
        for off in range(0, BLOCK, 128):
            spot = pl.ds(aligned(at + off, 128), 128)
            xhat, sigma = norm_stats(mid_s[spot])
            grad = gm_s[spot] + rb2[spot].astype(F32)
            cot = cot_s[spot].astype(F32)
            back = cot + norm_back(grad, ln2_gain, xhat, sigma)
            gm_s[spot] = back
            n2_s[spot] = back.astype(BF16)
            early[0:1] += column_sum(back)
            early[1:2] += column_sum(grad * xhat)
            early[2:3] += column_sum(grad)
            early[3:4] += column_sum(cot)
        dm_half(at).start()

    loop(count, BLOCK, second_back)
    hook("lb")
    for at in range(0, count, BLOCK):
        att_half(at).wait_send()
    loop(count, BLOCK, mlp_sib)
    mlp_copy = remote(sb1, rb1, csem, 8, sib)
    first_small.start()
    hook("ln2")

    loop(rows, 64, back_rotations)
    for at in range(0, count, BLOCK):
        dm_half(at).wait_recv()

    start = base_a + quarter
    zero = jnp.zeros((count, 128), BF16)
    grad_s = dq_s = ou_s
    n1_copy.wait_send()

    def keep_gradient(j, c):
        to = oth if j == 1 else own
        low = start + c * quarter
        dt = ot_s.at[j * quarter : (j + 1) * quarter]

        def columns(at):
            to[low : low + quarter, pl.ds(at, BLOCK)] = dot(dt[...], nr_s[:, pl.ds(at, BLOCK)]).astype(BF16)

        loop(width, BLOCK, columns)
        ready(first_att + 1 + c, j)
        if c != 1:
            d = g_s[:, (3 * j + c) * BLOCK : (3 * j + c) * BLOCK + quarter]
            late[2 + c // 2 + 2 * j : 3 + c // 2 + 2 * j, :quarter] = column_sum(d.astype(F32))

    def values_back(j):
        base = j * quarter
        to = oth if j == 1 else own

        def weight(at):
            to[base_a : base_a + quarter, pl.ds(at, BLOCK)] = dot(ou_s[base : base + quarter], n2_s[:, pl.ds(at, BLOCK)]).astype(BF16)

        loop(width, BLOCK, weight)
        ready(first_att, j)

        def output(at):
            grad_s[base : base + quarter, pl.ds(at, BLOCK)] = dot_nt(wo_s[base : base + quarter], n2_s[pl.ds(at, BLOCK)]).astype(BF16)

        loop(rows, BLOCK, output)
        hook(f"w{j}.0")
        go_s = n1_s.at[:, 256 * j : 256 * (j + 1)]

        def scale(at):
            here = pl.ds(at, BLOCK)
            grad_t = dot_nt(grad_s[base : base + quarter], roll_s[here])
            for head in range(heads):
                row = j * heads + head
                r = r_s[row : row + 1, here]
                g = grad_t[head * HEAD : (head + 1) * HEAD]
                at_head = slice(base + head * HEAD, base + (head + 1) * HEAD)
                in_s[row : row + 1, here] = column_sum(g * ot_s[at_head, here].astype(F32)) * r
                gt_s[at_head, here] = (g * r).astype(BF16)
            go_s[here, :quarter] = gt_s[base : base + quarter, here].T

        loop(rows, BLOCK, scale)

        def block(at):
            here = pl.ds(at, count)
            b = at // count
            dv = [None, None]
            for head in range(heads):
                tile = head // 2
                gh = jnp.where(lane_half(count, head % 2 == 1), go_s[here, 128 * tile : 128 * tile + 128], zero)
                part = dot(e_s[j * heads + head, b], gh)
                dv[tile] = part if dv[tile] is None else dv[tile] + part
            dv = jnp.concatenate(dv, axis=1)[:, :quarter].astype(BF16)
            g_s[here, (3 * j + 2) * BLOCK : (3 * j + 2) * BLOCK + quarter] = dv
            ot_s[base : base + quarter, here] = dv.T

        loop(rows, count, block)
        hook(f"w{j}.1")
        keep_gradient(j, 2)
        hook(f"v{j}")

    def scores_back(j):
        base = j * quarter

        def block(at):
            here = pl.ds(at, count)
            b = at // count
            dk = [None, None]
            for head in range(heads):
                tile = head // 2
                row = j * heads + head
                half = lane_half(count, head % 2 == 1)
                lanes = slice(128 * tile, 128 * tile + 128)
                vh = jnp.where(half, v_s[j, here, lanes], zero)
                qh = jnp.where(half, q_s[j, here, lanes], zero)
                last_row = min(128 * tile + 128, quarter)
                vh = vh[:, : last_row - 128 * tile]
                ds = n2t_s.at[:count, head * count : (head + 1) * count] if head < 2 else ds_s
                for off in range(0, count, BLOCK):
                    some = pl.ds(aligned(at + off, BLOCK), BLOCK)
                    dp_t = dot(vh, gt_s[base + 128 * tile : base + last_row, some])
                    grad = (dp_t - in_s[row : row + 1, some]).astype(BF16)
                    ds[:, off : off + BLOCK] = grad * e_s[row, b, :, off : off + BLOCK]
                part = dot(ds[...], qh)
                dk[tile] = part if dk[tile] is None else dk[tile] + part
                kth = kt_s[base + head * HEAD : base + head * HEAD + HEAD, here]
                dq_s[base + head * HEAD : base + head * HEAD + HEAD, here] = dot(kth, ds[...]).astype(BF16)
            dk = jnp.concatenate(dk, axis=1)[:, :quarter].astype(BF16)
            g_s[here, (3 * j + 1) * BLOCK : (3 * j + 1) * BLOCK + quarter] = dk
            ot_s[base : base + quarter, here] = dk.T
            g_s[here, 3 * j * BLOCK : 3 * j * BLOCK + quarter] = dq_s[base : base + quarter, here].T

        loop(rows, count, block, service(f"b{j}.", hook))
        keep_gradient(j, 1)
        hook(f"k{j}")
        ot_s[base : base + quarter] = dq_s[base : base + quarter]
        keep_gradient(j, 0)
        hook(f"s{j}")

    values_back(1)
    scores_back(1)
    values_back(0)
    scores_back(0)

    def finish_out(at):
        span = pl.ds(at, BLOCK)
        mid_s[span] = mid_s[span] + mlp_part(at) + fc2_bias

    loop(count, BLOCK, finish_out)
    hook("fo")
    mlp_copy.wait_recv()

    def write_out(at):
        spot = pl.ds(at, 128)
        tok_s[spot] = (mid_s[spot] + rb1[spot].astype(F32)).astype(BF16)

    loop(count, 128, write_out)
    put_out = local(tok_s, out_h)
    hook("fin")

    def back_one(at):
        total = None
        for j in range(2):
            for c in range(3):
                d = g_s[pl.ds(at, BLOCK), (3 * j + c) * BLOCK : (3 * j + c) * BLOCK + quarter]
                term = dot(d, wq_s[j, c])
                total = term if total is None else total + term
        n2_s[pl.ds(at, BLOCK)] = total.astype(BF16)

    for at in range(0, count, BLOCK):
        dm_half(at).wait_send()
    loop(rows, BLOCK, back_one, service("d.", hook), 2)
    for at in range(0, count, BLOCK):
        gn2_half(at).wait_send()

    def gn1_half(at):
        return half_copy(sb2.at[pl.ds(at, BLOCK)], rb2.at[pl.ds(at, BLOCK)], 12, at)

    def back_one_sib(at):
        sb2[pl.ds(at, BLOCK)] = dot(back_s[pl.ds(count + at, BLOCK)], n2_s[...]).astype(BF16)
        gn1_half(at).start()

    def back_one_mine(at):
        mid_s[pl.ds(at, BLOCK)] = dot(back_s[pl.ds(at, BLOCK)], n2_s[...])

    loop(count, BLOCK, back_one_sib)
    loop(count, BLOCK, back_one_mine)
    hook("e.0")
    mlp_copy.wait_send()

    def first_back(at):
        gn1_half(at).wait_recv()
        for off in range(0, BLOCK, 128):
            spot = pl.ds(aligned(at + off, 128), 128)
            xhat, sigma = norm_stats(sin_s[spot])
            grad = mid_s[spot] + rb2[spot].astype(F32)
            sb1[spot] = (gm_s[spot] + norm_back(grad, ln1_gain, xhat, sigma)).astype(BF16)
            late[0:1] += column_sum(grad * xhat)
            late[1:2] += column_sum(grad)

    loop(count, BLOCK, first_back)
    put_in = local(sb1, ing_h)
    last_small.start()
    hook("e.1")
    hook("tail")
    left = [first_small, last_small] + chunks
    while left:
        for item in left:
            item.advance()
            write_finished()
        left = [item for item in left if not item.finished]

    for row, source, at in ((0, late, 0), (1, late, 1), (2, early, 0), (3, early, 1), (4, early, 2), (5, early, 3), (8, early, 4), (9, late, 2), (10, late, 3)):
        small_o[row : row + 1] = source[at : at + 1]

    passed = [copy for item in pieces for copy in item.copies]
    for copy in [unit_copy, head_copy, cot_copy] + [gn1_half(at) for at in range(0, count, BLOCK)] + passed:
        copy.wait_send()
    for chunk in chunks:
        for copy in chunk.sent:
            copy.wait_send()
        chunk.done.wait()
    put_out.wait()
    put_in.wait()


def copies_of(full):
    most = 0
    for kind in ORDERS:
        first, after = KINDS[kind]
        most = max(most, 1 + full + 2 * sum((1 << len(bits)) - 1 for bits in after) + (0 if first is None else 3))
    return most


def call_layer(dp_size, tokens, cotangent, ids, vectors, wq, wo, w1, w2):
    count, width = tokens.shape
    rows = 2 * count
    quarter = wo.shape[0]
    units = w1.shape[1]
    heads = quarter // HEAD
    grad_rows = units + 4 * quarter
    parts = units // BLOCK
    bits = [b for b in range(20) if (1 << b) < dp_size]
    half_bits = bits[:3]
    shape = jax.ShapeDtypeStruct
    vm = pltpu.VMEM
    regions = 2 * (units // BLOCK) + 4
    steps = copies_of(len(bits) - len(half_bits))
    fetched = 4 + 2 * (units // BLOCK)
    scratch = (
        [vm((count, width), BF16), vm((rows, width), BF16)]
        + [vm((count, width), F32)] * 3
        + [vm((rows, width), BF16)] * 2
        + [vm((width, rows), BF16)]
        + [vm((2,) + wq.shape, BF16), vm((2 * quarter, width), BF16), vm((2, units // BLOCK, width, BLOCK), BF16), vm((2,) + w2.shape, BF16)]
        + [vm((2, rows, 256), BF16)] * 2
        + [vm((2 * quarter, rows), BF16)] * 4
        + [vm((8, rows), F32)] * 2
        + [vm((2 * heads, 2, count, count), BF16)]
        + [vm((rows, rows), BF16)] * 2
        + [vm((rows, width), BF16), vm((count, count), BF16)]
        + [vm((rows, 2 * units), BF16)] * 2
        + [vm((count, width), BF16)] * 4
        + [vm((grad_rows, width), BF16)] * 3
        + [vm((7 * units // 8 + 4 * quarter, width), BF16), vm((units // 2, width), BF16)]
        + [vm((parts, width, BLOCK), BF16)] * 3
        + [vm((parts, 7 * width // 8, BLOCK), BF16), vm((parts, width // 2, BLOCK), BF16)]
        + [vm((grad_rows >> len(half_bits), width), BF16)] * (len(bits) - len(half_bits))
        + [vm((parts, width // 8, BLOCK), BF16)] * (len(bits) - len(half_bits))
        + [vm((SIDE, width // 3), F32), vm((units,), F32), vm((2, quarter), F32), vm((8, width), F32), vm((8, width), F32)]
        + [vm((6, 8, width), F32), vm((14 + 2 * (len(bits) - 3), 8, width), F32)]
        + [pltpu.SemaphoreType.DMA((8 + units // BLOCK + regions,))]
        + [pltpu.SemaphoreType.DMA((2, n)) for n in (3 * fetched + 2, 14, regions * steps, 2 * (10 + len(bits) - 3))]
    )
    anywhere = pl.BlockSpec(memory_space=pl.ANY)
    inside = pl.BlockSpec(memory_space=pltpu.VMEM)
    return pl.pallas_call(
        functools.partial(layer, dp_size, half_bits),
        out_shape=[shape((count, width), BF16)] * 2
        + [shape(w2.shape, BF16), shape(w1.shape, BF16), shape(wo.shape, BF16), shape(wq.shape, BF16), shape((16, width), F32)],
        in_specs=[anywhere] * 2 + [inside] * (1 + len(vectors)) + [anywhere] * 4,
        out_specs=[anywhere] * 6 + [inside],
        scratch_shapes=scratch,
        compiler_params=pltpu.CompilerParams(vmem_limit_bytes=VMEM_LIMIT, collective_id=0, has_side_effects=True),
        name="layer",
    )(tokens, cotangent, ids, *vectors, wq, wo, w1, w2)


def finish(*refs):
    sources, small, rest = refs[:6], refs[6], refs[7:]
    results, vectors, rest = rest[:6], rest[6:14], rest[14:]
    narrow, wide, (get, put) = rest[:6], rest[6:10], rest[10:]
    blocks = []
    for k, src in enumerate(sources):
        if src.ndim == 3:
            places = list(range(src.shape[0]))
        else:
            step = min(BLOCK, src.shape[0])
            places = [pl.ds(at, step) for at in range(0, src.shape[0], step)]
        for at in places:
            low = narrow[k].at[at]
            blocks.append((src.at[at], low, low if k < 2 else wide[k - 2].at[at], results[k].at[at]))
    reads = [pltpu.make_async_copy(src, low, get.at[n]) for n, (src, low, _, _) in enumerate(blocks)]
    writes = [pltpu.make_async_copy(high, dst, put.at[n]) for n, (_, _, high, dst) in enumerate(blocks)]
    for copy in reads:
        copy.start()
    for i in range(6):
        vectors[i][...] = small[i]
    vectors[6][...] = small[8, : vectors[6].shape[0]]
    vectors[7][...] = small[9:11, : vectors[7].shape[1]]
    for read, write, (_, low, high, _) in zip(reads, writes, blocks):
        read.wait()
        if high is not low:

            def cast(at, low=low, high=high):
                high[pl.ds(at, 64)] = low[pl.ds(at, 64)].astype(F32)

            loop(low.shape[0], 64, cast)
        write.start()
    for copy in writes:
        copy.wait()


def call_finish(arrays, small, units, quarter):
    width = small.shape[1]
    shape = jax.ShapeDtypeStruct
    extents = [(width,)] * 6 + [(units,), (2, quarter)]
    kinds = [BF16, BF16, F32, F32, F32, F32]
    anywhere = pl.BlockSpec(memory_space=pl.ANY)
    inside = pl.BlockSpec(memory_space=pltpu.VMEM)
    grads = arrays[2:]
    return pl.pallas_call(
        finish,
        in_specs=[anywhere] * len(arrays) + [inside],
        out_specs=[anywhere] * len(arrays) + [inside] * len(extents),
        out_shape=[shape(a.shape, k) for a, k in zip(arrays, kinds)] + [shape(e, F32) for e in extents],
        scratch_shapes=[pltpu.VMEM(a.shape, BF16) for a in arrays]
        + [pltpu.VMEM(a.shape, F32) for a in grads]
        + [pltpu.SemaphoreType.DMA((16,)), pltpu.SemaphoreType.DMA((16,))],
        compiler_params=pltpu.CompilerParams(vmem_limit_bytes=VMEM_LIMIT),
        name="finish",
    )(*arrays, small)


def per_device(
    tokens, segment_ids, ln1_gain, ln1_bias, qkv_weight, qv_bias, out_weight, out_bias,
    ln2_gain, ln2_bias, fc1_weight, fc1_bias, fc2_weight, fc2_bias, cotangent,
):
    vectors = (ln1_gain, ln1_bias, out_bias, ln2_gain, ln2_bias, fc2_bias, fc1_bias, qv_bias)
    *arrays, small = call_layer(
        lax.axis_size("dp"), tokens, cotangent, segment_ids, vectors, qkv_weight.transpose(0, 2, 1), out_weight, fc1_weight, fc2_weight
    )
    out, ing, g2, g1, go, gq, a0, a1, a2, a3, a4, a5, g_units, g_heads = call_finish(arrays, small, fc1_weight.shape[1], out_weight.shape[0])
    return (out, ing, a0, a1, gq.transpose(0, 2, 1), g_heads, go, a2, a3, a4, g1, g_units, g2, a5)


def solution(mesh):
    placed = (
        P(("dp", "tensor"), None),
        P("dp", None),
        P(),
        P(),
        P(None, None, "tensor"),
        P(None, "tensor"),
        P("tensor", None),
        P(),
        P(),
        P(),
        P(None, "tensor"),
        P("tensor"),
        P("tensor", None),
        P(),
        P(("dp", "tensor"), None),
    )
    return jax.shard_map(
        per_device,
        mesh=mesh,
        in_specs=placed,
        out_specs=(
            P(("dp", "tensor"), None),
            P(("dp", "tensor"), None),
            P(),
            P(),
            P(None, None, "tensor"),
            P(None, "tensor"),
            P("tensor", None),
            P(),
            P(),
            P(),
            P(None, "tensor"),
            P("tensor"),
            P("tensor", None),
            P(),
        ),
        check_vma=False,
    )
```

```python
import functools
import math

import jax
import jax.numpy as jnp
from jax import lax
from jax.experimental import pallas as pl
from jax.experimental.pallas import tpu as pltpu
from jax.sharding import PartitionSpec as P

HEAD = 64
SIDE = 16
EPSILON = 1e-06
NEG_LARGE = -1e30
SCALE = HEAD ** (-0.5)
F32 = jnp.float32
BF16 = jnp.bfloat16
VMEM_LIMIT = 64 * 1024 * 1024 - 128 * 1024
MESH = pl.DeviceIdType.MESH
BLOCK = 256
KINDS = {
    "A": (None, ((0,), (1,), (2,))),
    "B": (None, ((1,), (0,), (2,))),
    "D": (None, ((0,), (1, 2))),
    "E": (None, ((0, 1, 2),)),
    "C": (None, ((0, 1), (2,))),
    "Y": (0, ((1,), (2,))),
    "Z": (1, ((0,), (2,))),
    "YD": (0, ((1, 2),)),
    "S": (None, (("p",), ("q",), (2,))),
    "SD": (None, (("p",), ("q", 2))),
    "SF": ("p", (("q",), (2,))),
    "SFD": ("p", (("q", 2),)),
}
ORDERS = ("D", "SFD", "SFD", "Z", "A", "YD", "D", "D", "C", "B")
WEIGHT_PLAN = {"p0": (0,), "a0": (1,), "a2": (2,), "p1": (3,), "c0": (4,), "c3": (5,), "n": (6,), "r10.1": (7,), "r00.1": (8,), "r11.1": (9,)}
PLAN = {
    "f01": (1,),
    "r12.1": (0,),
    "r02.0": (2,),
    "r02.1": (1,),
    "g0": (0,),
    "lb": (3, 4, 1),
    "w1.0": (2, 0),
    "w1.1": (-1, 5),
    "v1": (3,),
    "b1.0": (4, 1),
    "b1.1": (-1, 2, 3),
    "k1": (0,),
    "s1": (4, 5),
    "w0.0": (6, 1, -1),
    "v0": (2, 9),
    "b0.0": (0, 3, 4, 6),
    "b0.1": (2, 5),
    "k0": (8, -1, 9),
    "s0": (3,),
    "fo": (7, 4),
    "d.0": (6,),
    "d.1": (9,),
    "e.0": (5, 8, 3),
    "e.1": (4, 7),
    "tail": (6, 9, 8, -2, 5, 3, 4, 7, 9, 8, 6, -2, 9, 7, 8, 9, 7),
}


def dot(a, b):
    return jnp.dot(a, b, preferred_element_type=F32)


def dot_nt(a, b):
    return lax.dot_general(a, b, (((1,), (1,)), ((), ())), preferred_element_type=F32)


def dot_tn(a, b):
    return lax.dot_general(a, b, (((0,), (0,)), ((), ())), preferred_element_type=F32)


def lane_half(rows, upper):
    lanes = lax.broadcasted_iota(jnp.int32, (rows, 128), 1)
    return lanes >= HEAD if upper else lanes < HEAD


def head_lanes(ref, head, filler):
    tile = ref[:, 128 * (head // 2) : 128 * (head // 2) + 128]
    return jnp.where(lane_half(tile.shape[0], head % 2 == 1), tile, filler)


def gelu_pair(h):
    cdf = 0.5 + 0.5 * lax.erf(h * 0.7071067811865476)
    return h * cdf, cdf + h * jnp.exp(-0.5 * h * h) * 0.3989422804014327


def norm_stats(v):
    centred = v - jnp.mean(v, axis=-1, keepdims=True)
    sigma = lax.rsqrt(jnp.mean(centred * centred, axis=-1, keepdims=True) + EPSILON)
    return centred * sigma, sigma


def norm_back(grad, gain, xhat, sigma):
    g = grad * gain
    return sigma * (g - jnp.mean(g, axis=-1, keepdims=True) - xhat * jnp.mean(g * xhat, axis=-1, keepdims=True))


def column_sum(v):
    return jnp.sum(v, axis=0, keepdims=True)


def aligned(v, unit):
    return v if isinstance(v, int) else pl.multiple_of(v, unit)


def loop(count, step, body, service=None, every=1):
    def run(i, carry):
        body(aligned(i * step, step))
        if service is not None:
            for k in range(count // step // every):
                if service(k, True):
                    pl.when(i == every * (k + 1) - 1)(functools.partial(service, k, False))
        return carry

    lax.fori_loop(0, count // step, run, 0)


def layer(
    dp_size, half_bits,
    tok_h, cot_h, ids, gain1, bias1, bias_o, gain2, bias2, bias_f, bias_u, bias_qv, wq_h, wo_h, w1_h, w2_h,
    out_h, ing_h, g2_h, g1_h, go_h, gq_h, small_o,
    tok_s, cot_s, sin_s, mid_s, gm_s, n1_s, n2_s, n2t_s, wq_s, wo_s, w1_s, w2_s,
    q_s, v_s, kt_s, ot_s, ou_s, gt_s, r_s, in_s, e_s, roll_s, back_s, nr_s, ds_s, a_s, g_s, sb1, sb2, rb1, rb2,
    own, oth, xr, land, land_both, own1, oth1, xr1, land1, land1_both, *rest,
):
    rest = list(rest)
    full_bits = [b for b in range(20) if (1 << b) < dp_size and b not in half_bits]
    rx = [rest.pop(0) for _ in full_bits]
    rx1 = [rest.pop(0) for _ in full_bits]
    table, uoth, voth, early, late, near, far, lsem, wsem, csem, gsem, ssem = rest

    count, width = tok_s.shape
    rows = 2 * count
    quarter = wo_h.shape[0]
    units = w1_h.shape[1]
    heads = quarter // HEAD
    place = lax.axis_index("tensor")
    dp = lax.axis_index("dp")
    chip = place // 2
    core = place % 2
    sib = {"tensor": chip * 2 + 1 - core}
    across = {"tensor": (1 - chip) * 2 + core}
    facing = {"tensor": (1 - chip) * 2 + 1 - core}
    all_bits = list(half_bits) + full_bits
    sides = {b: (dp // (1 << b)) % 2 for b in all_bits}

    ways = {b: (1 - 2 * sides[b]) * (1 << b) for b in all_bits}
    sides["p"] = sides[0] + (sides[1] - sides[0]) * core
    sides["q"] = sides[1] + (sides[0] - sides[1]) * core
    ways["p"] = ways[0] + (ways[1] - ways[0]) * core
    ways["q"] = ways[1] + (ways[0] - ways[1]) * core

    def mate(bits):
        return {"dp": dp + sum(ways[b] for b in bits)}

    def described(src, dst, sems, index, device):
        return pltpu.make_async_remote_copy(
            src_ref=src, dst_ref=dst, send_sem=sems.at[0, index], recv_sem=sems.at[1, index], device_id=device, device_id_type=MESH
        )

    mates = {b: mate((b,)) for b in all_bits}
    groups = {(b,) for b in full_bits}
    for mask in range(1, 1 << len(half_bits)):
        groups.add(tuple(b for k, b in enumerate(half_bits) if mask >> k & 1))

    barrier = pltpu.get_barrier_semaphore()
    partners = [sib, across, facing] + [mate(bits) for bits in sorted(groups)]
    for partner in partners:
        pl.semaphore_signal(barrier, inc=1, device_id=partner, device_id_type=MESH)

    sq_s, sk_s, k_s = a_s.at[:, 0:128], a_s.at[:, 128:256], a_s.at[:, 256:512]
    local_used = [0]

    def local(src, dst):
        copy = pltpu.make_async_copy(src, dst, lsem.at[local_used[0]])
        local_used[0] += 1
        copy.start()
        return copy

    def remote(src, dst, sems, index, device):
        copy = pltpu.make_async_remote_copy(
            src_ref=src, dst_ref=dst, send_sem=sems.at[0, index], recv_sem=sems.at[1, index], device_id=device, device_id_type=MESH
        )
        copy.start()
        return copy

    def half_copy(src, dst, first, at):
        return pltpu.make_async_remote_copy(
            src_ref=src,
            dst_ref=dst,
            send_sem=csem.at[0, first + at // BLOCK],
            recv_sem=csem.at[1, first + at // BLOCK],
            device_id=sib,
            device_id_type=MESH,
        )

    get_tok = local(tok_h, tok_s)
    get_wq = local(wq_h, wq_s.at[0])
    get_cot = local(cot_h, cot_s.at[pl.ds(0, count)])
    get_wo = local(wo_h, wo_s.at[pl.ds(0, quarter)])
    get_w1 = [local(w1_h.at[:, pl.ds(i * BLOCK, BLOCK)], w1_s.at[0, i]) for i in range(units // BLOCK)]
    get_w2 = local(w2_h, w2_s.at[0])

    part = (sides[0] + sides[1]) % 2

    class Piece:
        def __init__(self, index, refs, at, extent):
            size = extent // 4

            def some(k, first, size):
                return refs[k].at[pl.ds(aligned(at[k] + part * (extent // 2) + first, 16), size)]

            self.copies = [described(some(0, 0, 2 * size), some(1, 0, 2 * size), wsem, 3 * index, across)]
            for k in range(2):
                block = some(1, k * size, size)
                self.copies.append(described(block, block, wsem, 3 * index + 1 + k, mates[k]))
            self.stage = 0

        def advance(self):
            if self.stage == 0:
                self.copies[0].wait_recv()
                self.copies[1].start()
                self.copies[2].start()
            else:
                self.copies[1].wait_recv()
                self.copies[2].wait_recv()
            self.stage += 1

    pieces = [Piece(c, (wq_h.at[c], wq_s.at[1, c]), (0, 0), quarter) for c in range(3)]
    pieces.append(Piece(3, (wo_h, wo_s), (0, quarter), quarter))
    for i in range(units // BLOCK):
        pieces.append(Piece(4 + 2 * i, (w1_s.at[0, i], w1_s.at[1, i]), (0, 0), width))
        pieces.append(Piece(5 + 2 * i, (w2_s.at[0], w2_s.at[1]), (i * BLOCK, i * BLOCK), BLOCK))
    pl.semaphore_wait(barrier, len(partners))
    unit_copy = remote(bias_u, uoth, wsem, 3 * len(pieces), across)
    head_copy = remote(bias_qv, voth, wsem, 3 * len(pieces) + 1, across)
    for item in pieces[:4]:
        item.copies[0].start()

    inside_loop = []

    def service(name, act):
        def at_point(k, ask):
            full = f"{name}{k}"
            if ask:
                return full in PLAN or full in WEIGHT_PLAN
            inside_loop.append(full)
            act(full)
            inside_loop.pop()

        return at_point

    def pass_on(name):
        for i in WEIGHT_PLAN.get(name, ()):
            if pieces[i].stage < 1:
                pieces[i].advance()

    def have_weight(*which):
        for i in which:
            while pieces[i].stage < 2:
                pieces[i].advance()

    ln1_gain, ln1_bias, out_bias, ln2_gain, ln2_bias, fc2_bias = (
        ref[...].reshape(1, width) for ref in (gain1, bias1, bias_o, gain2, bias2, bias_f)
    )
    third = width // 6
    place_k = lax.broadcasted_iota(jnp.int32, (SIDE, third), 1).astype(F32)
    angles = lax.broadcasted_iota(jnp.int32, (SIDE, third), 0).astype(F32) * jnp.exp(place_k * (-math.log(10000.0) / third))
    table[:, :third] = jnp.sin(angles)
    table[:, third:] = jnp.cos(angles)
    get_tok.wait()

    def first_norm(at):
        plane = core * (count // (SIDE * SIDE)) + at // (SIDE * SIDE)
        line = (at // SIDE) % SIDE
        shape = (SIDE, width // 3)
        for k in range(4):
            spot = jnp.concatenate(
                [jnp.broadcast_to(table[pl.ds(plane, 1)], shape), jnp.broadcast_to(table[pl.ds(line + k, 1)], shape), table[...]], axis=1
            )
            span = pl.ds(aligned(at + k * SIDE, SIDE), SIDE)
            stream = tok_s[span].astype(F32) + spot
            sin_s[span] = stream
            xhat, _ = norm_stats(stream)
            n1_s[span] = (xhat * ln1_gain + ln1_bias).astype(BF16)

    loop(count, 4 * SIDE, first_norm)
    doc = ids[pl.ds(chip, 1), :]
    starts = [jnp.zeros((1, 1), F32)]
    starts += [jnp.sum(jnp.where(doc < v, 1.0, 0.0), axis=1, keepdims=True) for v in range(1, 4)]
    starts.append(jnp.full((1, 1), rows, F32))
    turn = jnp.zeros((1, 1), F32)
    for v in range(4):
        turn += jnp.where(starts[v + 1] - starts[v] == count, starts[v], 0.0)
    turn_here = turn - (core * count).astype(F32)

    def wrapped(v):
        v = jnp.where(v >= rows, v - rows, v)
        return jnp.where(v < 0, v + rows, v)

    def rotations(at):
        down = (lax.broadcasted_iota(jnp.int32, (64, rows), 0) + at).astype(F32)
        along = lax.broadcasted_iota(jnp.int32, (64, rows), 1).astype(F32)
        roll_s[pl.ds(at, 64)] = jnp.where(wrapped(down + turn_here) == along, 1.0, 0.0).astype(BF16)
        back_s[pl.ds(at, 64)] = jnp.where(wrapped(down - turn_here) == along, 1.0, 0.0).astype(BF16)
        where = wrapped((lax.broadcasted_iota(jnp.int32, (64, 128), 0) + at).astype(F32) + turn)
        mine = sum(jnp.where(where >= starts[v], 1.0, 0.0) for v in range(1, 4))
        slot = (lax.broadcasted_iota(jnp.int32, (64, 128), 1) % HEAD).astype(F32)
        sq_s[pl.ds(at, 64)] = jnp.where((slot < 4) & (slot != mine), 1.0, 0.0).astype(BF16)
        sk_s[pl.ds(at, 64)] = jnp.where(slot == mine, NEG_LARGE, 0.0).astype(BF16)


    get_wq.wait()
    get_wo.wait()
    for copy in get_w1:
        copy.wait()
    get_w2.wait()
    for item in pieces[4:]:
        item.copies[0].start()
    n1_copy = remote(n1_s.at[pl.ds(0, count)], n1_s.at[pl.ds(count, count)], csem, 0, sib)
    get_cot.wait()
    cot_copy = remote(cot_s.at[pl.ds(0, count)], cot_s.at[pl.ds(count, count)], csem, 1, sib)

    def rotate(at):
        nr_s[pl.ds(at, BLOCK)] = dot(roll_s[pl.ds(at, BLOCK)], n1_s[...]).astype(BF16)

    def project(j, at):
        n = nr_s[pl.ds(at, BLOCK)]
        biases = bias_qv if j == 0 else voth
        q = (dot_nt(n, wq_s[j, 0]) + biases[0:1]).astype(BF16) * SCALE
        k = dot_nt(n, wq_s[j, 1]).astype(BF16)
        v = (dot_nt(n, wq_s[j, 2]) + biases[1:2]).astype(BF16)
        q_s[j, pl.ds(at, BLOCK), :quarter] = q
        k_s[pl.ds(at, BLOCK), :quarter] = k
        v_s[j, pl.ds(at, BLOCK), :quarter] = v
        kt_s[j * quarter : (j + 1) * quarter, pl.ds(at, BLOCK)] = k.T * SCALE

    blocks = [(b, at) for b in range(2) for at in range(0, count, BLOCK)]

    def attend(j):
        for head in range(heads):
            at = 512 + 256 * head
            a_s[:, at : at + 128] = head_lanes(q_s.at[j], head, sq_s[...])
            a_s[:, at + 128 : at + 256] = head_lanes(k_s, head, sk_s[...])
        for at in range(0, rows, BLOCK):
            ou_s[:quarter, at : at + BLOCK] = v_s[j, at : at + BLOCK, :quarter].T

        def tile(here):
            b = here // count
            at = aligned(here % count, BLOCK)
            keys = pl.ds(aligned(b * count, count), count)
            for head in range(heads):
                column = 512 + 256 * head
                s = dot_nt(a_s[keys, column + 128 : column + 256], a_s[pl.ds(here, BLOCK), column : column + 128])
                m = jnp.max(s, axis=0, keepdims=True)
                e = jnp.exp(s - m)
                r = 1.0 / column_sum(e)
                low = e.astype(BF16)
                span = slice(head * HEAD, head * HEAD + HEAD)
                to = slice(j * quarter + head * HEAD, j * quarter + head * HEAD + HEAD)
                e_s[j * heads + head, b, :, pl.ds(at, BLOCK)] = low
                ot_s[to, pl.ds(here, BLOCK)] = (dot(ou_s[span, keys], low) * r).astype(BF16)
                r_s[j * heads + head : j * heads + head + 1, pl.ds(here, BLOCK)] = r

        return tile

    loop(rows, 64, rotations)
    n1_copy.wait_recv()
    loop(rows, BLOCK, rotate)
    loop(rows, BLOCK, lambda at: project(0, at))
    pass_on("p0")
    loop(rows, BLOCK, attend(0), service("a", pass_on))
    head_copy.wait_recv()
    have_weight(0, 1, 2)
    loop(rows, BLOCK, lambda at: project(1, at))
    pass_on("p1")
    loop(rows, BLOCK, attend(1), service("c", pass_on))

    have_weight(3)

    def unrotate(at):
        ou_s[:, pl.ds(at, BLOCK)] = dot(ot_s[...], roll_s[:, pl.ds(at, BLOCK)]).astype(BF16)

    loop(rows, BLOCK, unrotate)
    pass_on("u")

    def out_part(at):
        return dot_tn(ou_s[:, pl.ds(at, BLOCK)], wo_s[...])

    def att_half(at):
        return half_copy(sb1.at[pl.ds(at, BLOCK)], rb1.at[pl.ds(at, BLOCK)], 2, at)

    def n2_half(at):
        return half_copy(n2_s.at[pl.ds(at, BLOCK)], n2_s.at[pl.ds(aligned(count + at, BLOCK), BLOCK)], 4, at)

    def out_sib(at):
        sb1[pl.ds(at, BLOCK)] = out_part(count + at).astype(BF16)
        att_half(at).start()

    loop(count, BLOCK, out_sib)

    def out_mine(at):
        mid_s[pl.ds(at, BLOCK)] = sin_s[pl.ds(at, BLOCK)] + out_part(at) + out_bias

    loop(count, BLOCK, out_mine)
    pass_on("o")

    def second_norm(at):
        att_half(at).wait_recv()
        for off in range(0, BLOCK, 128):
            spot = pl.ds(aligned(at + off, 128), 128)
            mid = mid_s[spot] + rb1[spot].astype(F32)
            mid_s[spot] = mid
            xhat, _ = norm_stats(mid)
            n2_s[spot] = (xhat * ln2_gain + ln2_bias).astype(BF16)
        n2_half(at).start()

    loop(count, BLOCK, second_norm)
    pass_on("n")

    base_a = units
    parts = units // BLOCK
    steps = copies_of(len(full_bits))

    class Region:
        def __init__(self, index, row, size, cols, slot, kind, refs, to):
            own_r, oth_r, xr_r, land_r, both_r, rx_r = refs
            self.place, self.slot, self.to, self.xr = (row, size, 0, cols), slot, to, xr_r
            first, after = KINDS[kind]
            self.first = first is not None
            self.stages, self.stage, self.finished, self.sent = [], -1, False, []
            now, parts, used, trail = self.place, 8, 0, []
            sems = iter(range(index * steps, (index + 1) * steps))

            def copy(src, src_at, dst, dst_at, device):
                return described(src.at[self.window(src_at)], dst.at[self.window(dst_at)], gsem, next(sems), device)

            def piece(bits, mask):
                where = now
                for k, b in enumerate(bits):
                    where = self.cut(where, 1 - sides[b] if mask >> k & 1 else sides[b])
                return where

            sums = 1 + len(after) + len(full_bits)
            if self.first:
                keep, give, there = piece((first,), 0), piece((first,), 1), (row // 2, size // 2, 0, cols)
                place = self.landing(0, 4)
                copies = [copy(own_r, give, land_r, place, mate((first,))), copy(oth_r, give, both_r, there, mate((first,)))]
                adds = [(own_r, own_r, keep, [(land_r, place)]), (oth_r, oth_r, keep, [(both_r, there)])]
                self.stages.append((copies, adds, False))
                trail.append(((first,), keep))
                now, parts, used = keep, 4, 4
            self.stages.append(([copy(oth_r, now, xr_r, now, across)], [(own_r, own_r, now, [(xr_r, now)])], False))
            for bits in after:
                parts >>= len(bits)
                keep, copies, terms = piece(bits, 0), [], []
                for mask in range(1, 1 << len(bits)):
                    place = self.landing(used, parts)
                    used += parts
                    terms.append((land_r, place))
                    copies.append(copy(own_r, piece(bits, mask), land_r, place, mate([b for k, b in enumerate(bits) if mask >> k & 1])))
                self.stages.append((copies, [(own_r, own_r, keep, terms)], False))
                trail.append((bits, keep))
                now = keep
            for i, b in enumerate(full_bits):
                place = self.small_place()
                self.stages.append(([copy(own_r, now, rx_r[i], place, mates[b])], [(own_r, own_r, now, [(rx_r[i], place)])], True))
            copies, adds, full = self.stages[-1]
            self.stages[-1] = (copies, [(xr_r,) + adds[0][1:]], full)
            for bits, keep in reversed(trail):
                copies = []
                for mask in range(1, 1 << len(bits)):
                    copies.append(copy(xr_r, keep, xr_r, keep, mate([b for k, b in enumerate(bits) if mask >> k & 1])))
                self.stages.append((copies, [], False))

        def window(self, where):
            row, size, col, cols = where
            return pl.ds(row, size), pl.ds(col, cols)

        def cut(self, where, side):
            row, size, col, cols = where
            if (size // 2) % 16 == 0:
                return aligned(row + side * (size // 2), 16), size // 2, col, cols
            return row, size, aligned(col + side * (cols // 2), 128), cols // 2

        def landing(self, at, parts_here):
            row, rows_one, cols_one = self.slot
            full = self.place[3]
            if cols_one == full:
                return row + at * rows_one, parts_here * rows_one, 0, full
            if parts_here == 1:
                return row + at // 2 * rows_one, rows_one, at % 2 * cols_one, cols_one
            return row + at // 2 * rows_one, parts_here // 2 * rows_one, 0, full

        def small_place(self):
            row, rows_one, cols_one = self.slot
            if cols_one == self.place[3]:
                return row // 7, rows_one, 0, cols_one
            k = (self.place[0] - base_a) // quarter
            return units // 8 + k // 2 * rows_one, rows_one, k % 2 * cols_one, cols_one

        def begin(self, copies):
            for copy in copies:
                copy.start()
            self.sent += copies

        def ready(self, j):
            if self.first:
                self.stage = 0
                self.begin([self.stages[0][0][j]])
            elif j == 1:
                self.stage = 0
                self.begin(self.stages[0][0])

        def add(self, into, base, where, terms):
            row, size, col, cols = where
            step = 64 if size % 64 == 0 else 48 if size % 48 == 0 else 32

            def body(off):
                to = (pl.ds(aligned(row + off, 16), step), pl.ds(col, cols))
                parts_in = [ref[pl.ds(aligned(r + off, 16), step), pl.ds(c, cols)] for ref, (r, _, c, _) in terms]
                if len(parts_in) == 1:
                    into[to] = base[to] + parts_in[0]
                else:
                    into[to] = sum((v.astype(F32) for v in parts_in), base[to].astype(F32)).astype(BF16)

            if inside_loop:
                for off in range(0, size, step):
                    body(off)
            else:
                loop(size, step, body)

        def advance(self):
            if self.finished or self.stage < 0:
                return
            copies, adds, full = self.stages[self.stage]
            for copy in copies:
                copy.wait_recv()
            if full:
                for copy in copies:
                    copy.wait_send()
                self.sent = [c for c in self.sent if all(c is not d for d in copies)]
            for item in adds:
                self.add(*item)
            self.stage += 1
            if self.stage < len(self.stages):
                self.begin(self.stages[self.stage][0])
                return
            self.finished = True
            to_write.append(self)

    chunks = []
    refs = (own, oth, xr, land, land_both, rx)
    for i in range(parts):
        slot = (i * 7 * (BLOCK // 8), BLOCK // 8, width)
        to = g2_h.at[pl.ds(i * BLOCK, BLOCK)]
        chunks.append(Region(2 * i, i * BLOCK, BLOCK, width, slot, ORDERS[2 * i], refs, to))
        refs_one = tuple(ref.at[i] for ref in (own1, oth1, xr1, land1, land1_both)) + ([ref.at[i] for ref in rx1],)
        to = g1_h.at[:, pl.ds(i * BLOCK, BLOCK)]
        chunks.append(Region(2 * i + 1, 0, width, BLOCK, (0, width // 8, BLOCK), ORDERS[2 * i + 1], refs_one, to))
    for i in range(4):
        slot = (7 * units // 8 + i * quarter, quarter // 4, width // 2)
        to = go_h if i == 0 else gq_h.at[i - 1]
        chunks.append(Region(2 * parts + i, base_a + i * quarter, quarter, width, slot, ORDERS[2 * parts + i], refs, to))
    first_att = 2 * parts

    class Small:
        def __init__(self, tile, index, everywhere, paired, groups):
            self.tile, self.everywhere, self.paired = tile, everywhere, paired
            landings = [near.at[3 * index + k] for k in range(3)] + [far.at[(7 + len(full_bits)) * index + k] for k in range(7 + len(full_bits))]
            sems = iter(range(index * len(landings), (index + 1) * len(landings)))
            landings = iter(landings)

            def stage(devices):
                places = [next(landings) for _ in devices]
                return places, [described(tile, dst, ssem, next(sems), d) for dst, d in zip(places, devices)]

            self.stages = [stage([sib, across, facing])]
            for bits in groups + [(b,) for b in full_bits]:
                masks = range(1, 1 << len(bits))
                self.stages.append(stage([mate([b for k, b in enumerate(bits) if mask >> k & 1]) for mask in masks]))
            self.stage, self.finished = -1, False

        def start(self):
            self.stage = 0
            for copy in self.stages[0][1]:
                copy.start()

        def advance(self):
            if self.finished or self.stage < 0:
                return
            places, copies = self.stages[self.stage]
            for copy in copies:
                copy.wait()
            tile = self.tile
            if self.stage == 0:
                beside, over, facing_ = places
                n, p = self.everywhere, self.paired
                tile[0:n] = (tile[0:n] + beside[0:n]) + (over[0:n] + facing_[0:n])
                tile[n : n + p] = tile[n : n + p] + over[n + p : n + 2 * p]
            else:
                got = [tile[...]] + [place[...] for place in places]
                while len(got) > 1:
                    got = [got[k] + got[k + 1] for k in range(0, len(got), 2)]
                tile[...] = got[0]
            self.stage += 1
            if self.stage == len(self.stages):
                self.finished = True
                return
            for copy in self.stages[self.stage][1]:
                copy.start()

    first_small = Small(early, 0, 4, 1, [(b,) for b in half_bits])
    last_small = Small(late, 1, 2, 2, [tuple(half_bits)])

    def ready(i, j):
        chunks[i].ready(j)

    to_write = []

    def write_finished():
        while to_write:
            region = to_write.pop()
            region.done = local(region.xr.at[region.window(region.place)], region.to)

    def hook(name):
        pass_on(name)
        for i in PLAN.get(name, ()):
            (chunks + [last_small, first_small])[i].advance()
            if not inside_loop:
                write_finished()

    def chunk_rows(j, i, at):
        span = pl.ds(at, BLOCK)
        cols = slice(j * units + i * BLOCK, j * units + (i + 1) * BLOCK)
        mine = slice(i * BLOCK, (i + 1) * BLOCK)
        bias = (bias_u if j == 0 else uoth)[mine].reshape(1, BLOCK)
        h = dot(n2_s[span], w1_s[j, i]) + bias
        a, slope = gelu_pair(h)
        a_s[span, cols] = a.astype(BF16)
        g = (dot_nt(cot_s[span], w2_s[j, mine]) * slope).astype(BF16)
        g_s[span, cols] = g

    def chunk_grads(j, i):
        cols = slice(j * units + i * BLOCK, j * units + (i + 1) * BLOCK)
        mine = slice(i * BLOCK, (i + 1) * BLOCK)
        to = oth if j == 1 else own

        def second(at):
            to[pl.ds(i * BLOCK + at, 128)] = dot_tn(a_s[:, pl.ds(cols.start + at, 128)], cot_s[...]).astype(BF16)

        loop(BLOCK, 128, second)
        ready(2 * i, j)
        g = g_s[:, cols]

        def first(at):
            (oth1 if j == 1 else own1)[i, pl.ds(at, BLOCK)] = dot(n2t_s[pl.ds(at, BLOCK)], g_s[:, cols]).astype(BF16)

        loop(width, BLOCK, first)
        ready(2 * i + 1, j)
        early[4 + j : 5 + j, mine] = column_sum(g.astype(F32))
        hook(f"f{j}{i}")

    def feed(j, i, first=False):
        if first:
            loop(count, BLOCK, lambda at: chunk_rows(j, i, at))
            hook(f"r{j}{i}.0")
            cot_copy.wait_recv()

            def received(at):
                n2_half(at).wait_recv()
                chunk_rows(j, i, count + at)

            loop(count, BLOCK, received)
            hook(f"r{j}{i}.1")

            def turned(at):
                n2t_s[:, pl.ds(at, BLOCK)] = n2_s[pl.ds(at, BLOCK)].T

            loop(rows, BLOCK, turned)
        else:
            loop(rows, BLOCK, lambda at: chunk_rows(j, i, at), service(f"r{j}{i}.", hook), 2)
        chunk_grads(j, i)

    early[...] = jnp.zeros_like(early)
    late[...] = jnp.zeros_like(late)

    def sum_cot(at):
        early[3:4] += column_sum(cot_s[pl.ds(at, 128)].astype(F32))

    loop(count, 128, sum_cot)
    unit_copy.wait_recv()
    for i in range(parts):
        have_weight(4 + 2 * i, 5 + 2 * i)
        feed(1, i, first=i == 0)
        feed(0, i)

    def back_two(at):
        span = pl.ds(at, BLOCK)
        total = None
        for j in range(2):
            for i in range(parts):
                at_col = j * units + i * BLOCK
                term = dot_nt(g_s[span, at_col : at_col + BLOCK], w1_s[j, i])
                total = term if total is None else total + term
        return total

    def mlp_part(at):
        span = pl.ds(at, BLOCK)
        return dot(a_s[span, :units], w2_s[0]) + dot(a_s[span, units:], w2_s[1])

    def gn2_half(at):
        return half_copy(sb2.at[pl.ds(at, BLOCK)], rb2.at[pl.ds(at, BLOCK)], 6, at)

    def dm_half(at):
        return half_copy(n2_s.at[pl.ds(at, BLOCK)], n2_s.at[pl.ds(aligned(count + at, BLOCK), BLOCK)], 10, at)

    def back_two_sib(at):
        sb2[pl.ds(at, BLOCK)] = back_two(count + at).astype(BF16)
        gn2_half(at).start()

    def back_two_mine(at):
        gm_s[pl.ds(at, BLOCK)] = back_two(at)

    def mlp_sib(at):
        sb1[pl.ds(at, BLOCK)] = mlp_part(count + at).astype(BF16)

    loop(count, BLOCK, back_two_sib)
    hook("g0")
    loop(count, BLOCK, back_two_mine)
    hook("gn2")

    def second_back(at):
        gn2_half(at).wait_recv()
        n2_half(at).wait_send()
        for off in range(0, BLOCK, 128):
            spot = pl.ds(aligned(at + off, 128), 128)
            xhat, sigma = norm_stats(mid_s[spot])
            grad = gm_s[spot] + rb2[spot].astype(F32)
            cot = cot_s[spot].astype(F32)
            back = cot + norm_back(grad, ln2_gain, xhat, sigma)
            gm_s[spot] = back
            n2_s[spot] = back.astype(BF16)
            early[0:1] += column_sum(back)
            early[1:2] += column_sum(grad * xhat)
            early[2:3] += column_sum(grad)
        dm_half(at).start()

    loop(count, BLOCK, second_back)
    hook("lb")
    for at in range(0, count, BLOCK):
        att_half(at).wait_send()
    loop(count, BLOCK, mlp_sib)
    mlp_copy = remote(sb1, rb1, csem, 8, sib)
    first_small.start()
    hook("ln2")

    for at in range(0, count, BLOCK):
        dm_half(at).wait_recv()

    start = base_a + quarter
    zero = jnp.zeros((count, 128), BF16)
    grad_s = dq_s = ou_s
    n1_copy.wait_send()

    def keep_gradient(j, c):
        to = oth if j == 1 else own
        low = start + c * quarter
        dt = ot_s.at[j * quarter : (j + 1) * quarter]

        def columns(at):
            to[low : low + quarter, pl.ds(at, BLOCK)] = dot(dt[...], nr_s[:, pl.ds(at, BLOCK)]).astype(BF16)

        loop(width, BLOCK, columns)
        ready(first_att + 1 + c, j)
        if c != 1:
            d = g_s[:, (3 * j + c) * BLOCK : (3 * j + c) * BLOCK + quarter]
            late[2 + c // 2 + 2 * j : 3 + c // 2 + 2 * j, :quarter] = column_sum(d.astype(F32))

    def values_back(j):
        base = j * quarter
        to = oth if j == 1 else own

        def weight(at):
            to[base_a : base_a + quarter, pl.ds(at, BLOCK)] = dot(ou_s[base : base + quarter], n2_s[:, pl.ds(at, BLOCK)]).astype(BF16)

        loop(width, BLOCK, weight)
        ready(first_att, j)

        def output(at):
            grad_s[base : base + quarter, pl.ds(at, BLOCK)] = dot_nt(wo_s[base : base + quarter], n2_s[pl.ds(at, BLOCK)]).astype(BF16)

        loop(rows, BLOCK, output)
        hook(f"w{j}.0")
        go_s = n1_s.at[:, 256 * j : 256 * (j + 1)]

        def scale(at):
            here = pl.ds(at, BLOCK)
            grad_t = dot_nt(grad_s[base : base + quarter], roll_s[here])
            for head in range(heads):
                row = j * heads + head
                r = r_s[row : row + 1, here]
                g = grad_t[head * HEAD : (head + 1) * HEAD]
                at_head = slice(base + head * HEAD, base + (head + 1) * HEAD)
                in_s[row : row + 1, here] = column_sum(g * ot_s[at_head, here].astype(F32)) * r
                gt_s[at_head, here] = (g * r).astype(BF16)
            go_s[here, :quarter] = gt_s[base : base + quarter, here].T

        loop(rows, BLOCK, scale)

        def block(at):
            here = pl.ds(at, count)
            b = at // count
            dv = [None, None]
            for head in range(heads):
                tile = head // 2
                gh = jnp.where(lane_half(count, head % 2 == 1), go_s[here, 128 * tile : 128 * tile + 128], zero)
                part = dot(e_s[j * heads + head, b], gh)
                dv[tile] = part if dv[tile] is None else dv[tile] + part
            dv = jnp.concatenate(dv, axis=1)[:, :quarter].astype(BF16)
            g_s[here, (3 * j + 2) * BLOCK : (3 * j + 2) * BLOCK + quarter] = dv
            ot_s[base : base + quarter, here] = dv.T

        loop(rows, count, block)
        hook(f"w{j}.1")
        keep_gradient(j, 2)
        hook(f"v{j}")

    def scores_back(j):
        base = j * quarter

        def block(at):
            here = pl.ds(at, count)
            b = at // count
            dk = [None, None]
            for head in range(heads):
                tile = head // 2
                row = j * heads + head
                half = lane_half(count, head % 2 == 1)
                lanes = slice(128 * tile, 128 * tile + 128)
                vh = jnp.where(half, v_s[j, here, lanes], zero)
                qh = jnp.where(half, q_s[j, here, lanes], zero)
                last_row = min(128 * tile + 128, quarter)
                vh = vh[:, : last_row - 128 * tile]
                ds = n2t_s.at[:count, head * count : (head + 1) * count] if head < 2 else ds_s
                for off in range(0, count, BLOCK):
                    some = pl.ds(aligned(at + off, BLOCK), BLOCK)
                    dp_t = dot(vh, gt_s[base + 128 * tile : base + last_row, some])
                    grad = (dp_t - in_s[row : row + 1, some]).astype(BF16)
                    ds[:, off : off + BLOCK] = grad * e_s[row, b, :, off : off + BLOCK]
                part = dot(ds[...], qh)
                dk[tile] = part if dk[tile] is None else dk[tile] + part
                kth = kt_s[base + head * HEAD : base + head * HEAD + HEAD, here]
                dq_s[base + head * HEAD : base + head * HEAD + HEAD, here] = dot(kth, ds[...]).astype(BF16)
            dk = jnp.concatenate(dk, axis=1)[:, :quarter].astype(BF16)
            g_s[here, (3 * j + 1) * BLOCK : (3 * j + 1) * BLOCK + quarter] = dk
            ot_s[base : base + quarter, here] = dk.T
            g_s[here, 3 * j * BLOCK : 3 * j * BLOCK + quarter] = dq_s[base : base + quarter, here].T

        loop(rows, count, block, service(f"b{j}.", hook))
        keep_gradient(j, 1)
        hook(f"k{j}")
        ot_s[base : base + quarter] = dq_s[base : base + quarter]
        keep_gradient(j, 0)
        hook(f"s{j}")

    values_back(1)
    scores_back(1)
    values_back(0)
    scores_back(0)

    def finish_out(at):
        span = pl.ds(at, BLOCK)
        mid_s[span] = mid_s[span] + mlp_part(at) + fc2_bias

    loop(count, BLOCK, finish_out)
    hook("fo")
    mlp_copy.wait_recv()

    def write_out(at):
        spot = pl.ds(at, 128)
        tok_s[spot] = (mid_s[spot] + rb1[spot].astype(F32)).astype(BF16)

    loop(count, 128, write_out)
    put_out = local(tok_s, out_h)
    hook("fin")

    def back_one(at):
        total = None
        for j in range(2):
            for c in range(3):
                d = g_s[pl.ds(at, BLOCK), (3 * j + c) * BLOCK : (3 * j + c) * BLOCK + quarter]
                term = dot(d, wq_s[j, c])
                total = term if total is None else total + term
        n2_s[pl.ds(at, BLOCK)] = total.astype(BF16)

    for at in range(0, count, BLOCK):
        dm_half(at).wait_send()
    loop(rows, BLOCK, back_one, service("d.", hook), 2)
    for at in range(0, count, BLOCK):
        gn2_half(at).wait_send()

    def gn1_half(at):
        return half_copy(sb2.at[pl.ds(at, BLOCK)], rb2.at[pl.ds(at, BLOCK)], 12, at)

    def back_one_sib(at):
        sb2[pl.ds(at, BLOCK)] = dot(back_s[pl.ds(count + at, BLOCK)], n2_s[...]).astype(BF16)
        gn1_half(at).start()

    def back_one_mine(at):
        mid_s[pl.ds(at, BLOCK)] = dot(back_s[pl.ds(at, BLOCK)], n2_s[...])

    loop(count, BLOCK, back_one_sib)
    loop(count, BLOCK, back_one_mine)
    hook("e.0")
    mlp_copy.wait_send()

    def first_back(at):
        gn1_half(at).wait_recv()
        for off in range(0, BLOCK, 128):
            spot = pl.ds(aligned(at + off, 128), 128)
            xhat, sigma = norm_stats(sin_s[spot])
            grad = mid_s[spot] + rb2[spot].astype(F32)
            sb1[spot] = (gm_s[spot] + norm_back(grad, ln1_gain, xhat, sigma)).astype(BF16)
            late[0:1] += column_sum(grad * xhat)
            late[1:2] += column_sum(grad)

    loop(count, BLOCK, first_back)
    put_in = local(sb1, ing_h)
    last_small.start()
    hook("e.1")
    hook("tail")
    left = [first_small, last_small] + chunks
    while left:
        for item in left:
            item.advance()
            write_finished()
        left = [item for item in left if not item.finished]

    for row, source, at in ((0, late, 0), (1, late, 1), (2, early, 0), (3, early, 1), (4, early, 2), (5, early, 3), (8, early, 4), (9, late, 2), (10, late, 3)):
        small_o[row : row + 1] = source[at : at + 1]

    passed = [copy for item in pieces for copy in item.copies]
    for copy in [unit_copy, head_copy, cot_copy] + [gn1_half(at) for at in range(0, count, BLOCK)] + passed:
        copy.wait_send()
    for chunk in chunks:
        for copy in chunk.sent:
            copy.wait_send()
        chunk.done.wait()
    put_out.wait()
    put_in.wait()


def copies_of(full):
    most = 0
    for kind in ORDERS:
        first, after = KINDS[kind]
        most = max(most, 1 + full + 2 * sum((1 << len(bits)) - 1 for bits in after) + (0 if first is None else 3))
    return most


def call_layer(dp_size, tokens, cotangent, ids, vectors, wq, wo, w1, w2):
    count, width = tokens.shape
    rows = 2 * count
    quarter = wo.shape[0]
    units = w1.shape[1]
    heads = quarter // HEAD
    grad_rows = units + 4 * quarter
    parts = units // BLOCK
    bits = [b for b in range(20) if (1 << b) < dp_size]
    half_bits = bits[:3]
    shape = jax.ShapeDtypeStruct
    vm = pltpu.VMEM
    regions = 2 * (units // BLOCK) + 4
    steps = copies_of(len(bits) - len(half_bits))
    fetched = 4 + 2 * (units // BLOCK)
    scratch = (
        [vm((count, width), BF16), vm((rows, width), BF16)]
        + [vm((count, width), F32)] * 3
        + [vm((rows, width), BF16)] * 2
        + [vm((width, rows), BF16)]
        + [vm((2,) + wq.shape, BF16), vm((2 * quarter, width), BF16), vm((2, units // BLOCK, width, BLOCK), BF16), vm((2,) + w2.shape, BF16)]
        + [vm((2, rows, 256), BF16)] * 2
        + [vm((2 * quarter, rows), BF16)] * 4
        + [vm((8, rows), F32)] * 2
        + [vm((2 * heads, 2, count, count), BF16)]
        + [vm((rows, rows), BF16)] * 2
        + [vm((rows, width), BF16), vm((count, count), BF16)]
        + [vm((rows, 2 * units), BF16)] * 2
        + [vm((count, width), BF16)] * 4
        + [vm((grad_rows, width), BF16)] * 3
        + [vm((7 * units // 8 + 4 * quarter, width), BF16), vm((units // 2, width), BF16)]
        + [vm((parts, width, BLOCK), BF16)] * 3
        + [vm((parts, 7 * width // 8, BLOCK), BF16), vm((parts, width // 2, BLOCK), BF16)]
        + [vm((grad_rows >> len(half_bits), width), BF16)] * (len(bits) - len(half_bits))
        + [vm((parts, width // 8, BLOCK), BF16)] * (len(bits) - len(half_bits))
        + [vm((SIDE, width // 3), F32), vm((units,), F32), vm((2, quarter), F32), vm((8, width), F32), vm((8, width), F32)]
        + [vm((6, 8, width), F32), vm((14 + 2 * (len(bits) - 3), 8, width), F32)]
        + [pltpu.SemaphoreType.DMA((8 + units // BLOCK + regions,))]
        + [pltpu.SemaphoreType.DMA((2, n)) for n in (3 * fetched + 2, 14, regions * steps, 2 * (10 + len(bits) - 3))]
    )
    anywhere = pl.BlockSpec(memory_space=pl.ANY)
    inside = pl.BlockSpec(memory_space=pltpu.VMEM)
    return pl.pallas_call(
        functools.partial(layer, dp_size, half_bits),
        out_shape=[shape((count, width), BF16)] * 2
        + [shape(w2.shape, BF16), shape(w1.shape, BF16), shape(wo.shape, BF16), shape(wq.shape, BF16), shape((16, width), F32)],
        in_specs=[anywhere] * 2 + [inside] * (1 + len(vectors)) + [anywhere] * 4,
        out_specs=[anywhere] * 6 + [inside],
        scratch_shapes=scratch,
        compiler_params=pltpu.CompilerParams(vmem_limit_bytes=VMEM_LIMIT, collective_id=0, has_side_effects=True),
        name="layer",
    )(tokens, cotangent, ids, *vectors, wq, wo, w1, w2)


def finish(*refs):
    sources, small, rest = refs[:6], refs[6], refs[7:]
    results, vectors, rest = rest[:6], rest[6:14], rest[14:]
    narrow, wide, (get, put) = rest[:6], rest[6:10], rest[10:]
    order = (2, 3, 5, 4, 0, 1)
    reads = {k: pltpu.make_async_copy(sources[k], narrow[k], get.at[k]) for k in order}
    for k in order:
        reads[k].start()
    for i in range(6):
        vectors[i][...] = small[i]
    vectors[6][...] = small[8, : vectors[6].shape[0]]
    vectors[7][...] = small[9:11, : vectors[7].shape[1]]
    writes = []
    for k in order:
        reads[k].wait()
        low = narrow[k]
        if k < 2:
            places = [slice(None)]
        elif low.ndim == 3:
            places = list(range(low.shape[0]))
        else:
            step = min(BLOCK, low.shape[0])
            places = [pl.ds(at, step) for at in range(0, low.shape[0], step)]
        for at in places:
            if k < 2:
                high = low
            else:
                part, high = low.at[at], wide[k - 2].at[at]

                def cast(row, part=part, high=high):
                    high[pl.ds(row, 64)] = part[pl.ds(row, 64)].astype(F32)

                loop(part.shape[0], 64, cast)
            to = results[k] if k < 2 else results[k].at[at]
            writes.append(pltpu.make_async_copy(high, to, put.at[len(writes)]))
            writes[-1].start()
    for copy in writes:
        copy.wait()


def call_finish(arrays, small, units, quarter):
    width = small.shape[1]
    shape = jax.ShapeDtypeStruct
    extents = [(width,)] * 6 + [(units,), (2, quarter)]
    kinds = [BF16, BF16, F32, F32, F32, F32]
    anywhere = pl.BlockSpec(memory_space=pl.ANY)
    inside = pl.BlockSpec(memory_space=pltpu.VMEM)
    grads = arrays[2:]
    return pl.pallas_call(
        finish,
        in_specs=[anywhere] * len(arrays) + [inside],
        out_specs=[anywhere] * len(arrays) + [inside] * len(extents),
        out_shape=[shape(a.shape, k) for a, k in zip(arrays, kinds)] + [shape(e, F32) for e in extents],
        scratch_shapes=[pltpu.VMEM(a.shape, BF16) for a in arrays]
        + [pltpu.VMEM(a.shape, F32) for a in grads]
        + [pltpu.SemaphoreType.DMA((16,)), pltpu.SemaphoreType.DMA((16,))],
        compiler_params=pltpu.CompilerParams(vmem_limit_bytes=VMEM_LIMIT),
        name="finish",
    )(*arrays, small)


def per_device(
    tokens, segment_ids, ln1_gain, ln1_bias, qkv_weight, qv_bias, out_weight, out_bias,
    ln2_gain, ln2_bias, fc1_weight, fc1_bias, fc2_weight, fc2_bias, cotangent,
):
    vectors = (ln1_gain, ln1_bias, out_bias, ln2_gain, ln2_bias, fc2_bias, fc1_bias, qv_bias)
    *arrays, small = call_layer(
        lax.axis_size("dp"), tokens, cotangent, segment_ids, vectors, qkv_weight.transpose(0, 2, 1), out_weight, fc1_weight, fc2_weight
    )
    out, ing, g2, g1, go, gq, a0, a1, a2, a3, a4, a5, g_units, g_heads = call_finish(arrays, small, fc1_weight.shape[1], out_weight.shape[0])
    return (out, ing, a0, a1, gq.transpose(0, 2, 1), g_heads, go, a2, a3, a4, g1, g_units, g2, a5)


def solution(mesh):
    placed = (
        P(("dp", "tensor"), None),
        P("dp", None),
        P(),
        P(),
        P(None, None, "tensor"),
        P(None, "tensor"),
        P("tensor", None),
        P(),
        P(),
        P(),
        P(None, "tensor"),
        P("tensor"),
        P("tensor", None),
        P(),
        P(("dp", "tensor"), None),
    )
    return jax.shard_map(
        per_device,
        mesh=mesh,
        in_specs=placed,
        out_specs=(
            P(("dp", "tensor"), None),
            P(("dp", "tensor"), None),
            P(),
            P(),
            P(None, None, "tensor"),
            P(None, "tensor"),
            P("tensor", None),
            P(),
            P(),
            P(),
            P(None, "tensor"),
            P("tensor"),
            P("tensor", None),
            P(),
        ),
        check_vma=False,
    )
```

```python
import functools
import math

import jax
import jax.numpy as jnp
from jax import lax
from jax.experimental import pallas as pl
from jax.experimental.pallas import tpu as pltpu
from jax.sharding import PartitionSpec as P

HEAD = 64
SIDE = 16
EPSILON = 1e-06
NEG_LARGE = -1e30
SCALE = HEAD ** (-0.5)
F32 = jnp.float32
BF16 = jnp.bfloat16
VMEM_LIMIT = 64 * 1024 * 1024 - 128 * 1024
MESH = pl.DeviceIdType.MESH
BLOCK = 256
KINDS = {
    "A": (None, ((0,), (1,), (2,))),
    "B": (None, ((1,), (0,), (2,))),
    "D": (None, ((0,), (1, 2))),
    "E": (None, ((0, 1, 2),)),
    "C": (None, ((0, 1), (2,))),
    "Y": (0, ((1,), (2,))),
    "Z": (1, ((0,), (2,))),
    "YD": (0, ((1, 2),)),
    "S": (None, (("p",), ("q",), (2,))),
    "SD": (None, (("p",), ("q", 2))),
    "SF": ("p", (("q",), (2,))),
    "SFD": ("p", (("q", 2),)),
}
ORDERS = ("SFD", "C", "SF", "SF", "D", "SF", "D", "D", "C", "D")
WEIGHT_PLAN = {"p0": (0, 1), "a2": (2,), "p1": (3,), "c0": (4,), "c3": (5,), "n": (6,), "f10": (7,), "f00": (8,), "r11.1": (9,)}
PLAN = {
    "r01.1": (0,),
    "r12.1": (1,),
    "r02.0": (0, 2),
    "f02": (3,),
    "lb": (1, 4, 0),
    "w1.0": (2, 5, 1, -1),
    "w1.1": (3, 4),
    "v1": (0,),
    "b1.0": (2, -1, 1, 3),
    "b1.1": (4,),
    "k1": (0,),
    "s1": (5, 2, -1),
    "w0.0": (6,),
    "w0.1": (1,),
    "v0": (9, 3),
    "b0.0": (4, 6, 5),
    "b0.1": (2, -1, 3, 9),
    "k0": (8,),
    "s0": (6, 4),
    "fo": (2, 7, 5, 3),
    "d.0": (9,),
    "d.1": (8,),
    "e.0": (6,),
    "e.1": (7, 2, 5),
    "tail": (3, -2, 6, 9, 8, 7, 5, 9, -2, 8, 7, 5, 8, 7),
}


def dot(a, b):
    return jnp.dot(a, b, preferred_element_type=F32)


def dot_nt(a, b):
    return lax.dot_general(a, b, (((1,), (1,)), ((), ())), preferred_element_type=F32)


def dot_tn(a, b):
    return lax.dot_general(a, b, (((0,), (0,)), ((), ())), preferred_element_type=F32)


def lane_half(rows, upper):
    lanes = lax.broadcasted_iota(jnp.int32, (rows, 128), 1)
    return lanes >= HEAD if upper else lanes < HEAD


def head_lanes(ref, head, filler):
    tile = ref[:, 128 * (head // 2) : 128 * (head // 2) + 128]
    return jnp.where(lane_half(tile.shape[0], head % 2 == 1), tile, filler)


def gelu_pair(h):
    cdf = 0.5 + 0.5 * lax.erf(h * 0.7071067811865476)
    return h * cdf, cdf + h * jnp.exp(-0.5 * h * h) * 0.3989422804014327


def norm_stats(v):
    centred = v - jnp.mean(v, axis=-1, keepdims=True)
    sigma = lax.rsqrt(jnp.mean(centred * centred, axis=-1, keepdims=True) + EPSILON)
    return centred * sigma, sigma


def norm_back(grad, gain, xhat, sigma):
    g = grad * gain
    return sigma * (g - jnp.mean(g, axis=-1, keepdims=True) - xhat * jnp.mean(g * xhat, axis=-1, keepdims=True))


def column_sum(v):
    return jnp.sum(v, axis=0, keepdims=True)


def aligned(v, unit):
    return v if isinstance(v, int) else pl.multiple_of(v, unit)


def loop(count, step, body, service=None, every=1):
    def run(i, carry):
        body(aligned(i * step, step))
        if service is not None:
            for k in range(count // step // every):
                if service(k, True):
                    pl.when(i == every * (k + 1) - 1)(functools.partial(service, k, False))
        return carry

    lax.fori_loop(0, count // step, run, 0)


def layer(
    dp_size, half_bits,
    tok_h, cot_h, ids, gain1, bias1, bias_o, gain2, bias2, bias_f, bias_u, bias_qv, wq_h, wo_h, w1_h, w2_h,
    out_h, ing_h, g2_h, g1_h, go_h, gq_h, small_o,
    tok_s, cot_s, sin_s, mid_s, gm_s, n1_s, n2_s, n2t_s, wq_s, wo_s, w1_s, w2_s,
    q_s, v_s, kt_s, ot_s, ou_s, gt_s, r_s, in_s, e_s, roll_s, back_s, nr_s, ds_s, a_s, g_s, sb1, sb2, rb1, rb2,
    own, oth, xr, land, land_both, own1, oth1, xr1, land1, land1_both, *rest,
):
    rest = list(rest)
    full_bits = [b for b in range(20) if (1 << b) < dp_size and b not in half_bits]
    rx = [rest.pop(0) for _ in full_bits]
    rx1 = [rest.pop(0) for _ in full_bits]
    table, uoth, voth, early, late, near, far, lsem, wsem, csem, gsem, ssem = rest

    count, width = tok_s.shape
    rows = 2 * count
    quarter = wo_h.shape[0]
    units = w1_h.shape[1]
    heads = quarter // HEAD
    place = lax.axis_index("tensor")
    dp = lax.axis_index("dp")
    chip = place // 2
    core = place % 2
    sib = {"tensor": chip * 2 + 1 - core}
    across = {"tensor": (1 - chip) * 2 + core}
    facing = {"tensor": (1 - chip) * 2 + 1 - core}
    all_bits = list(half_bits) + full_bits
    sides = {b: (dp // (1 << b)) % 2 for b in all_bits}

    ways = {b: (1 - 2 * sides[b]) * (1 << b) for b in all_bits}
    sides["p"] = sides[0] + (sides[1] - sides[0]) * core
    sides["q"] = sides[1] + (sides[0] - sides[1]) * core
    ways["p"] = ways[0] + (ways[1] - ways[0]) * core
    ways["q"] = ways[1] + (ways[0] - ways[1]) * core

    def mate(bits):
        return {"dp": dp + sum(ways[b] for b in bits)}

    def described(src, dst, sems, index, device):
        return pltpu.make_async_remote_copy(
            src_ref=src, dst_ref=dst, send_sem=sems.at[0, index], recv_sem=sems.at[1, index], device_id=device, device_id_type=MESH
        )

    mates = {b: mate((b,)) for b in all_bits}
    groups = {(b,) for b in full_bits}
    for mask in range(1, 1 << len(half_bits)):
        groups.add(tuple(b for k, b in enumerate(half_bits) if mask >> k & 1))

    barrier = pltpu.get_barrier_semaphore()
    partners = [sib, across, facing] + [mate(bits) for bits in sorted(groups)]
    for partner in partners:
        pl.semaphore_signal(barrier, inc=1, device_id=partner, device_id_type=MESH)

    sq_s, sk_s, k_s = a_s.at[:, 0:128], a_s.at[:, 128:256], a_s.at[:, 256:512]
    local_used = [0]

    def local(src, dst):
        copy = pltpu.make_async_copy(src, dst, lsem.at[local_used[0]])
        local_used[0] += 1
        copy.start()
        return copy

    def remote(src, dst, sems, index, device):
        copy = pltpu.make_async_remote_copy(
            src_ref=src, dst_ref=dst, send_sem=sems.at[0, index], recv_sem=sems.at[1, index], device_id=device, device_id_type=MESH
        )
        copy.start()
        return copy

    def half_copy(src, dst, first, at):
        return pltpu.make_async_remote_copy(
            src_ref=src,
            dst_ref=dst,
            send_sem=csem.at[0, first + at // BLOCK],
            recv_sem=csem.at[1, first + at // BLOCK],
            device_id=sib,
            device_id_type=MESH,
        )

    get_tok = local(tok_h, tok_s)
    get_wq = local(wq_h, wq_s.at[0])
    get_cot = local(cot_h, cot_s.at[pl.ds(0, count)])
    get_wo = local(wo_h, wo_s.at[pl.ds(0, quarter)])
    get_w1 = [local(w1_h.at[:, pl.ds(i * BLOCK, BLOCK)], w1_s.at[0, i]) for i in range(units // BLOCK)]
    get_w2 = local(w2_h, w2_s.at[0])

    part = (sides[0] + sides[1]) % 2

    class Piece:
        def __init__(self, index, refs, at, extent):
            size = extent // 4

            def some(k, first, size):
                return refs[k].at[pl.ds(aligned(at[k] + part * (extent // 2) + first, 16), size)]

            self.copies = [described(some(0, 0, 2 * size), some(1, 0, 2 * size), wsem, 3 * index, across)]
            for k in range(2):
                block = some(1, k * size, size)
                self.copies.append(described(block, block, wsem, 3 * index + 1 + k, mates[k]))
            self.stage = 0

        def advance(self):
            if self.stage == 0:
                self.copies[0].wait_recv()
                self.copies[1].start()
                self.copies[2].start()
            else:
                self.copies[1].wait_recv()
                self.copies[2].wait_recv()
            self.stage += 1

    pieces = [Piece(c, (wq_h.at[c], wq_s.at[1, c]), (0, 0), quarter) for c in range(3)]
    pieces.append(Piece(3, (wo_h, wo_s), (0, quarter), quarter))
    for i in range(units // BLOCK):
        pieces.append(Piece(4 + 2 * i, (w1_s.at[0, i], w1_s.at[1, i]), (0, 0), width))
        pieces.append(Piece(5 + 2 * i, (w2_s.at[0], w2_s.at[1]), (i * BLOCK, i * BLOCK), BLOCK))
    pl.semaphore_wait(barrier, len(partners))
    unit_copy = remote(bias_u, uoth, wsem, 3 * len(pieces), across)
    head_copy = remote(bias_qv, voth, wsem, 3 * len(pieces) + 1, across)
    for item in pieces[:4]:
        item.copies[0].start()

    inside_loop = []

    def service(name, act):
        def at_point(k, ask):
            full = f"{name}{k}"
            if ask:
                return full in PLAN or full in WEIGHT_PLAN
            inside_loop.append(full)
            act(full)
            inside_loop.pop()

        return at_point

    def pass_on(name):
        for i in WEIGHT_PLAN.get(name, ()):
            if pieces[i].stage < 1:
                pieces[i].advance()

    def have_weight(*which):
        for i in which:
            while pieces[i].stage < 2:
                pieces[i].advance()

    ln1_gain, ln1_bias, out_bias, ln2_gain, ln2_bias, fc2_bias = (
        ref[...].reshape(1, width) for ref in (gain1, bias1, bias_o, gain2, bias2, bias_f)
    )
    third = width // 6
    place_k = lax.broadcasted_iota(jnp.int32, (SIDE, third), 1).astype(F32)
    angles = lax.broadcasted_iota(jnp.int32, (SIDE, third), 0).astype(F32) * jnp.exp(place_k * (-math.log(10000.0) / third))
    table[:, :third] = jnp.sin(angles)
    table[:, third:] = jnp.cos(angles)
    get_tok.wait()

    def first_norm(at):
        plane = core * (count // (SIDE * SIDE)) + at // (SIDE * SIDE)
        line = (at // SIDE) % SIDE
        shape = (SIDE, width // 3)
        for k in range(4):
            spot = jnp.concatenate(
                [jnp.broadcast_to(table[pl.ds(plane, 1)], shape), jnp.broadcast_to(table[pl.ds(line + k, 1)], shape), table[...]], axis=1
            )
            span = pl.ds(aligned(at + k * SIDE, SIDE), SIDE)
            stream = tok_s[span].astype(F32) + spot
            sin_s[span] = stream
            xhat, _ = norm_stats(stream)
            n1_s[span] = (xhat * ln1_gain + ln1_bias).astype(BF16)

    loop(count, 4 * SIDE, first_norm)
    doc = ids[pl.ds(chip, 1), :]
    starts = [jnp.zeros((1, 1), F32)]
    starts += [jnp.sum(jnp.where(doc < v, 1.0, 0.0), axis=1, keepdims=True) for v in range(1, 4)]
    starts.append(jnp.full((1, 1), rows, F32))
    turn = jnp.zeros((1, 1), F32)
    for v in range(4):
        turn += jnp.where(starts[v + 1] - starts[v] == count, starts[v], 0.0)
    turn_here = turn - (core * count).astype(F32)

    def wrapped(v):
        v = jnp.where(v >= rows, v - rows, v)
        return jnp.where(v < 0, v + rows, v)

    def rotations(at):
        down = (lax.broadcasted_iota(jnp.int32, (64, rows), 0) + at).astype(F32)
        along = lax.broadcasted_iota(jnp.int32, (64, rows), 1).astype(F32)
        roll_s[pl.ds(at, 64)] = jnp.where(wrapped(down + turn_here) == along, 1.0, 0.0).astype(BF16)
        back_s[pl.ds(at, 64)] = jnp.where(wrapped(down - turn_here) == along, 1.0, 0.0).astype(BF16)
        where = wrapped((lax.broadcasted_iota(jnp.int32, (64, 128), 0) + at).astype(F32) + turn)
        mine = sum(jnp.where(where >= starts[v], 1.0, 0.0) for v in range(1, 4))
        slot = (lax.broadcasted_iota(jnp.int32, (64, 128), 1) % HEAD).astype(F32)
        sq_s[pl.ds(at, 64)] = jnp.where((slot < 4) & (slot != mine), 1.0, 0.0).astype(BF16)
        sk_s[pl.ds(at, 64)] = jnp.where(slot == mine, NEG_LARGE, 0.0).astype(BF16)


    get_wq.wait()
    get_wo.wait()
    for copy in get_w1:
        copy.wait()
    get_w2.wait()
    for item in pieces[4:]:
        item.copies[0].start()
    n1_copy = remote(n1_s.at[pl.ds(0, count)], n1_s.at[pl.ds(count, count)], csem, 0, sib)
    get_cot.wait()
    cot_copy = remote(cot_s.at[pl.ds(0, count)], cot_s.at[pl.ds(count, count)], csem, 1, sib)

    def rotate(at):
        nr_s[pl.ds(at, BLOCK)] = dot(roll_s[pl.ds(at, BLOCK)], n1_s[...]).astype(BF16)

    def project(j, at):
        n = nr_s[pl.ds(at, BLOCK)]
        biases = bias_qv if j == 0 else voth
        q = (dot_nt(n, wq_s[j, 0]) + biases[0:1]).astype(BF16) * SCALE
        k = dot_nt(n, wq_s[j, 1]).astype(BF16)
        v = (dot_nt(n, wq_s[j, 2]) + biases[1:2]).astype(BF16)
        q_s[j, pl.ds(at, BLOCK), :quarter] = q
        k_s[pl.ds(at, BLOCK), :quarter] = k
        v_s[j, pl.ds(at, BLOCK), :quarter] = v
        kt_s[j * quarter : (j + 1) * quarter, pl.ds(at, BLOCK)] = k.T * SCALE

    blocks = [(b, at) for b in range(2) for at in range(0, count, BLOCK)]

    def attend(j):
        for head in range(heads):
            at = 512 + 256 * head
            a_s[:, at : at + 128] = head_lanes(q_s.at[j], head, sq_s[...])
            a_s[:, at + 128 : at + 256] = head_lanes(k_s, head, sk_s[...])
        for at in range(0, rows, BLOCK):
            ou_s[:quarter, at : at + BLOCK] = v_s[j, at : at + BLOCK, :quarter].T

        def tile(here):
            b = here // count
            at = aligned(here % count, BLOCK)
            keys = pl.ds(aligned(b * count, count), count)
            for head in range(heads):
                column = 512 + 256 * head
                s = dot_nt(a_s[keys, column + 128 : column + 256], a_s[pl.ds(here, BLOCK), column : column + 128])
                m = jnp.max(s, axis=0, keepdims=True)
                e = jnp.exp(s - m)
                r = 1.0 / column_sum(e)
                low = e.astype(BF16)
                span = slice(head * HEAD, head * HEAD + HEAD)
                to = slice(j * quarter + head * HEAD, j * quarter + head * HEAD + HEAD)
                e_s[j * heads + head, b, :, pl.ds(at, BLOCK)] = low
                ot_s[to, pl.ds(here, BLOCK)] = (dot(ou_s[span, keys], low) * r).astype(BF16)
                r_s[j * heads + head : j * heads + head + 1, pl.ds(here, BLOCK)] = r

        return tile

    loop(rows, 64, rotations)
    n1_copy.wait_recv()
    loop(rows, BLOCK, rotate)
    loop(rows, BLOCK, lambda at: project(0, at))
    pass_on("p0")
    loop(rows, BLOCK, attend(0), service("a", pass_on))
    head_copy.wait_recv()
    have_weight(0, 1, 2)
    loop(rows, BLOCK, lambda at: project(1, at))
    pass_on("p1")
    loop(rows, BLOCK, attend(1), service("c", pass_on))

    have_weight(3)

    def unrotate(at):
        ou_s[:, pl.ds(at, BLOCK)] = dot(ot_s[...], roll_s[:, pl.ds(at, BLOCK)]).astype(BF16)

    loop(rows, BLOCK, unrotate)
    pass_on("u")

    def out_part(at):
        return dot_tn(ou_s[:, pl.ds(at, BLOCK)], wo_s[...])

    def att_half(at):
        return half_copy(sb1.at[pl.ds(at, BLOCK)], rb1.at[pl.ds(at, BLOCK)], 2, at)

    def n2_half(at):
        return half_copy(n2_s.at[pl.ds(at, BLOCK)], n2_s.at[pl.ds(aligned(count + at, BLOCK), BLOCK)], 4, at)

    def out_sib(at):
        sb1[pl.ds(at, BLOCK)] = out_part(count + at).astype(BF16)
        att_half(at).start()

    loop(count, BLOCK, out_sib)

    def out_mine(at):
        mid_s[pl.ds(at, BLOCK)] = sin_s[pl.ds(at, BLOCK)] + out_part(at) + out_bias

    loop(count, BLOCK, out_mine)
    pass_on("o")

    def second_norm(at):
        att_half(at).wait_recv()
        for off in range(0, BLOCK, 128):
            spot = pl.ds(aligned(at + off, 128), 128)
            mid = mid_s[spot] + rb1[spot].astype(F32)
            mid_s[spot] = mid
            xhat, _ = norm_stats(mid)
            n2_s[spot] = (xhat * ln2_gain + ln2_bias).astype(BF16)
        n2_half(at).start()

    loop(count, BLOCK, second_norm)
    pass_on("n")

    base_a = units
    parts = units // BLOCK
    steps = copies_of(len(full_bits))

    class Region:
        def __init__(self, index, row, size, cols, slot, kind, refs, to):
            own_r, oth_r, xr_r, land_r, both_r, rx_r = refs
            self.place, self.slot, self.to, self.xr = (row, size, 0, cols), slot, to, xr_r
            first, after = KINDS[kind]
            self.first = first is not None
            self.stages, self.stage, self.finished, self.sent = [], -1, False, []
            now, parts, used, trail = self.place, 8, 0, []
            sems = iter(range(index * steps, (index + 1) * steps))

            def copy(src, src_at, dst, dst_at, device):
                return described(src.at[self.window(src_at)], dst.at[self.window(dst_at)], gsem, next(sems), device)

            def piece(bits, mask):
                where = now
                for k, b in enumerate(bits):
                    where = self.cut(where, 1 - sides[b] if mask >> k & 1 else sides[b])
                return where

            sums = 1 + len(after) + len(full_bits)
            if self.first:
                keep, give, there = piece((first,), 0), piece((first,), 1), (row // 2, size // 2, 0, cols)
                place = self.landing(0, 4)
                copies = [copy(own_r, give, land_r, place, mate((first,))), copy(oth_r, give, both_r, there, mate((first,)))]
                adds = [(own_r, own_r, keep, [(land_r, place)]), (oth_r, oth_r, keep, [(both_r, there)])]
                self.stages.append((copies, adds, False))
                trail.append(((first,), keep))
                now, parts, used = keep, 4, 4
            self.stages.append(([copy(oth_r, now, xr_r, now, across)], [(own_r, own_r, now, [(xr_r, now)])], False))
            for bits in after:
                parts >>= len(bits)
                keep, copies, terms = piece(bits, 0), [], []
                for mask in range(1, 1 << len(bits)):
                    place = self.landing(used, parts)
                    used += parts
                    terms.append((land_r, place))
                    copies.append(copy(own_r, piece(bits, mask), land_r, place, mate([b for k, b in enumerate(bits) if mask >> k & 1])))
                self.stages.append((copies, [(own_r, own_r, keep, terms)], False))
                trail.append((bits, keep))
                now = keep
            for i, b in enumerate(full_bits):
                place = self.small_place()
                self.stages.append(([copy(own_r, now, rx_r[i], place, mates[b])], [(own_r, own_r, now, [(rx_r[i], place)])], True))
            copies, adds, full = self.stages[-1]
            self.stages[-1] = (copies, [(xr_r,) + adds[0][1:]], full)
            for bits, keep in reversed(trail):
                copies = []
                for mask in range(1, 1 << len(bits)):
                    copies.append(copy(xr_r, keep, xr_r, keep, mate([b for k, b in enumerate(bits) if mask >> k & 1])))
                self.stages.append((copies, [], False))

        def window(self, where):
            row, size, col, cols = where
            return pl.ds(row, size), pl.ds(col, cols)

        def cut(self, where, side):
            row, size, col, cols = where
            if (size // 2) % 16 == 0:
                return aligned(row + side * (size // 2), 16), size // 2, col, cols
            return row, size, aligned(col + side * (cols // 2), 128), cols // 2

        def landing(self, at, parts_here):
            row, rows_one, cols_one = self.slot
            full = self.place[3]
            if cols_one == full:
                return row + at * rows_one, parts_here * rows_one, 0, full
            if parts_here == 1:
                return row + at // 2 * rows_one, rows_one, at % 2 * cols_one, cols_one
            return row + at // 2 * rows_one, parts_here // 2 * rows_one, 0, full

        def small_place(self):
            row, rows_one, cols_one = self.slot
            if cols_one == self.place[3]:
                return row // 7, rows_one, 0, cols_one
            k = (self.place[0] - base_a) // quarter
            return units // 8 + k // 2 * rows_one, rows_one, k % 2 * cols_one, cols_one

        def begin(self, copies):
            for copy in copies:
                copy.start()
            self.sent += copies

        def ready(self, j):
            if self.first:
                self.stage = 0
                self.begin([self.stages[0][0][j]])
            elif j == 1:
                self.stage = 0
                self.begin(self.stages[0][0])

        def add(self, into, base, where, terms):
            row, size, col, cols = where
            step = 64 if size % 64 == 0 else 48 if size % 48 == 0 else 32

            def body(off):
                to = (pl.ds(aligned(row + off, 16), step), pl.ds(col, cols))
                parts_in = [ref[pl.ds(aligned(r + off, 16), step), pl.ds(c, cols)] for ref, (r, _, c, _) in terms]
                if len(parts_in) == 1:
                    into[to] = base[to] + parts_in[0]
                else:
                    into[to] = sum((v.astype(F32) for v in parts_in), base[to].astype(F32)).astype(BF16)

            if inside_loop:
                for off in range(0, size, step):
                    body(off)
            else:
                loop(size, step, body)

        def advance(self):
            if self.finished or self.stage < 0:
                return
            copies, adds, full = self.stages[self.stage]
            for copy in copies:
                copy.wait_recv()
            if full:
                for copy in copies:
                    copy.wait_send()
                self.sent = [c for c in self.sent if all(c is not d for d in copies)]
            for item in adds:
                self.add(*item)
            self.stage += 1
            if self.stage < len(self.stages):
                self.begin(self.stages[self.stage][0])
                return
            self.finished = True
            to_write.append(self)

    chunks = []
    refs = (own, oth, xr, land, land_both, rx)
    for i in range(parts):
        slot = (i * 7 * (BLOCK // 8), BLOCK // 8, width)
        to = g2_h.at[pl.ds(i * BLOCK, BLOCK)]
        chunks.append(Region(2 * i, i * BLOCK, BLOCK, width, slot, ORDERS[2 * i], refs, to))
        refs_one = tuple(ref.at[i] for ref in (own1, oth1, xr1, land1, land1_both)) + ([ref.at[i] for ref in rx1],)
        to = g1_h.at[:, pl.ds(i * BLOCK, BLOCK)]
        chunks.append(Region(2 * i + 1, 0, width, BLOCK, (0, width // 8, BLOCK), ORDERS[2 * i + 1], refs_one, to))
    for i in range(4):
        slot = (7 * units // 8 + i * quarter, quarter // 4, width // 2)
        to = go_h if i == 0 else gq_h.at[i - 1]
        chunks.append(Region(2 * parts + i, base_a + i * quarter, quarter, width, slot, ORDERS[2 * parts + i], refs, to))
    first_att = 2 * parts

    class Small:
        def __init__(self, tile, index, everywhere, paired, groups):
            self.tile, self.everywhere, self.paired = tile, everywhere, paired
            landings = [near.at[3 * index + k] for k in range(3)] + [far.at[(7 + len(full_bits)) * index + k] for k in range(7 + len(full_bits))]
            sems = iter(range(index * len(landings), (index + 1) * len(landings)))
            landings = iter(landings)

            def stage(devices):
                places = [next(landings) for _ in devices]
                return places, [described(tile, dst, ssem, next(sems), d) for dst, d in zip(places, devices)]

            self.stages = [stage([sib, across, facing])]
            for bits in groups + [(b,) for b in full_bits]:
                masks = range(1, 1 << len(bits))
                self.stages.append(stage([mate([b for k, b in enumerate(bits) if mask >> k & 1]) for mask in masks]))
            self.stage, self.finished = -1, False

        def start(self):
            self.stage = 0
            for copy in self.stages[0][1]:
                copy.start()

        def advance(self):
            if self.finished or self.stage < 0:
                return
            places, copies = self.stages[self.stage]
            for copy in copies:
                copy.wait()
            tile = self.tile
            if self.stage == 0:
                beside, over, facing_ = places
                n, p = self.everywhere, self.paired
                tile[0:n] = (tile[0:n] + beside[0:n]) + (over[0:n] + facing_[0:n])
                tile[n : n + p] = tile[n : n + p] + over[n + p : n + 2 * p]
            else:
                got = [tile[...]] + [place[...] for place in places]
                while len(got) > 1:
                    got = [got[k] + got[k + 1] for k in range(0, len(got), 2)]
                tile[...] = got[0]
            self.stage += 1
            if self.stage == len(self.stages):
                self.finished = True
                return
            for copy in self.stages[self.stage][1]:
                copy.start()

    first_small = Small(early, 0, 4, 1, [(b,) for b in half_bits])
    last_small = Small(late, 1, 2, 2, [tuple(half_bits)])

    def ready(i, j):
        chunks[i].ready(j)

    to_write = []

    def write_finished():
        while to_write:
            region = to_write.pop()
            region.done = local(region.xr.at[region.window(region.place)], region.to)

    def hook(name):
        pass_on(name)
        for i in PLAN.get(name, ()):
            (chunks + [last_small, first_small])[i].advance()
            if not inside_loop:
                write_finished()

    def chunk_rows(j, i, at):
        span = pl.ds(at, BLOCK)
        cols = slice(j * units + i * BLOCK, j * units + (i + 1) * BLOCK)
        mine = slice(i * BLOCK, (i + 1) * BLOCK)
        bias = (bias_u if j == 0 else uoth)[mine].reshape(1, BLOCK)
        h = dot(n2_s[span], w1_s[j, i]) + bias
        a, slope = gelu_pair(h)
        a_s[span, cols] = a.astype(BF16)
        g = (dot_nt(cot_s[span], w2_s[j, mine]) * slope).astype(BF16)
        g_s[span, cols] = g

    def chunk_grads(j, i):
        cols = slice(j * units + i * BLOCK, j * units + (i + 1) * BLOCK)
        mine = slice(i * BLOCK, (i + 1) * BLOCK)
        to = oth if j == 1 else own

        def second(at):
            to[pl.ds(i * BLOCK + at, 128)] = dot_tn(a_s[:, pl.ds(cols.start + at, 128)], cot_s[...]).astype(BF16)

        loop(BLOCK, 128, second)
        ready(2 * i, j)
        g = g_s[:, cols]

        def first(at):
            (oth1 if j == 1 else own1)[i, pl.ds(at, BLOCK)] = dot(n2t_s[pl.ds(at, BLOCK)], g_s[:, cols]).astype(BF16)

        loop(width, BLOCK, first)
        ready(2 * i + 1, j)
        early[4 + j : 5 + j, mine] = column_sum(g.astype(F32))
        hook(f"f{j}{i}")

    def feed(j, i, first=False):
        if first:
            loop(count, BLOCK, lambda at: chunk_rows(j, i, at))
            hook(f"r{j}{i}.0")
            cot_copy.wait_recv()

            def received(at):
                n2_half(at).wait_recv()
                chunk_rows(j, i, count + at)

            loop(count, BLOCK, received)
            hook(f"r{j}{i}.1")

            def turned(at):
                n2t_s[:, pl.ds(at, BLOCK)] = n2_s[pl.ds(at, BLOCK)].T

            loop(rows, BLOCK, turned)
        else:
            loop(rows, BLOCK, lambda at: chunk_rows(j, i, at), service(f"r{j}{i}.", hook), 2)
        chunk_grads(j, i)

    early[...] = jnp.zeros_like(early)
    late[...] = jnp.zeros_like(late)

    def sum_cot(at):
        early[3:4] += column_sum(cot_s[pl.ds(at, 128)].astype(F32))

    loop(count, 128, sum_cot)
    unit_copy.wait_recv()
    for i in range(parts):
        have_weight(4 + 2 * i, 5 + 2 * i)
        feed(1, i, first=i == 0)
        feed(0, i)

    def back_two(at):
        span = pl.ds(at, BLOCK)
        total = None
        for j in range(2):
            for i in range(parts):
                at_col = j * units + i * BLOCK
                term = dot_nt(g_s[span, at_col : at_col + BLOCK], w1_s[j, i])
                total = term if total is None else total + term
        return total

    def mlp_part(at):
        span = pl.ds(at, BLOCK)
        return dot(a_s[span, :units], w2_s[0]) + dot(a_s[span, units:], w2_s[1])

    def gn2_half(at):
        return half_copy(sb2.at[pl.ds(at, BLOCK)], rb2.at[pl.ds(at, BLOCK)], 6, at)

    def dm_half(at):
        return half_copy(n2_s.at[pl.ds(at, BLOCK)], n2_s.at[pl.ds(aligned(count + at, BLOCK), BLOCK)], 10, at)

    def back_two_sib(at):
        sb2[pl.ds(at, BLOCK)] = back_two(count + at).astype(BF16)
        gn2_half(at).start()

    def back_two_mine(at):
        gm_s[pl.ds(at, BLOCK)] = back_two(at)

    def mlp_sib(at):
        sb1[pl.ds(at, BLOCK)] = mlp_part(count + at).astype(BF16)

    loop(count, BLOCK, back_two_sib)
    hook("g0")
    loop(count, BLOCK, back_two_mine)
    hook("gn2")

    def second_back(at):
        gn2_half(at).wait_recv()
        n2_half(at).wait_send()
        for off in range(0, BLOCK, 128):
            spot = pl.ds(aligned(at + off, 128), 128)
            xhat, sigma = norm_stats(mid_s[spot])
            grad = gm_s[spot] + rb2[spot].astype(F32)
            cot = cot_s[spot].astype(F32)
            back = cot + norm_back(grad, ln2_gain, xhat, sigma)
            gm_s[spot] = back
            n2_s[spot] = back.astype(BF16)
            early[0:1] += column_sum(back)
            early[1:2] += column_sum(grad * xhat)
            early[2:3] += column_sum(grad)
        dm_half(at).start()

    loop(count, BLOCK, second_back)
    hook("lb")
    for at in range(0, count, BLOCK):
        att_half(at).wait_send()
    loop(count, BLOCK, mlp_sib)
    mlp_copy = remote(sb1, rb1, csem, 8, sib)
    first_small.start()
    hook("ln2")

    for at in range(0, count, BLOCK):
        dm_half(at).wait_recv()

    start = base_a + quarter
    zero = jnp.zeros((count, 128), BF16)
    grad_s = dq_s = ou_s
    n1_copy.wait_send()

    def keep_gradient(j, c):
        to = oth if j == 1 else own
        low = start + c * quarter
        dt = ot_s.at[j * quarter : (j + 1) * quarter]

        def columns(at):
            to[low : low + quarter, pl.ds(at, BLOCK)] = dot(dt[...], nr_s[:, pl.ds(at, BLOCK)]).astype(BF16)

        loop(width, BLOCK, columns)
        ready(first_att + 1 + c, j)
        if c != 1:
            d = g_s[:, (3 * j + c) * BLOCK : (3 * j + c) * BLOCK + quarter]
            late[2 + c // 2 + 2 * j : 3 + c // 2 + 2 * j, :quarter] = column_sum(d.astype(F32))

    def values_back(j):
        base = j * quarter
        to = oth if j == 1 else own

        def weight(at):
            to[base_a : base_a + quarter, pl.ds(at, BLOCK)] = dot(ou_s[base : base + quarter], n2_s[:, pl.ds(at, BLOCK)]).astype(BF16)

        loop(width, BLOCK, weight)
        ready(first_att, j)

        def output(at):
            grad_s[base : base + quarter, pl.ds(at, BLOCK)] = dot_nt(wo_s[base : base + quarter], n2_s[pl.ds(at, BLOCK)]).astype(BF16)

        loop(rows, BLOCK, output)
        hook(f"w{j}.0")
        go_s = n1_s.at[:, 256 * j : 256 * (j + 1)]

        def scale(at):
            here = pl.ds(at, BLOCK)
            grad_t = dot_nt(grad_s[base : base + quarter], roll_s[here])
            for head in range(heads):
                row = j * heads + head
                r = r_s[row : row + 1, here]
                g = grad_t[head * HEAD : (head + 1) * HEAD]
                at_head = slice(base + head * HEAD, base + (head + 1) * HEAD)
                in_s[row : row + 1, here] = column_sum(g * ot_s[at_head, here].astype(F32)) * r
                gt_s[at_head, here] = (g * r).astype(BF16)
            go_s[here, :quarter] = gt_s[base : base + quarter, here].T

        loop(rows, BLOCK, scale)

        def block(at):
            here = pl.ds(at, count)
            b = at // count
            dv = [None, None]
            for head in range(heads):
                tile = head // 2
                gh = jnp.where(lane_half(count, head % 2 == 1), go_s[here, 128 * tile : 128 * tile + 128], zero)
                part = dot(e_s[j * heads + head, b], gh)
                dv[tile] = part if dv[tile] is None else dv[tile] + part
            dv = jnp.concatenate(dv, axis=1)[:, :quarter].astype(BF16)
            g_s[here, (3 * j + 2) * BLOCK : (3 * j + 2) * BLOCK + quarter] = dv
            ot_s[base : base + quarter, here] = dv.T

        loop(rows, count, block)
        hook(f"w{j}.1")
        keep_gradient(j, 2)
        hook(f"v{j}")

    def scores_back(j):
        base = j * quarter

        def block(at):
            here = pl.ds(at, count)
            b = at // count
            dk = [None, None]
            for head in range(heads):
                tile = head // 2
                row = j * heads + head
                half = lane_half(count, head % 2 == 1)
                lanes = slice(128 * tile, 128 * tile + 128)
                vh = jnp.where(half, v_s[j, here, lanes], zero)
                qh = jnp.where(half, q_s[j, here, lanes], zero)
                last_row = min(128 * tile + 128, quarter)
                vh = vh[:, : last_row - 128 * tile]
                ds = n2t_s.at[:count, head * count : (head + 1) * count] if head < 2 else ds_s
                for off in range(0, count, BLOCK):
                    some = pl.ds(aligned(at + off, BLOCK), BLOCK)
                    dp_t = dot(vh, gt_s[base + 128 * tile : base + last_row, some])
                    grad = (dp_t - in_s[row : row + 1, some]).astype(BF16)
                    ds[:, off : off + BLOCK] = grad * e_s[row, b, :, off : off + BLOCK]
                part = dot(ds[...], qh)
                dk[tile] = part if dk[tile] is None else dk[tile] + part
                kth = kt_s[base + head * HEAD : base + head * HEAD + HEAD, here]
                dq_s[base + head * HEAD : base + head * HEAD + HEAD, here] = dot(kth, ds[...]).astype(BF16)
            dk = jnp.concatenate(dk, axis=1)[:, :quarter].astype(BF16)
            g_s[here, (3 * j + 1) * BLOCK : (3 * j + 1) * BLOCK + quarter] = dk
            ot_s[base : base + quarter, here] = dk.T
            g_s[here, 3 * j * BLOCK : 3 * j * BLOCK + quarter] = dq_s[base : base + quarter, here].T

        loop(rows, count, block, service(f"b{j}.", hook))
        keep_gradient(j, 1)
        hook(f"k{j}")
        ot_s[base : base + quarter] = dq_s[base : base + quarter]
        keep_gradient(j, 0)
        hook(f"s{j}")

    values_back(1)
    scores_back(1)
    values_back(0)
    scores_back(0)

    def finish_out(at):
        span = pl.ds(at, BLOCK)
        mid_s[span] = mid_s[span] + mlp_part(at) + fc2_bias

    loop(count, BLOCK, finish_out)
    hook("fo")
    mlp_copy.wait_recv()

    def write_out(at):
        spot = pl.ds(at, 128)
        tok_s[spot] = (mid_s[spot] + rb1[spot].astype(F32)).astype(BF16)

    loop(count, 128, write_out)
    put_out = local(tok_s, out_h)
    hook("fin")

    def back_one(at):
        total = None
        for j in range(2):
            for c in range(3):
                d = g_s[pl.ds(at, BLOCK), (3 * j + c) * BLOCK : (3 * j + c) * BLOCK + quarter]
                term = dot(d, wq_s[j, c])
                total = term if total is None else total + term
        n2_s[pl.ds(at, BLOCK)] = total.astype(BF16)

    for at in range(0, count, BLOCK):
        dm_half(at).wait_send()
    loop(rows, BLOCK, back_one, service("d.", hook), 2)
    for at in range(0, count, BLOCK):
        gn2_half(at).wait_send()

    def gn1_half(at):
        return half_copy(sb2.at[pl.ds(at, BLOCK)], rb2.at[pl.ds(at, BLOCK)], 12, at)

    def back_one_sib(at):
        sb2[pl.ds(at, BLOCK)] = dot(back_s[pl.ds(count + at, BLOCK)], n2_s[...]).astype(BF16)
        gn1_half(at).start()

    def back_one_mine(at):
        mid_s[pl.ds(at, BLOCK)] = dot(back_s[pl.ds(at, BLOCK)], n2_s[...])

    loop(count, BLOCK, back_one_sib)
    loop(count, BLOCK, back_one_mine)
    hook("e.0")
    mlp_copy.wait_send()

    def first_back(at):
        gn1_half(at).wait_recv()
        for off in range(0, BLOCK, 128):
            spot = pl.ds(aligned(at + off, 128), 128)
            xhat, sigma = norm_stats(sin_s[spot])
            grad = mid_s[spot] + rb2[spot].astype(F32)
            sb1[spot] = (gm_s[spot] + norm_back(grad, ln1_gain, xhat, sigma)).astype(BF16)
            late[0:1] += column_sum(grad * xhat)
            late[1:2] += column_sum(grad)

    loop(count, BLOCK, first_back)
    put_in = local(sb1, ing_h)
    last_small.start()
    hook("e.1")
    hook("tail")
    left = [first_small, last_small] + chunks
    while left:
        for item in left:
            item.advance()
            write_finished()
        left = [item for item in left if not item.finished]

    for row, source, at in ((0, late, 0), (1, late, 1), (2, early, 0), (3, early, 1), (4, early, 2), (5, early, 3), (8, early, 4), (9, late, 2), (10, late, 3)):
        small_o[row : row + 1] = source[at : at + 1]

    passed = [copy for item in pieces for copy in item.copies]
    for copy in [unit_copy, head_copy, cot_copy] + [gn1_half(at) for at in range(0, count, BLOCK)] + passed:
        copy.wait_send()
    for chunk in chunks:
        for copy in chunk.sent:
            copy.wait_send()
        chunk.done.wait()
    put_out.wait()
    put_in.wait()


def copies_of(full):
    most = 0
    for kind in ORDERS:
        first, after = KINDS[kind]
        most = max(most, 1 + full + 2 * sum((1 << len(bits)) - 1 for bits in after) + (0 if first is None else 3))
    return most


def call_layer(dp_size, tokens, cotangent, ids, vectors, wq, wo, w1, w2):
    count, width = tokens.shape
    rows = 2 * count
    quarter = wo.shape[0]
    units = w1.shape[1]
    heads = quarter // HEAD
    grad_rows = units + 4 * quarter
    parts = units // BLOCK
    bits = [b for b in range(20) if (1 << b) < dp_size]
    half_bits = bits[:3]
    shape = jax.ShapeDtypeStruct
    vm = pltpu.VMEM
    regions = 2 * (units // BLOCK) + 4
    steps = copies_of(len(bits) - len(half_bits))
    fetched = 4 + 2 * (units // BLOCK)
    scratch = (
        [vm((count, width), BF16), vm((rows, width), BF16)]
        + [vm((count, width), F32)] * 3
        + [vm((rows, width), BF16)] * 2
        + [vm((width, rows), BF16)]
        + [vm((2,) + wq.shape, BF16), vm((2 * quarter, width), BF16), vm((2, units // BLOCK, width, BLOCK), BF16), vm((2,) + w2.shape, BF16)]
        + [vm((2, rows, 256), BF16)] * 2
        + [vm((2 * quarter, rows), BF16)] * 4
        + [vm((8, rows), F32)] * 2
        + [vm((2 * heads, 2, count, count), BF16)]
        + [vm((rows, rows), BF16)] * 2
        + [vm((rows, width), BF16), vm((count, count), BF16)]
        + [vm((rows, 2 * units), BF16)] * 2
        + [vm((count, width), BF16)] * 4
        + [vm((grad_rows, width), BF16)] * 3
        + [vm((7 * units // 8 + 4 * quarter, width), BF16), vm((units // 2, width), BF16)]
        + [vm((parts, width, BLOCK), BF16)] * 3
        + [vm((parts, 7 * width // 8, BLOCK), BF16), vm((parts, width // 2, BLOCK), BF16)]
        + [vm((grad_rows >> len(half_bits), width), BF16)] * (len(bits) - len(half_bits))
        + [vm((parts, width // 8, BLOCK), BF16)] * (len(bits) - len(half_bits))
        + [vm((SIDE, width // 3), F32), vm((units,), F32), vm((2, quarter), F32), vm((8, width), F32), vm((8, width), F32)]
        + [vm((6, 8, width), F32), vm((14 + 2 * (len(bits) - 3), 8, width), F32)]
        + [pltpu.SemaphoreType.DMA((8 + units // BLOCK + regions,))]
        + [pltpu.SemaphoreType.DMA((2, n)) for n in (3 * fetched + 2, 14, regions * steps, 2 * (10 + len(bits) - 3))]
    )
    anywhere = pl.BlockSpec(memory_space=pl.ANY)
    inside = pl.BlockSpec(memory_space=pltpu.VMEM)
    return pl.pallas_call(
        functools.partial(layer, dp_size, half_bits),
        out_shape=[shape((count, width), BF16)] * 2
        + [shape(w2.shape, BF16), shape(w1.shape, BF16), shape(wo.shape, BF16), shape(wq.shape, BF16), shape((16, width), F32)],
        in_specs=[anywhere] * 2 + [inside] * (1 + len(vectors)) + [anywhere] * 4,
        out_specs=[anywhere] * 6 + [inside],
        scratch_shapes=scratch,
        compiler_params=pltpu.CompilerParams(vmem_limit_bytes=VMEM_LIMIT, collective_id=0, has_side_effects=True),
        name="layer",
    )(tokens, cotangent, ids, *vectors, wq, wo, w1, w2)


def finish(*refs):
    sources, small, rest = refs[:6], refs[6], refs[7:]
    results, vectors, rest = rest[:6], rest[6:14], rest[14:]
    narrow, wide, (get, put) = rest[:6], rest[6:10], rest[10:]
    blocks = []
    for k, src in enumerate(sources):
        if src.ndim == 3:
            places = list(range(src.shape[0]))
        else:
            step = min(BLOCK, src.shape[0])
            places = [pl.ds(at, step) for at in range(0, src.shape[0], step)]
        for at in places:
            low = narrow[k].at[at]
            blocks.append((src.at[at], low, low if k < 2 else wide[k - 2].at[at], results[k].at[at]))
    reads = [pltpu.make_async_copy(src, low, get.at[n]) for n, (src, low, _, _) in enumerate(blocks)]
    writes = [pltpu.make_async_copy(high, dst, put.at[n]) for n, (_, _, high, dst) in enumerate(blocks)]
    for copy in reads:
        copy.start()
    for i in range(6):
        vectors[i][...] = small[i]
    vectors[6][...] = small[8, : vectors[6].shape[0]]
    vectors[7][...] = small[9:11, : vectors[7].shape[1]]
    for read, write, (_, low, high, _) in zip(reads, writes, blocks):
        read.wait()
        if high is not low:

            def cast(at, low=low, high=high):
                high[pl.ds(at, 64)] = low[pl.ds(at, 64)].astype(F32)

            loop(low.shape[0], 64, cast)
        write.start()
    for copy in writes:
        copy.wait()


def call_finish(arrays, small, units, quarter):
    width = small.shape[1]
    shape = jax.ShapeDtypeStruct
    extents = [(width,)] * 6 + [(units,), (2, quarter)]
    kinds = [BF16, BF16, F32, F32, F32, F32]
    anywhere = pl.BlockSpec(memory_space=pl.ANY)
    inside = pl.BlockSpec(memory_space=pltpu.VMEM)
    grads = arrays[2:]
    return pl.pallas_call(
        finish,
        in_specs=[anywhere] * len(arrays) + [inside],
        out_specs=[anywhere] * len(arrays) + [inside] * len(extents),
        out_shape=[shape(a.shape, k) for a, k in zip(arrays, kinds)] + [shape(e, F32) for e in extents],
        scratch_shapes=[pltpu.VMEM(a.shape, BF16) for a in arrays]
        + [pltpu.VMEM(a.shape, F32) for a in grads]
        + [pltpu.SemaphoreType.DMA((16,)), pltpu.SemaphoreType.DMA((16,))],
        compiler_params=pltpu.CompilerParams(vmem_limit_bytes=VMEM_LIMIT),
        name="finish",
    )(*arrays, small)


def per_device(
    tokens, segment_ids, ln1_gain, ln1_bias, qkv_weight, qv_bias, out_weight, out_bias,
    ln2_gain, ln2_bias, fc1_weight, fc1_bias, fc2_weight, fc2_bias, cotangent,
):
    vectors = (ln1_gain, ln1_bias, out_bias, ln2_gain, ln2_bias, fc2_bias, fc1_bias, qv_bias)
    *arrays, small = call_layer(
        lax.axis_size("dp"), tokens, cotangent, segment_ids, vectors, qkv_weight.transpose(0, 2, 1), out_weight, fc1_weight, fc2_weight
    )
    out, ing, g2, g1, go, gq, a0, a1, a2, a3, a4, a5, g_units, g_heads = call_finish(arrays, small, fc1_weight.shape[1], out_weight.shape[0])
    return (out, ing, a0, a1, gq.transpose(0, 2, 1), g_heads, go, a2, a3, a4, g1, g_units, g2, a5)


def solution(mesh):
    placed = (
        P(("dp", "tensor"), None),
        P("dp", None),
        P(),
        P(),
        P(None, None, "tensor"),
        P(None, "tensor"),
        P("tensor", None),
        P(),
        P(),
        P(),
        P(None, "tensor"),
        P("tensor"),
        P("tensor", None),
        P(),
        P(("dp", "tensor"), None),
    )
    return jax.shard_map(
        per_device,
        mesh=mesh,
        in_specs=placed,
        out_specs=(
            P(("dp", "tensor"), None),
            P(("dp", "tensor"), None),
            P(),
            P(),
            P(None, None, "tensor"),
            P(None, "tensor"),
            P("tensor", None),
            P(),
            P(),
            P(),
            P(None, "tensor"),
            P("tensor"),
            P("tensor", None),
            P(),
        ),
        check_vma=False,
    )
```

```python
import functools

import jax
import jax.numpy as jnp
from jax import lax
from jax.experimental import pallas as pl
from jax.experimental.pallas import tpu as pltpu
from jax.sharding import PartitionSpec as P

HEAD = 64
SIDE = 16
EPSILON = 1e-06
NEG_LARGE = -1e30
SCALE = HEAD ** (-0.5)
F32 = jnp.float32
BF16 = jnp.bfloat16
VMEM_LIMIT = 64 * 1024 * 1024 - 128 * 1024
MESH = pl.DeviceIdType.MESH
BLOCK = 256
KINDS = {
    "A": (None, ((0,), (1,), (2,))),
    "B": (None, ((1,), (0,), (2,))),
    "D": (None, ((0,), (1, 2))),
    "E": (None, ((0, 1, 2),)),
    "C": (None, ((0, 1), (2,))),
    "Y": (0, ((1,), (2,))),
    "Z": (1, ((0,), (2,))),
    "YD": (0, ((1, 2),)),
    "S": (None, (("p",), ("q",), (2,))),
    "SD": (None, (("p",), ("q", 2))),
    "SF": ("p", (("q",), (2,))),
    "SFD": ("p", (("q", 2),)),
}
ORDERS = ("SFD", "SD", "SF", "SFD", "D", "SF", "D", "SD", "C", "D")
WEIGHT_PLAN = {"p0": (0,), "a0": (1,), "a2": (2,), "p1": (3,), "c0": (4,), "c3": (5,), "n": (6,), "r10.1": (7,), "r00.1": (8,), "r11.0": (9,)}
PLAN = {
    "f01": (0,),
    "r12.0": (1,),
    "r02.0": (2,),
    "r02.1": (0,),
    "f02": (3,),
    "g0": (1,),
    "lb": (4, 0),
    "w1.0": (5, 2, 1, -1),
    "w1.1": (3,),
    "v1": (4, 0),
    "b1.0": (2, -1),
    "b1.1": (1,),
    "s1": (5, 3),
    "w0.0": (6, 0),
    "w0.1": (4, -1, 2, 1),
    "v0": (9, 5),
    "b0.0": (3, 6),
    "b0.1": (4, 9, -1),
    "k0": (8, 2, 3),
    "s0": (7, 5),
    "d.0": (6, 4),
    "d.1": (9,),
    "e.0": (8, 2),
    "e.1": (5, 7),
    "tail": (6, 9, -2, 8, 2, 5, 7, 6, 9, 8, -2, 5, 7, 8, 7),
}


def dot(a, b):
    return jnp.dot(a, b, preferred_element_type=F32)


def dot_nt(a, b):
    return lax.dot_general(a, b, (((1,), (1,)), ((), ())), preferred_element_type=F32)


def dot_tn(a, b):
    return lax.dot_general(a, b, (((0,), (0,)), ((), ())), preferred_element_type=F32)


def lane_half(rows, upper):
    lanes = lax.broadcasted_iota(jnp.int32, (rows, 128), 1)
    return lanes >= HEAD if upper else lanes < HEAD


def head_lanes(ref, head, filler):
    tile = ref[:, 128 * (head // 2) : 128 * (head // 2) + 128]
    return jnp.where(lane_half(tile.shape[0], head % 2 == 1), tile, filler)


def gelu_pair(h):
    cdf = 0.5 + 0.5 * lax.erf(h * 0.7071067811865476)
    return h * cdf, cdf + h * jnp.exp(-0.5 * h * h) * 0.3989422804014327


def norm_stats(v):
    centred = v - jnp.mean(v, axis=-1, keepdims=True)
    sigma = lax.rsqrt(jnp.mean(centred * centred, axis=-1, keepdims=True) + EPSILON)
    return centred * sigma, sigma


def norm_back(grad, gain, xhat, sigma):
    g = grad * gain
    return sigma * (g - jnp.mean(g, axis=-1, keepdims=True) - xhat * jnp.mean(g * xhat, axis=-1, keepdims=True))


def column_sum(v):
    return jnp.sum(v, axis=0, keepdims=True)


def aligned(v, unit):
    return v if isinstance(v, int) else pl.multiple_of(v, unit)


def loop(count, step, body, service=None, every=1):
    def run(i, carry):
        body(aligned(i * step, step))
        if service is not None:
            for k in range(count // step // every):
                if service(k, True):
                    pl.when(i == every * (k + 1) - 1)(functools.partial(service, k, False))
        return carry

    lax.fori_loop(0, count // step, run, 0)


def layer(
    dp_size, half_bits,
    tok_h, cot_h, ids, table, gain1, bias1, bias_o, gain2, bias2, bias_f, bias_u, bias_qv, wq_h, wo_h, w1_h, w2_h,
    out_h, ing_h, g2_h, g1_h, go_h, gq_h, small_o,
    tok_s, cot_s, sin_s, mid_s, gm_s, n1_s, n2_s, n2t_s, wq_s, wo_s, w1_s, w2_s,
    q_s, v_s, kt_s, ot_s, ou_s, gt_s, r_s, in_s, e_s, roll_s, back_s, nr_s, ds_s, a_s, g_s, sb1, sb2, rb1, rb2,
    own, oth, xr, land, land_both, own1, oth1, xr1, land1, land1_both, *rest,
):
    rest = list(rest)
    full_bits = [b for b in range(20) if (1 << b) < dp_size and b not in half_bits]
    rx = [rest.pop(0) for _ in full_bits]
    rx1 = [rest.pop(0) for _ in full_bits]
    uoth, voth, early, late, near, far, lsem, wsem, csem, gsem, ssem = rest

    count, width = tok_s.shape
    rows = 2 * count
    quarter = wo_h.shape[0]
    units = w1_h.shape[1]
    heads = quarter // HEAD
    place = lax.axis_index("tensor")
    dp = lax.axis_index("dp")
    chip = place // 2
    core = place % 2
    sib = {"tensor": chip * 2 + 1 - core}
    across = {"tensor": (1 - chip) * 2 + core}
    facing = {"tensor": (1 - chip) * 2 + 1 - core}
    all_bits = list(half_bits) + full_bits
    sides = {b: (dp // (1 << b)) % 2 for b in all_bits}

    ways = {b: (1 - 2 * sides[b]) * (1 << b) for b in all_bits}
    sides["p"] = sides[0] + (sides[1] - sides[0]) * core
    sides["q"] = sides[1] + (sides[0] - sides[1]) * core
    ways["p"] = ways[0] + (ways[1] - ways[0]) * core
    ways["q"] = ways[1] + (ways[0] - ways[1]) * core

    def mate(bits):
        return {"dp": dp + sum(ways[b] for b in bits)}

    def described(src, dst, sems, index, device):
        return pltpu.make_async_remote_copy(
            src_ref=src, dst_ref=dst, send_sem=sems.at[0, index], recv_sem=sems.at[1, index], device_id=device, device_id_type=MESH
        )

    mates = {b: mate((b,)) for b in all_bits}
    groups = {(b,) for b in full_bits}
    for mask in range(1, 1 << len(half_bits)):
        groups.add(tuple(b for k, b in enumerate(half_bits) if mask >> k & 1))

    barrier = pltpu.get_barrier_semaphore()
    partners = [sib, across, facing] + [mate(bits) for bits in sorted(groups)]
    for partner in partners:
        pl.semaphore_signal(barrier, inc=1, device_id=partner, device_id_type=MESH)

    sq_s, sk_s, k_s = a_s.at[:, 0:128], a_s.at[:, 128:256], a_s.at[:, 256:512]
    local_used = [0]

    def local(src, dst):
        copy = pltpu.make_async_copy(src, dst, lsem.at[local_used[0]])
        local_used[0] += 1
        copy.start()
        return copy

    def remote(src, dst, sems, index, device):
        copy = pltpu.make_async_remote_copy(
            src_ref=src, dst_ref=dst, send_sem=sems.at[0, index], recv_sem=sems.at[1, index], device_id=device, device_id_type=MESH
        )
        copy.start()
        return copy

    def half_copy(src, dst, first, at):
        return pltpu.make_async_remote_copy(
            src_ref=src,
            dst_ref=dst,
            send_sem=csem.at[0, first + at // BLOCK],
            recv_sem=csem.at[1, first + at // BLOCK],
            device_id=sib,
            device_id_type=MESH,
        )

    get_wq = local(wq_h, wq_s.at[0])
    get_tok = local(tok_h, tok_s)
    get_cot = local(cot_h, cot_s.at[pl.ds(0, count)])
    get_wo = local(wo_h, wo_s.at[pl.ds(0, quarter)])
    get_w1 = [local(w1_h.at[:, pl.ds(i * BLOCK, BLOCK)], w1_s.at[0, i]) for i in range(units // BLOCK)]
    get_w2 = local(w2_h, w2_s.at[0])

    part = (sides[0] + sides[1]) % 2

    class Piece:
        def __init__(self, index, refs, at, extent):
            size = extent // 4

            def some(k, first, size):
                return refs[k].at[pl.ds(aligned(at[k] + part * (extent // 2) + first, 16), size)]

            self.copies = [described(some(0, 0, 2 * size), some(1, 0, 2 * size), wsem, 3 * index, across)]
            for k in range(2):
                block = some(1, k * size, size)
                self.copies.append(described(block, block, wsem, 3 * index + 1 + k, mates[k]))
            self.stage = 0

        def advance(self):
            if self.stage == 0:
                self.copies[0].wait_recv()
                self.copies[1].start()
                self.copies[2].start()
            else:
                self.copies[1].wait_recv()
                self.copies[2].wait_recv()
            self.stage += 1

    pieces = [Piece(c, (wq_s.at[0, c], wq_s.at[1, c]), (0, 0), quarter) for c in range(3)]
    pieces.append(Piece(3, (wo_s, wo_s), (0, quarter), quarter))
    for i in range(units // BLOCK):
        pieces.append(Piece(4 + 2 * i, (w1_s.at[0, i], w1_s.at[1, i]), (0, 0), width))
        pieces.append(Piece(5 + 2 * i, (w2_s.at[0], w2_s.at[1]), (i * BLOCK, i * BLOCK), BLOCK))
    pl.semaphore_wait(barrier, len(partners))
    unit_copy = remote(bias_u, uoth, wsem, 3 * len(pieces), across)
    head_copy = remote(bias_qv, voth, wsem, 3 * len(pieces) + 1, across)
    get_wq.wait()
    get_wo.wait()
    for item in pieces[:4]:
        item.copies[0].start()

    inside_loop = []

    def service(name, act):
        def at_point(k, ask):
            full = f"{name}{k}"
            if ask:
                return full in PLAN or full in WEIGHT_PLAN
            inside_loop.append(full)
            act(full)
            inside_loop.pop()

        return at_point

    def pass_on(name):
        for i in WEIGHT_PLAN.get(name, ()):
            if pieces[i].stage < 1:
                pieces[i].advance()

    def have_weight(*which):
        for i in which:
            while pieces[i].stage < 2:
                pieces[i].advance()

    ln1_gain, ln1_bias, out_bias, ln2_gain, ln2_bias, fc2_bias = (
        ref[...].reshape(1, width) for ref in (gain1, bias1, bias_o, gain2, bias2, bias_f)
    )
    get_tok.wait()

    def first_norm(at):
        plane = core * (count // (SIDE * SIDE)) + at // (SIDE * SIDE)
        line = (at // SIDE) % SIDE
        shape = (SIDE, width // 3)
        for k in range(4):
            spot = jnp.concatenate(
                [jnp.broadcast_to(table[pl.ds(plane, 1)], shape), jnp.broadcast_to(table[pl.ds(line + k, 1)], shape), table[...]], axis=1
            )
            span = pl.ds(aligned(at + k * SIDE, SIDE), SIDE)
            stream = tok_s[span].astype(F32) + spot
            sin_s[span] = stream
            xhat, _ = norm_stats(stream)
            n1_s[span] = (xhat * ln1_gain + ln1_bias).astype(BF16)

    loop(count, 4 * SIDE, first_norm)
    doc = ids[pl.ds(chip, 1), :]
    starts = [jnp.zeros((1, 1), F32)]
    starts += [jnp.sum(jnp.where(doc < v, 1.0, 0.0), axis=1, keepdims=True) for v in range(1, 4)]
    starts.append(jnp.full((1, 1), rows, F32))
    turn = jnp.zeros((1, 1), F32)
    for v in range(4):
        turn += jnp.where(starts[v + 1] - starts[v] == count, starts[v], 0.0)
    turn_here = turn - (core * count).astype(F32)

    def wrapped(v):
        v = jnp.where(v >= rows, v - rows, v)
        return jnp.where(v < 0, v + rows, v)

    def rotations(at):
        down = (lax.broadcasted_iota(jnp.int32, (64, rows), 0) + at).astype(F32)
        along = lax.broadcasted_iota(jnp.int32, (64, rows), 1).astype(F32)
        roll_s[pl.ds(at, 64)] = jnp.where(wrapped(down + turn_here) == along, 1.0, 0.0).astype(BF16)
        back_s[pl.ds(at, 64)] = jnp.where(wrapped(down - turn_here) == along, 1.0, 0.0).astype(BF16)
        where = wrapped((lax.broadcasted_iota(jnp.int32, (64, 128), 0) + at).astype(F32) + turn)
        mine = sum(jnp.where(where >= starts[v], 1.0, 0.0) for v in range(1, 4))
        slot = (lax.broadcasted_iota(jnp.int32, (64, 128), 1) % HEAD).astype(F32)
        sq_s[pl.ds(at, 64)] = jnp.where((slot < 4) & (slot != mine), 1.0, 0.0).astype(BF16)
        sk_s[pl.ds(at, 64)] = jnp.where(slot == mine, NEG_LARGE, 0.0).astype(BF16)


    for copy in get_w1:
        copy.wait()
    get_w2.wait()
    for item in pieces[4:]:
        item.copies[0].start()
    n1_copy = remote(n1_s.at[pl.ds(0, count)], n1_s.at[pl.ds(count, count)], csem, 0, sib)
    get_cot.wait()
    cot_copy = remote(cot_s.at[pl.ds(0, count)], cot_s.at[pl.ds(count, count)], csem, 1, sib)

    def rotate(at):
        nr_s[pl.ds(at, BLOCK)] = dot(roll_s[pl.ds(at, BLOCK)], n1_s[...]).astype(BF16)

    def project(j, at):
        n = nr_s[pl.ds(at, BLOCK)]
        biases = bias_qv if j == 0 else voth
        q = (dot_nt(n, wq_s[j, 0]) + biases[0:1]).astype(BF16) * SCALE
        k = dot_nt(n, wq_s[j, 1]).astype(BF16)
        v = (dot_nt(n, wq_s[j, 2]) + biases[1:2]).astype(BF16)
        q_s[j, pl.ds(at, BLOCK), :quarter] = q
        k_s[pl.ds(at, BLOCK), :quarter] = k
        v_s[j, pl.ds(at, BLOCK), :quarter] = v
        kt_s[j * quarter : (j + 1) * quarter, pl.ds(at, BLOCK)] = k.T * SCALE

    blocks = [(b, at) for b in range(2) for at in range(0, count, BLOCK)]

    def attend(j):
        for head in range(heads):
            at = 512 + 256 * head
            a_s[:, at : at + 128] = head_lanes(q_s.at[j], head, sq_s[...])
            a_s[:, at + 128 : at + 256] = head_lanes(k_s, head, sk_s[...])
        for at in range(0, rows, BLOCK):
            ou_s[:quarter, at : at + BLOCK] = v_s[j, at : at + BLOCK, :quarter].T

        def tile(here):
            b = here // count
            at = aligned(here % count, BLOCK)
            keys = pl.ds(aligned(b * count, count), count)
            for head in range(heads):
                column = 512 + 256 * head
                s = dot_nt(a_s[keys, column + 128 : column + 256], a_s[pl.ds(here, BLOCK), column : column + 128])
                m = jnp.max(s, axis=0, keepdims=True)
                e = jnp.exp(s - m)
                r = 1.0 / column_sum(e)
                low = e.astype(BF16)
                span = slice(head * HEAD, head * HEAD + HEAD)
                to = slice(j * quarter + head * HEAD, j * quarter + head * HEAD + HEAD)
                e_s[j * heads + head, b, :, pl.ds(at, BLOCK)] = low
                ot_s[to, pl.ds(here, BLOCK)] = (dot(ou_s[span, keys], low) * r).astype(BF16)
                r_s[j * heads + head : j * heads + head + 1, pl.ds(here, BLOCK)] = r

        return tile

    loop(rows, 64, rotations)
    n1_copy.wait_recv()
    loop(rows, BLOCK, rotate)
    loop(rows, BLOCK, lambda at: project(0, at))
    pass_on("p0")
    loop(rows, BLOCK, attend(0), service("a", pass_on))
    head_copy.wait_recv()
    have_weight(0, 1, 2)
    loop(rows, BLOCK, lambda at: project(1, at))
    pass_on("p1")
    loop(rows, BLOCK, attend(1), service("c", pass_on))

    have_weight(3)

    def unrotate(at):
        ou_s[:, pl.ds(at, BLOCK)] = dot(ot_s[...], roll_s[:, pl.ds(at, BLOCK)]).astype(BF16)

    loop(rows, BLOCK, unrotate)
    pass_on("u")

    def out_part(at):
        return dot_tn(ou_s[:, pl.ds(at, BLOCK)], wo_s[...])

    def att_half(at):
        return half_copy(sb1.at[pl.ds(at, BLOCK)], rb1.at[pl.ds(at, BLOCK)], 2, at)

    def n2_half(at):
        return half_copy(n2_s.at[pl.ds(at, BLOCK)], n2_s.at[pl.ds(aligned(count + at, BLOCK), BLOCK)], 4, at)

    def out_sib(at):
        sb1[pl.ds(at, BLOCK)] = out_part(count + at).astype(BF16)
        att_half(at).start()

    loop(count, BLOCK, out_sib)

    def out_mine(at):
        mid_s[pl.ds(at, BLOCK)] = sin_s[pl.ds(at, BLOCK)] + out_part(at) + out_bias

    loop(count, BLOCK, out_mine)
    pass_on("o")

    def second_norm(at):
        att_half(at).wait_recv()
        for off in range(0, BLOCK, 128):
            spot = pl.ds(aligned(at + off, 128), 128)
            mid = mid_s[spot] + rb1[spot].astype(F32)
            mid_s[spot] = mid
            xhat, _ = norm_stats(mid)
            n2_s[spot] = (xhat * ln2_gain + ln2_bias).astype(BF16)
        n2_half(at).start()

    loop(count, BLOCK, second_norm)
    pass_on("n")

    base_a = units
    parts = units // BLOCK
    steps = copies_of(len(full_bits))

    class Region:
        def __init__(self, index, row, size, cols, slot, kind, refs, to):
            own_r, oth_r, xr_r, land_r, both_r, rx_r = refs
            self.place, self.slot, self.to, self.xr = (row, size, 0, cols), slot, to, xr_r
            first, after = KINDS[kind]
            self.first = first is not None
            self.stages, self.stage, self.finished, self.sent = [], -1, False, []
            now, parts, used, trail = self.place, 8, 0, []
            sems = iter(range(index * steps, (index + 1) * steps))

            def copy(src, src_at, dst, dst_at, device):
                return described(src.at[self.window(src_at)], dst.at[self.window(dst_at)], gsem, next(sems), device)

            def piece(bits, mask):
                where = now
                for k, b in enumerate(bits):
                    where = self.cut(where, 1 - sides[b] if mask >> k & 1 else sides[b])
                return where

            sums = 1 + len(after) + len(full_bits)
            if self.first:
                keep, give, there = piece((first,), 0), piece((first,), 1), (row // 2, size // 2, 0, cols)
                place = self.landing(0, 4)
                copies = [copy(own_r, give, land_r, place, mate((first,))), copy(oth_r, give, both_r, there, mate((first,)))]
                adds = [(own_r, own_r, keep, [(land_r, place)]), (oth_r, oth_r, keep, [(both_r, there)])]
                self.stages.append((copies, adds, False))
                trail.append(((first,), keep))
                now, parts, used = keep, 4, 4
            self.stages.append(([copy(oth_r, now, xr_r, now, across)], [(own_r, own_r, now, [(xr_r, now)])], False))
            for bits in after:
                parts >>= len(bits)
                keep, copies, terms = piece(bits, 0), [], []
                for mask in range(1, 1 << len(bits)):
                    place = self.landing(used, parts)
                    used += parts
                    terms.append((land_r, place))
                    copies.append(copy(own_r, piece(bits, mask), land_r, place, mate([b for k, b in enumerate(bits) if mask >> k & 1])))
                self.stages.append((copies, [(own_r, own_r, keep, terms)], False))
                trail.append((bits, keep))
                now = keep
            for i, b in enumerate(full_bits):
                place = self.small_place()
                self.stages.append(([copy(own_r, now, rx_r[i], place, mates[b])], [(own_r, own_r, now, [(rx_r[i], place)])], True))
            copies, adds, full = self.stages[-1]
            self.stages[-1] = (copies, [(xr_r,) + adds[0][1:]], full)
            for bits, keep in reversed(trail):
                copies = []
                for mask in range(1, 1 << len(bits)):
                    copies.append(copy(xr_r, keep, xr_r, keep, mate([b for k, b in enumerate(bits) if mask >> k & 1])))
                self.stages.append((copies, [], False))

        def window(self, where):
            row, size, col, cols = where
            return pl.ds(row, size), pl.ds(col, cols)

        def cut(self, where, side):
            row, size, col, cols = where
            if (size // 2) % 16 == 0:
                return aligned(row + side * (size // 2), 16), size // 2, col, cols
            return row, size, aligned(col + side * (cols // 2), 128), cols // 2

        def landing(self, at, parts_here):
            row, rows_one, cols_one = self.slot
            full = self.place[3]
            if cols_one == full:
                return row + at * rows_one, parts_here * rows_one, 0, full
            if parts_here == 1:
                return row + at // 2 * rows_one, rows_one, at % 2 * cols_one, cols_one
            return row + at // 2 * rows_one, parts_here // 2 * rows_one, 0, full

        def small_place(self):
            row, rows_one, cols_one = self.slot
            if cols_one == self.place[3]:
                return row // 7, rows_one, 0, cols_one
            k = (self.place[0] - base_a) // quarter
            return units // 8 + k // 2 * rows_one, rows_one, k % 2 * cols_one, cols_one

        def begin(self, copies):
            for copy in copies:
                copy.start()
            self.sent += copies

        def ready(self, j):
            if self.first:
                self.stage = 0
                self.begin([self.stages[0][0][j]])
            elif j == 1:
                self.stage = 0
                self.begin(self.stages[0][0])

        def add(self, into, base, where, terms):
            row, size, col, cols = where
            step = 64 if size % 64 == 0 else 48 if size % 48 == 0 else 32

            def body(off):
                to = (pl.ds(aligned(row + off, 16), step), pl.ds(col, cols))
                parts_in = [ref[pl.ds(aligned(r + off, 16), step), pl.ds(c, cols)] for ref, (r, _, c, _) in terms]
                if len(parts_in) == 1:
                    into[to] = base[to] + parts_in[0]
                else:
                    into[to] = sum((v.astype(F32) for v in parts_in), base[to].astype(F32)).astype(BF16)

            if inside_loop:
                for off in range(0, size, step):
                    body(off)
            else:
                loop(size, step, body)

        def advance(self):
            if self.finished or self.stage < 0:
                return
            copies, adds, full = self.stages[self.stage]
            for copy in copies:
                copy.wait_recv()
            if full:
                for copy in copies:
                    copy.wait_send()
                self.sent = [c for c in self.sent if all(c is not d for d in copies)]
            for item in adds:
                self.add(*item)
            self.stage += 1
            if self.stage < len(self.stages):
                self.begin(self.stages[self.stage][0])
                return
            self.finished = True
            to_write.append(self)

    chunks = []
    refs = (own, oth, xr, land, land_both, rx)
    for i in range(parts):
        slot = (i * 7 * (BLOCK // 8), BLOCK // 8, width)
        to = g2_h.at[pl.ds(i * BLOCK, BLOCK)]
        chunks.append(Region(2 * i, i * BLOCK, BLOCK, width, slot, ORDERS[2 * i], refs, to))
        refs_one = tuple(ref.at[i] for ref in (own1, oth1, xr1, land1, land1_both)) + ([ref.at[i] for ref in rx1],)
        to = g1_h.at[:, pl.ds(i * BLOCK, BLOCK)]
        chunks.append(Region(2 * i + 1, 0, width, BLOCK, (0, width // 8, BLOCK), ORDERS[2 * i + 1], refs_one, to))
    for i in range(4):
        slot = (7 * units // 8 + i * quarter, quarter // 4, width // 2)
        to = go_h if i == 0 else gq_h.at[i - 1]
        chunks.append(Region(2 * parts + i, base_a + i * quarter, quarter, width, slot, ORDERS[2 * parts + i], refs, to))
    first_att = 2 * parts

    class Small:
        def __init__(self, tile, index, everywhere, paired, groups):
            self.tile, self.everywhere, self.paired = tile, everywhere, paired
            landings = [near.at[3 * index + k] for k in range(3)] + [far.at[(7 + len(full_bits)) * index + k] for k in range(7 + len(full_bits))]
            sems = iter(range(index * len(landings), (index + 1) * len(landings)))
            landings = iter(landings)

            def stage(devices):
                places = [next(landings) for _ in devices]
                return places, [described(tile, dst, ssem, next(sems), d) for dst, d in zip(places, devices)]

            self.stages = [stage([sib, across, facing])]
            for bits in groups + [(b,) for b in full_bits]:
                masks = range(1, 1 << len(bits))
                self.stages.append(stage([mate([b for k, b in enumerate(bits) if mask >> k & 1]) for mask in masks]))
            self.stage, self.finished = -1, False

        def start(self):
            self.stage = 0
            for copy in self.stages[0][1]:
                copy.start()

        def advance(self):
            if self.finished or self.stage < 0:
                return
            places, copies = self.stages[self.stage]
            for copy in copies:
                copy.wait()
            tile = self.tile
            if self.stage == 0:
                beside, over, facing_ = places
                n, p = self.everywhere, self.paired
                tile[0:n] = (tile[0:n] + beside[0:n]) + (over[0:n] + facing_[0:n])
                tile[n : n + p] = tile[n : n + p] + over[n + p : n + 2 * p]
            else:
                got = [tile[...]] + [place[...] for place in places]
                while len(got) > 1:
                    got = [got[k] + got[k + 1] for k in range(0, len(got), 2)]
                tile[...] = got[0]
            self.stage += 1
            if self.stage == len(self.stages):
                self.finished = True
                return
            for copy in self.stages[self.stage][1]:
                copy.start()

    first_small = Small(early, 0, 4, 1, [(b,) for b in half_bits])
    last_small = Small(late, 1, 2, 2, [tuple(half_bits)])

    def ready(i, j):
        chunks[i].ready(j)

    to_write = []

    def write_finished():
        while to_write:
            region = to_write.pop()
            region.done = local(region.xr.at[region.window(region.place)], region.to)

    def hook(name):
        pass_on(name)
        for i in PLAN.get(name, ()):
            (chunks + [last_small, first_small])[i].advance()
            if not inside_loop:
                write_finished()

    def chunk_rows(j, i, at):
        span = pl.ds(at, BLOCK)
        cols = slice(j * units + i * BLOCK, j * units + (i + 1) * BLOCK)
        mine = slice(i * BLOCK, (i + 1) * BLOCK)
        bias = (bias_u if j == 0 else uoth)[mine].reshape(1, BLOCK)
        h = dot(n2_s[span], w1_s[j, i]) + bias
        a, slope = gelu_pair(h)
        a_s[span, cols] = a.astype(BF16)
        g = (dot_nt(cot_s[span], w2_s[j, mine]) * slope).astype(BF16)
        g_s[span, cols] = g

    def chunk_grads(j, i):
        cols = slice(j * units + i * BLOCK, j * units + (i + 1) * BLOCK)
        mine = slice(i * BLOCK, (i + 1) * BLOCK)
        to = oth if j == 1 else own

        def second(at):
            to[pl.ds(i * BLOCK + at, 128)] = dot_tn(a_s[:, pl.ds(cols.start + at, 128)], cot_s[...]).astype(BF16)

        loop(BLOCK, 128, second)
        ready(2 * i, j)
        g = g_s[:, cols]

        def first(at):
            (oth1 if j == 1 else own1)[i, pl.ds(at, BLOCK)] = dot(n2t_s[pl.ds(at, BLOCK)], g_s[:, cols]).astype(BF16)

        loop(width, BLOCK, first)
        ready(2 * i + 1, j)
        early[4 + j : 5 + j, mine] = column_sum(g.astype(F32))
        hook(f"f{j}{i}")

    def feed(j, i, first=False):
        if first:
            loop(count, BLOCK, lambda at: chunk_rows(j, i, at))
            hook(f"r{j}{i}.0")
            cot_copy.wait_recv()

            def received(at):
                n2_half(at).wait_recv()
                chunk_rows(j, i, count + at)

            loop(count, BLOCK, received)
            hook(f"r{j}{i}.1")

            def turned(at):
                n2t_s[:, pl.ds(at, BLOCK)] = n2_s[pl.ds(at, BLOCK)].T

            loop(rows, BLOCK, turned)
        else:
            loop(rows, BLOCK, lambda at: chunk_rows(j, i, at), service(f"r{j}{i}.", hook), 2)
        chunk_grads(j, i)

    early[...] = jnp.zeros_like(early)
    late[...] = jnp.zeros_like(late)
    unit_copy.wait_recv()
    for i in range(parts):
        have_weight(4 + 2 * i, 5 + 2 * i)
        feed(1, i, first=i == 0)
        feed(0, i)

    def back_two(at):
        span = pl.ds(at, BLOCK)
        total = None
        for j in range(2):
            for i in range(parts):
                at_col = j * units + i * BLOCK
                term = dot_nt(g_s[span, at_col : at_col + BLOCK], w1_s[j, i])
                total = term if total is None else total + term
        return total

    def mlp_part(at):
        span = pl.ds(at, BLOCK)
        return dot(a_s[span, :units], w2_s[0]) + dot(a_s[span, units:], w2_s[1])

    def gn2_half(at):
        return half_copy(sb2.at[pl.ds(at, BLOCK)], rb2.at[pl.ds(at, BLOCK)], 6, at)

    def dm_half(at):
        return half_copy(n2_s.at[pl.ds(at, BLOCK)], n2_s.at[pl.ds(aligned(count + at, BLOCK), BLOCK)], 10, at)

    def back_two_sib(at):
        sb2[pl.ds(at, BLOCK)] = back_two(count + at).astype(BF16)
        gn2_half(at).start()

    def back_two_mine(at):
        gm_s[pl.ds(at, BLOCK)] = back_two(at)

    def mlp_sib(at):
        sb1[pl.ds(at, BLOCK)] = mlp_part(count + at).astype(BF16)

    loop(count, BLOCK, back_two_sib)
    hook("g0")
    loop(count, BLOCK, back_two_mine)
    hook("gn2")

    def second_back(at):
        gn2_half(at).wait_recv()
        n2_half(at).wait_send()
        for off in range(0, BLOCK, 128):
            spot = pl.ds(aligned(at + off, 128), 128)
            xhat, sigma = norm_stats(mid_s[spot])
            grad = gm_s[spot] + rb2[spot].astype(F32)
            cot = cot_s[spot].astype(F32)
            back = cot + norm_back(grad, ln2_gain, xhat, sigma)
            gm_s[spot] = back
            n2_s[spot] = back.astype(BF16)
            early[0:1] += column_sum(back)
            early[1:2] += column_sum(grad * xhat)
            early[2:3] += column_sum(grad)
            early[3:4] += column_sum(cot)
        dm_half(at).start()

    loop(count, BLOCK, second_back)
    hook("lb")
    for at in range(0, count, BLOCK):
        att_half(at).wait_send()
    loop(count, BLOCK, mlp_sib)
    mlp_copy = remote(sb1, rb1, csem, 8, sib)
    first_small.start()
    hook("ln2")

    for at in range(0, count, BLOCK):
        dm_half(at).wait_recv()

    start = base_a + quarter
    zero = jnp.zeros((count, 128), BF16)
    grad_s = dq_s = ou_s
    n1_copy.wait_send()

    def keep_gradient(j, c):
        to = oth if j == 1 else own
        low = start + c * quarter
        dt = ot_s.at[j * quarter : (j + 1) * quarter]

        def columns(at):
            to[low : low + quarter, pl.ds(at, BLOCK)] = dot(dt[...], nr_s[:, pl.ds(at, BLOCK)]).astype(BF16)

        loop(width, BLOCK, columns)
        ready(first_att + 1 + c, j)
        if c != 1:
            d = g_s[:, (3 * j + c) * BLOCK : (3 * j + c) * BLOCK + quarter]
            late[2 + c // 2 + 2 * j : 3 + c // 2 + 2 * j, :quarter] = column_sum(d.astype(F32))

    def values_back(j):
        base = j * quarter
        to = oth if j == 1 else own

        def weight(at):
            to[base_a : base_a + quarter, pl.ds(at, BLOCK)] = dot(ou_s[base : base + quarter], n2_s[:, pl.ds(at, BLOCK)]).astype(BF16)

        loop(width, BLOCK, weight)
        ready(first_att, j)

        def output(at):
            grad_s[base : base + quarter, pl.ds(at, BLOCK)] = dot_nt(wo_s[base : base + quarter], n2_s[pl.ds(at, BLOCK)]).astype(BF16)

        loop(rows, BLOCK, output)
        hook(f"w{j}.0")
        go_s = n1_s.at[:, 256 * j : 256 * (j + 1)]

        def scale(at):
            here = pl.ds(at, BLOCK)
            grad_t = dot_nt(grad_s[base : base + quarter], roll_s[here])
            for head in range(heads):
                row = j * heads + head
                r = r_s[row : row + 1, here]
                g = grad_t[head * HEAD : (head + 1) * HEAD]
                at_head = slice(base + head * HEAD, base + (head + 1) * HEAD)
                in_s[row : row + 1, here] = column_sum(g * ot_s[at_head, here].astype(F32)) * r
                gt_s[at_head, here] = (g * r).astype(BF16)
            go_s[here, :quarter] = gt_s[base : base + quarter, here].T

        loop(rows, BLOCK, scale)

        def block(at):
            here = pl.ds(at, count)
            b = at // count
            dv = [None, None]
            for head in range(heads):
                tile = head // 2
                gh = jnp.where(lane_half(count, head % 2 == 1), go_s[here, 128 * tile : 128 * tile + 128], zero)
                part = dot(e_s[j * heads + head, b], gh)
                dv[tile] = part if dv[tile] is None else dv[tile] + part
            dv = jnp.concatenate(dv, axis=1)[:, :quarter].astype(BF16)
            g_s[here, (3 * j + 2) * BLOCK : (3 * j + 2) * BLOCK + quarter] = dv
            ot_s[base : base + quarter, here] = dv.T

        loop(rows, count, block)
        hook(f"w{j}.1")
        keep_gradient(j, 2)
        hook(f"v{j}")

    def scores_back(j):
        base = j * quarter

        def block(at):
            here = pl.ds(at, count)
            b = at // count
            dk = [None, None]
            for head in range(heads):
                tile = head // 2
                row = j * heads + head
                half = lane_half(count, head % 2 == 1)
                lanes = slice(128 * tile, 128 * tile + 128)
                vh = jnp.where(half, v_s[j, here, lanes], zero)
                qh = jnp.where(half, q_s[j, here, lanes], zero)
                last_row = min(128 * tile + 128, quarter)
                vh = vh[:, : last_row - 128 * tile]
                ds = n2t_s.at[:count, head * count : (head + 1) * count] if head < 2 else ds_s
                for off in range(0, count, BLOCK):
                    some = pl.ds(aligned(at + off, BLOCK), BLOCK)
                    dp_t = dot(vh, gt_s[base + 128 * tile : base + last_row, some])
                    grad = (dp_t - in_s[row : row + 1, some]).astype(BF16)
                    ds[:, off : off + BLOCK] = grad * e_s[row, b, :, off : off + BLOCK]
                part = dot(ds[...], qh)
                dk[tile] = part if dk[tile] is None else dk[tile] + part
                kth = kt_s[base + head * HEAD : base + head * HEAD + HEAD, here]
                dq_s[base + head * HEAD : base + head * HEAD + HEAD, here] = dot(kth, ds[...]).astype(BF16)
            dk = jnp.concatenate(dk, axis=1)[:, :quarter].astype(BF16)
            g_s[here, (3 * j + 1) * BLOCK : (3 * j + 1) * BLOCK + quarter] = dk
            ot_s[base : base + quarter, here] = dk.T
            g_s[here, 3 * j * BLOCK : 3 * j * BLOCK + quarter] = dq_s[base : base + quarter, here].T

        loop(rows, count, block, service(f"b{j}.", hook))
        keep_gradient(j, 1)
        hook(f"k{j}")
        ot_s[base : base + quarter] = dq_s[base : base + quarter]
        keep_gradient(j, 0)
        hook(f"s{j}")

    values_back(1)
    scores_back(1)
    values_back(0)
    scores_back(0)

    def finish_out(at):
        span = pl.ds(at, BLOCK)
        mid_s[span] = mid_s[span] + mlp_part(at) + fc2_bias

    loop(count, BLOCK, finish_out)
    hook("fo")
    mlp_copy.wait_recv()

    def write_out(at):
        spot = pl.ds(at, 128)
        tok_s[spot] = (mid_s[spot] + rb1[spot].astype(F32)).astype(BF16)

    loop(count, 128, write_out)
    put_out = local(tok_s, out_h)
    hook("fin")

    def back_one(at):
        total = None
        for j in range(2):
            for c in range(3):
                d = g_s[pl.ds(at, BLOCK), (3 * j + c) * BLOCK : (3 * j + c) * BLOCK + quarter]
                term = dot(d, wq_s[j, c])
                total = term if total is None else total + term
        n2_s[pl.ds(at, BLOCK)] = total.astype(BF16)

    for at in range(0, count, BLOCK):
        dm_half(at).wait_send()
    loop(rows, BLOCK, back_one, service("d.", hook), 2)
    for at in range(0, count, BLOCK):
        gn2_half(at).wait_send()

    def gn1_half(at):
        return half_copy(sb2.at[pl.ds(at, BLOCK)], rb2.at[pl.ds(at, BLOCK)], 12, at)

    def back_one_sib(at):
        sb2[pl.ds(at, BLOCK)] = dot(back_s[pl.ds(count + at, BLOCK)], n2_s[...]).astype(BF16)
        gn1_half(at).start()

    def back_one_mine(at):
        mid_s[pl.ds(at, BLOCK)] = dot(back_s[pl.ds(at, BLOCK)], n2_s[...])

    loop(count, BLOCK, back_one_sib)
    loop(count, BLOCK, back_one_mine)
    hook("e.0")
    mlp_copy.wait_send()

    def first_back(at):
        gn1_half(at).wait_recv()
        for off in range(0, BLOCK, 128):
            spot = pl.ds(aligned(at + off, 128), 128)
            xhat, sigma = norm_stats(sin_s[spot])
            grad = mid_s[spot] + rb2[spot].astype(F32)
            sb1[spot] = (gm_s[spot] + norm_back(grad, ln1_gain, xhat, sigma)).astype(BF16)
            late[0:1] += column_sum(grad * xhat)
            late[1:2] += column_sum(grad)

    loop(count, BLOCK, first_back)
    put_in = local(sb1, ing_h)
    last_small.start()
    hook("e.1")
    hook("tail")
    left = [first_small, last_small] + chunks
    while left:
        for item in left:
            item.advance()
            write_finished()
        left = [item for item in left if not item.finished]

    for row, source, at in ((0, late, 0), (1, late, 1), (2, early, 0), (3, early, 1), (4, early, 2), (5, early, 3), (8, early, 4), (9, late, 2), (10, late, 3)):
        small_o[row : row + 1] = source[at : at + 1]

    passed = [copy for item in pieces for copy in item.copies]
    for copy in [unit_copy, head_copy, cot_copy] + [gn1_half(at) for at in range(0, count, BLOCK)] + passed:
        copy.wait_send()
    for chunk in chunks:
        for copy in chunk.sent:
            copy.wait_send()
        chunk.done.wait()
    put_out.wait()
    put_in.wait()


def copies_of(full):
    most = 0
    for kind in ORDERS:
        first, after = KINDS[kind]
        most = max(most, 1 + full + 2 * sum((1 << len(bits)) - 1 for bits in after) + (0 if first is None else 3))
    return most


def call_layer(dp_size, tokens, cotangent, ids, table, vectors, wq, wo, w1, w2):
    count, width = tokens.shape
    rows = 2 * count
    quarter = wo.shape[0]
    units = w1.shape[1]
    heads = quarter // HEAD
    grad_rows = units + 4 * quarter
    parts = units // BLOCK
    bits = [b for b in range(20) if (1 << b) < dp_size]
    half_bits = bits[:3]
    shape = jax.ShapeDtypeStruct
    vm = pltpu.VMEM
    regions = 2 * (units // BLOCK) + 4
    steps = copies_of(len(bits) - len(half_bits))
    fetched = 4 + 2 * (units // BLOCK)
    scratch = (
        [vm((count, width), BF16), vm((rows, width), BF16)]
        + [vm((count, width), F32)] * 3
        + [vm((rows, width), BF16)] * 2
        + [vm((width, rows), BF16)]
        + [vm((2,) + wq.shape, BF16), vm((2 * quarter, width), BF16), vm((2, units // BLOCK, width, BLOCK), BF16), vm((2,) + w2.shape, BF16)]
        + [vm((2, rows, 256), BF16)] * 2
        + [vm((2 * quarter, rows), BF16)] * 4
        + [vm((8, rows), F32)] * 2
        + [vm((2 * heads, 2, count, count), BF16)]
        + [vm((rows, rows), BF16)] * 2
        + [vm((rows, width), BF16), vm((count, count), BF16)]
        + [vm((rows, 2 * units), BF16)] * 2
        + [vm((count, width), BF16)] * 4
        + [vm((grad_rows, width), BF16)] * 3
        + [vm((7 * units // 8 + 4 * quarter, width), BF16), vm((units // 2, width), BF16)]
        + [vm((parts, width, BLOCK), BF16)] * 3
        + [vm((parts, 7 * width // 8, BLOCK), BF16), vm((parts, width // 2, BLOCK), BF16)]
        + [vm((grad_rows >> len(half_bits), width), BF16)] * (len(bits) - len(half_bits))
        + [vm((parts, width // 8, BLOCK), BF16)] * (len(bits) - len(half_bits))
        + [vm((units,), F32), vm((2, quarter), F32), vm((8, width), F32), vm((8, width), F32)]
        + [vm((6, 8, width), F32), vm((14 + 2 * (len(bits) - 3), 8, width), F32)]
        + [pltpu.SemaphoreType.DMA((8 + units // BLOCK + regions,))]
        + [pltpu.SemaphoreType.DMA((2, n)) for n in (3 * fetched + 2, 14, regions * steps, 2 * (10 + len(bits) - 3))]
    )
    anywhere = pl.BlockSpec(memory_space=pl.ANY)
    inside = pl.BlockSpec(memory_space=pltpu.VMEM)
    return pl.pallas_call(
        functools.partial(layer, dp_size, half_bits),
        out_shape=[shape((count, width), BF16)] * 2
        + [shape(w2.shape, BF16), shape(w1.shape, BF16), shape(wo.shape, BF16), shape(wq.shape, BF16), shape((16, width), F32)],
        in_specs=[anywhere] * 2 + [inside] * (2 + len(vectors)) + [anywhere] * 4,
        out_specs=[anywhere] * 6 + [inside],
        scratch_shapes=scratch,
        compiler_params=pltpu.CompilerParams(vmem_limit_bytes=VMEM_LIMIT, collective_id=0, has_side_effects=True),
        name="layer",
    )(tokens, cotangent, ids, table, *vectors, wq, wo, w1, w2)


def finish(*refs):
    sources, small, rest = refs[:6], refs[6], refs[7:]
    results, vectors, rest = rest[:6], rest[6:14], rest[14:]
    narrow, wide, (get, put) = rest[:6], rest[6:10], rest[10:]
    blocks = []
    for k, src in enumerate(sources):
        if src.ndim == 3:
            places = list(range(src.shape[0]))
        else:
            step = min(BLOCK, src.shape[0])
            places = [pl.ds(at, step) for at in range(0, src.shape[0], step)]
        for at in places:
            low = narrow[k].at[at]
            blocks.append((src.at[at], low, low if k < 2 else wide[k - 2].at[at], results[k].at[at]))
    reads = [pltpu.make_async_copy(src, low, get.at[n]) for n, (src, low, _, _) in enumerate(blocks)]
    writes = [pltpu.make_async_copy(high, dst, put.at[n]) for n, (_, _, high, dst) in enumerate(blocks)]
    for copy in reads:
        copy.start()
    for i in range(6):
        vectors[i][...] = small[i]
    vectors[6][...] = small[8, : vectors[6].shape[0]]
    vectors[7][...] = small[9:11, : vectors[7].shape[1]]
    for read, write, (_, low, high, _) in zip(reads, writes, blocks):
        read.wait()
        if high is not low:

            def cast(at, low=low, high=high):
                high[pl.ds(at, 64)] = low[pl.ds(at, 64)].astype(F32)

            loop(low.shape[0], 64, cast)
        write.start()
    for copy in writes:
        copy.wait()


def call_finish(arrays, small, units, quarter):
    width = small.shape[1]
    shape = jax.ShapeDtypeStruct
    extents = [(width,)] * 6 + [(units,), (2, quarter)]
    kinds = [BF16, BF16, F32, F32, F32, F32]
    anywhere = pl.BlockSpec(memory_space=pl.ANY)
    inside = pl.BlockSpec(memory_space=pltpu.VMEM)
    grads = arrays[2:]
    return pl.pallas_call(
        finish,
        in_specs=[anywhere] * len(arrays) + [inside],
        out_specs=[anywhere] * len(arrays) + [inside] * len(extents),
        out_shape=[shape(a.shape, k) for a, k in zip(arrays, kinds)] + [shape(e, F32) for e in extents],
        scratch_shapes=[pltpu.VMEM(a.shape, BF16) for a in arrays]
        + [pltpu.VMEM(a.shape, F32) for a in grads]
        + [pltpu.SemaphoreType.DMA((16,)), pltpu.SemaphoreType.DMA((16,))],
        compiler_params=pltpu.CompilerParams(vmem_limit_bytes=VMEM_LIMIT),
        name="finish",
    )(*arrays, small)


def per_device(
    tokens, segment_ids, ln1_gain, ln1_bias, qkv_weight, qv_bias, out_weight, out_bias,
    ln2_gain, ln2_bias, fc1_weight, fc1_bias, fc2_weight, fc2_bias, cotangent,
):
    width = tokens.shape[1]
    freq_count = width // 6
    frequency = 10000.0 ** (-jnp.arange(freq_count, dtype=F32) / freq_count)
    angles = jnp.arange(SIDE, dtype=F32)[:, None] * frequency[None, :]
    table = jnp.concatenate([jnp.sin(angles), jnp.cos(angles)], axis=1)
    vectors = (ln1_gain, ln1_bias, out_bias, ln2_gain, ln2_bias, fc2_bias, fc1_bias, qv_bias)
    *arrays, small = call_layer(
        lax.axis_size("dp"), tokens, cotangent, segment_ids, table, vectors, qkv_weight.transpose(0, 2, 1), out_weight, fc1_weight, fc2_weight
    )
    out, ing, g2, g1, go, gq, a0, a1, a2, a3, a4, a5, g_units, g_heads = call_finish(arrays, small, fc1_weight.shape[1], out_weight.shape[0])
    return (out, ing, a0, a1, gq.transpose(0, 2, 1), g_heads, go, a2, a3, a4, g1, g_units, g2, a5)


def solution(mesh):
    placed = (
        P(("dp", "tensor"), None),
        P("dp", None),
        P(),
        P(),
        P(None, None, "tensor"),
        P(None, "tensor"),
        P("tensor", None),
        P(),
        P(),
        P(),
        P(None, "tensor"),
        P("tensor"),
        P("tensor", None),
        P(),
        P(("dp", "tensor"), None),
    )
    return jax.shard_map(
        per_device,
        mesh=mesh,
        in_specs=placed,
        out_specs=(
            P(("dp", "tensor"), None),
            P(("dp", "tensor"), None),
            P(),
            P(),
            P(None, None, "tensor"),
            P(None, "tensor"),
            P("tensor", None),
            P(),
            P(),
            P(),
            P(None, "tensor"),
            P("tensor"),
            P("tensor", None),
            P(),
        ),
        check_vma=False,
    )
```

```python
import functools

import jax
import jax.numpy as jnp
from jax import lax
from jax.experimental import pallas as pl
from jax.experimental.pallas import tpu as pltpu
from jax.sharding import PartitionSpec as P

HEAD = 64
SIDE = 16
EPSILON = 1e-06
NEG_LARGE = -1e30
SCALE = HEAD ** (-0.5)
F32 = jnp.float32
BF16 = jnp.bfloat16
VMEM_LIMIT = 64 * 1024 * 1024 - 128 * 1024
MESH = pl.DeviceIdType.MESH
BLOCK = 256
KINDS = {
    "A": (None, ((0,), (1,), (2,))),
    "B": (None, ((1,), (0,), (2,))),
    "D": (None, ((0,), (1, 2))),
    "E": (None, ((0, 1, 2),)),
    "C": (None, ((0, 1), (2,))),
    "Y": (0, ((1,), (2,))),
    "Z": (1, ((0,), (2,))),
    "YD": (0, ((1, 2),)),
    "S": (None, (("p",), ("q",), (2,))),
    "SD": (None, (("p",), ("q", 2))),
    "SF": ("p", (("q",), (2,))),
    "SFD": ("p", (("q", 2),)),
}
ORDERS = ("D", "YD", "Z", "D", "Y", "A", "D", "D", "C", "B")
WEIGHT_PLAN = {"p0": (0,), "a0": (1,), "a2": (2,), "p1": (3,), "c0": (4,), "c3": (5,), "n": (6,), "r10.1": (7,), "r00.1": (8,), "r11.1": (9,)}
PLAN = {
    "r12.0": (0, 1),
    "r02.0": (3, 2),
    "f02": (0, 1),
    "lb": (3,),
    "w1.0": (5, 0),
    "w1.1": (-1, 2, 4, 1),
    "b1.0": (3, 5, -1),
    "b1.1": (2, 0, 4),
    "w0.0": (6, 1, 5, -1),
    "v0": (9, 3, 0, 4, 2),
    "b0.0": (5, 6, -1),
    "b0.1": (9, 1, 4),
    "k0": (8, 2),
    "s0": (7, 5, 3),
    "fin": (9, 6),
    "d.0": (4, 8),
    "d.1": (2, 5),
    "e.0": (9,),
    "e.1": (7, 6, 4),
    "tail": (8, 5, -2, 2, 9, 6, 7, 8, 4, -2, 9, 7, 8, 9, 7),
}


def dot(a, b):
    return jnp.dot(a, b, preferred_element_type=F32)


def dot_nt(a, b):
    return lax.dot_general(a, b, (((1,), (1,)), ((), ())), preferred_element_type=F32)


def dot_tn(a, b):
    return lax.dot_general(a, b, (((0,), (0,)), ((), ())), preferred_element_type=F32)


def lane_half(rows, upper):
    lanes = lax.broadcasted_iota(jnp.int32, (rows, 128), 1)
    return lanes >= HEAD if upper else lanes < HEAD


def head_lanes(ref, head, filler):
    tile = ref[:, 128 * (head // 2) : 128 * (head // 2) + 128]
    return jnp.where(lane_half(tile.shape[0], head % 2 == 1), tile, filler)


def gelu_pair(h):
    cdf = 0.5 + 0.5 * lax.erf(h * 0.7071067811865476)
    return h * cdf, cdf + h * jnp.exp(-0.5 * h * h) * 0.3989422804014327


def norm_stats(v):
    centred = v - jnp.mean(v, axis=-1, keepdims=True)
    sigma = lax.rsqrt(jnp.mean(centred * centred, axis=-1, keepdims=True) + EPSILON)
    return centred * sigma, sigma


def norm_back(grad, gain, xhat, sigma):
    g = grad * gain
    return sigma * (g - jnp.mean(g, axis=-1, keepdims=True) - xhat * jnp.mean(g * xhat, axis=-1, keepdims=True))


def column_sum(v):
    return jnp.sum(v, axis=0, keepdims=True)


def aligned(v, unit):
    return v if isinstance(v, int) else pl.multiple_of(v, unit)


def loop(count, step, body, service=None, every=1):
    def run(i, carry):
        body(aligned(i * step, step))
        if service is not None:
            for k in range(count // step // every):
                if service(k, True):
                    pl.when(i == every * (k + 1) - 1)(functools.partial(service, k, False))
        return carry

    lax.fori_loop(0, count // step, run, 0)


def layer(
    dp_size, half_bits,
    tok_h, cot_h, ids, table, gain1, bias1, bias_o, gain2, bias2, bias_f, bias_u, bias_qv, wq_h, wo_h, w1_h, w2_h,
    out_h, ing_h, g2_h, g1_h, go_h, gq_h, small_o,
    tok_s, cot_s, sin_s, mid_s, gm_s, n1_s, n2_s, n2t_s, wq_s, wo_s, w1_s, w2_s,
    q_s, v_s, kt_s, ot_s, ou_s, gt_s, r_s, in_s, e_s, roll_s, back_s, nr_s, ds_s, a_s, g_s, sb1, sb2, rb1, rb2,
    own, oth, xr, land, land_both, own1, oth1, xr1, land1, land1_both, *rest,
):
    rest = list(rest)
    full_bits = [b for b in range(20) if (1 << b) < dp_size and b not in half_bits]
    rx = [rest.pop(0) for _ in full_bits]
    rx1 = [rest.pop(0) for _ in full_bits]
    uoth, voth, early, late, near, far, lsem, wsem, csem, gsem, ssem = rest

    count, width = tok_s.shape
    rows = 2 * count
    quarter = wo_h.shape[0]
    units = w1_h.shape[1]
    heads = quarter // HEAD
    place = lax.axis_index("tensor")
    dp = lax.axis_index("dp")
    chip = place // 2
    core = place % 2
    sib = {"tensor": chip * 2 + 1 - core}
    across = {"tensor": (1 - chip) * 2 + core}
    facing = {"tensor": (1 - chip) * 2 + 1 - core}
    all_bits = list(half_bits) + full_bits
    sides = {b: (dp // (1 << b)) % 2 for b in all_bits}

    ways = {b: (1 - 2 * sides[b]) * (1 << b) for b in all_bits}
    sides["p"] = sides[0] + (sides[1] - sides[0]) * core
    sides["q"] = sides[1] + (sides[0] - sides[1]) * core
    ways["p"] = ways[0] + (ways[1] - ways[0]) * core
    ways["q"] = ways[1] + (ways[0] - ways[1]) * core

    def mate(bits):
        return {"dp": dp + sum(ways[b] for b in bits)}

    def described(src, dst, sems, index, device):
        return pltpu.make_async_remote_copy(
            src_ref=src, dst_ref=dst, send_sem=sems.at[0, index], recv_sem=sems.at[1, index], device_id=device, device_id_type=MESH
        )

    mates = {b: mate((b,)) for b in all_bits}
    groups = {(b,) for b in full_bits}
    for mask in range(1, 1 << len(half_bits)):
        groups.add(tuple(b for k, b in enumerate(half_bits) if mask >> k & 1))

    barrier = pltpu.get_barrier_semaphore()
    partners = [sib, across, facing] + [mate(bits) for bits in sorted(groups)]
    for partner in partners:
        pl.semaphore_signal(barrier, inc=1, device_id=partner, device_id_type=MESH)

    sq_s, sk_s, k_s = a_s.at[:, 0:128], a_s.at[:, 128:256], a_s.at[:, 256:512]
    local_used = [0]

    def local(src, dst):
        copy = pltpu.make_async_copy(src, dst, lsem.at[local_used[0]])
        local_used[0] += 1
        copy.start()
        return copy

    def remote(src, dst, sems, index, device):
        copy = pltpu.make_async_remote_copy(
            src_ref=src, dst_ref=dst, send_sem=sems.at[0, index], recv_sem=sems.at[1, index], device_id=device, device_id_type=MESH
        )
        copy.start()
        return copy

    def half_copy(src, dst, first, at):
        return pltpu.make_async_remote_copy(
            src_ref=src,
            dst_ref=dst,
            send_sem=csem.at[0, first + at // BLOCK],
            recv_sem=csem.at[1, first + at // BLOCK],
            device_id=sib,
            device_id_type=MESH,
        )

    get_wq = local(wq_h, wq_s.at[0])
    get_tok = local(tok_h, tok_s)
    get_cot = local(cot_h, cot_s.at[pl.ds(0, count)])
    get_wo = local(wo_h, wo_s.at[pl.ds(0, quarter)])
    get_w1 = [local(w1_h.at[:, pl.ds(i * BLOCK, BLOCK)], w1_s.at[0, i]) for i in range(units // BLOCK)]
    get_w2 = local(w2_h, w2_s.at[0])

    part = (sides[0] + sides[1]) % 2

    class Piece:
        def __init__(self, index, refs, at, extent):
            size = extent // 4

            def some(k, first, size):
                return refs[k].at[pl.ds(aligned(at[k] + part * (extent // 2) + first, 16), size)]

            self.copies = [described(some(0, 0, 2 * size), some(1, 0, 2 * size), wsem, 3 * index, across)]
            for k in range(2):
                block = some(1, k * size, size)
                self.copies.append(described(block, block, wsem, 3 * index + 1 + k, mates[k]))
            self.stage = 0

        def advance(self):
            if self.stage == 0:
                self.copies[0].wait_recv()
                self.copies[1].start()
                self.copies[2].start()
            else:
                self.copies[1].wait_recv()
                self.copies[2].wait_recv()
            self.stage += 1

    pieces = [Piece(c, (wq_s.at[0, c], wq_s.at[1, c]), (0, 0), quarter) for c in range(3)]
    pieces.append(Piece(3, (wo_s, wo_s), (0, quarter), quarter))
    for i in range(units // BLOCK):
        pieces.append(Piece(4 + 2 * i, (w1_s.at[0, i], w1_s.at[1, i]), (0, 0), width))
        pieces.append(Piece(5 + 2 * i, (w2_s.at[0], w2_s.at[1]), (i * BLOCK, i * BLOCK), BLOCK))
    pl.semaphore_wait(barrier, len(partners))
    unit_copy = remote(bias_u, uoth, wsem, 3 * len(pieces), across)
    head_copy = remote(bias_qv, voth, wsem, 3 * len(pieces) + 1, across)
    get_wq.wait()
    get_wo.wait()
    for item in pieces[:4]:
        item.copies[0].start()

    inside_loop = []

    def service(name, act):
        def at_point(k, ask):
            full = f"{name}{k}"
            if ask:
                return full in PLAN or full in WEIGHT_PLAN
            inside_loop.append(full)
            act(full)
            inside_loop.pop()

        return at_point

    def pass_on(name):
        for i in WEIGHT_PLAN.get(name, ()):
            if pieces[i].stage < 1:
                pieces[i].advance()

    def have_weight(*which):
        for i in which:
            while pieces[i].stage < 2:
                pieces[i].advance()

    ln1_gain, ln1_bias, out_bias, ln2_gain, ln2_bias, fc2_bias = (
        ref[...].reshape(1, width) for ref in (gain1, bias1, bias_o, gain2, bias2, bias_f)
    )
    get_tok.wait()

    def first_norm(at):
        plane = core * (count // (SIDE * SIDE)) + at // (SIDE * SIDE)
        line = (at // SIDE) % SIDE
        shape = (SIDE, width // 3)
        for k in range(4):
            spot = jnp.concatenate(
                [jnp.broadcast_to(table[pl.ds(plane, 1)], shape), jnp.broadcast_to(table[pl.ds(line + k, 1)], shape), table[...]], axis=1
            )
            span = pl.ds(aligned(at + k * SIDE, SIDE), SIDE)
            stream = tok_s[span].astype(F32) + spot
            sin_s[span] = stream
            xhat, _ = norm_stats(stream)
            n1_s[span] = (xhat * ln1_gain + ln1_bias).astype(BF16)

    loop(count, 4 * SIDE, first_norm)
    doc = ids[pl.ds(chip, 1), :]
    starts = [jnp.zeros((1, 1), F32)]
    starts += [jnp.sum(jnp.where(doc < v, 1.0, 0.0), axis=1, keepdims=True) for v in range(1, 4)]
    starts.append(jnp.full((1, 1), rows, F32))
    turn = jnp.zeros((1, 1), F32)
    for v in range(4):
        turn += jnp.where(starts[v + 1] - starts[v] == count, starts[v], 0.0)
    turn_here = turn - (core * count).astype(F32)

    def wrapped(v):
        v = jnp.where(v >= rows, v - rows, v)
        return jnp.where(v < 0, v + rows, v)

    def rotations(at):
        down = (lax.broadcasted_iota(jnp.int32, (64, rows), 0) + at).astype(F32)
        along = lax.broadcasted_iota(jnp.int32, (64, rows), 1).astype(F32)
        roll_s[pl.ds(at, 64)] = jnp.where(wrapped(down + turn_here) == along, 1.0, 0.0).astype(BF16)
        back_s[pl.ds(at, 64)] = jnp.where(wrapped(down - turn_here) == along, 1.0, 0.0).astype(BF16)
        where = wrapped((lax.broadcasted_iota(jnp.int32, (64, 128), 0) + at).astype(F32) + turn)
        mine = sum(jnp.where(where >= starts[v], 1.0, 0.0) for v in range(1, 4))
        slot = (lax.broadcasted_iota(jnp.int32, (64, 128), 1) % HEAD).astype(F32)
        sq_s[pl.ds(at, 64)] = jnp.where((slot < 4) & (slot != mine), 1.0, 0.0).astype(BF16)
        sk_s[pl.ds(at, 64)] = jnp.where(slot == mine, NEG_LARGE, 0.0).astype(BF16)


    for copy in get_w1:
        copy.wait()
    get_w2.wait()
    for item in pieces[4:]:
        item.copies[0].start()
    n1_copy = remote(n1_s.at[pl.ds(0, count)], n1_s.at[pl.ds(count, count)], csem, 0, sib)
    get_cot.wait()
    cot_copy = remote(cot_s.at[pl.ds(0, count)], cot_s.at[pl.ds(count, count)], csem, 1, sib)

    def rotate(at):
        nr_s[pl.ds(at, BLOCK)] = dot(roll_s[pl.ds(at, BLOCK)], n1_s[...]).astype(BF16)

    def project(j, at):
        n = nr_s[pl.ds(at, BLOCK)]
        biases = bias_qv if j == 0 else voth
        q = (dot_nt(n, wq_s[j, 0]) + biases[0:1]).astype(BF16) * SCALE
        k = dot_nt(n, wq_s[j, 1]).astype(BF16)
        v = (dot_nt(n, wq_s[j, 2]) + biases[1:2]).astype(BF16)
        q_s[j, pl.ds(at, BLOCK), :quarter] = q
        k_s[pl.ds(at, BLOCK), :quarter] = k
        v_s[j, pl.ds(at, BLOCK), :quarter] = v
        kt_s[j * quarter : (j + 1) * quarter, pl.ds(at, BLOCK)] = k.T * SCALE

    blocks = [(b, at) for b in range(2) for at in range(0, count, BLOCK)]

    def attend(j):
        for head in range(heads):
            at = 512 + 256 * head
            a_s[:, at : at + 128] = head_lanes(q_s.at[j], head, sq_s[...])
            a_s[:, at + 128 : at + 256] = head_lanes(k_s, head, sk_s[...])
        for at in range(0, rows, BLOCK):
            ou_s[:quarter, at : at + BLOCK] = v_s[j, at : at + BLOCK, :quarter].T

        def tile(here):
            b = here // count
            at = aligned(here % count, BLOCK)
            keys = pl.ds(aligned(b * count, count), count)
            for head in range(heads):
                column = 512 + 256 * head
                s = dot_nt(a_s[keys, column + 128 : column + 256], a_s[pl.ds(here, BLOCK), column : column + 128])
                m = jnp.max(s, axis=0, keepdims=True)
                e = jnp.exp(s - m)
                r = 1.0 / column_sum(e)
                low = e.astype(BF16)
                span = slice(head * HEAD, head * HEAD + HEAD)
                to = slice(j * quarter + head * HEAD, j * quarter + head * HEAD + HEAD)
                e_s[j * heads + head, b, :, pl.ds(at, BLOCK)] = low
                ot_s[to, pl.ds(here, BLOCK)] = (dot(ou_s[span, keys], low) * r).astype(BF16)
                r_s[j * heads + head : j * heads + head + 1, pl.ds(here, BLOCK)] = r

        return tile

    loop(rows, 64, rotations)
    n1_copy.wait_recv()
    loop(rows, BLOCK, rotate)
    loop(rows, BLOCK, lambda at: project(0, at))
    pass_on("p0")
    loop(rows, BLOCK, attend(0), service("a", pass_on))
    head_copy.wait_recv()
    have_weight(0, 1, 2)
    loop(rows, BLOCK, lambda at: project(1, at))
    pass_on("p1")
    loop(rows, BLOCK, attend(1), service("c", pass_on))

    have_weight(3)

    def unrotate(at):
        ou_s[:, pl.ds(at, BLOCK)] = dot(ot_s[...], roll_s[:, pl.ds(at, BLOCK)]).astype(BF16)

    loop(rows, BLOCK, unrotate)
    pass_on("u")

    def out_part(at):
        return dot_tn(ou_s[:, pl.ds(at, BLOCK)], wo_s[...])

    def att_half(at):
        return half_copy(sb1.at[pl.ds(at, BLOCK)], rb1.at[pl.ds(at, BLOCK)], 2, at)

    def n2_half(at):
        return half_copy(n2_s.at[pl.ds(at, BLOCK)], n2_s.at[pl.ds(aligned(count + at, BLOCK), BLOCK)], 4, at)

    def out_sib(at):
        sb1[pl.ds(at, BLOCK)] = out_part(count + at).astype(BF16)
        att_half(at).start()

    loop(count, BLOCK, out_sib)

    def out_mine(at):
        mid_s[pl.ds(at, BLOCK)] = sin_s[pl.ds(at, BLOCK)] + out_part(at) + out_bias

    loop(count, BLOCK, out_mine)
    pass_on("o")

    def second_norm(at):
        att_half(at).wait_recv()
        for off in range(0, BLOCK, 128):
            spot = pl.ds(aligned(at + off, 128), 128)
            mid = mid_s[spot] + rb1[spot].astype(F32)
            mid_s[spot] = mid
            xhat, _ = norm_stats(mid)
            n2_s[spot] = (xhat * ln2_gain + ln2_bias).astype(BF16)
        n2_half(at).start()

    loop(count, BLOCK, second_norm)
    pass_on("n")

    base_a = units
    parts = units // BLOCK
    steps = copies_of(len(full_bits))

    class Region:
        def __init__(self, index, row, size, cols, slot, kind, refs, to):
            own_r, oth_r, xr_r, land_r, both_r, rx_r = refs
            self.place, self.slot, self.to, self.xr = (row, size, 0, cols), slot, to, xr_r
            first, after = KINDS[kind]
            self.first = first is not None
            self.stages, self.stage, self.finished, self.sent = [], -1, False, []
            now, parts, used, trail = self.place, 8, 0, []
            sems = iter(range(index * steps, (index + 1) * steps))

            def copy(src, src_at, dst, dst_at, device):
                return described(src.at[self.window(src_at)], dst.at[self.window(dst_at)], gsem, next(sems), device)

            def piece(bits, mask):
                where = now
                for k, b in enumerate(bits):
                    where = self.cut(where, 1 - sides[b] if mask >> k & 1 else sides[b])
                return where

            sums = 1 + len(after) + len(full_bits)
            if self.first:
                keep, give, there = piece((first,), 0), piece((first,), 1), (row // 2, size // 2, 0, cols)
                place = self.landing(0, 4)
                copies = [copy(own_r, give, land_r, place, mate((first,))), copy(oth_r, give, both_r, there, mate((first,)))]
                adds = [(own_r, own_r, keep, [(land_r, place)]), (oth_r, oth_r, keep, [(both_r, there)])]
                self.stages.append((copies, adds, False))
                trail.append(((first,), keep))
                now, parts, used = keep, 4, 4
            self.stages.append(([copy(oth_r, now, xr_r, now, across)], [(own_r, own_r, now, [(xr_r, now)])], False))
            for bits in after:
                parts >>= len(bits)
                keep, copies, terms = piece(bits, 0), [], []
                for mask in range(1, 1 << len(bits)):
                    place = self.landing(used, parts)
                    used += parts
                    terms.append((land_r, place))
                    copies.append(copy(own_r, piece(bits, mask), land_r, place, mate([b for k, b in enumerate(bits) if mask >> k & 1])))
                self.stages.append((copies, [(own_r, own_r, keep, terms)], False))
                trail.append((bits, keep))
                now = keep
            for i, b in enumerate(full_bits):
                place = self.small_place()
                self.stages.append(([copy(own_r, now, rx_r[i], place, mates[b])], [(own_r, own_r, now, [(rx_r[i], place)])], True))
            copies, adds, full = self.stages[-1]
            self.stages[-1] = (copies, [(xr_r,) + adds[0][1:]], full)
            for bits, keep in reversed(trail):
                copies = []
                for mask in range(1, 1 << len(bits)):
                    copies.append(copy(xr_r, keep, xr_r, keep, mate([b for k, b in enumerate(bits) if mask >> k & 1])))
                self.stages.append((copies, [], False))

        def window(self, where):
            row, size, col, cols = where
            return pl.ds(row, size), pl.ds(col, cols)

        def cut(self, where, side):
            row, size, col, cols = where
            if (size // 2) % 16 == 0:
                return aligned(row + side * (size // 2), 16), size // 2, col, cols
            return row, size, aligned(col + side * (cols // 2), 128), cols // 2

        def landing(self, at, parts_here):
            row, rows_one, cols_one = self.slot
            full = self.place[3]
            if cols_one == full:
                return row + at * rows_one, parts_here * rows_one, 0, full
            if parts_here == 1:
                return row + at // 2 * rows_one, rows_one, at % 2 * cols_one, cols_one
            return row + at // 2 * rows_one, parts_here // 2 * rows_one, 0, full

        def small_place(self):
            row, rows_one, cols_one = self.slot
            if cols_one == self.place[3]:
                return row // 7, rows_one, 0, cols_one
            k = (self.place[0] - base_a) // quarter
            return units // 8 + k // 2 * rows_one, rows_one, k % 2 * cols_one, cols_one

        def begin(self, copies):
            for copy in copies:
                copy.start()
            self.sent += copies

        def ready(self, j):
            if self.first:
                self.stage = 0
                self.begin([self.stages[0][0][j]])
            elif j == 1:
                self.stage = 0
                self.begin(self.stages[0][0])

        def add(self, into, base, where, terms):
            row, size, col, cols = where
            step = 64 if size % 64 == 0 else 48 if size % 48 == 0 else 32

            def body(off):
                to = (pl.ds(aligned(row + off, 16), step), pl.ds(col, cols))
                parts_in = [ref[pl.ds(aligned(r + off, 16), step), pl.ds(c, cols)] for ref, (r, _, c, _) in terms]
                if len(parts_in) == 1:
                    into[to] = base[to] + parts_in[0]
                else:
                    into[to] = sum((v.astype(F32) for v in parts_in), base[to].astype(F32)).astype(BF16)

            if inside_loop:
                for off in range(0, size, step):
                    body(off)
            else:
                loop(size, step, body)

        def advance(self):
            if self.finished or self.stage < 0:
                return
            copies, adds, full = self.stages[self.stage]
            for copy in copies:
                copy.wait_recv()
            if full:
                for copy in copies:
                    copy.wait_send()
                self.sent = [c for c in self.sent if all(c is not d for d in copies)]
            for item in adds:
                self.add(*item)
            self.stage += 1
            if self.stage < len(self.stages):
                self.begin(self.stages[self.stage][0])
                return
            self.finished = True
            to_write.append(self)

    chunks = []
    refs = (own, oth, xr, land, land_both, rx)
    for i in range(parts):
        slot = (i * 7 * (BLOCK // 8), BLOCK // 8, width)
        to = g2_h.at[pl.ds(i * BLOCK, BLOCK)]
        chunks.append(Region(2 * i, i * BLOCK, BLOCK, width, slot, ORDERS[2 * i], refs, to))
        refs_one = tuple(ref.at[i] for ref in (own1, oth1, xr1, land1, land1_both)) + ([ref.at[i] for ref in rx1],)
        to = g1_h.at[:, pl.ds(i * BLOCK, BLOCK)]
        chunks.append(Region(2 * i + 1, 0, width, BLOCK, (0, width // 8, BLOCK), ORDERS[2 * i + 1], refs_one, to))
    for i in range(4):
        slot = (7 * units // 8 + i * quarter, quarter // 4, width // 2)
        to = go_h if i == 0 else gq_h.at[i - 1]
        chunks.append(Region(2 * parts + i, base_a + i * quarter, quarter, width, slot, ORDERS[2 * parts + i], refs, to))
    first_att = 2 * parts

    class Small:
        def __init__(self, tile, index, everywhere, paired, groups):
            self.tile, self.everywhere, self.paired = tile, everywhere, paired
            landings = [near.at[3 * index + k] for k in range(3)] + [far.at[(7 + len(full_bits)) * index + k] for k in range(7 + len(full_bits))]
            sems = iter(range(index * len(landings), (index + 1) * len(landings)))
            landings = iter(landings)

            def stage(devices):
                places = [next(landings) for _ in devices]
                return places, [described(tile, dst, ssem, next(sems), d) for dst, d in zip(places, devices)]

            self.stages = [stage([sib, across, facing])]
            for bits in groups + [(b,) for b in full_bits]:
                masks = range(1, 1 << len(bits))
                self.stages.append(stage([mate([b for k, b in enumerate(bits) if mask >> k & 1]) for mask in masks]))
            self.stage, self.finished = -1, False

        def start(self):
            self.stage = 0
            for copy in self.stages[0][1]:
                copy.start()

        def advance(self):
            if self.finished or self.stage < 0:
                return
            places, copies = self.stages[self.stage]
            for copy in copies:
                copy.wait()
            tile = self.tile
            if self.stage == 0:
                beside, over, facing_ = places
                n, p = self.everywhere, self.paired
                tile[0:n] = (tile[0:n] + beside[0:n]) + (over[0:n] + facing_[0:n])
                tile[n : n + p] = tile[n : n + p] + over[n + p : n + 2 * p]
            else:
                got = [tile[...]] + [place[...] for place in places]
                while len(got) > 1:
                    got = [got[k] + got[k + 1] for k in range(0, len(got), 2)]
                tile[...] = got[0]
            self.stage += 1
            if self.stage == len(self.stages):
                self.finished = True
                return
            for copy in self.stages[self.stage][1]:
                copy.start()

    first_small = Small(early, 0, 4, 1, [(b,) for b in half_bits])
    last_small = Small(late, 1, 2, 2, [tuple(half_bits)])

    def ready(i, j):
        chunks[i].ready(j)

    to_write = []

    def write_finished():
        while to_write:
            region = to_write.pop()
            region.done = local(region.xr.at[region.window(region.place)], region.to)

    def hook(name):
        pass_on(name)
        for i in PLAN.get(name, ()):
            (chunks + [last_small, first_small])[i].advance()
            if not inside_loop:
                write_finished()

    def chunk_rows(j, i, at):
        span = pl.ds(at, BLOCK)
        cols = slice(j * units + i * BLOCK, j * units + (i + 1) * BLOCK)
        mine = slice(i * BLOCK, (i + 1) * BLOCK)
        bias = (bias_u if j == 0 else uoth)[mine].reshape(1, BLOCK)
        h = dot(n2_s[span], w1_s[j, i]) + bias
        a, slope = gelu_pair(h)
        a_s[span, cols] = a.astype(BF16)
        g = (dot_nt(cot_s[span], w2_s[j, mine]) * slope).astype(BF16)
        g_s[span, cols] = g

    def chunk_grads(j, i):
        cols = slice(j * units + i * BLOCK, j * units + (i + 1) * BLOCK)
        mine = slice(i * BLOCK, (i + 1) * BLOCK)
        to = oth if j == 1 else own

        def second(at):
            to[pl.ds(i * BLOCK + at, 128)] = dot_tn(a_s[:, pl.ds(cols.start + at, 128)], cot_s[...]).astype(BF16)

        loop(BLOCK, 128, second)
        ready(2 * i, j)
        g = g_s[:, cols]

        def first(at):
            (oth1 if j == 1 else own1)[i, pl.ds(at, BLOCK)] = dot(n2t_s[pl.ds(at, BLOCK)], g_s[:, cols]).astype(BF16)

        loop(width, BLOCK, first)
        ready(2 * i + 1, j)
        early[4 + j : 5 + j, mine] = column_sum(g.astype(F32))
        hook(f"f{j}{i}")

    def feed(j, i, first=False):
        if first:
            loop(count, BLOCK, lambda at: chunk_rows(j, i, at))
            hook(f"r{j}{i}.0")
            cot_copy.wait_recv()

            def received(at):
                n2_half(at).wait_recv()
                chunk_rows(j, i, count + at)

            loop(count, BLOCK, received)
            hook(f"r{j}{i}.1")

            def turned(at):
                n2t_s[:, pl.ds(at, BLOCK)] = n2_s[pl.ds(at, BLOCK)].T

            loop(rows, BLOCK, turned)
        else:
            loop(rows, BLOCK, lambda at: chunk_rows(j, i, at), service(f"r{j}{i}.", hook), 2)
        chunk_grads(j, i)

    early[...] = jnp.zeros_like(early)
    late[...] = jnp.zeros_like(late)
    unit_copy.wait_recv()
    for i in range(parts):
        have_weight(4 + 2 * i, 5 + 2 * i)
        feed(1, i, first=i == 0)
        feed(0, i)

    def back_two(at):
        span = pl.ds(at, BLOCK)
        total = None
        for j in range(2):
            for i in range(parts):
                at_col = j * units + i * BLOCK
                term = dot_nt(g_s[span, at_col : at_col + BLOCK], w1_s[j, i])
                total = term if total is None else total + term
        return total

    def mlp_part(at):
        span = pl.ds(at, BLOCK)
        return dot(a_s[span, :units], w2_s[0]) + dot(a_s[span, units:], w2_s[1])

    def gn2_half(at):
        return half_copy(sb2.at[pl.ds(at, BLOCK)], rb2.at[pl.ds(at, BLOCK)], 6, at)

    def dm_half(at):
        return half_copy(n2_s.at[pl.ds(at, BLOCK)], n2_s.at[pl.ds(aligned(count + at, BLOCK), BLOCK)], 10, at)

    def back_two_sib(at):
        sb2[pl.ds(at, BLOCK)] = back_two(count + at).astype(BF16)
        gn2_half(at).start()

    def back_two_mine(at):
        gm_s[pl.ds(at, BLOCK)] = back_two(at)

    def mlp_sib(at):
        sb1[pl.ds(at, BLOCK)] = mlp_part(count + at).astype(BF16)

    loop(count, BLOCK, back_two_sib)
    hook("g0")
    loop(count, BLOCK, back_two_mine)
    hook("gn2")

    def second_back(at):
        gn2_half(at).wait_recv()
        n2_half(at).wait_send()
        for off in range(0, BLOCK, 128):
            spot = pl.ds(aligned(at + off, 128), 128)
            xhat, sigma = norm_stats(mid_s[spot])
            grad = gm_s[spot] + rb2[spot].astype(F32)
            cot = cot_s[spot].astype(F32)
            back = cot + norm_back(grad, ln2_gain, xhat, sigma)
            gm_s[spot] = back
            n2_s[spot] = back.astype(BF16)
            early[0:1] += column_sum(back)
            early[1:2] += column_sum(grad * xhat)
            early[2:3] += column_sum(grad)
            early[3:4] += column_sum(cot)
        dm_half(at).start()

    loop(count, BLOCK, second_back)
    hook("lb")
    for at in range(0, count, BLOCK):
        att_half(at).wait_send()
    loop(count, BLOCK, mlp_sib)
    mlp_copy = remote(sb1, rb1, csem, 8, sib)
    first_small.start()
    hook("ln2")

    for at in range(0, count, BLOCK):
        dm_half(at).wait_recv()

    start = base_a + quarter
    zero = jnp.zeros((count, 128), BF16)
    grad_s = dq_s = ou_s
    n1_copy.wait_send()

    def keep_gradient(j, c):
        to = oth if j == 1 else own
        low = start + c * quarter
        dt = ot_s.at[j * quarter : (j + 1) * quarter]

        def columns(at):
            to[low : low + quarter, pl.ds(at, BLOCK)] = dot(dt[...], nr_s[:, pl.ds(at, BLOCK)]).astype(BF16)

        loop(width, BLOCK, columns)
        ready(first_att + 1 + c, j)
        if c != 1:
            d = g_s[:, (3 * j + c) * BLOCK : (3 * j + c) * BLOCK + quarter]
            late[2 + c // 2 + 2 * j : 3 + c // 2 + 2 * j, :quarter] = column_sum(d.astype(F32))

    def values_back(j):
        base = j * quarter
        to = oth if j == 1 else own

        def weight(at):
            to[base_a : base_a + quarter, pl.ds(at, BLOCK)] = dot(ou_s[base : base + quarter], n2_s[:, pl.ds(at, BLOCK)]).astype(BF16)

        loop(width, BLOCK, weight)
        ready(first_att, j)

        def output(at):
            grad_s[base : base + quarter, pl.ds(at, BLOCK)] = dot_nt(wo_s[base : base + quarter], n2_s[pl.ds(at, BLOCK)]).astype(BF16)

        loop(rows, BLOCK, output)
        hook(f"w{j}.0")
        go_s = n1_s.at[:, 256 * j : 256 * (j + 1)]

        def scale(at):
            here = pl.ds(at, BLOCK)
            grad_t = dot_nt(grad_s[base : base + quarter], roll_s[here])
            for head in range(heads):
                row = j * heads + head
                r = r_s[row : row + 1, here]
                g = grad_t[head * HEAD : (head + 1) * HEAD]
                at_head = slice(base + head * HEAD, base + (head + 1) * HEAD)
                in_s[row : row + 1, here] = column_sum(g * ot_s[at_head, here].astype(F32)) * r
                gt_s[at_head, here] = (g * r).astype(BF16)
            go_s[here, :quarter] = gt_s[base : base + quarter, here].T

        loop(rows, BLOCK, scale)

        def block(at):
            here = pl.ds(at, count)
            b = at // count
            dv = [None, None]
            for head in range(heads):
                tile = head // 2
                gh = jnp.where(lane_half(count, head % 2 == 1), go_s[here, 128 * tile : 128 * tile + 128], zero)
                part = dot(e_s[j * heads + head, b], gh)
                dv[tile] = part if dv[tile] is None else dv[tile] + part
            dv = jnp.concatenate(dv, axis=1)[:, :quarter].astype(BF16)
            g_s[here, (3 * j + 2) * BLOCK : (3 * j + 2) * BLOCK + quarter] = dv
            ot_s[base : base + quarter, here] = dv.T

        loop(rows, count, block)
        hook(f"w{j}.1")
        keep_gradient(j, 2)
        hook(f"v{j}")

    def scores_back(j):
        base = j * quarter

        def block(at):
            here = pl.ds(at, count)
            b = at // count
            dk = [None, None]
            for head in range(heads):
                tile = head // 2
                row = j * heads + head
                half = lane_half(count, head % 2 == 1)
                lanes = slice(128 * tile, 128 * tile + 128)
                vh = jnp.where(half, v_s[j, here, lanes], zero)
                qh = jnp.where(half, q_s[j, here, lanes], zero)
                last_row = min(128 * tile + 128, quarter)
                vh = vh[:, : last_row - 128 * tile]
                ds = n2t_s.at[:count, head * count : (head + 1) * count] if head < 2 else ds_s
                for off in range(0, count, BLOCK):
                    some = pl.ds(aligned(at + off, BLOCK), BLOCK)
                    dp_t = dot(vh, gt_s[base + 128 * tile : base + last_row, some])
                    grad = (dp_t - in_s[row : row + 1, some]).astype(BF16)
                    ds[:, off : off + BLOCK] = grad * e_s[row, b, :, off : off + BLOCK]
                part = dot(ds[...], qh)
                dk[tile] = part if dk[tile] is None else dk[tile] + part
                kth = kt_s[base + head * HEAD : base + head * HEAD + HEAD, here]
                dq_s[base + head * HEAD : base + head * HEAD + HEAD, here] = dot(kth, ds[...]).astype(BF16)
            dk = jnp.concatenate(dk, axis=1)[:, :quarter].astype(BF16)
            g_s[here, (3 * j + 1) * BLOCK : (3 * j + 1) * BLOCK + quarter] = dk
            ot_s[base : base + quarter, here] = dk.T
            g_s[here, 3 * j * BLOCK : 3 * j * BLOCK + quarter] = dq_s[base : base + quarter, here].T

        loop(rows, count, block, service(f"b{j}.", hook))
        keep_gradient(j, 1)
        hook(f"k{j}")
        ot_s[base : base + quarter] = dq_s[base : base + quarter]
        keep_gradient(j, 0)
        hook(f"s{j}")

    values_back(1)
    scores_back(1)
    values_back(0)
    scores_back(0)

    def finish_out(at):
        span = pl.ds(at, BLOCK)
        mid_s[span] = mid_s[span] + mlp_part(at) + fc2_bias

    loop(count, BLOCK, finish_out)
    hook("fo")
    mlp_copy.wait_recv()

    def write_out(at):
        spot = pl.ds(at, 128)
        tok_s[spot] = (mid_s[spot] + rb1[spot].astype(F32)).astype(BF16)

    loop(count, 128, write_out)
    put_out = local(tok_s, out_h)
    hook("fin")

    def back_one(at):
        total = None
        for j in range(2):
            for c in range(3):
                d = g_s[pl.ds(at, BLOCK), (3 * j + c) * BLOCK : (3 * j + c) * BLOCK + quarter]
                term = dot(d, wq_s[j, c])
                total = term if total is None else total + term
        n2_s[pl.ds(at, BLOCK)] = total.astype(BF16)

    for at in range(0, count, BLOCK):
        dm_half(at).wait_send()
    loop(rows, BLOCK, back_one, service("d.", hook), 2)
    for at in range(0, count, BLOCK):
        gn2_half(at).wait_send()

    def gn1_half(at):
        return half_copy(sb2.at[pl.ds(at, BLOCK)], rb2.at[pl.ds(at, BLOCK)], 12, at)

    def back_one_sib(at):
        sb2[pl.ds(at, BLOCK)] = dot(back_s[pl.ds(count + at, BLOCK)], n2_s[...]).astype(BF16)
        gn1_half(at).start()

    def back_one_mine(at):
        mid_s[pl.ds(at, BLOCK)] = dot(back_s[pl.ds(at, BLOCK)], n2_s[...])

    loop(count, BLOCK, back_one_sib)
    loop(count, BLOCK, back_one_mine)
    hook("e.0")
    mlp_copy.wait_send()

    def first_back(at):
        gn1_half(at).wait_recv()
        for off in range(0, BLOCK, 128):
            spot = pl.ds(aligned(at + off, 128), 128)
            xhat, sigma = norm_stats(sin_s[spot])
            grad = mid_s[spot] + rb2[spot].astype(F32)
            sb1[spot] = (gm_s[spot] + norm_back(grad, ln1_gain, xhat, sigma)).astype(BF16)
            late[0:1] += column_sum(grad * xhat)
            late[1:2] += column_sum(grad)

    loop(count, BLOCK, first_back)
    put_in = local(sb1, ing_h)
    last_small.start()
    hook("e.1")
    hook("tail")
    left = [first_small, last_small] + chunks
    while left:
        for item in left:
            item.advance()
            write_finished()
        left = [item for item in left if not item.finished]

    for row, source, at in ((0, late, 0), (1, late, 1), (2, early, 0), (3, early, 1), (4, early, 2), (5, early, 3), (8, early, 4), (9, late, 2), (10, late, 3)):
        small_o[row : row + 1] = source[at : at + 1]

    passed = [copy for item in pieces for copy in item.copies]
    for copy in [unit_copy, head_copy, cot_copy] + [gn1_half(at) for at in range(0, count, BLOCK)] + passed:
        copy.wait_send()
    for chunk in chunks:
        for copy in chunk.sent:
            copy.wait_send()
        chunk.done.wait()
    put_out.wait()
    put_in.wait()


def copies_of(full):
    most = 0
    for kind in ORDERS:
        first, after = KINDS[kind]
        most = max(most, 1 + full + 2 * sum((1 << len(bits)) - 1 for bits in after) + (0 if first is None else 3))
    return most


def call_layer(dp_size, tokens, cotangent, ids, table, vectors, wq, wo, w1, w2):
    count, width = tokens.shape
    rows = 2 * count
    quarter = wo.shape[0]
    units = w1.shape[1]
    heads = quarter // HEAD
    grad_rows = units + 4 * quarter
    parts = units // BLOCK
    bits = [b for b in range(20) if (1 << b) < dp_size]
    half_bits = bits[:3]
    shape = jax.ShapeDtypeStruct
    vm = pltpu.VMEM
    regions = 2 * (units // BLOCK) + 4
    steps = copies_of(len(bits) - len(half_bits))
    fetched = 4 + 2 * (units // BLOCK)
    scratch = (
        [vm((count, width), BF16), vm((rows, width), BF16)]
        + [vm((count, width), F32)] * 3
        + [vm((rows, width), BF16)] * 2
        + [vm((width, rows), BF16)]
        + [vm((2,) + wq.shape, BF16), vm((2 * quarter, width), BF16), vm((2, units // BLOCK, width, BLOCK), BF16), vm((2,) + w2.shape, BF16)]
        + [vm((2, rows, 256), BF16)] * 2
        + [vm((2 * quarter, rows), BF16)] * 4
        + [vm((8, rows), F32)] * 2
        + [vm((2 * heads, 2, count, count), BF16)]
        + [vm((rows, rows), BF16)] * 2
        + [vm((rows, width), BF16), vm((count, count), BF16)]
        + [vm((rows, 2 * units), BF16)] * 2
        + [vm((count, width), BF16)] * 4
        + [vm((grad_rows, width), BF16)] * 3
        + [vm((7 * units // 8 + 4 * quarter, width), BF16), vm((units // 2, width), BF16)]
        + [vm((parts, width, BLOCK), BF16)] * 3
        + [vm((parts, 7 * width // 8, BLOCK), BF16), vm((parts, width // 2, BLOCK), BF16)]
        + [vm((grad_rows >> len(half_bits), width), BF16)] * (len(bits) - len(half_bits))
        + [vm((parts, width // 8, BLOCK), BF16)] * (len(bits) - len(half_bits))
        + [vm((units,), F32), vm((2, quarter), F32), vm((8, width), F32), vm((8, width), F32)]
        + [vm((6, 8, width), F32), vm((14 + 2 * (len(bits) - 3), 8, width), F32)]
        + [pltpu.SemaphoreType.DMA((8 + units // BLOCK + regions,))]
        + [pltpu.SemaphoreType.DMA((2, n)) for n in (3 * fetched + 2, 14, regions * steps, 2 * (10 + len(bits) - 3))]
    )
    anywhere = pl.BlockSpec(memory_space=pl.ANY)
    inside = pl.BlockSpec(memory_space=pltpu.VMEM)
    return pl.pallas_call(
        functools.partial(layer, dp_size, half_bits),
        out_shape=[shape((count, width), BF16)] * 2
        + [shape(w2.shape, BF16), shape(w1.shape, BF16), shape(wo.shape, BF16), shape(wq.shape, BF16), shape((16, width), F32)],
        in_specs=[anywhere] * 2 + [inside] * (2 + len(vectors)) + [anywhere] * 4,
        out_specs=[anywhere] * 6 + [inside],
        scratch_shapes=scratch,
        compiler_params=pltpu.CompilerParams(vmem_limit_bytes=VMEM_LIMIT, collective_id=0, has_side_effects=True),
        name="layer",
    )(tokens, cotangent, ids, table, *vectors, wq, wo, w1, w2)


def finish(*refs):
    sources, small, rest = refs[:6], refs[6], refs[7:]
    results, vectors, rest = rest[:6], rest[6:14], rest[14:]
    narrow, wide, (get, put) = rest[:6], rest[6:10], rest[10:]
    blocks = []
    for k, src in enumerate(sources):
        if src.ndim == 3:
            places = list(range(src.shape[0]))
        else:
            step = min(BLOCK, src.shape[0])
            places = [pl.ds(at, step) for at in range(0, src.shape[0], step)]
        for at in places:
            low = narrow[k].at[at]
            blocks.append((src.at[at], low, low if k < 2 else wide[k - 2].at[at], results[k].at[at]))
    reads = [pltpu.make_async_copy(src, low, get.at[n]) for n, (src, low, _, _) in enumerate(blocks)]
    writes = [pltpu.make_async_copy(high, dst, put.at[n]) for n, (_, _, high, dst) in enumerate(blocks)]
    for copy in reads:
        copy.start()
    for i in range(6):
        vectors[i][...] = small[i]
    vectors[6][...] = small[8, : vectors[6].shape[0]]
    vectors[7][...] = small[9:11, : vectors[7].shape[1]]
    for read, write, (_, low, high, _) in zip(reads, writes, blocks):
        read.wait()
        if high is not low:

            def cast(at, low=low, high=high):
                high[pl.ds(at, 64)] = low[pl.ds(at, 64)].astype(F32)

            loop(low.shape[0], 64, cast)
        write.start()
    for copy in writes:
        copy.wait()


def call_finish(arrays, small, units, quarter):
    width = small.shape[1]
    shape = jax.ShapeDtypeStruct
    extents = [(width,)] * 6 + [(units,), (2, quarter)]
    kinds = [BF16, BF16, F32, F32, F32, F32]
    anywhere = pl.BlockSpec(memory_space=pl.ANY)
    inside = pl.BlockSpec(memory_space=pltpu.VMEM)
    grads = arrays[2:]
    return pl.pallas_call(
        finish,
        in_specs=[anywhere] * len(arrays) + [inside],
        out_specs=[anywhere] * len(arrays) + [inside] * len(extents),
        out_shape=[shape(a.shape, k) for a, k in zip(arrays, kinds)] + [shape(e, F32) for e in extents],
        scratch_shapes=[pltpu.VMEM(a.shape, BF16) for a in arrays]
        + [pltpu.VMEM(a.shape, F32) for a in grads]
        + [pltpu.SemaphoreType.DMA((16,)), pltpu.SemaphoreType.DMA((16,))],
        compiler_params=pltpu.CompilerParams(vmem_limit_bytes=VMEM_LIMIT),
        name="finish",
    )(*arrays, small)


def per_device(
    tokens, segment_ids, ln1_gain, ln1_bias, qkv_weight, qv_bias, out_weight, out_bias,
    ln2_gain, ln2_bias, fc1_weight, fc1_bias, fc2_weight, fc2_bias, cotangent,
):
    width = tokens.shape[1]
    freq_count = width // 6
    frequency = 10000.0 ** (-jnp.arange(freq_count, dtype=F32) / freq_count)
    angles = jnp.arange(SIDE, dtype=F32)[:, None] * frequency[None, :]
    table = jnp.concatenate([jnp.sin(angles), jnp.cos(angles)], axis=1)
    vectors = (ln1_gain, ln1_bias, out_bias, ln2_gain, ln2_bias, fc2_bias, fc1_bias, qv_bias)
    *arrays, small = call_layer(
        lax.axis_size("dp"), tokens, cotangent, segment_ids, table, vectors, qkv_weight.transpose(0, 2, 1), out_weight, fc1_weight, fc2_weight
    )
    out, ing, g2, g1, go, gq, a0, a1, a2, a3, a4, a5, g_units, g_heads = call_finish(arrays, small, fc1_weight.shape[1], out_weight.shape[0])
    return (out, ing, a0, a1, gq.transpose(0, 2, 1), g_heads, go, a2, a3, a4, g1, g_units, g2, a5)


def solution(mesh):
    placed = (
        P(("dp", "tensor"), None),
        P("dp", None),
        P(),
        P(),
        P(None, None, "tensor"),
        P(None, "tensor"),
        P("tensor", None),
        P(),
        P(),
        P(),
        P(None, "tensor"),
        P("tensor"),
        P("tensor", None),
        P(),
        P(("dp", "tensor"), None),
    )
    return jax.shard_map(
        per_device,
        mesh=mesh,
        in_specs=placed,
        out_specs=(
            P(("dp", "tensor"), None),
            P(("dp", "tensor"), None),
            P(),
            P(),
            P(None, None, "tensor"),
            P(None, "tensor"),
            P("tensor", None),
            P(),
            P(),
            P(),
            P(None, "tensor"),
            P("tensor"),
            P("tensor", None),
            P(),
        ),
        check_vma=False,
    )
```

```python
import functools

import jax
import jax.numpy as jnp
from jax import lax
from jax.experimental import pallas as pl
from jax.experimental.pallas import tpu as pltpu
from jax.sharding import PartitionSpec as P

HEAD = 64
SIDE = 16
EPSILON = 1e-06
NEG_LARGE = -1e30
SCALE = HEAD ** (-0.5)
F32 = jnp.float32
BF16 = jnp.bfloat16
VMEM_LIMIT = 64 * 1024 * 1024 - 128 * 1024
MESH = pl.DeviceIdType.MESH
BLOCK = 256
KINDS = {
    "A": (None, ((0,), (1,), (2,))),
    "B": (None, ((1,), (0,), (2,))),
    "D": (None, ((0,), (1, 2))),
    "E": (None, ((0, 1, 2),)),
    "C": (None, ((0, 1), (2,))),
    "Y": (0, ((1,), (2,))),
    "Z": (1, ((0,), (2,))),
    "YD": (0, ((1, 2),)),
    "S": (None, (("p",), ("q",), (2,))),
    "SD": (None, (("p",), ("q", 2))),
    "SF": ("p", (("q",), (2,))),
    "SFD": ("p", (("q", 2),)),
}
ORDERS = ("D", "SFD", "SFD", "Z", "A", "YD", "D", "D", "C", "B")
WEIGHT_PLAN = {"p0": (0,), "a0": (1,), "a2": (2,), "p1": (3,), "c0": (4,), "c3": (5,), "n": (6,), "r10.1": (7,), "r00.1": (8,), "r11.1": (9,)}
PLAN = {
    "f01": (1,),
    "r12.1": (0,),
    "r02.0": (2,),
    "r02.1": (1,),
    "g0": (0,),
    "lb": (3, 4, 1),
    "w1.0": (2, 0),
    "w1.1": (-1, 5),
    "v1": (3,),
    "b1.0": (4, 1),
    "b1.1": (-1, 2, 3),
    "k1": (0,),
    "s1": (4, 5),
    "w0.0": (6, 1, -1),
    "v0": (2, 9),
    "b0.0": (0, 3, 4, 6),
    "b0.1": (2, 5),
    "k0": (8, -1, 9),
    "s0": (3,),
    "fo": (7, 4),
    "d.0": (6,),
    "d.1": (9,),
    "e.0": (5, 8, 3),
    "e.1": (4, 7),
    "tail": (6, 9, 8, -2, 5, 3, 4, 7, 9, 8, 6, -2, 9, 7, 8, 9, 7),
}


def dot(a, b):
    return jnp.dot(a, b, preferred_element_type=F32)


def dot_nt(a, b):
    return lax.dot_general(a, b, (((1,), (1,)), ((), ())), preferred_element_type=F32)


def dot_tn(a, b):
    return lax.dot_general(a, b, (((0,), (0,)), ((), ())), preferred_element_type=F32)


def lane_half(rows, upper):
    lanes = lax.broadcasted_iota(jnp.int32, (rows, 128), 1)
    return lanes >= HEAD if upper else lanes < HEAD


def head_lanes(ref, head, filler):
    tile = ref[:, 128 * (head // 2) : 128 * (head // 2) + 128]
    return jnp.where(lane_half(tile.shape[0], head % 2 == 1), tile, filler)


def gelu_pair(h):
    cdf = 0.5 + 0.5 * lax.erf(h * 0.7071067811865476)
    return h * cdf, cdf + h * jnp.exp(-0.5 * h * h) * 0.3989422804014327


def norm_stats(v):
    centred = v - jnp.mean(v, axis=-1, keepdims=True)
    sigma = lax.rsqrt(jnp.mean(centred * centred, axis=-1, keepdims=True) + EPSILON)
    return centred * sigma, sigma


def norm_back(grad, gain, xhat, sigma):
    g = grad * gain
    return sigma * (g - jnp.mean(g, axis=-1, keepdims=True) - xhat * jnp.mean(g * xhat, axis=-1, keepdims=True))


def column_sum(v):
    return jnp.sum(v, axis=0, keepdims=True)


def aligned(v, unit):
    return v if isinstance(v, int) else pl.multiple_of(v, unit)


def loop(count, step, body, service=None, every=1):
    def run(i, carry):
        body(aligned(i * step, step))
        if service is not None:
            for k in range(count // step // every):
                if service(k, True):
                    pl.when(i == every * (k + 1) - 1)(functools.partial(service, k, False))
        return carry

    lax.fori_loop(0, count // step, run, 0)


def layer(
    dp_size, half_bits,
    tok_h, cot_h, ids, table, gain1, bias1, bias_o, gain2, bias2, bias_f, bias_u, bias_qv, wq_h, wo_h, w1_h, w2_h,
    out_h, ing_h, g2_h, g1_h, go_h, gq_h, small_o,
    tok_s, cot_s, sin_s, mid_s, gm_s, n1_s, n2_s, n2t_s, wq_s, wo_s, w1_s, w2_s,
    q_s, v_s, kt_s, ot_s, ou_s, gt_s, r_s, in_s, e_s, roll_s, back_s, nr_s, ds_s, a_s, g_s, sb1, sb2, rb1, rb2,
    own, oth, xr, land, land_both, own1, oth1, xr1, land1, land1_both, *rest,
):
    rest = list(rest)
    full_bits = [b for b in range(20) if (1 << b) < dp_size and b not in half_bits]
    rx = [rest.pop(0) for _ in full_bits]
    rx1 = [rest.pop(0) for _ in full_bits]
    uoth, voth, early, late, near, far, lsem, wsem, csem, gsem, ssem = rest

    count, width = tok_s.shape
    rows = 2 * count
    quarter = wo_h.shape[0]
    units = w1_h.shape[1]
    heads = quarter // HEAD
    place = lax.axis_index("tensor")
    dp = lax.axis_index("dp")
    chip = place // 2
    core = place % 2
    sib = {"tensor": chip * 2 + 1 - core}
    across = {"tensor": (1 - chip) * 2 + core}
    facing = {"tensor": (1 - chip) * 2 + 1 - core}
    all_bits = list(half_bits) + full_bits
    sides = {b: (dp // (1 << b)) % 2 for b in all_bits}

    ways = {b: (1 - 2 * sides[b]) * (1 << b) for b in all_bits}
    sides["p"] = sides[0] + (sides[1] - sides[0]) * core
    sides["q"] = sides[1] + (sides[0] - sides[1]) * core
    ways["p"] = ways[0] + (ways[1] - ways[0]) * core
    ways["q"] = ways[1] + (ways[0] - ways[1]) * core

    def mate(bits):
        return {"dp": dp + sum(ways[b] for b in bits)}

    def described(src, dst, sems, index, device):
        return pltpu.make_async_remote_copy(
            src_ref=src, dst_ref=dst, send_sem=sems.at[0, index], recv_sem=sems.at[1, index], device_id=device, device_id_type=MESH
        )

    mates = {b: mate((b,)) for b in all_bits}
    groups = {(b,) for b in full_bits}
    for mask in range(1, 1 << len(half_bits)):
        groups.add(tuple(b for k, b in enumerate(half_bits) if mask >> k & 1))

    barrier = pltpu.get_barrier_semaphore()
    partners = [sib, across, facing] + [mate(bits) for bits in sorted(groups)]
    for partner in partners:
        pl.semaphore_signal(barrier, inc=1, device_id=partner, device_id_type=MESH)

    sq_s, sk_s, k_s = a_s.at[:, 0:128], a_s.at[:, 128:256], a_s.at[:, 256:512]
    local_used = [0]

    def local(src, dst):
        copy = pltpu.make_async_copy(src, dst, lsem.at[local_used[0]])
        local_used[0] += 1
        copy.start()
        return copy

    def remote(src, dst, sems, index, device):
        copy = pltpu.make_async_remote_copy(
            src_ref=src, dst_ref=dst, send_sem=sems.at[0, index], recv_sem=sems.at[1, index], device_id=device, device_id_type=MESH
        )
        copy.start()
        return copy

    def half_copy(src, dst, first, at):
        return pltpu.make_async_remote_copy(
            src_ref=src,
            dst_ref=dst,
            send_sem=csem.at[0, first + at // BLOCK],
            recv_sem=csem.at[1, first + at // BLOCK],
            device_id=sib,
            device_id_type=MESH,
        )

    get_wq = local(wq_h, wq_s.at[0])
    get_tok = local(tok_h, tok_s)
    get_cot = local(cot_h, cot_s.at[pl.ds(0, count)])
    get_wo = local(wo_h, wo_s.at[pl.ds(0, quarter)])
    get_w1 = [local(w1_h.at[:, pl.ds(i * BLOCK, BLOCK)], w1_s.at[0, i]) for i in range(units // BLOCK)]
    get_w2 = local(w2_h, w2_s.at[0])

    part = (sides[0] + sides[1]) % 2

    class Piece:
        def __init__(self, index, refs, at, extent):
            size = extent // 4

            def some(k, first, size):
                return refs[k].at[pl.ds(aligned(at[k] + part * (extent // 2) + first, 16), size)]

            self.copies = [described(some(0, 0, 2 * size), some(1, 0, 2 * size), wsem, 3 * index, across)]
            for k in range(2):
                block = some(1, k * size, size)
                self.copies.append(described(block, block, wsem, 3 * index + 1 + k, mates[k]))
            self.stage = 0

        def advance(self):
            if self.stage == 0:
                self.copies[0].wait_recv()
                self.copies[1].start()
                self.copies[2].start()
            else:
                self.copies[1].wait_recv()
                self.copies[2].wait_recv()
            self.stage += 1

    pieces = [Piece(c, (wq_s.at[0, c], wq_s.at[1, c]), (0, 0), quarter) for c in range(3)]
    pieces.append(Piece(3, (wo_s, wo_s), (0, quarter), quarter))
    for i in range(units // BLOCK):
        pieces.append(Piece(4 + 2 * i, (w1_s.at[0, i], w1_s.at[1, i]), (0, 0), width))
        pieces.append(Piece(5 + 2 * i, (w2_s.at[0], w2_s.at[1]), (i * BLOCK, i * BLOCK), BLOCK))
    pl.semaphore_wait(barrier, len(partners))
    unit_copy = remote(bias_u, uoth, wsem, 3 * len(pieces), across)
    head_copy = remote(bias_qv, voth, wsem, 3 * len(pieces) + 1, across)
    get_wq.wait()
    get_wo.wait()
    for item in pieces[:4]:
        item.copies[0].start()

    inside_loop = []

    def service(name, act):
        def at_point(k, ask):
            full = f"{name}{k}"
            if ask:
                return full in PLAN or full in WEIGHT_PLAN
            inside_loop.append(full)
            act(full)
            inside_loop.pop()

        return at_point

    def pass_on(name):
        for i in WEIGHT_PLAN.get(name, ()):
            if pieces[i].stage < 1:
                pieces[i].advance()

    def have_weight(*which):
        for i in which:
            while pieces[i].stage < 2:
                pieces[i].advance()

    ln1_gain, ln1_bias, out_bias, ln2_gain, ln2_bias, fc2_bias = (
        ref[...].reshape(1, width) for ref in (gain1, bias1, bias_o, gain2, bias2, bias_f)
    )
    get_tok.wait()

    def first_norm(at):
        plane = core * (count // (SIDE * SIDE)) + at // (SIDE * SIDE)
        line = (at // SIDE) % SIDE
        shape = (SIDE, width // 3)
        for k in range(4):
            spot = jnp.concatenate(
                [jnp.broadcast_to(table[pl.ds(plane, 1)], shape), jnp.broadcast_to(table[pl.ds(line + k, 1)], shape), table[...]], axis=1
            )
            span = pl.ds(aligned(at + k * SIDE, SIDE), SIDE)
            stream = tok_s[span].astype(F32) + spot
            sin_s[span] = stream
            xhat, _ = norm_stats(stream)
            n1_s[span] = (xhat * ln1_gain + ln1_bias).astype(BF16)

    loop(count, 4 * SIDE, first_norm)
    doc = ids[pl.ds(chip, 1), :]
    starts = [jnp.zeros((1, 1), F32)]
    starts += [jnp.sum(jnp.where(doc < v, 1.0, 0.0), axis=1, keepdims=True) for v in range(1, 4)]
    starts.append(jnp.full((1, 1), rows, F32))
    turn = jnp.zeros((1, 1), F32)
    for v in range(4):
        turn += jnp.where(starts[v + 1] - starts[v] == count, starts[v], 0.0)
    turn_here = turn - (core * count).astype(F32)

    def wrapped(v):
        v = jnp.where(v >= rows, v - rows, v)
        return jnp.where(v < 0, v + rows, v)

    def rotations(at):
        down = (lax.broadcasted_iota(jnp.int32, (64, rows), 0) + at).astype(F32)
        along = lax.broadcasted_iota(jnp.int32, (64, rows), 1).astype(F32)
        roll_s[pl.ds(at, 64)] = jnp.where(wrapped(down + turn_here) == along, 1.0, 0.0).astype(BF16)
        back_s[pl.ds(at, 64)] = jnp.where(wrapped(down - turn_here) == along, 1.0, 0.0).astype(BF16)
        where = wrapped((lax.broadcasted_iota(jnp.int32, (64, 128), 0) + at).astype(F32) + turn)
        mine = sum(jnp.where(where >= starts[v], 1.0, 0.0) for v in range(1, 4))
        slot = (lax.broadcasted_iota(jnp.int32, (64, 128), 1) % HEAD).astype(F32)
        sq_s[pl.ds(at, 64)] = jnp.where((slot < 4) & (slot != mine), 1.0, 0.0).astype(BF16)
        sk_s[pl.ds(at, 64)] = jnp.where(slot == mine, NEG_LARGE, 0.0).astype(BF16)


    for copy in get_w1:
        copy.wait()
    get_w2.wait()
    for item in pieces[4:]:
        item.copies[0].start()
    n1_copy = remote(n1_s.at[pl.ds(0, count)], n1_s.at[pl.ds(count, count)], csem, 0, sib)
    get_cot.wait()
    cot_copy = remote(cot_s.at[pl.ds(0, count)], cot_s.at[pl.ds(count, count)], csem, 1, sib)

    def rotate(at):
        nr_s[pl.ds(at, BLOCK)] = dot(roll_s[pl.ds(at, BLOCK)], n1_s[...]).astype(BF16)

    def project(j, at):
        n = nr_s[pl.ds(at, BLOCK)]
        biases = bias_qv if j == 0 else voth
        q = (dot_nt(n, wq_s[j, 0]) + biases[0:1]).astype(BF16) * SCALE
        k = dot_nt(n, wq_s[j, 1]).astype(BF16)
        v = (dot_nt(n, wq_s[j, 2]) + biases[1:2]).astype(BF16)
        q_s[j, pl.ds(at, BLOCK), :quarter] = q
        k_s[pl.ds(at, BLOCK), :quarter] = k
        v_s[j, pl.ds(at, BLOCK), :quarter] = v
        kt_s[j * quarter : (j + 1) * quarter, pl.ds(at, BLOCK)] = k.T * SCALE

    blocks = [(b, at) for b in range(2) for at in range(0, count, BLOCK)]

    def attend(j):
        for head in range(heads):
            at = 512 + 256 * head
            a_s[:, at : at + 128] = head_lanes(q_s.at[j], head, sq_s[...])
            a_s[:, at + 128 : at + 256] = head_lanes(k_s, head, sk_s[...])
        for at in range(0, rows, BLOCK):
            ou_s[:quarter, at : at + BLOCK] = v_s[j, at : at + BLOCK, :quarter].T

        def tile(here):
            b = here // count
            at = aligned(here % count, BLOCK)
            keys = pl.ds(aligned(b * count, count), count)
            for head in range(heads):
                column = 512 + 256 * head
                s = dot_nt(a_s[keys, column + 128 : column + 256], a_s[pl.ds(here, BLOCK), column : column + 128])
                m = jnp.max(s, axis=0, keepdims=True)
                e = jnp.exp(s - m)
                r = 1.0 / column_sum(e)
                low = e.astype(BF16)
                span = slice(head * HEAD, head * HEAD + HEAD)
                to = slice(j * quarter + head * HEAD, j * quarter + head * HEAD + HEAD)
                e_s[j * heads + head, b, :, pl.ds(at, BLOCK)] = low
                ot_s[to, pl.ds(here, BLOCK)] = (dot(ou_s[span, keys], low) * r).astype(BF16)
                r_s[j * heads + head : j * heads + head + 1, pl.ds(here, BLOCK)] = r

        return tile

    loop(rows, 64, rotations)
    n1_copy.wait_recv()
    loop(rows, BLOCK, rotate)
    loop(rows, BLOCK, lambda at: project(0, at))
    pass_on("p0")
    loop(rows, BLOCK, attend(0), service("a", pass_on))
    head_copy.wait_recv()
    have_weight(0, 1, 2)
    loop(rows, BLOCK, lambda at: project(1, at))
    pass_on("p1")
    loop(rows, BLOCK, attend(1), service("c", pass_on))

    have_weight(3)

    def unrotate(at):
        ou_s[:, pl.ds(at, BLOCK)] = dot(ot_s[...], roll_s[:, pl.ds(at, BLOCK)]).astype(BF16)

    loop(rows, BLOCK, unrotate)
    pass_on("u")

    def out_part(at):
        return dot_tn(ou_s[:, pl.ds(at, BLOCK)], wo_s[...])

    def att_half(at):
        return half_copy(sb1.at[pl.ds(at, BLOCK)], rb1.at[pl.ds(at, BLOCK)], 2, at)

    def n2_half(at):
        return half_copy(n2_s.at[pl.ds(at, BLOCK)], n2_s.at[pl.ds(aligned(count + at, BLOCK), BLOCK)], 4, at)

    def out_sib(at):
        sb1[pl.ds(at, BLOCK)] = out_part(count + at).astype(BF16)
        att_half(at).start()

    loop(count, BLOCK, out_sib)

    def out_mine(at):
        mid_s[pl.ds(at, BLOCK)] = sin_s[pl.ds(at, BLOCK)] + out_part(at) + out_bias

    loop(count, BLOCK, out_mine)
    pass_on("o")

    def second_norm(at):
        att_half(at).wait_recv()
        for off in range(0, BLOCK, 128):
            spot = pl.ds(aligned(at + off, 128), 128)
            mid = mid_s[spot] + rb1[spot].astype(F32)
            mid_s[spot] = mid
            xhat, _ = norm_stats(mid)
            n2_s[spot] = (xhat * ln2_gain + ln2_bias).astype(BF16)
        n2_half(at).start()

    loop(count, BLOCK, second_norm)
    pass_on("n")

    base_a = units
    parts = units // BLOCK
    steps = copies_of(len(full_bits))

    class Region:
        def __init__(self, index, row, size, cols, slot, kind, refs, to):
            own_r, oth_r, xr_r, land_r, both_r, rx_r = refs
            self.place, self.slot, self.to, self.xr = (row, size, 0, cols), slot, to, xr_r
            first, after = KINDS[kind]
            self.first = first is not None
            self.stages, self.stage, self.finished, self.sent = [], -1, False, []
            now, parts, used, trail = self.place, 8, 0, []
            sems = iter(range(index * steps, (index + 1) * steps))

            def copy(src, src_at, dst, dst_at, device):
                return described(src.at[self.window(src_at)], dst.at[self.window(dst_at)], gsem, next(sems), device)

            def piece(bits, mask):
                where = now
                for k, b in enumerate(bits):
                    where = self.cut(where, 1 - sides[b] if mask >> k & 1 else sides[b])
                return where

            sums = 1 + len(after) + len(full_bits)
            if self.first:
                keep, give, there = piece((first,), 0), piece((first,), 1), (row // 2, size // 2, 0, cols)
                place = self.landing(0, 4)
                copies = [copy(own_r, give, land_r, place, mate((first,))), copy(oth_r, give, both_r, there, mate((first,)))]
                adds = [(own_r, own_r, keep, [(land_r, place)]), (oth_r, oth_r, keep, [(both_r, there)])]
                self.stages.append((copies, adds, False))
                trail.append(((first,), keep))
                now, parts, used = keep, 4, 4
            self.stages.append(([copy(oth_r, now, xr_r, now, across)], [(own_r, own_r, now, [(xr_r, now)])], False))
            for bits in after:
                parts >>= len(bits)
                keep, copies, terms = piece(bits, 0), [], []
                for mask in range(1, 1 << len(bits)):
                    place = self.landing(used, parts)
                    used += parts
                    terms.append((land_r, place))
                    copies.append(copy(own_r, piece(bits, mask), land_r, place, mate([b for k, b in enumerate(bits) if mask >> k & 1])))
                self.stages.append((copies, [(own_r, own_r, keep, terms)], False))
                trail.append((bits, keep))
                now = keep
            for i, b in enumerate(full_bits):
                place = self.small_place()
                self.stages.append(([copy(own_r, now, rx_r[i], place, mates[b])], [(own_r, own_r, now, [(rx_r[i], place)])], True))
            copies, adds, full = self.stages[-1]
            self.stages[-1] = (copies, [(xr_r,) + adds[0][1:]], full)
            for bits, keep in reversed(trail):
                copies = []
                for mask in range(1, 1 << len(bits)):
                    copies.append(copy(xr_r, keep, xr_r, keep, mate([b for k, b in enumerate(bits) if mask >> k & 1])))
                self.stages.append((copies, [], False))

        def window(self, where):
            row, size, col, cols = where
            return pl.ds(row, size), pl.ds(col, cols)

        def cut(self, where, side):
            row, size, col, cols = where
            if (size // 2) % 16 == 0:
                return aligned(row + side * (size // 2), 16), size // 2, col, cols
            return row, size, aligned(col + side * (cols // 2), 128), cols // 2

        def landing(self, at, parts_here):
            row, rows_one, cols_one = self.slot
            full = self.place[3]
            if cols_one == full:
                return row + at * rows_one, parts_here * rows_one, 0, full
            if parts_here == 1:
                return row + at // 2 * rows_one, rows_one, at % 2 * cols_one, cols_one
            return row + at // 2 * rows_one, parts_here // 2 * rows_one, 0, full

        def small_place(self):
            row, rows_one, cols_one = self.slot
            if cols_one == self.place[3]:
                return row // 7, rows_one, 0, cols_one
            k = (self.place[0] - base_a) // quarter
            return units // 8 + k // 2 * rows_one, rows_one, k % 2 * cols_one, cols_one

        def begin(self, copies):
            for copy in copies:
                copy.start()
            self.sent += copies

        def ready(self, j):
            if self.first:
                self.stage = 0
                self.begin([self.stages[0][0][j]])
            elif j == 1:
                self.stage = 0
                self.begin(self.stages[0][0])

        def add(self, into, base, where, terms):
            row, size, col, cols = where
            step = 128 if size % 128 == 0 else 64 if size % 64 == 0 else 48 if size % 48 == 0 else 32

            def body(off):
                to = (pl.ds(aligned(row + off, 16), step), pl.ds(col, cols))
                parts_in = [ref[pl.ds(aligned(r + off, 16), step), pl.ds(c, cols)] for ref, (r, _, c, _) in terms]
                if len(parts_in) == 1:
                    into[to] = base[to] + parts_in[0]
                else:
                    into[to] = sum((v.astype(F32) for v in parts_in), base[to].astype(F32)).astype(BF16)

            if inside_loop:
                for off in range(0, size, step):
                    body(off)
            else:
                loop(size, step, body)

        def advance(self):
            if self.finished or self.stage < 0:
                return
            copies, adds, full = self.stages[self.stage]
            for copy in copies:
                copy.wait_recv()
            if full:
                for copy in copies:
                    copy.wait_send()
                self.sent = [c for c in self.sent if all(c is not d for d in copies)]
            for item in adds:
                self.add(*item)
            self.stage += 1
            if self.stage < len(self.stages):
                self.begin(self.stages[self.stage][0])
                return
            self.finished = True
            to_write.append(self)

    chunks = []
    refs = (own, oth, xr, land, land_both, rx)
    for i in range(parts):
        slot = (i * 7 * (BLOCK // 8), BLOCK // 8, width)
        to = g2_h.at[pl.ds(i * BLOCK, BLOCK)]
        chunks.append(Region(2 * i, i * BLOCK, BLOCK, width, slot, ORDERS[2 * i], refs, to))
        refs_one = tuple(ref.at[i] for ref in (own1, oth1, xr1, land1, land1_both)) + ([ref.at[i] for ref in rx1],)
        to = g1_h.at[:, pl.ds(i * BLOCK, BLOCK)]
        chunks.append(Region(2 * i + 1, 0, width, BLOCK, (0, width // 8, BLOCK), ORDERS[2 * i + 1], refs_one, to))
    for i in range(4):
        slot = (7 * units // 8 + i * quarter, quarter // 4, width // 2)
        to = go_h if i == 0 else gq_h.at[i - 1]
        chunks.append(Region(2 * parts + i, base_a + i * quarter, quarter, width, slot, ORDERS[2 * parts + i], refs, to))
    first_att = 2 * parts

    class Small:
        def __init__(self, tile, index, everywhere, paired, groups):
            self.tile, self.everywhere, self.paired = tile, everywhere, paired
            landings = [near.at[3 * index + k] for k in range(3)] + [far.at[(7 + len(full_bits)) * index + k] for k in range(7 + len(full_bits))]
            sems = iter(range(index * len(landings), (index + 1) * len(landings)))
            landings = iter(landings)

            def stage(devices):
                places = [next(landings) for _ in devices]
                return places, [described(tile, dst, ssem, next(sems), d) for dst, d in zip(places, devices)]

            self.stages = [stage([sib, across, facing])]
            for bits in groups + [(b,) for b in full_bits]:
                masks = range(1, 1 << len(bits))
                self.stages.append(stage([mate([b for k, b in enumerate(bits) if mask >> k & 1]) for mask in masks]))
            self.stage, self.finished = -1, False

        def start(self):
            self.stage = 0
            for copy in self.stages[0][1]:
                copy.start()

        def advance(self):
            if self.finished or self.stage < 0:
                return
            places, copies = self.stages[self.stage]
            for copy in copies:
                copy.wait()
            tile = self.tile
            if self.stage == 0:
                beside, over, facing_ = places
                n, p = self.everywhere, self.paired
                tile[0:n] = (tile[0:n] + beside[0:n]) + (over[0:n] + facing_[0:n])
                tile[n : n + p] = tile[n : n + p] + over[n + p : n + 2 * p]
            else:
                got = [tile[...]] + [place[...] for place in places]
                while len(got) > 1:
                    got = [got[k] + got[k + 1] for k in range(0, len(got), 2)]
                tile[...] = got[0]
            self.stage += 1
            if self.stage == len(self.stages):
                self.finished = True
                return
            for copy in self.stages[self.stage][1]:
                copy.start()

    first_small = Small(early, 0, 4, 1, [(b,) for b in half_bits])
    last_small = Small(late, 1, 2, 2, [tuple(half_bits)])

    def ready(i, j):
        chunks[i].ready(j)

    to_write = []

    def write_finished():
        while to_write:
            region = to_write.pop()
            region.done = local(region.xr.at[region.window(region.place)], region.to)

    def hook(name):
        pass_on(name)
        for i in PLAN.get(name, ()):
            (chunks + [last_small, first_small])[i].advance()
            if not inside_loop:
                write_finished()

    def chunk_rows(j, i, at):
        span = pl.ds(at, BLOCK)
        cols = slice(j * units + i * BLOCK, j * units + (i + 1) * BLOCK)
        mine = slice(i * BLOCK, (i + 1) * BLOCK)
        bias = (bias_u if j == 0 else uoth)[mine].reshape(1, BLOCK)
        h = dot(n2_s[span], w1_s[j, i]) + bias
        a, slope = gelu_pair(h)
        a_s[span, cols] = a.astype(BF16)
        g = (dot_nt(cot_s[span], w2_s[j, mine]) * slope).astype(BF16)
        g_s[span, cols] = g

    def chunk_grads(j, i):
        cols = slice(j * units + i * BLOCK, j * units + (i + 1) * BLOCK)
        mine = slice(i * BLOCK, (i + 1) * BLOCK)
        to = oth if j == 1 else own

        def second(at):
            to[pl.ds(i * BLOCK + at, 128)] = dot_tn(a_s[:, pl.ds(cols.start + at, 128)], cot_s[...]).astype(BF16)

        loop(BLOCK, 128, second)
        ready(2 * i, j)
        g = g_s[:, cols]

        def first(at):
            (oth1 if j == 1 else own1)[i, pl.ds(at, BLOCK)] = dot(n2t_s[pl.ds(at, BLOCK)], g_s[:, cols]).astype(BF16)

        loop(width, BLOCK, first)
        ready(2 * i + 1, j)
        early[4 + j : 5 + j, mine] = column_sum(g.astype(F32))
        hook(f"f{j}{i}")

    def feed(j, i, first=False):
        if first:
            loop(count, BLOCK, lambda at: chunk_rows(j, i, at))
            hook(f"r{j}{i}.0")
            cot_copy.wait_recv()

            def received(at):
                n2_half(at).wait_recv()
                chunk_rows(j, i, count + at)

            loop(count, BLOCK, received)
            hook(f"r{j}{i}.1")

            def turned(at):
                n2t_s[:, pl.ds(at, BLOCK)] = n2_s[pl.ds(at, BLOCK)].T

            loop(rows, BLOCK, turned)
        else:
            loop(rows, BLOCK, lambda at: chunk_rows(j, i, at), service(f"r{j}{i}.", hook), 2)
        chunk_grads(j, i)

    early[...] = jnp.zeros_like(early)
    late[...] = jnp.zeros_like(late)

    def sum_cot(at):
        early[3:4] += column_sum(cot_s[pl.ds(at, 128)].astype(F32))

    loop(count, 128, sum_cot)
    unit_copy.wait_recv()
    for i in range(parts):
        have_weight(4 + 2 * i, 5 + 2 * i)
        feed(1, i, first=i == 0)
        feed(0, i)

    def back_two(at):
        span = pl.ds(at, BLOCK)
        total = None
        for j in range(2):
            for i in range(parts):
                at_col = j * units + i * BLOCK
                term = dot_nt(g_s[span, at_col : at_col + BLOCK], w1_s[j, i])
                total = term if total is None else total + term
        return total

    def mlp_part(at):
        span = pl.ds(at, BLOCK)
        return dot(a_s[span, :units], w2_s[0]) + dot(a_s[span, units:], w2_s[1])

    def gn2_half(at):
        return half_copy(sb2.at[pl.ds(at, BLOCK)], rb2.at[pl.ds(at, BLOCK)], 6, at)

    def dm_half(at):
        return half_copy(n2_s.at[pl.ds(at, BLOCK)], n2_s.at[pl.ds(aligned(count + at, BLOCK), BLOCK)], 10, at)

    def back_two_sib(at):
        sb2[pl.ds(at, BLOCK)] = back_two(count + at).astype(BF16)
        gn2_half(at).start()

    def back_two_mine(at):
        gm_s[pl.ds(at, BLOCK)] = back_two(at)

    def mlp_sib(at):
        sb1[pl.ds(at, BLOCK)] = mlp_part(count + at).astype(BF16)

    loop(count, BLOCK, back_two_sib)
    hook("g0")
    loop(count, BLOCK, back_two_mine)
    hook("gn2")

    def second_back(at):
        gn2_half(at).wait_recv()
        n2_half(at).wait_send()
        for off in range(0, BLOCK, 128):
            spot = pl.ds(aligned(at + off, 128), 128)
            xhat, sigma = norm_stats(mid_s[spot])
            grad = gm_s[spot] + rb2[spot].astype(F32)
            cot = cot_s[spot].astype(F32)
            back = cot + norm_back(grad, ln2_gain, xhat, sigma)
            gm_s[spot] = back
            n2_s[spot] = back.astype(BF16)
            early[0:1] += column_sum(back)
            early[1:2] += column_sum(grad * xhat)
            early[2:3] += column_sum(grad)
        dm_half(at).start()

    loop(count, BLOCK, second_back)
    hook("lb")
    for at in range(0, count, BLOCK):
        att_half(at).wait_send()
    loop(count, BLOCK, mlp_sib)
    mlp_copy = remote(sb1, rb1, csem, 8, sib)
    first_small.start()
    hook("ln2")

    for at in range(0, count, BLOCK):
        dm_half(at).wait_recv()

    start = base_a + quarter
    zero = jnp.zeros((count, 128), BF16)
    grad_s = dq_s = ou_s
    n1_copy.wait_send()

    def keep_gradient(j, c):
        to = oth if j == 1 else own
        low = start + c * quarter
        dt = ot_s.at[j * quarter : (j + 1) * quarter]

        def columns(at):
            to[low : low + quarter, pl.ds(at, BLOCK)] = dot(dt[...], nr_s[:, pl.ds(at, BLOCK)]).astype(BF16)

        loop(width, BLOCK, columns)
        ready(first_att + 1 + c, j)
        if c != 1:
            d = g_s[:, (3 * j + c) * BLOCK : (3 * j + c) * BLOCK + quarter]
            late[2 + c // 2 + 2 * j : 3 + c // 2 + 2 * j, :quarter] = column_sum(d.astype(F32))

    def values_back(j):
        base = j * quarter
        to = oth if j == 1 else own

        def weight(at):
            to[base_a : base_a + quarter, pl.ds(at, BLOCK)] = dot(ou_s[base : base + quarter], n2_s[:, pl.ds(at, BLOCK)]).astype(BF16)

        loop(width, BLOCK, weight)
        ready(first_att, j)

        def output(at):
            grad_s[base : base + quarter, pl.ds(at, BLOCK)] = dot_nt(wo_s[base : base + quarter], n2_s[pl.ds(at, BLOCK)]).astype(BF16)

        loop(rows, BLOCK, output)
        hook(f"w{j}.0")
        go_s = n1_s.at[:, 256 * j : 256 * (j + 1)]

        def scale(at):
            here = pl.ds(at, BLOCK)
            grad_t = dot_nt(grad_s[base : base + quarter], roll_s[here])
            for head in range(heads):
                row = j * heads + head
                r = r_s[row : row + 1, here]
                g = grad_t[head * HEAD : (head + 1) * HEAD]
                at_head = slice(base + head * HEAD, base + (head + 1) * HEAD)
                in_s[row : row + 1, here] = column_sum(g * ot_s[at_head, here].astype(F32)) * r
                gt_s[at_head, here] = (g * r).astype(BF16)
            go_s[here, :quarter] = gt_s[base : base + quarter, here].T

        loop(rows, BLOCK, scale)

        def block(at):
            here = pl.ds(at, count)
            b = at // count
            dv = [None, None]
            for head in range(heads):
                tile = head // 2
                gh = jnp.where(lane_half(count, head % 2 == 1), go_s[here, 128 * tile : 128 * tile + 128], zero)
                part = dot(e_s[j * heads + head, b], gh)
                dv[tile] = part if dv[tile] is None else dv[tile] + part
            dv = jnp.concatenate(dv, axis=1)[:, :quarter].astype(BF16)
            g_s[here, (3 * j + 2) * BLOCK : (3 * j + 2) * BLOCK + quarter] = dv
            ot_s[base : base + quarter, here] = dv.T

        loop(rows, count, block)
        hook(f"w{j}.1")
        keep_gradient(j, 2)
        hook(f"v{j}")

    def scores_back(j):
        base = j * quarter

        def block(at):
            here = pl.ds(at, count)
            b = at // count
            dk = [None, None]
            for head in range(heads):
                tile = head // 2
                row = j * heads + head
                half = lane_half(count, head % 2 == 1)
                lanes = slice(128 * tile, 128 * tile + 128)
                vh = jnp.where(half, v_s[j, here, lanes], zero)
                qh = jnp.where(half, q_s[j, here, lanes], zero)
                last_row = min(128 * tile + 128, quarter)
                vh = vh[:, : last_row - 128 * tile]
                ds = n2t_s.at[:count, head * count : (head + 1) * count] if head < 2 else ds_s
                for off in range(0, count, BLOCK):
                    some = pl.ds(aligned(at + off, BLOCK), BLOCK)
                    dp_t = dot(vh, gt_s[base + 128 * tile : base + last_row, some])
                    grad = (dp_t - in_s[row : row + 1, some]).astype(BF16)
                    ds[:, off : off + BLOCK] = grad * e_s[row, b, :, off : off + BLOCK]
                part = dot(ds[...], qh)
                dk[tile] = part if dk[tile] is None else dk[tile] + part
                kth = kt_s[base + head * HEAD : base + head * HEAD + HEAD, here]
                dq_s[base + head * HEAD : base + head * HEAD + HEAD, here] = dot(kth, ds[...]).astype(BF16)
            dk = jnp.concatenate(dk, axis=1)[:, :quarter].astype(BF16)
            g_s[here, (3 * j + 1) * BLOCK : (3 * j + 1) * BLOCK + quarter] = dk
            ot_s[base : base + quarter, here] = dk.T
            g_s[here, 3 * j * BLOCK : 3 * j * BLOCK + quarter] = dq_s[base : base + quarter, here].T

        loop(rows, count, block, service(f"b{j}.", hook))
        keep_gradient(j, 1)
        hook(f"k{j}")
        ot_s[base : base + quarter] = dq_s[base : base + quarter]
        keep_gradient(j, 0)
        hook(f"s{j}")

    values_back(1)
    scores_back(1)
    values_back(0)
    scores_back(0)

    def finish_out(at):
        span = pl.ds(at, BLOCK)
        mid_s[span] = mid_s[span] + mlp_part(at) + fc2_bias

    loop(count, BLOCK, finish_out)
    hook("fo")
    mlp_copy.wait_recv()

    def write_out(at):
        spot = pl.ds(at, 128)
        tok_s[spot] = (mid_s[spot] + rb1[spot].astype(F32)).astype(BF16)

    loop(count, 128, write_out)
    put_out = local(tok_s, out_h)
    hook("fin")

    def back_one(at):
        total = None
        for j in range(2):
            for c in range(3):
                d = g_s[pl.ds(at, BLOCK), (3 * j + c) * BLOCK : (3 * j + c) * BLOCK + quarter]
                term = dot(d, wq_s[j, c])
                total = term if total is None else total + term
        n2_s[pl.ds(at, BLOCK)] = total.astype(BF16)

    for at in range(0, count, BLOCK):
        dm_half(at).wait_send()
    loop(rows, BLOCK, back_one, service("d.", hook), 2)
    for at in range(0, count, BLOCK):
        gn2_half(at).wait_send()

    def gn1_half(at):
        return half_copy(sb2.at[pl.ds(at, BLOCK)], rb2.at[pl.ds(at, BLOCK)], 12, at)

    def back_one_sib(at):
        sb2[pl.ds(at, BLOCK)] = dot(back_s[pl.ds(count + at, BLOCK)], n2_s[...]).astype(BF16)
        gn1_half(at).start()

    def back_one_mine(at):
        mid_s[pl.ds(at, BLOCK)] = dot(back_s[pl.ds(at, BLOCK)], n2_s[...])

    loop(count, BLOCK, back_one_sib)
    loop(count, BLOCK, back_one_mine)
    hook("e.0")
    mlp_copy.wait_send()

    def first_back(at):
        gn1_half(at).wait_recv()
        for off in range(0, BLOCK, 128):
            spot = pl.ds(aligned(at + off, 128), 128)
            xhat, sigma = norm_stats(sin_s[spot])
            grad = mid_s[spot] + rb2[spot].astype(F32)
            sb1[spot] = (gm_s[spot] + norm_back(grad, ln1_gain, xhat, sigma)).astype(BF16)
            late[0:1] += column_sum(grad * xhat)
            late[1:2] += column_sum(grad)

    loop(count, BLOCK, first_back)
    put_in = local(sb1, ing_h)
    last_small.start()
    hook("e.1")
    hook("tail")
    left = [first_small, last_small] + chunks
    while left:
        for item in left:
            item.advance()
            write_finished()
        left = [item for item in left if not item.finished]

    for row, source, at in ((0, late, 0), (1, late, 1), (2, early, 0), (3, early, 1), (4, early, 2), (5, early, 3), (8, early, 4), (9, late, 2), (10, late, 3)):
        small_o[row : row + 1] = source[at : at + 1]

    passed = [copy for item in pieces for copy in item.copies]
    for copy in [unit_copy, head_copy, cot_copy] + [gn1_half(at) for at in range(0, count, BLOCK)] + passed:
        copy.wait_send()
    for chunk in chunks:
        for copy in chunk.sent:
            copy.wait_send()
        chunk.done.wait()
    put_out.wait()
    put_in.wait()


def copies_of(full):
    most = 0
    for kind in ORDERS:
        first, after = KINDS[kind]
        most = max(most, 1 + full + 2 * sum((1 << len(bits)) - 1 for bits in after) + (0 if first is None else 3))
    return most


def call_layer(dp_size, tokens, cotangent, ids, table, vectors, wq, wo, w1, w2):
    count, width = tokens.shape
    rows = 2 * count
    quarter = wo.shape[0]
    units = w1.shape[1]
    heads = quarter // HEAD
    grad_rows = units + 4 * quarter
    parts = units // BLOCK
    bits = [b for b in range(20) if (1 << b) < dp_size]
    half_bits = bits[:3]
    shape = jax.ShapeDtypeStruct
    vm = pltpu.VMEM
    regions = 2 * (units // BLOCK) + 4
    steps = copies_of(len(bits) - len(half_bits))
    fetched = 4 + 2 * (units // BLOCK)
    scratch = (
        [vm((count, width), BF16), vm((rows, width), BF16)]
        + [vm((count, width), F32)] * 3
        + [vm((rows, width), BF16)] * 2
        + [vm((width, rows), BF16)]
        + [vm((2,) + wq.shape, BF16), vm((2 * quarter, width), BF16), vm((2, units // BLOCK, width, BLOCK), BF16), vm((2,) + w2.shape, BF16)]
        + [vm((2, rows, 256), BF16)] * 2
        + [vm((2 * quarter, rows), BF16)] * 4
        + [vm((8, rows), F32)] * 2
        + [vm((2 * heads, 2, count, count), BF16)]
        + [vm((rows, rows), BF16)] * 2
        + [vm((rows, width), BF16), vm((count, count), BF16)]
        + [vm((rows, 2 * units), BF16)] * 2
        + [vm((count, width), BF16)] * 4
        + [vm((grad_rows, width), BF16)] * 3
        + [vm((7 * units // 8 + 4 * quarter, width), BF16), vm((units // 2, width), BF16)]
        + [vm((parts, width, BLOCK), BF16)] * 3
        + [vm((parts, 7 * width // 8, BLOCK), BF16), vm((parts, width // 2, BLOCK), BF16)]
        + [vm((grad_rows >> len(half_bits), width), BF16)] * (len(bits) - len(half_bits))
        + [vm((parts, width // 8, BLOCK), BF16)] * (len(bits) - len(half_bits))
        + [vm((units,), F32), vm((2, quarter), F32), vm((8, width), F32), vm((8, width), F32)]
        + [vm((6, 8, width), F32), vm((14 + 2 * (len(bits) - 3), 8, width), F32)]
        + [pltpu.SemaphoreType.DMA((8 + units // BLOCK + regions,))]
        + [pltpu.SemaphoreType.DMA((2, n)) for n in (3 * fetched + 2, 14, regions * steps, 2 * (10 + len(bits) - 3))]
    )
    anywhere = pl.BlockSpec(memory_space=pl.ANY)
    inside = pl.BlockSpec(memory_space=pltpu.VMEM)
    return pl.pallas_call(
        functools.partial(layer, dp_size, half_bits),
        out_shape=[shape((count, width), BF16)] * 2
        + [shape(w2.shape, BF16), shape(w1.shape, BF16), shape(wo.shape, BF16), shape(wq.shape, BF16), shape((16, width), F32)],
        in_specs=[anywhere] * 2 + [inside] * (2 + len(vectors)) + [anywhere] * 4,
        out_specs=[anywhere] * 6 + [inside],
        scratch_shapes=scratch,
        compiler_params=pltpu.CompilerParams(vmem_limit_bytes=VMEM_LIMIT, collective_id=0, has_side_effects=True),
        name="layer",
    )(tokens, cotangent, ids, table, *vectors, wq, wo, w1, w2)


def finish(*refs):
    sources, small, rest = refs[:6], refs[6], refs[7:]
    results, vectors, rest = rest[:6], rest[6:14], rest[14:]
    narrow, wide, (get, put) = rest[:6], rest[6:10], rest[10:]
    blocks = []
    for k, src in enumerate(sources):
        if src.ndim == 3:
            places = list(range(src.shape[0]))
        else:
            step = min(BLOCK, src.shape[0])
            places = [pl.ds(at, step) for at in range(0, src.shape[0], step)]
        for at in places:
            low = narrow[k].at[at]
            blocks.append((src.at[at], low, low if k < 2 else wide[k - 2].at[at], results[k].at[at]))
    reads = [pltpu.make_async_copy(src, low, get.at[n]) for n, (src, low, _, _) in enumerate(blocks)]
    writes = [pltpu.make_async_copy(high, dst, put.at[n]) for n, (_, _, high, dst) in enumerate(blocks)]
    for copy in reads:
        copy.start()
    for i in range(6):
        vectors[i][...] = small[i]
    vectors[6][...] = small[8, : vectors[6].shape[0]]
    vectors[7][...] = small[9:11, : vectors[7].shape[1]]
    for read, write, (_, low, high, _) in zip(reads, writes, blocks):
        read.wait()
        if high is not low:

            def cast(at, low=low, high=high):
                high[pl.ds(at, 64)] = low[pl.ds(at, 64)].astype(F32)

            loop(low.shape[0], 64, cast)
        write.start()
    for copy in writes:
        copy.wait()


def call_finish(arrays, small, units, quarter):
    width = small.shape[1]
    shape = jax.ShapeDtypeStruct
    extents = [(width,)] * 6 + [(units,), (2, quarter)]
    kinds = [BF16, BF16, F32, F32, F32, F32]
    anywhere = pl.BlockSpec(memory_space=pl.ANY)
    inside = pl.BlockSpec(memory_space=pltpu.VMEM)
    grads = arrays[2:]
    return pl.pallas_call(
        finish,
        in_specs=[anywhere] * len(arrays) + [inside],
        out_specs=[anywhere] * len(arrays) + [inside] * len(extents),
        out_shape=[shape(a.shape, k) for a, k in zip(arrays, kinds)] + [shape(e, F32) for e in extents],
        scratch_shapes=[pltpu.VMEM(a.shape, BF16) for a in arrays]
        + [pltpu.VMEM(a.shape, F32) for a in grads]
        + [pltpu.SemaphoreType.DMA((16,)), pltpu.SemaphoreType.DMA((16,))],
        compiler_params=pltpu.CompilerParams(vmem_limit_bytes=VMEM_LIMIT),
        name="finish",
    )(*arrays, small)


def per_device(
    tokens, segment_ids, ln1_gain, ln1_bias, qkv_weight, qv_bias, out_weight, out_bias,
    ln2_gain, ln2_bias, fc1_weight, fc1_bias, fc2_weight, fc2_bias, cotangent,
):
    width = tokens.shape[1]
    freq_count = width // 6
    frequency = 10000.0 ** (-jnp.arange(freq_count, dtype=F32) / freq_count)
    angles = jnp.arange(SIDE, dtype=F32)[:, None] * frequency[None, :]
    table = jnp.concatenate([jnp.sin(angles), jnp.cos(angles)], axis=1)
    vectors = (ln1_gain, ln1_bias, out_bias, ln2_gain, ln2_bias, fc2_bias, fc1_bias, qv_bias)
    *arrays, small = call_layer(
        lax.axis_size("dp"), tokens, cotangent, segment_ids, table, vectors, qkv_weight.transpose(0, 2, 1), out_weight, fc1_weight, fc2_weight
    )
    out, ing, g2, g1, go, gq, a0, a1, a2, a3, a4, a5, g_units, g_heads = call_finish(arrays, small, fc1_weight.shape[1], out_weight.shape[0])
    return (out, ing, a0, a1, gq.transpose(0, 2, 1), g_heads, go, a2, a3, a4, g1, g_units, g2, a5)


def solution(mesh):
    placed = (
        P(("dp", "tensor"), None),
        P("dp", None),
        P(),
        P(),
        P(None, None, "tensor"),
        P(None, "tensor"),
        P("tensor", None),
        P(),
        P(),
        P(),
        P(None, "tensor"),
        P("tensor"),
        P("tensor", None),
        P(),
        P(("dp", "tensor"), None),
    )
    return jax.shard_map(
        per_device,
        mesh=mesh,
        in_specs=placed,
        out_specs=(
            P(("dp", "tensor"), None),
            P(("dp", "tensor"), None),
            P(),
            P(),
            P(None, None, "tensor"),
            P(None, "tensor"),
            P("tensor", None),
            P(),
            P(),
            P(),
            P(None, "tensor"),
            P("tensor"),
            P("tensor", None),
            P(),
        ),
        check_vma=False,
    )
```
